128 devices in a mesh: rep: 16 (over y, z_hi, core), shard: 8 (over z_lo, x).
Axes of the slice: x: 4, y: 4, z: 4 (z_hi: 2, z_lo: 2; z = z_hi * 2 + z_lo), core: 2. Of those that a mesh axis runs over, the one named last changes fastest.
Arguments:
- tokens: bfloat16 [16384, 2048], P(('rep', 'shard')), may hold values from -6 to 6
- doc_lengths: int32 [128, 3], P(('rep', 'shard')), may hold values from 1 to 64, 128 in all within a row
- cotangent: bfloat16 [16384, 2048], P(('rep', 'shard')), may hold values from -6 to 6
- ln1_gain: bfloat16 [2048], P('shard'), may hold values from 0.5 to 1.5
- ln1_bias: bfloat16 [2048], P('shard'), may hold values from -1.5 to 1.5
- ln2_gain: bfloat16 [2048], P('shard'), may hold values from 0.5 to 1.5
- ln2_bias: bfloat16 [2048], P('shard'), may hold values from -1.5 to 1.5
- qkv_weight: bfloat16 [2048, 6144], P('shard'), may hold values from -0.125 to 0.125
- qkv_bias: bfloat16 [6144], P('shard'), may hold values from -3 to 3
- out_weight: bfloat16 [2048, 2048], P('shard'), may hold values from -0.5 to 0.5
- out_bias: bfloat16 [2048], P('shard'), may hold values from -3 to 3
- up_weight: bfloat16 [2048, 8192], P('shard'), may hold values from -0.125 to 0.125
- up_bias: bfloat16 [8192], P('shard'), may hold values from -3 to 3
- down_weight: bfloat16 [8192, 2048], P('shard'), may hold values from -0.09375 to 0.09375
- down_bias: bfloat16 [2048], P('shard'), may hold values from -3 to 3
Outputs:
- mixed: bfloat16 [16384, 2048], P(('rep', 'shard'))
- tokens_grad: float32 [16384, 2048], P(('rep', 'shard'))
- ln1_gain_grad: float32 [2048], P('shard')
- ln1_bias_grad: float32 [2048], P('shard')
- ln2_gain_grad: float32 [2048], P('shard')
- ln2_bias_grad: float32 [2048], P('shard')
- qkv_weight_grad: float32 [2048, 6144], P('shard')
- qkv_bias_grad: float32 [6144], P('shard')
- out_weight_grad: float32 [2048, 2048], P('shard')
- out_bias_grad: float32 [2048], P('shard')
- up_weight_grad: float32 [2048, 8192], P('shard')
- up_bias_grad: float32 [8192], P('shard')
- down_weight_grad: float32 [8192, 2048], P('shard')
- down_bias_grad: float32 [2048], P('shard')
The draws below stay inside these ranges and needn't reach their ends.
Inputs may be any that keep to these rules, and one draw needn't show every extreme that they name: `doc_lengths`: each row sums to 128; some document has exactly 64 tokens.
All inputs are finite; a program needn't handle non-finite values.
Results may differ from the reference program's by a relative error of at most 0.02.
Values may be sent and summed in bfloat16 or wider, within the bound.
No kernel may reach another device: no remote copies, remote signals or barrier semaphores. Data moves between devices by JAX's collectives and lax.ppermute only.
A program may use at most 448 MiB of HBM per device.

```python
import math
import jax
import jax.numpy as jnp
import numpy as np
from jax import lax

D = 2048
HEADS = 8
HEAD_DIM = 256
ROT = 64
FF = 8192
TOK_DEV = 128
DOCS_DEV = 3
TOKENS = 16384
N_REP = 16
N_SHARD = 8


def shard_levels(own_key, shape, shards, smallest, top_value):
    level, own = 1.0, jax.random.fold_in(own_key, 6)
    for axis_at, blocks in shards:
        steps = jnp.exp(jax.random.uniform(jax.random.fold_in(own, axis_at), (blocks,), jnp.float32, smallest / len(shards), top_value / len(shards)))
        level = level * jnp.repeat(steps, shape[axis_at] // blocks).reshape([-1 if axis == axis_at else 1 for axis in range(len(shape))])
    return level


def split_up(number_of, total, bound, skew):
    weights = [(1 << 20) // math.isqrt(grade ** skew) + 1 for grade in range(2, number_of + 1)]
    rest, counts = total - bound - (number_of - 1), [1] * (number_of - 1)
    while rest > 0:
        candidates = [i for i in range(number_of - 1) if counts[i] < bound]
        whole, left = sum([weights[i] for i in candidates]), rest
        for i in candidates:
            more = min(bound - counts[i], max(1, left * weights[i] // whole), rest)
            counts[i] = counts[i] + more
            rest = rest - more
    return np.array([bound] + counts)


def ragged(own_key, count, total, most, lean):
    if count == 2:
        one = jax.random.randint(own_key, (), max(1, total - most), min(most, total - 1) + 1)
        return jnp.stack([one, total - one])
    sizes = jnp.asarray(split_up(count, total, most, lean), jnp.int32)
    twos = (count - 1) // 2
    giver, sink = sizes[1:1 + 2 * twos:2], sizes[2:2 + 2 * twos:2]
    slack = jnp.minimum(giver - 1, most - sink)
    passed = jax.random.randint(jax.random.fold_in(own_key, 1), (twos,), 0, 1 << 20) % (slack + 1)
    sizes = sizes.at[1:1 + 2 * twos:2].set(giver - passed).at[2:2 + 2 * twos:2].set(sink + passed)
    return sizes[jax.random.permutation(jax.random.fold_in(own_key, 2), count)]


def noise(own_key, dims, deviation, limit, pieces=(), kind=jnp.bfloat16):
    level = shard_levels(own_key, dims, pieces, -0.22, 0.18) if pieces else 1.0
    entries = jax.random.normal(own_key, dims, jnp.float32) * deviation * level
    return jnp.minimum(jnp.maximum(entries, -limit), limit).astype(kind)


def setup_inputs(seed: int = 0) -> dict:
    key_of = jax.random.split(jax.random.key(seed), 16)
    return {
        "tokens": noise(key_of[0], (TOKENS, D), 1.0, 6.0, ((0, 128),)),
        "doc_lengths": jax.vmap(lambda own: ragged(own, DOCS_DEV, TOK_DEV, TOK_DEV // 2, 2))(jax.random.split(key_of[1], (N_REP * N_SHARD))).reshape((N_REP * N_SHARD, DOCS_DEV)).astype(jnp.int32),
        "cotangent": noise(key_of[2], (TOKENS, D), 1.0, 6.0, ((0, 128),)),
        "ln1_gain": jnp.clip(1.0 + 0.1 * jax.random.normal(key_of[3], (D,), jnp.float32), 0.5, 1.5).astype(jnp.bfloat16),
        "ln1_bias": noise(key_of[4], (D,), 0.3, 1.5, ((0, 8),)),
        "ln2_gain": jnp.clip(1.0 + 0.1 * jax.random.normal(key_of[5], (D,), jnp.float32), 0.5, 1.5).astype(jnp.bfloat16),
        "ln2_bias": noise(key_of[6], (D,), 0.3, 1.5, ((0, 8),)),
        "qkv_weight": noise(key_of[7], (D, 3 * D), D ** -0.5, 0.125, ((0, 8),)),
        "qkv_bias": noise(key_of[8], (3 * D,), 0.5, 3.0, ((0, 8),)),
        "out_weight": noise(key_of[9], (D, D), (D // 16) ** -0.5, 0.5, ((0, 8),)),
        "out_bias": noise(key_of[10], (D,), 0.5, 3.0, ((0, 8),)),
        "up_weight": noise(key_of[11], (D, FF), D ** -0.5, 0.125, ((0, 8),)),
        "up_bias": noise(key_of[12], (FF,), 0.5, 3.0, ((0, 8),)),
        "down_weight": noise(key_of[13], (FF, D), (FF // 2) ** -0.5, 0.09375, ((0, 8),)),
        "down_bias": noise(key_of[14], (D,), 0.5, 3.0, ((0, 8),)),
    }


EPS = 1e-05

@jax.custom_vjp
def low(v):
    return lax.optimization_barrier(v.astype(jnp.bfloat16)).astype(jnp.float32)

@jax.custom_vjp
def low_back(v):
    return v

def low_keep(v):
    return (low(v), None)

def low_pass(kept, grad):
    return (grad,)

def back_keep(v):
    return (v, None)

def back_low(kept, grad):
    return (low(grad),)
low.defvjp(low_keep, low_pass)
low_back.defvjp(back_keep, back_low)

def layer_norm(value, gain, bias):
    centre = value - lax.optimization_barrier(jnp.mean(value, -1, keepdims=True))
    spread = lax.optimization_barrier(jnp.mean(centre * centre, -1, keepdims=True))
    return centre * lax.rsqrt(spread + EPS) * gain + bias

def product(left, right):
    return jnp.dot(left, right, precision=lax.Precision.HIGHEST)

def rotate(value, cosine, sine):
    half = ROT // 2
    first = value[..., :half]
    second = value[..., half:ROT]
    return jnp.concatenate([first * cosine - second * sine, second * cosine + first * sine, value[..., ROT:]], -1)

def reference(tokens, doc_lengths, cotangent, ln1_gain, ln1_bias, ln2_gain, ln2_bias, qkv_weight, qkv_bias, out_weight, out_bias, up_weight, up_bias, down_weight, down_bias):
    blocks = doc_lengths.shape[0]
    ends = jnp.cumsum(doc_lengths, 1).astype(jnp.int32)
    starts = (ends - doc_lengths).astype(jnp.int32)
    steps_t = jnp.arange(TOK_DEV, dtype=jnp.int32)
    segment = lax.optimization_barrier(jnp.sum((steps_t[None, :, None] >= ends[:, None, :]).astype(jnp.int32), -1))
    slots = jnp.arange(DOCS_DEV, dtype=jnp.int32)
    begin = lax.optimization_barrier(jnp.sum(jnp.where(segment[:, :, None] == slots[None, None, :], starts[:, None, :], 0), -1))
    position = (steps_t[None, :] - begin).astype(jnp.float32)
    freq = 10000.0 ** (-2.0 * jnp.arange(ROT // 2, dtype=jnp.float32) / ROT)
    angle = position[:, :, None, None] * freq[None, None, None, :]
    cosine = jnp.cos(angle)
    sine = jnp.sin(angle)
    allowed = (segment[:, :, None] == segment[:, None, :]) & (steps_t[None, None, :] <= steps_t[None, :, None])
    scale = HEAD_DIM ** (-0.5)

    def forward(xf, l1g, l1b, l2g, l2b, wqkv, bqkv, wout, bout, wup, bup, wdown, bdown):
        h1 = low(layer_norm(xf, l1g, l1b))
        h2 = low(layer_norm(xf, l2g, l2b))
        qkv = low_back(product(h1, wqkv) + bqkv)
        query = qkv[:, :D].reshape(blocks, TOK_DEV, HEADS, HEAD_DIM)
        key = qkv[:, D:2 * D].reshape(blocks, TOK_DEV, HEADS, HEAD_DIM)
        value = qkv[:, 2 * D:].reshape(blocks, TOK_DEV, HEADS, HEAD_DIM)
        ql = low(rotate(query, cosine, sine))
        kl = low(rotate(key, cosine, sine))
        vl = low(value)
        scores = low_back(jnp.einsum('bqhd,bkhd->bhqk', ql, kl, precision=lax.Precision.HIGHEST) * scale)
        masked = jnp.where(allowed[:, None], scores, -1e+30)
        shifted = jnp.exp(masked - lax.optimization_barrier(jnp.max(masked, -1, keepdims=True)))
        probs = low(shifted / lax.optimization_barrier(jnp.sum(shifted, -1, keepdims=True)))
        attended = jnp.einsum('bhqk,bkhd->bqhd', probs, vl, precision=lax.Precision.HIGHEST).reshape(blocks * TOK_DEV, D)
        attended = low(low_back(attended))
        branch_attn = product(attended, wout) + bout
        hidden = low_back(product(h2, wup) + bup)
        active = low(jax.nn.gelu(hidden, approximate=False))
        branch_ff = product(active, wdown) + bdown
        return xf + branch_attn + branch_ff
    params = [p.astype(jnp.float32) for p in (ln1_gain, ln1_bias, ln2_gain, ln2_bias, qkv_weight, qkv_bias, out_weight, out_bias, up_weight, up_bias, down_weight, down_bias)]
    result, pull = jax.vjp(forward, tokens.astype(jnp.float32), *params)
    grads = pull(cotangent.astype(jnp.float32))
    return (result.astype(jnp.bfloat16), grads[0], grads[1], grads[2], grads[3], grads[4], grads[5], grads[6], grads[7], grads[8], grads[9], grads[10], grads[11], grads[12])
```

```python
import math

import jax
import jax.numpy as jnp
from jax import lax
from jax.sharding import PartitionSpec as P

HEADS = 8
ROT = 64
EPS = 1e-05
f32 = jnp.float32
bf16 = jnp.bfloat16
BOTH = ("rep", "shard")
SIZES = (4, 2, 2, 2, 4)


def coords():
    for y in range(4):
        for h in range(2):
            for c in range(2):
                for l in range(2):
                    for x in range(4):
                        yield (y, h, c, l, x)


def linear(t):
    y, h, c, l, x = (v % m for v, m in zip(t, SIZES))
    return ((y * 2 + h) * 2 + c) * 8 + l * 4 + x


def move(value, y=0, h=0, c=0, l=0, x=0):
    step = (y, h, c, l, x)
    pairs = [(linear(t), linear(tuple(a + b for a, b in zip(t, step)))) for t in coords()]
    return lax.ppermute(value, BOTH, pairs)


def pick(value, index, axis):
    return lax.dynamic_index_in_dim(value, index, axis, keepdims=False)


def ring_gather(own, axis, cut):
    below = move(own, **{axis: 1})
    above = move(own, **{axis: -1})
    far_low = move(below[:cut], **{axis: 1})
    far_high = move(above[cut:], **{axis: -1})
    return [own, above, jnp.concatenate([far_low, far_high], 0), below]


def ring_reduce(pieces, axis, cut):
    own, above, far, below = pieces
    low = move(far[:cut].astype(bf16), **{axis: 1})
    high = move(far[cut:].astype(bf16), **{axis: -1})
    up = jnp.concatenate([above[:cut].astype(f32) + low.astype(f32), above[cut:].astype(f32)], 0)
    down = jnp.concatenate([below[:cut].astype(f32), below[cut:].astype(f32) + high.astype(f32)], 0)
    from_below = move(up.astype(bf16), **{axis: 1})
    from_above = move(down.astype(bf16), **{axis: -1})
    return own.astype(f32) + from_below.astype(f32) + from_above.astype(f32)


def group_gather(own, cut):
    other = move(own, l=1)
    return ring_gather(own, "x", cut) + ring_gather(other, "x", cut)


def group_reduce(pieces, cut):
    other = ring_reduce(pieces[4:], "x", cut)
    crossed = move(other.astype(bf16), l=1)
    return ring_reduce(pieces[:4], "x", cut) + crossed.astype(f32)


def place(pieces, start, count, axis):
    full = jnp.stack(pieces + pieces[:-1], axis)
    return lax.dynamic_slice_in_dim(full, (count - start) % count, count, axis)


def rotate(value, cosine, sine):
    half = ROT // 2
    first = value[..., :half]
    second = value[..., half:ROT]
    return jnp.concatenate(
        [first * cosine - second * sine, second * cosine + first * sine, value[..., ROT:]], -1
    )


def gelu_slope(hidden):
    normal_cdf = 0.5 * (1.0 + jax.scipy.special.erf(hidden / math.sqrt(2.0)))
    normal_pdf = jnp.exp(-0.5 * hidden * hidden) / math.sqrt(2.0 * math.pi)
    return normal_cdf + hidden * normal_pdf


def dot(a, b, ca=1, cb=0):
    return lax.dot_general(a, b, (((ca,), (cb,)), ((), ())), preferred_element_type=f32)


def normalize(value):
    xf = value.astype(f32)
    centre = xf - jnp.mean(xf, -1, keepdims=True)
    inverse = lax.rsqrt(jnp.mean(centre * centre, -1, keepdims=True) + EPS)
    return centre * inverse, inverse


def local(
    tokens,
    doc_lengths,
    cotangent,
    ln1_gain,
    ln1_bias,
    ln2_gain,
    ln2_bias,
    qkv_weight,
    qkv_bias,
    out_weight,
    out_bias,
    up_weight,
    up_bias,
    down_weight,
    down_bias,
):
    rows, width = tokens.shape
    head = width // HEADS
    scale = head ** (-0.5)
    group = 8
    rep = lax.axis_index("rep")
    shard = lax.axis_index("shard")
    y, h, c = rep // 4, (rep // 2) % 2, rep % 2
    l, x = shard // 4, shard % 4
    ff = up_bias.shape[0]

    part = lax.dynamic_slice_in_dim(qkv_weight, y * 64 + c * 32, 32, 0).reshape(32, 3, 8, head)
    part_up = lax.dynamic_slice_in_dim(up_weight, y * 64 + c * 32, 32, 0).reshape(32, 8, ff)
    part = jnp.concatenate(
        [part.transpose(2, 0, 1, 3).reshape(8, 32, 3 * head), part_up.transpose(1, 0, 2)], -1
    )
    cols = part.shape[-1]
    part = lax.all_to_all(part, "shard", 0, 0)
    ring = ring_gather(part, "y", 4)
    mine = place(ring, y, 4, 1)
    yours = move(mine, c=1)
    w_mixed = jnp.where(
        c == 0, jnp.stack([mine, yours], 2), jnp.stack([yours, mine], 2)
    ).reshape(width, cols)
    w_qkv = w_mixed[:, : 3 * head]
    w_up = w_mixed[:, 3 * head :]

    small = jnp.concatenate(
        [ln1_gain, ln1_bias, ln2_gain, ln2_bias, qkv_bias, doc_lengths[0].astype(bf16)]
    )
    small = jnp.pad(small[None], ((0, 7), (0, width - small.shape[0])))
    pieces = group_gather(jnp.concatenate([tokens, small], 0), 72)
    x_all = jnp.concatenate([p[:rows] for p in pieces], 0)
    infos = jnp.stack([p[rows] for p in pieces], 0)
    dy_all = jnp.concatenate(group_gather(cotangent, 64), 0)

    spots = jnp.arange(8)
    wanted = ((spots // 4) ^ l) * 4 + (spots % 4 - x) % 4
    chosen = (wanted[:, None] == spots[None, :]).astype(bf16)
    ordered = dot(chosen, infos)
    gains = ordered[:, :1024].reshape(8, 4, 256).transpose(1, 0, 2).reshape(4, width)
    g1, b1, g2, b2 = gains[0], gains[1], gains[2], gains[3]
    qkv_b = ordered[:, 1024:1792].reshape(3, 8, head)
    qkv_b = pick(qkv_b, shard, 1).reshape(3 * head)
    lengths = infos[:, 1792:1795].astype(jnp.int32)

    ends = jnp.cumsum(lengths, 1)
    starts = ends - lengths
    steps_t = jnp.arange(rows, dtype=jnp.int32)
    segment = jnp.sum((steps_t[None, :, None] >= ends[:, None, :]).astype(jnp.int32), -1)
    slots = jnp.arange(lengths.shape[1], dtype=jnp.int32)
    begin = jnp.sum(
        jnp.where(segment[:, :, None] == slots[None, None, :], starts[:, None, :], 0), -1
    )
    position = (steps_t[None, :] - begin).astype(f32)
    freq = 10000.0 ** (-2.0 * jnp.arange(ROT // 2, dtype=f32) / ROT)
    angle = position[:, :, None] * freq[None, None, :]
    cosine = jnp.cos(angle)
    sine = jnp.sin(angle)
    allowed = (segment[:, :, None] == segment[:, None, :]) & (
        steps_t[None, None, :] <= steps_t[None, :, None]
    )

    normed, _ = normalize(x_all)
    h1 = (normed * g1 + b1).astype(bf16)
    h2 = (normed * g2 + b2).astype(bf16)

    hidden = dot(h2, w_up) + up_bias.astype(f32)
    active = jax.nn.gelu(hidden, approximate=False).astype(bf16)
    qkv = (dot(h1, w_qkv) + qkv_b).reshape(group, rows, 3 * head)
    ql = rotate(qkv[..., :head], cosine, sine).astype(bf16)
    kl = rotate(qkv[..., head : 2 * head], cosine, sine).astype(bf16)
    vl = qkv[..., 2 * head :].astype(bf16)
    scores = jnp.einsum("bqd,bkd->bqk", ql, kl, preferred_element_type=f32) * scale
    masked = jnp.where(allowed, scores, -1e30)
    shifted = jnp.exp(masked - jnp.max(masked, -1, keepdims=True))
    probs = shifted / jnp.sum(shifted, -1, keepdims=True)
    probs_low = probs.astype(bf16)
    attended = (
        jnp.einsum("bqk,bkd->bqd", probs_low, vl, preferred_element_type=f32)
        .astype(bf16)
        .reshape(group * rows, head)
    )
    both_bias = (out_bias.astype(f32) + down_bias.astype(f32))[None, :]
    wide_bias = lax.dynamic_update_slice(jnp.zeros((1, width), f32), both_bias, (0, shard * 256))
    mix = dot(attended, out_weight) + dot(active, down_weight) + wide_bias
    mix = mix.astype(bf16).reshape(group, rows, width)
    mixed = group_reduce([mix[k] for k in range(group)], 64)
    mixed = (tokens.astype(f32) + mixed).astype(bf16)

    d_down_w = dot(active, dy_all, 0, 0)
    d_out_w = dot(attended, dy_all, 0, 0)
    d_active = dot(dy_all, down_weight, 1, 1)
    d_hidden = (d_active * gelu_slope(hidden)).astype(bf16)
    d_up_w = dot(h2, d_hidden, 0, 0)
    d_attended = dot(dy_all, out_weight, 1, 1).astype(bf16).reshape(group, rows, head)
    d_value = jnp.einsum("bqk,bqd->bkd", probs_low, d_attended, preferred_element_type=f32)
    d_probs = jnp.einsum("bqd,bkd->bqk", d_attended, vl, preferred_element_type=f32)
    centred = d_probs - jnp.sum(d_probs * probs, -1, keepdims=True)
    d_scores = (probs * centred).astype(bf16)
    d_query = jnp.einsum("bqk,bkd->bqd", d_scores, kl, preferred_element_type=f32) * scale
    d_key = jnp.einsum("bqk,bqd->bkd", d_scores, ql, preferred_element_type=f32) * scale
    d_query = rotate(d_query, cosine, -sine)
    d_key = rotate(d_key, cosine, -sine)
    d_qkv = (
        jnp.concatenate([d_query, d_key, d_value], -1).astype(bf16).reshape(group * rows, 3 * head)
    )
    d_qkv_w = dot(h1, d_qkv, 0, 0)
    d_h1 = dot(d_qkv, w_qkv, 1, 1)
    d_h2 = dot(d_hidden, w_up, 1, 1)
    sums = (d_h1 * g1 + d_h2 * g2).astype(bf16).reshape(group, rows, width)
    own_sum = group_reduce([sums[k] for k in range(group)], 64)
    own_normed, own_inverse = normalize(tokens)
    tokens_grad = cotangent.astype(f32) + own_inverse * (
        own_sum
        - jnp.mean(own_sum, -1, keepdims=True)
        - own_normed * jnp.mean(own_sum * own_normed, -1, keepdims=True)
    )

    dy_sum = jnp.sum(dy_all.astype(f32), 0)
    dy_own = lax.dynamic_slice_in_dim(dy_sum, shard * 256, 256)
    up_b = jnp.sum(d_hidden.astype(f32), 0)
    qkv_bg = jnp.sum(d_qkv.astype(f32), 0).reshape(3, 1, head)
    wide_qkv = lax.dynamic_update_slice(jnp.zeros((3, 8, head), f32), qkv_bg, (0, shard, 0))
    wide_up = lax.dynamic_update_slice(jnp.zeros((8 * ff,), f32), up_b, (shard * ff,))
    wide_dy = lax.dynamic_update_slice(jnp.zeros((width,), f32), dy_own, (shard * 256,))
    smalls = lax.psum(
        jnp.concatenate(
            [
                jnp.sum(d_h1 * normed, 0),
                jnp.sum(d_h1, 0),
                jnp.sum(d_h2 * normed, 0),
                jnp.sum(d_h2, 0),
                wide_dy,
                wide_qkv.reshape(-1),
                wide_up,
            ]
        ).reshape(-1, 256),
        BOTH,
    ).reshape(-1)

    def small_at(start, size):
        return lax.dynamic_slice_in_dim(smalls, start + shard * size, size)

    def sum_rep(grad, axis, first):
        away = pick(grad, 1 - c, axis + 2).astype(bf16)
        kept = pick(grad, c, axis + 2) + move(away, c=1).astype(f32)
        for name in first:
            if name == "y":
                parts = [pick(kept, (y + k) % 4, axis) for k in range(4)]
                kept = ring_reduce(parts, "y", parts[0].shape[0] // 2)
            else:
                at = axis if first == "yh" else axis + 1
                away = pick(kept, 1 - h, at).astype(bf16)
                kept = pick(kept, h, at) + move(away, h=1).astype(f32)
        return kept.astype(bf16)

    def gather_rep(chunk, first):
        got = chunk
        for name in reversed(first):
            if name == "y":
                got = place(ring_gather(got, "y", got.shape[0] // 2), y, 4, 0)
            else:
                other = move(got, h=1)
                got = jnp.where(h == 0, jnp.stack([got, other]), jnp.stack([other, got]))
        if first == "hy":
            got = got.swapaxes(0, 1)
        other = move(got, c=1)
        return jnp.where(c == 0, jnp.stack([got, other], 2), jnp.stack([other, got], 2))

    late = jnp.concatenate([d_down_w.reshape(4, 2, 2, -1, width), d_out_w.reshape(4, 2, 2, -1, width)], 3)
    late = late.transpose(3, 0, 1, 2, 4)
    late = gather_rep(sum_rep(late, 1, "hy"), "hy").astype(f32)
    down_rows = down_weight.shape[0] // 16
    down_grad = late[:, :, :, :down_rows].reshape(down_weight.shape)
    out_grad = late[:, :, :, down_rows:].reshape(out_weight.shape)

    wide = jnp.concatenate([d_qkv_w, d_up_w], 1).reshape(8, 4, 2, 2, 16, cols)
    wide = sum_rep(wide, 1, "yh")
    wide = lax.all_to_all(wide, "shard", 0, 0).transpose(1, 0, 2)
    wide = gather_rep(wide, "yh").astype(f32).reshape(256, 8, cols)
    qkv_grad = wide[:, :, : 3 * head].reshape(256, 8, 3, head).transpose(0, 2, 1, 3)
    qkv_grad = qkv_grad.reshape(256, 3 * width)
    up_grad = wide[:, :, 3 * head :].reshape(256, 8 * ff)

    dy_total = small_at(4 * width, 256)
    return (
        mixed,
        tokens_grad,
        small_at(0, 256),
        small_at(width, 256),
        small_at(2 * width, 256),
        small_at(3 * width, 256),
        qkv_grad,
        small_at(5 * width, 768),
        out_grad,
        dy_total,
        up_grad,
        small_at(8 * width, ff),
        down_grad,
        dy_total,
    )


def solution(mesh):
    rows = P(BOTH, None)
    vector, matrix = P("shard"), P("shard", None)
    return jax.shard_map(
        local,
        mesh=mesh,
        in_specs=(rows, rows, rows, vector, vector, vector, vector)
        + (matrix, vector, matrix, vector, matrix, vector, matrix, vector),
        out_specs=(rows, rows, vector, vector, vector, vector)
        + (matrix, vector, matrix, vector, matrix, vector, matrix, vector),
        check_vma=False,
    )
```

```python
import math

import jax
import jax.numpy as jnp
from jax import lax
from jax.experimental import pallas as pl
from jax.experimental.pallas import tpu as pltpu
from jax.sharding import PartitionSpec as P

HEADS = 8
ROT = 64
EPS = 1e-05
f32 = jnp.float32
bf16 = jnp.bfloat16
BOTH = ("rep", "shard")
SIZES = (4, 2, 2, 2, 4)


def coords():
    for y in range(4):
        for h in range(2):
            for c in range(2):
                for l in range(2):
                    for x in range(4):
                        yield (y, h, c, l, x)


def linear(t):
    y, h, c, l, x = (v % m for v, m in zip(t, SIZES))
    return ((y * 2 + h) * 2 + c) * 8 + l * 4 + x


def move(value, y=0, h=0, c=0, l=0, x=0):
    step = (y, h, c, l, x)
    pairs = [(linear(t), linear(tuple(a + b for a, b in zip(t, step)))) for t in coords()]
    return lax.ppermute(value, BOTH, pairs)


def swap(value, axis, bit):
    at = "yhclx".index(axis)
    pairs = [(linear(t), linear(t[:at] + (t[at] ^ bit,) + t[at + 1 :])) for t in coords()]
    return lax.ppermute(value, BOTH, pairs)


def pick(value, index, axis):
    return lax.dynamic_index_in_dim(value, index, axis, keepdims=False)


def ring_gather(own, axis, cut):
    below = move(own, **{axis: 1})
    above = move(own, **{axis: -1})
    far_low = move(below[:cut], **{axis: 1})
    far_high = move(above[cut:], **{axis: -1})
    return [own, above, jnp.concatenate([far_low, far_high], 0), below]


def ring_reduce(pieces, axis, cut):
    own, above, far, below = pieces
    low = move(far[:cut].astype(bf16), **{axis: 1})
    high = move(far[cut:].astype(bf16), **{axis: -1})
    up = jnp.concatenate([above[:cut].astype(f32) + low.astype(f32), above[cut:].astype(f32)], 0)
    down = jnp.concatenate([below[:cut].astype(f32), below[cut:].astype(f32) + high.astype(f32)], 0)
    from_below = move(up.astype(bf16), **{axis: 1})
    from_above = move(down.astype(bf16), **{axis: -1})
    return own.astype(f32) + from_below.astype(f32) + from_above.astype(f32)


def group_gather(own, cut):
    other = move(own, l=1)
    return ring_gather(own, "x", cut) + ring_gather(other, "x", cut)


def group_reduce(pieces, cut):
    other = ring_reduce(pieces[4:], "x", cut)
    crossed = move(other.astype(bf16), l=1)
    return ring_reduce(pieces[:4], "x", cut) + crossed.astype(f32)


def place(pieces, start, count, axis):
    full = jnp.stack(pieces + pieces[:-1], axis)
    return lax.dynamic_slice_in_dim(full, (count - start) % count, count, axis)


def rotate(value, cosine, sine):
    half = ROT // 2
    first = value[..., :half]
    second = value[..., half:ROT]
    return jnp.concatenate(
        [first * cosine - second * sine, second * cosine + first * sine, value[..., ROT:]], -1
    )


def gelu_slope(hidden):
    normal_cdf = 0.5 * (1.0 + jax.scipy.special.erf(hidden / math.sqrt(2.0)))
    normal_pdf = jnp.exp(-0.5 * hidden * hidden) / math.sqrt(2.0 * math.pi)
    return normal_cdf + hidden * normal_pdf


def dot(a, b, ca=1, cb=0):
    return lax.dot_general(a, b, (((ca,), (cb,)), ((), ())), preferred_element_type=f32)


def normalize(value):
    xf = value.astype(f32)
    centre = xf - jnp.mean(xf, -1, keepdims=True)
    inverse = lax.rsqrt(jnp.mean(centre * centre, -1, keepdims=True) + EPS)
    return centre * inverse, inverse


def kernel_params():
    return pltpu.CompilerParams(vmem_limit_bytes=48 * 1024 * 1024)


def dot_rows(a, b):
    return lax.dot_general(a, b, (((0,), (0,)), ((), ())), preferred_element_type=f32)


def sorted_weight(mine, yours, spots):
    sources, rows, cols = mine.shape[1:]

    def body(spot_ref, mine_ref, yours_ref, out_ref):
        step = pl.program_id(0)

        @pl.when(step < 4)
        def _():
            out_ref[:, 0] = mine_ref[0]

        @pl.when(step >= 4)
        def _():
            out_ref[:, 0] = yours_ref[0]

    block = (1, sources, rows, cols)
    return pl.pallas_call(
        body,
        out_shape=jax.ShapeDtypeStruct((sources, 8, rows, cols), bf16),
        grid_spec=pltpu.PrefetchScalarGridSpec(
            num_scalar_prefetch=1,
            grid=(8,),
            in_specs=[
                pl.BlockSpec(block, lambda i, spot: (jnp.minimum(i, 3), 0, 0, 0)),
                pl.BlockSpec(block, lambda i, spot: (jnp.maximum(i - 4, 0), 0, 0, 0)),
            ],
            out_specs=pl.BlockSpec(
                (sources, 1, rows, cols), lambda i, spot: (0, spot[i], 0, 0)
            ),
        ),
        compiler_params=kernel_params(),
        cost_estimate=pl.CostEstimate(flops=0, bytes_accessed=16 * 1024 * 1024, transcendentals=0),
        name="sorted_weight",
    )(spots, mine, yours).reshape(sources * 8 * rows, cols)


def late_grads(active, attended, dy, core):
    width = dy.shape[1]

    def body(core_ref, act_ref, ol_ref, dy_ref, keep_ref, send_ref):
        step = pl.program_id(0)
        first = core_ref[0] == 0

        @pl.when(step < 4)
        def _():
            part = dot_rows(act_ref[...], dy_ref[...]).astype(bf16).reshape(2, 2, 64, width)
            at = pl.ds(step * 2, 2)

            @pl.when(first)
            def _():
                keep_ref[at, 0:64] = part[:, 0]
                send_ref[at, 0:64] = part[:, 1]

            @pl.when(jnp.logical_not(first))
            def _():
                keep_ref[at, 0:64] = part[:, 1]
                send_ref[at, 0:64] = part[:, 0]

        @pl.when(step == 4)
        def _():
            part = dot_rows(ol_ref[...], dy_ref[...]).astype(bf16).reshape(8, 2, 16, width)

            @pl.when(first)
            def _():
                keep_ref[:, 64:80] = part[:, 0]
                send_ref[:, 64:80] = part[:, 1]

            @pl.when(jnp.logical_not(first))
            def _():
                keep_ref[:, 64:80] = part[:, 1]
                send_ref[:, 64:80] = part[:, 0]

    rows = dy.shape[0]
    out = jax.ShapeDtypeStruct((8, 80, width), bf16)
    whole = pl.BlockSpec((8, 80, width), lambda i, core: (0, 0, 0))
    keep, send = pl.pallas_call(
        body,
        out_shape=(out, out),
        grid_spec=pltpu.PrefetchScalarGridSpec(
            num_scalar_prefetch=1,
            grid=(5,),
            in_specs=[
                pl.BlockSpec((rows, 256), lambda i, core: (0, jnp.minimum(i, 3))),
                pl.BlockSpec((rows, 256), lambda i, core: (0, 0)),
                pl.BlockSpec((rows, width), lambda i, core: (0, 0)),
            ],
            out_specs=(whole, whole),
        ),
        compiler_params=kernel_params(),
        cost_estimate=pl.CostEstimate(
            flops=2 * rows * 1280 * width, bytes_accessed=12 * 1024 * 1024, transcendentals=0
        ),
        name="late_grads",
    )(core, active, attended, dy)
    return keep.reshape(4, 2, 80, width), send.reshape(4, 2, 80, width)


def early_grads(h1, h2, d_qkv, d_hidden, core):
    rows, width = h1.shape
    n1, n2 = d_qkv.shape[1], d_hidden.shape[1]

    def body(core_ref, h1_ref, h2_ref, dq_ref, du_ref, keep_ref, send_ref):
        first = core_ref[0] == 0
        left = dot_rows(h1_ref[...], dq_ref[...]).astype(bf16).reshape(8, 2, 16, n1)
        right = dot_rows(h2_ref[...], du_ref[...]).astype(bf16).reshape(8, 2, 16, n2)

        @pl.when(first)
        def _():
            keep_ref[0, :, :, 0:n1] = left[:, 0]
            keep_ref[0, :, :, n1:] = right[:, 0]
            send_ref[0, :, :, 0:n1] = left[:, 1]
            send_ref[0, :, :, n1:] = right[:, 1]

        @pl.when(jnp.logical_not(first))
        def _():
            keep_ref[0, :, :, 0:n1] = left[:, 1]
            keep_ref[0, :, :, n1:] = right[:, 1]
            send_ref[0, :, :, 0:n1] = left[:, 0]
            send_ref[0, :, :, n1:] = right[:, 0]

    out = jax.ShapeDtypeStruct((8, 8, 16, n1 + n2), bf16)
    block = pl.BlockSpec((1, 8, 16, n1 + n2), lambda i, core: (i, 0, 0, 0))
    keep, send = pl.pallas_call(
        body,
        out_shape=(out, out),
        grid_spec=pltpu.PrefetchScalarGridSpec(
            num_scalar_prefetch=1,
            grid=(8,),
            in_specs=[
                pl.BlockSpec((rows, width // 8), lambda i, core: (0, i)),
                pl.BlockSpec((rows, width // 8), lambda i, core: (0, i)),
                pl.BlockSpec((rows, n1), lambda i, core: (0, 0)),
                pl.BlockSpec((rows, n2), lambda i, core: (0, 0)),
            ],
            out_specs=(block, block),
        ),
        compiler_params=kernel_params(),
        cost_estimate=pl.CostEstimate(
            flops=2 * rows * width * (n1 + n2), bytes_accessed=20 * 1024 * 1024, transcendentals=0
        ),
        name="early_grads",
    )(core, h1, h2, d_qkv, d_hidden)
    return keep.reshape(8, 4, 2, 16, n1 + n2), send.reshape(8, 4, 2, 16, n1 + n2)


def late_outputs(groups, spots):
    width = groups[0].shape[-1]

    def body(spot_ref, *refs):
        ins, down_ref, out_ref = refs[:4], refs[4], refs[5]
        step = pl.program_id(0)
        for at, ref in enumerate(ins):

            @pl.when(step // 4 == at)
            def _(ref=ref):
                down_ref[...] = ref[0, 0:64].astype(f32)
                out_ref[...] = ref[0, 64:80].astype(f32)

    def chosen(at):
        return pl.BlockSpec(
            (1, 80, width), lambda i, spot: (jnp.clip(i - 4 * at, 0, 3), 0, 0)
        )

    return pl.pallas_call(
        body,
        out_shape=(
            jax.ShapeDtypeStruct((1024, width), f32),
            jax.ShapeDtypeStruct((256, width), f32),
        ),
        grid_spec=pltpu.PrefetchScalarGridSpec(
            num_scalar_prefetch=1,
            grid=(16,),
            in_specs=[chosen(at) for at in range(4)],
            out_specs=(
                pl.BlockSpec((64, width), lambda i, spot: (spot[i], 0)),
                pl.BlockSpec((16, width), lambda i, spot: (spot[i], 0)),
            ),
        ),
        compiler_params=kernel_params(),
        cost_estimate=pl.CostEstimate(flops=0, bytes_accessed=16 * 1024 * 1024, transcendentals=0),
        name="late_outputs",
    )(spots, *groups)


def early_outputs(mine, yours, spots, n1):
    cols = mine.shape[-1]
    n2 = cols - n1
    head = n1 // 3

    def body(spot_ref, mine_ref, yours_ref, qkv_ref, up_ref):
        step = pl.program_id(0)

        def put(ref):
            for source in range(8):
                for third in range(3):
                    at = (third * 8 + source) * head
                    qkv_ref[:, at : at + head] = ref[
                        0, source, :, third * head : (third + 1) * head
                    ].astype(f32)
                up_ref[:, source * n2 : (source + 1) * n2] = ref[0, source, :, n1:].astype(f32)

        @pl.when(step < 8)
        def _():
            put(mine_ref)

        @pl.when(step >= 8)
        def _():
            put(yours_ref)

    block = (1, 8, 16, cols)
    return pl.pallas_call(
        body,
        out_shape=(
            jax.ShapeDtypeStruct((256, 8 * n1), f32),
            jax.ShapeDtypeStruct((256, 8 * n2), f32),
        ),
        grid_spec=pltpu.PrefetchScalarGridSpec(
            num_scalar_prefetch=1,
            grid=(16,),
            in_specs=[
                pl.BlockSpec(block, lambda i, spot: (jnp.minimum(i, 7), 0, 0, 0)),
                pl.BlockSpec(block, lambda i, spot: (jnp.maximum(i - 8, 0), 0, 0, 0)),
            ],
            out_specs=(
                pl.BlockSpec((16, 8 * n1), lambda i, spot: (spot[i], 0)),
                pl.BlockSpec((16, 8 * n2), lambda i, spot: (spot[i], 0)),
            ),
        ),
        compiler_params=kernel_params(),
        cost_estimate=pl.CostEstimate(flops=0, bytes_accessed=24 * 1024 * 1024, transcendentals=0),
        name="early_outputs",
    )(spots, mine, yours)


def local(
    tokens,
    doc_lengths,
    cotangent,
    ln1_gain,
    ln1_bias,
    ln2_gain,
    ln2_bias,
    qkv_weight,
    qkv_bias,
    out_weight,
    out_bias,
    up_weight,
    up_bias,
    down_weight,
    down_bias,
):
    rows, width = tokens.shape
    head = width // HEADS
    scale = head ** (-0.5)
    group = 8
    rep = lax.axis_index("rep")
    shard = lax.axis_index("shard")
    y, h, c = rep // 4, (rep // 2) % 2, rep % 2
    l, x = shard // 4, shard % 4
    ff = up_bias.shape[0]

    cols = 3 * head + ff
    part = lax.dynamic_slice_in_dim(qkv_weight, y * 64 + c * 32, 32, 0).reshape(32, 3, 8, head)
    part_up = lax.dynamic_slice_in_dim(up_weight, y * 64 + c * 32, 32, 0).reshape(32, 8, ff)
    small = jnp.concatenate([ln1_gain, ln1_bias, ln2_gain, ln2_bias, qkv_bias])
    size = jnp.pad(doc_lengths[0].astype(bf16), (0, cols - doc_lengths.shape[1]))
    small = jnp.pad(jnp.stack([small, size]), ((0, 6), (0, 0)))
    part = jnp.concatenate(
        [part.transpose(2, 0, 1, 3).reshape(8, 32, 3 * head), part_up.transpose(1, 0, 2)], -1
    )
    part = jnp.concatenate([part, jnp.broadcast_to(small[None], (8, 8, cols))], 1)
    part = lax.all_to_all(part, "shard", 0, 0)
    infos = part[:, 32:34]
    mine = jnp.stack(ring_gather(part[:, :32], "y", 4))
    yours = move(mine, c=1)
    steps4 = (y + jnp.arange(4)) % 4
    spots = jnp.concatenate([steps4 * 2 + c, steps4 * 2 + 1 - c]).astype(jnp.int32)
    w_mixed = sorted_weight(mine, yours, spots)
    w_qkv = w_mixed[:, : 3 * head]
    w_up = w_mixed[:, 3 * head :]

    x_all = jnp.concatenate(group_gather(tokens, 64), 0)
    dy_all = jnp.concatenate(group_gather(cotangent, 64), 0)

    gains = infos[:, 0, :1024].reshape(8, 4, 256).transpose(1, 0, 2).reshape(4, width).astype(f32)
    g1, b1, g2, b2 = gains[0], gains[1], gains[2], gains[3]
    qkv_b = infos[:, 0, 1024:].astype(f32).reshape(8 * 3, head)
    qkv_b = jnp.concatenate(
        [lax.dynamic_index_in_dim(qkv_b, third * 8 + shard, 0, False) for third in range(3)]
    )
    steps8 = jnp.arange(8)
    sources = ((steps8 // 4) ^ l) * 4 + (x + steps8 % 4) % 4
    lengths = infos[:, 1, :3].astype(f32)
    lengths = jnp.sum(
        jnp.where(sources[:, None, None] == steps8[None, :, None], lengths[None], 0.0), 1
    ).astype(jnp.int32)

    ends = jnp.cumsum(lengths, 1)
    starts = ends - lengths
    steps_t = jnp.arange(rows, dtype=jnp.int32)
    segment = jnp.sum((steps_t[None, :, None] >= ends[:, None, :]).astype(jnp.int32), -1)
    slots = jnp.arange(lengths.shape[1], dtype=jnp.int32)
    begin = jnp.sum(
        jnp.where(segment[:, :, None] == slots[None, None, :], starts[:, None, :], 0), -1
    )
    position = (steps_t[None, :] - begin).astype(f32)
    freq = 10000.0 ** (-2.0 * jnp.arange(ROT // 2, dtype=f32) / ROT)
    angle = position[:, :, None] * freq[None, None, :]
    cosine = jnp.cos(angle)
    sine = jnp.sin(angle)
    allowed = (segment[:, :, None] == segment[:, None, :]) & (
        steps_t[None, None, :] <= steps_t[None, :, None]
    )

    normed, _ = normalize(x_all)
    h1 = (normed * g1 + b1).astype(bf16)
    h2 = (normed * g2 + b2).astype(bf16)

    hidden = dot(h2, w_up) + up_bias.astype(f32)
    active = jax.nn.gelu(hidden, approximate=False).astype(bf16)
    qkv = (dot(h1, w_qkv) + qkv_b).reshape(group, rows, 3 * head)
    ql = rotate(qkv[..., :head], cosine, sine).astype(bf16)
    kl = rotate(qkv[..., head : 2 * head], cosine, sine).astype(bf16)
    vl = qkv[..., 2 * head :].astype(bf16)
    scores = jnp.einsum("bqd,bkd->bqk", ql, kl, preferred_element_type=f32) * scale
    masked = jnp.where(allowed, scores, -1e30)
    shifted = jnp.exp(masked - jnp.max(masked, -1, keepdims=True))
    probs = shifted / jnp.sum(shifted, -1, keepdims=True)
    probs_low = probs.astype(bf16)
    attended = (
        jnp.einsum("bqk,bkd->bqd", probs_low, vl, preferred_element_type=f32)
        .astype(bf16)
        .reshape(group * rows, head)
    )
    both_bias = (out_bias.astype(f32) + down_bias.astype(f32))[None, :]
    wide_bias = lax.dynamic_update_slice(jnp.zeros((1, width), f32), both_bias, (0, shard * 256))
    mix = dot(attended, out_weight) + dot(active, down_weight) + wide_bias
    mix = mix.astype(bf16).reshape(group, rows, width)
    mixed = group_reduce([mix[k] for k in range(group)], 64)
    mixed = (tokens.astype(f32) + mixed).astype(bf16)

    core = c.astype(jnp.int32).reshape(1)
    late_keep, late_send = late_grads(active, attended, dy_all, core)
    d_active = dot(dy_all, down_weight, 1, 1)
    d_hidden = (d_active * gelu_slope(hidden)).astype(bf16)
    d_attended = dot(dy_all, out_weight, 1, 1).astype(bf16).reshape(group, rows, head)
    d_value = jnp.einsum("bqk,bqd->bkd", probs_low, d_attended, preferred_element_type=f32)
    d_probs = jnp.einsum("bqd,bkd->bqk", d_attended, vl, preferred_element_type=f32)
    centred = d_probs - jnp.sum(d_probs * probs, -1, keepdims=True)
    d_scores = (probs * centred).astype(bf16)
    d_query = jnp.einsum("bqk,bkd->bqd", d_scores, kl, preferred_element_type=f32) * scale
    d_key = jnp.einsum("bqk,bqd->bkd", d_scores, ql, preferred_element_type=f32) * scale
    d_query = rotate(d_query, cosine, -sine)
    d_key = rotate(d_key, cosine, -sine)
    d_qkv = (
        jnp.concatenate([d_query, d_key, d_value], -1).astype(bf16).reshape(group * rows, 3 * head)
    )
    early_keep, early_send = early_grads(h1, h2, d_qkv, d_hidden, core)
    d_h1 = dot(d_qkv, w_qkv, 1, 1)
    d_h2 = dot(d_hidden, w_up, 1, 1)
    sums = (d_h1 * g1 + d_h2 * g2).astype(bf16).reshape(group, rows, width)
    own_sum = group_reduce([sums[k] for k in range(group)], 64)
    own_normed, own_inverse = normalize(tokens)
    tokens_grad = cotangent.astype(f32) + own_inverse * (
        own_sum
        - jnp.mean(own_sum, -1, keepdims=True)
        - own_normed * jnp.mean(own_sum * own_normed, -1, keepdims=True)
    )

    dy_sum = jnp.sum(dy_all.astype(f32), 0)
    dy_own = lax.dynamic_slice_in_dim(dy_sum, shard * 256, 256)
    up_b = jnp.sum(d_hidden.astype(f32), 0)
    qkv_bg = jnp.sum(d_qkv.astype(f32), 0).reshape(3, 1, head)
    wide_qkv = lax.dynamic_update_slice(jnp.zeros((3, 8, head), f32), qkv_bg, (0, shard, 0))
    wide_up = lax.dynamic_update_slice(jnp.zeros((8 * ff,), f32), up_b, (shard * ff,))
    wide_dy = lax.dynamic_update_slice(jnp.zeros((width,), f32), dy_own, (shard * 256,))
    smalls = jnp.concatenate(
        [
            jnp.sum(d_h1 * normed, 0),
            jnp.sum(d_h1, 0),
            jnp.sum(d_h2 * normed, 0),
            jnp.sum(d_h2, 0),
            wide_dy,
            wide_qkv.reshape(-1),
            wide_up,
        ]
    )
    smalls = smalls.reshape(-1, 1024)
    for axis, bit in (("c", 1), ("l", 1), ("h", 1), ("x", 1), ("y", 1), ("x", 2), ("y", 2)):
        smalls = smalls + swap(smalls, axis, bit)
    smalls = smalls.reshape(-1)

    def small_at(start, size):
        return lax.dynamic_slice_in_dim(smalls, start + shard * size, size)

    got = move(late_send, c=1)

    def late_part(high, index):
        both = [pick(pick(v, high, 1), index, 0).astype(f32) for v in (late_keep, got)]
        return both[0] + both[1]

    away = (pick(late_keep, 1 - h, 1).astype(f32) + pick(got, 1 - h, 1).astype(f32)).astype(bf16)
    crossed = move(away, h=1)
    parts = [late_part(h, (y + k) % 4) + pick(crossed, (y + k) % 4, 0).astype(f32) for k in range(4)]
    late = ring_reduce(parts, "y", 40).astype(bf16)
    late = jnp.stack(ring_gather(late, "y", 40))
    late_h = move(late, h=1)
    late_c = move(late, c=1)
    late_hc = move(late_h, c=1)
    spots = [
        (steps4 * 2 + high) * 2 + low for high, low in ((h, c), (1 - h, c), (h, 1 - c), (1 - h, 1 - c))
    ]
    down_grad, out_grad = late_outputs(
        (late, late_h, late_c, late_hc), jnp.concatenate(spots).astype(jnp.int32)
    )

    got_early = move(early_send, c=1)
    parts = [
        pick(early_keep, (y + k) % 4, 1).astype(f32) + pick(got_early, (y + k) % 4, 1).astype(f32)
        for k in range(4)
    ]
    early = ring_reduce(parts, "y", 4)
    crossed = move(pick(early, 1 - h, 1).astype(bf16), h=1)
    early = (pick(early, h, 1) + crossed.astype(f32)).astype(bf16)
    early = lax.all_to_all(early, "shard", 0, 0)
    early = jnp.stack([early, move(early, h=1)])
    early = jnp.concatenate(ring_gather(early, "y", 1), 0)
    early_c = move(early, c=1)
    spots = [
        ((steps4[:, None] * 2 + jnp.stack([h, 1 - h])[None, :]) * 2 + low).reshape(8)
        for low in (c, 1 - c)
    ]
    qkv_grad, up_grad = early_outputs(
        early, early_c, jnp.concatenate(spots).astype(jnp.int32), 3 * head
    )

    dy_total = small_at(4 * width, 256)
    return (
        mixed,
        tokens_grad,
        small_at(0, 256),
        small_at(width, 256),
        small_at(2 * width, 256),
        small_at(3 * width, 256),
        qkv_grad,
        small_at(5 * width, 768),
        out_grad,
        dy_total,
        up_grad,
        small_at(8 * width, ff),
        down_grad,
        dy_total,
    )


def solution(mesh):
    rows = P(BOTH, None)
    vector, matrix = P("shard"), P("shard", None)
    return jax.shard_map(
        local,
        mesh=mesh,
        in_specs=(rows, rows, rows, vector, vector, vector, vector)
        + (matrix, vector, matrix, vector, matrix, vector, matrix, vector),
        out_specs=(rows, rows, vector, vector, vector, vector)
        + (matrix, vector, matrix, vector, matrix, vector, matrix, vector),
        check_vma=False,
    )
```

```python
import math

import jax
import jax.numpy as jnp
from jax import lax
from jax.experimental import pallas as pl
from jax.experimental.pallas import tpu as pltpu
from jax.sharding import PartitionSpec as P

HEADS = 8
ROT = 64
EPS = 1e-05
f32 = jnp.float32
bf16 = jnp.bfloat16
COST = pl.CostEstimate(flops=1000, bytes_accessed=1000, transcendentals=0)
BOTH = ("rep", "shard")
SIZES = (4, 2, 2, 2, 4)


def coords():
    for y in range(4):
        for h in range(2):
            for c in range(2):
                for l in range(2):
                    for x in range(4):
                        yield (y, h, c, l, x)


def linear(t):
    y, h, c, l, x = (v % m for v, m in zip(t, SIZES))
    return ((y * 2 + h) * 2 + c) * 8 + l * 4 + x


def move(value, y=0, h=0, c=0, l=0, x=0):
    step = (y, h, c, l, x)
    pairs = [(linear(t), linear(tuple(a + b for a, b in zip(t, step)))) for t in coords()]
    return lax.ppermute(value, BOTH, pairs)


def swap(value, axis, bit):
    at = "yhclx".index(axis)
    pairs = [(linear(t), linear(t[:at] + (t[at] ^ bit,) + t[at + 1 :])) for t in coords()]
    return lax.ppermute(value, BOTH, pairs)


def pick(value, index, axis):
    return lax.dynamic_index_in_dim(value, index, axis, keepdims=False)


def ring_gather(own, axis, cut):
    below = move(own, **{axis: 1})
    above = move(own, **{axis: -1})
    far_low = move(below[:cut], **{axis: 1})
    far_high = move(above[cut:], **{axis: -1})
    return [own, above, jnp.concatenate([far_low, far_high], 0), below]


def ring_reduce(pieces, axis, cut):
    own, above, far, below = pieces
    low = move(far[:cut].astype(bf16), **{axis: 1})
    high = move(far[cut:].astype(bf16), **{axis: -1})
    up = jnp.concatenate([above[:cut].astype(f32) + low.astype(f32), above[cut:].astype(f32)], 0)
    down = jnp.concatenate([below[:cut].astype(f32), below[cut:].astype(f32) + high.astype(f32)], 0)
    from_below = move(up.astype(bf16), **{axis: 1})
    from_above = move(down.astype(bf16), **{axis: -1})
    return own.astype(f32) + from_below.astype(f32) + from_above.astype(f32)


def group_gather(own, cut):
    other = move(own, l=1)
    return ring_gather(own, "x", cut) + ring_gather(other, "x", cut)


def group_reduce(pieces, cut):
    other = ring_reduce(pieces[4:], "x", cut)
    crossed = move(other.astype(bf16), l=1)
    return ring_reduce(pieces[:4], "x", cut) + crossed.astype(f32)


def place(pieces, start, count, axis):
    full = jnp.stack(pieces + pieces[:-1], axis)
    return lax.dynamic_slice_in_dim(full, (count - start) % count, count, axis)


def normalize(value):
    xf = value.astype(f32)
    centre = xf - jnp.mean(xf, -1, keepdims=True)
    inverse = lax.rsqrt(jnp.mean(centre * centre, -1, keepdims=True) + EPS)
    return centre * inverse, inverse


def kernel_params():
    return pltpu.CompilerParams(vmem_limit_bytes=56 * 1024 * 1024)


def dot(a, b, ca=1, cb=0):
    return lax.dot_general(a, b, (((ca,), (cb,)), ((), ())), preferred_element_type=f32)


def hidden_part(h2, weight, first, bias):
    rows, width = h2.shape
    ff = bias.shape[1]

    def body(h_ref, w_ref, b_ref, act_ref, slope_ref):
        u = dot(h_ref[...], w_ref[...]) + b_ref[...]
        cdf = 0.5 * (1.0 + lax.erf(u * math.sqrt(0.5)))
        pdf = jnp.exp(-0.5 * u * u) * (1.0 / math.sqrt(2.0 * math.pi))
        act_ref[...] = (u * cdf).astype(bf16)
        slope_ref[...] = cdf + u * pdf

    return pl.pallas_call(
        body,
        out_shape=(
            jax.ShapeDtypeStruct((rows, ff), bf16),
            jax.ShapeDtypeStruct((rows, ff), f32),
        ),
        grid=(ff // 256,),
        in_specs=[
            pl.BlockSpec((rows, width), lambda i: (0, 0)),
            pl.BlockSpec((width, 256), lambda i: (0, i + first)),
            pl.BlockSpec((1, 256), lambda i: (0, i)),
        ],
        out_specs=(
            pl.BlockSpec((rows, 256), lambda i: (0, i)),
            pl.BlockSpec((rows, 256), lambda i: (0, i)),
        ),
        compiler_params=kernel_params(),
        cost_estimate=COST,
        name="hidden_part",
    )(h2, weight, bias)


def swap_halves(value):
    lane = lax.broadcasted_iota(jnp.int32, value.shape, 1)
    return jnp.where(lane < 32, pltpu.roll(value, 96, 1), pltpu.roll(value, 32, 1))


def allowed_mask(lengths_ref, block, rows):
    e0 = lengths_ref[block, 0]
    e1 = e0 + lengths_ref[block, 1]
    t = lax.broadcasted_iota(jnp.int32, (rows, rows), 0)
    s = lax.broadcasted_iota(jnp.int32, (rows, rows), 1)
    seg_t = (t >= e0).astype(jnp.int32) + (t >= e1).astype(jnp.int32)
    seg_s = (s >= e0).astype(jnp.int32) + (s >= e1).astype(jnp.int32)
    return (seg_t == seg_s) & (s <= t)


def attention(h1, weight, bias, cosine, sine, lengths, rows=128, head=256):
    total, width = h1.shape
    blocks = total // rows
    scale = head ** (-0.5)

    def body(len_ref, h_ref, w_ref, b_ref, cos_ref, sin_ref, qkv_ref, p_ref, o_ref, work):
        step = pl.program_id(0)

        @pl.when(step < 3)
        def _():
            work[step] = dot(h_ref[...], w_ref[...]) + b_ref[0]

        @pl.when(step >= 3)
        def _():
            block = step - 3
            at = pl.ds(block * rows, rows)
            cos, sin = cos_ref[...], sin_ref[...]

            def turned(value):
                left = value[:, :128]
                left = left * cos + swap_halves(left) * sin
                return jnp.concatenate([left, value[:, 128:]], 1).astype(bf16)

            q, k = turned(work[0, at, :]), turned(work[1, at, :])
            v = work[2, at, :].astype(bf16)
            qkv_ref[:, 0:head] = q
            qkv_ref[:, head : 2 * head] = k
            qkv_ref[:, 2 * head :] = v
            scores = dot(q, k, 1, 1) * scale
            masked = jnp.where(allowed_mask(len_ref, block, rows), scores, -1e30)
            shifted = jnp.exp(masked - jnp.max(masked, 1, keepdims=True))
            probs = shifted / jnp.sum(shifted, 1, keepdims=True)
            p_ref[...] = probs
            o_ref[...] = dot(probs.astype(bf16), v).astype(bf16)

    def at_block(i, lens):
        return (jnp.maximum(i - 3, 0), 0)

    return pl.pallas_call(
        body,
        out_shape=(
            jax.ShapeDtypeStruct((total, 3 * head), bf16),
            jax.ShapeDtypeStruct((total, rows), f32),
            jax.ShapeDtypeStruct((total, head), bf16),
        ),
        grid_spec=pltpu.PrefetchScalarGridSpec(
            num_scalar_prefetch=1,
            grid=(3 + blocks,),
            in_specs=[
                pl.BlockSpec((total, width), lambda i, lens: (0, 0)),
                pl.BlockSpec((width, head), lambda i, lens: (0, jnp.minimum(i, 2))),
                pl.BlockSpec((1, 1, head), lambda i, lens: (jnp.minimum(i, 2), 0, 0)),
                pl.BlockSpec((rows, 128), at_block),
                pl.BlockSpec((rows, 128), at_block),
            ],
            out_specs=(
                pl.BlockSpec((rows, 3 * head), at_block),
                pl.BlockSpec((rows, rows), at_block),
                pl.BlockSpec((rows, head), at_block),
            ),
            scratch_shapes=[pltpu.VMEM((3, total, head), f32)],
        ),
        compiler_params=kernel_params(),
        cost_estimate=COST,
        name="attention",
    )(lengths, h1, weight, bias, cosine, sine)


def mixed_part(active, attended, down, out, bias):
    rows, ff = active.shape
    head, width = out.shape

    def body(act_ref, ol_ref, wd_ref, wo_ref, b_ref, mix_ref):
        total = dot(act_ref[...], wd_ref[...]) + dot(ol_ref[...], wo_ref[...]) + b_ref[...]
        mix_ref[...] = total.astype(bf16)

    return pl.pallas_call(
        body,
        out_shape=jax.ShapeDtypeStruct((rows, width), bf16),
        grid=(width // 256,),
        in_specs=[
            pl.BlockSpec((rows, ff), lambda i: (0, 0)),
            pl.BlockSpec((rows, head), lambda i: (0, 0)),
            pl.BlockSpec((ff, 256), lambda i: (0, i)),
            pl.BlockSpec((head, 256), lambda i: (0, i)),
            pl.BlockSpec((1, 256), lambda i: (0, i)),
        ],
        out_specs=pl.BlockSpec((rows, 256), lambda i: (0, i)),
        compiler_params=kernel_params(),
        cost_estimate=COST,
        name="mixed_part",
    )(active, attended, down, out, bias)


def back_inner(dy, down, out, slope, qkv, probs, cosine, sine, rows=128):
    total, width = dy.shape
    ff, head = down.shape[0], out.shape[0]
    steps = ff // 256
    blocks = total // rows
    scale = head ** (-0.5)

    def body(dy_ref, wd_ref, wo_ref, s_ref, qkv_ref, p_ref, cos_ref, sin_ref, du_ref, db_ref, dq_ref, dqb_ref, work):
        step = pl.program_id(0)

        @pl.when(step < steps)
        def _():
            du = (dot(dy_ref[...], wd_ref[...], 1, 1) * s_ref[...]).astype(bf16)
            du_ref[...] = du
            db_ref[...] = jnp.sum(du.astype(f32), 0, keepdims=True)

        @pl.when(step == steps)
        def _():
            work[...] = dot(dy_ref[...], wo_ref[...], 1, 1).astype(bf16)
            dqb_ref[...] = jnp.zeros_like(dqb_ref)

        @pl.when(step > steps)
        def _():
            block = step - steps - 1
            cos, sin = cos_ref[...], sin_ref[...]
            q, k, v = (qkv_ref[:, n * head : (n + 1) * head] for n in range(3))
            probs = p_ref[...]
            d_out = work[pl.ds(block * rows, rows), :]
            d_value = dot(probs.astype(bf16), d_out, 0, 0)
            d_probs = dot(d_out, v, 1, 1)
            centred = d_probs - jnp.sum(d_probs * probs, 1, keepdims=True)
            d_scores = (probs * centred).astype(bf16)

            def back(value):
                value = value * scale
                left = value[:, :128]
                left = left * cos - swap_halves(left) * sin
                return jnp.concatenate([left, value[:, 128:]], 1).astype(bf16)

            for n, grad in enumerate(
                (back(dot(d_scores, k)), back(dot(d_scores, q, 0, 0)), d_value.astype(bf16))
            ):
                dq_ref[:, n * head : (n + 1) * head] = grad
                dqb_ref[:, n * head : (n + 1) * head] += jnp.sum(grad.astype(f32), 0, keepdims=True)

    def part(i):
        return jnp.minimum(i, steps - 1)

    def at_block(i):
        return (jnp.maximum(i - steps - 1, 0), 0)

    return pl.pallas_call(
        body,
        out_shape=(
            jax.ShapeDtypeStruct((total, ff), bf16),
            jax.ShapeDtypeStruct((1, ff), f32),
            jax.ShapeDtypeStruct((total, 3 * head), bf16),
            jax.ShapeDtypeStruct((1, 3 * head), f32),
        ),
        grid=(steps + 1 + blocks,),
        in_specs=[
            pl.BlockSpec((total, width), lambda i: (0, 0)),
            pl.BlockSpec((256, width), lambda i: (part(i), 0)),
            pl.BlockSpec((head, width), lambda i: (0, 0)),
            pl.BlockSpec((total, 256), lambda i: (0, part(i))),
            pl.BlockSpec((rows, 3 * head), at_block),
            pl.BlockSpec((rows, rows), at_block),
            pl.BlockSpec((rows, 128), at_block),
            pl.BlockSpec((rows, 128), at_block),
        ],
        out_specs=(
            pl.BlockSpec((total, 256), lambda i: (0, part(i))),
            pl.BlockSpec((1, 256), lambda i: (0, part(i))),
            pl.BlockSpec((rows, 3 * head), at_block),
            pl.BlockSpec((1, 3 * head), lambda i: (0, 0)),
        ),
        scratch_shapes=[pltpu.VMEM((total, head), bf16)],
        compiler_params=kernel_params(),
        cost_estimate=COST,
        name="back_inner",
    )(dy, down, out, slope, qkv, probs, cosine, sine)


def back_norms(d_qkv, d_hidden, weight, tokens, mean, inverse, gains):
    total, n1 = d_qkv.shape
    n2 = d_hidden.shape[1]
    width = tokens.shape[1]

    def body(dq_ref, du_ref, w_ref, x_ref, m_ref, i_ref, g_ref, s_ref, sums_ref):
        d1 = dot(dq_ref[...], w_ref[:, :n1], 1, 1)
        d2 = dot(du_ref[...], w_ref[:, n1:], 1, 1)
        normed = (x_ref[...].astype(f32) - m_ref[...]) * i_ref[...]
        s_ref[...] = (d1 * g_ref[0:1] + d2 * g_ref[1:2]).astype(bf16)
        sums_ref[0:1] = jnp.sum(d1 * normed, 0, keepdims=True)
        sums_ref[1:2] = jnp.sum(d1, 0, keepdims=True)
        sums_ref[2:3] = jnp.sum(d2 * normed, 0, keepdims=True)
        sums_ref[3:4] = jnp.sum(d2, 0, keepdims=True)

    return pl.pallas_call(
        body,
        out_shape=(
            jax.ShapeDtypeStruct((total, width), bf16),
            jax.ShapeDtypeStruct((4, width), f32),
        ),
        grid=(width // 256,),
        in_specs=[
            pl.BlockSpec((total, n1), lambda i: (0, 0)),
            pl.BlockSpec((total, n2), lambda i: (0, 0)),
            pl.BlockSpec((256, n1 + n2), lambda i: (i, 0)),
            pl.BlockSpec((total, 256), lambda i: (0, i)),
            pl.BlockSpec((total, 1), lambda i: (0, 0)),
            pl.BlockSpec((total, 1), lambda i: (0, 0)),
            pl.BlockSpec((2, 256), lambda i: (0, i)),
        ],
        out_specs=(
            pl.BlockSpec((total, 256), lambda i: (0, i)),
            pl.BlockSpec((4, 256), lambda i: (0, i)),
        ),
        compiler_params=kernel_params(),
        cost_estimate=COST,
        name="back_norms",
    )(d_qkv, d_hidden, weight, tokens, mean, inverse, gains)


def norms(tokens, gains):
    total, width = tokens.shape
    rows = 128

    def body(x_ref, g_ref, h1_ref, h2_ref, m_ref, i_ref):
        x = x_ref[...].astype(f32)
        mean = jnp.mean(x, 1, keepdims=True)
        centre = x - mean
        inverse = lax.rsqrt(jnp.mean(centre * centre, 1, keepdims=True) + 1e-5)
        normed = centre * inverse
        m_ref[...] = mean
        i_ref[...] = inverse
        h1_ref[...] = (normed * g_ref[0:1] + g_ref[1:2]).astype(bf16)
        h2_ref[...] = (normed * g_ref[2:3] + g_ref[3:4]).astype(bf16)

    column = jax.ShapeDtypeStruct((total, 1), f32)
    wide = jax.ShapeDtypeStruct((total, width), bf16)
    block = pl.BlockSpec((rows, width), lambda i: (i, 0))
    thin = pl.BlockSpec((rows, 1), lambda i: (i, 0))
    return pl.pallas_call(
        body,
        out_shape=(wide, wide, column, column),
        grid=(total // rows,),
        in_specs=[block, pl.BlockSpec((4, width), lambda i: (0, 0))],
        out_specs=(block, block, thin, thin),
        compiler_params=kernel_params(),
        cost_estimate=COST,
        name="norms",
    )(tokens, gains)


def dot_rows(a, b):
    return lax.dot_general(a, b, (((0,), (0,)), ((), ())), preferred_element_type=f32)


def sorted_weight(mine, yours, spots):
    sources, rows, cols = mine.shape[1:]

    def body(spot_ref, mine_ref, yours_ref, out_ref):
        step = pl.program_id(0)

        @pl.when(step < 4)
        def _():
            out_ref[:, 0] = mine_ref[0]

        @pl.when(step >= 4)
        def _():
            out_ref[:, 0] = yours_ref[0]

    block = (1, sources, rows, cols)
    return pl.pallas_call(
        body,
        out_shape=jax.ShapeDtypeStruct((sources, 8, rows, cols), bf16),
        grid_spec=pltpu.PrefetchScalarGridSpec(
            num_scalar_prefetch=1,
            grid=(8,),
            in_specs=[
                pl.BlockSpec(block, lambda i, spot: (jnp.minimum(i, 3), 0, 0, 0)),
                pl.BlockSpec(block, lambda i, spot: (jnp.maximum(i - 4, 0), 0, 0, 0)),
            ],
            out_specs=pl.BlockSpec(
                (sources, 1, rows, cols), lambda i, spot: (0, spot[i], 0, 0)
            ),
        ),
        compiler_params=kernel_params(),
        cost_estimate=COST,
        name="sorted_weight",
    )(spots, mine, yours).reshape(sources * 8 * rows, cols)


def late_grads(active, attended, dy, core):
    width = dy.shape[1]

    def body(core_ref, act_ref, ol_ref, dy_ref, keep_ref, send_ref):
        step = pl.program_id(0)
        first = core_ref[0] == 0

        @pl.when(step < 4)
        def _():
            part = dot_rows(act_ref[...], dy_ref[...]).astype(bf16).reshape(2, 2, 64, width)
            at = pl.ds(step * 2, 2)

            @pl.when(first)
            def _():
                keep_ref[at, 0:64] = part[:, 0]
                send_ref[at, 0:64] = part[:, 1]

            @pl.when(jnp.logical_not(first))
            def _():
                keep_ref[at, 0:64] = part[:, 1]
                send_ref[at, 0:64] = part[:, 0]

        @pl.when(step == 4)
        def _():
            part = dot_rows(ol_ref[...], dy_ref[...]).astype(bf16).reshape(8, 2, 16, width)

            @pl.when(first)
            def _():
                keep_ref[:, 64:80] = part[:, 0]
                send_ref[:, 64:80] = part[:, 1]

            @pl.when(jnp.logical_not(first))
            def _():
                keep_ref[:, 64:80] = part[:, 1]
                send_ref[:, 64:80] = part[:, 0]

    rows = dy.shape[0]
    out = jax.ShapeDtypeStruct((8, 80, width), bf16)
    whole = pl.BlockSpec((8, 80, width), lambda i, core: (0, 0, 0))
    keep, send = pl.pallas_call(
        body,
        out_shape=(out, out),
        grid_spec=pltpu.PrefetchScalarGridSpec(
            num_scalar_prefetch=1,
            grid=(5,),
            in_specs=[
                pl.BlockSpec((rows, 256), lambda i, core: (0, jnp.minimum(i, 3))),
                pl.BlockSpec((rows, 256), lambda i, core: (0, 0)),
                pl.BlockSpec((rows, width), lambda i, core: (0, 0)),
            ],
            out_specs=(whole, whole),
        ),
        compiler_params=kernel_params(),
        cost_estimate=COST,
        name="late_grads",
    )(core, active, attended, dy)
    return keep.reshape(4, 2, 80, width), send.reshape(4, 2, 80, width)


def early_grads(h1, h2, d_qkv, d_hidden, core):
    rows, width = h1.shape
    n1, n2 = d_qkv.shape[1], d_hidden.shape[1]

    def body(core_ref, h1_ref, h2_ref, dq_ref, du_ref, keep_ref, send_ref):
        first = core_ref[0] == 0
        left = dot_rows(h1_ref[...], dq_ref[...]).astype(bf16).reshape(4, 2, 2, 16, n1)
        right = dot_rows(h2_ref[...], du_ref[...]).astype(bf16).reshape(4, 2, 2, 16, n2)

        @pl.when(first)
        def _():
            keep_ref[:, 0, :, :, 0:n1] = left[:, :, 0]
            keep_ref[:, 0, :, :, n1:] = right[:, :, 0]
            send_ref[:, 0, :, :, 0:n1] = left[:, :, 1]
            send_ref[:, 0, :, :, n1:] = right[:, :, 1]

        @pl.when(jnp.logical_not(first))
        def _():
            keep_ref[:, 0, :, :, 0:n1] = left[:, :, 1]
            keep_ref[:, 0, :, :, n1:] = right[:, :, 1]
            send_ref[:, 0, :, :, 0:n1] = left[:, :, 0]
            send_ref[:, 0, :, :, n1:] = right[:, :, 0]

    out = jax.ShapeDtypeStruct((4, 8, 2, 16, n1 + n2), bf16)
    block = pl.BlockSpec((4, 1, 2, 16, n1 + n2), lambda i, core: (0, i, 0, 0, 0))
    return pl.pallas_call(
        body,
        out_shape=(out, out),
        grid_spec=pltpu.PrefetchScalarGridSpec(
            num_scalar_prefetch=1,
            grid=(8,),
            in_specs=[
                pl.BlockSpec((rows, width // 8), lambda i, core: (0, i)),
                pl.BlockSpec((rows, width // 8), lambda i, core: (0, i)),
                pl.BlockSpec((rows, n1), lambda i, core: (0, 0)),
                pl.BlockSpec((rows, n2), lambda i, core: (0, 0)),
            ],
            out_specs=(block, block),
        ),
        compiler_params=kernel_params(),
        cost_estimate=COST,
        name="early_grads",
    )(core, h1, h2, d_qkv, d_hidden)


def late_outputs(groups, spots):
    width = groups[0].shape[-1]

    def body(spot_ref, *refs):
        ins, down_ref, out_ref = refs[:4], refs[4], refs[5]
        step = pl.program_id(0)
        for at, ref in enumerate(ins):

            @pl.when(step // 4 == at)
            def _(ref=ref):
                down_ref[...] = ref[0, 0:64].astype(f32)
                out_ref[...] = ref[0, 64:80].astype(f32)

    def chosen(at):
        return pl.BlockSpec(
            (1, 80, width), lambda i, spot: (jnp.clip(i - 4 * at, 0, 3), 0, 0)
        )

    return pl.pallas_call(
        body,
        out_shape=(
            jax.ShapeDtypeStruct((1024, width), f32),
            jax.ShapeDtypeStruct((256, width), f32),
        ),
        grid_spec=pltpu.PrefetchScalarGridSpec(
            num_scalar_prefetch=1,
            grid=(16,),
            in_specs=[chosen(at) for at in range(4)],
            out_specs=(
                pl.BlockSpec((64, width), lambda i, spot: (spot[i], 0)),
                pl.BlockSpec((16, width), lambda i, spot: (spot[i], 0)),
            ),
        ),
        compiler_params=kernel_params(),
        cost_estimate=COST,
        name="late_outputs",
    )(spots, *groups)


def early_outputs(mine, yours, spots, n1):
    cols = mine.shape[-1]
    n2 = cols - n1
    head = n1 // 3

    def body(spot_ref, mine_ref, yours_ref, qkv_ref, up_ref):
        step = pl.program_id(0)

        def put(ref):
            for source in range(8):
                for third in range(3):
                    at = (third * 8 + source) * head
                    qkv_ref[:, at : at + head] = ref[
                        0, source, :, third * head : (third + 1) * head
                    ].astype(f32)
                up_ref[:, source * n2 : (source + 1) * n2] = ref[0, source, :, n1:].astype(f32)

        @pl.when(step < 8)
        def _():
            put(mine_ref)

        @pl.when(step >= 8)
        def _():
            put(yours_ref)

    block = (1, 8, 16, cols)
    return pl.pallas_call(
        body,
        out_shape=(
            jax.ShapeDtypeStruct((256, 8 * n1), f32),
            jax.ShapeDtypeStruct((256, 8 * n2), f32),
        ),
        grid_spec=pltpu.PrefetchScalarGridSpec(
            num_scalar_prefetch=1,
            grid=(16,),
            in_specs=[
                pl.BlockSpec(block, lambda i, spot: (jnp.minimum(i, 7), 0, 0, 0)),
                pl.BlockSpec(block, lambda i, spot: (jnp.maximum(i - 8, 0), 0, 0, 0)),
            ],
            out_specs=(
                pl.BlockSpec((16, 8 * n1), lambda i, spot: (spot[i], 0)),
                pl.BlockSpec((16, 8 * n2), lambda i, spot: (spot[i], 0)),
            ),
        ),
        compiler_params=kernel_params(),
        cost_estimate=COST,
        name="early_outputs",
    )(spots, mine, yours)


def local(
    tokens,
    doc_lengths,
    cotangent,
    ln1_gain,
    ln1_bias,
    ln2_gain,
    ln2_bias,
    qkv_weight,
    qkv_bias,
    out_weight,
    out_bias,
    up_weight,
    up_bias,
    down_weight,
    down_bias,
):
    rows, width = tokens.shape
    head = width // HEADS
    group = 8
    rep = lax.axis_index("rep")
    shard = lax.axis_index("shard")
    y, h, c = rep // 4, (rep // 2) % 2, rep % 2
    l, x = shard // 4, shard % 4
    ff = up_bias.shape[0]

    cols = 3 * head + ff
    part = lax.dynamic_slice_in_dim(qkv_weight, y * 64 + c * 32, 32, 0).reshape(32, 3, 8, head)
    part_up = lax.dynamic_slice_in_dim(up_weight, y * 64 + c * 32, 32, 0).reshape(32, 8, ff)
    small = jnp.concatenate([ln1_gain, ln1_bias, ln2_gain, ln2_bias, qkv_bias])
    size = jnp.pad(doc_lengths[0].astype(bf16), (0, cols - doc_lengths.shape[1]))
    small = jnp.pad(jnp.stack([small, size]), ((0, 6), (0, 0)))
    part = jnp.concatenate(
        [part.transpose(2, 0, 1, 3).reshape(8, 32, 3 * head), part_up.transpose(1, 0, 2)], -1
    )
    part = jnp.concatenate([part, jnp.broadcast_to(small[None], (8, 8, cols))], 1)
    part = lax.all_to_all(part, "shard", 0, 0)
    infos = part[:, 32:34]
    mine = jnp.stack(ring_gather(part[:, :32], "y", 4))
    yours = move(mine, c=1)
    steps4 = (y + jnp.arange(4)) % 4
    spots = jnp.concatenate([steps4 * 2 + c, steps4 * 2 + 1 - c]).astype(jnp.int32)
    w_mixed = sorted_weight(mine, yours, spots)

    places = [((l ^ (k // 4)) * 4 + (x + k % 4) % 4) for k in range(8)]
    x_all = jnp.zeros((group * rows, width), bf16)
    for place_of, piece in zip(places, group_gather(tokens, 64)):
        x_all = lax.dynamic_update_slice(x_all, piece, (place_of * rows, 0))
    dy_all = lax.all_gather(cotangent, "shard", axis=0, tiled=True)

    gains = infos[:, 0, :1024].reshape(8, 4, 256).transpose(1, 0, 2).reshape(4, width).astype(f32)
    qkv_b = infos[:, 0, 1024:].astype(f32).reshape(8 * 3, 1, head)
    qkv_b = jnp.stack(
        [lax.dynamic_index_in_dim(qkv_b, third * 8 + shard, 0, False) for third in range(3)]
    )
    lengths = infos[:, 1, :3].astype(jnp.int32)
    ends = jnp.cumsum(lengths, 1)
    starts = ends - lengths
    steps_t = jnp.arange(rows, dtype=jnp.int32)
    segment = jnp.sum((steps_t[None, :, None] >= ends[:, None, :]).astype(jnp.int32), -1)
    slots = jnp.arange(lengths.shape[1], dtype=jnp.int32)
    begin = jnp.sum(
        jnp.where(segment[:, :, None] == slots[None, None, :], starts[:, None, :], 0), -1
    )
    position = (steps_t[None, :] - begin).astype(f32).reshape(group * rows, 1)
    lane = jnp.arange(128)
    freq = 10000.0 ** (-2.0 * (lane % (ROT // 2)).astype(f32) / ROT)
    angle = position * freq[None, :]
    cosine = jnp.where(lane < ROT, jnp.cos(angle), 1.0)
    sine = jnp.sin(angle)
    sine = jnp.where(lane < ROT // 2, -sine, jnp.where(lane < ROT, sine, 0.0))

    h1, h2, mean, inverse = norms(x_all, gains)
    active, slope = hidden_part(h2, w_mixed, 3 * head // 256, up_bias.astype(f32)[None])
    qkv, probs, attended = attention(h1, w_mixed, qkv_b, cosine, sine, lengths)
    both_bias = (out_bias.astype(f32) + down_bias.astype(f32))[None, :]
    wide_bias = lax.dynamic_update_slice(jnp.zeros((1, width), f32), both_bias, (0, shard * 256))
    mix = mixed_part(active, attended, down_weight, out_weight, wide_bias)
    mixed = lax.psum_scatter(mix, "shard", scatter_dimension=0, tiled=True)
    mixed = (tokens.astype(f32) + mixed.astype(f32)).astype(bf16)

    core = c.astype(jnp.int32).reshape(1)
    late_keep, late_send = late_grads(active, attended, dy_all, core)
    d_hidden, up_b, d_qkv, qkv_bg = back_inner(
        dy_all, down_weight, out_weight, slope, qkv, probs, cosine, sine
    )
    early_keep, early_send = early_grads(h1, h2, d_qkv, d_hidden, core)
    sums, norm_sums = back_norms(
        d_qkv, d_hidden, w_mixed, x_all, mean, inverse, jnp.stack([gains[0], gains[2]])
    )
    sums = sums.reshape(group, rows, width)
    own_sum = group_reduce([pick(sums, place_of, 0) for place_of in places], 64)
    own_normed, own_inverse = normalize(tokens)
    tokens_grad = cotangent.astype(f32) + own_inverse * (
        own_sum
        - jnp.mean(own_sum, -1, keepdims=True)
        - own_normed * jnp.mean(own_sum * own_normed, -1, keepdims=True)
    )

    dy_sum = jnp.sum(dy_all.astype(f32), 0)
    dy_own = lax.dynamic_slice_in_dim(dy_sum, shard * 256, 256)
    wide_qkv = lax.dynamic_update_slice(
        jnp.zeros((3, 8, head), f32), qkv_bg.reshape(3, 1, head), (0, shard, 0)
    )
    wide_up = lax.dynamic_update_slice(jnp.zeros((8 * ff,), f32), up_b.reshape(-1), (shard * ff,))
    wide_dy = lax.dynamic_update_slice(jnp.zeros((width,), f32), dy_own, (shard * 256,))
    smalls = jnp.concatenate([norm_sums.reshape(-1), wide_dy, wide_qkv.reshape(-1), wide_up])
    smalls = smalls.reshape(-1, 1024)
    for axis, bit in (("c", 1), ("l", 1), ("h", 1), ("x", 1), ("y", 1), ("x", 2), ("y", 2)):
        smalls = smalls + swap(smalls, axis, bit)
    smalls = smalls.reshape(-1)

    def small_at(start, size):
        return lax.dynamic_slice_in_dim(smalls, start + shard * size, size)

    got = move(late_send, c=1)

    def late_part(high, index):
        both = [pick(pick(v, high, 1), index, 0).astype(f32) for v in (late_keep, got)]
        return both[0] + both[1]

    away = (pick(late_keep, 1 - h, 1).astype(f32) + pick(got, 1 - h, 1).astype(f32)).astype(bf16)
    crossed = move(away, h=1)
    parts = [late_part(h, (y + k) % 4) + pick(crossed, (y + k) % 4, 0).astype(f32) for k in range(4)]
    late = ring_reduce(parts, "y", 40).astype(bf16)
    late = jnp.stack(ring_gather(late, "y", 40))
    late_h = move(late, h=1)
    late_c = move(late, c=1)
    late_hc = move(late_h, c=1)
    spots = [
        (steps4 * 2 + high) * 2 + low for high, low in ((h, c), (1 - h, c), (h, 1 - c), (1 - h, 1 - c))
    ]
    down_grad, out_grad = late_outputs(
        (late, late_h, late_c, late_hc), jnp.concatenate(spots).astype(jnp.int32)
    )

    got_early = move(early_send, c=1)
    parts = [
        pick(early_keep, (y + k) % 4, 0).astype(f32) + pick(got_early, (y + k) % 4, 0).astype(f32)
        for k in range(4)
    ]
    early = ring_reduce(parts, "y", 4)
    crossed = move(pick(early, 1 - h, 1).astype(bf16), h=1)
    early = (pick(early, h, 1) + crossed.astype(f32)).astype(bf16)
    early = lax.all_to_all(early, "shard", 0, 0)
    early = jnp.stack([early, move(early, h=1)])
    early = jnp.concatenate(ring_gather(early, "y", 1), 0)
    early_c = move(early, c=1)
    spots = [
        ((steps4[:, None] * 2 + jnp.stack([h, 1 - h])[None, :]) * 2 + low).reshape(8)
        for low in (c, 1 - c)
    ]
    qkv_grad, up_grad = early_outputs(
        early, early_c, jnp.concatenate(spots).astype(jnp.int32), 3 * head
    )

    dy_total = small_at(4 * width, 256)
    return (
        mixed,
        tokens_grad,
        small_at(0, 256),
        small_at(width, 256),
        small_at(2 * width, 256),
        small_at(3 * width, 256),
        qkv_grad,
        small_at(5 * width, 768),
        out_grad,
        dy_total,
        up_grad,
        small_at(8 * width, ff),
        down_grad,
        dy_total,
    )


def solution(mesh):
    rows = P(BOTH, None)
    vector, matrix = P("shard"), P("shard", None)
    return jax.shard_map(
        local,
        mesh=mesh,
        in_specs=(rows, rows, rows, vector, vector, vector, vector)
        + (matrix, vector, matrix, vector, matrix, vector, matrix, vector),
        out_specs=(rows, rows, vector, vector, vector, vector)
        + (matrix, vector, matrix, vector, matrix, vector, matrix, vector),
        check_vma=False,
    )
```

```python
import math

import jax
import jax.numpy as jnp
from jax import lax
from jax.experimental import pallas as pl
from jax.experimental.pallas import tpu as pltpu
from jax.sharding import PartitionSpec as P

HEADS = 8
ROT = 64
EPS = 1e-05
f32 = jnp.float32
bf16 = jnp.bfloat16
COST = pl.CostEstimate(flops=1000, bytes_accessed=1000, transcendentals=0)
BOTH = ("rep", "shard")
SIZES = (4, 2, 2, 2, 4)
SAME_CORE = [[2 * n + c for n in range(8)] for c in range(2)]
SAME_CORE_ALL = [[(2 * n + c) * 8 + s for n in range(8) for s in range(8)] for c in range(2)]


def coords():
    for y in range(4):
        for h in range(2):
            for c in range(2):
                for l in range(2):
                    for x in range(4):
                        yield (y, h, c, l, x)


def linear(t):
    y, h, c, l, x = (v % m for v, m in zip(t, SIZES))
    return ((y * 2 + h) * 2 + c) * 8 + l * 4 + x


def move(value, y=0, h=0, c=0, l=0, x=0):
    step = (y, h, c, l, x)
    pairs = [(linear(t), linear(tuple(a + b for a, b in zip(t, step)))) for t in coords()]
    return lax.ppermute(value, BOTH, pairs)


def swap(value, axis, bit):
    at = "yhclx".index(axis)
    pairs = [(linear(t), linear(t[:at] + (t[at] ^ bit,) + t[at + 1 :])) for t in coords()]
    return lax.ppermute(value, BOTH, pairs)


def pick(value, index, axis):
    return lax.dynamic_index_in_dim(value, index, axis, keepdims=False)


def ring_gather(own, axis, cut):
    below = move(own, **{axis: 1})
    above = move(own, **{axis: -1})
    far_low = move(below[:cut], **{axis: 1})
    far_high = move(above[cut:], **{axis: -1})
    return [own, above, jnp.concatenate([far_low, far_high], 0), below]


def normalize(value):
    xf = value.astype(f32)
    centre = xf - jnp.mean(xf, -1, keepdims=True)
    inverse = lax.rsqrt(jnp.mean(centre * centre, -1, keepdims=True) + EPS)
    return centre * inverse, inverse


def kernel_params():
    return pltpu.CompilerParams(vmem_limit_bytes=56 * 1024 * 1024)


def after_inputs(body, count, extra):
    return lambda *refs: body(*refs[:count], *refs[count + extra :])


def anywhere(count):
    return [pl.BlockSpec(memory_space=pl.ANY)] * count


def dot(a, b, ca=1, cb=0):
    return lax.dot_general(a, b, (((ca,), (cb,)), ((), ())), preferred_element_type=f32)


def hidden_part(h2, weight, first, bias):
    rows, width = h2.shape
    ff = bias.shape[1]

    def body(h_ref, w_ref, b_ref, act_ref, slope_ref):
        u = dot(h_ref[...], w_ref[...]) + b_ref[...]
        cdf = 0.5 * (1.0 + lax.erf(u * math.sqrt(0.5)))
        pdf = jnp.exp(-0.5 * u * u) * (1.0 / math.sqrt(2.0 * math.pi))
        act_ref[...] = (u * cdf).astype(bf16)
        slope_ref[...] = cdf + u * pdf

    return pl.pallas_call(
        body,
        out_shape=(
            jax.ShapeDtypeStruct((rows, ff), bf16),
            jax.ShapeDtypeStruct((rows, ff), f32),
        ),
        grid=(ff // 256,),
        in_specs=[
            pl.BlockSpec((rows, width), lambda i: (0, 0)),
            pl.BlockSpec((width, 256), lambda i: (0, i + first)),
            pl.BlockSpec((1, 256), lambda i: (0, i)),
        ],
        out_specs=(
            pl.BlockSpec((rows, 256), lambda i: (0, i)),
            pl.BlockSpec((rows, 256), lambda i: (0, i)),
        ),
        compiler_params=kernel_params(),
        cost_estimate=COST,
        name="hidden_part",
    )(h2, weight, bias)


def swap_halves(value):
    lane = lax.broadcasted_iota(jnp.int32, value.shape, 1)
    return jnp.where(lane < 32, pltpu.roll(value, 96, 1), pltpu.roll(value, 32, 1))


def allowed_mask(lengths_ref, block, rows):
    e0 = lengths_ref[block, 0]
    e1 = e0 + lengths_ref[block, 1]
    t = lax.broadcasted_iota(jnp.int32, (rows, rows), 0)
    s = lax.broadcasted_iota(jnp.int32, (rows, rows), 1)
    seg_t = (t >= e0).astype(jnp.int32) + (t >= e1).astype(jnp.int32)
    seg_s = (s >= e0).astype(jnp.int32) + (s >= e1).astype(jnp.int32)
    return (seg_t == seg_s) & (s <= t)


def attention(h1, weight, bias, cosine, sine, lengths, rows=128, head=256):
    total, width = h1.shape
    blocks = total // rows
    scale = head ** (-0.5)

    def body(len_ref, h_ref, w_ref, b_ref, cos_ref, sin_ref, qkv_ref, p_ref, o_ref, work):
        step = pl.program_id(0)

        @pl.when(step < 3)
        def _():
            work[step] = dot(h_ref[...], w_ref[...]) + b_ref[0]

        @pl.when(step >= 3)
        def _():
            block = step - 3
            at = pl.ds(block * rows, rows)
            cos, sin = cos_ref[...], sin_ref[...]

            def turned(value):
                left = value[:, :128]
                left = left * cos + swap_halves(left) * sin
                return jnp.concatenate([left, value[:, 128:]], 1).astype(bf16)

            q, k = turned(work[0, at, :]), turned(work[1, at, :])
            v = work[2, at, :].astype(bf16)
            qkv_ref[:, 0:head] = q
            qkv_ref[:, head : 2 * head] = k
            qkv_ref[:, 2 * head :] = v
            scores = dot(q, k, 1, 1) * scale
            masked = jnp.where(allowed_mask(len_ref, block, rows), scores, -1e30)
            shifted = jnp.exp(masked - jnp.max(masked, 1, keepdims=True))
            probs = shifted / jnp.sum(shifted, 1, keepdims=True)
            p_ref[...] = probs
            o_ref[...] = dot(probs.astype(bf16), v).astype(bf16)

    def at_block(i, lens):
        return (jnp.maximum(i - 3, 0), 0)

    return pl.pallas_call(
        body,
        out_shape=(
            jax.ShapeDtypeStruct((total, 3 * head), bf16),
            jax.ShapeDtypeStruct((total, rows), f32),
            jax.ShapeDtypeStruct((total, head), bf16),
        ),
        grid_spec=pltpu.PrefetchScalarGridSpec(
            num_scalar_prefetch=1,
            grid=(3 + blocks,),
            in_specs=[
                pl.BlockSpec((total, width), lambda i, lens: (0, 0)),
                pl.BlockSpec((width, head), lambda i, lens: (0, jnp.minimum(i, 2))),
                pl.BlockSpec((1, 1, head), lambda i, lens: (jnp.minimum(i, 2), 0, 0)),
                pl.BlockSpec((rows, 128), at_block),
                pl.BlockSpec((rows, 128), at_block),
            ],
            out_specs=(
                pl.BlockSpec((rows, 3 * head), at_block),
                pl.BlockSpec((rows, rows), at_block),
                pl.BlockSpec((rows, head), at_block),
            ),
            scratch_shapes=[pltpu.VMEM((3, total, head), f32)],
        ),
        compiler_params=kernel_params(),
        cost_estimate=COST,
        name="attention",
    )(lengths, h1, weight, bias, cosine, sine)


def mixed_part(active, attended, down, out, bias, after):
    rows, ff = active.shape
    head, width = out.shape
    count = rows // 128

    def body(act_ref, ol_ref, wd_ref, wo_ref, b_ref, *refs):
        total = dot(act_ref[...], wd_ref[...]) + dot(ol_ref[...], wo_ref[...]) + b_ref[...]
        for at in range(count):
            refs[at][...] = total[at * 128 : (at + 1) * 128].astype(bf16)

    return pl.pallas_call(
        after_inputs(body, 5, len(after)),
        out_shape=(jax.ShapeDtypeStruct((128, width), bf16),) * count,
        grid=(width // 256,),
        in_specs=[
            pl.BlockSpec((rows, ff), lambda i: (0, 0)),
            pl.BlockSpec((rows, head), lambda i: (0, 0)),
            pl.BlockSpec((ff, 256), lambda i: (0, i)),
            pl.BlockSpec((head, 256), lambda i: (0, i)),
            pl.BlockSpec((1, 256), lambda i: (0, i)),
        ]
        + anywhere(len(after)),
        out_specs=(pl.BlockSpec((128, 256), lambda i: (0, i)),) * count,
        compiler_params=kernel_params(),
        cost_estimate=COST,
        name="mixed_part",
    )(active, attended, down, out, bias, *after)


def back_inner(dy, down, out, slope, qkv, probs, cosine, sine, after, rows=128):
    width = dy[0].shape[1]
    count = len(dy)
    total = count * rows
    ff, head = down.shape[0], out.shape[0]
    steps = ff // 256
    blocks = total // rows
    scale = head ** (-0.5)

    def body(*refs):
        wd_ref, wo_ref, s_ref, qkv_ref, p_ref, cos_ref, sin_ref = refs[count : count + 7]
        du_ref, db_ref, dq_ref, dqb_ref, work, dy_ref, sems = refs[count + 7 :]
        step = pl.program_id(0)

        @pl.when(step == 0)
        def _():
            fetch(refs[:count], dy_ref, sems, rows)

        @pl.when(step < steps)
        def _():
            du = (dot(dy_ref[...], wd_ref[...], 1, 1) * s_ref[...]).astype(bf16)
            du_ref[...] = du
            db_ref[...] = jnp.sum(du.astype(f32), 0, keepdims=True)

        @pl.when(step == steps)
        def _():
            work[...] = dot(dy_ref[...], wo_ref[...], 1, 1).astype(bf16)
            dqb_ref[...] = jnp.zeros_like(dqb_ref)

        @pl.when(step > steps)
        def _():
            block = step - steps - 1
            cos, sin = cos_ref[...], sin_ref[...]
            q, k, v = (qkv_ref[:, n * head : (n + 1) * head] for n in range(3))
            probs = p_ref[...]
            d_out = work[pl.ds(block * rows, rows), :]
            d_value = dot(probs.astype(bf16), d_out, 0, 0)
            d_probs = dot(d_out, v, 1, 1)
            centred = d_probs - jnp.sum(d_probs * probs, 1, keepdims=True)
            d_scores = (probs * centred).astype(bf16)

            def back(value):
                value = value * scale
                left = value[:, :128]
                left = left * cos - swap_halves(left) * sin
                return jnp.concatenate([left, value[:, 128:]], 1).astype(bf16)

            for n, grad in enumerate(
                (back(dot(d_scores, k)), back(dot(d_scores, q, 0, 0)), d_value.astype(bf16))
            ):
                dq_ref[:, n * head : (n + 1) * head] = grad
                dqb_ref[:, n * head : (n + 1) * head] += jnp.sum(grad.astype(f32), 0, keepdims=True)

    def part(i):
        return jnp.minimum(i, steps - 1)

    def at_block(i):
        return (jnp.maximum(i - steps - 1, 0), 0)

    return pl.pallas_call(
        after_inputs(body, count + 7, len(after)),
        out_shape=(
            jax.ShapeDtypeStruct((total, ff), bf16),
            jax.ShapeDtypeStruct((1, ff), f32),
            jax.ShapeDtypeStruct((total, 3 * head), bf16),
            jax.ShapeDtypeStruct((1, 3 * head), f32),
        ),
        grid=(steps + 1 + blocks,),
        in_specs=anywhere(count)
        + [
            pl.BlockSpec((256, width), lambda i: (part(i), 0)),
            pl.BlockSpec((head, width), lambda i: (0, 0)),
            pl.BlockSpec((total, 256), lambda i: (0, part(i))),
            pl.BlockSpec((rows, 3 * head), at_block),
            pl.BlockSpec((rows, rows), at_block),
            pl.BlockSpec((rows, 128), at_block),
            pl.BlockSpec((rows, 128), at_block),
        ]
        + anywhere(len(after)),
        out_specs=(
            pl.BlockSpec((total, 256), lambda i: (0, part(i))),
            pl.BlockSpec((1, 256), lambda i: (0, part(i))),
            pl.BlockSpec((rows, 3 * head), at_block),
            pl.BlockSpec((1, 3 * head), lambda i: (0, 0)),
        ),
        scratch_shapes=[
            pltpu.VMEM((total, head), bf16),
            pltpu.VMEM((total, width), bf16),
            pltpu.SemaphoreType.DMA((count,)),
        ],
        compiler_params=kernel_params(),
        cost_estimate=COST,
        name="back_inner",
    )(*dy, down, out, slope, qkv, probs, cosine, sine, *after)


def back_norms(d_qkv, d_hidden, weight, tokens, mean, inverse, gains, after):
    total, n1 = d_qkv.shape
    n2 = d_hidden.shape[1]
    width = tokens.shape[1]
    count = total // 128

    def body(dq_ref, du_ref, w_ref, x_ref, m_ref, i_ref, g_ref, sums_ref, *refs):
        d1 = dot(dq_ref[...], w_ref[:, :n1], 1, 1)
        d2 = dot(du_ref[...], w_ref[:, n1:], 1, 1)
        normed = (x_ref[...].astype(f32) - m_ref[...]) * i_ref[...]
        both = (d1 * g_ref[0:1] + d2 * g_ref[1:2]).astype(bf16)
        for at in range(count):
            refs[at][...] = both[at * 128 : (at + 1) * 128]
        sums_ref[0:1] = jnp.sum(d1 * normed, 0, keepdims=True)
        sums_ref[1:2] = jnp.sum(d1, 0, keepdims=True)
        sums_ref[2:3] = jnp.sum(d2 * normed, 0, keepdims=True)
        sums_ref[3:4] = jnp.sum(d2, 0, keepdims=True)

    return pl.pallas_call(
        after_inputs(body, 7, len(after)),
        out_shape=(jax.ShapeDtypeStruct((4, width), f32),)
        + (jax.ShapeDtypeStruct((128, width), bf16),) * count,
        grid=(width // 256,),
        in_specs=[
            pl.BlockSpec((total, n1), lambda i: (0, 0)),
            pl.BlockSpec((total, n2), lambda i: (0, 0)),
            pl.BlockSpec((256, n1 + n2), lambda i: (i, 0)),
            pl.BlockSpec((total, 256), lambda i: (0, i)),
            pl.BlockSpec((total, 1), lambda i: (0, 0)),
            pl.BlockSpec((total, 1), lambda i: (0, 0)),
            pl.BlockSpec((2, 256), lambda i: (0, i)),
        ]
        + anywhere(len(after)),
        out_specs=(pl.BlockSpec((4, 256), lambda i: (0, i)),)
        + (pl.BlockSpec((128, 256), lambda i: (0, i)),) * count,
        compiler_params=kernel_params(),
        cost_estimate=COST,
        name="back_norms",
    )(d_qkv, d_hidden, weight, tokens, mean, inverse, gains, *after)


def norms(pieces, gains):
    rows, width = pieces[0].shape
    count = len(pieces)
    total = rows * count

    def body(*refs):
        g_ref, x_ref, h1_ref, h2_ref, m_ref, i_ref = refs[count:]
        for at in range(count):

            @pl.when(pl.program_id(0) == at)
            def _(at=at):
                x_ref[...] = refs[at][...]

        x = x_ref[...].astype(f32)
        mean = jnp.mean(x, 1, keepdims=True)
        centre = x - mean
        inverse = lax.rsqrt(jnp.mean(centre * centre, 1, keepdims=True) + EPS)
        normed = centre * inverse
        m_ref[...] = mean
        i_ref[...] = inverse
        h1_ref[...] = (normed * g_ref[0:1] + g_ref[1:2]).astype(bf16)
        h2_ref[...] = (normed * g_ref[2:3] + g_ref[3:4]).astype(bf16)

    column = jax.ShapeDtypeStruct((total, 1), f32)
    wide = jax.ShapeDtypeStruct((total, width), bf16)
    block = pl.BlockSpec((rows, width), lambda i: (i, 0))
    thin = pl.BlockSpec((rows, 1), lambda i: (i, 0))
    return pl.pallas_call(
        body,
        out_shape=(wide, wide, wide, column, column),
        grid=(count,),
        in_specs=[pl.BlockSpec((rows, width), lambda i: (0, 0))] * count
        + [pl.BlockSpec((4, width), lambda i: (0, 0))],
        out_specs=(block, block, block, thin, thin),
        compiler_params=kernel_params(),
        cost_estimate=COST,
        name="norms",
    )(*pieces, gains)


def fetch(pieces, target, sems, rows):
    copies = [
        pltpu.make_async_copy(piece, target.at[pl.ds(at * rows, rows)], sems.at[at])
        for at, piece in enumerate(pieces)
    ]
    for copy in copies:
        copy.start()
    for copy in copies:
        copy.wait()


def dot_rows(a, b):
    return lax.dot_general(a, b, (((0,), (0,)), ((), ())), preferred_element_type=f32)


def packed(qkv_weight, up_weight, vectors, lengths, place, head):
    wide, up_wide = qkv_weight.shape[1], up_weight.shape[1]
    part, up_part = 3 * head, up_wide // 8
    cols = part + up_part

    def body(place_ref, len_ref, q_ref, u_ref, v_ref, out_ref):
        lane = lax.broadcasted_iota(jnp.int32, (8, cols), 1)
        row = lax.broadcasted_iota(jnp.int32, (8, cols), 0)
        sizes = jnp.zeros((8, cols), f32)
        for at in range(3):
            sizes = jnp.where(lane == at, len_ref[0, at].astype(f32), sizes)
        vector = jnp.broadcast_to(v_ref[...].astype(f32), (8, cols))
        tail = jnp.where(row == 0, vector, jnp.where(row == 1, sizes, 0.0)).astype(bf16)
        for owner in range(8):
            pieces = [
                q_ref[:, (third * 8 + owner) * head : (third * 8 + owner + 1) * head]
                for third in range(3)
            ]
            pieces.append(u_ref[:, owner * up_part : (owner + 1) * up_part])
            out_ref[owner] = jnp.concatenate([jnp.concatenate(pieces, 1), tail], 0)

    return pl.pallas_call(
        body,
        out_shape=jax.ShapeDtypeStruct((8, 40, cols), bf16),
        grid_spec=pltpu.PrefetchScalarGridSpec(
            num_scalar_prefetch=2,
            grid=(1,),
            in_specs=[
                pl.BlockSpec((32, wide), lambda i, place, lens: (place[0], 0)),
                pl.BlockSpec((32, up_wide), lambda i, place, lens: (place[0], 0)),
                pl.BlockSpec((1, cols), lambda i, place, lens: (0, 0)),
            ],
            out_specs=pl.BlockSpec((8, 40, cols), lambda i, place, lens: (0, 0, 0)),
        ),
        compiler_params=kernel_params(),
        cost_estimate=COST,
        name="packed",
    )(place, lengths, qkv_weight, up_weight, vectors)


def unpacked(part, after):
    owners, _, cols = part.shape

    def body(part_ref, rows_ref, info_ref):
        rows_ref[0] = part_ref[0, 0:32]
        info_ref[0] = part_ref[0, 32:40].astype(f32)

    def block(rows):
        return pl.BlockSpec((1, rows, cols), lambda i: (i, 0, 0))

    return pl.pallas_call(
        after_inputs(body, 1, len(after)),
        out_shape=(
            jax.ShapeDtypeStruct((owners, 32, cols), bf16),
            jax.ShapeDtypeStruct((owners, 8, cols), f32),
        ),
        grid=(owners,),
        in_specs=[block(40)] + anywhere(len(after)),
        out_specs=(block(32), block(8)),
        compiler_params=kernel_params(),
        cost_estimate=COST,
        name="unpacked",
    )(part, *after)


def added(left, right, after):
    count, rows, cols = left.shape

    def body(left_ref, right_ref, out_ref):
        out_ref[...] = (left_ref[...].astype(f32) + right_ref[...].astype(f32)).astype(bf16)

    block = pl.BlockSpec((1, rows, cols), lambda i: (i, 0, 0))
    return pl.pallas_call(
        after_inputs(body, 2, len(after)),
        out_shape=jax.ShapeDtypeStruct(left.shape, bf16),
        grid=(count,),
        in_specs=[block, block] + anywhere(len(after)),
        out_specs=block,
        compiler_params=kernel_params(),
        cost_estimate=COST,
        name="added",
    )(left, right, *after)


def summed(parts, after):
    count, blocks, rows, cols = parts.shape

    def body(parts_ref, out_ref):
        out_ref[0] = jnp.sum(parts_ref[:, 0].astype(f32), 0).astype(bf16)

    return pl.pallas_call(
        after_inputs(body, 1, len(after)),
        out_shape=jax.ShapeDtypeStruct((blocks, rows, cols), bf16),
        grid=(blocks,),
        in_specs=[pl.BlockSpec((count, 1, rows, cols), lambda i: (0, i, 0, 0))]
        + anywhere(len(after)),
        out_specs=pl.BlockSpec((1, rows, cols), lambda i: (i, 0, 0)),
        compiler_params=kernel_params(),
        cost_estimate=COST,
        name="summed",
    )(parts, *after)


def sorted_weight(pieces, spots):
    rows, cols = pieces[0][0].shape[1:]
    count = len(pieces)

    def body(spot_ref, *refs):
        out_ref, sems = refs[count], refs[count + 1]
        copies = []
        for at, (array, first, spot) in enumerate(pieces):
            target = out_ref.at[pl.ds(first, array.shape[0]), spot_ref[spot]]
            copies.append(pltpu.make_async_copy(refs[at], target, sems.at[at]))
        for copy in copies:
            copy.start()
        for copy in copies:
            copy.wait()

    return pl.pallas_call(
        body,
        out_shape=jax.ShapeDtypeStruct((8, 8, rows, cols), bf16),
        grid_spec=pltpu.PrefetchScalarGridSpec(
            num_scalar_prefetch=1,
            grid=(1,),
            in_specs=anywhere(count),
            out_specs=pl.BlockSpec(memory_space=pl.ANY),
            scratch_shapes=[pltpu.SemaphoreType.DMA((count,))],
        ),
        compiler_params=kernel_params(),
        cost_estimate=COST,
        name="sorted_weight",
    )(spots, *[piece[0] for piece in pieces]).reshape(64 * rows, cols)


def late_grads(active, attended, dy, numbers):
    piece_rows, width = dy[0].shape
    count = len(dy)

    def body(number_ref, act_ref, ol_ref, *refs):
        keep_ref, send_ref, sum_ref, dy_ref, sems = refs[count:]
        step = pl.program_id(0)
        first = number_ref[0] == 0

        @pl.when(step == 0)
        def _():
            fetch(refs[:count], dy_ref, sems, piece_rows)
            own = dy_ref[:, pl.ds(pl.multiple_of(number_ref[1] * 256, 256), 256)]
            sum_ref[...] = jnp.sum(own.astype(f32), 0, keepdims=True)

        @pl.when(step < 4)
        def _():
            part = dot_rows(act_ref[...], dy_ref[...]).astype(bf16).reshape(2, 2, 64, width)
            at = pl.ds(step * 2, 2)

            @pl.when(first)
            def _():
                keep_ref[at, 0:64] = part[:, 0]
                send_ref[at, 0:64] = part[:, 1]

            @pl.when(jnp.logical_not(first))
            def _():
                keep_ref[at, 0:64] = part[:, 1]
                send_ref[at, 0:64] = part[:, 0]

        @pl.when(step == 4)
        def _():
            part = dot_rows(ol_ref[...], dy_ref[...]).astype(bf16).reshape(8, 2, 16, width)

            @pl.when(first)
            def _():
                keep_ref[:, 64:80] = part[:, 0]
                send_ref[:, 64:80] = part[:, 1]

            @pl.when(jnp.logical_not(first))
            def _():
                keep_ref[:, 64:80] = part[:, 1]
                send_ref[:, 64:80] = part[:, 0]

    rows = active.shape[0]
    out = jax.ShapeDtypeStruct((8, 80, width), bf16)
    whole = pl.BlockSpec((8, 80, width), lambda i, core: (0, 0, 0))
    keep, send, sums = pl.pallas_call(
        body,
        out_shape=(out, out, jax.ShapeDtypeStruct((1, 256), f32)),
        grid_spec=pltpu.PrefetchScalarGridSpec(
            num_scalar_prefetch=1,
            grid=(5,),
            in_specs=[
                pl.BlockSpec((rows, 256), lambda i, core: (0, jnp.minimum(i, 3))),
                pl.BlockSpec((rows, 256), lambda i, core: (0, 0)),
            ]
            + anywhere(count),
            out_specs=(whole, whole, pl.BlockSpec((1, 256), lambda i, core: (0, 0))),
            scratch_shapes=[
                pltpu.VMEM((rows, width), bf16),
                pltpu.SemaphoreType.DMA((count,)),
            ],
        ),
        compiler_params=kernel_params(),
        cost_estimate=COST,
        name="late_grads",
    )(numbers, active, attended, *dy)
    return keep, send, sums


def early_grads(h1, h2, d_qkv, d_hidden, numbers, after):
    rows, width = h1.shape
    n1, n2 = d_qkv.shape[1], d_hidden.shape[1]

    def body(core_ref, h1_ref, h2_ref, dq_ref, du_ref, keep_ref, send_ref):
        first = core_ref[0] == 0
        left = dot_rows(h1_ref[...], dq_ref[...]).astype(bf16).reshape(4, 2, 2, 16, n1)
        right = dot_rows(h2_ref[...], du_ref[...]).astype(bf16).reshape(4, 2, 2, 16, n2)

        @pl.when(first)
        def _():
            keep_ref[:, :, 0, :, 0:n1] = left[:, :, 0]
            keep_ref[:, :, 0, :, n1:] = right[:, :, 0]
            send_ref[:, :, 0, :, 0:n1] = left[:, :, 1]
            send_ref[:, :, 0, :, n1:] = right[:, :, 1]

        @pl.when(jnp.logical_not(first))
        def _():
            keep_ref[:, :, 0, :, 0:n1] = left[:, :, 1]
            keep_ref[:, :, 0, :, n1:] = right[:, :, 1]
            send_ref[:, :, 0, :, 0:n1] = left[:, :, 0]
            send_ref[:, :, 0, :, n1:] = right[:, :, 0]

    out = jax.ShapeDtypeStruct((4, 2, 8, 16, n1 + n2), bf16)
    block = pl.BlockSpec((4, 2, 1, 16, n1 + n2), lambda i, core: (0, 0, i, 0, 0))
    return pl.pallas_call(
        after_inputs(body, 5, len(after)),
        out_shape=(out, out),
        grid_spec=pltpu.PrefetchScalarGridSpec(
            num_scalar_prefetch=1,
            grid=(8,),
            in_specs=[
                pl.BlockSpec((rows, width // 8), lambda i, core: (0, i)),
                pl.BlockSpec((rows, width // 8), lambda i, core: (0, i)),
                pl.BlockSpec((rows, n1), lambda i, core: (0, 0)),
                pl.BlockSpec((rows, n2), lambda i, core: (0, 0)),
            ]
            + anywhere(len(after)),
            out_specs=(block, block),
        ),
        compiler_params=kernel_params(),
        cost_estimate=COST,
        name="early_grads",
    )(numbers, h1, h2, d_qkv, d_hidden, *after)


def late_outputs(groups, spots):
    width = groups[0].shape[-1]

    def body(spot_ref, *refs):
        ins, down_ref, out_ref = refs[:4], refs[4], refs[5]
        step = pl.program_id(0)
        for at, ref in enumerate(ins):

            @pl.when(step // 4 == at)
            def _(ref=ref):
                down_ref[...] = ref[0, 0:64].astype(f32)
                out_ref[...] = ref[0, 64:80].astype(f32)

    def chosen(at):
        return pl.BlockSpec(
            (1, 80, width), lambda i, spot: (jnp.clip(i - 4 * at, 0, 3), 0, 0)
        )

    return pl.pallas_call(
        body,
        out_shape=(
            jax.ShapeDtypeStruct((1024, width), f32),
            jax.ShapeDtypeStruct((256, width), f32),
        ),
        grid_spec=pltpu.PrefetchScalarGridSpec(
            num_scalar_prefetch=1,
            grid=(16,),
            in_specs=[chosen(at) for at in range(4)],
            out_specs=(
                pl.BlockSpec((64, width), lambda i, spot: (spot[i], 0)),
                pl.BlockSpec((16, width), lambda i, spot: (spot[i], 0)),
            ),
        ),
        compiler_params=kernel_params(),
        cost_estimate=COST,
        name="late_outputs",
    )(spots, *groups)


def early_outputs(mine, yours, spots, n1):
    cols = mine.shape[-1]
    n2 = cols - n1
    head = n1 // 3

    def body(spot_ref, mine_ref, yours_ref, qkv_ref, up_ref):
        step = pl.program_id(0)

        def put(ref):
            for source in range(8):
                for third in range(3):
                    at = (third * 8 + source) * head
                    qkv_ref[:, at : at + head] = ref[
                        0, source, :, third * head : (third + 1) * head
                    ].astype(f32)
                up_ref[:, source * n2 : (source + 1) * n2] = ref[0, source, :, n1:].astype(f32)

        @pl.when(step < 8)
        def _():
            put(mine_ref)

        @pl.when(step >= 8)
        def _():
            put(yours_ref)

    block = (1, 8, 16, cols)
    return pl.pallas_call(
        body,
        out_shape=(
            jax.ShapeDtypeStruct((256, 8 * n1), f32),
            jax.ShapeDtypeStruct((256, 8 * n2), f32),
        ),
        grid_spec=pltpu.PrefetchScalarGridSpec(
            num_scalar_prefetch=1,
            grid=(16,),
            in_specs=[
                pl.BlockSpec(block, lambda i, spot: (jnp.minimum(i, 7), 0, 0, 0)),
                pl.BlockSpec(block, lambda i, spot: (jnp.maximum(i - 8, 0), 0, 0, 0)),
            ],
            out_specs=(
                pl.BlockSpec((16, 8 * n1), lambda i, spot: (spot[i], 0)),
                pl.BlockSpec((16, 8 * n2), lambda i, spot: (spot[i], 0)),
            ),
        ),
        compiler_params=kernel_params(),
        cost_estimate=COST,
        name="early_outputs",
    )(spots, mine, yours)


def local(
    tokens,
    doc_lengths,
    cotangent,
    ln1_gain,
    ln1_bias,
    ln2_gain,
    ln2_bias,
    qkv_weight,
    qkv_bias,
    out_weight,
    out_bias,
    up_weight,
    up_bias,
    down_weight,
    down_bias,
):
    rows, width = tokens.shape
    head = width // HEADS
    group = 8
    rep = lax.axis_index("rep")
    shard = lax.axis_index("shard")
    y, h, c = rep // 4, (rep // 2) % 2, rep % 2
    l, x = shard // 4, shard % 4
    ff = up_bias.shape[0]

    x_below, x_above = move(tokens, x=1), move(tokens, x=-1)
    x_other = move(tokens, l=1)
    x_other_below, x_other_above = move(x_other, x=1), move(x_other, x=-1)
    x_far, x_other_far = move(x_below, x=1), move(x_other_below, x=1)
    dy_other = move(cotangent, l=1)
    dy_below, dy_above = move(cotangent, x=1), move(cotangent, x=-1)
    dy_other_below, dy_other_above = move(dy_other, x=1), move(dy_other, x=-1)
    dy_far, dy_other_far = move(dy_above, x=-1), move(dy_other_above, x=-1)
    x_all = (tokens, x_above, x_far, x_below, x_other, x_other_above, x_other_far, x_other_below)
    dy_all = (
        cotangent,
        dy_above,
        dy_far,
        dy_below,
        dy_other,
        dy_other_above,
        dy_other_far,
        dy_other_below,
    )

    vectors = jnp.concatenate([ln1_gain, ln1_bias, ln2_gain, ln2_bias, qkv_bias])[None]
    place = (y * 2 + c).astype(jnp.int32).reshape(1)
    part = packed(qkv_weight, up_weight, vectors, doc_lengths, place, head)
    part = lax.all_to_all(part, "shard", 0, 0)
    cols = part.shape[-1]
    own, infos = unpacked(part, (x_other, x_below, x_above))
    below, above = move(own, y=1), move(own, y=-1)
    far_low, far_high = move(below[:4], y=1), move(above[4:], y=-1)
    mine = ((own, 0, 0), (above, 0, 1), (far_low, 0, 2), (far_high, 4, 2), (below, 0, 3))
    yours = tuple((move(array, c=1), first, spot + 4) for array, first, spot in mine)
    steps4 = (y + jnp.arange(4)) % 4
    spots = jnp.concatenate([steps4 * 2 + c, steps4 * 2 + 1 - c]).astype(jnp.int32)
    w_mixed = sorted_weight(mine + yours, spots)

    gains = infos[:, 0, :1024].reshape(8, 4, 256).transpose(1, 0, 2).reshape(4, width)
    qkv_b = infos[:, 0, 1024:].reshape(8 * 3, 1, head)
    qkv_b = jnp.stack(
        [lax.dynamic_index_in_dim(qkv_b, third * 8 + shard, 0, False) for third in range(3)]
    )
    steps8 = jnp.arange(8)
    sources = ((steps8 // 4) ^ l) * 4 + (x + steps8 % 4) % 4
    lengths = infos[:, 1, :3]
    lengths = jnp.sum(
        jnp.where(sources[:, None, None] == steps8[None, :, None], lengths[None], 0.0), 1
    ).astype(jnp.int32)
    ends = jnp.cumsum(lengths, 1)
    starts = ends - lengths
    steps_t = jnp.arange(rows, dtype=jnp.int32)
    segment = jnp.sum((steps_t[None, :, None] >= ends[:, None, :]).astype(jnp.int32), -1)
    slots = jnp.arange(lengths.shape[1], dtype=jnp.int32)
    begin = jnp.sum(
        jnp.where(segment[:, :, None] == slots[None, None, :], starts[:, None, :], 0), -1
    )
    position = (steps_t[None, :] - begin).astype(f32).reshape(group * rows, 1)
    lane = jnp.arange(128)
    freq = 10000.0 ** (-2.0 * (lane % (ROT // 2)).astype(f32) / ROT)
    angle = position * freq[None, :]
    cosine = jnp.where(lane < ROT, jnp.cos(angle), 1.0)
    sine = jnp.sin(angle)
    sine = jnp.where(lane < ROT // 2, -sine, jnp.where(lane < ROT, sine, 0.0))

    x_rows, h1, h2, mean, inverse = norms(x_all, gains)
    active, slope = hidden_part(h2, w_mixed, 3 * head // 256, up_bias.astype(f32)[None])
    qkv, probs, attended = attention(h1, w_mixed, qkv_b, cosine, sine, lengths)
    both_bias = (out_bias.astype(f32) + down_bias.astype(f32))[None, :]
    wide_bias = lax.dynamic_update_slice(jnp.zeros((1, width), f32), both_bias, (0, shard * 256))
    numbers = jnp.stack([c, shard]).astype(jnp.int32)

    late_keep, late_send, dy_sums = late_grads(active, attended, dy_all, numbers)
    late_got = move(late_send, c=1)
    d_hidden, up_b, d_qkv, qkv_bg = back_inner(
        dy_all, down_weight, out_weight, slope, qkv, probs, cosine, sine, (late_send,)
    )
    late = (late_keep.astype(f32) + late_got.astype(f32)).astype(bf16)
    early_keep, early_send = early_grads(h1, h2, d_qkv, d_hidden, numbers, (late,))
    early_got = move(early_send, c=1)
    late = lax.all_to_all(late, "rep", 0, 0, axis_index_groups=SAME_CORE)
    norm_sums, *sums = back_norms(
        d_qkv,
        d_hidden,
        w_mixed,
        x_rows,
        mean,
        inverse,
        jnp.stack([gains[0], gains[2]]),
        (early_send,),
    )
    late = summed(late[:, None], (sums[0],))[0]
    early = added(early_keep.reshape(8, 128, cols), early_got.reshape(8, 128, cols), (late,))
    early = early.reshape(64, 16, cols)
    mix = mixed_part(active, attended, down_weight, out_weight, wide_bias, (early, sums[0]))
    early = lax.all_to_all(early, BOTH, 0, 0, axis_index_groups=SAME_CORE_ALL)

    def ring(at):
        mix_low = move(mix[at + 2], x=1)
        sum_high = move(sums[at + 2], x=-1)
        mix_above = (mix[at + 1].astype(f32) + mix_low.astype(f32)).astype(bf16)
        sum_below = (sums[at + 3].astype(f32) + sum_high.astype(f32)).astype(bf16)
        mix_total = (
            mix[at].astype(f32)
            + move(mix_above, x=1).astype(f32)
            + move(mix[at + 3], x=-1).astype(f32)
        )
        sum_total = (
            sums[at].astype(f32)
            + move(sums[at + 1], x=1).astype(f32)
            + move(sum_below, x=-1).astype(f32)
        )
        return mix_total, sum_total

    mix_other, sum_other = (move(v.astype(bf16), l=1).astype(f32) for v in ring(4))
    mix_own, sum_own = ring(0)
    mixed = (tokens.astype(f32) + mix_own + mix_other).astype(bf16)
    own_sum = sum_own + sum_other
    own_normed, own_inverse = normalize(tokens)
    tokens_grad = cotangent.astype(f32) + own_inverse * (
        own_sum
        - jnp.mean(own_sum, -1, keepdims=True)
        - own_normed * jnp.mean(own_sum * own_normed, -1, keepdims=True)
    )

    dy_own = dy_sums.reshape(256)
    wide_qkv = lax.dynamic_update_slice(
        jnp.zeros((3, 8, head), f32), qkv_bg.reshape(3, 1, head), (0, shard, 0)
    )
    wide_up = lax.dynamic_update_slice(jnp.zeros((8 * ff,), f32), up_b.reshape(-1), (shard * ff,))
    wide_dy = lax.dynamic_update_slice(jnp.zeros((width,), f32), dy_own, (shard * 256,))
    smalls = jnp.concatenate([norm_sums.reshape(-1), wide_dy, wide_qkv.reshape(-1), wide_up])
    smalls = smalls.reshape(-1, 1024)
    for axis, bit in (("c", 1), ("l", 1), ("h", 1), ("x", 1), ("y", 1), ("x", 2), ("y", 2)):
        smalls = smalls + swap(smalls, axis, bit)
    smalls = smalls.reshape(-1)

    def small_at(start, size):
        return lax.dynamic_slice_in_dim(smalls, start + shard * size, size)

    late = jnp.stack(ring_gather(late, "y", 40))
    late_h = move(late, h=1)
    late_c = move(late, c=1)
    late_hc = move(late_h, c=1)
    spots = [
        (steps4 * 2 + high) * 2 + low for high, low in ((h, c), (1 - h, c), (h, 1 - c), (1 - h, 1 - c))
    ]
    down_grad, out_grad = late_outputs(
        (late, late_h, late_c, late_hc), jnp.concatenate(spots).astype(jnp.int32)
    )

    early = summed(early.reshape(8, 8, 16, cols), (mix[0],))
    early = jnp.stack([early, move(early, h=1)])
    early = jnp.concatenate(ring_gather(early, "y", 1), 0)
    early_c = move(early, c=1)
    spots = [
        ((steps4[:, None] * 2 + jnp.stack([h, 1 - h])[None, :]) * 2 + low).reshape(8)
        for low in (c, 1 - c)
    ]
    qkv_grad, up_grad = early_outputs(
        early, early_c, jnp.concatenate(spots).astype(jnp.int32), 3 * head
    )

    dy_total = small_at(4 * width, 256)
    return (
        mixed,
        tokens_grad,
        small_at(0, 256),
        small_at(width, 256),
        small_at(2 * width, 256),
        small_at(3 * width, 256),
        qkv_grad,
        small_at(5 * width, 768),
        out_grad,
        dy_total,
        up_grad,
        small_at(8 * width, ff),
        down_grad,
        dy_total,
    )


def solution(mesh):
    rows = P(BOTH, None)
    vector, matrix = P("shard"), P("shard", None)
    return jax.shard_map(
        local,
        mesh=mesh,
        in_specs=(rows, rows, rows, vector, vector, vector, vector)
        + (matrix, vector, matrix, vector, matrix, vector, matrix, vector),
        out_specs=(rows, rows, vector, vector, vector, vector)
        + (matrix, vector, matrix, vector, matrix, vector, matrix, vector),
        check_vma=False,
    )
```

```python
import functools
import math

import jax
import jax.numpy as jnp
from jax import lax
from jax.experimental import pallas as pl
from jax.experimental.pallas import tpu as pltpu
from jax.sharding import PartitionSpec as P

HEADS = 8
ROT = 64
EPS = 1e-05
f32 = jnp.float32
bf16 = jnp.bfloat16


def cost(time):
    return pl.CostEstimate(flops=int(time * 1.15e9), bytes_accessed=1000, transcendentals=0)


BOTH = ("rep", "shard")
SIZES = (4, 2, 2, 2, 4)
SAME_CORE = [[2 * n + c for n in range(8)] for c in range(2)]
SAME_CORE_ALL = [[(2 * n + c) * 8 + s for n in range(8) for s in range(8)] for c in range(2)]


def coords():
    for y in range(4):
        for h in range(2):
            for c in range(2):
                for l in range(2):
                    for x in range(4):
                        yield (y, h, c, l, x)


def linear(t):
    y, h, c, l, x = (v % m for v, m in zip(t, SIZES))
    return ((y * 2 + h) * 2 + c) * 8 + l * 4 + x


def move(value, y=0, h=0, c=0, l=0, x=0):
    step = (y, h, c, l, x)
    pairs = [(linear(t), linear(tuple(a + b for a, b in zip(t, step)))) for t in coords()]
    return lax.ppermute(value, BOTH, pairs)


def swap(value, axis, bit):
    at = "yhclx".index(axis)
    pairs = [(linear(t), linear(t[:at] + (t[at] ^ bit,) + t[at + 1 :])) for t in coords()]
    return lax.ppermute(value, BOTH, pairs)


def pick(value, index, axis):
    return lax.dynamic_index_in_dim(value, index, axis, keepdims=False)


def ring_gather(own, axis, cut):
    below = move(own, **{axis: 1})
    above = move(own, **{axis: -1})
    far_low = move(below[:cut], **{axis: 1})
    far_high = move(above[cut:], **{axis: -1})
    return [own, above, jnp.concatenate([far_low, far_high], 0), below]


def ring_reduce(pieces, axis, cut):
    own, above, far, below = pieces
    low = move(far[:cut].astype(bf16), **{axis: 1})
    high = move(far[cut:].astype(bf16), **{axis: -1})
    up = jnp.concatenate([above[:cut].astype(f32) + low.astype(f32), above[cut:].astype(f32)], 0)
    down = jnp.concatenate([below[:cut].astype(f32), below[cut:].astype(f32) + high.astype(f32)], 0)
    from_below = move(up.astype(bf16), **{axis: 1})
    from_above = move(down.astype(bf16), **{axis: -1})
    return own.astype(f32) + from_below.astype(f32) + from_above.astype(f32)


def normalize(value):
    xf = value.astype(f32)
    centre = xf - jnp.mean(xf, -1, keepdims=True)
    inverse = lax.rsqrt(jnp.mean(centre * centre, -1, keepdims=True) + EPS)
    return centre * inverse, inverse


def kernel_params():
    return pltpu.CompilerParams(vmem_limit_bytes=56 * 1024 * 1024)


def after_inputs(body, count, extra):
    return lambda *refs: body(*refs[:count], *refs[count + extra :])


def anywhere(count):
    return [pl.BlockSpec(memory_space=pl.ANY)] * count


def dot(a, b, ca=1, cb=0):
    return lax.dot_general(a, b, (((ca,), (cb,)), ((), ())), preferred_element_type=f32)


def hidden_part(h2, weight, first, bias):
    rows, width = h2.shape
    ff = bias.shape[1]

    def body(h_ref, w_ref, b_ref, act_ref, slope_ref):
        u = dot(h_ref[...], w_ref[...]) + b_ref[...]
        cdf = 0.5 * (1.0 + lax.erf(u * math.sqrt(0.5)))
        pdf = jnp.exp(-0.5 * u * u) * (1.0 / math.sqrt(2.0 * math.pi))
        act_ref[...] = (u * cdf).astype(bf16)
        slope_ref[...] = cdf + u * pdf

    return pl.pallas_call(
        body,
        out_shape=(
            jax.ShapeDtypeStruct((rows, ff), bf16),
            jax.ShapeDtypeStruct((rows, ff), f32),
        ),
        grid=(ff // 256,),
        in_specs=[
            pl.BlockSpec((rows, width), lambda i: (0, 0)),
            pl.BlockSpec((width, 256), lambda i: (0, i + first)),
            pl.BlockSpec((1, 256), lambda i: (0, i)),
        ],
        out_specs=(
            pl.BlockSpec((rows, 256), lambda i: (0, i)),
            pl.BlockSpec((rows, 256), lambda i: (0, i)),
        ),
        compiler_params=kernel_params(),
        cost_estimate=cost(10),
        name="hidden_part",
    )(h2, weight, bias)


def swap_halves(value):
    lane = lax.broadcasted_iota(jnp.int32, value.shape, 1)
    return jnp.where(lane < 32, pltpu.roll(value, 96, 1), pltpu.roll(value, 32, 1))


def allowed_mask(lengths_ref, block, rows):
    e0 = lengths_ref[block, 0]
    e1 = e0 + lengths_ref[block, 1]
    t = lax.broadcasted_iota(jnp.int32, (rows, rows), 0)
    s = lax.broadcasted_iota(jnp.int32, (rows, rows), 1)
    seg_t = (t >= e0).astype(jnp.int32) + (t >= e1).astype(jnp.int32)
    seg_s = (s >= e0).astype(jnp.int32) + (s >= e1).astype(jnp.int32)
    return (seg_t == seg_s) & (s <= t)


def attention(h1, weight, bias, cosine, sine, lengths, after, rows=128, head=256):
    total, width = h1.shape
    blocks = total // rows
    scale = head ** (-0.5)

    def body(len_ref, h_ref, w_ref, b_ref, cos_ref, sin_ref, qkv_ref, p_ref, o_ref, work):
        step = pl.program_id(0)

        @pl.when(step < 3)
        def _():
            work[step] = dot(h_ref[...], w_ref[...]) + b_ref[0]

        @pl.when(step >= 3)
        def _():
            block = step - 3
            at = pl.ds(block * rows, rows)
            cos, sin = cos_ref[...], sin_ref[...]

            def turned(value):
                left = value[:, :128]
                left = left * cos + swap_halves(left) * sin
                return jnp.concatenate([left, value[:, 128:]], 1).astype(bf16)

            q, k = turned(work[0, at, :]), turned(work[1, at, :])
            v = work[2, at, :].astype(bf16)
            qkv_ref[:, 0:head] = q
            qkv_ref[:, head : 2 * head] = k
            qkv_ref[:, 2 * head :] = v
            scores = dot(q, k, 1, 1) * scale
            masked = jnp.where(allowed_mask(len_ref, block, rows), scores, -1e30)
            shifted = jnp.exp(masked - jnp.max(masked, 1, keepdims=True))
            probs = shifted / jnp.sum(shifted, 1, keepdims=True)
            p_ref[...] = probs
            o_ref[...] = dot(probs.astype(bf16), v).astype(bf16)

    def at_block(i, lens):
        return (jnp.maximum(i - 3, 0), 0)

    return pl.pallas_call(
        after_inputs(body, 6, len(after)),
        out_shape=(
            jax.ShapeDtypeStruct((total, 3 * head), bf16),
            jax.ShapeDtypeStruct((total, rows), f32),
            jax.ShapeDtypeStruct((total, head), bf16),
        ),
        grid_spec=pltpu.PrefetchScalarGridSpec(
            num_scalar_prefetch=1,
            grid=(3 + blocks,),
            in_specs=[
                pl.BlockSpec((total, width), lambda i, lens: (0, 0)),
                pl.BlockSpec((width, head), lambda i, lens: (0, jnp.minimum(i, 2))),
                pl.BlockSpec((1, 1, head), lambda i, lens: (jnp.minimum(i, 2), 0, 0)),
                pl.BlockSpec((rows, 128), at_block),
                pl.BlockSpec((rows, 128), at_block),
            ]
            + anywhere(len(after)),
            out_specs=(
                pl.BlockSpec((rows, 3 * head), at_block),
                pl.BlockSpec((rows, rows), at_block),
                pl.BlockSpec((rows, head), at_block),
            ),
            scratch_shapes=[pltpu.VMEM((3, total, head), f32)],
        ),
        compiler_params=kernel_params(),
        cost_estimate=cost(14),
        name="attention",
    )(lengths, h1, weight, bias, cosine, sine, *after)


def mixed_part(active, attended, down, out, bias, sources, after):
    rows, ff = active.shape
    head, width = out.shape

    def body(source_ref, act_ref, ol_ref, wd_ref, wo_ref, b_ref, mix_ref):
        total = dot(act_ref[...], wd_ref[...]) + dot(ol_ref[...], wo_ref[...]) + b_ref[...]
        total = total.astype(bf16)
        for at in range(rows // 128):
            to = pl.ds(pl.multiple_of(source_ref[at] * 128, 128), 128)
            mix_ref[to, :] = total[at * 128 : (at + 1) * 128]

    return pl.pallas_call(
        after_inputs(body, 6, len(after)),
        out_shape=jax.ShapeDtypeStruct((rows, width), bf16),
        grid_spec=pltpu.PrefetchScalarGridSpec(
            num_scalar_prefetch=1,
            grid=(width // 256,),
            in_specs=[
                pl.BlockSpec((rows, ff), lambda i, n: (0, 0)),
                pl.BlockSpec((rows, head), lambda i, n: (0, 0)),
                pl.BlockSpec((ff, 256), lambda i, n: (0, i)),
                pl.BlockSpec((head, 256), lambda i, n: (0, i)),
                pl.BlockSpec((1, 256), lambda i, n: (0, i)),
            ]
            + anywhere(len(after)),
            out_specs=pl.BlockSpec((rows, 256), lambda i, n: (0, i)),
        ),
        compiler_params=kernel_params(),
        cost_estimate=cost(11),
        name="mixed_part",
    )(sources, active, attended, down, out, bias, *after)


def inner_grad(dy, down, slope, after):
    rows, width = dy[0].shape[1:]
    count = len(dy)
    total = count * rows
    ff = down.shape[0]

    def body(*refs):
        wd_ref, s_ref, du_ref, db_ref, dy_ref, sems = refs[count:]

        @pl.when(pl.program_id(0) == 0)
        def _():
            fetch(refs[:count], dy_ref, sems, rows)

        du = (dot(dy_ref[...], wd_ref[...], 1, 1) * s_ref[...]).astype(bf16)
        du_ref[...] = du
        db_ref[...] = jnp.sum(du.astype(f32), 0, keepdims=True)

    return pl.pallas_call(
        after_inputs(body, count + 2, len(after)),
        out_shape=(
            jax.ShapeDtypeStruct((total, ff), bf16),
            jax.ShapeDtypeStruct((1, ff), f32),
        ),
        grid=(ff // 256,),
        in_specs=anywhere(count)
        + [
            pl.BlockSpec((256, width), lambda i: (i, 0)),
            pl.BlockSpec((total, 256), lambda i: (0, i)),
        ]
        + anywhere(len(after)),
        out_specs=(
            pl.BlockSpec((total, 256), lambda i: (0, i)),
            pl.BlockSpec((1, 256), lambda i: (0, i)),
        ),
        scratch_shapes=[
            pltpu.VMEM((total, width), bf16),
            pltpu.SemaphoreType.DMA((count,)),
        ],
        compiler_params=kernel_params(),
        cost_estimate=cost(8),
        name="inner_grad",
    )(*dy, down, slope, *after)


def back_norms(d_qkv, d_hidden, weight, tokens, mean, inverse, gains, after):
    total, n1 = d_qkv.shape
    n2 = d_hidden.shape[1]
    width = tokens.shape[1]
    count = total // 128

    def body(dq_ref, du_ref, w_ref, x_ref, m_ref, i_ref, g_ref, sums_ref, *refs):
        d1 = dot(dq_ref[...], w_ref[:, :n1], 1, 1)
        d2 = dot(du_ref[...], w_ref[:, n1:], 1, 1)
        normed = (x_ref[...].astype(f32) - m_ref[...]) * i_ref[...]
        both = (d1 * g_ref[0:1] + d2 * g_ref[1:2]).astype(bf16)
        for at in range(count):
            refs[at][...] = both[at * 128 : (at + 1) * 128]
        sums_ref[0:1] = jnp.sum(d1 * normed, 0, keepdims=True)
        sums_ref[1:2] = jnp.sum(d1, 0, keepdims=True)
        sums_ref[2:3] = jnp.sum(d2 * normed, 0, keepdims=True)
        sums_ref[3:4] = jnp.sum(d2, 0, keepdims=True)

    return pl.pallas_call(
        after_inputs(body, 7, len(after)),
        out_shape=(jax.ShapeDtypeStruct((4, width), f32),)
        + (jax.ShapeDtypeStruct((128, width), bf16),) * count,
        grid=(width // 256,),
        in_specs=[
            pl.BlockSpec((total, n1), lambda i: (0, 0)),
            pl.BlockSpec((total, n2), lambda i: (0, 0)),
            pl.BlockSpec((256, n1 + n2), lambda i: (i, 0)),
            pl.BlockSpec((total, 256), lambda i: (0, i)),
            pl.BlockSpec((total, 1), lambda i: (0, 0)),
            pl.BlockSpec((total, 1), lambda i: (0, 0)),
            pl.BlockSpec((2, 256), lambda i: (0, i)),
        ]
        + anywhere(len(after)),
        out_specs=(pl.BlockSpec((4, 256), lambda i: (0, i)),)
        + (pl.BlockSpec((128, 256), lambda i: (0, i)),) * count,
        compiler_params=kernel_params(),
        cost_estimate=cost(15),
        name="back_norms",
    )(d_qkv, d_hidden, weight, tokens, mean, inverse, gains, *after)


def norms(pieces, gains):
    rows, width = pieces[0].shape[1:]
    count = len(pieces)
    total = rows * count

    def body(*refs):
        g_ref, x_ref, h1_ref, h2_ref, m_ref, i_ref = refs[count:]
        for at in range(count):

            @pl.when(pl.program_id(0) == at)
            def _(at=at):
                x_ref[...] = refs[at][0]

        x = x_ref[...].astype(f32)
        mean = jnp.mean(x, 1, keepdims=True)
        centre = x - mean
        inverse = lax.rsqrt(jnp.mean(centre * centre, 1, keepdims=True) + EPS)
        normed = centre * inverse
        m_ref[...] = mean
        i_ref[...] = inverse
        h1_ref[...] = (normed * g_ref[0:1] + g_ref[1:2]).astype(bf16)
        h2_ref[...] = (normed * g_ref[2:3] + g_ref[3:4]).astype(bf16)

    column = jax.ShapeDtypeStruct((total, 1), f32)
    wide = jax.ShapeDtypeStruct((total, width), bf16)
    block = pl.BlockSpec((rows, width), lambda i: (i, 0))
    thin = pl.BlockSpec((rows, 1), lambda i: (i, 0))
    return pl.pallas_call(
        body,
        out_shape=(wide, wide, wide, column, column),
        grid=(count,),
        in_specs=[pl.BlockSpec((1, rows, width), lambda i: (0, 0, 0))] * count
        + [pl.BlockSpec((4, width), lambda i: (0, 0))],
        out_specs=(block, block, block, thin, thin),
        compiler_params=kernel_params(),
        cost_estimate=cost(9),
        name="norms",
    )(*pieces, gains)


def fetch(pieces, target, sems, rows):
    copies = [
        pltpu.make_async_copy(
            piece.at[1] if len(piece.shape) == 3 else piece,
            target.at[pl.ds(at * rows, rows)],
            sems.at[at],
        )
        for at, piece in enumerate(pieces)
    ]
    for copy in copies:
        copy.start()
    for copy in copies:
        copy.wait()


def dot_rows(a, b):
    return lax.dot_general(a, b, (((0,), (0,)), ((), ())), preferred_element_type=f32)


def packed(qkv_weight, up_weight, vectors, lengths, place, head):
    wide, up_wide = qkv_weight.shape[1], up_weight.shape[1]
    part, up_part = 3 * head, up_wide // 8
    cols = part + up_part

    def body(place_ref, len_ref, q_ref, u_ref, v_ref, out_ref):
        lane = lax.broadcasted_iota(jnp.int32, (8, cols), 1)
        row = lax.broadcasted_iota(jnp.int32, (8, cols), 0)
        sizes = jnp.zeros((8, cols), f32)
        for at in range(3):
            sizes = jnp.where(lane == at, len_ref[0, at].astype(f32), sizes)
        vector = jnp.broadcast_to(v_ref[...].astype(f32), (8, cols))
        tail = jnp.where(row == 0, vector, jnp.where(row == 1, sizes, 0.0)).astype(bf16)
        for owner in range(8):
            pieces = [
                q_ref[:, (third * 8 + owner) * head : (third * 8 + owner + 1) * head]
                for third in range(3)
            ]
            pieces.append(u_ref[:, owner * up_part : (owner + 1) * up_part])
            out_ref[owner] = jnp.concatenate([jnp.concatenate(pieces, 1), tail], 0)

    return pl.pallas_call(
        body,
        out_shape=jax.ShapeDtypeStruct((8, 40, cols), bf16),
        grid_spec=pltpu.PrefetchScalarGridSpec(
            num_scalar_prefetch=2,
            grid=(1,),
            in_specs=[
                pl.BlockSpec((32, wide), lambda i, place, lens: (place[0], 0)),
                pl.BlockSpec((32, up_wide), lambda i, place, lens: (place[0], 0)),
                pl.BlockSpec((1, cols), lambda i, place, lens: (0, 0)),
            ],
            out_specs=pl.BlockSpec((8, 40, cols), lambda i, place, lens: (0, 0, 0)),
        ),
        compiler_params=kernel_params(),
        cost_estimate=cost(3),
        name="packed",
    )(place, lengths, qkv_weight, up_weight, vectors)


def sorted_weight(pieces, spots):
    rows, cols = pieces[0][0].shape[1:]
    count = len(pieces)

    def body(spot_ref, *refs):
        step = pl.program_id(0)
        for ref, (array, first, at) in zip(refs, pieces):

            @pl.when(step == at)
            def _(ref=ref, first=first, size=array.shape[0]):
                refs[count][first : first + size, 0] = ref[...]

    return pl.pallas_call(
        body,
        out_shape=jax.ShapeDtypeStruct((8, 8, rows, cols), bf16),
        grid_spec=pltpu.PrefetchScalarGridSpec(
            num_scalar_prefetch=1,
            grid=(8,),
            in_specs=[
                pl.BlockSpec(array.shape, lambda i, spot: (0, 0, 0)) for array, _, _ in pieces
            ],
            out_specs=pl.BlockSpec((8, 1, rows, cols), lambda i, spot: (0, spot[i], 0, 0)),
        ),
        compiler_params=kernel_params(),
        cost_estimate=cost(6),
        name="sorted_weight",
    )(spots, *[piece[0] for piece in pieces]).reshape(64 * rows, cols)


def split(part, first, keep_ref, send_ref, index):
    @pl.when(first)
    def _():
        keep_ref[index] = part[:, 0]
        send_ref[index] = part[:, 1]

    @pl.when(jnp.logical_not(first))
    def _():
        keep_ref[index] = part[:, 1]
        send_ref[index] = part[:, 0]


def inner_weight_grads(active, h2, dy, d_hidden, numbers):
    piece_rows, width = dy[0].shape[1:]
    count = len(dy)
    rows, ff = active.shape
    downs = ff // 256

    def body(number_ref, act_ref, h2_ref, du_ref, *refs):
        keep_ref, send_ref, sum_ref, dy_ref, sems = refs[count:]
        step = pl.program_id(0)
        first = number_ref[0] == 0

        @pl.when(step == 0)
        def _():
            fetch(refs[:count], dy_ref, sems, piece_rows)
            own = dy_ref[:, pl.ds(pl.multiple_of(number_ref[1] * 256, 256), 256)]
            sum_ref[...] = jnp.sum(own.astype(f32), 0, keepdims=True)

        @pl.when(step < downs)
        def _():
            part = dot_rows(act_ref[...], dy_ref[...]).astype(bf16).reshape(2, 2, 64, width)
            split(part, first, keep_ref, send_ref, (pl.ds(step * 2, 2), pl.ds(0, 64)))

        for owner in range(8):

            @pl.when(step == downs + owner)
            def _(owner=owner):
                part = dot_rows(h2_ref[...], du_ref[...]).astype(bf16).reshape(8, 2, 16, ff)
                at = (slice(None), pl.ds(64 + 16 * (owner % 4), 16), pl.ds(owner // 4 * ff, ff))
                split(part, first, keep_ref, send_ref, at)

    out = jax.ShapeDtypeStruct((8, 128, width), bf16)
    whole = pl.BlockSpec((8, 128, width), lambda i, n: (0, 0, 0))
    return pl.pallas_call(
        body,
        out_shape=(out, out, jax.ShapeDtypeStruct((1, 256), f32)),
        grid_spec=pltpu.PrefetchScalarGridSpec(
            num_scalar_prefetch=1,
            grid=(downs + 8,),
            in_specs=[
                pl.BlockSpec((rows, 256), lambda i, n: (0, jnp.minimum(i, downs - 1))),
                pl.BlockSpec((rows, 256), lambda i, n: (0, jnp.maximum(i - downs, 0))),
                pl.BlockSpec((rows, ff), lambda i, n: (0, 0)),
            ]
            + anywhere(count),
            out_specs=(whole, whole, pl.BlockSpec((1, 256), lambda i, n: (0, 0))),
            scratch_shapes=[
                pltpu.VMEM((rows, width), bf16),
                pltpu.SemaphoreType.DMA((count,)),
            ],
        ),
        compiler_params=kernel_params(),
        cost_estimate=cost(16),
        name="inner_weight_grads",
    )(numbers, active, h2, d_hidden, *dy)


def attention_grads(dy, out, qkv, probs, cosine, sine, h1, attended, numbers, after, rows=128):
    width = dy[0].shape[2]
    count = len(dy)
    total = count * rows
    head = out.shape[0]
    blocks = total // rows
    scale = head ** (-0.5)

    def body(number_ref, *refs):
        wo_ref, qkv_ref, p_ref, cos_ref, sin_ref, h1_ref, ol_ref = refs[count : count + 7]
        dq_ref, dqb_ref, keep_ref, send_ref, d_att, dy_ref, sems = refs[count + 7 :]
        step = pl.program_id(0)
        first = number_ref[0] == 0

        @pl.when(step == 0)
        def _():
            fetch(refs[:count], dy_ref, sems, rows)
            d_att[...] = dot(dy_ref[...], wo_ref[...], 1, 1).astype(bf16)
            dqb_ref[...] = jnp.zeros_like(dqb_ref)
            part = dot_rows(ol_ref[...], dy_ref[...]).astype(bf16).reshape(8, 2, 16, width)
            split(part, first, keep_ref, send_ref, (slice(None), pl.ds(48, 16)))

        @pl.when((step > 0) & (step <= blocks))
        def _():
            at = pl.ds(pl.multiple_of((step - 1) * rows, rows), rows)
            cos, sin = cos_ref[...], sin_ref[...]
            q, k, v = (qkv_ref[:, n * head : (n + 1) * head] for n in range(3))
            probs = p_ref[...]
            d_out = d_att[at, :]
            d_value = dot(probs.astype(bf16), d_out, 0, 0)
            d_probs = dot(d_out, v, 1, 1)
            centred = d_probs - jnp.sum(d_probs * probs, 1, keepdims=True)
            d_scores = (probs * centred).astype(bf16)

            def back(value):
                value = value * scale
                left = value[:, :128]
                left = left * cos - swap_halves(left) * sin
                return jnp.concatenate([left, value[:, 128:]], 1).astype(bf16)

            for n, grad in enumerate(
                (back(dot(d_scores, k)), back(dot(d_scores, q, 0, 0)), d_value.astype(bf16))
            ):
                dq_ref[at, n * head : (n + 1) * head] = grad
                dqb_ref[:, n * head : (n + 1) * head] += jnp.sum(grad.astype(f32), 0, keepdims=True)

        for owner in range(8):

            @pl.when(step == blocks + 1 + owner)
            def _(owner=owner):
                part = dot_rows(h1_ref[...], dq_ref[...]).astype(bf16).reshape(8, 2, 16, 3 * head)
                for third in range(3):
                    at = (slice(None), pl.ds(16 * third, 16), pl.ds(owner * head, head))
                    split(
                        part[..., third * head : (third + 1) * head],
                        first,
                        keep_ref,
                        send_ref,
                        at,
                    )

    def at_block(i, n):
        return (jnp.clip(i - 1, 0, blocks - 1), 0)

    grads = jax.ShapeDtypeStruct((8, 64, width), bf16)

    def whole(*shape):
        return pl.BlockSpec(shape, lambda i, n: (0,) * len(shape))

    return pl.pallas_call(
        after_inputs(body, 8 + count, len(after)),
        out_shape=(
            jax.ShapeDtypeStruct((total, 3 * head), bf16),
            jax.ShapeDtypeStruct((1, 3 * head), f32),
            grads,
            grads,
        ),
        grid_spec=pltpu.PrefetchScalarGridSpec(
            num_scalar_prefetch=1,
            grid=(1 + blocks + 8,),
            in_specs=anywhere(count)
            + [
                whole(head, width),
                pl.BlockSpec((rows, 3 * head), at_block),
                pl.BlockSpec((rows, rows), at_block),
                pl.BlockSpec((rows, 128), at_block),
                pl.BlockSpec((rows, 128), at_block),
                pl.BlockSpec((total, 256), lambda i, n: (0, jnp.maximum(i - 1 - blocks, 0))),
                whole(total, head),
            ]
            + anywhere(len(after)),
            out_specs=(
                whole(total, 3 * head),
                whole(1, 3 * head),
                whole(8, 64, width),
                whole(8, 64, width),
            ),
            scratch_shapes=[
                pltpu.VMEM((total, head), bf16),
                pltpu.VMEM((total, width), bf16),
                pltpu.SemaphoreType.DMA((count,)),
            ],
        ),
        compiler_params=kernel_params(),
        cost_estimate=cost(20),
        name="attention_grads",
    )(numbers, *dy, out, qkv, probs, cosine, sine, h1, attended, *after)


def added(terms, groups, numbers, after):
    rows, cols = terms[0][0].shape[1:]
    firsts = [sum(groups[:n]) for n in range(len(groups))]

    def body(number_ref, *refs):
        step = pl.program_id(0)
        total = None
        for ref, (_, _, steps) in zip(refs, terms):
            value = ref[0].astype(f32)
            if steps is not None:
                counts = functools.reduce(jnp.logical_or, [step == at for at in steps])
                value = jnp.where(counts, value, 0.0)
            total = value if total is None else total + value
        total = total.astype(bf16)
        for ref, first, size in zip(refs[len(terms) :], firsts, groups):

            @pl.when((step >= first) & (step < first + size))
            def _(ref=ref):
                ref[0] = total

    def came(place):
        return pl.BlockSpec((1, rows, cols), lambda i, n: (place(i, n), 0, 0))

    def goes(first, size):
        return pl.BlockSpec((1, rows, cols), lambda i, n: (jnp.clip(i - first, 0, size - 1), 0, 0))

    return pl.pallas_call(
        after_inputs(body, 1 + len(terms), len(after)),
        out_shape=tuple(jax.ShapeDtypeStruct((size, rows, cols), bf16) for size in groups),
        grid_spec=pltpu.PrefetchScalarGridSpec(
            num_scalar_prefetch=1,
            grid=(sum(groups),),
            in_specs=[came(place) for _, place, _ in terms] + anywhere(len(after)),
            out_specs=tuple(goes(first, size) for first, size in zip(firsts, groups)),
        ),
        compiler_params=kernel_params(),
        cost_estimate=cost(4),
        name="added",
    )(numbers, *[term[0] for term in terms], *after)


def spread(pieces, spots, targets):
    rows, cols = pieces[0].shape[1:]
    firsts, total = [], 0
    for piece in pieces:
        firsts.append(total)
        total += piece.shape[0]

    def body(spot_ref, *refs):
        step = pl.program_id(0)
        for ref, first, piece in zip(refs, firsts, pieces):

            @pl.when((step >= first) & (step < first + piece.shape[0]))
            def _(ref=ref):
                for out_ref, (_, high, parts) in zip(refs[len(pieces) :], targets):
                    for to, row, col, size in parts:
                        out_ref[:, to : to + size] = ref[0, row : row + high, col : col + size].astype(
                            f32
                        )

    def chosen(first, size):
        return pl.BlockSpec(
            (1, rows, cols), lambda i, spot: (jnp.clip(i - first, 0, size - 1), 0, 0)
        )

    return pl.pallas_call(
        body,
        out_shape=tuple(
            jax.ShapeDtypeStruct((total * high, wide), f32) for wide, high, _ in targets
        ),
        grid_spec=pltpu.PrefetchScalarGridSpec(
            num_scalar_prefetch=1,
            grid=(total,),
            in_specs=[chosen(first, piece.shape[0]) for first, piece in zip(firsts, pieces)],
            out_specs=tuple(
                pl.BlockSpec((high, wide), lambda i, spot: (spot[i], 0))
                for wide, high, _ in targets
            ),
        ),
        compiler_params=kernel_params(),
        cost_estimate=cost(10),
        name="spread",
    )(spots, *pieces)


def small_sums(norm_sums, qkv_sums, up_sums, dy_sums, numbers):
    def body(number_ref, norm_ref, q_ref, u_ref, y_ref, out_ref, work):
        shard = number_ref[1]
        for owner in range(8):
            mine = shard == owner
            for n in range(4):
                for half in range(2):
                    at = owner * 256 + half * 128
                    work[owner, n * 2 + half : n * 2 + half + 1] = norm_ref[n : n + 1, at : at + 128]
            for n in range(3):
                third, source = divmod(owner * 3 + n, 8)
                for half in range(2):
                    at = third * 256 + half * 128
                    work[owner, 8 + n * 2 + half : 9 + n * 2 + half] = jnp.where(
                        shard == source, q_ref[:, at : at + 128], 0.0
                    )
            for n in range(8):
                work[owner, 14 + n : 15 + n] = jnp.where(
                    mine, u_ref[:, n * 128 : (n + 1) * 128], 0.0
                )
            for n in range(2):
                work[owner, 22 + n : 23 + n] = jnp.where(
                    mine, y_ref[:, n * 128 : (n + 1) * 128], 0.0
                )
        out_ref[0] = work[...].astype(bf16)

    def whole(*shape):
        return pl.BlockSpec(shape, lambda i, n: (0,) * len(shape))

    return pl.pallas_call(
        body,
        out_shape=jax.ShapeDtypeStruct((16, 8, 24, 128), bf16),
        grid_spec=pltpu.PrefetchScalarGridSpec(
            num_scalar_prefetch=1,
            grid=(16,),
            in_specs=[whole(4, 2048), whole(1, 768), whole(1, 1024), whole(1, 256)],
            out_specs=pl.BlockSpec((1, 8, 24, 128), lambda i, n: (i, 0, 0, 0)),
            scratch_shapes=[pltpu.VMEM((8, 24, 128), f32)],
        ),
        compiler_params=kernel_params(),
        cost_estimate=cost(3),
        name="small_sums",
    )(numbers, norm_sums, qkv_sums, up_sums, dy_sums)


def local(
    tokens,
    doc_lengths,
    cotangent,
    ln1_gain,
    ln1_bias,
    ln2_gain,
    ln2_bias,
    qkv_weight,
    qkv_bias,
    out_weight,
    out_bias,
    up_weight,
    up_bias,
    down_weight,
    down_bias,
):
    rows, width = tokens.shape
    head = width // HEADS
    group = 8
    rep = lax.axis_index("rep")
    shard = lax.axis_index("shard")
    y, h, c = rep // 4, (rep // 2) % 2, rep % 2
    l, x = shard // 4, shard % 4
    ff = up_bias.shape[0]

    pair = jnp.stack([tokens, cotangent])
    below, above, other = move(pair, x=1), move(pair, x=-1), move(pair, l=1)
    far, other_above, other_below = move(below, x=1), move(other, x=-1), move(below, l=1)
    x_other_far, dy_other_far = move(other_below[0], x=1), move(other_above[1], x=-1)
    pairs = (pair, above, far, below, other, other_above, None, other_below)
    x_all = tuple(x_other_far[None] if p is None else p for p in pairs)
    dy_all = tuple(dy_other_far if p is None else p for p in pairs)

    vectors = jnp.concatenate([ln1_gain, ln1_bias, ln2_gain, ln2_bias, qkv_bias])[None]
    place = (y * 2 + c).astype(jnp.int32).reshape(1)
    part = packed(qkv_weight, up_weight, vectors, doc_lengths, place, head)
    part = lax.all_to_all(part, "shard", 0, 0)
    cols = part.shape[-1]
    own, infos = part[:, :32], part[:, 32:].astype(f32)
    below, above = move(own, y=1), move(own, y=-1)
    far_low, far_high = move(below[:4], y=1), move(above[4:], y=-1)
    mine = ((own, 0, 0), (above, 0, 1), (far_low, 0, 2), (far_high, 4, 2), (below, 0, 3))
    yours = tuple((move(array, c=1), first, spot + 4) for array, first, spot in mine)
    steps4 = (y + jnp.arange(4)) % 4
    spots = jnp.concatenate([steps4 * 2 + c, steps4 * 2 + 1 - c]).astype(jnp.int32)
    w_mixed = sorted_weight(mine + yours, spots)

    gains = infos[:, 0, :1024].reshape(8, 4, 256).transpose(1, 0, 2).reshape(4, width)
    qkv_b = infos[:, 0, 1024:].reshape(8 * 3, 1, head)
    qkv_b = jnp.stack(
        [lax.dynamic_index_in_dim(qkv_b, third * 8 + shard, 0, False) for third in range(3)]
    )
    steps8 = jnp.arange(8)
    sources = ((steps8 // 4) ^ l) * 4 + (x + steps8 % 4) % 4
    sources = sources.astype(jnp.int32)
    lengths = infos[:, 1, :3]
    lengths = jnp.sum(
        jnp.where(sources[:, None, None] == steps8[None, :, None], lengths[None], 0.0), 1
    ).astype(jnp.int32)
    ends = jnp.cumsum(lengths, 1)
    starts = ends - lengths
    steps_t = jnp.arange(rows, dtype=jnp.int32)
    segment = jnp.sum((steps_t[None, :, None] >= ends[:, None, :]).astype(jnp.int32), -1)
    slots = jnp.arange(lengths.shape[1], dtype=jnp.int32)
    begin = jnp.sum(
        jnp.where(segment[:, :, None] == slots[None, None, :], starts[:, None, :], 0), -1
    )
    position = (steps_t[None, :] - begin).astype(f32).reshape(group * rows, 1)
    lane = jnp.arange(128)
    freq = 10000.0 ** (-2.0 * (lane % (ROT // 2)).astype(f32) / ROT)
    angle = position * freq[None, :]
    cosine = jnp.where(lane < ROT, jnp.cos(angle), 1.0)
    sine = jnp.sin(angle)
    sine = jnp.where(lane < ROT // 2, -sine, jnp.where(lane < ROT, sine, 0.0))

    x_rows, h1, h2, mean, inverse = norms(x_all, gains)
    active, slope = hidden_part(h2, w_mixed, 3 * head // 256, up_bias.astype(f32)[None])
    both_bias = (out_bias.astype(f32) + down_bias.astype(f32))[None, :]
    wide_bias = lax.dynamic_update_slice(jnp.zeros((1, width), f32), both_bias, (0, shard * 256))
    numbers = jnp.stack([c, shard, y, h]).astype(jnp.int32)

    d_hidden, up_sums = inner_grad(dy_all, down_weight, slope, ())
    keep, send, dy_sums = inner_weight_grads(active, h2, dy_all, d_hidden, numbers)
    got = move(send, c=1)
    qkv, probs, attended = attention(h1, w_mixed, qkv_b, cosine, sine, lengths, (send,))

    def turn(k):
        return lambda i, n: (n[2] + k) % 4 * 2 + i % 2

    low, high = added([(keep, turn(2), None), (got, turn(2), None)], (1, 1), numbers, (attended,))
    from_low, from_high = move(low, y=1), move(high, y=-1)
    mix = mixed_part(
        active, attended, down_weight, out_weight, wide_bias, sources, (low, high)
    )
    def sides(i, n):
        return (n[2] + 1 + i // 2 * 2) % 4 * 2 + i % 2

    above, below = added(
        [
            (keep, sides, None),
            (got, sides, None),
            (from_low, lambda i, n: 0, (0,)),
            (from_high, lambda i, n: 0, (3,)),
        ],
        (2, 2),
        numbers,
        (mix,),
    )
    from_below, from_above = move(above, y=1), move(below, y=-1)
    d_qkv, qkv_sums, a_keep, a_send = attention_grads(
        dy_all, out_weight, qkv, probs, cosine, sine, h1, attended, numbers, (above, below)
    )
    a_got = move(a_send, c=1)

    def ends_at(i, n):
        return n[2] * 2 + jnp.where(i == 0, 1 - n[3], n[3])

    def crosses(i, n):
        return jnp.where(i == 0, 1 - n[3], n[3])

    leaves, inner = added(
        [
            (keep, ends_at, None),
            (got, ends_at, None),
            (from_below, crosses, None),
            (from_above, crosses, None),
        ],
        (1, 1),
        numbers,
        (a_send,),
    )
    crossed = move(leaves, h=1)

    def away(i, n):
        return i * 2 + 1 - n[3]

    (a_away,) = added([(a_keep, away, None), (a_got, away, None)], (4,), numbers, (leaves,))
    a_crossed = move(a_away, h=1)

    def around(i, n):
        return (n[2] + 2 - i) % 4

    def around_here(i, n):
        return around(i, n) * 2 + n[3]

    a_far, a_above, a_own, a_below = added(
        [
            (a_keep, around_here, None),
            (a_got, around_here, None),
            (a_crossed, around, None),
        ],
        (1, 1, 1, 1),
        numbers,
        (),
    )
    norm_sums, *sums = back_norms(
        d_qkv,
        d_hidden,
        w_mixed,
        x_rows,
        mean,
        inverse,
        jnp.stack([gains[0], gains[2]]),
        (a_away,),
    )
    ((inner,),) = added(
        [(inner, lambda i, n: 0, None), (crossed, lambda i, n: 0, None)], (1,), numbers, (sums[0],)
    )
    up = inner[64:].reshape(4, 16, 2, ff).transpose(2, 0, 1, 3).reshape(8, 16, ff)
    up = lax.all_to_all(up, "shard", 0, 0)
    up = up.reshape(2, 4, 16, ff).transpose(1, 2, 0, 3).reshape(64, width)
    inner = jnp.concatenate([inner[:64], up], 0)
    inner = jnp.stack([inner, move(inner, h=1)])

    a_sum = ring_reduce([a_own[0], a_above[0], a_far[0], a_below[0]], "y", 32).astype(bf16)
    third = a_sum[:48].reshape(48, 8, head).transpose(1, 0, 2)
    third = lax.all_to_all(third, "shard", 0, 0).transpose(1, 0, 2).reshape(48, width)
    a_sum = jnp.concatenate([third, a_sum[48:]], 0)

    def ring(pieces, way):
        own, above, far, below = pieces if way == 1 else (pieces[n] for n in (0, 3, 2, 1))
        passed = move(far, x=way)
        above = (above.astype(f32) + passed.astype(f32)).astype(bf16)
        return (
            own.astype(f32) + move(above, x=way).astype(f32) + move(below, x=-way).astype(f32)
        )

    sum_other = move(ring(sums[4:], 1).astype(bf16), l=1)
    own_sum = ring(sums[:4], -1) + sum_other.astype(f32)
    mixed = lax.psum_scatter(mix, "shard", scatter_dimension=0, tiled=True)
    mixed = (tokens.astype(f32) + mixed.astype(f32)).astype(bf16)
    own_normed, own_inverse = normalize(tokens)
    tokens_grad = cotangent.astype(f32) + own_inverse * (
        own_sum
        - jnp.mean(own_sum, -1, keepdims=True)
        - own_normed * jnp.mean(own_sum * own_normed, -1, keepdims=True)
    )

    smalls = small_sums(norm_sums, qkv_sums, up_sums, dy_sums, numbers)
    smalls = lax.all_to_all(smalls.reshape(128, 24, 128), BOTH, 0, 0)
    smalls = jnp.sum(smalls.astype(f32), 0)
    norm_grads = smalls[:8].reshape(4, 256)
    dy_total = smalls[22:].reshape(256)

    below, above = move(inner, y=1), move(inner, y=-1)
    far_low, far_high = move(below[:1], y=1), move(above[1:], y=-1)
    pieces = [inner, above, far_low, far_high, below]
    pieces += [move(piece, c=1) for piece in pieces]
    spots = []
    for low in (c, 1 - c):
        for k, highs in ((0, (h, 1 - h)), (1, (h, 1 - h)), (2, (h,)), (2, (1 - h,)), (3, (h, 1 - h))):
            spots += [(((y + k) % 4) * 2 + high) * 2 + low for high in highs]
    up_parts = [
        (source * ff, 64 + 16 * (source % 4), source // 4 * ff, ff) for source in range(8)
    ]
    down_grad, up_grad = spread(
        pieces,
        jnp.stack(spots).astype(jnp.int32),
        [(width, 64, [(0, 0, 0, width)]), (8 * ff, 16, up_parts)],
    )

    a_sum = jnp.stack(ring_gather(a_sum, "y", 32))
    a_other = move(a_sum, h=1)
    pieces = [a_sum, a_other, move(a_sum, c=1), move(a_other, c=1)]
    spots = [
        (steps4 * 2 + high) * 2 + low for low in (c, 1 - c) for high in (h, 1 - h)
    ]
    out_grad, qkv_grad = spread(
        pieces,
        jnp.concatenate(spots).astype(jnp.int32),
        [
            (width, 16, [(0, 48, 0, width)]),
            (3 * width, 16, [(n * width, 16 * n, 0, width) for n in range(3)]),
        ],
    )
    return (
        mixed,
        tokens_grad,
        norm_grads[0],
        norm_grads[1],
        norm_grads[2],
        norm_grads[3],
        qkv_grad,
        smalls[8:14].reshape(768),
        out_grad,
        dy_total,
        up_grad,
        smalls[14:22].reshape(ff),
        down_grad,
        dy_total,
    )


def solution(mesh):
    rows = P(BOTH, None)
    vector, matrix = P("shard"), P("shard", None)
    return jax.shard_map(
        local,
        mesh=mesh,
        in_specs=(rows, rows, rows, vector, vector, vector, vector)
        + (matrix, vector, matrix, vector, matrix, vector, matrix, vector),
        out_specs=(rows, rows, vector, vector, vector, vector)
        + (matrix, vector, matrix, vector, matrix, vector, matrix, vector),
        check_vma=False,
    )
```

```python
import functools
import math

import jax
import jax.numpy as jnp
from jax import lax
from jax.experimental import pallas as pl
from jax.experimental.pallas import tpu as pltpu
from jax.sharding import PartitionSpec as P

HEADS = 8
ROT = 64
EPS = 1e-05
f32 = jnp.float32
bf16 = jnp.bfloat16


def cost(time):
    return pl.CostEstimate(flops=int(time * 1.15e9), bytes_accessed=1000, transcendentals=0)


BOTH = ("rep", "shard")
SIZES = (4, 2, 2, 2, 4)
SAME_CORE = [[2 * n + c for n in range(8)] for c in range(2)]
SAME_CORE_ALL = [[(2 * n + c) * 8 + s for n in range(8) for s in range(8)] for c in range(2)]


def coords():
    for y in range(4):
        for h in range(2):
            for c in range(2):
                for l in range(2):
                    for x in range(4):
                        yield (y, h, c, l, x)


def linear(t):
    y, h, c, l, x = (v % m for v, m in zip(t, SIZES))
    return ((y * 2 + h) * 2 + c) * 8 + l * 4 + x


def move(value, y=0, h=0, c=0, l=0, x=0):
    step = (y, h, c, l, x)
    pairs = [(linear(t), linear(tuple(a + b for a, b in zip(t, step)))) for t in coords()]
    return lax.ppermute(value, BOTH, pairs)


def pick(value, index, axis):
    return lax.dynamic_index_in_dim(value, index, axis, keepdims=False)


def ring_gather(own, axis, cut):
    below = move(own, **{axis: 1})
    above = move(own, **{axis: -1})
    far_low = move(below[:cut], **{axis: 1})
    far_high = move(above[cut:], **{axis: -1})
    return [own, above, jnp.concatenate([far_low, far_high], 0), below]


def normalize(value):
    xf = value.astype(f32)
    centre = xf - jnp.mean(xf, -1, keepdims=True)
    inverse = lax.rsqrt(jnp.mean(centre * centre, -1, keepdims=True) + EPS)
    return centre * inverse, inverse


def kernel_params():
    return pltpu.CompilerParams(vmem_limit_bytes=56 * 1024 * 1024)


def after_inputs(body, count, extra):
    return lambda *refs: body(*refs[:count], *refs[count + extra :])


def anywhere(count):
    return [pl.BlockSpec(memory_space=pl.ANY)] * count


def dot(a, b, ca=1, cb=0):
    return lax.dot_general(a, b, (((ca,), (cb,)), ((), ())), preferred_element_type=f32)


def swap_halves(value):
    lane = lax.broadcasted_iota(jnp.int32, value.shape, 1)
    return jnp.where(lane < 32, pltpu.roll(value, 96, 1), pltpu.roll(value, 32, 1))


def allowed_mask(lengths_ref, block, rows):
    e0 = lengths_ref[block, 0]
    e1 = e0 + lengths_ref[block, 1]
    t = lax.broadcasted_iota(jnp.int32, (rows, rows), 0)
    s = lax.broadcasted_iota(jnp.int32, (rows, rows), 1)
    seg_t = (t >= e0).astype(jnp.int32) + (t >= e1).astype(jnp.int32)
    seg_s = (s >= e0).astype(jnp.int32) + (s >= e1).astype(jnp.int32)
    return (seg_t == seg_s) & (s <= t)


def dot_rows(a, b):
    return lax.dot_general(a, b, (((0,), (0,)), ((), ())), preferred_element_type=f32)


def loads(copies):
    for copy in copies:
        copy.start()
    return copies


def piece_copies(pieces, half, target, sems, rows):
    return [
        pltpu.make_async_copy(
            piece.at[half] if len(piece.shape) == 3 else piece,
            target.at[pl.ds(at * rows, rows)],
            sems.at[at],
        )
        for at, piece in enumerate(pieces)
    ]


def feed_forward(x, dy, gains, weight, down, bias, numbers, first, after):
    rows, width = x[0].shape[1:]
    count = len(x)
    total = rows * count
    ff = bias.shape[1]

    def body(number_ref, g_ref, b_ref, *refs):
        x_refs, dy_refs = refs[:count], refs[count : 2 * count]
        w_hbm, d_hbm = refs[2 * count : 2 * count + 2]
        (h1_hbm, act_hbm, du_hbm, keep_hbm, send_hbm, m_ref, i_ref, db_ref, sum_ref) = refs[
            2 * count + 2 : 2 * count + 11
        ]
        (x_v, dy_v, h1_v, h2_v, w_v, d_v, act_v, du_v, keep_v, send_v, x_sem, dy_sem, sems) = refs[
            2 * count + 11 :
        ]
        own = number_ref[0] == 0
        x_copies = loads(piece_copies(x_refs, 0, x_v, x_sem, rows))
        w_copy = pltpu.make_async_copy(w_hbm.at[:, pl.ds(first, ff)], w_v, sems.at[0])
        w_copy.start()
        dy_copies = loads(piece_copies(dy_refs, 1, dy_v, dy_sem, rows))
        d_copy = pltpu.make_async_copy(d_hbm, d_v, sems.at[1])
        d_copy.start()
        for copy in x_copies:
            copy.wait()

        @pl.loop(0, count)
        def _(n):
            at = pl.ds(pl.multiple_of(n * rows, rows), rows)
            value = x_v[at, :].astype(f32)
            mean = jnp.mean(value, 1, keepdims=True)
            centre = value - mean
            inverse = lax.rsqrt(jnp.mean(centre * centre, 1, keepdims=True) + EPS)
            normed = centre * inverse
            m_ref[at, :] = mean
            i_ref[at, :] = inverse
            h1_v[at, :] = (normed * g_ref[0:1] + g_ref[1:2]).astype(bf16)
            h2_v[at, :] = (normed * g_ref[2:3] + g_ref[3:4]).astype(bf16)

        h1_copy = pltpu.make_async_copy(h1_v, h1_hbm, sems.at[2])
        h1_copy.start()
        w_copy.wait()
        for copy in dy_copies:
            copy.wait()
        d_copy.wait()
        mine = dy_v[:, pl.ds(pl.multiple_of(number_ref[1] * 256, 256), 256)]
        sum_ref[...] = jnp.sum(mine.astype(f32), 0, keepdims=True)

        def split(part, places, high, wide):
            at = (places, high, wide)

            @pl.when(own)
            def _():
                keep_v[at] = part[:, 0]
                send_v[at] = part[:, 1]

            @pl.when(jnp.logical_not(own))
            def _():
                keep_v[at] = part[:, 1]
                send_v[at] = part[:, 0]

        def leaving(n):
            at = (pl.ds(n * 2, 2), pl.ds(0, 64))
            return (
                pltpu.make_async_copy(keep_v.at[at], keep_hbm.at[at], sems.at[3]),
                pltpu.make_async_copy(send_v.at[at], send_hbm.at[at], sems.at[4]),
            )

        @pl.loop(0, ff // 256)
        def _(n):
            at = pl.ds(pl.multiple_of(n * 256, 256), 256)
            u = dot(h2_v[...], w_v[:, at]) + b_ref[:, at]
            cdf = 0.5 * (1.0 + lax.erf(u * math.sqrt(0.5)))
            pdf = jnp.exp(-0.5 * u * u) * (1.0 / math.sqrt(2.0 * math.pi))
            act = (u * cdf).astype(bf16)
            act_v[:, at] = act
            du = (dot(dy_v[...], d_v[at, :], 1, 1) * (cdf + u * pdf)).astype(bf16)
            du_v[:, at] = du
            db_ref[:, at] = jnp.sum(du.astype(f32), 0, keepdims=True)
            part = dot_rows(act, dy_v[...]).astype(bf16).reshape(2, 2, 64, width)
            split(part, pl.ds(n * 2, 2), pl.ds(0, 64), slice(None))
            for copy in leaving(n):
                copy.start()

        act_copy = pltpu.make_async_copy(act_v, act_hbm, sems.at[0])
        act_copy.start()
        du_copy = pltpu.make_async_copy(du_v, du_hbm, sems.at[1])
        du_copy.start()
        for n in range(ff // 256):
            for copy in leaving(n):
                copy.wait()

        def block(n):
            at = (
                slice(None),
                pl.ds(pl.multiple_of(64 + 16 * (n % 4), 16), 16),
                pl.ds(pl.multiple_of(n // 4 * ff, ff), ff),
            )
            return at

        def away(n):
            at = block(n)
            return (
                pltpu.make_async_copy(keep_v.at[at], keep_hbm.at[at], sems.at[3]),
                pltpu.make_async_copy(send_v.at[at], send_hbm.at[at], sems.at[4]),
            )

        @pl.loop(0, 8)
        def _(n):
            lanes = pl.ds(pl.multiple_of(n * 256, 256), 256)
            part = dot_rows(h2_v[:, lanes], du_v[...]).astype(bf16).reshape(8, 2, 16, ff)
            split(part, *block(n))
            for copy in away(n):
                copy.start()

        for n in range(8):
            for copy in away(n):
                copy.wait()
        h1_copy.wait()
        act_copy.wait()
        du_copy.wait()

    wide = jax.ShapeDtypeStruct((total, width), bf16)
    thin = jax.ShapeDtypeStruct((total, ff), bf16)
    column = jax.ShapeDtypeStruct((total, 1), f32)
    grads = jax.ShapeDtypeStruct((8, 128, width), bf16)
    vmem = pl.BlockSpec(memory_space=pltpu.VMEM)
    return pl.pallas_call(
        after_inputs(body, 5 + 2 * count, len(after)),
        out_shape=(
            wide,
            thin,
            thin,
            grads,
            grads,
            column,
            column,
            jax.ShapeDtypeStruct((1, ff), f32),
            jax.ShapeDtypeStruct((1, 256), f32),
        ),
        in_specs=[pl.BlockSpec(memory_space=pltpu.SMEM), vmem, vmem]
        + anywhere(2 * count + 2 + len(after)),
        out_specs=tuple(anywhere(5)) + (vmem,) * 4,
        scratch_shapes=[
            pltpu.VMEM((total, width), bf16),
            pltpu.VMEM((total, width), bf16),
            pltpu.VMEM((total, width), bf16),
            pltpu.VMEM((total, width), bf16),
            pltpu.VMEM((width, ff), bf16),
            pltpu.VMEM((ff, width), bf16),
            pltpu.VMEM((total, ff), bf16),
            pltpu.VMEM((total, ff), bf16),
            pltpu.VMEM((8, 128, width), bf16),
            pltpu.VMEM((8, 128, width), bf16),
            pltpu.SemaphoreType.DMA((count,)),
            pltpu.SemaphoreType.DMA((count,)),
            pltpu.SemaphoreType.DMA((5,)),
        ],
        compiler_params=kernel_params(),
        cost_estimate=cost(32),
        name="feed_forward",
    )(numbers, gains, bias, *x, *dy, weight, down, *after)


def attend(h1, dy, weight, out, bias, cosine, sine, lengths, numbers, after, rows=128):
    total, width = h1.shape
    count = len(dy)
    head = out.shape[0]
    scale = head ** (-0.5)

    def body(number_ref, len_ref, b_ref, *refs):
        dy_refs = refs[:count]
        h1_hbm, w_hbm, out_hbm, cos_hbm, sin_hbm = refs[count : count + 5]
        ol_hbm, dq_hbm, keep_hbm, send_hbm, sum_ref = refs[count + 5 : count + 10]
        (dy_v, h1_v, w_v, wo_v, cos_v, sin_v, qkv_v, do_v, ol_v, dq_v, keep_v, send_v, dy_sem, sems) = (
            refs[count + 10 :]
        )
        own = number_ref[0] == 0
        pairs = (
            (h1_hbm, h1_v),
            (w_hbm.at[:, pl.ds(0, 3 * head)], w_v),
            (out_hbm, wo_v),
            (cos_hbm, cos_v),
            (sin_hbm, sin_v),
        )
        copies = loads(
            [pltpu.make_async_copy(*pair, sems.at[n]) for n, pair in enumerate(pairs)]
        )
        dy_copies = loads(piece_copies(dy_refs, 1, dy_v, dy_sem, rows))
        copies[0].wait()
        copies[1].wait()

        @pl.loop(0, 3)
        def _(n):
            at = pl.ds(pl.multiple_of(n * head, head), head)
            qkv_v[:, at] = dot(h1_v[...], w_v[:, at]) + b_ref[n]

        for copy in copies[2:] + dy_copies:
            copy.wait()
        do_v[...] = dot(dy_v[...], wo_v[...], 1, 1).astype(bf16)
        sum_ref[...] = jnp.zeros_like(sum_ref)

        @pl.loop(0, total // rows)
        def _(block):
            at = pl.ds(pl.multiple_of(block * rows, rows), rows)
            cos, sin = cos_v[at, :], sin_v[at, :]

            def turned(value, sign):
                left = value[:, :128]
                left = left * cos + swap_halves(left) * (sin * sign)
                return jnp.concatenate([left, value[:, 128:]], 1).astype(bf16)

            q, k = turned(qkv_v[at, 0:head], 1.0), turned(qkv_v[at, head : 2 * head], 1.0)
            v = qkv_v[at, 2 * head :].astype(bf16)
            scores = dot(q, k, 1, 1) * scale
            masked = jnp.where(allowed_mask(len_ref, block, rows), scores, -1e30)
            shifted = jnp.exp(masked - jnp.max(masked, 1, keepdims=True))
            probs = shifted / jnp.sum(shifted, 1, keepdims=True)
            low = probs.astype(bf16)
            ol_v[at, :] = dot(low, v).astype(bf16)
            d_out = do_v[at, :]
            d_value = dot(low, d_out, 0, 0)
            d_probs = dot(d_out, v, 1, 1)
            centred = d_probs - jnp.sum(d_probs * probs, 1, keepdims=True)
            d_scores = (probs * centred).astype(bf16)
            d_query = turned(dot(d_scores, k) * scale, -1.0)
            d_key = turned(dot(d_scores, q, 0, 0) * scale, -1.0)
            for n, grad in enumerate((d_query, d_key, d_value.astype(bf16))):
                lanes = slice(n * head, (n + 1) * head)
                dq_v[at, lanes] = grad
                sum_ref[:, lanes] += jnp.sum(grad.astype(f32), 0, keepdims=True)

        ol_copy = pltpu.make_async_copy(ol_v, ol_hbm, sems.at[0])
        ol_copy.start()
        dq_copy = pltpu.make_async_copy(dq_v, dq_hbm, sems.at[1])
        dq_copy.start()

        def split(part, high, wide):
            at = (slice(None), high, wide)

            @pl.when(own)
            def _():
                keep_v[at] = part[:, 0]
                send_v[at] = part[:, 1]

            @pl.when(jnp.logical_not(own))
            def _():
                keep_v[at] = part[:, 1]
                send_v[at] = part[:, 0]

        part = dot_rows(ol_v[...], dy_v[...]).astype(bf16).reshape(8, 2, 16, width)
        split(part, pl.ds(48, 16), slice(None))

        @pl.loop(0, 8)
        def _(n):
            lanes = pl.ds(pl.multiple_of(n * 256, 256), 256)
            part = dot_rows(h1_v[:, lanes], dq_v[...]).astype(bf16).reshape(8, 2, 16, 3 * head)
            for third in range(3):
                split(
                    part[..., third * head : (third + 1) * head],
                    pl.ds(16 * third, 16),
                    pl.ds(pl.multiple_of(n * head, head), head),
                )

        keep_copy = pltpu.make_async_copy(keep_v, keep_hbm, sems.at[2])
        keep_copy.start()
        send_copy = pltpu.make_async_copy(send_v, send_hbm, sems.at[3])
        send_copy.start()
        for copy in (ol_copy, dq_copy, keep_copy, send_copy):
            copy.wait()

    grads = jax.ShapeDtypeStruct((8, 64, width), bf16)
    vmem = pl.BlockSpec(memory_space=pltpu.VMEM)
    smem = pl.BlockSpec(memory_space=pltpu.SMEM)
    return pl.pallas_call(
        after_inputs(body, 8 + count, len(after)),
        out_shape=(
            jax.ShapeDtypeStruct((total, head), bf16),
            jax.ShapeDtypeStruct((total, 3 * head), bf16),
            grads,
            grads,
            jax.ShapeDtypeStruct((1, 3 * head), f32),
        ),
        in_specs=[smem, smem, vmem] + anywhere(count + 5 + len(after)),
        out_specs=tuple(anywhere(4)) + (vmem,),
        scratch_shapes=[
            pltpu.VMEM((total, width), bf16),
            pltpu.VMEM((total, width), bf16),
            pltpu.VMEM((width, 3 * head), bf16),
            pltpu.VMEM((head, width), bf16),
            pltpu.VMEM((total, 128), f32),
            pltpu.VMEM((total, 128), f32),
            pltpu.VMEM((total, 3 * head), f32),
            pltpu.VMEM((total, head), bf16),
            pltpu.VMEM((total, head), bf16),
            pltpu.VMEM((total, 3 * head), bf16),
            pltpu.VMEM((8, 64, width), bf16),
            pltpu.VMEM((8, 64, width), bf16),
            pltpu.SemaphoreType.DMA((count,)),
            pltpu.SemaphoreType.DMA((5,)),
        ],
        compiler_params=kernel_params(),
        cost_estimate=cost(22),
        name="attend",
    )(numbers, lengths, bias, *dy, h1, weight, out, cosine, sine, *after)


def mixed_part(active, attended, down, out, bias, sources, after):
    rows, ff = active.shape
    head, width = out.shape
    step = 512

    def body(source_ref, act_ref, ol_ref, wd_ref, wo_ref, b_ref, mix_ref):
        total = dot(act_ref[...], wd_ref[...]) + dot(ol_ref[...], wo_ref[...]) + b_ref[...]
        total = total.astype(bf16)
        for at in range(rows // 128):
            to = pl.ds(pl.multiple_of(source_ref[at] * 128, 128), 128)
            mix_ref[to, :] = total[at * 128 : (at + 1) * 128]

    return pl.pallas_call(
        after_inputs(body, 6, len(after)),
        out_shape=jax.ShapeDtypeStruct((rows, width), bf16),
        grid_spec=pltpu.PrefetchScalarGridSpec(
            num_scalar_prefetch=1,
            grid=(width // step,),
            in_specs=[
                pl.BlockSpec((rows, ff), lambda i, n: (0, 0)),
                pl.BlockSpec((rows, head), lambda i, n: (0, 0)),
                pl.BlockSpec((ff, step), lambda i, n: (0, i)),
                pl.BlockSpec((head, step), lambda i, n: (0, i)),
                pl.BlockSpec((1, step), lambda i, n: (0, i)),
            ]
            + anywhere(len(after)),
            out_specs=pl.BlockSpec((rows, step), lambda i, n: (0, i)),
        ),
        compiler_params=kernel_params(),
        cost_estimate=cost(10),
        name="mixed_part",
    )(sources, active, attended, down, out, bias, *after)


def back_norms(d_qkv, d_hidden, weight, tokens, mean, inverse, gains, after):
    total, n1 = d_qkv.shape
    n2 = d_hidden.shape[1]
    count = len(tokens)
    width = tokens[0].shape[2]
    step = 512

    def body(dq_ref, du_ref, w_ref, m_ref, i_ref, g_ref, *refs):
        x_refs, sums_ref, outs = refs[:count], refs[count], refs[count + 1 :]
        d1 = dot(dq_ref[...], w_ref[:, :n1], 1, 1)
        d2 = dot(du_ref[...], w_ref[:, n1:], 1, 1)
        both = (d1 * g_ref[0:1] + d2 * g_ref[1:2]).astype(bf16)
        for at in range(count):
            outs[at][...] = both[at * 128 : (at + 1) * 128]
        x = jnp.concatenate([ref[0] for ref in x_refs], 0)
        normed = (x.astype(f32) - m_ref[...]) * i_ref[...]
        sums_ref[0:1] = jnp.sum(d1 * normed, 0, keepdims=True)
        sums_ref[1:2] = jnp.sum(d1, 0, keepdims=True)
        sums_ref[2:3] = jnp.sum(d2 * normed, 0, keepdims=True)
        sums_ref[3:4] = jnp.sum(d2, 0, keepdims=True)

    return pl.pallas_call(
        after_inputs(body, 6 + count, len(after)),
        out_shape=(jax.ShapeDtypeStruct((4, width), f32),)
        + (jax.ShapeDtypeStruct((128, width), bf16),) * count,
        grid=(width // step,),
        in_specs=[
            pl.BlockSpec((total, n1), lambda i: (0, 0)),
            pl.BlockSpec((total, n2), lambda i: (0, 0)),
            pl.BlockSpec((step, n1 + n2), lambda i: (i, 0)),
            pl.BlockSpec((total, 1), lambda i: (0, 0)),
            pl.BlockSpec((total, 1), lambda i: (0, 0)),
            pl.BlockSpec((2, step), lambda i: (0, i)),
        ]
        + [pl.BlockSpec((1, 128, step), lambda i: (0, 0, i))] * count
        + anywhere(len(after)),
        out_specs=(pl.BlockSpec((4, step), lambda i: (0, i)),)
        + (pl.BlockSpec((128, step), lambda i: (0, i)),) * count,
        compiler_params=kernel_params(),
        cost_estimate=cost(14),
        name="back_norms",
    )(d_qkv, d_hidden, weight, mean, inverse, gains, *tokens, *after)


def unpacked(part, after):
    owners, _, cols = part.shape

    def body(part_ref, rows_ref, info_ref):
        for owner in range(owners):
            rows_ref[owner] = part_ref[owner, 0:32]
            info_ref[owner] = part_ref[owner, 32:40].astype(f32)

    return pl.pallas_call(
        after_inputs(body, 1, len(after)),
        out_shape=(
            jax.ShapeDtypeStruct((owners, 32, cols), bf16),
            jax.ShapeDtypeStruct((owners, 8, cols), f32),
        ),
        in_specs=[pl.BlockSpec(memory_space=pltpu.VMEM)] + anywhere(len(after)),
        out_specs=(pl.BlockSpec(memory_space=pltpu.VMEM),) * 2,
        compiler_params=kernel_params(),
        cost_estimate=cost(3),
        name="unpacked",
    )(part, *after)


def halves(below, above, after):
    _, rows, cols = below.shape

    def body(below_ref, above_ref, low_ref, high_ref):
        low_ref[...] = below_ref[...]
        high_ref[...] = above_ref[...]

    out = jax.ShapeDtypeStruct((4, rows, cols), bf16)
    return pl.pallas_call(
        after_inputs(body, 2, len(after)),
        out_shape=(out, out),
        grid=(1,),
        in_specs=[
            pl.BlockSpec((4, rows, cols), lambda i: (0, 0, 0)),
            pl.BlockSpec((4, rows, cols), lambda i: (1, 0, 0)),
        ]
        + anywhere(len(after)),
        out_specs=(pl.BlockSpec((4, rows, cols), lambda i: (0, 0, 0)),) * 2,
        compiler_params=kernel_params(),
        cost_estimate=cost(3),
        name="halves",
    )(below, above, *after)


def packed_sums(inner, own, below, above, ff, head, after):
    width = inner.shape[1]

    def body(inner_ref, own_ref, below_ref, above_ref, out_ref, down_ref, stay_ref):
        total = own_ref[...].astype(f32) + below_ref[...].astype(f32) + above_ref[...].astype(f32)
        total = total.astype(bf16)
        for owner in range(8):
            pieces = [
                total[16 * third : 16 * third + 16, owner * head : (owner + 1) * head]
                for third in range(3)
            ]
            row, col = 64 + 16 * (owner % 4), owner // 4 * ff
            pieces.append(inner_ref[row : row + 16, col : col + ff])
            out_ref[owner] = jnp.concatenate(pieces, 1)
        down_ref[...] = inner_ref[0:64, :]
        stay_ref[...] = total[48:64]

    vmem = pl.BlockSpec(memory_space=pltpu.VMEM)
    return pl.pallas_call(
        after_inputs(body, 4, len(after)),
        out_shape=(
            jax.ShapeDtypeStruct((8, 16, 3 * head + ff), bf16),
            jax.ShapeDtypeStruct((64, width), bf16),
            jax.ShapeDtypeStruct((16, width), bf16),
        ),
        in_specs=[vmem] * 4 + anywhere(len(after)),
        out_specs=(vmem,) * 3,
        compiler_params=kernel_params(),
        cost_estimate=cost(3),
        name="packed_sums",
    )(inner, own, below, above, *after)


def unpacked_sums(part, down, stay, ff, head, after):
    width = down.shape[1]

    def body(part_ref, down_ref, stay_ref, inner_ref, out_ref):
        inner_ref[0:64] = down_ref[...]
        out_ref[48:64] = stay_ref[...]
        for source in range(8):
            for third in range(3):
                out_ref[16 * third : 16 * third + 16, source * head : (source + 1) * head] = part_ref[
                    source, :, third * head : (third + 1) * head
                ]
            row, col = 64 + 16 * (source % 4), source // 4 * ff
            inner_ref[row : row + 16, col : col + ff] = part_ref[source, :, 3 * head :]

    vmem = pl.BlockSpec(memory_space=pltpu.VMEM)
    return pl.pallas_call(
        after_inputs(body, 3, len(after)),
        out_shape=(
            jax.ShapeDtypeStruct((128, width), bf16),
            jax.ShapeDtypeStruct((64, width), bf16),
        ),
        in_specs=[vmem] * 3 + anywhere(len(after)),
        out_specs=(vmem,) * 2,
        compiler_params=kernel_params(),
        cost_estimate=cost(3),
        name="unpacked_sums",
    )(part, down, stay, *after)


def spread(pieces, places, core, targets):
    rows, cols = pieces[0][0].shape[1:]
    firsts, total = [], 0
    for mine, _ in pieces:
        firsts.append(total)
        total += mine.shape[0]

    def body(place_ref, core_ref, *refs):
        step = pl.program_id(0)
        outs = refs[2 * len(pieces) :]
        first_core = core_ref[0] == 0

        def fill(ref, low):
            for out_ref, (_, high, parts) in zip(outs, targets):
                for to, row, col, size in parts:
                    out_ref[low * high : (low + 1) * high, to : to + size] = ref[
                        0, row : row + high, col : col + size
                    ].astype(f32)

        for n, (first, (mine, _)) in enumerate(zip(firsts, pieces)):
            here = (step >= first) & (step < first + mine.shape[0])

            @pl.when(here & first_core)
            def _(n=n):
                fill(refs[2 * n], 0)
                fill(refs[2 * n + 1], 1)

            @pl.when(here & jnp.logical_not(first_core))
            def _(n=n):
                fill(refs[2 * n], 1)
                fill(refs[2 * n + 1], 0)

    def chosen(first, size):
        return pl.BlockSpec(
            (1, rows, cols), lambda i, place, core: (jnp.clip(i - first, 0, size - 1), 0, 0)
        )

    specs, arrays = [], []
    for first, (mine, yours) in zip(firsts, pieces):
        specs += [chosen(first, mine.shape[0])] * 2
        arrays += [mine, yours]
    return pl.pallas_call(
        body,
        out_shape=tuple(
            jax.ShapeDtypeStruct((2 * total * high, wide), f32) for wide, high, _ in targets
        ),
        grid_spec=pltpu.PrefetchScalarGridSpec(
            num_scalar_prefetch=2,
            grid=(total,),
            in_specs=specs,
            out_specs=tuple(
                pl.BlockSpec((2 * high, wide), lambda i, place, core: (place[i], 0))
                for wide, high, _ in targets
            ),
        ),
        compiler_params=kernel_params(),
        cost_estimate=cost(10),
        name="spread",
    )(places, core, *arrays)


def small_sums(norm_sums, qkv_sums, up_sums, dy_sums, numbers):
    def body(number_ref, norm_ref, q_ref, u_ref, y_ref, out_ref, work):
        shard = number_ref[1]
        for owner in range(8):
            mine = shard == owner
            for n in range(4):
                for half in range(2):
                    at = owner * 256 + half * 128
                    work[owner, n * 2 + half : n * 2 + half + 1] = norm_ref[n : n + 1, at : at + 128]
            for n in range(3):
                third, source = divmod(owner * 3 + n, 8)
                for half in range(2):
                    at = third * 256 + half * 128
                    work[owner, 8 + n * 2 + half : 9 + n * 2 + half] = jnp.where(
                        shard == source, q_ref[:, at : at + 128], 0.0
                    )
            for n in range(8):
                work[owner, 14 + n : 15 + n] = jnp.where(
                    mine, u_ref[:, n * 128 : (n + 1) * 128], 0.0
                )
            for n in range(2):
                work[owner, 22 + n : 23 + n] = jnp.where(
                    mine, y_ref[:, n * 128 : (n + 1) * 128], 0.0
                )
        out_ref[...] = work[...].astype(bf16)

    vmem = pl.BlockSpec(memory_space=pltpu.VMEM)
    return pl.pallas_call(
        body,
        out_shape=jax.ShapeDtypeStruct((8, 24, 128), bf16),
        in_specs=[pl.BlockSpec(memory_space=pltpu.SMEM)] + [vmem] * 4,
        out_specs=vmem,
        scratch_shapes=[pltpu.VMEM((8, 24, 128), f32)],
        compiler_params=kernel_params(),
        cost_estimate=cost(3),
        name="small_sums",
    )(numbers, norm_sums, qkv_sums, up_sums, dy_sums)


def packed(qkv_weight, up_weight, vectors, lengths, place, head):
    wide, up_wide = qkv_weight.shape[1], up_weight.shape[1]
    part, up_part = 3 * head, up_wide // 8
    cols = part + up_part

    def body(place_ref, len_ref, q_ref, u_ref, v_ref, out_ref):
        lane = lax.broadcasted_iota(jnp.int32, (8, cols), 1)
        row = lax.broadcasted_iota(jnp.int32, (8, cols), 0)
        sizes = jnp.zeros((8, cols), f32)
        for at in range(3):
            sizes = jnp.where(lane == at, len_ref[0, at].astype(f32), sizes)
        vector = jnp.broadcast_to(v_ref[...].astype(f32), (8, cols))
        tail = jnp.where(row == 0, vector, jnp.where(row == 1, sizes, 0.0)).astype(bf16)
        for owner in range(8):
            pieces = [
                q_ref[:, (third * 8 + owner) * head : (third * 8 + owner + 1) * head]
                for third in range(3)
            ]
            pieces.append(u_ref[:, owner * up_part : (owner + 1) * up_part])
            out_ref[owner] = jnp.concatenate([jnp.concatenate(pieces, 1), tail], 0)

    return pl.pallas_call(
        body,
        out_shape=jax.ShapeDtypeStruct((8, 40, cols), bf16),
        grid_spec=pltpu.PrefetchScalarGridSpec(
            num_scalar_prefetch=2,
            grid=(1,),
            in_specs=[
                pl.BlockSpec((32, wide), lambda i, place, lens: (place[0], 0)),
                pl.BlockSpec((32, up_wide), lambda i, place, lens: (place[0], 0)),
                pl.BlockSpec((1, cols), lambda i, place, lens: (0, 0)),
            ],
            out_specs=pl.BlockSpec((8, 40, cols), lambda i, place, lens: (0, 0, 0)),
        ),
        compiler_params=kernel_params(),
        cost_estimate=cost(3),
        name="packed",
    )(place, lengths, qkv_weight, up_weight, vectors)


def sorted_weight(pieces, spots):
    rows, cols = pieces[0][0].shape[1:]
    count = len(pieces)

    def body(spot_ref, *refs):
        step = pl.program_id(0)
        for ref, (array, first, at) in zip(refs, pieces):

            @pl.when(step == at)
            def _(ref=ref, first=first, size=array.shape[0]):
                refs[count][first : first + size, 0] = ref[...]

    return pl.pallas_call(
        body,
        out_shape=jax.ShapeDtypeStruct((8, 8, rows, cols), bf16),
        grid_spec=pltpu.PrefetchScalarGridSpec(
            num_scalar_prefetch=1,
            grid=(8,),
            in_specs=[
                pl.BlockSpec(array.shape, lambda i, spot: (0, 0, 0)) for array, _, _ in pieces
            ],
            out_specs=pl.BlockSpec((8, 1, rows, cols), lambda i, spot: (0, spot[i], 0, 0)),
        ),
        compiler_params=kernel_params(),
        cost_estimate=cost(6),
        name="sorted_weight",
    )(spots, *[piece[0] for piece in pieces]).reshape(64 * rows, cols)


def added(terms, groups, numbers, after):
    rows, cols = terms[0][0].shape[1:]
    firsts = [sum(groups[:n]) for n in range(len(groups))]

    def body(number_ref, *refs):
        step = pl.program_id(0)
        total = None
        for ref, (_, _, steps) in zip(refs, terms):
            value = ref[0].astype(f32)
            if steps is not None:
                counts = functools.reduce(jnp.logical_or, [step == at for at in steps])
                value = jnp.where(counts, value, 0.0)
            total = value if total is None else total + value
        total = total.astype(bf16)
        for ref, first, size in zip(refs[len(terms) :], firsts, groups):

            @pl.when((step >= first) & (step < first + size))
            def _(ref=ref):
                ref[0] = total

    def came(place):
        return pl.BlockSpec((1, rows, cols), lambda i, n: (place(i, n), 0, 0))

    def goes(first, size):
        return pl.BlockSpec((1, rows, cols), lambda i, n: (jnp.clip(i - first, 0, size - 1), 0, 0))

    return pl.pallas_call(
        after_inputs(body, 1 + len(terms), len(after)),
        out_shape=tuple(jax.ShapeDtypeStruct((size, rows, cols), bf16) for size in groups),
        grid_spec=pltpu.PrefetchScalarGridSpec(
            num_scalar_prefetch=1,
            grid=(sum(groups),),
            in_specs=[came(place) for _, place, _ in terms] + anywhere(len(after)),
            out_specs=tuple(goes(first, size) for first, size in zip(firsts, groups)),
        ),
        compiler_params=kernel_params(),
        cost_estimate=cost(4),
        name="added",
    )(numbers, *[term[0] for term in terms], *after)


def local(
    tokens,
    doc_lengths,
    cotangent,
    ln1_gain,
    ln1_bias,
    ln2_gain,
    ln2_bias,
    qkv_weight,
    qkv_bias,
    out_weight,
    out_bias,
    up_weight,
    up_bias,
    down_weight,
    down_bias,
):
    rows, width = tokens.shape
    head = width // HEADS
    group = 8
    rep = lax.axis_index("rep")
    shard = lax.axis_index("shard")
    y, h, c = rep // 4, (rep // 2) % 2, rep % 2
    l, x = shard // 4, shard % 4
    ff = up_bias.shape[0]

    pair = jnp.stack([tokens, cotangent])
    below, above, other = move(pair, x=1), move(pair, x=-1), move(pair, l=1)
    far, other_above, other_below = move(below, x=1), move(other, x=-1), move(below, l=1)
    x_other_far, dy_other_far = move(other_below[0], x=1), move(other_above[1], x=-1)
    pairs = (pair, above, far, below, other, other_above, None, other_below)
    x_all = tuple(x_other_far[None] if p is None else p for p in pairs)
    dy_all = tuple(dy_other_far if p is None else p for p in pairs)

    vectors = jnp.concatenate([ln1_gain, ln1_bias, ln2_gain, ln2_bias, qkv_bias])[None]
    place = (y * 2 + c).astype(jnp.int32).reshape(1)
    part = packed(qkv_weight, up_weight, vectors, doc_lengths, place, head)
    part = lax.all_to_all(part, "shard", 0, 0)
    cols = part.shape[-1]
    own, infos = unpacked(part, (pairs[1], pairs[3], pairs[4]))
    below, above = move(own, y=1), move(own, y=-1)
    low, high = halves(below, above, (pairs[2], pairs[5], pairs[7]))
    far_low, far_high = move(low, y=1), move(high, y=-1)
    mine = ((own, 0, 0), (above, 0, 1), (far_low, 0, 2), (far_high, 4, 2), (below, 0, 3))
    yours = tuple((move(array, c=1), first, spot + 4) for array, first, spot in mine)
    steps4 = (y + jnp.arange(4)) % 4
    spots = jnp.concatenate([steps4 * 2 + c, steps4 * 2 + 1 - c]).astype(jnp.int32)
    w_mixed = sorted_weight(mine + yours, spots)

    gains = infos[:, 0, :1024].reshape(8, 4, 256).transpose(1, 0, 2).reshape(4, width)
    qkv_b = infos[:, 0, 1024:].reshape(8 * 3, 1, head)
    qkv_b = jnp.stack(
        [lax.dynamic_index_in_dim(qkv_b, third * 8 + shard, 0, False) for third in range(3)]
    )
    steps8 = jnp.arange(8)
    sources = ((steps8 // 4) ^ l) * 4 + (x + steps8 % 4) % 4
    sources = sources.astype(jnp.int32)
    lengths = infos[:, 1, :3]
    lengths = jnp.sum(
        jnp.where(sources[:, None, None] == steps8[None, :, None], lengths[None], 0.0), 1
    ).astype(jnp.int32)
    ends = jnp.cumsum(lengths, 1)
    starts = ends - lengths
    steps_t = jnp.arange(rows, dtype=jnp.int32)
    segment = jnp.sum((steps_t[None, :, None] >= ends[:, None, :]).astype(jnp.int32), -1)
    slots = jnp.arange(lengths.shape[1], dtype=jnp.int32)
    begin = jnp.sum(
        jnp.where(segment[:, :, None] == slots[None, None, :], starts[:, None, :], 0), -1
    )
    position = (steps_t[None, :] - begin).astype(f32).reshape(group * rows, 1)
    lane = jnp.arange(128)
    freq = 10000.0 ** (-2.0 * (lane % (ROT // 2)).astype(f32) / ROT)
    angle = position * freq[None, :]
    cosine = jnp.where(lane < ROT, jnp.cos(angle), 1.0)
    sine = jnp.sin(angle)
    sine = jnp.where(lane < ROT // 2, -sine, jnp.where(lane < ROT, sine, 0.0))

    both_bias = (out_bias.astype(f32) + down_bias.astype(f32))[None, :]
    wide_bias = lax.dynamic_update_slice(jnp.zeros((1, width), f32), both_bias, (0, shard * 256))
    numbers = jnp.stack([c, shard, y, h]).astype(jnp.int32)

    h1, active, d_hidden, keep, send, mean, inverse, up_sums, dy_sums = feed_forward(
        x_all,
        dy_all,
        gains,
        w_mixed,
        down_weight,
        up_bias.astype(f32)[None],
        numbers,
        3 * head,
        (cosine, sine),
    )
    got = move(send, c=1)
    attended, d_qkv, a_keep, a_send, qkv_sums = attend(
        h1, dy_all, w_mixed, out_weight, qkv_b, cosine, sine, lengths, numbers, (send,)
    )

    def turn(k):
        return lambda i, n: (n[2] + k) % 4 * 2 + i % 2

    low, high = added([(keep, turn(2), None), (got, turn(2), None)], (1, 1), numbers, (attended,))
    from_low, from_high = move(low, y=1), move(high, y=-1)
    a_got = move(a_send, c=1)
    mix = mixed_part(
        active, attended, down_weight, out_weight, wide_bias, sources, (low, high)
    )

    def sides(i, n):
        return (n[2] + 1 + i // 2 * 2) % 4 * 2 + i % 2

    above, below = added(
        [
            (keep, sides, None),
            (got, sides, None),
            (from_low, lambda i, n: 0, (0,)),
            (from_high, lambda i, n: 0, (3,)),
        ],
        (2, 2),
        numbers,
        (mix,),
    )
    from_below, from_above = move(above, y=1), move(below, y=-1)
    def away(i, n):
        return i * 2 + 1 - n[3]

    (a_away,) = added([(a_keep, away, None), (a_got, away, None)], (4,), numbers, (above,))
    a_crossed = move(a_away, h=1)
    norm_sums, *sums = back_norms(
        d_qkv,
        d_hidden,
        w_mixed,
        x_all,
        mean,
        inverse,
        jnp.stack([gains[0], gains[2]]),
        (a_away,),
    )

    def ends_at(i, n):
        return n[2] * 2 + jnp.where(i == 0, 1 - n[3], n[3])

    def crosses(i, n):
        return jnp.where(i == 0, 1 - n[3], n[3])

    leaves, inner = added(
        [
            (keep, ends_at, None),
            (got, ends_at, None),
            (from_below, crosses, None),
            (from_above, crosses, None),
        ],
        (1, 1),
        numbers,
        (sums[0],),
    )
    crossed = move(leaves, h=1)

    def around(i, n):
        return (n[2] + 2 - i) % 4

    def around_here(i, n):
        return around(i, n) * 2 + n[3]

    a_far, a_above, a_own, a_below = added(
        [
            (a_keep, around_here, None),
            (a_got, around_here, None),
            (a_crossed, around, None),
        ],
        (1, 1, 1, 1),
        numbers,
        (),
    )
    a_low, a_high = move(a_far[0, :32], y=1), move(a_far[0, 32:], y=-1)
    ((inner,),) = added(
        [(inner, lambda i, n: 0, None), (crossed, lambda i, n: 0, None)],
        (1,),
        numbers,
        (a_low, a_high),
    )
    a_above = jnp.concatenate(
        [a_above[0, :32].astype(f32) + a_low.astype(f32), a_above[0, 32:].astype(f32)], 0
    )
    a_below = jnp.concatenate(
        [a_below[0, :32].astype(f32), a_below[0, 32:].astype(f32) + a_high.astype(f32)], 0
    )
    a_from_below, a_from_above = move(a_above.astype(bf16), y=1), move(a_below.astype(bf16), y=-1)

    part, down_stays, out_stays = packed_sums(
        inner, a_own[0], a_from_below, a_from_above, ff, head, ()
    )
    part = lax.all_to_all(part, "shard", 0, 0)
    inner, a_sum = unpacked_sums(part, down_stays, out_stays, ff, head, ())
    inner = jnp.stack([inner, move(inner, h=1)])

    def ring(pieces, way):
        own, above, far, below = pieces if way == 1 else (pieces[n] for n in (0, 3, 2, 1))
        passed = move(far, x=way)
        above = (above.astype(f32) + passed.astype(f32)).astype(bf16)
        return (
            own.astype(f32) + move(above, x=way).astype(f32) + move(below, x=-way).astype(f32)
        )

    sum_other = move(ring(sums[4:], 1).astype(bf16), l=1)
    own_sum = ring(sums[:4], -1) + sum_other.astype(f32)
    mixed = lax.psum_scatter(mix, "shard", scatter_dimension=0, tiled=True)
    mixed = (tokens.astype(f32) + mixed.astype(f32)).astype(bf16)
    own_normed, own_inverse = normalize(tokens)
    tokens_grad = cotangent.astype(f32) + own_inverse * (
        own_sum
        - jnp.mean(own_sum, -1, keepdims=True)
        - own_normed * jnp.mean(own_sum * own_normed, -1, keepdims=True)
    )

    smalls = small_sums(norm_sums, qkv_sums, up_sums, dy_sums, numbers)
    smalls = jnp.broadcast_to(smalls[None], (16, 8, 24, 128)).reshape(128, 24, 128)
    smalls = lax.all_to_all(smalls, BOTH, 0, 0)
    smalls = jnp.sum(smalls.astype(f32), 0)
    norm_grads = smalls[:8].reshape(4, 256)
    dy_total = smalls[22:].reshape(256)

    below, above = move(inner, y=1), move(inner, y=-1)
    far_low, far_high = move(below[:1], y=1), move(above[1:], y=-1)
    pieces = [(v, move(v, c=1)) for v in (inner, above, far_low, far_high, below)]
    order = ((0, h), (0, 1 - h), (1, h), (1, 1 - h), (2, h), (2, 1 - h), (3, h), (3, 1 - h))
    places = jnp.stack([(y + k) % 4 * 2 + high for k, high in order]).astype(jnp.int32)
    up_parts = [
        (source * ff, 64 + 16 * (source % 4), source // 4 * ff, ff) for source in range(8)
    ]
    down_grad, up_grad = spread(
        pieces,
        places,
        numbers[:1],
        [(width, 64, [(0, 0, 0, width)]), (8 * ff, 16, up_parts)],
    )

    a_sum = jnp.stack(ring_gather(a_sum, "y", 32))
    a_other = move(a_sum, h=1)
    places = jnp.concatenate([steps4 * 2 + h, steps4 * 2 + 1 - h]).astype(jnp.int32)
    out_grad, qkv_grad = spread(
        [(a_sum, move(a_sum, c=1)), (a_other, move(a_other, c=1))],
        places,
        numbers[:1],
        [
            (width, 16, [(0, 48, 0, width)]),
            (3 * width, 16, [(n * width, 16 * n, 0, width) for n in range(3)]),
        ],
    )
    return (
        mixed,
        tokens_grad,
        norm_grads[0],
        norm_grads[1],
        norm_grads[2],
        norm_grads[3],
        qkv_grad,
        smalls[8:14].reshape(768),
        out_grad,
        dy_total,
        up_grad,
        smalls[14:22].reshape(ff),
        down_grad,
        dy_total,
    )


def solution(mesh):
    rows = P(BOTH, None)
    vector, matrix = P("shard"), P("shard", None)
    return jax.shard_map(
        local,
        mesh=mesh,
        in_specs=(rows, rows, rows, vector, vector, vector, vector)
        + (matrix, vector, matrix, vector, matrix, vector, matrix, vector),
        out_specs=(rows, rows, vector, vector, vector, vector)
        + (matrix, vector, matrix, vector, matrix, vector, matrix, vector),
        check_vma=False,
    )
```

```python
import functools
import math

import jax
import jax.numpy as jnp
from jax import lax
from jax.experimental import pallas as pl
from jax.experimental.pallas import tpu as pltpu
from jax.sharding import PartitionSpec as P

HEADS = 8
ROT = 64
EPS = 1e-05
f32 = jnp.float32
bf16 = jnp.bfloat16


def cost(time):
    return pl.CostEstimate(flops=int(time * 1.15e9), bytes_accessed=1000, transcendentals=0)


BOTH = ("rep", "shard")
SIZES = (4, 2, 2, 2, 4)
SAME_CORE = [[2 * n + c for n in range(8)] for c in range(2)]
SAME_CORE_ALL = [[(2 * n + c) * 8 + s for n in range(8) for s in range(8)] for c in range(2)]


def coords():
    for y in range(4):
        for h in range(2):
            for c in range(2):
                for l in range(2):
                    for x in range(4):
                        yield (y, h, c, l, x)


def linear(t):
    y, h, c, l, x = (v % m for v, m in zip(t, SIZES))
    return ((y * 2 + h) * 2 + c) * 8 + l * 4 + x


def move(value, y=0, h=0, c=0, l=0, x=0):
    step = (y, h, c, l, x)
    pairs = [(linear(t), linear(tuple(a + b for a, b in zip(t, step)))) for t in coords()]
    return lax.ppermute(value, BOTH, pairs)


def pick(value, index, axis):
    return lax.dynamic_index_in_dim(value, index, axis, keepdims=False)


def normalize(value):
    xf = value.astype(f32)
    centre = xf - jnp.mean(xf, -1, keepdims=True)
    inverse = lax.rsqrt(jnp.mean(centre * centre, -1, keepdims=True) + EPS)
    return centre * inverse, inverse


def kernel_params():
    return pltpu.CompilerParams(vmem_limit_bytes=56 * 1024 * 1024)


def after_inputs(body, count, extra):
    return lambda *refs: body(*refs[:count], *refs[count + extra :])


def anywhere(count):
    return [pl.BlockSpec(memory_space=pl.ANY)] * count


def dot(a, b, ca=1, cb=0):
    return lax.dot_general(a, b, (((ca,), (cb,)), ((), ())), preferred_element_type=f32)


def swap_halves(value):
    lane = lax.broadcasted_iota(jnp.int32, value.shape, 1)
    return jnp.where(lane < 32, pltpu.roll(value, 96, 1), pltpu.roll(value, 32, 1))


def allowed_mask(lengths_ref, block, rows):
    e0 = lengths_ref[block, 0]
    e1 = e0 + lengths_ref[block, 1]
    t = lax.broadcasted_iota(jnp.int32, (rows, rows), 0)
    s = lax.broadcasted_iota(jnp.int32, (rows, rows), 1)
    seg_t = (t >= e0).astype(jnp.int32) + (t >= e1).astype(jnp.int32)
    seg_s = (s >= e0).astype(jnp.int32) + (s >= e1).astype(jnp.int32)
    return (seg_t == seg_s) & (s <= t)


def dot_rows(a, b):
    return lax.dot_general(a, b, (((0,), (0,)), ((), ())), preferred_element_type=f32)


def loads(copies):
    for copy in copies:
        copy.start()
    return copies


def piece_copies(pieces, half, target, sems, rows):
    return [
        pltpu.make_async_copy(
            piece.at[half] if len(piece.shape) == 3 else piece,
            target.at[pl.ds(at * rows, rows)],
            sems.at[at],
        )
        for at, piece in enumerate(pieces)
    ]


def weight_copies(pieces, refs, spot_ref, target, lanes, sems):
    return [
        pltpu.make_async_copy(
            ref.at[:, :, lanes],
            target.at[pl.ds(first, array.shape[0]), spot_ref[spot]],
            sems.at[at],
        )
        for at, (ref, (array, first, spot)) in enumerate(zip(refs, pieces))
    ]


def feed_forward(x, dy, gains, weight, spots, down, bias, numbers, first, after):
    rows, width = x[0].shape[1:]
    count = len(x)
    total = rows * count
    ff = bias.shape[1]

    parts = len(weight)

    def body(number_ref, spot_ref, g_ref, b_ref, *refs):
        w_refs, refs = refs[:parts], refs[parts:]
        x_refs, dy_refs, d_hbm = refs[:count], refs[count : 2 * count], refs[2 * count]
        (h1_hbm, act_hbm, du_hbm, keep_hbm, send_hbm, m_ref, i_ref, db_ref, sum_ref) = refs[
            2 * count + 1 : 2 * count + 10
        ]
        (x_v, dy_v, h1_v, h2_v, w_v, d_v, act_v, du_v, keep_v, send_v, x_sem, dy_sem, w_sem, sems) = refs[
            2 * count + 10 :
        ]
        own = number_ref[0] == 0
        x_copies = loads(piece_copies(x_refs, 0, x_v, x_sem, rows))
        w_copies = loads(
            weight_copies(weight, w_refs, spot_ref, w_v, pl.ds(first, ff), w_sem)
        )
        dy_copies = loads(piece_copies(dy_refs, 1, dy_v, dy_sem, rows))
        d_copy = pltpu.make_async_copy(d_hbm, d_v, sems.at[1])
        d_copy.start()
        for copy in x_copies:
            copy.wait()

        @pl.loop(0, count)
        def _(n):
            at = pl.ds(pl.multiple_of(n * rows, rows), rows)
            value = x_v[at, :].astype(f32)
            mean = jnp.mean(value, 1, keepdims=True)
            centre = value - mean
            inverse = lax.rsqrt(jnp.mean(centre * centre, 1, keepdims=True) + EPS)
            normed = centre * inverse
            m_ref[at, :] = mean
            i_ref[at, :] = inverse
            h1_v[at, :] = (normed * g_ref[0:1] + g_ref[1:2]).astype(bf16)
            h2_v[at, :] = (normed * g_ref[2:3] + g_ref[3:4]).astype(bf16)

        h1_copy = pltpu.make_async_copy(h1_v, h1_hbm, sems.at[2])
        h1_copy.start()
        for copy in w_copies + dy_copies:
            copy.wait()
        d_copy.wait()
        mine = dy_v[:, pl.ds(pl.multiple_of(number_ref[1] * 256, 256), 256)]
        sum_ref[...] = jnp.sum(mine.astype(f32), 0, keepdims=True)

        def split(part, places, high, wide):
            at = (places, high, wide)

            @pl.when(own)
            def _():
                keep_v[at] = part[:, 0]
                send_v[at] = part[:, 1]

            @pl.when(jnp.logical_not(own))
            def _():
                keep_v[at] = part[:, 1]
                send_v[at] = part[:, 0]

        def leaving(n):
            at = (pl.ds(n * 2, 2), pl.ds(0, 64))
            return (
                pltpu.make_async_copy(keep_v.at[at], keep_hbm.at[at], sems.at[3]),
                pltpu.make_async_copy(send_v.at[at], send_hbm.at[at], sems.at[4]),
            )

        @pl.loop(0, ff // 256)
        def _(n):
            at = pl.ds(pl.multiple_of(n * 256, 256), 256)
            u = dot(h2_v[...], w_v[:, :, :, at].reshape(width, 256)) + b_ref[:, at]
            cdf = 0.5 * (1.0 + lax.erf(u * math.sqrt(0.5)))
            pdf = jnp.exp(-0.5 * u * u) * (1.0 / math.sqrt(2.0 * math.pi))
            act = (u * cdf).astype(bf16)
            act_v[:, at] = act
            du = (dot(dy_v[...], d_v[at, :], 1, 1) * (cdf + u * pdf)).astype(bf16)
            du_v[:, at] = du
            db_ref[:, at] = jnp.sum(du.astype(f32), 0, keepdims=True)
            part = dot_rows(act, dy_v[...]).astype(bf16).reshape(2, 2, 64, width)
            split(part, pl.ds(n * 2, 2), pl.ds(0, 64), slice(None))
            for copy in leaving(n):
                copy.start()

        act_copy = pltpu.make_async_copy(act_v, act_hbm, sems.at[0])
        act_copy.start()
        du_copy = pltpu.make_async_copy(du_v, du_hbm, sems.at[1])
        du_copy.start()
        for n in range(ff // 256):
            for copy in leaving(n):
                copy.wait()

        def block(n):
            at = (
                slice(None),
                pl.ds(pl.multiple_of(64 + 16 * (n % 4), 16), 16),
                pl.ds(pl.multiple_of(n // 4 * ff, ff), ff),
            )
            return at

        def away(n):
            at = block(n)
            return (
                pltpu.make_async_copy(keep_v.at[at], keep_hbm.at[at], sems.at[3]),
                pltpu.make_async_copy(send_v.at[at], send_hbm.at[at], sems.at[4]),
            )

        @pl.loop(0, 8)
        def _(n):
            lanes = pl.ds(pl.multiple_of(n * 256, 256), 256)
            part = dot_rows(h2_v[:, lanes], du_v[...]).astype(bf16).reshape(8, 2, 16, ff)
            split(part, *block(n))
            for copy in away(n):
                copy.start()

        for n in range(8):
            for copy in away(n):
                copy.wait()
        h1_copy.wait()
        act_copy.wait()
        du_copy.wait()

    wide = jax.ShapeDtypeStruct((total, width), bf16)
    thin = jax.ShapeDtypeStruct((total, ff), bf16)
    column = jax.ShapeDtypeStruct((total, 1), f32)
    grads = jax.ShapeDtypeStruct((8, 128, width), bf16)
    vmem = pl.BlockSpec(memory_space=pltpu.VMEM)
    return pl.pallas_call(
        after_inputs(body, 5 + parts + 2 * count, len(after)),
        out_shape=(
            wide,
            thin,
            thin,
            grads,
            grads,
            column,
            column,
            jax.ShapeDtypeStruct((1, ff), f32),
            jax.ShapeDtypeStruct((1, 256), f32),
        ),
        in_specs=[pl.BlockSpec(memory_space=pltpu.SMEM)] * 2
        + [vmem, vmem]
        + anywhere(parts + 2 * count + 1 + len(after)),
        out_specs=tuple(anywhere(5)) + (vmem,) * 4,
        scratch_shapes=[
            pltpu.VMEM((total, width), bf16),
            pltpu.VMEM((total, width), bf16),
            pltpu.VMEM((total, width), bf16),
            pltpu.VMEM((total, width), bf16),
            pltpu.VMEM((8, 8, width // 64, ff), bf16),
            pltpu.VMEM((ff, width), bf16),
            pltpu.VMEM((total, ff), bf16),
            pltpu.VMEM((total, ff), bf16),
            pltpu.VMEM((8, 128, width), bf16),
            pltpu.VMEM((8, 128, width), bf16),
            pltpu.SemaphoreType.DMA((count,)),
            pltpu.SemaphoreType.DMA((count,)),
            pltpu.SemaphoreType.DMA((parts,)),
            pltpu.SemaphoreType.DMA((5,)),
        ],
        compiler_params=kernel_params(),
        cost_estimate=cost(32),
        name="feed_forward",
    )(numbers, spots, gains, bias, *[p[0] for p in weight], *x, *dy, down, *after)


def attend(h1, dy, weight, spots, out, bias, cosine, sine, lengths, numbers, after, rows=128):
    total, width = h1.shape
    count = len(dy)
    head = out.shape[0]
    scale = head ** (-0.5)

    parts = len(weight)

    def body(number_ref, len_ref, spot_ref, b_ref, *refs):
        w_refs, refs = refs[:parts], refs[parts:]
        dy_refs = refs[:count]
        h1_hbm, out_hbm, cos_hbm, sin_hbm = refs[count : count + 4]
        ol_hbm, dq_hbm, keep_hbm, send_hbm, sum_ref = refs[count + 4 : count + 9]
        (dy_v, h1_v, w_v, wo_v, cos_v, sin_v, qkv_v, do_v, ol_v, dq_v, keep_v, send_v, dy_sem, w_sem, sems) = (
            refs[count + 9 :]
        )
        own = number_ref[0] == 0
        pairs = (
            (h1_hbm, h1_v),
            (out_hbm, wo_v),
            (cos_hbm, cos_v),
            (sin_hbm, sin_v),
        )
        copies = loads(
            [pltpu.make_async_copy(*pair, sems.at[n]) for n, pair in enumerate(pairs)]
        )
        w_copies = loads(
            weight_copies(weight, w_refs, spot_ref, w_v, pl.ds(0, 3 * head), w_sem)
        )
        dy_copies = loads(piece_copies(dy_refs, 1, dy_v, dy_sem, rows))
        for copy in copies[:1] + w_copies:
            copy.wait()

        @pl.loop(0, 3)
        def _(n):
            at = pl.ds(pl.multiple_of(n * head, head), head)
            qkv_v[:, at] = dot(h1_v[...], w_v[:, :, :, at].reshape(width, head)) + b_ref[n]

        for copy in copies[1:] + dy_copies:
            copy.wait()
        do_v[...] = dot(dy_v[...], wo_v[...], 1, 1).astype(bf16)
        sum_ref[...] = jnp.zeros_like(sum_ref)

        @pl.loop(0, total // rows)
        def _(block):
            at = pl.ds(pl.multiple_of(block * rows, rows), rows)
            cos, sin = cos_v[at, :], sin_v[at, :]

            def turned(value, sign):
                left = value[:, :128]
                left = left * cos + swap_halves(left) * (sin * sign)
                return jnp.concatenate([left, value[:, 128:]], 1).astype(bf16)

            q, k = turned(qkv_v[at, 0:head], 1.0), turned(qkv_v[at, head : 2 * head], 1.0)
            v = qkv_v[at, 2 * head :].astype(bf16)
            scores = dot(q, k, 1, 1) * scale
            masked = jnp.where(allowed_mask(len_ref, block, rows), scores, -1e30)
            shifted = jnp.exp(masked - jnp.max(masked, 1, keepdims=True))
            probs = shifted / jnp.sum(shifted, 1, keepdims=True)
            low = probs.astype(bf16)
            ol_v[at, :] = dot(low, v).astype(bf16)
            d_out = do_v[at, :]
            d_value = dot(low, d_out, 0, 0)
            d_probs = dot(d_out, v, 1, 1)
            centred = d_probs - jnp.sum(d_probs * probs, 1, keepdims=True)
            d_scores = (probs * centred).astype(bf16)
            d_query = turned(dot(d_scores, k) * scale, -1.0)
            d_key = turned(dot(d_scores, q, 0, 0) * scale, -1.0)
            for n, grad in enumerate((d_query, d_key, d_value.astype(bf16))):
                lanes = slice(n * head, (n + 1) * head)
                dq_v[at, lanes] = grad
                sum_ref[:, lanes] += jnp.sum(grad.astype(f32), 0, keepdims=True)

        ol_copy = pltpu.make_async_copy(ol_v, ol_hbm, sems.at[0])
        ol_copy.start()
        dq_copy = pltpu.make_async_copy(dq_v, dq_hbm, sems.at[1])
        dq_copy.start()

        def split(part, high, wide):
            at = (slice(None), high, wide)

            @pl.when(own)
            def _():
                keep_v[at] = part[:, 0]
                send_v[at] = part[:, 1]

            @pl.when(jnp.logical_not(own))
            def _():
                keep_v[at] = part[:, 1]
                send_v[at] = part[:, 0]

        part = dot_rows(ol_v[...], dy_v[...]).astype(bf16).reshape(8, 2, 16, width)
        split(part, pl.ds(48, 16), slice(None))

        @pl.loop(0, 8)
        def _(n):
            lanes = pl.ds(pl.multiple_of(n * 256, 256), 256)
            part = dot_rows(h1_v[:, lanes], dq_v[...]).astype(bf16).reshape(8, 2, 16, 3 * head)
            for third in range(3):
                split(
                    part[..., third * head : (third + 1) * head],
                    pl.ds(16 * third, 16),
                    pl.ds(pl.multiple_of(n * head, head), head),
                )

        keep_copy = pltpu.make_async_copy(keep_v, keep_hbm, sems.at[2])
        keep_copy.start()
        send_copy = pltpu.make_async_copy(send_v, send_hbm, sems.at[3])
        send_copy.start()
        for copy in (ol_copy, dq_copy, keep_copy, send_copy):
            copy.wait()

    grads = jax.ShapeDtypeStruct((8, 64, width), bf16)
    vmem = pl.BlockSpec(memory_space=pltpu.VMEM)
    smem = pl.BlockSpec(memory_space=pltpu.SMEM)
    return pl.pallas_call(
        after_inputs(body, 8 + parts + count, len(after)),
        out_shape=(
            jax.ShapeDtypeStruct((total, head), bf16),
            jax.ShapeDtypeStruct((total, 3 * head), bf16),
            grads,
            grads,
            jax.ShapeDtypeStruct((1, 3 * head), f32),
        ),
        in_specs=[smem, smem, smem, vmem] + anywhere(parts + count + 4 + len(after)),
        out_specs=tuple(anywhere(4)) + (vmem,),
        scratch_shapes=[
            pltpu.VMEM((total, width), bf16),
            pltpu.VMEM((total, width), bf16),
            pltpu.VMEM((8, 8, width // 64, 3 * head), bf16),
            pltpu.VMEM((head, width), bf16),
            pltpu.VMEM((total, 128), f32),
            pltpu.VMEM((total, 128), f32),
            pltpu.VMEM((total, 3 * head), f32),
            pltpu.VMEM((total, head), bf16),
            pltpu.VMEM((total, head), bf16),
            pltpu.VMEM((total, 3 * head), bf16),
            pltpu.VMEM((8, 64, width), bf16),
            pltpu.VMEM((8, 64, width), bf16),
            pltpu.SemaphoreType.DMA((count,)),
            pltpu.SemaphoreType.DMA((parts,)),
            pltpu.SemaphoreType.DMA((4,)),
        ],
        compiler_params=kernel_params(),
        cost_estimate=cost(22),
        name="attend",
    )(
        numbers,
        lengths,
        spots,
        bias,
        *[p[0] for p in weight],
        *dy,
        h1,
        out,
        cosine,
        sine,
        *after,
    )


def mixed_part(active, attended, down, out, bias, sources, after):
    rows, ff = active.shape
    head, width = out.shape
    step = 512

    def body(source_ref, act_ref, ol_ref, wd_ref, wo_ref, b_ref, mix_ref):
        total = dot(act_ref[...], wd_ref[...]) + dot(ol_ref[...], wo_ref[...]) + b_ref[...]
        total = total.astype(bf16)
        for at in range(rows // 128):
            to = pl.ds(pl.multiple_of(source_ref[at] * 128, 128), 128)
            mix_ref[to, :] = total[at * 128 : (at + 1) * 128]

    return pl.pallas_call(
        after_inputs(body, 6, len(after)),
        out_shape=jax.ShapeDtypeStruct((rows, width), bf16),
        grid_spec=pltpu.PrefetchScalarGridSpec(
            num_scalar_prefetch=1,
            grid=(width // step,),
            in_specs=[
                pl.BlockSpec((rows, ff), lambda i, n: (0, 0)),
                pl.BlockSpec((rows, head), lambda i, n: (0, 0)),
                pl.BlockSpec((ff, step), lambda i, n: (0, i)),
                pl.BlockSpec((head, step), lambda i, n: (0, i)),
                pl.BlockSpec((1, step), lambda i, n: (0, i)),
            ]
            + anywhere(len(after)),
            out_specs=pl.BlockSpec((rows, step), lambda i, n: (0, i)),
        ),
        compiler_params=kernel_params(),
        cost_estimate=cost(10),
        name="mixed_part",
    )(sources, active, attended, down, out, bias, *after)


def packed(qkv_weight, up_weight, vectors, lengths, place, head, tokens, cotangent):
    wide, up_wide = qkv_weight.shape[1], up_weight.shape[1]
    part, up_part = 3 * head, up_wide // 8
    cols = part + up_part

    def body(place_ref, len_ref, q_ref, u_ref, x_ref, dy_ref, *refs):
        v_refs, out_ref, pair_ref = refs[: len(vectors)], refs[-2], refs[-1]
        pair_ref[0] = x_ref[...]
        pair_ref[1] = dy_ref[...]
        lane = lax.broadcasted_iota(jnp.int32, (8, cols), 1)
        row = lax.broadcasted_iota(jnp.int32, (8, cols), 0)
        sizes = jnp.zeros((8, cols), f32)
        for at in range(3):
            sizes = jnp.where(lane == at, len_ref[0, at].astype(f32), sizes)
        vector = jnp.concatenate([ref[...].astype(f32) for ref in v_refs], 1)
        vector = jnp.broadcast_to(vector, (8, cols))
        tail = jnp.where(row == 0, vector, jnp.where(row == 1, sizes, 0.0)).astype(bf16)
        for owner in range(8):
            pieces = [
                q_ref[:, (third * 8 + owner) * head : (third * 8 + owner + 1) * head]
                for third in range(3)
            ]
            pieces.append(u_ref[:, owner * up_part : (owner + 1) * up_part])
            out_ref[owner] = jnp.concatenate([jnp.concatenate(pieces, 1), tail], 0)

    return pl.pallas_call(
        body,
        out_shape=(
            jax.ShapeDtypeStruct((8, 40, cols), bf16),
            jax.ShapeDtypeStruct((2,) + tokens.shape, bf16),
        ),
        grid_spec=pltpu.PrefetchScalarGridSpec(
            num_scalar_prefetch=2,
            grid=(1,),
            in_specs=[
                pl.BlockSpec((32, wide), lambda i, place, lens: (place[0], 0)),
                pl.BlockSpec((32, up_wide), lambda i, place, lens: (place[0], 0)),
                pl.BlockSpec(tokens.shape, lambda i, place, lens: (0, 0)),
                pl.BlockSpec(tokens.shape, lambda i, place, lens: (0, 0)),
            ]
            + [pl.BlockSpec(v.shape, lambda i, place, lens: (0, 0)) for v in vectors],
            out_specs=(
                pl.BlockSpec((8, 40, cols), lambda i, place, lens: (0, 0, 0)),
                pl.BlockSpec((2,) + tokens.shape, lambda i, place, lens: (0, 0, 0)),
            ),
        ),
        compiler_params=kernel_params(),
        cost_estimate=cost(3),
        name="packed",
    )(place, lengths, qkv_weight, up_weight, tokens, cotangent, *vectors)


def back_norms(d_qkv, d_hidden, weight, spots, tokens, mean, inverse, gains, after):
    total, n1 = d_qkv.shape
    n2 = d_hidden.shape[1]
    count = len(tokens)
    parts = len(weight)
    width = tokens[0].shape[-1]
    step = 512

    def body(spot_ref, m_ref, i_ref, g_ref, *refs):
        w_refs, x_refs = refs[:parts], refs[parts : parts + count]
        dq_hbm, du_hbm = refs[parts + count : parts + count + 2]
        sums_ref = refs[parts + count + 2]
        outs = refs[parts + count + 3 : parts + 2 * count + 3]
        dq_v, du_v, w_v, x_v, s_v, w_sem, x_sem, sems = refs[parts + 2 * count + 3 :]
        copies = loads(
            [
                pltpu.make_async_copy(dq_hbm, dq_v, sems.at[0]),
                pltpu.make_async_copy(du_hbm, du_v, sems.at[1]),
            ]
            + weight_copies(weight, w_refs, spot_ref, w_v, slice(None), w_sem)
            + piece_copies(x_refs, 0, x_v, x_sem, 128)
        )
        for copy in copies:
            copy.wait()

        def leaving(n):
            lanes = pl.ds(pl.multiple_of(n * step, step), step)
            return [
                pltpu.make_async_copy(
                    s_v.at[pl.ds(at * 128, 128), lanes], outs[at].at[:, lanes], x_sem.at[at]
                )
                for at in range(count)
            ]

        @pl.loop(0, width // step)
        def _(n):
            lanes = pl.ds(pl.multiple_of(n * step, step), step)
            sources = pl.ds(n * (step // 256), step // 256)
            d1 = dot(dq_v[...], w_v[sources, :, :, 0:n1].reshape(step, n1), 1, 1)
            d2 = dot(du_v[...], w_v[sources, :, :, n1:].reshape(step, n2), 1, 1)
            s_v[:, lanes] = (d1 * g_ref[0:1, lanes] + d2 * g_ref[1:2, lanes]).astype(bf16)
            for copy in leaving(n):
                copy.start()
            normed = (x_v[:, lanes].astype(f32) - m_ref[...]) * i_ref[...]
            sums_ref[0:1, lanes] = jnp.sum(d1 * normed, 0, keepdims=True)
            sums_ref[1:2, lanes] = jnp.sum(d1, 0, keepdims=True)
            sums_ref[2:3, lanes] = jnp.sum(d2 * normed, 0, keepdims=True)
            sums_ref[3:4, lanes] = jnp.sum(d2, 0, keepdims=True)

        for n in range(width // step):
            for copy in leaving(n):
                copy.wait()

    vmem = pl.BlockSpec(memory_space=pltpu.VMEM)
    return pl.pallas_call(
        after_inputs(body, 6 + parts + count, len(after)),
        out_shape=(jax.ShapeDtypeStruct((4, width), f32),)
        + (jax.ShapeDtypeStruct((128, width), bf16),) * count,
        in_specs=[pl.BlockSpec(memory_space=pltpu.SMEM), vmem, vmem, vmem]
        + anywhere(parts + count + 2 + len(after)),
        out_specs=(vmem,) + tuple(anywhere(count)),
        scratch_shapes=[
            pltpu.VMEM((total, n1), bf16),
            pltpu.VMEM((total, n2), bf16),
            pltpu.VMEM((8, 8, width // 64, n1 + n2), bf16),
            pltpu.VMEM((total, width), bf16),
            pltpu.VMEM((total, width), bf16),
            pltpu.SemaphoreType.DMA((parts,)),
            pltpu.SemaphoreType.DMA((count,)),
            pltpu.SemaphoreType.DMA((2,)),
        ],
        compiler_params=kernel_params(),
        cost_estimate=cost(14),
        name="back_norms",
    )(spots, mean, inverse, gains, *[p[0] for p in weight], *tokens, d_qkv, d_hidden, *after)


def unpacked(part, after):
    owners, _, cols = part.shape

    def body(part_ref, rows_ref, info_ref):
        for owner in range(owners):
            rows_ref[owner] = part_ref[owner, 0:32]
            info_ref[owner] = part_ref[owner, 32:40].astype(f32)

    return pl.pallas_call(
        after_inputs(body, 1, len(after)),
        out_shape=(
            jax.ShapeDtypeStruct((owners, 32, cols), bf16),
            jax.ShapeDtypeStruct((owners, 8, cols), f32),
        ),
        in_specs=[pl.BlockSpec(memory_space=pltpu.VMEM)] + anywhere(len(after)),
        out_specs=(pl.BlockSpec(memory_space=pltpu.VMEM),) * 2,
        compiler_params=kernel_params(),
        cost_estimate=cost(3),
        name="unpacked",
    )(part, *after)


def halves(below, above, after):
    count, rows, cols = below.shape
    half = (count // 2, rows, cols) if count > 1 else (1, rows // 2, cols)
    at = (1, 0, 0) if count > 1 else (0, 1, 0)

    def body(below_ref, above_ref, low_ref, high_ref):
        low_ref[...] = below_ref[...]
        high_ref[...] = above_ref[...]

    out = jax.ShapeDtypeStruct(half, bf16)
    return pl.pallas_call(
        after_inputs(body, 2, len(after)),
        out_shape=(out, out),
        grid=(1,),
        in_specs=[
            pl.BlockSpec(half, lambda i: (0, 0, 0)),
            pl.BlockSpec(half, lambda i: at),
        ]
        + anywhere(len(after)),
        out_specs=(pl.BlockSpec(half, lambda i: (0, 0, 0)),) * 2,
        compiler_params=kernel_params(),
        cost_estimate=cost(3),
        name="halves",
    )(below, above, *after)


def packed_sums(inner, own, below, above, ff, head, after):
    width = inner.shape[1]

    def body(inner_ref, own_ref, below_ref, above_ref, out_ref, down_ref, stay_ref):
        total = own_ref[...].astype(f32) + below_ref[...].astype(f32) + above_ref[...].astype(f32)
        total = total.astype(bf16)
        for owner in range(8):
            pieces = [
                total[16 * third : 16 * third + 16, owner * head : (owner + 1) * head]
                for third in range(3)
            ]
            row, col = 64 + 16 * (owner % 4), owner // 4 * ff
            pieces.append(inner_ref[row : row + 16, col : col + ff])
            out_ref[owner] = jnp.concatenate(pieces, 1)
        down_ref[...] = inner_ref[0:64, :]
        stay_ref[...] = total[48:64]

    vmem = pl.BlockSpec(memory_space=pltpu.VMEM)
    return pl.pallas_call(
        after_inputs(body, 4, len(after)),
        out_shape=(
            jax.ShapeDtypeStruct((8, 16, 3 * head + ff), bf16),
            jax.ShapeDtypeStruct((64, width), bf16),
            jax.ShapeDtypeStruct((16, width), bf16),
        ),
        in_specs=[vmem] * 4 + anywhere(len(after)),
        out_specs=(vmem,) * 3,
        compiler_params=kernel_params(),
        cost_estimate=cost(3),
        name="packed_sums",
    )(inner, own, below, above, *after)


def unpacked_sums(part, down, stay, ff, head, after):
    width = down.shape[1]

    def body(part_ref, down_ref, stay_ref, inner_ref, out_ref):
        inner_ref[0:64] = down_ref[...]
        out_ref[48:64] = stay_ref[...]
        for source in range(8):
            for third in range(3):
                out_ref[16 * third : 16 * third + 16, source * head : (source + 1) * head] = part_ref[
                    source, :, third * head : (third + 1) * head
                ]
            row, col = 64 + 16 * (source % 4), source // 4 * ff
            inner_ref[row : row + 16, col : col + ff] = part_ref[source, :, 3 * head :]

    vmem = pl.BlockSpec(memory_space=pltpu.VMEM)
    return pl.pallas_call(
        after_inputs(body, 3, len(after)),
        out_shape=(
            jax.ShapeDtypeStruct((128, width), bf16),
            jax.ShapeDtypeStruct((64, width), bf16),
        ),
        in_specs=[vmem] * 3 + anywhere(len(after)),
        out_specs=(vmem,) * 2,
        compiler_params=kernel_params(),
        cost_estimate=cost(3),
        name="unpacked_sums",
    )(part, down, stay, *after)


def spread(pieces, places, core, targets, count, before, after):
    rows, cols = pieces[0][0].shape[1:]
    firsts, total = [], 0
    for mine, _ in pieces:
        firsts.append(total)
        total += mine.shape[0]

    def body(place_ref, core_ref, *refs):
        step = pl.program_id(0)
        outs = refs[2 * len(pieces) + len(before) :]
        first_core = core_ref[0] == 0

        def fill(ref, low):
            for out_ref, (_, high, parts) in zip(outs, targets):
                for to, row, col, size in parts:
                    out_ref[low * high : (low + 1) * high, to : to + size] = ref[
                        0, row : row + high, col : col + size
                    ].astype(f32)

        for n, (first, (mine, _)) in enumerate(zip(firsts, pieces)):
            here = (step >= first) & (step < first + mine.shape[0])

            @pl.when(here & first_core)
            def _(n=n):
                fill(refs[2 * n], 0)
                fill(refs[2 * n + 1], 1)

            @pl.when(here & jnp.logical_not(first_core))
            def _(n=n):
                fill(refs[2 * n], 1)
                fill(refs[2 * n + 1], 0)

    def chosen(first, size):
        return pl.BlockSpec(
            (1, rows, cols), lambda i, place, core: (jnp.clip(i - first, 0, size - 1), 0, 0)
        )

    specs, arrays = [], []
    for first, (mine, yours) in zip(firsts, pieces):
        specs += [chosen(first, mine.shape[0])] * 2
        arrays += [mine, yours]
    return pl.pallas_call(
        after_inputs(body, 2 + 2 * len(pieces) + len(before), len(after)),
        out_shape=tuple(
            jax.ShapeDtypeStruct((2 * count * high, wide), f32) for wide, high, _ in targets
        ),
        grid_spec=pltpu.PrefetchScalarGridSpec(
            num_scalar_prefetch=2,
            grid=(total,),
            in_specs=specs + anywhere(len(before) + len(after)),
            out_specs=tuple(
                pl.BlockSpec((2 * high, wide), lambda i, place, core: (place[i], 0))
                for wide, high, _ in targets
            ),
        ),
        input_output_aliases={2 + len(arrays) + n: n for n in range(len(before))},
        compiler_params=kernel_params(),
        cost_estimate=cost(1.2 * total),
        name="spread",
    )(places, core, *arrays, *before, *after)


def small_sums(norm_sums, qkv_sums, up_sums, dy_sums, numbers):
    def body(number_ref, norm_ref, q_ref, u_ref, y_ref, out_ref, work):
        shard = number_ref[1]
        for owner in range(8):
            mine = shard == owner
            for n in range(4):
                for half in range(2):
                    at = owner * 256 + half * 128
                    work[owner, n * 2 + half : n * 2 + half + 1] = norm_ref[n : n + 1, at : at + 128]
            for n in range(3):
                third, source = divmod(owner * 3 + n, 8)
                for half in range(2):
                    at = third * 256 + half * 128
                    work[owner, 8 + n * 2 + half : 9 + n * 2 + half] = jnp.where(
                        shard == source, q_ref[:, at : at + 128], 0.0
                    )
            for n in range(8):
                work[owner, 14 + n : 15 + n] = jnp.where(
                    mine, u_ref[:, n * 128 : (n + 1) * 128], 0.0
                )
            for n in range(2):
                work[owner, 22 + n : 23 + n] = jnp.where(
                    mine, y_ref[:, n * 128 : (n + 1) * 128], 0.0
                )
        out_ref[...] = work[...].astype(bf16)

    vmem = pl.BlockSpec(memory_space=pltpu.VMEM)
    return pl.pallas_call(
        body,
        out_shape=jax.ShapeDtypeStruct((8, 24, 128), bf16),
        in_specs=[pl.BlockSpec(memory_space=pltpu.SMEM)] + [vmem] * 4,
        out_specs=vmem,
        scratch_shapes=[pltpu.VMEM((8, 24, 128), f32)],
        compiler_params=kernel_params(),
        cost_estimate=cost(3),
        name="small_sums",
    )(numbers, norm_sums, qkv_sums, up_sums, dy_sums)


def added(terms, groups, numbers, after):
    rows, cols = terms[0][0].shape[1:]
    firsts = [sum(groups[:n]) for n in range(len(groups))]

    def body(number_ref, *refs):
        step = pl.program_id(0)
        total = None
        for ref, (_, _, steps) in zip(refs, terms):
            value = ref[0].astype(f32)
            if steps is not None:
                counts = functools.reduce(jnp.logical_or, [step == at for at in steps])
                value = jnp.where(counts, value, 0.0)
            total = value if total is None else total + value
        total = total.astype(bf16)
        for ref, first, size in zip(refs[len(terms) :], firsts, groups):

            @pl.when((step >= first) & (step < first + size))
            def _(ref=ref):
                ref[0] = total

    def came(place):
        return pl.BlockSpec((1, rows, cols), lambda i, n: (place(i, n), 0, 0))

    def goes(first, size):
        return pl.BlockSpec((1, rows, cols), lambda i, n: (jnp.clip(i - first, 0, size - 1), 0, 0))

    return pl.pallas_call(
        after_inputs(body, 1 + len(terms), len(after)),
        out_shape=tuple(jax.ShapeDtypeStruct((size, rows, cols), bf16) for size in groups),
        grid_spec=pltpu.PrefetchScalarGridSpec(
            num_scalar_prefetch=1,
            grid=(sum(groups),),
            in_specs=[came(place) for _, place, _ in terms] + anywhere(len(after)),
            out_specs=tuple(goes(first, size) for first, size in zip(firsts, groups)),
        ),
        compiler_params=kernel_params(),
        cost_estimate=cost(4),
        name="added",
    )(numbers, *[term[0] for term in terms], *after)


def local(
    tokens,
    doc_lengths,
    cotangent,
    ln1_gain,
    ln1_bias,
    ln2_gain,
    ln2_bias,
    qkv_weight,
    qkv_bias,
    out_weight,
    out_bias,
    up_weight,
    up_bias,
    down_weight,
    down_bias,
):
    rows, width = tokens.shape
    head = width // HEADS
    group = 8
    rep = lax.axis_index("rep")
    shard = lax.axis_index("shard")
    y, h, c = rep // 4, (rep // 2) % 2, rep % 2
    l, x = shard // 4, shard % 4
    ff = up_bias.shape[0]

    cols = 3 * head + ff
    vectors = [v[None] for v in (ln1_gain, ln1_bias, ln2_gain, ln2_bias, qkv_bias)]
    place = (y * 2 + c).astype(jnp.int32).reshape(1)
    part, pair = packed(
        qkv_weight, up_weight, vectors, doc_lengths, place, head, tokens, cotangent
    )
    below, above, other = move(pair, x=1), move(pair, x=-1), move(pair, l=1)
    far, other_above, other_below = move(below, x=1), move(other, x=-1), move(below, l=1)
    x_other_far, dy_other_far = move(other_below[0], x=1), move(other_above[1], x=-1)
    pairs = (pair, above, far, below, other, other_above, None, other_below)
    x_all = tuple(x_other_far if p is None else p for p in pairs)
    dy_all = tuple(dy_other_far if p is None else p for p in pairs)

    part = lax.all_to_all(part, "shard", 0, 0)
    own, infos = unpacked(part, (pairs[1], pairs[3], pairs[4]))
    below, above = move(own, y=1), move(own, y=-1)
    low, high = halves(below, above, (pairs[2], pairs[5], pairs[7]))
    far_low, far_high = move(low, y=1), move(high, y=-1)
    mine = ((own, 0, 0), (above, 0, 1), (far_low, 0, 2), (far_high, 4, 2), (below, 0, 3))
    yours = tuple((move(array, c=1), first, spot + 4) for array, first, spot in mine)
    steps4 = (y + jnp.arange(4)) % 4
    spots = jnp.concatenate([steps4 * 2 + c, steps4 * 2 + 1 - c]).astype(jnp.int32)
    weight = mine + yours

    gains = infos[:, 0, :1024].reshape(8, 4, 256).transpose(1, 0, 2).reshape(4, width)
    qkv_b = infos[:, 0, 1024:].reshape(8 * 3, 1, head)
    qkv_b = jnp.stack(
        [lax.dynamic_index_in_dim(qkv_b, third * 8 + shard, 0, False) for third in range(3)]
    )
    steps8 = jnp.arange(8)
    sources = ((steps8 // 4) ^ l) * 4 + (x + steps8 % 4) % 4
    sources = sources.astype(jnp.int32)
    lengths = infos[:, 1, :3]
    lengths = jnp.sum(
        jnp.where(sources[:, None, None] == steps8[None, :, None], lengths[None], 0.0), 1
    ).astype(jnp.int32)
    ends = jnp.cumsum(lengths, 1)
    starts = ends - lengths
    steps_t = jnp.arange(rows, dtype=jnp.int32)
    segment = jnp.sum((steps_t[None, :, None] >= ends[:, None, :]).astype(jnp.int32), -1)
    slots = jnp.arange(lengths.shape[1], dtype=jnp.int32)
    begin = jnp.sum(
        jnp.where(segment[:, :, None] == slots[None, None, :], starts[:, None, :], 0), -1
    )
    position = (steps_t[None, :] - begin).astype(f32).reshape(group * rows, 1)
    lane = jnp.arange(128)
    freq = 10000.0 ** (-2.0 * (lane % (ROT // 2)).astype(f32) / ROT)
    angle = position * freq[None, :]
    cosine = jnp.where(lane < ROT, jnp.cos(angle), 1.0)
    sine = jnp.sin(angle)
    sine = jnp.where(lane < ROT // 2, -sine, jnp.where(lane < ROT, sine, 0.0))

    both_bias = (out_bias.astype(f32) + down_bias.astype(f32))[None, :]
    wide_bias = lax.dynamic_update_slice(jnp.zeros((1, width), f32), both_bias, (0, shard * 256))
    numbers = jnp.stack([c, shard, y, h]).astype(jnp.int32)

    h1, active, d_hidden, keep, send, mean, inverse, up_sums, dy_sums = feed_forward(
        x_all,
        dy_all,
        gains,
        weight,
        spots,
        down_weight,
        up_bias.astype(f32)[None],
        numbers,
        3 * head,
        (cosine, sine),
    )
    got = move(send, c=1)
    attended, d_qkv, a_keep, a_send, qkv_sums = attend(
        h1, dy_all, weight, spots, out_weight, qkv_b, cosine, sine, lengths, numbers, (send,)
    )

    def turn(k):
        return lambda i, n: (n[2] + k) % 4 * 2 + i % 2

    low, high = added([(keep, turn(2), None), (got, turn(2), None)], (1, 1), numbers, (attended,))
    from_low, from_high = move(low, y=1), move(high, y=-1)
    a_got = move(a_send, c=1)
    norm_sums, *sums = back_norms(
        d_qkv,
        d_hidden,
        weight,
        spots,
        x_all,
        mean,
        inverse,
        jnp.stack([gains[0], gains[2]]),
        (low, high),
    )

    def sides(i, n):
        return (n[2] + 1 + i // 2 * 2) % 4 * 2 + i % 2

    above, below = added(
        [
            (keep, sides, None),
            (got, sides, None),
            (from_low, lambda i, n: 0, (0,)),
            (from_high, lambda i, n: 0, (3,)),
        ],
        (2, 2),
        numbers,
        (sums[0],),
    )
    from_below, from_above = move(above, y=1), move(below, y=-1)
    def away(i, n):
        return i * 2 + 1 - n[3]

    (a_away,) = added([(a_keep, away, None), (a_got, away, None)], (4,), numbers, (above,))
    a_crossed = move(a_away, h=1)
    mix = mixed_part(
        active, attended, down_weight, out_weight, wide_bias, sources, (above, below, a_away)
    )

    smalls = small_sums(norm_sums, qkv_sums, up_sums, dy_sums, numbers)
    smalls = jnp.broadcast_to(smalls[None], (16, 8, 24, 128)).reshape(128, 24, 128)
    smalls = lax.all_to_all(smalls, BOTH, 0, 0)
    smalls = jnp.sum(smalls.astype(f32), 0)

    def ends_at(i, n):
        return n[2] * 2 + jnp.where(i == 0, 1 - n[3], n[3])

    def crosses(i, n):
        return jnp.where(i == 0, 1 - n[3], n[3])

    leaves, inner = added(
        [
            (keep, ends_at, None),
            (got, ends_at, None),
            (from_below, crosses, None),
            (from_above, crosses, None),
        ],
        (1, 1),
        numbers,
        (mix,),
    )
    crossed = move(leaves, h=1)

    def around(i, n):
        return (n[2] + 2 - i) % 4

    def around_here(i, n):
        return around(i, n) * 2 + n[3]

    a_far, a_above, a_own, a_below = added(
        [
            (a_keep, around_here, None),
            (a_got, around_here, None),
            (a_crossed, around, None),
        ],
        (1, 1, 1, 1),
        numbers,
        (),
    )
    a_low, a_high = move(a_far[0, :32], y=1), move(a_far[0, 32:], y=-1)
    ((inner,),) = added(
        [(inner, lambda i, n: 0, None), (crossed, lambda i, n: 0, None)],
        (1,),
        numbers,
        (a_low, a_high),
    )
    a_above = jnp.concatenate(
        [a_above[0, :32].astype(f32) + a_low.astype(f32), a_above[0, 32:].astype(f32)], 0
    )
    a_below = jnp.concatenate(
        [a_below[0, :32].astype(f32), a_below[0, 32:].astype(f32) + a_high.astype(f32)], 0
    )
    a_from_below, a_from_above = move(a_above.astype(bf16), y=1), move(a_below.astype(bf16), y=-1)

    part, down_stays, out_stays = packed_sums(
        inner, a_own[0], a_from_below, a_from_above, ff, head, (smalls,)
    )
    part = lax.all_to_all(part, "shard", 0, 0)
    inner, a_sum = unpacked_sums(part, down_stays, out_stays, ff, head, ())
    inner_other = move(inner, h=1)
    inner = jnp.stack([inner, inner_other])

    def ring(pieces, way):
        own, above, far, below = pieces if way == 1 else (pieces[n] for n in (0, 3, 2, 1))
        passed = move(far, x=way)
        above = (above.astype(f32) + passed.astype(f32)).astype(bf16)
        return (
            own.astype(f32) + move(above, x=way).astype(f32) + move(below, x=-way).astype(f32)
        )

    sum_other = move(ring(sums[4:], 1).astype(bf16), l=1)
    own_sum = ring(sums[:4], -1) + sum_other.astype(f32)
    mixed = lax.psum_scatter(mix, "shard", scatter_dimension=0, tiled=True)
    mixed = (tokens.astype(f32) + mixed.astype(f32)).astype(bf16)
    own_normed, own_inverse = normalize(tokens)
    tokens_grad = cotangent.astype(f32) + own_inverse * (
        own_sum
        - jnp.mean(own_sum, -1, keepdims=True)
        - own_normed * jnp.mean(own_sum * own_normed, -1, keepdims=True)
    )

    norm_grads = smalls[:8].reshape(4, 256)
    dy_total = smalls[22:].reshape(256)

    below, above = move(inner, y=1), move(inner, y=-1)
    far_low, far_high = move(below[:1], y=1), move(above[1:], y=-1)
    pieces = [(v, move(v, c=1)) for v in (inner, above, far_low, far_high, below)]
    order = ((0, h), (0, 1 - h), (1, h), (1, 1 - h), (2, h), (2, 1 - h), (3, h), (3, 1 - h))
    places = jnp.stack([(y + k) % 4 * 2 + high for k, high in order]).astype(jnp.int32)
    up_parts = [
        (source * ff, 64 + 16 * (source % 4), source // 4 * ff, ff) for source in range(8)
    ]
    targets = [(width, 64, [(0, 0, 0, width)]), (8 * ff, 16, up_parts)]
    near = pieces[:2] + pieces[4:]
    near_places = jnp.concatenate([places[:4], places[6:]])
    grads = spread(near, near_places, numbers[:1], targets, 8, (), ())
    down_grad, up_grad = spread(
        pieces[2:4], places[4:6], numbers[:1], targets, 8, grads, (tokens_grad, mixed)
    )

    a_below, a_above = move(a_sum, y=1), move(a_sum, y=-1)
    a_low, a_high = halves(a_below[None], a_above[None], (inner_other,))
    a_far = jnp.concatenate([move(a_low, y=1), move(a_high, y=-1)], 1)
    a_sum = jnp.concatenate([a_sum[None], a_above[None], a_far, a_below[None]])
    a_other = move(a_sum, h=1)
    places = jnp.concatenate([steps4 * 2 + h, steps4 * 2 + 1 - h]).astype(jnp.int32)
    out_grad, qkv_grad = spread(
        [(a_sum, move(a_sum, c=1)), (a_other, move(a_other, c=1))],
        places,
        numbers[:1],
        [
            (width, 16, [(0, 48, 0, width)]),
            (3 * width, 16, [(n * width, 16 * n, 0, width) for n in range(3)]),
        ],
        8,
        (),
        (),
    )
    return (
        mixed,
        tokens_grad,
        norm_grads[0],
        norm_grads[1],
        norm_grads[2],
        norm_grads[3],
        qkv_grad,
        smalls[8:14].reshape(768),
        out_grad,
        dy_total,
        up_grad,
        smalls[14:22].reshape(ff),
        down_grad,
        dy_total,
    )


def solution(mesh):
    rows = P(BOTH, None)
    vector, matrix = P("shard"), P("shard", None)
    return jax.shard_map(
        local,
        mesh=mesh,
        in_specs=(rows, rows, rows, vector, vector, vector, vector)
        + (matrix, vector, matrix, vector, matrix, vector, matrix, vector),
        out_specs=(rows, rows, vector, vector, vector, vector)
        + (matrix, vector, matrix, vector, matrix, vector, matrix, vector),
        check_vma=False,
    )
```

```python
import functools
import math

import jax
import jax.numpy as jnp
from jax import lax
from jax.experimental import pallas as pl
from jax.experimental.pallas import tpu as pltpu
from jax.sharding import PartitionSpec as P

HEADS = 8
ROT = 64
EPS = 1e-05
f32 = jnp.float32
bf16 = jnp.bfloat16


def cost(time):
    return pl.CostEstimate(flops=int(time * 1.15e9), bytes_accessed=1000, transcendentals=0)


BOTH = ("rep", "shard")
SIZES = (4, 2, 2, 2, 4)
SAME_CORE = [[2 * n + c for n in range(8)] for c in range(2)]
SAME_CORE_ALL = [[(2 * n + c) * 8 + s for n in range(8) for s in range(8)] for c in range(2)]


def coords():
    for y in range(4):
        for h in range(2):
            for c in range(2):
                for l in range(2):
                    for x in range(4):
                        yield (y, h, c, l, x)


def linear(t):
    y, h, c, l, x = (v % m for v, m in zip(t, SIZES))
    return ((y * 2 + h) * 2 + c) * 8 + l * 4 + x


def move(value, y=0, h=0, c=0, l=0, x=0):
    step = (y, h, c, l, x)
    pairs = [(linear(t), linear(tuple(a + b for a, b in zip(t, step)))) for t in coords()]
    return lax.ppermute(value, BOTH, pairs)


def pick(value, index, axis):
    return lax.dynamic_index_in_dim(value, index, axis, keepdims=False)


def normalize(value):
    xf = value.astype(f32)
    centre = xf - jnp.mean(xf, -1, keepdims=True)
    inverse = lax.rsqrt(jnp.mean(centre * centre, -1, keepdims=True) + EPS)
    return centre * inverse, inverse


def kernel_params():
    return pltpu.CompilerParams(vmem_limit_bytes=56 * 1024 * 1024)


def after_inputs(body, count, extra):
    return lambda *refs: body(*refs[:count], *refs[count + extra :])


def anywhere(count):
    return [pl.BlockSpec(memory_space=pl.ANY)] * count


def dot(a, b, ca=1, cb=0):
    return lax.dot_general(a, b, (((ca,), (cb,)), ((), ())), preferred_element_type=f32)


def swap_halves(value):
    lane = lax.broadcasted_iota(jnp.int32, value.shape, 1)
    return jnp.where(lane < 32, pltpu.roll(value, 96, 1), pltpu.roll(value, 32, 1))


def allowed_mask(lengths_ref, block, rows):
    e0 = lengths_ref[block, 0]
    e1 = e0 + lengths_ref[block, 1]
    t = lax.broadcasted_iota(jnp.int32, (rows, rows), 0)
    s = lax.broadcasted_iota(jnp.int32, (rows, rows), 1)
    seg_t = (t >= e0).astype(jnp.int32) + (t >= e1).astype(jnp.int32)
    seg_s = (s >= e0).astype(jnp.int32) + (s >= e1).astype(jnp.int32)
    return (seg_t == seg_s) & (s <= t)


def dot_rows(a, b):
    return lax.dot_general(a, b, (((0,), (0,)), ((), ())), preferred_element_type=f32)


def loads(copies):
    for copy in copies:
        copy.start()
    return copies


def piece_copies(pieces, half, target, sems, rows):
    return [
        pltpu.make_async_copy(
            piece.at[half] if len(piece.shape) == 3 else piece,
            target.at[pl.ds(at * rows, rows)],
            sems.at[at],
        )
        for at, piece in enumerate(pieces)
    ]


def weight_copies(pieces, refs, spot_ref, target, lanes, sems):
    return [
        pltpu.make_async_copy(
            ref.at[pl.ds(begin, size), :, lanes],
            target.at[pl.ds(first, size), spot_ref[spot]],
            sems.at[at],
        )
        for at, (ref, (_, begin, size, first, spot)) in enumerate(zip(refs, pieces))
    ]


def feed_forward(x, dy, gains, weight, spots, down, bias, numbers, first, after):
    rows, width = x[0].shape[1:]
    count = len(x)
    total = rows * count
    ff = bias.shape[1]

    parts = len(weight)

    def body(number_ref, spot_ref, g_ref, b_ref, *refs):
        w_refs, refs = refs[:parts], refs[parts:]
        x_refs, dy_refs, d_hbm = refs[:count], refs[count : 2 * count], refs[2 * count]
        (h1_hbm, act_hbm, du_hbm, keep_hbm, send_hbm, m_ref, i_ref, db_ref, sum_ref) = refs[
            2 * count + 1 : 2 * count + 10
        ]
        (x_v, dy_v, h1_v, h2_v, w_v, d_v, act_v, du_v, keep_v, send_v, x_sem, dy_sem, w_sem, sems) = refs[
            2 * count + 10 :
        ]
        own = number_ref[0] == 0
        x_copies = loads(piece_copies(x_refs, 0, x_v, x_sem, rows))
        w_copies = loads(
            weight_copies(weight, w_refs, spot_ref, w_v, pl.ds(first, ff), w_sem)
        )
        dy_copies = loads(piece_copies(dy_refs, 1, dy_v, dy_sem, rows))
        d_copy = pltpu.make_async_copy(d_hbm, d_v, sems.at[1])
        d_copy.start()
        for copy in x_copies:
            copy.wait()

        @pl.loop(0, count)
        def _(n):
            at = pl.ds(pl.multiple_of(n * rows, rows), rows)
            value = x_v[at, :].astype(f32)
            mean = jnp.mean(value, 1, keepdims=True)
            centre = value - mean
            inverse = lax.rsqrt(jnp.mean(centre * centre, 1, keepdims=True) + EPS)
            normed = centre * inverse
            m_ref[at, :] = mean
            i_ref[at, :] = inverse
            h1_v[at, :] = (normed * g_ref[0:1] + g_ref[1:2]).astype(bf16)
            h2_v[at, :] = (normed * g_ref[2:3] + g_ref[3:4]).astype(bf16)

        h1_copy = pltpu.make_async_copy(h1_v, h1_hbm, sems.at[2])
        h1_copy.start()
        for copy in w_copies + dy_copies:
            copy.wait()
        d_copy.wait()
        mine = dy_v[:, pl.ds(pl.multiple_of(number_ref[1] * 256, 256), 256)]
        sum_ref[...] = jnp.sum(mine.astype(f32), 0, keepdims=True)

        def split(part, places, high, wide):
            at = (places, high, wide)

            @pl.when(own)
            def _():
                keep_v[at] = part[:, 0]
                send_v[at] = part[:, 1]

            @pl.when(jnp.logical_not(own))
            def _():
                keep_v[at] = part[:, 1]
                send_v[at] = part[:, 0]

        def leaving(n):
            at = (pl.ds(n * 2, 2), pl.ds(0, 64))
            return (
                pltpu.make_async_copy(keep_v.at[at], keep_hbm.at[at], sems.at[3]),
                pltpu.make_async_copy(send_v.at[at], send_hbm.at[at], sems.at[4]),
            )

        @pl.loop(0, ff // 256)
        def _(n):
            at = pl.ds(pl.multiple_of(n * 256, 256), 256)
            u = dot(h2_v[...], w_v[:, :, :, at].reshape(width, 256)) + b_ref[:, at]
            cdf = 0.5 * (1.0 + lax.erf(u * math.sqrt(0.5)))
            pdf = jnp.exp(-0.5 * u * u) * (1.0 / math.sqrt(2.0 * math.pi))
            act = (u * cdf).astype(bf16)
            act_v[:, at] = act
            du = (dot(dy_v[...], d_v[at, :], 1, 1) * (cdf + u * pdf)).astype(bf16)
            du_v[:, at] = du
            db_ref[:, at] = jnp.sum(du.astype(f32), 0, keepdims=True)
            part = dot_rows(act, dy_v[...]).astype(bf16).reshape(2, 2, 64, width)
            split(part, pl.ds(n * 2, 2), pl.ds(0, 64), slice(None))
            for copy in leaving(n):
                copy.start()

        act_copy = pltpu.make_async_copy(act_v, act_hbm, sems.at[0])
        act_copy.start()
        du_copy = pltpu.make_async_copy(du_v, du_hbm, sems.at[1])
        du_copy.start()
        for n in range(ff // 256):
            for copy in leaving(n):
                copy.wait()

        def block(n):
            at = (
                slice(None),
                pl.ds(pl.multiple_of(64 + 16 * (n % 4), 16), 16),
                pl.ds(pl.multiple_of(n // 4 * ff, ff), ff),
            )
            return at

        def away(n):
            at = block(n)
            return (
                pltpu.make_async_copy(keep_v.at[at], keep_hbm.at[at], sems.at[3]),
                pltpu.make_async_copy(send_v.at[at], send_hbm.at[at], sems.at[4]),
            )

        @pl.loop(0, 8)
        def _(n):
            lanes = pl.ds(pl.multiple_of(n * 256, 256), 256)
            part = dot_rows(h2_v[:, lanes], du_v[...]).astype(bf16).reshape(8, 2, 16, ff)
            split(part, *block(n))
            for copy in away(n):
                copy.start()

        for n in range(8):
            for copy in away(n):
                copy.wait()
        h1_copy.wait()
        act_copy.wait()
        du_copy.wait()

    wide = jax.ShapeDtypeStruct((total, width), bf16)
    thin = jax.ShapeDtypeStruct((total, ff), bf16)
    column = jax.ShapeDtypeStruct((total, 1), f32)
    grads = jax.ShapeDtypeStruct((8, 128, width), bf16)
    vmem = pl.BlockSpec(memory_space=pltpu.VMEM)
    return pl.pallas_call(
        after_inputs(body, 5 + parts + 2 * count, len(after)),
        out_shape=(
            wide,
            thin,
            thin,
            grads,
            grads,
            column,
            column,
            jax.ShapeDtypeStruct((1, ff), f32),
            jax.ShapeDtypeStruct((1, 256), f32),
        ),
        in_specs=[pl.BlockSpec(memory_space=pltpu.SMEM)] * 2
        + [vmem, vmem]
        + anywhere(parts + 2 * count + 1 + len(after)),
        out_specs=tuple(anywhere(5)) + (vmem,) * 4,
        scratch_shapes=[
            pltpu.VMEM((total, width), bf16),
            pltpu.VMEM((total, width), bf16),
            pltpu.VMEM((total, width), bf16),
            pltpu.VMEM((total, width), bf16),
            pltpu.VMEM((8, 8, width // 64, ff), bf16),
            pltpu.VMEM((ff, width), bf16),
            pltpu.VMEM((total, ff), bf16),
            pltpu.VMEM((total, ff), bf16),
            pltpu.VMEM((8, 128, width), bf16),
            pltpu.VMEM((8, 128, width), bf16),
            pltpu.SemaphoreType.DMA((count,)),
            pltpu.SemaphoreType.DMA((count,)),
            pltpu.SemaphoreType.DMA((parts,)),
            pltpu.SemaphoreType.DMA((5,)),
        ],
        compiler_params=kernel_params(),
        cost_estimate=cost(32),
        name="feed_forward",
    )(numbers, spots, gains, bias, *[p[0] for p in weight], *x, *dy, down, *after)


def packed(qkv_weight, up_weight, vectors, lengths, place, head, tokens, cotangent):
    wide, up_wide = qkv_weight.shape[1], up_weight.shape[1]
    part, up_part = 3 * head, up_wide // 8
    cols = part + up_part

    def body(place_ref, len_ref, q_ref, u_ref, x_ref, dy_ref, *refs):
        v_refs, out_ref, pair_ref = refs[: len(vectors)], refs[-2], refs[-1]
        pair_ref[0] = x_ref[...]
        pair_ref[1] = dy_ref[...]
        lane = lax.broadcasted_iota(jnp.int32, (8, cols), 1)
        row = lax.broadcasted_iota(jnp.int32, (8, cols), 0)
        sizes = jnp.zeros((8, cols), f32)
        for at in range(3):
            sizes = jnp.where(lane == at, len_ref[0, at].astype(f32), sizes)
        vector = jnp.concatenate([ref[...].astype(f32) for ref in v_refs], 1)
        vector = jnp.broadcast_to(vector, (8, cols))
        tail = jnp.where(row == 0, vector, jnp.where(row == 1, sizes, 0.0)).astype(bf16)
        for owner in range(8):
            pieces = [
                q_ref[:, (third * 8 + owner) * head : (third * 8 + owner + 1) * head]
                for third in range(3)
            ]
            pieces.append(u_ref[:, owner * up_part : (owner + 1) * up_part])
            out_ref[owner] = jnp.concatenate([jnp.concatenate(pieces, 1), tail], 0)

    return pl.pallas_call(
        body,
        out_shape=(
            jax.ShapeDtypeStruct((8, 40, cols), bf16),
            jax.ShapeDtypeStruct((2,) + tokens.shape, bf16),
        ),
        grid_spec=pltpu.PrefetchScalarGridSpec(
            num_scalar_prefetch=2,
            grid=(1,),
            in_specs=[
                pl.BlockSpec((32, wide), lambda i, place, lens: (place[0], 0)),
                pl.BlockSpec((32, up_wide), lambda i, place, lens: (place[0], 0)),
                pl.BlockSpec(tokens.shape, lambda i, place, lens: (0, 0)),
                pl.BlockSpec(tokens.shape, lambda i, place, lens: (0, 0)),
            ]
            + [pl.BlockSpec(v.shape, lambda i, place, lens: (0, 0)) for v in vectors],
            out_specs=(
                pl.BlockSpec((8, 40, cols), lambda i, place, lens: (0, 0, 0)),
                pl.BlockSpec((2,) + tokens.shape, lambda i, place, lens: (0, 0, 0)),
            ),
        ),
        compiler_params=kernel_params(),
        cost_estimate=cost(3),
        name="packed",
    )(place, lengths, qkv_weight, up_weight, tokens, cotangent, *vectors)


def attend(h1, dy, weight, spots, out, bias, cosine, sine, lengths, numbers, after, rows=128):
    total, width = h1.shape
    count = len(dy)
    head = out.shape[0]
    scale = head ** (-0.5)

    parts = len(weight)

    def body(number_ref, len_ref, spot_ref, b_ref, *refs):
        w_refs, refs = refs[:parts], refs[parts:]
        dy_refs = refs[:count]
        h1_hbm, out_hbm, cos_hbm, sin_hbm = refs[count : count + 4]
        ol_hbm, dq_hbm, keep_hbm, send_hbm, sum_ref = refs[count + 4 : count + 9]
        (dy_v, h1_v, w_v, wo_v, cos_v, sin_v, qkv_v, do_v, ol_v, dq_v, keep_v, send_v, dy_sem, w_sem, sems) = (
            refs[count + 9 :]
        )
        own = number_ref[0] == 0
        pairs = (
            (h1_hbm, h1_v),
            (out_hbm, wo_v),
            (cos_hbm, cos_v),
            (sin_hbm, sin_v),
        )
        copies = loads(
            [pltpu.make_async_copy(*pair, sems.at[n]) for n, pair in enumerate(pairs)]
        )
        w_copies = loads(
            weight_copies(weight, w_refs, spot_ref, w_v, pl.ds(0, 3 * head), w_sem)
        )
        dy_copies = loads(piece_copies(dy_refs, 1, dy_v, dy_sem, rows))
        for copy in copies[:1] + w_copies:
            copy.wait()

        @pl.loop(0, 3)
        def _(n):
            at = pl.ds(pl.multiple_of(n * head, head), head)
            qkv_v[:, at] = dot(h1_v[...], w_v[:, :, :, at].reshape(width, head)) + b_ref[n]

        for copy in copies[1:] + dy_copies:
            copy.wait()
        do_v[...] = dot(dy_v[...], wo_v[...], 1, 1).astype(bf16)
        sum_ref[...] = jnp.zeros_like(sum_ref)

        @pl.loop(0, total // rows)
        def _(block):
            at = pl.ds(pl.multiple_of(block * rows, rows), rows)
            cos, sin = cos_v[at, :], sin_v[at, :]

            def turned(value, sign):
                left = value[:, :128]
                left = left * cos + swap_halves(left) * (sin * sign)
                return jnp.concatenate([left, value[:, 128:]], 1).astype(bf16)

            q, k = turned(qkv_v[at, 0:head], 1.0), turned(qkv_v[at, head : 2 * head], 1.0)
            v = qkv_v[at, 2 * head :].astype(bf16)
            scores = dot(q, k, 1, 1) * scale
            masked = jnp.where(allowed_mask(len_ref, block, rows), scores, -1e30)
            shifted = jnp.exp(masked - jnp.max(masked, 1, keepdims=True))
            probs = shifted / jnp.sum(shifted, 1, keepdims=True)
            low = probs.astype(bf16)
            ol_v[at, :] = dot(low, v).astype(bf16)
            d_out = do_v[at, :]
            d_value = dot(low, d_out, 0, 0)
            d_probs = dot(d_out, v, 1, 1)
            centred = d_probs - jnp.sum(d_probs * probs, 1, keepdims=True)
            d_scores = (probs * centred).astype(bf16)
            d_query = turned(dot(d_scores, k) * scale, -1.0)
            d_key = turned(dot(d_scores, q, 0, 0) * scale, -1.0)
            for n, grad in enumerate((d_query, d_key, d_value.astype(bf16))):
                lanes = slice(n * head, (n + 1) * head)
                dq_v[at, lanes] = grad
                sum_ref[:, lanes] += jnp.sum(grad.astype(f32), 0, keepdims=True)

        ol_copy = pltpu.make_async_copy(ol_v, ol_hbm, sems.at[0])
        ol_copy.start()
        dq_copy = pltpu.make_async_copy(dq_v, dq_hbm, sems.at[1])
        dq_copy.start()

        def split(part, high, lanes):
            for z_hi in range(2):
                at = (pl.ds(4 * z_hi, 4), high, lanes)

                @pl.when(own)
                def _(z_hi=z_hi, at=at):
                    keep_v[at] = part[:, z_hi, 0]
                    send_v[at] = part[:, z_hi, 1]

                @pl.when(jnp.logical_not(own))
                def _(z_hi=z_hi, at=at):
                    keep_v[at] = part[:, z_hi, 1]
                    send_v[at] = part[:, z_hi, 0]

        part = dot_rows(ol_v[...], dy_v[...]).astype(bf16).reshape(4, 2, 2, 16, width)
        split(part, pl.ds(48, 16), slice(None))

        @pl.loop(0, 8)
        def _(n):
            lanes = pl.ds(pl.multiple_of(n * 256, 256), 256)
            part = dot_rows(h1_v[:, lanes], dq_v[...]).astype(bf16).reshape(4, 2, 2, 16, 3 * head)
            for third in range(3):
                split(
                    part[..., third * head : (third + 1) * head],
                    pl.ds(16 * third, 16),
                    pl.ds(pl.multiple_of(n * head, head), head),
                )

        keep_copy = pltpu.make_async_copy(keep_v, keep_hbm, sems.at[2])
        keep_copy.start()
        send_copy = pltpu.make_async_copy(send_v, send_hbm, sems.at[3])
        send_copy.start()
        for copy in (ol_copy, dq_copy, keep_copy, send_copy):
            copy.wait()

    grads = jax.ShapeDtypeStruct((8, 64, width), bf16)
    vmem = pl.BlockSpec(memory_space=pltpu.VMEM)
    smem = pl.BlockSpec(memory_space=pltpu.SMEM)
    return pl.pallas_call(
        after_inputs(body, 8 + parts + count, len(after)),
        out_shape=(
            jax.ShapeDtypeStruct((total, head), bf16),
            jax.ShapeDtypeStruct((total, 3 * head), bf16),
            grads,
            grads,
            jax.ShapeDtypeStruct((1, 3 * head), f32),
        ),
        in_specs=[smem, smem, smem, vmem] + anywhere(parts + count + 4 + len(after)),
        out_specs=tuple(anywhere(4)) + (vmem,),
        scratch_shapes=[
            pltpu.VMEM((total, width), bf16),
            pltpu.VMEM((total, width), bf16),
            pltpu.VMEM((8, 8, width // 64, 3 * head), bf16),
            pltpu.VMEM((head, width), bf16),
            pltpu.VMEM((total, 128), f32),
            pltpu.VMEM((total, 128), f32),
            pltpu.VMEM((total, 3 * head), f32),
            pltpu.VMEM((total, head), bf16),
            pltpu.VMEM((total, head), bf16),
            pltpu.VMEM((total, 3 * head), bf16),
            pltpu.VMEM((8, 64, width), bf16),
            pltpu.VMEM((8, 64, width), bf16),
            pltpu.SemaphoreType.DMA((count,)),
            pltpu.SemaphoreType.DMA((parts,)),
            pltpu.SemaphoreType.DMA((4,)),
        ],
        compiler_params=kernel_params(),
        cost_estimate=cost(22),
        name="attend",
    )(
        numbers,
        lengths,
        spots,
        bias,
        *[p[0] for p in weight],
        *dy,
        h1,
        out,
        cosine,
        sine,
        *after,
    )


def outer(d_qkv, d_hidden, weight, spots, x, mean, inverse, gains, active, attended, down, out, bias, after):
    total, n1 = d_qkv.shape
    n2 = d_hidden.shape[1]
    count = len(x)
    parts = len(weight)
    head, width = out.shape
    step = 512

    def body(spot_ref, m_ref, i_ref, g_ref, b_ref, *refs):
        w_refs, refs = refs[:parts], refs[parts:]
        x_refs, refs = refs[:count], refs[count:]
        plain, sums_ref, outs = refs[:6], refs[6], refs[7 : 7 + count]
        dq_v, du_v, act_v, ol_v, wd_v, wo_v, w_v, x_v, pair_v, w_sem, x_sem, sems, out_sem = refs[
            7 + count :
        ]
        plain_v = (dq_v, du_v, act_v, ol_v, wd_v, wo_v)
        copies = loads(
            [
                pltpu.make_async_copy(source, target, sems.at[n])
                for n, (source, target) in enumerate(zip(plain[:2], plain_v[:2]))
            ]
            + weight_copies(weight, w_refs, spot_ref, w_v, slice(None), w_sem)
            + piece_copies(x_refs, 0, x_v, x_sem, 128)
        )
        later = loads(
            [
                pltpu.make_async_copy(plain[n], plain_v[n], sems.at[n]) for n in range(2, 6)
            ]
        )
        for copy in copies:
            copy.wait()

        def leaving(n, half):
            lanes = pl.ds(pl.multiple_of(n * step, step), step)
            return [
                pltpu.make_async_copy(
                    pair_v.at[half, pl.ds(at * 128, 128), lanes],
                    outs[at].at[half, :, lanes],
                    out_sem.at[half, at],
                )
                for at in range(count)
            ]

        @pl.loop(0, width // step)
        def _(n):
            lanes = pl.ds(pl.multiple_of(n * step, step), step)
            sources = pl.ds(n * (step // 256), step // 256)
            d1 = dot(dq_v[...], w_v[sources, :, :, 0:n1].reshape(step, n1), 1, 1)
            d2 = dot(du_v[...], w_v[sources, :, :, n1:].reshape(step, n2), 1, 1)
            pair_v[1, :, lanes] = (d1 * g_ref[0:1, lanes] + d2 * g_ref[1:2, lanes]).astype(bf16)
            for copy in leaving(n, 1):
                copy.start()
            normed = (x_v[:, lanes].astype(f32) - m_ref[...]) * i_ref[...]
            sums_ref[0:1, lanes] = jnp.sum(d1 * normed, 0, keepdims=True)
            sums_ref[1:2, lanes] = jnp.sum(d1, 0, keepdims=True)
            sums_ref[2:3, lanes] = jnp.sum(d2 * normed, 0, keepdims=True)
            sums_ref[3:4, lanes] = jnp.sum(d2, 0, keepdims=True)

        for copy in later:
            copy.wait()

        @pl.loop(0, width // step)
        def _(n):
            lanes = pl.ds(pl.multiple_of(n * step, step), step)
            mix = dot(act_v[...], wd_v[:, lanes]) + dot(ol_v[...], wo_v[:, lanes])
            pair_v[0, :, lanes] = (mix + b_ref[:, lanes]).astype(bf16)
            for copy in leaving(n, 0):
                copy.start()

        for n in range(width // step):
            for half in range(2):
                for copy in leaving(n, half):
                    copy.wait()

    vmem = pl.BlockSpec(memory_space=pltpu.VMEM)
    return pl.pallas_call(
        after_inputs(body, 11 + parts + count, len(after)),
        out_shape=(jax.ShapeDtypeStruct((4, width), f32),)
        + (jax.ShapeDtypeStruct((2, 128, width), bf16),) * count,
        in_specs=[pl.BlockSpec(memory_space=pltpu.SMEM)]
        + [vmem] * 4
        + anywhere(parts + count + 6 + len(after)),
        out_specs=(vmem,) + tuple(anywhere(count)),
        scratch_shapes=[
            pltpu.VMEM((total, n1), bf16),
            pltpu.VMEM((total, n2), bf16),
            pltpu.VMEM((total, n2), bf16),
            pltpu.VMEM((total, head), bf16),
            pltpu.VMEM((n2, width), bf16),
            pltpu.VMEM((head, width), bf16),
            pltpu.VMEM((8, 8, width // 64, n1 + n2), bf16),
            pltpu.VMEM((total, width), bf16),
            pltpu.VMEM((2, total, width), bf16),
            pltpu.SemaphoreType.DMA((parts,)),
            pltpu.SemaphoreType.DMA((count,)),
            pltpu.SemaphoreType.DMA((6,)),
            pltpu.SemaphoreType.DMA((2, count)),
        ],
        compiler_params=kernel_params(),
        cost_estimate=cost(20),
        name="outer",
    )(
        spots,
        mean,
        inverse,
        gains,
        bias,
        *[p[0] for p in weight],
        *x,
        d_qkv,
        d_hidden,
        active,
        attended,
        down,
        out,
        *after,
    )


def unpacked(part, after):
    owners, _, cols = part.shape

    def body(part_ref, rows_ref, info_ref):
        for owner in range(owners):
            rows_ref[owner] = part_ref[owner, 0:32]
            info_ref[owner] = part_ref[owner, 32:40].astype(f32)

    return pl.pallas_call(
        after_inputs(body, 1, len(after)),
        out_shape=(
            jax.ShapeDtypeStruct((owners, 32, cols), bf16),
            jax.ShapeDtypeStruct((owners, 8, cols), f32),
        ),
        in_specs=[pl.BlockSpec(memory_space=pltpu.VMEM)] + anywhere(len(after)),
        out_specs=(pl.BlockSpec(memory_space=pltpu.VMEM),) * 2,
        compiler_params=kernel_params(),
        cost_estimate=cost(3),
        name="unpacked",
    )(part, *after)


def packed_sums(stays, crossed, own, below, above, ff, head, after):
    width = own.shape[1]

    def body(stay_ref, cross_ref, own_ref, below_ref, above_ref, out_ref, keep_ref):
        inner = (stay_ref[0].astype(f32) + cross_ref[0].astype(f32)).astype(bf16)
        total = wide(own_ref, below_ref, above_ref).astype(bf16)
        for owner in range(8):
            pieces = [
                total[16 * third : 16 * third + 16, owner * head : (owner + 1) * head]
                for third in range(3)
            ]
            row, col = 64 + 16 * (owner % 4), owner // 4 * ff
            pieces.append(inner[row : row + 16, col : col + ff])
            out_ref[owner] = jnp.concatenate(pieces, 1)
        keep_ref[0:64] = inner[0:64]
        keep_ref[64:80] = total[48:64]

    vmem = pl.BlockSpec(memory_space=pltpu.VMEM)
    return pl.pallas_call(
        after_inputs(body, 5, len(after)),
        out_shape=(
            jax.ShapeDtypeStruct((8, 16, 3 * head + ff), bf16),
            jax.ShapeDtypeStruct((80, width), bf16),
        ),
        in_specs=[vmem] * 5 + anywhere(len(after)),
        out_specs=(vmem,) * 2,
        compiler_params=kernel_params(),
        cost_estimate=cost(3),
        name="packed_sums",
    )(stays, crossed, own, below, above, *after)


def stayed(parts, after):
    count, _, width = parts.shape
    step = 4

    def body(part_ref, down_ref, out_ref):
        for at in range(step):
            down_ref[at * 64 : (at + 1) * 64] = part_ref[at, 0:64].astype(f32)
            out_ref[at * 16 : (at + 1) * 16] = part_ref[at, 64:80].astype(f32)

    return pl.pallas_call(
        after_inputs(body, 1, len(after)),
        out_shape=(
            jax.ShapeDtypeStruct((count * 64, width), f32),
            jax.ShapeDtypeStruct((count * 16, width), f32),
        ),
        grid=(count // step,),
        in_specs=[pl.BlockSpec((step, 80, width), lambda i: (i, 0, 0))] + anywhere(len(after)),
        out_specs=(
            pl.BlockSpec((step * 64, width), lambda i: (i, 0)),
            pl.BlockSpec((step * 16, width), lambda i: (i, 0)),
        ),
        compiler_params=kernel_params(),
        cost_estimate=cost(6),
        name="stayed",
    )(parts, *after)


def halves(below, above, x_pair, dy_pair, after):
    count, rows, cols = below.shape
    _, tokens, width = x_pair.shape
    half = (count // 2, rows, cols)

    def body(below_ref, above_ref, x_ref, dy_ref, low_ref, high_ref, x_out, dy_out):
        low_ref[...] = below_ref[...]
        high_ref[...] = above_ref[...]
        x_out[...] = x_ref[0]
        dy_out[...] = dy_ref[0]

    def at(block, first):
        return pl.BlockSpec(block, lambda i: (first,) + (0,) * (len(block) - 1))

    return pl.pallas_call(
        after_inputs(body, 4, len(after)),
        out_shape=(jax.ShapeDtypeStruct(half, bf16),) * 2
        + (jax.ShapeDtypeStruct((tokens, width), bf16),) * 2,
        grid=(1,),
        in_specs=[
            at(half, 0),
            at(half, 1),
            at((1, tokens, width), 0),
            at((1, tokens, width), 1),
        ]
        + anywhere(len(after)),
        out_specs=(at(half, 0), at(half, 0), at((tokens, width), 0), at((tokens, width), 0)),
        compiler_params=kernel_params(),
        cost_estimate=cost(3),
        name="halves",
    )(below, above, x_pair, dy_pair, *after)


def joined(arrays, after):
    size, rows, cols = arrays[0].shape
    count = len(arrays)

    def body(*refs):
        for at in range(count):

            @pl.when(pl.program_id(0) == at)
            def _(at=at):
                refs[count][...] = refs[at][...]

    block = pl.BlockSpec((size, rows, cols), lambda i: (0, 0, 0))
    return pl.pallas_call(
        after_inputs(body, count, len(after)),
        out_shape=jax.ShapeDtypeStruct((size * count, rows, cols), bf16),
        grid=(count,),
        in_specs=[block] * count + anywhere(len(after)),
        out_specs=pl.BlockSpec((size, rows, cols), lambda i: (i, 0, 0)),
        compiler_params=kernel_params(),
        cost_estimate=cost(3),
        name="joined",
    )(*arrays, *after)


def blocks_call(name, body, numbers, terms, outs, after):
    def came(block, index):
        rest = (0,) * (len(block) - 1)
        return pl.BlockSpec(block, lambda i, n: (index(n),) + rest)

    return pl.pallas_call(
        after_inputs(body, 1 + len(terms), len(after)),
        out_shape=tuple(jax.ShapeDtypeStruct(out, bf16) for out in outs),
        grid_spec=pltpu.PrefetchScalarGridSpec(
            num_scalar_prefetch=1,
            grid=(1,),
            in_specs=[came(block, index) for _, block, index in terms] + anywhere(len(after)),
            out_specs=tuple(
                pl.BlockSpec(out, lambda i, n, size=len(out): (0,) * size) for out in outs
            ),
        ),
        compiler_params=kernel_params(),
        cost_estimate=cost(3),
        name=name,
    )(numbers, *[array for array, _, _ in terms], *after)


def wide(*refs):
    return functools.reduce(jnp.add, [ref[...].astype(f32) for ref in refs])


def spread(pieces, places, core, targets, count, before, after):
    rows, cols = pieces[0][0].shape[1:]
    firsts, total = [], 0
    for mine, _ in pieces:
        firsts.append(total)
        total += mine.shape[0]

    def body(place_ref, core_ref, *refs):
        step = pl.program_id(0)
        outs = refs[2 * len(pieces) + len(before) :]
        first_core = core_ref[0] == 0

        def fill(ref, low):
            for out_ref, (_, high, parts) in zip(outs, targets):
                for to, row, col, size in parts:
                    out_ref[low * high : (low + 1) * high, to : to + size] = ref[
                        0, row : row + high, col : col + size
                    ].astype(f32)

        for n, (first, (mine, _)) in enumerate(zip(firsts, pieces)):
            here = (step >= first) & (step < first + mine.shape[0])

            @pl.when(here & first_core)
            def _(n=n):
                fill(refs[2 * n], 0)
                fill(refs[2 * n + 1], 1)

            @pl.when(here & jnp.logical_not(first_core))
            def _(n=n):
                fill(refs[2 * n], 1)
                fill(refs[2 * n + 1], 0)

    def chosen(first, size):
        return pl.BlockSpec(
            (1, rows, cols), lambda i, place, core: (jnp.clip(i - first, 0, size - 1), 0, 0)
        )

    specs, arrays = [], []
    for first, (mine, yours) in zip(firsts, pieces):
        specs += [chosen(first, mine.shape[0])] * 2
        arrays += [mine, yours]
    return pl.pallas_call(
        after_inputs(body, 2 + 2 * len(pieces) + len(before), len(after)),
        out_shape=tuple(
            jax.ShapeDtypeStruct((2 * count * high, wide), f32) for wide, high, _ in targets
        ),
        grid_spec=pltpu.PrefetchScalarGridSpec(
            num_scalar_prefetch=2,
            grid=(total,),
            in_specs=specs + anywhere(len(before) + len(after)),
            out_specs=tuple(
                pl.BlockSpec((2 * high, wide), lambda i, place, core: (place[i], 0))
                for wide, high, _ in targets
            ),
        ),
        input_output_aliases={2 + len(arrays) + n: n for n in range(len(before))},
        compiler_params=kernel_params(),
        cost_estimate=cost(1.2 * total),
        name="spread",
    )(places, core, *arrays, *before, *after)


def small_sums(norm_sums, qkv_sums, up_sums, dy_sums, numbers):
    def body(number_ref, norm_ref, q_ref, u_ref, y_ref, out_ref, work):
        shard = number_ref[1]
        for owner in range(8):
            mine = shard == owner
            for n in range(4):
                for half in range(2):
                    at = owner * 256 + half * 128
                    work[owner, n * 2 + half : n * 2 + half + 1] = norm_ref[n : n + 1, at : at + 128]
            for n in range(3):
                third, source = divmod(owner * 3 + n, 8)
                for half in range(2):
                    at = third * 256 + half * 128
                    work[owner, 8 + n * 2 + half : 9 + n * 2 + half] = jnp.where(
                        shard == source, q_ref[:, at : at + 128], 0.0
                    )
            for n in range(8):
                work[owner, 14 + n : 15 + n] = jnp.where(
                    mine, u_ref[:, n * 128 : (n + 1) * 128], 0.0
                )
            for n in range(2):
                work[owner, 22 + n : 23 + n] = jnp.where(
                    mine, y_ref[:, n * 128 : (n + 1) * 128], 0.0
                )
        out_ref[...] = work[...].astype(bf16)

    vmem = pl.BlockSpec(memory_space=pltpu.VMEM)
    return pl.pallas_call(
        body,
        out_shape=jax.ShapeDtypeStruct((8, 24, 128), bf16),
        in_specs=[pl.BlockSpec(memory_space=pltpu.SMEM)] + [vmem] * 4,
        out_specs=vmem,
        scratch_shapes=[pltpu.VMEM((8, 24, 128), f32)],
        compiler_params=kernel_params(),
        cost_estimate=cost(3),
        name="small_sums",
    )(numbers, norm_sums, qkv_sums, up_sums, dy_sums)


def local(
    tokens,
    doc_lengths,
    cotangent,
    ln1_gain,
    ln1_bias,
    ln2_gain,
    ln2_bias,
    qkv_weight,
    qkv_bias,
    out_weight,
    out_bias,
    up_weight,
    up_bias,
    down_weight,
    down_bias,
):
    rows, width = tokens.shape
    head = width // HEADS
    group = 8
    rep = lax.axis_index("rep")
    shard = lax.axis_index("shard")
    y, h, c = rep // 4, (rep // 2) % 2, rep % 2
    l, x = shard // 4, shard % 4
    ff = up_bias.shape[0]

    cols = 3 * head + ff
    vectors = [v[None] for v in (ln1_gain, ln1_bias, ln2_gain, ln2_bias, qkv_bias)]
    place = (y * 2 + c).astype(jnp.int32).reshape(1)
    part, pair = packed(
        qkv_weight, up_weight, vectors, doc_lengths, place, head, tokens, cotangent
    )
    below, above, other = move(pair, x=1), move(pair, x=-1), move(pair, l=1)
    far, other_above, other_below = move(below, x=1), move(other, x=-1), move(below, l=1)
    pairs = (pair, above, far, below, other, other_above, None, other_below)

    part = lax.all_to_all(part, "shard", 0, 0)
    own, infos = unpacked(part, (pairs[1], pairs[3], pairs[4]))
    below, above = move(own, y=1), move(own, y=-1)
    low, high, x_half, dy_half = halves(below, above, other_below, other_above, (far,))
    far_low, far_high = move(low, y=1), move(high, y=-1)
    x_other_far, dy_other_far = move(x_half, x=1), move(dy_half, x=-1)
    x_all = tuple(x_other_far if p is None else p for p in pairs)
    dy_all = tuple(dy_other_far if p is None else p for p in pairs)
    yours = move(joined((own, above, below), (low,)), c=1)
    far_low_c, far_high_c = move(far_low, c=1), move(far_high, c=1)
    weight = (
        (own, 0, 8, 0, 0),
        (above, 0, 8, 0, 1),
        (far_low, 0, 4, 0, 2),
        (far_high, 0, 4, 4, 2),
        (below, 0, 8, 0, 3),
        (yours, 0, 8, 0, 4),
        (yours, 8, 8, 0, 5),
        (far_low_c, 0, 4, 0, 6),
        (far_high_c, 0, 4, 4, 6),
        (yours, 16, 8, 0, 7),
    )
    steps4 = (y + jnp.arange(4)) % 4
    spots = jnp.concatenate([steps4 * 2 + c, steps4 * 2 + 1 - c]).astype(jnp.int32)

    gains = infos[:, 0, :1024].reshape(8, 4, 256).transpose(1, 0, 2).reshape(4, width)
    qkv_b = infos[:, 0, 1024:].reshape(8 * 3, 1, head)
    qkv_b = jnp.stack(
        [lax.dynamic_index_in_dim(qkv_b, third * 8 + shard, 0, False) for third in range(3)]
    )
    steps8 = jnp.arange(8)
    sources = ((steps8 // 4) ^ l) * 4 + (x + steps8 % 4) % 4
    sources = sources.astype(jnp.int32)
    lengths = infos[:, 1, :3]
    lengths = jnp.sum(
        jnp.where(sources[:, None, None] == steps8[None, :, None], lengths[None], 0.0), 1
    ).astype(jnp.int32)
    ends = jnp.cumsum(lengths, 1)
    starts = ends - lengths
    steps_t = jnp.arange(rows, dtype=jnp.int32)
    segment = jnp.sum((steps_t[None, :, None] >= ends[:, None, :]).astype(jnp.int32), -1)
    slots = jnp.arange(lengths.shape[1], dtype=jnp.int32)
    begin = jnp.sum(
        jnp.where(segment[:, :, None] == slots[None, None, :], starts[:, None, :], 0), -1
    )
    position = (steps_t[None, :] - begin).astype(f32).reshape(group * rows, 1)
    lane = jnp.arange(128)
    freq = 10000.0 ** (-2.0 * (lane % (ROT // 2)).astype(f32) / ROT)
    angle = position * freq[None, :]
    cosine = jnp.where(lane < ROT, jnp.cos(angle), 1.0)
    sine = jnp.sin(angle)
    sine = jnp.where(lane < ROT // 2, -sine, jnp.where(lane < ROT, sine, 0.0))

    both_bias = (out_bias.astype(f32) + down_bias.astype(f32))[None, :]
    wide_bias = lax.dynamic_update_slice(jnp.zeros((1, width), f32), both_bias, (0, shard * 256))
    numbers = jnp.stack([c, shard, y, h]).astype(jnp.int32)

    h1, active, d_hidden, keep, send, mean, inverse, up_sums, dy_sums = feed_forward(
        x_all,
        dy_all,
        gains,
        weight,
        spots,
        down_weight,
        up_bias.astype(f32)[None],
        numbers,
        3 * head,
        (cosine, sine),
    )
    got = move(send, c=1)
    attended, d_qkv, a_keep, a_send, qkv_sums = attend(
        h1, dy_all, weight, spots, out_weight, qkv_b, cosine, sine, lengths, numbers, (send,)
    )

    pair_shape, one = (2, 128, width), (1, 128, width)

    def turn(k):
        return lambda n: (n[2] + k) % 4

    def far_body(n_ref, keep_ref, got_ref, low_ref, high_ref):
        total = wide(keep_ref, got_ref).astype(bf16)
        low_ref[0] = total[0]
        high_ref[0] = total[1]

    low, high = blocks_call(
        "far_sums",
        far_body,
        numbers,
        [(keep, pair_shape, turn(2)), (got, pair_shape, turn(2))],
        (one, one),
        (attended,),
    )
    from_low, from_high = move(low, y=1), move(high, y=-1)
    a_got = move(a_send, c=1)
    norm_sums, *pairs_out = outer(
        d_qkv,
        d_hidden,
        weight,
        spots,
        x_all,
        mean,
        inverse,
        jnp.stack([gains[0], gains[2]]),
        active,
        attended,
        down_weight,
        out_weight,
        wide_bias,
        (low, high),
    )

    def near_body(n_ref, k1_ref, g1_ref, k3_ref, g3_ref, low_ref, high_ref, above_ref, below_ref):
        above, below = wide(k1_ref, g1_ref), wide(k3_ref, g3_ref)
        above_ref[0] = (above[0] + low_ref[0].astype(f32)).astype(bf16)
        above_ref[1] = above[1].astype(bf16)
        below_ref[0] = below[0].astype(bf16)
        below_ref[1] = (below[1] + high_ref[0].astype(f32)).astype(bf16)

    above, below = blocks_call(
        "near_sums",
        near_body,
        numbers,
        [(v, pair_shape, turn(k)) for k in (1, 3) for v in (keep, got)]
        + [(v, one, lambda n: 0) for v in (from_low, from_high)],
        (pair_shape, pair_shape),
        (pairs_out[0],),
    )
    from_below, from_above = move(above, y=1), move(below, y=-1)

    four, part_shape = (4, 64, width), (1, 64, width)

    def away_body(n_ref, keep_ref, got_ref, out_ref):
        out_ref[...] = wide(keep_ref, got_ref).astype(bf16)

    (a_away,) = blocks_call(
        "away_sums",
        away_body,
        numbers,
        [(v, four, lambda n: 1 - n[3]) for v in (a_keep, a_got)],
        (four,),
        (above,),
    )
    a_crossed = move(a_away, h=1)

    smalls = small_sums(norm_sums, qkv_sums, up_sums, dy_sums, numbers)
    smalls = jnp.broadcast_to(smalls[None], (16, 8, 24, 128)).reshape(128, 24, 128)
    smalls = lax.all_to_all(smalls, BOTH, 0, 0)
    smalls = jnp.sum(smalls.astype(f32), 0)

    def ring_start(pieces, way):
        return move(pieces[2], x=way)

    def ring_middle(pieces, passed, way):
        above, below = (pieces[1], pieces[3]) if way == 1 else (pieces[3], pieces[1])
        above = (above.astype(f32) + passed.astype(f32)).astype(bf16)
        return move(above, x=way), move(below, x=-way)

    def ring_end(pieces, arrived):
        return functools.reduce(jnp.add, [v.astype(f32) for v in (pieces[0],) + arrived])

    passed_other, passed_own = ring_start(pairs_out[4:], 1), ring_start(pairs_out[:4], -1)
    arrived_other = ring_middle(pairs_out[4:], passed_other, 1)
    arrived_own = ring_middle(pairs_out[:4], passed_own, -1)
    total_other = move(ring_end(pairs_out[4:], arrived_other).astype(bf16), l=1)
    totals = ring_end(pairs_out[:4], arrived_own) + total_other.astype(f32)
    mixed = (tokens.astype(f32) + totals[0]).astype(bf16)
    own_sum = totals[1]
    own_normed, own_inverse = normalize(tokens)
    tokens_grad = cotangent.astype(f32) + own_inverse * (
        own_sum
        - jnp.mean(own_sum, -1, keepdims=True)
        - own_normed * jnp.mean(own_sum * own_normed, -1, keepdims=True)
    )

    def ends_body(n_ref, keep_ref, got_ref, below_ref, above_ref, leave_ref, stay_ref):
        total = wide(keep_ref, got_ref, below_ref, above_ref).astype(bf16)
        first = n_ref[3] == 0
        leave_ref[0] = jnp.where(first, total[1], total[0])
        stay_ref[0] = jnp.where(first, total[0], total[1])

    leaves, stays = blocks_call(
        "end_sums",
        ends_body,
        numbers,
        [(v, pair_shape, turn(0)) for v in (keep, got)]
        + [(v, pair_shape, lambda n: 0) for v in (from_below, from_above)],
        (one, one),
        (a_away, passed_other, passed_own),
    )
    crossed = move(leaves, h=1)

    def around_body(n_ref, keep_ref, got_ref, crossed_ref, low_ref, high_ref, above_ref, own_ref, below_ref):
        def part(k):
            at = (n_ref[2] + k) % 4
            return wide(keep_ref.at[at], got_ref.at[at], crossed_ref.at[at]).astype(bf16)

        far = part(2)
        low_ref[...] = far[:32]
        high_ref[...] = far[32:]
        above_ref[...] = part(1)
        own_ref[...] = part(0)
        below_ref[...] = part(3)

    a_low, a_high, a_above, a_own, a_below = blocks_call(
        "around_sums",
        around_body,
        numbers,
        [(v, four, lambda n: n[3]) for v in (a_keep, a_got)] + [(a_crossed, four, lambda n: 0)],
        ((32, width), (32, width), (64, width), (64, width), (64, width)),
        (leaves,),
    )
    a_low, a_high = move(a_low, y=1), move(a_high, y=-1)

    def beside_body(n_ref, above_ref, below_ref, low_ref, high_ref, up_ref, down_ref):
        up_ref[0:32] = (above_ref[0:32].astype(f32) + low_ref[...].astype(f32)).astype(bf16)
        up_ref[32:64] = above_ref[32:64]
        down_ref[0:32] = below_ref[0:32]
        down_ref[32:64] = (below_ref[32:64].astype(f32) + high_ref[...].astype(f32)).astype(bf16)

    a_above, a_below = blocks_call(
        "beside_sums",
        beside_body,
        numbers,
        [(v, v.shape, lambda n: 0) for v in (a_above, a_below, a_low, a_high)],
        ((64, width), (64, width)),
        (),
    )
    a_from_below, a_from_above = move(a_above, y=1), move(a_below, y=-1)

    part, stays = packed_sums(
        stays, crossed, a_own, a_from_below, a_from_above, ff, head, (smalls, *arrived_other)
    )
    stays = lax.all_gather(stays, "rep", axis=0)
    part = lax.all_to_all(part, "shard", 0, 0).reshape(1, 128, cols)

    part = jnp.concatenate([part, move(part, h=1)])
    below, above = move(part, y=1), move(part, y=-1)
    far_low, far_high = move(below[:1], y=1), move(above[1:], y=-1)
    pieces = [(v, move(v, c=1)) for v in (part, above, below, far_low, far_high)]
    order = ((0, h), (0, 1 - h), (1, h), (1, 1 - h), (3, h), (3, 1 - h), (2, h), (2, 1 - h))
    places = jnp.stack([(y + k) % 4 * 2 + high for k, high in order]).astype(jnp.int32)
    targets = [
        (
            3 * width,
            16,
            [
                ((third * 8 + source) * head, 16 * source, third * head, head)
                for source in range(8)
                for third in range(3)
            ],
        ),
        (8 * ff, 16, [(source * ff, 16 * source, 3 * head, ff) for source in range(8)]),
    ]
    down_grad, out_grad = stayed(stays, ())
    grads = spread(pieces[:3], places[:6], numbers[:1], targets, 8, (), ())
    qkv_grad, up_grad = spread(
        pieces[3:], places[6:], numbers[:1], targets, 8, grads, (tokens_grad, mixed, down_grad)
    )
    norm_grads = smalls[:8].reshape(4, 256)
    dy_total = smalls[22:].reshape(256)
    return (
        mixed,
        tokens_grad,
        norm_grads[0],
        norm_grads[1],
        norm_grads[2],
        norm_grads[3],
        qkv_grad,
        smalls[8:14].reshape(768),
        out_grad,
        dy_total,
        up_grad,
        smalls[14:22].reshape(ff),
        down_grad,
        dy_total,
    )


def solution(mesh):
    rows = P(BOTH, None)
    vector, matrix = P("shard"), P("shard", None)
    return jax.shard_map(
        local,
        mesh=mesh,
        in_specs=(rows, rows, rows, vector, vector, vector, vector)
        + (matrix, vector, matrix, vector, matrix, vector, matrix, vector),
        out_specs=(rows, rows, vector, vector, vector, vector)
        + (matrix, vector, matrix, vector, matrix, vector, matrix, vector),
        check_vma=False,
    )
```

```python
import functools
import math

import jax
import jax.numpy as jnp
from jax import lax
from jax.experimental import pallas as pl
from jax.experimental.pallas import tpu as pltpu
from jax.sharding import PartitionSpec as P

HEADS = 8
ROT = 64
EPS = 1e-05
f32 = jnp.float32
bf16 = jnp.bfloat16


def cost(time):
    return pl.CostEstimate(flops=int(time * 1.15e9), bytes_accessed=1000, transcendentals=0)


BOTH = ("rep", "shard")
SIZES = (4, 2, 2, 2, 4)
SAME_CORE = [[2 * n + c for n in range(8)] for c in range(2)]
SAME_CORE_ALL = [[(2 * n + c) * 8 + s for n in range(8) for s in range(8)] for c in range(2)]


def coords():
    for y in range(4):
        for h in range(2):
            for c in range(2):
                for l in range(2):
                    for x in range(4):
                        yield (y, h, c, l, x)


def linear(t):
    y, h, c, l, x = (v % m for v, m in zip(t, SIZES))
    return ((y * 2 + h) * 2 + c) * 8 + l * 4 + x


def move(value, y=0, h=0, c=0, l=0, x=0):
    step = (y, h, c, l, x)
    pairs = [(linear(t), linear(tuple(a + b for a, b in zip(t, step)))) for t in coords()]
    return lax.ppermute(value, BOTH, pairs)


def pick(value, index, axis):
    return lax.dynamic_index_in_dim(value, index, axis, keepdims=False)


def normalize(value):
    xf = value.astype(f32)
    centre = xf - jnp.mean(xf, -1, keepdims=True)
    inverse = lax.rsqrt(jnp.mean(centre * centre, -1, keepdims=True) + EPS)
    return centre * inverse, inverse


def kernel_params():
    return pltpu.CompilerParams(vmem_limit_bytes=56 * 1024 * 1024)


def after_inputs(body, count, extra):
    return lambda *refs: body(*refs[:count], *refs[count + extra :])


def anywhere(count):
    return [pl.BlockSpec(memory_space=pl.ANY)] * count


def dot(a, b, ca=1, cb=0):
    return lax.dot_general(a, b, (((ca,), (cb,)), ((), ())), preferred_element_type=f32)


def swap_halves(value):
    lane = lax.broadcasted_iota(jnp.int32, value.shape, 1)
    return jnp.where(lane < 32, pltpu.roll(value, 96, 1), pltpu.roll(value, 32, 1))


def allowed_mask(lengths_ref, block, rows):
    e0 = lengths_ref[block, 0]
    e1 = e0 + lengths_ref[block, 1]
    t = lax.broadcasted_iota(jnp.int32, (rows, rows), 0)
    s = lax.broadcasted_iota(jnp.int32, (rows, rows), 1)
    seg_t = (t >= e0).astype(jnp.int32) + (t >= e1).astype(jnp.int32)
    seg_s = (s >= e0).astype(jnp.int32) + (s >= e1).astype(jnp.int32)
    return (seg_t == seg_s) & (s <= t)


def dot_rows(a, b):
    return lax.dot_general(a, b, (((0,), (0,)), ((), ())), preferred_element_type=f32)


def loads(copies):
    for copy in copies:
        copy.start()
    return copies


def piece_copies(pieces, half, target, sems, rows):
    return [
        pltpu.make_async_copy(
            piece.at[half] if len(piece.shape) == 3 else piece,
            target.at[pl.ds(at * rows, rows)],
            sems.at[at],
        )
        for at, piece in enumerate(pieces)
    ]


def weight_copies(pieces, refs, spot_ref, target, lanes, sems):
    return [
        pltpu.make_async_copy(
            ref.at[pl.ds(begin, size), :, lanes],
            target.at[pl.ds(first, size), spot_ref[spot]],
            sems.at[at],
        )
        for at, (ref, (_, begin, size, first, spot)) in enumerate(zip(refs, pieces))
    ]


def feed_forward(x, dy, gains, weight, spots, down, bias, numbers, first, after):
    rows, width = x[0].shape[1:]
    count = len(x)
    total = rows * count
    ff = bias.shape[1]

    parts = len(weight)

    def body(number_ref, spot_ref, g_ref, b_ref, *refs):
        w_refs, refs = refs[:parts], refs[parts:]
        x_refs, dy_refs, d_hbm = refs[:count], refs[count : 2 * count], refs[2 * count]
        (h1_hbm, act_hbm, du_hbm, keep_hbm, send_hbm, m_ref, i_ref, db_ref, sum_ref) = refs[
            2 * count + 1 : 2 * count + 10
        ]
        (x_v, dy_v, h1_v, h2_v, w_v, d_v, act_v, du_v, keep_v, send_v, x_sem, dy_sem, w_sem, sems) = refs[
            2 * count + 10 :
        ]
        own = number_ref[0] == 0
        x_copies = loads(piece_copies(x_refs, 0, x_v, x_sem, rows))
        w_copies = loads(
            weight_copies(weight, w_refs, spot_ref, w_v, pl.ds(first, ff), w_sem)
        )
        dy_copies = loads(piece_copies(dy_refs, 1, dy_v, dy_sem, rows))
        d_copy = pltpu.make_async_copy(d_hbm, d_v, sems.at[1])
        d_copy.start()
        for copy in x_copies:
            copy.wait()

        @pl.loop(0, count)
        def _(n):
            at = pl.ds(pl.multiple_of(n * rows, rows), rows)
            value = x_v[at, :].astype(f32)
            mean = jnp.mean(value, 1, keepdims=True)
            centre = value - mean
            inverse = lax.rsqrt(jnp.mean(centre * centre, 1, keepdims=True) + EPS)
            normed = centre * inverse
            m_ref[at, :] = mean
            i_ref[at, :] = inverse
            h1_v[at, :] = (normed * g_ref[0:1] + g_ref[1:2]).astype(bf16)
            h2_v[at, :] = (normed * g_ref[2:3] + g_ref[3:4]).astype(bf16)

        h1_copy = pltpu.make_async_copy(h1_v, h1_hbm, sems.at[2])
        h1_copy.start()
        for copy in w_copies + dy_copies:
            copy.wait()
        d_copy.wait()
        mine = dy_v[:, pl.ds(pl.multiple_of(number_ref[1] * 256, 256), 256)]
        sum_ref[...] = jnp.sum(mine.astype(f32), 0, keepdims=True)

        def split(part, places, high, wide):
            at = (places, high, wide)

            @pl.when(own)
            def _():
                keep_v[at] = part[:, 0]
                send_v[at] = part[:, 1]

            @pl.when(jnp.logical_not(own))
            def _():
                keep_v[at] = part[:, 1]
                send_v[at] = part[:, 0]

        def leaving(n):
            at = (pl.ds(n * 2, 2), pl.ds(0, 64))
            return (
                pltpu.make_async_copy(keep_v.at[at], keep_hbm.at[at], sems.at[3]),
                pltpu.make_async_copy(send_v.at[at], send_hbm.at[at], sems.at[4]),
            )

        @pl.loop(0, ff // 256)
        def _(n):
            at = pl.ds(pl.multiple_of(n * 256, 256), 256)
            u = dot(h2_v[...], w_v[:, :, :, at].reshape(width, 256)) + b_ref[:, at]
            cdf = 0.5 * (1.0 + lax.erf(u * math.sqrt(0.5)))
            pdf = jnp.exp(-0.5 * u * u) * (1.0 / math.sqrt(2.0 * math.pi))
            act = (u * cdf).astype(bf16)
            act_v[:, at] = act
            du = (dot(dy_v[...], d_v[at, :], 1, 1) * (cdf + u * pdf)).astype(bf16)
            du_v[:, at] = du
            db_ref[:, at] = jnp.sum(du.astype(f32), 0, keepdims=True)
            part = dot_rows(act, dy_v[...]).astype(bf16).reshape(2, 2, 64, width)
            split(part, pl.ds(n * 2, 2), pl.ds(0, 64), slice(None))
            for copy in leaving(n):
                copy.start()

        act_copy = pltpu.make_async_copy(act_v, act_hbm, sems.at[0])
        act_copy.start()
        du_copy = pltpu.make_async_copy(du_v, du_hbm, sems.at[1])
        du_copy.start()
        for n in range(ff // 256):
            for copy in leaving(n):
                copy.wait()

        def block(n):
            at = (
                slice(None),
                pl.ds(pl.multiple_of(64 + 16 * (n % 4), 16), 16),
                pl.ds(pl.multiple_of(n // 4 * ff, ff), ff),
            )
            return at

        def away(n):
            at = block(n)
            return (
                pltpu.make_async_copy(keep_v.at[at], keep_hbm.at[at], sems.at[3]),
                pltpu.make_async_copy(send_v.at[at], send_hbm.at[at], sems.at[4]),
            )

        @pl.loop(0, 8)
        def _(n):
            lanes = pl.ds(pl.multiple_of(n * 256, 256), 256)
            part = dot_rows(h2_v[:, lanes], du_v[...]).astype(bf16).reshape(8, 2, 16, ff)
            split(part, *block(n))
            for copy in away(n):
                copy.start()

        for n in range(8):
            for copy in away(n):
                copy.wait()
        h1_copy.wait()
        act_copy.wait()
        du_copy.wait()

    wide = jax.ShapeDtypeStruct((total, width), bf16)
    thin = jax.ShapeDtypeStruct((total, ff), bf16)
    column = jax.ShapeDtypeStruct((total, 1), f32)
    grads = jax.ShapeDtypeStruct((8, 128, width), bf16)
    vmem = pl.BlockSpec(memory_space=pltpu.VMEM)
    return pl.pallas_call(
        after_inputs(body, 5 + parts + 2 * count, len(after)),
        out_shape=(
            wide,
            thin,
            thin,
            grads,
            grads,
            column,
            column,
            jax.ShapeDtypeStruct((1, ff), f32),
            jax.ShapeDtypeStruct((1, 256), f32),
        ),
        in_specs=[pl.BlockSpec(memory_space=pltpu.SMEM)] * 2
        + [vmem, vmem]
        + anywhere(parts + 2 * count + 1 + len(after)),
        out_specs=tuple(anywhere(5)) + (vmem,) * 4,
        scratch_shapes=[
            pltpu.VMEM((total, width), bf16),
            pltpu.VMEM((total, width), bf16),
            pltpu.VMEM((total, width), bf16),
            pltpu.VMEM((total, width), bf16),
            pltpu.VMEM((8, 8, width // 64, ff), bf16),
            pltpu.VMEM((ff, width), bf16),
            pltpu.VMEM((total, ff), bf16),
            pltpu.VMEM((total, ff), bf16),
            pltpu.VMEM((8, 128, width), bf16),
            pltpu.VMEM((8, 128, width), bf16),
            pltpu.SemaphoreType.DMA((count,)),
            pltpu.SemaphoreType.DMA((count,)),
            pltpu.SemaphoreType.DMA((parts,)),
            pltpu.SemaphoreType.DMA((5,)),
        ],
        compiler_params=kernel_params(),
        cost_estimate=cost(32),
        name="feed_forward",
    )(numbers, spots, gains, bias, *[p[0] for p in weight], *x, *dy, down, *after)


def packed(qkv_weight, up_weight, vectors, lengths, place, head, tokens, cotangent):
    wide, up_wide = qkv_weight.shape[1], up_weight.shape[1]
    part, up_part = 3 * head, up_wide // 8
    cols = part + up_part

    def body(place_ref, len_ref, q_ref, u_ref, x_ref, dy_ref, *refs):
        v_refs, out_ref, pair_ref = refs[: len(vectors)], refs[-2], refs[-1]
        pair_ref[0] = x_ref[...]
        pair_ref[1] = dy_ref[...]
        lane = lax.broadcasted_iota(jnp.int32, (8, cols), 1)
        row = lax.broadcasted_iota(jnp.int32, (8, cols), 0)
        sizes = jnp.zeros((8, cols), f32)
        for at in range(3):
            sizes = jnp.where(lane == at, len_ref[0, at].astype(f32), sizes)
        vector = jnp.concatenate([ref[...].astype(f32) for ref in v_refs])[None, :]
        vector = jnp.broadcast_to(vector, (8, cols))
        tail = jnp.where(row == 0, vector, jnp.where(row == 1, sizes, 0.0)).astype(bf16)
        for owner in range(8):
            pieces = [
                q_ref[:, (third * 8 + owner) * head : (third * 8 + owner + 1) * head]
                for third in range(3)
            ]
            pieces.append(u_ref[:, owner * up_part : (owner + 1) * up_part])
            out_ref[owner] = jnp.concatenate([jnp.concatenate(pieces, 1), tail], 0)

    return pl.pallas_call(
        body,
        out_shape=(
            jax.ShapeDtypeStruct((8, 40, cols), bf16),
            jax.ShapeDtypeStruct((2,) + tokens.shape, bf16),
        ),
        grid_spec=pltpu.PrefetchScalarGridSpec(
            num_scalar_prefetch=2,
            grid=(1,),
            in_specs=[
                pl.BlockSpec((32, wide), lambda i, place, lens: (place[0], 0)),
                pl.BlockSpec((32, up_wide), lambda i, place, lens: (place[0], 0)),
                pl.BlockSpec(tokens.shape, lambda i, place, lens: (0, 0)),
                pl.BlockSpec(tokens.shape, lambda i, place, lens: (0, 0)),
            ]
            + [pl.BlockSpec(v.shape, lambda i, place, lens: (0,)) for v in vectors],
            out_specs=(
                pl.BlockSpec((8, 40, cols), lambda i, place, lens: (0, 0, 0)),
                pl.BlockSpec((2,) + tokens.shape, lambda i, place, lens: (0, 0, 0)),
            ),
        ),
        compiler_params=kernel_params(),
        cost_estimate=cost(3),
        name="packed",
    )(place, lengths, qkv_weight, up_weight, tokens, cotangent, *vectors)


def attend(h1, dy, weight, spots, out, bias, cosine, sine, lengths, numbers, after, rows=128):
    total, width = h1.shape
    count = len(dy)
    head = out.shape[0]
    scale = head ** (-0.5)

    parts = len(weight)

    def body(number_ref, len_ref, spot_ref, b_ref, *refs):
        w_refs, refs = refs[:parts], refs[parts:]
        dy_refs = refs[:count]
        h1_hbm, out_hbm, cos_hbm, sin_hbm = refs[count : count + 4]
        ol_hbm, dq_hbm, keep_hbm, send_hbm, sum_ref = refs[count + 4 : count + 9]
        (dy_v, h1_v, w_v, wo_v, cos_v, sin_v, qkv_v, do_v, ol_v, dq_v, keep_v, send_v, dy_sem, w_sem, sems) = (
            refs[count + 9 :]
        )
        own = number_ref[0] == 0
        pairs = (
            (h1_hbm, h1_v),
            (out_hbm, wo_v),
            (cos_hbm, cos_v),
            (sin_hbm, sin_v),
        )
        copies = loads(
            [pltpu.make_async_copy(*pair, sems.at[n]) for n, pair in enumerate(pairs)]
        )
        w_copies = loads(
            weight_copies(weight, w_refs, spot_ref, w_v, pl.ds(0, 3 * head), w_sem)
        )
        dy_copies = loads(piece_copies(dy_refs, 1, dy_v, dy_sem, rows))
        for copy in copies[:1] + w_copies:
            copy.wait()

        @pl.loop(0, 3)
        def _(n):
            at = pl.ds(pl.multiple_of(n * head, head), head)
            qkv_v[:, at] = dot(h1_v[...], w_v[:, :, :, at].reshape(width, head)) + b_ref[n]

        for copy in copies[1:] + dy_copies:
            copy.wait()
        do_v[...] = dot(dy_v[...], wo_v[...], 1, 1).astype(bf16)
        sum_ref[...] = jnp.zeros_like(sum_ref)

        @pl.loop(0, total // rows)
        def _(block):
            at = pl.ds(pl.multiple_of(block * rows, rows), rows)
            cos, sin = cos_v[at, :], sin_v[at, :]

            def turned(value, sign):
                left = value[:, :128]
                left = left * cos + swap_halves(left) * (sin * sign)
                return jnp.concatenate([left, value[:, 128:]], 1).astype(bf16)

            q, k = turned(qkv_v[at, 0:head], 1.0), turned(qkv_v[at, head : 2 * head], 1.0)
            v = qkv_v[at, 2 * head :].astype(bf16)
            scores = dot(q, k, 1, 1) * scale
            masked = jnp.where(allowed_mask(len_ref, block, rows), scores, -1e30)
            shifted = jnp.exp(masked - jnp.max(masked, 1, keepdims=True))
            probs = shifted / jnp.sum(shifted, 1, keepdims=True)
            low = probs.astype(bf16)
            ol_v[at, :] = dot(low, v).astype(bf16)
            d_out = do_v[at, :]
            d_value = dot(low, d_out, 0, 0)
            d_probs = dot(d_out, v, 1, 1)
            centred = d_probs - jnp.sum(d_probs * probs, 1, keepdims=True)
            d_scores = (probs * centred).astype(bf16)
            d_query = turned(dot(d_scores, k) * scale, -1.0)
            d_key = turned(dot(d_scores, q, 0, 0) * scale, -1.0)
            for n, grad in enumerate((d_query, d_key, d_value.astype(bf16))):
                lanes = slice(n * head, (n + 1) * head)
                dq_v[at, lanes] = grad
                sum_ref[:, lanes] += jnp.sum(grad.astype(f32), 0, keepdims=True)

        ol_copy = pltpu.make_async_copy(ol_v, ol_hbm, sems.at[0])
        ol_copy.start()
        dq_copy = pltpu.make_async_copy(dq_v, dq_hbm, sems.at[1])
        dq_copy.start()

        def split(part, high, lanes):
            for z_hi in range(2):
                at = (pl.ds(4 * z_hi, 4), high, lanes)

                @pl.when(own)
                def _(z_hi=z_hi, at=at):
                    keep_v[at] = part[:, z_hi, 0]
                    send_v[at] = part[:, z_hi, 1]

                @pl.when(jnp.logical_not(own))
                def _(z_hi=z_hi, at=at):
                    keep_v[at] = part[:, z_hi, 1]
                    send_v[at] = part[:, z_hi, 0]

        part = dot_rows(ol_v[...], dy_v[...]).astype(bf16).reshape(4, 2, 2, 16, width)
        split(part, pl.ds(48, 16), slice(None))

        @pl.loop(0, 8)
        def _(n):
            lanes = pl.ds(pl.multiple_of(n * 256, 256), 256)
            part = dot_rows(h1_v[:, lanes], dq_v[...]).astype(bf16).reshape(4, 2, 2, 16, 3 * head)
            for third in range(3):
                split(
                    part[..., third * head : (third + 1) * head],
                    pl.ds(16 * third, 16),
                    pl.ds(pl.multiple_of(n * head, head), head),
                )

        keep_copy = pltpu.make_async_copy(keep_v, keep_hbm, sems.at[2])
        keep_copy.start()
        send_copy = pltpu.make_async_copy(send_v, send_hbm, sems.at[3])
        send_copy.start()
        for copy in (ol_copy, dq_copy, keep_copy, send_copy):
            copy.wait()

    grads = jax.ShapeDtypeStruct((8, 64, width), bf16)
    vmem = pl.BlockSpec(memory_space=pltpu.VMEM)
    smem = pl.BlockSpec(memory_space=pltpu.SMEM)
    return pl.pallas_call(
        after_inputs(body, 8 + parts + count, len(after)),
        out_shape=(
            jax.ShapeDtypeStruct((total, head), bf16),
            jax.ShapeDtypeStruct((total, 3 * head), bf16),
            grads,
            grads,
            jax.ShapeDtypeStruct((1, 3 * head), f32),
        ),
        in_specs=[smem, smem, smem, vmem] + anywhere(parts + count + 4 + len(after)),
        out_specs=tuple(anywhere(4)) + (vmem,),
        scratch_shapes=[
            pltpu.VMEM((total, width), bf16),
            pltpu.VMEM((total, width), bf16),
            pltpu.VMEM((8, 8, width // 64, 3 * head), bf16),
            pltpu.VMEM((head, width), bf16),
            pltpu.VMEM((total, 128), f32),
            pltpu.VMEM((total, 128), f32),
            pltpu.VMEM((total, 3 * head), f32),
            pltpu.VMEM((total, head), bf16),
            pltpu.VMEM((total, head), bf16),
            pltpu.VMEM((total, 3 * head), bf16),
            pltpu.VMEM((8, 64, width), bf16),
            pltpu.VMEM((8, 64, width), bf16),
            pltpu.SemaphoreType.DMA((count,)),
            pltpu.SemaphoreType.DMA((parts,)),
            pltpu.SemaphoreType.DMA((4,)),
        ],
        compiler_params=kernel_params(),
        cost_estimate=cost(22),
        name="attend",
    )(
        numbers,
        lengths,
        spots,
        bias,
        *[p[0] for p in weight],
        *dy,
        h1,
        out,
        cosine,
        sine,
        *after,
    )


def outer(d_qkv, d_hidden, weight, spots, x, mean, inverse, gains, active, attended, down, out, bias, after):
    total, n1 = d_qkv.shape
    n2 = d_hidden.shape[1]
    count = len(x)
    parts = len(weight)
    head, width = out.shape
    step = 512

    def body(spot_ref, m_ref, i_ref, g_ref, b_ref, *refs):
        w_refs, refs = refs[:parts], refs[parts:]
        x_refs, refs = refs[:count], refs[count:]
        plain, sums_ref, outs = refs[:6], refs[6], refs[7 : 7 + count]
        dq_v, du_v, act_v, ol_v, wd_v, wo_v, w_v, x_v, pair_v, w_sem, x_sem, sems, out_sem = refs[
            7 + count :
        ]
        plain_v = (dq_v, du_v, act_v, ol_v, wd_v, wo_v)
        copies = loads(
            [
                pltpu.make_async_copy(source, target, sems.at[n])
                for n, (source, target) in enumerate(zip(plain[:2], plain_v[:2]))
            ]
            + weight_copies(weight, w_refs, spot_ref, w_v, slice(None), w_sem)
            + piece_copies(x_refs, 0, x_v, x_sem, 128)
        )
        later = loads(
            [
                pltpu.make_async_copy(plain[n], plain_v[n], sems.at[n]) for n in range(2, 6)
            ]
        )
        for copy in copies:
            copy.wait()

        def leaving(n, half):
            lanes = pl.ds(pl.multiple_of(n * step, step), step)
            return [
                pltpu.make_async_copy(
                    pair_v.at[half, pl.ds(at * 128, 128), lanes],
                    outs[at].at[half, :, lanes],
                    out_sem.at[half, at],
                )
                for at in range(count)
            ]

        @pl.loop(0, width // step)
        def _(n):
            lanes = pl.ds(pl.multiple_of(n * step, step), step)
            sources = pl.ds(n * (step // 256), step // 256)
            d1 = dot(dq_v[...], w_v[sources, :, :, 0:n1].reshape(step, n1), 1, 1)
            d2 = dot(du_v[...], w_v[sources, :, :, n1:].reshape(step, n2), 1, 1)
            pair_v[1, :, lanes] = (d1 * g_ref[0:1, lanes] + d2 * g_ref[1:2, lanes]).astype(bf16)
            for copy in leaving(n, 1):
                copy.start()
            normed = (x_v[:, lanes].astype(f32) - m_ref[...]) * i_ref[...]
            sums_ref[0:1, lanes] = jnp.sum(d1 * normed, 0, keepdims=True)
            sums_ref[1:2, lanes] = jnp.sum(d1, 0, keepdims=True)
            sums_ref[2:3, lanes] = jnp.sum(d2 * normed, 0, keepdims=True)
            sums_ref[3:4, lanes] = jnp.sum(d2, 0, keepdims=True)

        for copy in later:
            copy.wait()

        @pl.loop(0, width // step)
        def _(n):
            lanes = pl.ds(pl.multiple_of(n * step, step), step)
            mix = dot(act_v[...], wd_v[:, lanes]) + dot(ol_v[...], wo_v[:, lanes])
            pair_v[0, :, lanes] = (mix + b_ref[:, lanes]).astype(bf16)
            for copy in leaving(n, 0):
                copy.start()

        for n in range(width // step):
            for half in range(2):
                for copy in leaving(n, half):
                    copy.wait()

    vmem = pl.BlockSpec(memory_space=pltpu.VMEM)
    return pl.pallas_call(
        after_inputs(body, 11 + parts + count, len(after)),
        out_shape=(jax.ShapeDtypeStruct((4, width), f32),)
        + (jax.ShapeDtypeStruct((2, 128, width), bf16),) * count,
        in_specs=[pl.BlockSpec(memory_space=pltpu.SMEM)]
        + [vmem] * 4
        + anywhere(parts + count + 6 + len(after)),
        out_specs=(vmem,) + tuple(anywhere(count)),
        scratch_shapes=[
            pltpu.VMEM((total, n1), bf16),
            pltpu.VMEM((total, n2), bf16),
            pltpu.VMEM((total, n2), bf16),
            pltpu.VMEM((total, head), bf16),
            pltpu.VMEM((n2, width), bf16),
            pltpu.VMEM((head, width), bf16),
            pltpu.VMEM((8, 8, width // 64, n1 + n2), bf16),
            pltpu.VMEM((total, width), bf16),
            pltpu.VMEM((2, total, width), bf16),
            pltpu.SemaphoreType.DMA((parts,)),
            pltpu.SemaphoreType.DMA((count,)),
            pltpu.SemaphoreType.DMA((6,)),
            pltpu.SemaphoreType.DMA((2, count)),
        ],
        compiler_params=kernel_params(),
        cost_estimate=cost(20),
        name="outer",
    )(
        spots,
        mean,
        inverse,
        gains,
        bias,
        *[p[0] for p in weight],
        *x,
        d_qkv,
        d_hidden,
        active,
        attended,
        down,
        out,
        *after,
    )


def unpacked(part, after):
    owners, _, cols = part.shape

    def body(part_ref, rows_ref, info_ref):
        for owner in range(owners):
            rows_ref[owner] = part_ref[owner, 0:32]
            info_ref[owner] = part_ref[owner, 32:40].astype(f32)

    return pl.pallas_call(
        after_inputs(body, 1, len(after)),
        out_shape=(
            jax.ShapeDtypeStruct((owners, 32, cols), bf16),
            jax.ShapeDtypeStruct((owners, 8, cols), f32),
        ),
        in_specs=[pl.BlockSpec(memory_space=pltpu.VMEM)] + anywhere(len(after)),
        out_specs=(pl.BlockSpec(memory_space=pltpu.VMEM),) * 2,
        compiler_params=kernel_params(),
        cost_estimate=cost(3),
        name="unpacked",
    )(part, *after)


def packed_sums(stays, crossed, own, below, above, ff, head, after):
    width = own.shape[1]

    def body(stay_ref, cross_ref, own_ref, below_ref, above_ref, out_ref, keep_ref):
        inner = (stay_ref[0].astype(f32) + cross_ref[0].astype(f32)).astype(bf16)
        total = wide(own_ref, below_ref, above_ref).astype(bf16)
        for owner in range(8):
            pieces = [
                total[16 * third : 16 * third + 16, owner * head : (owner + 1) * head]
                for third in range(3)
            ]
            row, col = 64 + 16 * (owner % 4), owner // 4 * ff
            pieces.append(inner[row : row + 16, col : col + ff])
            out_ref[owner] = jnp.concatenate(pieces, 1)
        keep_ref[0:64] = inner[0:64]
        keep_ref[64:80] = total[48:64]

    vmem = pl.BlockSpec(memory_space=pltpu.VMEM)
    return pl.pallas_call(
        after_inputs(body, 5, len(after)),
        out_shape=(
            jax.ShapeDtypeStruct((8, 16, 3 * head + ff), bf16),
            jax.ShapeDtypeStruct((80, width), bf16),
        ),
        in_specs=[vmem] * 5 + anywhere(len(after)),
        out_specs=(vmem,) * 2,
        compiler_params=kernel_params(),
        cost_estimate=cost(3),
        name="packed_sums",
    )(stays, crossed, own, below, above, *after)


def halves(below, above, x_pair, dy_pair, after):
    count, rows, cols = below.shape
    _, tokens, width = x_pair.shape
    half = (count // 2, rows, cols)

    def body(below_ref, above_ref, x_ref, dy_ref, low_ref, high_ref, x_out, dy_out):
        low_ref[...] = below_ref[...]
        high_ref[...] = above_ref[...]
        x_out[...] = x_ref[0]
        dy_out[...] = dy_ref[0]

    def at(block, first):
        return pl.BlockSpec(block, lambda i: (first,) + (0,) * (len(block) - 1))

    return pl.pallas_call(
        after_inputs(body, 4, len(after)),
        out_shape=(jax.ShapeDtypeStruct(half, bf16),) * 2
        + (jax.ShapeDtypeStruct((tokens, width), bf16),) * 2,
        grid=(1,),
        in_specs=[
            at(half, 0),
            at(half, 1),
            at((1, tokens, width), 0),
            at((1, tokens, width), 1),
        ]
        + anywhere(len(after)),
        out_specs=(at(half, 0), at(half, 0), at((tokens, width), 0), at((tokens, width), 0)),
        compiler_params=kernel_params(),
        cost_estimate=cost(3),
        name="halves",
    )(below, above, x_pair, dy_pair, *after)


def joined(arrays, after):
    sizes = [array.shape[0] for array in arrays]
    unit = math.gcd(*sizes)
    block = (unit,) + arrays[0].shape[1:]
    count = len(arrays)
    firsts = [sum(sizes[:n]) // unit for n in range(count)]

    def body(*refs):
        step = pl.program_id(0)
        for ref, first, size in zip(refs, firsts, sizes):

            @pl.when((step >= first) & (step < first + size // unit))
            def _(ref=ref):
                refs[count][...] = ref[...]

    def came(first, size):
        return pl.BlockSpec(block, lambda i: (jnp.clip(i - first, 0, size // unit - 1), 0, 0))

    return pl.pallas_call(
        after_inputs(body, count, len(after)),
        out_shape=jax.ShapeDtypeStruct((sum(sizes),) + block[1:], bf16),
        grid=(sum(sizes) // unit,),
        in_specs=[came(first, size) for first, size in zip(firsts, sizes)] + anywhere(len(after)),
        out_specs=pl.BlockSpec(block, lambda i: (i, 0, 0)),
        compiler_params=kernel_params(),
        cost_estimate=cost(3),
        name="joined",
    )(*arrays, *after)


def blocks_call(name, body, numbers, terms, outs, after):
    def came(block, index):
        rest = (0,) * (len(block) - 1)
        return pl.BlockSpec(block, lambda i, n: (index(n),) + rest)

    return pl.pallas_call(
        after_inputs(body, 1 + len(terms), len(after)),
        out_shape=tuple(jax.ShapeDtypeStruct(out, bf16) for out in outs),
        grid_spec=pltpu.PrefetchScalarGridSpec(
            num_scalar_prefetch=1,
            grid=(1,),
            in_specs=[came(block, index) for _, block, index in terms] + anywhere(len(after)),
            out_specs=tuple(
                pl.BlockSpec(out, lambda i, n, size=len(out): (0,) * size) for out in outs
            ),
        ),
        compiler_params=kernel_params(),
        cost_estimate=cost(3),
        name=name,
    )(numbers, *[array for array, _, _ in terms], *after)


def wide(*refs):
    return functools.reduce(jnp.add, [ref[...].astype(f32) for ref in refs])


def spread(pieces, places, core, targets, count, before, after):
    rows, cols = pieces[0][0].shape[1:]
    firsts, total = [], 0
    for mine, _ in pieces:
        firsts.append(total)
        total += mine.shape[0]

    def body(place_ref, core_ref, *refs):
        step = pl.program_id(0)
        outs = refs[2 * len(pieces) + len(before) :]
        first_core = core_ref[0] == 0

        def fill(ref, low):
            for out_ref, (_, high, parts) in zip(outs, targets):
                for to, row, col, size in parts:
                    out_ref[low * high : (low + 1) * high, to : to + size] = ref[
                        0, row : row + high, col : col + size
                    ].astype(f32)

        for n, (first, (mine, _)) in enumerate(zip(firsts, pieces)):
            here = (step >= first) & (step < first + mine.shape[0])

            @pl.when(here & first_core)
            def _(n=n):
                fill(refs[2 * n], 0)
                fill(refs[2 * n + 1], 1)

            @pl.when(here & jnp.logical_not(first_core))
            def _(n=n):
                fill(refs[2 * n], 1)
                fill(refs[2 * n + 1], 0)

    def chosen(first, size):
        return pl.BlockSpec(
            (1, rows, cols), lambda i, place, core: (jnp.clip(i - first, 0, size - 1), 0, 0)
        )

    specs, arrays = [], []
    for first, (mine, yours) in zip(firsts, pieces):
        specs += [chosen(first, mine.shape[0])] * 2
        arrays += [mine, yours]
    return pl.pallas_call(
        after_inputs(body, 2 + 2 * len(pieces) + len(before), len(after)),
        out_shape=tuple(
            jax.ShapeDtypeStruct((2 * count * high, wide), f32) for wide, high, _ in targets
        ),
        grid_spec=pltpu.PrefetchScalarGridSpec(
            num_scalar_prefetch=2,
            grid=(total,),
            in_specs=specs + anywhere(len(before) + len(after)),
            out_specs=tuple(
                pl.BlockSpec((2 * high, wide), lambda i, place, core: (place[i], 0))
                for wide, high, _ in targets
            ),
        ),
        input_output_aliases={2 + len(arrays) + n: n for n in range(len(before))},
        compiler_params=kernel_params(),
        cost_estimate=cost(1.2 * total),
        name="spread",
    )(places, core, *arrays, *before, *after)


def small_sums(norm_sums, qkv_sums, up_sums, dy_sums, numbers):
    def body(number_ref, norm_ref, q_ref, u_ref, y_ref, out_ref, work):
        shard = number_ref[1]
        for owner in range(8):
            mine = shard == owner
            for n in range(4):
                for half in range(2):
                    at = owner * 256 + half * 128
                    work[owner, n * 2 + half : n * 2 + half + 1] = norm_ref[n : n + 1, at : at + 128]
            for n in range(3):
                third, source = divmod(owner * 3 + n, 8)
                for half in range(2):
                    at = third * 256 + half * 128
                    work[owner, 8 + n * 2 + half : 9 + n * 2 + half] = jnp.where(
                        shard == source, q_ref[:, at : at + 128], 0.0
                    )
            for n in range(8):
                work[owner, 14 + n : 15 + n] = jnp.where(
                    mine, u_ref[:, n * 128 : (n + 1) * 128], 0.0
                )
            for n in range(2):
                work[owner, 22 + n : 23 + n] = jnp.where(
                    mine, y_ref[:, n * 128 : (n + 1) * 128], 0.0
                )
        out_ref[...] = work[...].astype(bf16)

    vmem = pl.BlockSpec(memory_space=pltpu.VMEM)
    return pl.pallas_call(
        body,
        out_shape=jax.ShapeDtypeStruct((8, 24, 128), bf16),
        in_specs=[pl.BlockSpec(memory_space=pltpu.SMEM)] + [vmem] * 4,
        out_specs=vmem,
        scratch_shapes=[pltpu.VMEM((8, 24, 128), f32)],
        compiler_params=kernel_params(),
        cost_estimate=cost(3),
        name="small_sums",
    )(numbers, norm_sums, qkv_sums, up_sums, dy_sums)


def local(
    tokens,
    doc_lengths,
    cotangent,
    ln1_gain,
    ln1_bias,
    ln2_gain,
    ln2_bias,
    qkv_weight,
    qkv_bias,
    out_weight,
    out_bias,
    up_weight,
    up_bias,
    down_weight,
    down_bias,
):
    rows, width = tokens.shape
    head = width // HEADS
    group = 8
    rep = lax.axis_index("rep")
    shard = lax.axis_index("shard")
    y, h, c = rep // 4, (rep // 2) % 2, rep % 2
    l, x = shard // 4, shard % 4
    ff = up_bias.shape[0]

    cols = 3 * head + ff
    vectors = [ln1_gain, ln1_bias, ln2_gain, ln2_bias, qkv_bias]
    place = (y * 2 + c).astype(jnp.int32).reshape(1)
    part, pair = packed(
        qkv_weight, up_weight, vectors, doc_lengths, place, head, tokens, cotangent
    )
    below, above, other = move(pair, x=1), move(pair, x=-1), move(pair, l=1)
    far, other_above, other_below = move(below, x=1), move(other, x=-1), move(below, l=1)
    pairs = (pair, above, far, below, other, other_above, None, other_below)

    part = lax.all_to_all(part, "shard", 0, 0)
    own, infos = unpacked(part, (pairs[1], pairs[3], pairs[4]))
    below, above = move(own, y=1), move(own, y=-1)
    low, high, x_half, dy_half = halves(below, above, other_below, other_above, (far,))
    far_low, far_high = move(low, y=1), move(high, y=-1)
    x_other_far, dy_other_far = move(x_half, x=1), move(dy_half, x=-1)
    x_all = tuple(x_other_far if p is None else p for p in pairs)
    dy_all = tuple(dy_other_far if p is None else p for p in pairs)
    yours = move(joined((own, above, below), (low,)), c=1)
    far_low_c, far_high_c = move(far_low, c=1), move(far_high, c=1)
    weight = (
        (own, 0, 8, 0, 0),
        (above, 0, 8, 0, 1),
        (far_low, 0, 4, 0, 2),
        (far_high, 0, 4, 4, 2),
        (below, 0, 8, 0, 3),
        (yours, 0, 8, 0, 4),
        (yours, 8, 8, 0, 5),
        (far_low_c, 0, 4, 0, 6),
        (far_high_c, 0, 4, 4, 6),
        (yours, 16, 8, 0, 7),
    )
    steps4 = (y + jnp.arange(4)) % 4
    spots = jnp.concatenate([steps4 * 2 + c, steps4 * 2 + 1 - c]).astype(jnp.int32)

    gains = infos[:, 0, :1024].reshape(8, 4, 256).transpose(1, 0, 2).reshape(4, width)
    qkv_b = infos[:, 0, 1024:].reshape(8 * 3, 1, head)
    qkv_b = jnp.stack(
        [lax.dynamic_index_in_dim(qkv_b, third * 8 + shard, 0, False) for third in range(3)]
    )
    steps8 = jnp.arange(8)
    sources = ((steps8 // 4) ^ l) * 4 + (x + steps8 % 4) % 4
    sources = sources.astype(jnp.int32)
    lengths = infos[:, 1, :3]
    lengths = jnp.sum(
        jnp.where(sources[:, None, None] == steps8[None, :, None], lengths[None], 0.0), 1
    ).astype(jnp.int32)
    ends = jnp.cumsum(lengths, 1)
    starts = ends - lengths
    steps_t = jnp.arange(rows, dtype=jnp.int32)
    segment = jnp.sum((steps_t[None, :, None] >= ends[:, None, :]).astype(jnp.int32), -1)
    slots = jnp.arange(lengths.shape[1], dtype=jnp.int32)
    begin = jnp.sum(
        jnp.where(segment[:, :, None] == slots[None, None, :], starts[:, None, :], 0), -1
    )
    position = (steps_t[None, :] - begin).astype(f32).reshape(group * rows, 1)
    lane = jnp.arange(128)
    freq = 10000.0 ** (-2.0 * (lane % (ROT // 2)).astype(f32) / ROT)
    angle = position * freq[None, :]
    cosine = jnp.where(lane < ROT, jnp.cos(angle), 1.0)
    sine = jnp.sin(angle)
    sine = jnp.where(lane < ROT // 2, -sine, jnp.where(lane < ROT, sine, 0.0))

    both_bias = (out_bias.astype(f32) + down_bias.astype(f32))[None, :]
    wide_bias = lax.dynamic_update_slice(jnp.zeros((1, width), f32), both_bias, (0, shard * 256))
    numbers = jnp.stack([c, shard, y, h]).astype(jnp.int32)

    h1, active, d_hidden, keep, send, mean, inverse, up_sums, dy_sums = feed_forward(
        x_all,
        dy_all,
        gains,
        weight,
        spots,
        down_weight,
        up_bias.astype(f32)[None],
        numbers,
        3 * head,
        (cosine, sine),
    )
    got = move(send, c=1)
    attended, d_qkv, a_keep, a_send, qkv_sums = attend(
        h1, dy_all, weight, spots, out_weight, qkv_b, cosine, sine, lengths, numbers, (send,)
    )

    pair_shape, one = (2, 128, width), (1, 128, width)

    def turn(k):
        return lambda n: (n[2] + k) % 4

    def far_body(n_ref, keep_ref, got_ref, low_ref, high_ref):
        total = wide(keep_ref, got_ref).astype(bf16)
        low_ref[0] = total[0]
        high_ref[0] = total[1]

    low, high = blocks_call(
        "far_sums",
        far_body,
        numbers,
        [(keep, pair_shape, turn(2)), (got, pair_shape, turn(2))],
        (one, one),
        (attended,),
    )
    from_low, from_high = move(low, y=1), move(high, y=-1)
    a_got = move(a_send, c=1)
    norm_sums, *pairs_out = outer(
        d_qkv,
        d_hidden,
        weight,
        spots,
        x_all,
        mean,
        inverse,
        jnp.stack([gains[0], gains[2]]),
        active,
        attended,
        down_weight,
        out_weight,
        wide_bias,
        (low, high),
    )

    def near_body(n_ref, k1_ref, g1_ref, k3_ref, g3_ref, low_ref, high_ref, above_ref, below_ref):
        above, below = wide(k1_ref, g1_ref), wide(k3_ref, g3_ref)
        above_ref[0] = (above[0] + low_ref[0].astype(f32)).astype(bf16)
        above_ref[1] = above[1].astype(bf16)
        below_ref[0] = below[0].astype(bf16)
        below_ref[1] = (below[1] + high_ref[0].astype(f32)).astype(bf16)

    above, below = blocks_call(
        "near_sums",
        near_body,
        numbers,
        [(v, pair_shape, turn(k)) for k in (1, 3) for v in (keep, got)]
        + [(v, one, lambda n: 0) for v in (from_low, from_high)],
        (pair_shape, pair_shape),
        (pairs_out[0],),
    )
    from_below, from_above = move(above, y=1), move(below, y=-1)

    four, part_shape = (4, 64, width), (1, 64, width)

    def away_body(n_ref, keep_ref, got_ref, out_ref):
        out_ref[...] = wide(keep_ref, got_ref).astype(bf16)

    (a_away,) = blocks_call(
        "away_sums",
        away_body,
        numbers,
        [(v, four, lambda n: 1 - n[3]) for v in (a_keep, a_got)],
        (four,),
        (above,),
    )
    a_crossed = move(a_away, h=1)

    smalls = small_sums(norm_sums, qkv_sums, up_sums, dy_sums, numbers)
    smalls = jnp.broadcast_to(smalls[None], (16, 8, 24, 128)).reshape(128, 24, 128)
    smalls = lax.all_to_all(smalls, BOTH, 0, 0)
    smalls = jnp.sum(smalls.astype(f32), 0)

    passed_below, passed_above = move(pairs_out[6], x=1), move(pairs_out[2], x=-1)

    def passed_body(n_ref, up_ref, from_below, here_ref, down_ref, from_above, there_ref, up_out, down_out):
        up_out[0:2] = wide(up_ref, from_below).astype(bf16)
        up_out[2:4] = here_ref[...]
        down_out[0:2] = wide(down_ref, from_above).astype(bf16)
        down_out[2:4] = there_ref[...]

    ups, downs = blocks_call(
        "passed_sums",
        passed_body,
        numbers,
        [
            (v, pair_shape, lambda n: 0)
            for v in (
                pairs_out[5],
                passed_below,
                pairs_out[1],
                pairs_out[3],
                passed_above,
                pairs_out[7],
            )
        ],
        ((4, 128, width),) * 2,
        (a_away,),
    )
    from_device_below, from_device_above = move(ups, x=1), move(downs, x=-1)

    def ends_body(n_ref, keep_ref, got_ref, below_ref, above_ref, leave_ref, stay_ref):
        total = wide(keep_ref, got_ref, below_ref, above_ref).astype(bf16)
        first = n_ref[3] == 0
        leave_ref[0] = jnp.where(first, total[1], total[0])
        stay_ref[0] = jnp.where(first, total[0], total[1])

    leaves, stays = blocks_call(
        "end_sums",
        ends_body,
        numbers,
        [(v, pair_shape, turn(0)) for v in (keep, got)]
        + [(v, pair_shape, lambda n: 0) for v in (from_below, from_above)],
        (one, one),
        (a_away,),
    )
    crossed = move(leaves, h=1)

    def around_body(n_ref, keep_ref, got_ref, crossed_ref, low_ref, high_ref, above_ref, own_ref, below_ref):
        def part(k):
            at = (n_ref[2] + k) % 4
            return wide(keep_ref.at[at], got_ref.at[at], crossed_ref.at[at]).astype(bf16)

        far = part(2)
        low_ref[...] = far[:32]
        high_ref[...] = far[32:]
        above_ref[...] = part(1)
        own_ref[...] = part(0)
        below_ref[...] = part(3)

    a_low, a_high, a_above, a_own, a_below = blocks_call(
        "around_sums",
        around_body,
        numbers,
        [(v, four, lambda n: n[3]) for v in (a_keep, a_got)] + [(a_crossed, four, lambda n: 0)],
        ((32, width), (32, width), (64, width), (64, width), (64, width)),
        (leaves,),
    )
    a_low, a_high = move(a_low, y=1), move(a_high, y=-1)

    def beside_body(n_ref, above_ref, below_ref, low_ref, high_ref, up_ref, down_ref):
        up_ref[0:32] = (above_ref[0:32].astype(f32) + low_ref[...].astype(f32)).astype(bf16)
        up_ref[32:64] = above_ref[32:64]
        down_ref[0:32] = below_ref[0:32]
        down_ref[32:64] = (below_ref[32:64].astype(f32) + high_ref[...].astype(f32)).astype(bf16)

    a_above, a_below = blocks_call(
        "beside_sums",
        beside_body,
        numbers,
        [(v, v.shape, lambda n: 0) for v in (a_above, a_below, a_low, a_high)],
        ((64, width), (64, width)),
        (crossed,),
    )
    a_from_below, a_from_above = move(a_above, y=1), move(a_below, y=-1)

    part, stays = packed_sums(
        stays,
        crossed,
        a_own,
        a_from_below,
        a_from_above,
        ff,
        head,
        (smalls,),
    )
    part = lax.all_to_all(part, "shard", 0, 0).reshape(1, 128, cols)

    total = pairs_out[4].astype(f32) + from_device_below[:2].astype(f32)
    total = (total + from_device_above[2:].astype(f32)).astype(bf16)
    totals = pairs_out[0].astype(f32) + from_device_below[2:].astype(f32)
    totals = totals + from_device_above[:2].astype(f32) + move(total, l=1).astype(f32)
    mixed = (tokens.astype(f32) + totals[0]).astype(bf16)
    own_sum = totals[1]
    own_normed, own_inverse = normalize(tokens)
    tokens_grad = cotangent.astype(f32) + own_inverse * (
        own_sum
        - jnp.mean(own_sum, -1, keepdims=True)
        - own_normed * jnp.mean(own_sum * own_normed, -1, keepdims=True)
    )

    order = ((0, h), (0, 1 - h), (1, h), (1, 1 - h), (3, h), (3, 1 - h), (2, h), (2, 1 - h))
    places = jnp.stack([(y + k) % 4 * 2 + high for k, high in order]).astype(jnp.int32)

    def rep_gather(own):
        own = jnp.concatenate([own, move(own, h=1)])
        below, above = move(own, y=1), move(own, y=-1)
        return (own, above, below), (move(below[:1], y=1), move(above[1:], y=-1))

    near, far = rep_gather(part)
    near = [(v, move(v, c=1)) for v in near]
    targets = [
        (
            3 * width,
            16,
            [
                ((third * 8 + source) * head, 16 * source, third * head, head)
                for source in range(8)
                for third in range(3)
            ],
        ),
        (8 * ff, 16, [(source * ff, 16 * source, 3 * head, ff) for source in range(8)]),
    ]
    grads = spread(near, places[:6], numbers[:1], targets, 8, (), ())
    far = joined(far, (grads[0],))

    near_stays, far_stays = rep_gather(stays[None])
    stays = joined(near_stays + far_stays, ())
    down_grad, out_grad = spread(
        [(stays, move(stays, c=1))],
        places,
        numbers[:1],
        [(width, 64, [(0, 0, 0, width)]), (width, 16, [(0, 64, 0, width)])],
        8,
        (),
        (),
    )
    qkv_grad, up_grad = spread(
        [(far, move(far, c=1))],
        places[6:],
        numbers[:1],
        targets,
        8,
        grads,
        (tokens_grad, mixed, down_grad),
    )
    norm_grads = smalls[:8].reshape(4, 256)
    dy_total = smalls[22:].reshape(256)
    return (
        mixed,
        tokens_grad,
        norm_grads[0],
        norm_grads[1],
        norm_grads[2],
        norm_grads[3],
        qkv_grad,
        smalls[8:14].reshape(768),
        out_grad,
        dy_total,
        up_grad,
        smalls[14:22].reshape(ff),
        down_grad,
        dy_total,
    )


def solution(mesh):
    rows = P(BOTH, None)
    vector, matrix = P("shard"), P("shard", None)
    return jax.shard_map(
        local,
        mesh=mesh,
        in_specs=(rows, rows, rows, vector, vector, vector, vector)
        + (matrix, vector, matrix, vector, matrix, vector, matrix, vector),
        out_specs=(rows, rows, vector, vector, vector, vector)
        + (matrix, vector, matrix, vector, matrix, vector, matrix, vector),
        check_vma=False,
    )
```

```python
import functools
import math

import jax
import jax.numpy as jnp
from jax import lax
from jax.experimental import pallas as pl
from jax.experimental.pallas import tpu as pltpu
from jax.sharding import PartitionSpec as P

HEADS = 8
ROT = 64
EPS = 1e-05
f32 = jnp.float32
bf16 = jnp.bfloat16


def cost(time):
    return pl.CostEstimate(flops=int(time * 1.15e9), bytes_accessed=1000, transcendentals=0)


BOTH = ("rep", "shard")
SIZES = (4, 2, 2, 2, 4)
SAME_CORE = [[2 * n + c for n in range(8)] for c in range(2)]
SAME_CORE_ALL = [[(2 * n + c) * 8 + s for n in range(8) for s in range(8)] for c in range(2)]


def coords():
    for y in range(4):
        for h in range(2):
            for c in range(2):
                for l in range(2):
                    for x in range(4):
                        yield (y, h, c, l, x)


def linear(t):
    y, h, c, l, x = (v % m for v, m in zip(t, SIZES))
    return ((y * 2 + h) * 2 + c) * 8 + l * 4 + x


def move(value, y=0, h=0, c=0, l=0, x=0):
    step = (y, h, c, l, x)
    pairs = [(linear(t), linear(tuple(a + b for a, b in zip(t, step)))) for t in coords()]
    return lax.ppermute(value, BOTH, pairs)


def pick(value, index, axis):
    return lax.dynamic_index_in_dim(value, index, axis, keepdims=False)


def kernel_params():
    return pltpu.CompilerParams(vmem_limit_bytes=56 * 1024 * 1024)


def after_inputs(body, count, extra):
    return lambda *refs: body(*refs[:count], *refs[count + extra :])


def anywhere(count):
    return [pl.BlockSpec(memory_space=pl.ANY)] * count


def dot(a, b, ca=1, cb=0):
    return lax.dot_general(a, b, (((ca,), (cb,)), ((), ())), preferred_element_type=f32)


def swap_halves(value):
    lane = lax.broadcasted_iota(jnp.int32, value.shape, 1)
    return jnp.where(lane < 32, pltpu.roll(value, 96, 1), pltpu.roll(value, 32, 1))


def allowed_mask(lengths_ref, block, rows):
    e0 = lengths_ref[block, 0]
    e1 = e0 + lengths_ref[block, 1]
    t = lax.broadcasted_iota(jnp.int32, (rows, rows), 0)
    s = lax.broadcasted_iota(jnp.int32, (rows, rows), 1)
    seg_t = (t >= e0).astype(jnp.int32) + (t >= e1).astype(jnp.int32)
    seg_s = (s >= e0).astype(jnp.int32) + (s >= e1).astype(jnp.int32)
    return (seg_t == seg_s) & (s <= t)


def dot_rows(a, b):
    return lax.dot_general(a, b, (((0,), (0,)), ((), ())), preferred_element_type=f32)


def loads(copies):
    for copy in copies:
        copy.start()
    return copies


def piece_copies(pieces, half, target, sems, rows):
    return [
        pltpu.make_async_copy(
            piece.at[half] if len(piece.shape) == 3 else piece,
            target.at[pl.ds(at * rows, rows)],
            sems.at[at],
        )
        for at, piece in enumerate(pieces)
    ]


def weight_copies(pieces, refs, spot_ref, target, lanes, sems):
    return [
        pltpu.make_async_copy(
            ref.at[pl.ds(begin, size), :, lanes],
            target.at[pl.ds(first, size), spot_ref[spot]],
            sems.at[at],
        )
        for at, (ref, (_, begin, size, first, spot)) in enumerate(zip(refs, pieces))
    ]


def feed_forward(x, dy, gains, weight, spots, down, bias, numbers, first, after):
    rows, width = x[0].shape[1:]
    count = len(x)
    total = rows * count
    ff = bias.shape[1]

    parts = len(weight)

    def body(number_ref, spot_ref, g_ref, b_ref, *refs):
        w_refs, refs = refs[:parts], refs[parts:]
        x_refs, dy_refs, d_hbm = refs[:count], refs[count : 2 * count], refs[2 * count]
        (h1_hbm, act_hbm, du_hbm, keep_hbm, send_hbm, m_ref, i_ref, db_ref, sum_ref) = refs[
            2 * count + 1 : 2 * count + 10
        ]
        (x_v, dy_v, h1_v, h2_v, w_v, d_v, act_v, du_v, keep_v, send_v, x_sem, dy_sem, w_sem, sems) = refs[
            2 * count + 10 :
        ]
        own = number_ref[0] == 0
        x_copies = loads(piece_copies(x_refs, 0, x_v, x_sem, rows))
        w_copies = loads(
            weight_copies(weight, w_refs, spot_ref, w_v, pl.ds(first, ff), w_sem)
        )
        dy_copies = loads(piece_copies(dy_refs, 1, dy_v, dy_sem, rows))
        d_copy = pltpu.make_async_copy(d_hbm, d_v, sems.at[1])
        d_copy.start()
        for copy in x_copies:
            copy.wait()

        @pl.loop(0, count)
        def _(n):
            at = pl.ds(pl.multiple_of(n * rows, rows), rows)
            value = x_v[at, :].astype(f32)
            mean = jnp.mean(value, 1, keepdims=True)
            centre = value - mean
            inverse = lax.rsqrt(jnp.mean(centre * centre, 1, keepdims=True) + EPS)
            normed = centre * inverse
            m_ref[at, :] = mean
            i_ref[at, :] = inverse
            h1_v[at, :] = (normed * g_ref[0:1] + g_ref[1:2]).astype(bf16)
            h2_v[at, :] = (normed * g_ref[2:3] + g_ref[3:4]).astype(bf16)

        h1_copy = pltpu.make_async_copy(h1_v, h1_hbm, sems.at[2])
        h1_copy.start()
        for copy in w_copies + dy_copies:
            copy.wait()
        d_copy.wait()
        mine = dy_v[:, pl.ds(pl.multiple_of(number_ref[1] * 256, 256), 256)]
        sum_ref[...] = jnp.sum(mine.astype(f32), 0, keepdims=True)

        def split(part, places, high, wide):
            at = (places, high, wide)

            @pl.when(own)
            def _():
                keep_v[at] = part[:, 0]
                send_v[at] = part[:, 1]

            @pl.when(jnp.logical_not(own))
            def _():
                keep_v[at] = part[:, 1]
                send_v[at] = part[:, 0]

        def leaving(n):
            at = (pl.ds(n * 2, 2), pl.ds(0, 64))
            return (
                pltpu.make_async_copy(keep_v.at[at], keep_hbm.at[at], sems.at[3]),
                pltpu.make_async_copy(send_v.at[at], send_hbm.at[at], sems.at[4]),
            )

        @pl.loop(0, ff // 256)
        def _(n):
            at = pl.ds(pl.multiple_of(n * 256, 256), 256)
            u = dot(h2_v[...], w_v[:, :, :, at].reshape(width, 256)) + b_ref[:, at]
            cdf = 0.5 * (1.0 + lax.erf(u * math.sqrt(0.5)))
            pdf = jnp.exp(-0.5 * u * u) * (1.0 / math.sqrt(2.0 * math.pi))
            act = (u * cdf).astype(bf16)
            act_v[:, at] = act
            du = (dot(dy_v[...], d_v[at, :], 1, 1) * (cdf + u * pdf)).astype(bf16)
            du_v[:, at] = du
            db_ref[:, at] = jnp.sum(du.astype(f32), 0, keepdims=True)
            part = dot_rows(act, dy_v[...]).astype(bf16).reshape(2, 2, 64, width)
            split(part, pl.ds(n * 2, 2), pl.ds(0, 64), slice(None))
            for copy in leaving(n):
                copy.start()

        act_copy = pltpu.make_async_copy(act_v, act_hbm, sems.at[0])
        act_copy.start()
        du_copy = pltpu.make_async_copy(du_v, du_hbm, sems.at[1])
        du_copy.start()
        for n in range(ff // 256):
            for copy in leaving(n):
                copy.wait()

        def block(n):
            at = (
                slice(None),
                pl.ds(pl.multiple_of(64 + 16 * (n % 4), 16), 16),
                pl.ds(pl.multiple_of(n // 4 * ff, ff), ff),
            )
            return at

        def away(n):
            at = block(n)
            return (
                pltpu.make_async_copy(keep_v.at[at], keep_hbm.at[at], sems.at[3]),
                pltpu.make_async_copy(send_v.at[at], send_hbm.at[at], sems.at[4]),
            )

        @pl.loop(0, 8)
        def _(n):
            lanes = pl.ds(pl.multiple_of(n * 256, 256), 256)
            part = dot_rows(h2_v[:, lanes], du_v[...]).astype(bf16).reshape(8, 2, 16, ff)
            split(part, *block(n))
            for copy in away(n):
                copy.start()

        for n in range(8):
            for copy in away(n):
                copy.wait()
        h1_copy.wait()
        act_copy.wait()
        du_copy.wait()

    wide = jax.ShapeDtypeStruct((total, width), bf16)
    thin = jax.ShapeDtypeStruct((total, ff), bf16)
    column = jax.ShapeDtypeStruct((total, 1), f32)
    grads = jax.ShapeDtypeStruct((8, 128, width), bf16)
    vmem = pl.BlockSpec(memory_space=pltpu.VMEM)
    return pl.pallas_call(
        after_inputs(body, 5 + parts + 2 * count, len(after)),
        out_shape=(
            wide,
            thin,
            thin,
            grads,
            grads,
            column,
            column,
            jax.ShapeDtypeStruct((1, ff), f32),
            jax.ShapeDtypeStruct((1, 256), f32),
        ),
        in_specs=[pl.BlockSpec(memory_space=pltpu.SMEM)] * 2
        + [vmem, vmem]
        + anywhere(parts + 2 * count + 1 + len(after)),
        out_specs=tuple(anywhere(5)) + (vmem,) * 4,
        scratch_shapes=[
            pltpu.VMEM((total, width), bf16),
            pltpu.VMEM((total, width), bf16),
            pltpu.VMEM((total, width), bf16),
            pltpu.VMEM((total, width), bf16),
            pltpu.VMEM((8, 8, width // 64, ff), bf16),
            pltpu.VMEM((ff, width), bf16),
            pltpu.VMEM((total, ff), bf16),
            pltpu.VMEM((total, ff), bf16),
            pltpu.VMEM((8, 128, width), bf16),
            pltpu.VMEM((8, 128, width), bf16),
            pltpu.SemaphoreType.DMA((count,)),
            pltpu.SemaphoreType.DMA((count,)),
            pltpu.SemaphoreType.DMA((parts,)),
            pltpu.SemaphoreType.DMA((5,)),
        ],
        compiler_params=kernel_params(),
        cost_estimate=cost(32),
        name="feed_forward",
    )(numbers, spots, gains, bias, *[p[0] for p in weight], *x, *dy, down, *after)


def packed(qkv_weight, up_weight, vectors, lengths, place, head, tokens, cotangent):
    wide, up_wide = qkv_weight.shape[1], up_weight.shape[1]
    part, up_part = 3 * head, up_wide // 8
    cols = part + up_part

    def body(place_ref, len_ref, q_ref, u_ref, x_ref, dy_ref, *refs):
        v_refs, out_ref, pair_ref = refs[: len(vectors)], refs[-2], refs[-1]
        pair_ref[0] = x_ref[...]
        pair_ref[1] = dy_ref[...]
        lane = lax.broadcasted_iota(jnp.int32, (8, cols), 1)
        row = lax.broadcasted_iota(jnp.int32, (8, cols), 0)
        sizes = jnp.zeros((8, cols), f32)
        for at in range(3):
            sizes = jnp.where(lane == at, len_ref[0, at].astype(f32), sizes)
        vector = jnp.concatenate([ref[...].astype(f32) for ref in v_refs])[None, :]
        vector = jnp.broadcast_to(vector, (8, cols))
        tail = jnp.where(row == 0, vector, jnp.where(row == 1, sizes, 0.0)).astype(bf16)
        for owner in range(8):
            pieces = [
                q_ref[:, (third * 8 + owner) * head : (third * 8 + owner + 1) * head]
                for third in range(3)
            ]
            pieces.append(u_ref[:, owner * up_part : (owner + 1) * up_part])
            out_ref[owner] = jnp.concatenate([jnp.concatenate(pieces, 1), tail], 0)

    return pl.pallas_call(
        body,
        out_shape=(
            jax.ShapeDtypeStruct((8, 40, cols), bf16),
            jax.ShapeDtypeStruct((2,) + tokens.shape, bf16),
        ),
        grid_spec=pltpu.PrefetchScalarGridSpec(
            num_scalar_prefetch=2,
            grid=(1,),
            in_specs=[
                pl.BlockSpec((32, wide), lambda i, place, lens: (place[0], 0)),
                pl.BlockSpec((32, up_wide), lambda i, place, lens: (place[0], 0)),
                pl.BlockSpec(tokens.shape, lambda i, place, lens: (0, 0)),
                pl.BlockSpec(tokens.shape, lambda i, place, lens: (0, 0)),
            ]
            + [pl.BlockSpec(v.shape, lambda i, place, lens: (0,)) for v in vectors],
            out_specs=(
                pl.BlockSpec((8, 40, cols), lambda i, place, lens: (0, 0, 0)),
                pl.BlockSpec((2,) + tokens.shape, lambda i, place, lens: (0, 0, 0)),
            ),
        ),
        compiler_params=kernel_params(),
        cost_estimate=cost(3),
        name="packed",
    )(place, lengths, qkv_weight, up_weight, tokens, cotangent, *vectors)


def attend(h1, dy, weight, spots, out, bias, cosine, sine, lengths, after, rows=128):
    total, width = h1.shape
    count = len(dy)
    head = out.shape[0]
    scale = head ** (-0.5)

    parts = len(weight)

    def body(len_ref, spot_ref, b_ref, *refs):
        w_refs, refs = refs[:parts], refs[parts:]
        dy_refs = refs[:count]
        h1_hbm, out_hbm, cos_hbm, sin_hbm = refs[count : count + 4]
        ol_hbm, dq_hbm, sum_ref = refs[count + 4 : count + 7]
        (dy_v, h1_v, w_v, wo_v, cos_v, sin_v, qkv_v, do_v, ol_v, dq_v, dy_sem, w_sem, sems) = (
            refs[count + 7 :]
        )
        pairs = (
            (h1_hbm, h1_v),
            (out_hbm, wo_v),
            (cos_hbm, cos_v),
            (sin_hbm, sin_v),
        )
        copies = loads(
            [pltpu.make_async_copy(*pair, sems.at[n]) for n, pair in enumerate(pairs)]
        )
        w_copies = loads(
            weight_copies(weight, w_refs, spot_ref, w_v, pl.ds(0, 3 * head), w_sem)
        )
        dy_copies = loads(piece_copies(dy_refs, 1, dy_v, dy_sem, rows))
        for copy in copies[:1] + w_copies:
            copy.wait()

        @pl.loop(0, 3)
        def _(n):
            at = pl.ds(pl.multiple_of(n * head, head), head)
            qkv_v[:, at] = dot(h1_v[...], w_v[:, :, :, at].reshape(width, head)) + b_ref[n]

        for copy in copies[1:] + dy_copies:
            copy.wait()
        do_v[...] = dot(dy_v[...], wo_v[...], 1, 1).astype(bf16)
        sum_ref[...] = jnp.zeros_like(sum_ref)

        @pl.loop(0, total // rows, unroll=2)
        def _(block):
            at = pl.ds(pl.multiple_of(block * rows, rows), rows)
            cos, sin = cos_v[at, :], sin_v[at, :]

            def turned(value, sign):
                left = value[:, :128]
                left = left * cos + swap_halves(left) * (sin * sign)
                return jnp.concatenate([left, value[:, 128:]], 1).astype(bf16)

            q, k = turned(qkv_v[at, 0:head], 1.0), turned(qkv_v[at, head : 2 * head], 1.0)
            v = qkv_v[at, 2 * head :].astype(bf16)
            scores = dot(q, k, 1, 1) * scale
            masked = jnp.where(allowed_mask(len_ref, block, rows), scores, -1e30)
            shifted = jnp.exp(masked - jnp.max(masked, 1, keepdims=True))
            probs = shifted / jnp.sum(shifted, 1, keepdims=True)
            low = probs.astype(bf16)
            ol_v[at, :] = dot(low, v).astype(bf16)
            d_out = do_v[at, :]
            d_value = dot(low, d_out, 0, 0)
            d_probs = dot(d_out, v, 1, 1)
            centred = d_probs - jnp.sum(d_probs * probs, 1, keepdims=True)
            d_scores = (probs * centred).astype(bf16)
            d_query = turned(dot(d_scores, k) * scale, -1.0)
            d_key = turned(dot(d_scores, q, 0, 0) * scale, -1.0)
            for n, grad in enumerate((d_query, d_key, d_value.astype(bf16))):
                lanes = slice(n * head, (n + 1) * head)
                dq_v[at, lanes] = grad
                sum_ref[:, lanes] += jnp.sum(grad.astype(f32), 0, keepdims=True)

        ol_copy = pltpu.make_async_copy(ol_v, ol_hbm, sems.at[0])
        ol_copy.start()
        dq_copy = pltpu.make_async_copy(dq_v, dq_hbm, sems.at[1])
        dq_copy.start()

        for copy in (ol_copy, dq_copy):
            copy.wait()

    vmem = pl.BlockSpec(memory_space=pltpu.VMEM)
    smem = pl.BlockSpec(memory_space=pltpu.SMEM)
    return pl.pallas_call(
        after_inputs(body, 7 + parts + count, len(after)),
        out_shape=(
            jax.ShapeDtypeStruct((total, head), bf16),
            jax.ShapeDtypeStruct((total, 3 * head), bf16),
            jax.ShapeDtypeStruct((1, 3 * head), f32),
        ),
        in_specs=[smem, smem, vmem] + anywhere(parts + count + 4 + len(after)),
        out_specs=tuple(anywhere(2)) + (vmem,),
        scratch_shapes=[
            pltpu.VMEM((total, width), bf16),
            pltpu.VMEM((total, width), bf16),
            pltpu.VMEM((8, 8, width // 64, 3 * head), bf16),
            pltpu.VMEM((head, width), bf16),
            pltpu.VMEM((total, 128), f32),
            pltpu.VMEM((total, 128), f32),
            pltpu.VMEM((total, 3 * head), f32),
            pltpu.VMEM((total, head), bf16),
            pltpu.VMEM((total, head), bf16),
            pltpu.VMEM((total, 3 * head), bf16),
            pltpu.SemaphoreType.DMA((count,)),
            pltpu.SemaphoreType.DMA((parts,)),
            pltpu.SemaphoreType.DMA((4,)),
        ],
        compiler_params=kernel_params(),
        cost_estimate=cost(17),
        name="attend",
    )(
        lengths,
        spots,
        bias,
        *[p[0] for p in weight],
        *dy,
        h1,
        out,
        cosine,
        sine,
        *after,
    )


def attention_grads(h1, dy, d_qkv, attended, numbers, after):
    total, width = h1.shape
    count = len(dy)
    rows = total // count
    head = attended.shape[1]

    def body(number_ref, *refs):
        dy_refs = refs[:count]
        h1_hbm, dq_hbm, ol_hbm, keep_hbm, send_hbm = refs[count : count + 5]
        dy_v, h1_v, dq_v, ol_v, keep_v, send_v, dy_sem, sems = refs[count + 5 :]
        own = number_ref[0] == 0
        pairs = ((h1_hbm, h1_v), (dq_hbm, dq_v), (ol_hbm, ol_v))
        copies = loads(
            [pltpu.make_async_copy(*pair, sems.at[n]) for n, pair in enumerate(pairs)]
        )
        dy_copies = loads(piece_copies(dy_refs, 1, dy_v, dy_sem, rows))
        for copy in copies:
            copy.wait()

        def split(part, high, lanes):
            for z_hi in range(2):
                at = (pl.ds(4 * z_hi, 4), high, lanes)

                @pl.when(own)
                def _(z_hi=z_hi, at=at):
                    keep_v[at] = part[:, z_hi, 0]
                    send_v[at] = part[:, z_hi, 1]

                @pl.when(jnp.logical_not(own))
                def _(z_hi=z_hi, at=at):
                    keep_v[at] = part[:, z_hi, 1]
                    send_v[at] = part[:, z_hi, 0]

        @pl.loop(0, 8)
        def _(n):
            lanes = pl.ds(pl.multiple_of(n * 256, 256), 256)
            part = dot_rows(h1_v[:, lanes], dq_v[...]).astype(bf16).reshape(4, 2, 2, 16, 3 * head)
            for third in range(3):
                split(
                    part[..., third * head : (third + 1) * head],
                    pl.ds(16 * third, 16),
                    pl.ds(pl.multiple_of(n * head, head), head),
                )

        for copy in dy_copies:
            copy.wait()
        part = dot_rows(ol_v[...], dy_v[...]).astype(bf16).reshape(4, 2, 2, 16, width)
        split(part, pl.ds(48, 16), slice(None))
        keep_copy = pltpu.make_async_copy(keep_v, keep_hbm, sems.at[0])
        keep_copy.start()
        send_copy = pltpu.make_async_copy(send_v, send_hbm, sems.at[1])
        send_copy.start()
        keep_copy.wait()
        send_copy.wait()

    grads = jax.ShapeDtypeStruct((8, 64, width), bf16)
    return pl.pallas_call(
        after_inputs(body, 4 + count, len(after)),
        out_shape=(grads, grads),
        in_specs=[pl.BlockSpec(memory_space=pltpu.SMEM)] + anywhere(count + 3 + len(after)),
        out_specs=tuple(anywhere(2)),
        scratch_shapes=[
            pltpu.VMEM((total, width), bf16),
            pltpu.VMEM((total, width), bf16),
            pltpu.VMEM((total, 3 * head), bf16),
            pltpu.VMEM((total, head), bf16),
            pltpu.VMEM((8, 64, width), bf16),
            pltpu.VMEM((8, 64, width), bf16),
            pltpu.SemaphoreType.DMA((count,)),
            pltpu.SemaphoreType.DMA((3,)),
        ],
        compiler_params=kernel_params(),
        cost_estimate=cost(12),
        name="attention_grads",
    )(numbers, *dy, h1, d_qkv, attended, *after)


def outer(d_qkv, d_hidden, weight, spots, x, mean, inverse, gains, active, attended, down, out, bias, after):
    total, n1 = d_qkv.shape
    n2 = d_hidden.shape[1]
    count = len(x)
    parts = len(weight)
    head, width = out.shape
    step = 512

    def body(spot_ref, m_ref, i_ref, g_ref, b_ref, *refs):
        w_refs, refs = refs[:parts], refs[parts:]
        x_refs, refs = refs[:count], refs[count:]
        plain, sums_ref, outs = refs[:6], refs[6], refs[7 : 7 + count]
        dq_v, du_v, act_v, ol_v, wd_v, wo_v, w_v, x_v, pair_v, w_sem, x_sem, sems, out_sem = refs[
            7 + count :
        ]
        plain_v = (dq_v, du_v, act_v, ol_v, wd_v, wo_v)
        first = loads(
            [
                pltpu.make_async_copy(plain[n], plain_v[n], sems.at[n]) for n in range(2, 6)
            ]
        )
        copies = loads(
            [
                pltpu.make_async_copy(plain[n], plain_v[n], sems.at[n]) for n in range(2)
            ]
            + weight_copies(weight, w_refs, spot_ref, w_v, slice(None), w_sem)
            + piece_copies(x_refs, 0, x_v, x_sem, 128)
        )
        for copy in first:
            copy.wait()

        def leaving(n, half):
            lanes = pl.ds(pl.multiple_of(n * step, step), step)
            return [
                pltpu.make_async_copy(
                    pair_v.at[half, pl.ds(at * 128, 128), lanes],
                    outs[at].at[half, :, lanes],
                    out_sem.at[half, at],
                )
                for at in range(count)
            ]

        @pl.loop(0, width // step)
        def _(n):
            lanes = pl.ds(pl.multiple_of(n * step, step), step)
            mix = dot(act_v[...], wd_v[:, lanes]) + dot(ol_v[...], wo_v[:, lanes])
            pair_v[0, :, lanes] = (mix + b_ref[:, lanes]).astype(bf16)
            for copy in leaving(n, 0):
                copy.start()

        for copy in copies:
            copy.wait()

        @pl.loop(0, width // step)
        def _(n):
            lanes = pl.ds(pl.multiple_of(n * step, step), step)
            sources = pl.ds(n * (step // 256), step // 256)
            d1 = dot(dq_v[...], w_v[sources, :, :, 0:n1].reshape(step, n1), 1, 1)
            d2 = dot(du_v[...], w_v[sources, :, :, n1:].reshape(step, n2), 1, 1)
            pair_v[1, :, lanes] = (d1 * g_ref[0:1, lanes] + d2 * g_ref[1:2, lanes]).astype(bf16)
            for copy in leaving(n, 1):
                copy.start()
            normed = (x_v[:, lanes].astype(f32) - m_ref[...]) * i_ref[...]
            sums_ref[0:1, lanes] = jnp.sum(d1 * normed, 0, keepdims=True)
            sums_ref[1:2, lanes] = jnp.sum(d1, 0, keepdims=True)
            sums_ref[2:3, lanes] = jnp.sum(d2 * normed, 0, keepdims=True)
            sums_ref[3:4, lanes] = jnp.sum(d2, 0, keepdims=True)

        for n in range(width // step):
            for half in range(2):
                for copy in leaving(n, half):
                    copy.wait()

    vmem = pl.BlockSpec(memory_space=pltpu.VMEM)
    return pl.pallas_call(
        after_inputs(body, 11 + parts + count, len(after)),
        out_shape=(jax.ShapeDtypeStruct((4, width), f32),)
        + (jax.ShapeDtypeStruct((2, 128, width), bf16),) * count,
        in_specs=[pl.BlockSpec(memory_space=pltpu.SMEM)]
        + [vmem] * 4
        + anywhere(parts + count + 6 + len(after)),
        out_specs=(vmem,) + tuple(anywhere(count)),
        scratch_shapes=[
            pltpu.VMEM((total, n1), bf16),
            pltpu.VMEM((total, n2), bf16),
            pltpu.VMEM((total, n2), bf16),
            pltpu.VMEM((total, head), bf16),
            pltpu.VMEM((n2, width), bf16),
            pltpu.VMEM((head, width), bf16),
            pltpu.VMEM((8, 8, width // 64, n1 + n2), bf16),
            pltpu.VMEM((total, width), bf16),
            pltpu.VMEM((2, total, width), bf16),
            pltpu.SemaphoreType.DMA((parts,)),
            pltpu.SemaphoreType.DMA((count,)),
            pltpu.SemaphoreType.DMA((6,)),
            pltpu.SemaphoreType.DMA((2, count)),
        ],
        compiler_params=kernel_params(),
        cost_estimate=cost(20),
        name="outer",
    )(
        spots,
        mean,
        inverse,
        gains,
        bias,
        *[p[0] for p in weight],
        *x,
        d_qkv,
        d_hidden,
        active,
        attended,
        down,
        out,
        *after,
    )


def unpacked(part, after):
    owners, _, cols = part.shape

    def body(part_ref, rows_ref, info_ref):
        for owner in range(owners):
            rows_ref[owner] = part_ref[owner, 0:32]
            info_ref[owner] = part_ref[owner, 32:40].astype(f32)

    return pl.pallas_call(
        after_inputs(body, 1, len(after)),
        out_shape=(
            jax.ShapeDtypeStruct((owners, 32, cols), bf16),
            jax.ShapeDtypeStruct((owners, 8, cols), f32),
        ),
        in_specs=[pl.BlockSpec(memory_space=pltpu.VMEM)] + anywhere(len(after)),
        out_specs=(pl.BlockSpec(memory_space=pltpu.VMEM),) * 2,
        compiler_params=kernel_params(),
        cost_estimate=cost(3),
        name="unpacked",
    )(part, *after)


def packed_sums(stays, crossed, own, below, above, ff, head, after):
    width = own.shape[1]

    def body(stay_ref, cross_ref, own_ref, below_ref, above_ref, out_ref, lanes_ref, keep_ref):
        inner = (stay_ref[0].astype(f32) + cross_ref[0].astype(f32)).astype(bf16)
        total = wide(own_ref, below_ref, above_ref).astype(bf16)
        for owner in range(8):
            pieces = [
                total[16 * third : 16 * third + 16, owner * head : (owner + 1) * head]
                for third in range(3)
            ]
            row, col = 64 + 16 * (owner % 4), owner // 4 * ff
            pieces.append(inner[row : row + 16, col : col + ff])
            out_ref[owner] = jnp.concatenate(pieces, 1)
            lanes_ref[owner] = total[48:64, owner * head : (owner + 1) * head]
        keep_ref[...] = inner[0:64]

    vmem = pl.BlockSpec(memory_space=pltpu.VMEM)
    return pl.pallas_call(
        after_inputs(body, 5, len(after)),
        out_shape=(
            jax.ShapeDtypeStruct((8, 16, 3 * head + ff), bf16),
            jax.ShapeDtypeStruct((8, 16, width // 8), bf16),
            jax.ShapeDtypeStruct((64, width), bf16),
        ),
        in_specs=[vmem] * 5 + anywhere(len(after)),
        out_specs=(vmem,) * 3,
        compiler_params=kernel_params(),
        cost_estimate=cost(3),
        name="packed_sums",
    )(stays, crossed, own, below, above, *after)


def joined(arrays, after):
    sizes = [array.shape[0] for array in arrays]
    unit = math.gcd(*sizes)
    block = (unit,) + arrays[0].shape[1:]
    count = len(arrays)
    firsts = [sum(sizes[:n]) // unit for n in range(count)]

    def body(*refs):
        step = pl.program_id(0)
        for ref, first, size in zip(refs, firsts, sizes):

            @pl.when((step >= first) & (step < first + size // unit))
            def _(ref=ref):
                refs[count][...] = ref[...]

    def came(first, size):
        return pl.BlockSpec(block, lambda i: (jnp.clip(i - first, 0, size // unit - 1), 0, 0))

    return pl.pallas_call(
        after_inputs(body, count, len(after)),
        out_shape=jax.ShapeDtypeStruct((sum(sizes),) + block[1:], bf16),
        grid=(sum(sizes) // unit,),
        in_specs=[came(first, size) for first, size in zip(firsts, sizes)] + anywhere(len(after)),
        out_specs=pl.BlockSpec(block, lambda i: (i, 0, 0)),
        compiler_params=kernel_params(),
        cost_estimate=cost(3),
        name="joined",
    )(*arrays, *after)


def halves(own, below, above, after):
    count, rows, cols = own.shape
    half = count // 2

    def body(own_ref, below_ref, above_ref, low_ref, high_ref, all_ref):
        step = pl.program_id(0)
        all_ref[0] = own_ref[...]
        all_ref[1] = above_ref[...]
        all_ref[2] = below_ref[...]

        @pl.when(step == 0)
        def _():
            low_ref[...] = below_ref[...]

        @pl.when(step == 1)
        def _():
            high_ref[...] = above_ref[...]

    block = pl.BlockSpec((half, rows, cols), lambda i: (i, 0, 0))
    whole = pl.BlockSpec((half, rows, cols), lambda i: (0, 0, 0))
    low, high, together = pl.pallas_call(
        after_inputs(body, 3, len(after)),
        out_shape=(jax.ShapeDtypeStruct((half, rows, cols), bf16),) * 2
        + (jax.ShapeDtypeStruct((3, count, rows, cols), bf16),),
        grid=(2,),
        in_specs=[block] * 3 + anywhere(len(after)),
        out_specs=(
            whole,
            whole,
            pl.BlockSpec((3, half, rows, cols), lambda i: (0, i, 0, 0)),
        ),
        compiler_params=kernel_params(),
        cost_estimate=cost(4),
        name="halves",
    )(own, below, above, *after)
    return low, high, together.reshape(3 * count, rows, cols)


def small_sums(norm_sums, qkv_sums, up_sums, dy_sums, numbers, after):
    def body(number_ref, norm_ref, q_ref, u_ref, y_ref, out_ref, work):
        shard = number_ref[1]
        for owner in range(8):
            mine = shard == owner
            for n in range(4):
                for half in range(2):
                    at = owner * 256 + half * 128
                    work[owner, n * 2 + half : n * 2 + half + 1] = norm_ref[n : n + 1, at : at + 128]
            for n in range(3):
                third, source = divmod(owner * 3 + n, 8)
                for half in range(2):
                    at = third * 256 + half * 128
                    work[owner, 8 + n * 2 + half : 9 + n * 2 + half] = jnp.where(
                        shard == source, q_ref[:, at : at + 128], 0.0
                    )
            for n in range(8):
                work[owner, 14 + n : 15 + n] = jnp.where(
                    mine, u_ref[:, n * 128 : (n + 1) * 128], 0.0
                )
            for n in range(2):
                work[owner, 22 + n : 23 + n] = jnp.where(
                    mine, y_ref[:, n * 128 : (n + 1) * 128], 0.0
                )
        out_ref[...] = work[...].astype(bf16)

    vmem = pl.BlockSpec(memory_space=pltpu.VMEM)
    return pl.pallas_call(
        after_inputs(body, 5, len(after)),
        out_shape=jax.ShapeDtypeStruct((8, 24, 128), bf16),
        in_specs=[pl.BlockSpec(memory_space=pltpu.SMEM)] + [vmem] * 4 + anywhere(len(after)),
        out_specs=vmem,
        scratch_shapes=[pltpu.VMEM((8, 24, 128), f32)],
        compiler_params=kernel_params(),
        cost_estimate=cost(3),
        name="small_sums",
    )(numbers, norm_sums, qkv_sums, up_sums, dy_sums, *after)


def finished(own, below, above, other, tokens, cotangent, after):
    rows, width = tokens.shape
    step = rows // 2

    def body(own_ref, below_ref, above_ref, other_ref, x_ref, dy_ref, mixed_ref, grad_ref):
        total = wide(own_ref, below_ref, above_ref, other_ref)
        x = x_ref[...].astype(f32)
        mixed_ref[...] = (x + total[0]).astype(bf16)
        centre = x - jnp.mean(x, 1, keepdims=True)
        inverse = lax.rsqrt(jnp.mean(centre * centre, 1, keepdims=True) + EPS)
        normed = centre * inverse
        gain = total[1]
        grad_ref[...] = dy_ref[...].astype(f32) + inverse * (
            gain
            - jnp.mean(gain, 1, keepdims=True)
            - normed * jnp.mean(gain * normed, 1, keepdims=True)
        )

    def pair(first):
        return pl.BlockSpec((2, step, width), lambda i: (first, i, 0))

    block = pl.BlockSpec((step, width), lambda i: (i, 0))
    return pl.pallas_call(
        after_inputs(body, 6, len(after)),
        out_shape=(
            jax.ShapeDtypeStruct((rows, width), bf16),
            jax.ShapeDtypeStruct((rows, width), f32),
        ),
        grid=(2,),
        in_specs=[pair(0), pair(1), pair(0), pair(0), block, block] + anywhere(len(after)),
        out_specs=(block, block),
        compiler_params=kernel_params(),
        cost_estimate=cost(3),
        name="finished",
    )(own, below, above, other, tokens, cotangent, *after)


def blocks_call(name, body, numbers, terms, outs, after, time=3):
    def came(block, index):
        rest = (0,) * (len(block) - 1)
        return pl.BlockSpec(block, lambda i, n: (index(n),) + rest)

    return pl.pallas_call(
        after_inputs(body, 1 + len(terms), len(after)),
        out_shape=tuple(jax.ShapeDtypeStruct(out, bf16) for out in outs),
        grid_spec=pltpu.PrefetchScalarGridSpec(
            num_scalar_prefetch=1,
            grid=(1,),
            in_specs=[came(block, index) for _, block, index in terms] + anywhere(len(after)),
            out_specs=tuple(
                pl.BlockSpec(out, lambda i, n, size=len(out): (0,) * size) for out in outs
            ),
        ),
        compiler_params=kernel_params(),
        cost_estimate=cost(time),
        name=name,
    )(numbers, *[array for array, _, _ in terms], *after)


def wide(*refs):
    return functools.reduce(jnp.add, [ref[...].astype(f32) for ref in refs])


def spread(pieces, places, core, targets, count, before, after):
    rows, cols = pieces[0][0].shape[1:]
    firsts, total = [], 0
    for mine, _ in pieces:
        firsts.append(total)
        total += mine.shape[0]

    def body(place_ref, core_ref, *refs):
        step = pl.program_id(0)
        outs = refs[2 * len(pieces) + len(before) :]
        first_core = core_ref[0] == 0

        def fill(ref, low):
            for out_ref, (_, high, parts) in zip(outs, targets):
                for to, row, col, size in parts:
                    out_ref[low * high : (low + 1) * high, to : to + size] = ref[
                        0, row : row + high, col : col + size
                    ].astype(f32)

        for n, (first, (mine, _)) in enumerate(zip(firsts, pieces)):
            here = (step >= first) & (step < first + mine.shape[0])

            @pl.when(here & first_core)
            def _(n=n):
                fill(refs[2 * n], 0)
                fill(refs[2 * n + 1], 1)

            @pl.when(here & jnp.logical_not(first_core))
            def _(n=n):
                fill(refs[2 * n], 1)
                fill(refs[2 * n + 1], 0)

    def chosen(first, size):
        return pl.BlockSpec(
            (1, rows, cols), lambda i, place, core: (jnp.clip(i - first, 0, size - 1), 0, 0)
        )

    specs, arrays = [], []
    for first, (mine, yours) in zip(firsts, pieces):
        specs += [chosen(first, mine.shape[0])] * 2
        arrays += [mine, yours]
    return pl.pallas_call(
        after_inputs(body, 2 + 2 * len(pieces) + len(before), len(after)),
        out_shape=tuple(
            jax.ShapeDtypeStruct((2 * count * high, wide), f32) for wide, high, _ in targets
        ),
        grid_spec=pltpu.PrefetchScalarGridSpec(
            num_scalar_prefetch=2,
            grid=(total,),
            in_specs=specs + anywhere(len(before) + len(after)),
            out_specs=tuple(
                pl.BlockSpec((2 * high, wide), lambda i, place, core: (place[i], 0))
                for wide, high, _ in targets
            ),
        ),
        input_output_aliases={2 + len(arrays) + n: n for n in range(len(before))},
        compiler_params=kernel_params(),
        cost_estimate=cost(0.3 * total),
        name="spread",
    )(places, core, *arrays, *before, *after)


def local(
    tokens,
    doc_lengths,
    cotangent,
    ln1_gain,
    ln1_bias,
    ln2_gain,
    ln2_bias,
    qkv_weight,
    qkv_bias,
    out_weight,
    out_bias,
    up_weight,
    up_bias,
    down_weight,
    down_bias,
):
    rows, width = tokens.shape
    head = width // HEADS
    group = 8
    rep = lax.axis_index("rep")
    shard = lax.axis_index("shard")
    y, h, c = rep // 4, (rep // 2) % 2, rep % 2
    l, x = shard // 4, shard % 4
    ff = up_bias.shape[0]

    cols = 3 * head + ff
    vectors = [ln1_gain, ln1_bias, ln2_gain, ln2_bias, qkv_bias]
    place = (y * 2 + c).astype(jnp.int32).reshape(1)
    part, pair = packed(
        qkv_weight, up_weight, vectors, doc_lengths, place, head, tokens, cotangent
    )
    below, above, other = move(pair, x=1), move(pair, x=-1), move(pair, l=1)
    far, other_above, other_below = move(below, x=1), move(other, x=-1), move(below, l=1)
    pairs = (pair, above, far, below, other, other_above, None, other_below)

    part = lax.all_to_all(part, "shard", 0, 0)
    own, infos = unpacked(part, (pairs[1], pairs[3], pairs[4]))
    below, above = move(own, y=1), move(own, y=-1)
    x_other_far, dy_other_far = move(other_below[0], x=1), move(other_above[1], x=-1)
    low, high, yours = halves(own, below, above, (far, other_above, other_below))
    far_low, far_high = move(low, y=1), move(high, y=-1)
    x_all = tuple(x_other_far if p is None else p for p in pairs)
    dy_all = tuple(dy_other_far if p is None else p for p in pairs)
    yours = move(yours, c=1)
    far_low_c, far_high_c = move(far_low, c=1), move(far_high, c=1)
    weight = (
        (own, 0, 8, 0, 0),
        (above, 0, 8, 0, 1),
        (far_low, 0, 4, 0, 2),
        (far_high, 0, 4, 4, 2),
        (below, 0, 8, 0, 3),
        (yours, 0, 8, 0, 4),
        (yours, 8, 8, 0, 5),
        (far_low_c, 0, 4, 0, 6),
        (far_high_c, 0, 4, 4, 6),
        (yours, 16, 8, 0, 7),
    )
    steps4 = (y + jnp.arange(4)) % 4
    spots = jnp.concatenate([steps4 * 2 + c, steps4 * 2 + 1 - c]).astype(jnp.int32)

    gains = infos[:, 0, :1024].reshape(8, 4, 256).transpose(1, 0, 2).reshape(4, width)
    qkv_b = infos[:, 0, 1024:].reshape(8 * 3, 1, head)
    qkv_b = jnp.stack(
        [lax.dynamic_index_in_dim(qkv_b, third * 8 + shard, 0, False) for third in range(3)]
    )
    steps8 = jnp.arange(8)
    sources = ((steps8 // 4) ^ l) * 4 + (x + steps8 % 4) % 4
    sources = sources.astype(jnp.int32)
    lengths = infos[:, 1, :3]
    lengths = jnp.sum(
        jnp.where(sources[:, None, None] == steps8[None, :, None], lengths[None], 0.0), 1
    ).astype(jnp.int32)
    ends = jnp.cumsum(lengths, 1)
    starts = ends - lengths
    steps_t = jnp.arange(rows, dtype=jnp.int32)
    segment = jnp.sum((steps_t[None, :, None] >= ends[:, None, :]).astype(jnp.int32), -1)
    slots = jnp.arange(lengths.shape[1], dtype=jnp.int32)
    begin = jnp.sum(
        jnp.where(segment[:, :, None] == slots[None, None, :], starts[:, None, :], 0), -1
    )
    position = (steps_t[None, :] - begin).astype(f32).reshape(group * rows, 1)
    lane = jnp.arange(128)
    freq = 10000.0 ** (-2.0 * (lane % (ROT // 2)).astype(f32) / ROT)
    angle = position * freq[None, :]
    cosine = jnp.where(lane < ROT, jnp.cos(angle), 1.0)
    sine = jnp.sin(angle)
    sine = jnp.where(lane < ROT // 2, -sine, jnp.where(lane < ROT, sine, 0.0))

    both_bias = (out_bias.astype(f32) + down_bias.astype(f32))[None, :]
    wide_bias = lax.dynamic_update_slice(jnp.zeros((1, width), f32), both_bias, (0, shard * 256))
    numbers = jnp.stack([c, shard, y, h]).astype(jnp.int32)

    h1, active, d_hidden, keep, send, mean, inverse, up_sums, dy_sums = feed_forward(
        x_all,
        dy_all,
        gains,
        weight,
        spots,
        down_weight,
        up_bias.astype(f32)[None],
        numbers,
        3 * head,
        (cosine, sine),
    )
    got = move(send, c=1)
    attended, d_qkv, qkv_sums = attend(
        h1, dy_all, weight, spots, out_weight, qkv_b, cosine, sine, lengths, (send,)
    )

    pair_shape, one = (2, 128, width), (1, 128, width)

    def turn(k):
        return lambda n: (n[2] + k) % 4

    def far_body(n_ref, keep_ref, got_ref, low_ref, high_ref):
        total = wide(keep_ref, got_ref).astype(bf16)
        low_ref[0] = total[0]
        high_ref[0] = total[1]

    low, high = blocks_call(
        "far_sums",
        far_body,
        numbers,
        [(keep, pair_shape, turn(2)), (got, pair_shape, turn(2))],
        (one, one),
        (attended,),
    )
    from_low, from_high = move(low, y=1), move(high, y=-1)
    a_keep, a_send = attention_grads(h1, dy_all, d_qkv, attended, numbers, (low, high))
    a_got = move(a_send, c=1)
    def near_body(n_ref, k1_ref, g1_ref, k3_ref, g3_ref, low_ref, high_ref, above_ref, below_ref):
        above, below = wide(k1_ref, g1_ref), wide(k3_ref, g3_ref)
        above_ref[0] = (above[0] + low_ref[0].astype(f32)).astype(bf16)
        above_ref[1] = above[1].astype(bf16)
        below_ref[0] = below[0].astype(bf16)
        below_ref[1] = (below[1] + high_ref[0].astype(f32)).astype(bf16)

    above, below = blocks_call(
        "near_sums",
        near_body,
        numbers,
        [(v, pair_shape, turn(k)) for k in (1, 3) for v in (keep, got)]
        + [(v, one, lambda n: 0) for v in (from_low, from_high)],
        (pair_shape, pair_shape),
        (a_send,),
        20,
    )
    from_below, from_above = move(above, y=1), move(below, y=-1)

    four, part_shape = (4, 64, width), (1, 64, width)

    def away_body(n_ref, keep_ref, got_ref, out_ref):
        out_ref[...] = wide(keep_ref, got_ref).astype(bf16)

    (a_away,) = blocks_call(
        "away_sums",
        away_body,
        numbers,
        [(v, four, lambda n: 1 - n[3]) for v in (a_keep, a_got)],
        (four,),
        (above,),
    )
    a_crossed = move(a_away, h=1)
    norm_sums, *pairs_out = outer(
        d_qkv,
        d_hidden,
        weight,
        spots,
        x_all,
        mean,
        inverse,
        jnp.stack([gains[0], gains[2]]),
        active,
        attended,
        down_weight,
        out_weight,
        wide_bias,
        (a_away, above, below),
    )

    smalls = small_sums(norm_sums, qkv_sums, up_sums, dy_sums, numbers, ())
    smalls = jnp.sum(lax.all_to_all(smalls, "shard", 0, 0).astype(f32), 0)
    smalls = jnp.pad(smalls.astype(bf16).reshape(-1), (0, 16 * width - 3072)).reshape(16, width)

    def ends_body(n_ref, keep_ref, got_ref, below_ref, above_ref, leave_ref, stay_ref):
        total = wide(keep_ref, got_ref, below_ref, above_ref).astype(bf16)
        first = n_ref[3] == 0
        leave_ref[0] = jnp.where(first, total[1], total[0])
        stay_ref[0] = jnp.where(first, total[0], total[1])

    leaves, stays = blocks_call(
        "end_sums",
        ends_body,
        numbers,
        [(v, pair_shape, turn(0)) for v in (keep, got)]
        + [(v, pair_shape, lambda n: 0) for v in (from_below, from_above)],
        (one, one),
        (norm_sums,),
    )
    crossed = move(leaves, h=1)

    passed_below, passed_above = move(pairs_out[6], x=1), move(pairs_out[2], x=-1)

    def around_body(n_ref, keep_ref, got_ref, crossed_ref, low_ref, high_ref, above_ref, own_ref, below_ref):
        def part(k):
            at = (n_ref[2] + k) % 4
            return wide(keep_ref.at[at], got_ref.at[at], crossed_ref.at[at]).astype(bf16)

        far = part(2)
        low_ref[...] = far[:32]
        high_ref[...] = far[32:]
        above_ref[...] = part(1)
        own_ref[...] = part(0)
        below_ref[...] = part(3)

    a_low, a_high, a_above, a_own, a_below = blocks_call(
        "around_sums",
        around_body,
        numbers,
        [(v, four, lambda n: n[3]) for v in (a_keep, a_got)] + [(a_crossed, four, lambda n: 0)],
        ((32, width), (32, width), (64, width), (64, width), (64, width)),
        (leaves,),
    )
    a_low, a_high = move(a_low, y=1), move(a_high, y=-1)

    def beside_body(n_ref, above_ref, below_ref, low_ref, high_ref, up_ref, down_ref):
        up_ref[0:32] = (above_ref[0:32].astype(f32) + low_ref[...].astype(f32)).astype(bf16)
        up_ref[32:64] = above_ref[32:64]
        down_ref[0:32] = below_ref[0:32]
        down_ref[32:64] = (below_ref[32:64].astype(f32) + high_ref[...].astype(f32)).astype(bf16)

    a_above, a_below = blocks_call(
        "beside_sums",
        beside_body,
        numbers,
        [(v, v.shape, lambda n: 0) for v in (a_above, a_below, a_low, a_high)],
        ((64, width), (64, width)),
        (crossed, smalls),
    )
    a_from_below, a_from_above = move(a_above, y=1), move(a_below, y=-1)

    def passed_body(n_ref, up_ref, from_below, here_ref, down_ref, from_above, there_ref, up_out, down_out):
        up_out[0:2] = wide(up_ref, from_below).astype(bf16)
        up_out[2:4] = here_ref[...]
        down_out[0:2] = wide(down_ref, from_above).astype(bf16)
        down_out[2:4] = there_ref[...]

    ups, downs = blocks_call(
        "passed_sums",
        passed_body,
        numbers,
        [
            (v, pair_shape, lambda n: 0)
            for v in (
                pairs_out[5],
                passed_below,
                pairs_out[1],
                pairs_out[3],
                passed_above,
                pairs_out[7],
            )
        ],
        ((4, 128, width),) * 2,
        (a_low,),
    )
    from_device_below, from_device_above = move(ups, x=1), move(downs, x=-1)

    part, outs, downs_sum = packed_sums(
        stays, crossed, a_own, a_from_below, a_from_above, ff, head, (ups,)
    )
    received = lax.all_to_all(part, "shard", 0, 0)
    part = jnp.concatenate([received, outs], 2).reshape(1, 128, width)
    def other_body(n_ref, own_ref, below_ref, above_ref, out_ref):
        out_ref[...] = wide(own_ref, below_ref, above_ref).astype(bf16)

    (total_other,) = blocks_call(
        "other_sums",
        other_body,
        numbers,
        [
            (pairs_out[4], pair_shape, lambda n: 0),
            (from_device_below, pair_shape, lambda n: 0),
            (from_device_above, pair_shape, lambda n: 1),
        ],
        (pair_shape,),
        (),
    )
    total_other, sent_other = move(total_other, l=1), total_other

    order = ((0, h), (0, 1 - h), (1, h), (1, 1 - h), (3, h), (3, 1 - h), (2, h), (2, 1 - h))
    places = jnp.stack([(y + k) % 4 * 2 + high for k, high in order]).astype(jnp.int32)

    def rep_gather(own, after):
        own = jnp.concatenate([own, move(own, h=1)])
        below, above = move(own, y=1), move(own, y=-1)
        low, high, near = halves(own, below, above, after)
        return near, (move(low, y=1), move(high, y=-1))

    near, far = rep_gather(jnp.concatenate([downs_sum, smalls])[None], ())
    downs_all = joined((near, *far), ())
    downs_yours = move(downs_all, c=1)
    (down_grad,) = spread(
        [(downs_all, downs_yours)],
        places,
        numbers[:1],
        [(width, 64, [(0, 0, 0, width)])],
        8,
        (),
        (),
    )
    near, far = rep_gather(part, (sent_other, downs_all))
    targets = [
        (
            3 * width,
            16,
            [
                ((third * 8 + source) * head, 16 * source, third * head, head)
                for source in range(8)
                for third in range(3)
            ],
        ),
        (8 * ff, 16, [(source * ff, 16 * source, 3 * head, ff) for source in range(8)]),
        (width, 16, [(source * head, 16 * source, cols, head) for source in range(8)]),
    ]
    grads = spread([(near, move(near, c=1))], places[:6], numbers[:1], targets, 8, (), (down_grad,))
    far = joined(far, (grads[0],))
    mixed, tokens_grad = finished(
        pairs_out[0], from_device_below, from_device_above, total_other, tokens, cotangent, (far,)
    )
    qkv_grad, up_grad, out_grad = spread(
        [(far, move(far, c=1))],
        places[6:],
        numbers[:1],
        targets,
        8,
        grads,
        (tokens_grad,),
    )
    smalls = jnp.concatenate([downs_all[:, 64:66], downs_yours[:, 64:66]]).astype(f32)
    smalls = jnp.sum(smalls, 0).reshape(-1)
    norm_grads = smalls[:1024].reshape(4, 256)
    dy_total = smalls[2816:3072]
    return (
        mixed,
        tokens_grad,
        norm_grads[0],
        norm_grads[1],
        norm_grads[2],
        norm_grads[3],
        qkv_grad,
        smalls[1024:1792],
        out_grad,
        dy_total,
        up_grad,
        smalls[1792:2816],
        down_grad,
        dy_total,
    )


def solution(mesh):
    rows = P(BOTH, None)
    vector, matrix = P("shard"), P("shard", None)
    return jax.shard_map(
        local,
        mesh=mesh,
        in_specs=(rows, rows, rows, vector, vector, vector, vector)
        + (matrix, vector, matrix, vector, matrix, vector, matrix, vector),
        out_specs=(rows, rows, vector, vector, vector, vector)
        + (matrix, vector, matrix, vector, matrix, vector, matrix, vector),
        check_vma=False,
    )
```

```python
import functools
import math

import jax
import jax.numpy as jnp
from jax import lax
from jax.experimental import pallas as pl
from jax.experimental.pallas import tpu as pltpu
from jax.sharding import PartitionSpec as P

HEADS = 8
ROT = 64
EPS = 1e-05
f32 = jnp.float32
bf16 = jnp.bfloat16


def cost(time):
    return pl.CostEstimate(flops=int(time * 1.15e9), bytes_accessed=1000, transcendentals=0)


BOTH = ("rep", "shard")
SIZES = (4, 2, 2, 2, 4)
SAME_CORE = [[2 * n + c for n in range(8)] for c in range(2)]
SAME_CORE_ALL = [[(2 * n + c) * 8 + s for n in range(8) for s in range(8)] for c in range(2)]


def coords():
    for y in range(4):
        for h in range(2):
            for c in range(2):
                for l in range(2):
                    for x in range(4):
                        yield (y, h, c, l, x)


def linear(t):
    y, h, c, l, x = (v % m for v, m in zip(t, SIZES))
    return ((y * 2 + h) * 2 + c) * 8 + l * 4 + x


def move(value, y=0, h=0, c=0, l=0, x=0):
    step = (y, h, c, l, x)
    pairs = [(linear(t), linear(tuple(a + b for a, b in zip(t, step)))) for t in coords()]
    return lax.ppermute(value, BOTH, pairs)


def pick(value, index, axis):
    return lax.dynamic_index_in_dim(value, index, axis, keepdims=False)


def kernel_params():
    return pltpu.CompilerParams(vmem_limit_bytes=56 * 1024 * 1024)


def after_inputs(body, count, extra):
    return lambda *refs: body(*refs[:count], *refs[count + extra :])


def anywhere(count):
    return [pl.BlockSpec(memory_space=pl.ANY)] * count


def dot(a, b, ca=1, cb=0):
    return lax.dot_general(a, b, (((ca,), (cb,)), ((), ())), preferred_element_type=f32)


def swap_halves(value):
    lane = lax.broadcasted_iota(jnp.int32, value.shape, 1)
    return jnp.where(lane < 32, pltpu.roll(value, 96, 1), pltpu.roll(value, 32, 1))


def allowed_mask(lengths_ref, block, rows):
    e0 = lengths_ref[block, 0]
    e1 = e0 + lengths_ref[block, 1]
    t = lax.broadcasted_iota(jnp.int32, (rows, rows), 0)
    s = lax.broadcasted_iota(jnp.int32, (rows, rows), 1)
    seg_t = (t >= e0).astype(jnp.int32) + (t >= e1).astype(jnp.int32)
    seg_s = (s >= e0).astype(jnp.int32) + (s >= e1).astype(jnp.int32)
    return (seg_t == seg_s) & (s <= t)


def dot_rows(a, b):
    return lax.dot_general(a, b, (((0,), (0,)), ((), ())), preferred_element_type=f32)


def loads(copies):
    for copy in copies:
        copy.start()
    return copies


def piece_copies(pieces, half, target, sems, rows):
    return [
        pltpu.make_async_copy(
            piece.at[half] if len(piece.shape) == 3 else piece,
            target.at[pl.ds(at * rows, rows)],
            sems.at[at],
        )
        for at, piece in enumerate(pieces)
    ]


def weight_copies(pieces, refs, spot_ref, target, lanes, sems):
    return [
        pltpu.make_async_copy(
            ref.at[pl.ds(begin, size), :, lanes],
            target.at[pl.ds(first, size), spot_ref[spot]],
            sems.at[at],
        )
        for at, (ref, (_, begin, size, first, spot)) in enumerate(zip(refs, pieces))
    ]


def feed_forward(x, dy, gains, weight, spots, down, bias, numbers, first, after):
    rows, width = x[0].shape[1:]
    count = len(x)
    total = rows * count
    ff = bias.shape[1]

    parts = len(weight)

    def body(number_ref, spot_ref, g_ref, b_ref, *refs):
        w_refs, refs = refs[:parts], refs[parts:]
        x_refs, dy_refs, d_hbm = refs[:count], refs[count : 2 * count], refs[2 * count]
        (h1_hbm, act_hbm, du_hbm, keep_hbm, send_hbm, m_ref, i_ref, db_ref, sum_ref) = refs[
            2 * count + 1 : 2 * count + 10
        ]
        (x_v, dy_v, h1_v, h2_v, w_v, d_v, act_v, du_v, keep_v, send_v, x_sem, dy_sem, w_sem, sems) = refs[
            2 * count + 10 :
        ]
        own = number_ref[0] == 0
        x_copies = loads(piece_copies(x_refs, 0, x_v, x_sem, rows))
        w_copies = loads(
            weight_copies(weight, w_refs, spot_ref, w_v, pl.ds(first, ff), w_sem)
        )
        dy_copies = loads(piece_copies(dy_refs, 1, dy_v, dy_sem, rows))
        d_copy = pltpu.make_async_copy(d_hbm, d_v, sems.at[1])
        d_copy.start()
        for copy in x_copies:
            copy.wait()

        @pl.loop(0, count)
        def _(n):
            at = pl.ds(pl.multiple_of(n * rows, rows), rows)
            value = x_v[at, :].astype(f32)
            mean = jnp.mean(value, 1, keepdims=True)
            centre = value - mean
            inverse = lax.rsqrt(jnp.mean(centre * centre, 1, keepdims=True) + EPS)
            normed = centre * inverse
            m_ref[at, :] = mean
            i_ref[at, :] = inverse
            h1_v[at, :] = (normed * g_ref[0:1] + g_ref[1:2]).astype(bf16)
            h2_v[at, :] = (normed * g_ref[2:3] + g_ref[3:4]).astype(bf16)

        h1_copy = pltpu.make_async_copy(h1_v, h1_hbm, sems.at[2])
        h1_copy.start()
        for copy in w_copies + dy_copies:
            copy.wait()
        d_copy.wait()
        mine = dy_v[:, pl.ds(pl.multiple_of(number_ref[1] * 256, 256), 256)]
        sum_ref[...] = jnp.sum(mine.astype(f32), 0, keepdims=True)

        def split(part, places, high, wide):
            at = (places, high, wide)

            @pl.when(own)
            def _():
                keep_v[at] = part[:, 0]
                send_v[at] = part[:, 1]

            @pl.when(jnp.logical_not(own))
            def _():
                keep_v[at] = part[:, 1]
                send_v[at] = part[:, 0]

        def leaving(n):
            at = (pl.ds(n * 2, 2), pl.ds(0, 64))
            return (
                pltpu.make_async_copy(keep_v.at[at], keep_hbm.at[at], sems.at[3]),
                pltpu.make_async_copy(send_v.at[at], send_hbm.at[at], sems.at[4]),
            )

        @pl.loop(0, ff // 256)
        def _(n):
            at = pl.ds(pl.multiple_of(n * 256, 256), 256)
            u = dot(h2_v[...], w_v[:, :, :, at].reshape(width, 256)) + b_ref[:, at]
            cdf = 0.5 * (1.0 + lax.erf(u * math.sqrt(0.5)))
            pdf = jnp.exp(-0.5 * u * u) * (1.0 / math.sqrt(2.0 * math.pi))
            act = (u * cdf).astype(bf16)
            act_v[:, at] = act
            du = (dot(dy_v[...], d_v[at, :], 1, 1) * (cdf + u * pdf)).astype(bf16)
            du_v[:, at] = du
            db_ref[:, at] = jnp.sum(du.astype(f32), 0, keepdims=True)
            part = dot_rows(act, dy_v[...]).astype(bf16).reshape(2, 2, 64, width)
            split(part, pl.ds(n * 2, 2), pl.ds(0, 64), slice(None))
            for copy in leaving(n):
                copy.start()

        act_copy = pltpu.make_async_copy(act_v, act_hbm, sems.at[0])
        act_copy.start()
        du_copy = pltpu.make_async_copy(du_v, du_hbm, sems.at[1])
        du_copy.start()
        for n in range(ff // 256):
            for copy in leaving(n):
                copy.wait()

        def block(n):
            at = (
                slice(None),
                pl.ds(pl.multiple_of(64 + 16 * (n % 4), 16), 16),
                pl.ds(pl.multiple_of(n // 4 * ff, ff), ff),
            )
            return at

        def away(n):
            at = block(n)
            return (
                pltpu.make_async_copy(keep_v.at[at], keep_hbm.at[at], sems.at[3]),
                pltpu.make_async_copy(send_v.at[at], send_hbm.at[at], sems.at[4]),
            )

        @pl.loop(0, 8)
        def _(n):
            lanes = pl.ds(pl.multiple_of(n * 256, 256), 256)
            part = dot_rows(h2_v[:, lanes], du_v[...]).astype(bf16).reshape(8, 2, 16, ff)
            split(part, *block(n))
            for copy in away(n):
                copy.start()

        for n in range(8):
            for copy in away(n):
                copy.wait()
        h1_copy.wait()
        act_copy.wait()
        du_copy.wait()

    wide = jax.ShapeDtypeStruct((total, width), bf16)
    thin = jax.ShapeDtypeStruct((total, ff), bf16)
    column = jax.ShapeDtypeStruct((total, 1), f32)
    grads = jax.ShapeDtypeStruct((8, 128, width), bf16)
    vmem = pl.BlockSpec(memory_space=pltpu.VMEM)
    return pl.pallas_call(
        after_inputs(body, 5 + parts + 2 * count, len(after)),
        out_shape=(
            wide,
            thin,
            thin,
            grads,
            grads,
            column,
            column,
            jax.ShapeDtypeStruct((1, ff), f32),
            jax.ShapeDtypeStruct((1, 256), f32),
        ),
        in_specs=[pl.BlockSpec(memory_space=pltpu.SMEM)] * 2
        + [vmem, vmem]
        + anywhere(parts + 2 * count + 1 + len(after)),
        out_specs=tuple(anywhere(5)) + (vmem,) * 4,
        scratch_shapes=[
            pltpu.VMEM((total, width), bf16),
            pltpu.VMEM((total, width), bf16),
            pltpu.VMEM((total, width), bf16),
            pltpu.VMEM((total, width), bf16),
            pltpu.VMEM((8, 8, width // 64, ff), bf16),
            pltpu.VMEM((ff, width), bf16),
            pltpu.VMEM((total, ff), bf16),
            pltpu.VMEM((total, ff), bf16),
            pltpu.VMEM((8, 128, width), bf16),
            pltpu.VMEM((8, 128, width), bf16),
            pltpu.SemaphoreType.DMA((count,)),
            pltpu.SemaphoreType.DMA((count,)),
            pltpu.SemaphoreType.DMA((parts,)),
            pltpu.SemaphoreType.DMA((5,)),
        ],
        compiler_params=kernel_params(),
        cost_estimate=cost(32),
        name="feed_forward",
    )(numbers, spots, gains, bias, *[p[0] for p in weight], *x, *dy, down, *after)


def packed(qkv_weight, up_weight, vectors, lengths, place, head, tokens, cotangent):
    wide, up_wide = qkv_weight.shape[1], up_weight.shape[1]
    part, up_part = 3 * head, up_wide // 8
    cols = part + up_part

    def body(place_ref, len_ref, q_ref, u_ref, x_ref, dy_ref, *refs):
        v_refs, out_ref, pair_ref = refs[: len(vectors)], refs[-2], refs[-1]
        pair_ref[0] = x_ref[...]
        pair_ref[1] = dy_ref[...]
        lane = lax.broadcasted_iota(jnp.int32, (8, cols), 1)
        row = lax.broadcasted_iota(jnp.int32, (8, cols), 0)
        sizes = jnp.zeros((8, cols), f32)
        for at in range(3):
            sizes = jnp.where(lane == at, len_ref[0, at].astype(f32), sizes)
        vector = jnp.concatenate([ref[...].astype(f32) for ref in v_refs])[None, :]
        vector = jnp.broadcast_to(vector, (8, cols))
        tail = jnp.where(row == 0, vector, jnp.where(row == 1, sizes, 0.0)).astype(bf16)
        for owner in range(8):
            pieces = [
                q_ref[:, (third * 8 + owner) * head : (third * 8 + owner + 1) * head]
                for third in range(3)
            ]
            pieces.append(u_ref[:, owner * up_part : (owner + 1) * up_part])
            out_ref[owner] = jnp.concatenate([jnp.concatenate(pieces, 1), tail], 0)

    return pl.pallas_call(
        body,
        out_shape=(
            jax.ShapeDtypeStruct((8, 40, cols), bf16),
            jax.ShapeDtypeStruct((2,) + tokens.shape, bf16),
        ),
        grid_spec=pltpu.PrefetchScalarGridSpec(
            num_scalar_prefetch=2,
            grid=(1,),
            in_specs=[
                pl.BlockSpec((32, wide), lambda i, place, lens: (place[0], 0)),
                pl.BlockSpec((32, up_wide), lambda i, place, lens: (place[0], 0)),
                pl.BlockSpec(tokens.shape, lambda i, place, lens: (0, 0)),
                pl.BlockSpec(tokens.shape, lambda i, place, lens: (0, 0)),
            ]
            + [pl.BlockSpec(v.shape, lambda i, place, lens: (0,)) for v in vectors],
            out_specs=(
                pl.BlockSpec((8, 40, cols), lambda i, place, lens: (0, 0, 0)),
                pl.BlockSpec((2,) + tokens.shape, lambda i, place, lens: (0, 0, 0)),
            ),
        ),
        compiler_params=kernel_params(),
        cost_estimate=cost(3),
        name="packed",
    )(place, lengths, qkv_weight, up_weight, tokens, cotangent, *vectors)


def attend(h1, dy, weight, spots, out, bias, cosine, sine, lengths, after, rows=128):
    total, width = h1.shape
    count = len(dy)
    head = out.shape[0]
    scale = head ** (-0.5)

    parts = len(weight)

    def body(len_ref, spot_ref, b_ref, *refs):
        w_refs, refs = refs[:parts], refs[parts:]
        dy_refs = refs[:count]
        h1_hbm, out_hbm, cos_hbm, sin_hbm = refs[count : count + 4]
        ol_hbm, dq_hbm, sum_ref = refs[count + 4 : count + 7]
        (dy_v, h1_v, w_v, wo_v, cos_v, sin_v, qkv_v, do_v, ol_v, dq_v, dy_sem, w_sem, sems) = (
            refs[count + 7 :]
        )
        pairs = (
            (h1_hbm, h1_v),
            (out_hbm, wo_v),
            (cos_hbm, cos_v),
            (sin_hbm, sin_v),
        )
        copies = loads(
            [pltpu.make_async_copy(*pair, sems.at[n]) for n, pair in enumerate(pairs)]
        )
        w_copies = loads(
            weight_copies(weight, w_refs, spot_ref, w_v, pl.ds(0, 3 * head), w_sem)
        )
        dy_copies = loads(piece_copies(dy_refs, 1, dy_v, dy_sem, rows))
        for copy in copies[:1] + w_copies:
            copy.wait()

        @pl.loop(0, 3)
        def _(n):
            at = pl.ds(pl.multiple_of(n * head, head), head)
            qkv_v[:, at] = dot(h1_v[...], w_v[:, :, :, at].reshape(width, head)) + b_ref[n]

        for copy in copies[1:] + dy_copies:
            copy.wait()
        do_v[...] = dot(dy_v[...], wo_v[...], 1, 1).astype(bf16)
        sum_ref[...] = jnp.zeros_like(sum_ref)

        @pl.loop(0, total // rows, unroll=2)
        def _(block):
            at = pl.ds(pl.multiple_of(block * rows, rows), rows)
            cos, sin = cos_v[at, :], sin_v[at, :]

            def turned(value, sign):
                left = value[:, :128]
                left = left * cos + swap_halves(left) * (sin * sign)
                return jnp.concatenate([left, value[:, 128:]], 1).astype(bf16)

            q, k = turned(qkv_v[at, 0:head], 1.0), turned(qkv_v[at, head : 2 * head], 1.0)
            v = qkv_v[at, 2 * head :].astype(bf16)
            scores = dot(q, k, 1, 1) * scale
            masked = jnp.where(allowed_mask(len_ref, block, rows), scores, -1e30)
            shifted = jnp.exp(masked - jnp.max(masked, 1, keepdims=True))
            probs = shifted / jnp.sum(shifted, 1, keepdims=True)
            low = probs.astype(bf16)
            ol_v[at, :] = dot(low, v).astype(bf16)
            d_out = do_v[at, :]
            d_value = dot(low, d_out, 0, 0)
            d_probs = dot(d_out, v, 1, 1)
            centred = d_probs - jnp.sum(d_probs * probs, 1, keepdims=True)
            d_scores = (probs * centred).astype(bf16)
            d_query = turned(dot(d_scores, k) * scale, -1.0)
            d_key = turned(dot(d_scores, q, 0, 0) * scale, -1.0)
            for n, grad in enumerate((d_query, d_key, d_value.astype(bf16))):
                lanes = slice(n * head, (n + 1) * head)
                dq_v[at, lanes] = grad
                sum_ref[:, lanes] += jnp.sum(grad.astype(f32), 0, keepdims=True)

        ol_copy = pltpu.make_async_copy(ol_v, ol_hbm, sems.at[0])
        ol_copy.start()
        dq_copy = pltpu.make_async_copy(dq_v, dq_hbm, sems.at[1])
        dq_copy.start()

        for copy in (ol_copy, dq_copy):
            copy.wait()

    vmem = pl.BlockSpec(memory_space=pltpu.VMEM)
    smem = pl.BlockSpec(memory_space=pltpu.SMEM)
    return pl.pallas_call(
        after_inputs(body, 7 + parts + count, len(after)),
        out_shape=(
            jax.ShapeDtypeStruct((total, head), bf16),
            jax.ShapeDtypeStruct((total, 3 * head), bf16),
            jax.ShapeDtypeStruct((1, 3 * head), f32),
        ),
        in_specs=[smem, smem, vmem] + anywhere(parts + count + 4 + len(after)),
        out_specs=tuple(anywhere(2)) + (vmem,),
        scratch_shapes=[
            pltpu.VMEM((total, width), bf16),
            pltpu.VMEM((total, width), bf16),
            pltpu.VMEM((8, 8, width // 64, 3 * head), bf16),
            pltpu.VMEM((head, width), bf16),
            pltpu.VMEM((total, 128), f32),
            pltpu.VMEM((total, 128), f32),
            pltpu.VMEM((total, 3 * head), f32),
            pltpu.VMEM((total, head), bf16),
            pltpu.VMEM((total, head), bf16),
            pltpu.VMEM((total, 3 * head), bf16),
            pltpu.SemaphoreType.DMA((count,)),
            pltpu.SemaphoreType.DMA((parts,)),
            pltpu.SemaphoreType.DMA((4,)),
        ],
        compiler_params=kernel_params(),
        cost_estimate=cost(17),
        name="attend",
    )(
        lengths,
        spots,
        bias,
        *[p[0] for p in weight],
        *dy,
        h1,
        out,
        cosine,
        sine,
        *after,
    )


def attention_grads(h1, dy, d_qkv, attended, numbers, after):
    total, width = h1.shape
    count = len(dy)
    rows = total // count
    head = attended.shape[1]

    def body(number_ref, *refs):
        dy_refs = refs[:count]
        h1_hbm, dq_hbm, ol_hbm, keep_hbm, send_hbm = refs[count : count + 5]
        dy_v, h1_v, dq_v, ol_v, keep_v, send_v, dy_sem, sems = refs[count + 5 :]
        own = number_ref[0] == 0
        pairs = ((h1_hbm, h1_v), (dq_hbm, dq_v), (ol_hbm, ol_v))
        copies = loads(
            [pltpu.make_async_copy(*pair, sems.at[n]) for n, pair in enumerate(pairs)]
        )
        dy_copies = loads(piece_copies(dy_refs, 1, dy_v, dy_sem, rows))
        for copy in copies:
            copy.wait()

        def split(part, high, lanes):
            for z_hi in range(2):
                at = (pl.ds(4 * z_hi, 4), high, lanes)

                @pl.when(own)
                def _(z_hi=z_hi, at=at):
                    keep_v[at] = part[:, z_hi, 0]
                    send_v[at] = part[:, z_hi, 1]

                @pl.when(jnp.logical_not(own))
                def _(z_hi=z_hi, at=at):
                    keep_v[at] = part[:, z_hi, 1]
                    send_v[at] = part[:, z_hi, 0]

        @pl.loop(0, 8)
        def _(n):
            lanes = pl.ds(pl.multiple_of(n * 256, 256), 256)
            part = dot_rows(h1_v[:, lanes], dq_v[...]).astype(bf16).reshape(4, 2, 2, 16, 3 * head)
            for third in range(3):
                split(
                    part[..., third * head : (third + 1) * head],
                    pl.ds(16 * third, 16),
                    pl.ds(pl.multiple_of(n * head, head), head),
                )

        for copy in dy_copies:
            copy.wait()
        part = dot_rows(ol_v[...], dy_v[...]).astype(bf16).reshape(4, 2, 2, 16, width)
        split(part, pl.ds(48, 16), slice(None))
        keep_copy = pltpu.make_async_copy(keep_v, keep_hbm, sems.at[0])
        keep_copy.start()
        send_copy = pltpu.make_async_copy(send_v, send_hbm, sems.at[1])
        send_copy.start()
        keep_copy.wait()
        send_copy.wait()

    grads = jax.ShapeDtypeStruct((8, 64, width), bf16)
    return pl.pallas_call(
        after_inputs(body, 4 + count, len(after)),
        out_shape=(grads, grads),
        in_specs=[pl.BlockSpec(memory_space=pltpu.SMEM)] + anywhere(count + 3 + len(after)),
        out_specs=tuple(anywhere(2)),
        scratch_shapes=[
            pltpu.VMEM((total, width), bf16),
            pltpu.VMEM((total, width), bf16),
            pltpu.VMEM((total, 3 * head), bf16),
            pltpu.VMEM((total, head), bf16),
            pltpu.VMEM((8, 64, width), bf16),
            pltpu.VMEM((8, 64, width), bf16),
            pltpu.SemaphoreType.DMA((count,)),
            pltpu.SemaphoreType.DMA((3,)),
        ],
        compiler_params=kernel_params(),
        cost_estimate=cost(12),
        name="attention_grads",
    )(numbers, *dy, h1, d_qkv, attended, *after)


def mixed_part(active, attended, down, out, bias, after):
    rows, ff = active.shape
    head, width = out.shape
    step = 512
    count = rows // 128

    def body(act_ref, ol_ref, wd_ref, wo_ref, b_ref, *refs):
        total = dot(act_ref[...], wd_ref[...]) + dot(ol_ref[...], wo_ref[...]) + b_ref[...]
        for at in range(count):
            refs[at][...] = total[at * 128 : (at + 1) * 128].astype(bf16)

    return pl.pallas_call(
        after_inputs(body, 5, len(after)),
        out_shape=(jax.ShapeDtypeStruct((128, width), bf16),) * count,
        grid=(width // step,),
        in_specs=[
            pl.BlockSpec((rows, ff), lambda i: (0, 0)),
            pl.BlockSpec((rows, head), lambda i: (0, 0)),
            pl.BlockSpec((ff, step), lambda i: (0, i)),
            pl.BlockSpec((head, step), lambda i: (0, i)),
            pl.BlockSpec((1, step), lambda i: (0, i)),
        ]
        + anywhere(len(after)),
        out_specs=(pl.BlockSpec((128, step), lambda i: (0, i)),) * count,
        compiler_params=kernel_params(),
        cost_estimate=cost(10),
        name="mixed_part",
    )(active, attended, down, out, bias, *after)


def back_norms(d_qkv, d_hidden, weight, spots, x, mean, inverse, gains, after):
    total, n1 = d_qkv.shape
    n2 = d_hidden.shape[1]
    count = len(x)
    parts = len(weight)
    width = x[0].shape[-1]
    step = 512

    def body(spot_ref, m_ref, i_ref, g_ref, *refs):
        w_refs, refs = refs[:parts], refs[parts:]
        x_refs, refs = refs[:count], refs[count:]
        plain, sums_ref, outs = refs[:2], refs[2], refs[3 : 3 + count]
        dq_v, du_v, w_v, x_v, s_v, w_sem, x_sem, sems, out_sem = refs[3 + count :]
        plain_v = (dq_v, du_v)
        copies = loads(
            [
                pltpu.make_async_copy(plain[n], plain_v[n], sems.at[n]) for n in range(2)
            ]
            + weight_copies(weight, w_refs, spot_ref, w_v, slice(None), w_sem)
            + piece_copies(x_refs, 0, x_v, x_sem, 128)
        )
        def leaving(n):
            lanes = pl.ds(pl.multiple_of(n * step, step), step)
            return [
                pltpu.make_async_copy(
                    s_v.at[pl.ds(at * 128, 128), lanes], outs[at].at[:, lanes], out_sem.at[at]
                )
                for at in range(count)
            ]

        for copy in copies:
            copy.wait()

        @pl.loop(0, width // step)
        def _(n):
            lanes = pl.ds(pl.multiple_of(n * step, step), step)
            sources = pl.ds(n * (step // 256), step // 256)
            d1 = dot(dq_v[...], w_v[sources, :, :, 0:n1].reshape(step, n1), 1, 1)
            d2 = dot(du_v[...], w_v[sources, :, :, n1:].reshape(step, n2), 1, 1)
            s_v[:, lanes] = (d1 * g_ref[0:1, lanes] + d2 * g_ref[1:2, lanes]).astype(bf16)
            for copy in leaving(n):
                copy.start()
            normed = (x_v[:, lanes].astype(f32) - m_ref[...]) * i_ref[...]
            sums_ref[0:1, lanes] = jnp.sum(d1 * normed, 0, keepdims=True)
            sums_ref[1:2, lanes] = jnp.sum(d1, 0, keepdims=True)
            sums_ref[2:3, lanes] = jnp.sum(d2 * normed, 0, keepdims=True)
            sums_ref[3:4, lanes] = jnp.sum(d2, 0, keepdims=True)

        for n in range(width // step):
            for copy in leaving(n):
                copy.wait()

    vmem = pl.BlockSpec(memory_space=pltpu.VMEM)
    return pl.pallas_call(
        after_inputs(body, 6 + parts + count, len(after)),
        out_shape=(jax.ShapeDtypeStruct((4, width), f32),)
        + (jax.ShapeDtypeStruct((128, width), bf16),) * count,
        in_specs=[pl.BlockSpec(memory_space=pltpu.SMEM)]
        + [vmem] * 3
        + anywhere(parts + count + 2 + len(after)),
        out_specs=(vmem,) + tuple(anywhere(count)),
        scratch_shapes=[
            pltpu.VMEM((total, n1), bf16),
            pltpu.VMEM((total, n2), bf16),
            pltpu.VMEM((8, 8, width // 64, n1 + n2), bf16),
            pltpu.VMEM((total, width), bf16),
            pltpu.VMEM((total, width), bf16),
            pltpu.SemaphoreType.DMA((parts,)),
            pltpu.SemaphoreType.DMA((count,)),
            pltpu.SemaphoreType.DMA((2,)),
            pltpu.SemaphoreType.DMA((count,)),
        ],
        compiler_params=kernel_params(),
        cost_estimate=cost(15),
        name="back_norms",
    )(
        spots,
        mean,
        inverse,
        gains,
        *[p[0] for p in weight],
        *x,
        d_qkv,
        d_hidden,
        *after,
    )


def unpacked(part, after):
    owners, _, cols = part.shape

    def body(part_ref, rows_ref, info_ref):
        for owner in range(owners):
            rows_ref[owner] = part_ref[owner, 0:32]
            info_ref[owner] = part_ref[owner, 32:40].astype(f32)

    return pl.pallas_call(
        after_inputs(body, 1, len(after)),
        out_shape=(
            jax.ShapeDtypeStruct((owners, 32, cols), bf16),
            jax.ShapeDtypeStruct((owners, 8, cols), f32),
        ),
        in_specs=[pl.BlockSpec(memory_space=pltpu.VMEM)] + anywhere(len(after)),
        out_specs=(pl.BlockSpec(memory_space=pltpu.VMEM),) * 2,
        compiler_params=kernel_params(),
        cost_estimate=cost(3),
        name="unpacked",
    )(part, *after)


def joined(arrays, after):
    sizes = [array.shape[0] for array in arrays]
    unit = math.gcd(*sizes)
    block = (unit,) + arrays[0].shape[1:]
    count = len(arrays)
    firsts = [sum(sizes[:n]) // unit for n in range(count)]

    def body(*refs):
        step = pl.program_id(0)
        for ref, first, size in zip(refs, firsts, sizes):

            @pl.when((step >= first) & (step < first + size // unit))
            def _(ref=ref):
                refs[count][...] = ref[...]

    def came(first, size):
        return pl.BlockSpec(block, lambda i: (jnp.clip(i - first, 0, size // unit - 1), 0, 0))

    return pl.pallas_call(
        after_inputs(body, count, len(after)),
        out_shape=jax.ShapeDtypeStruct((sum(sizes),) + block[1:], bf16),
        grid=(sum(sizes) // unit,),
        in_specs=[came(first, size) for first, size in zip(firsts, sizes)] + anywhere(len(after)),
        out_specs=pl.BlockSpec(block, lambda i: (i, 0, 0)),
        compiler_params=kernel_params(),
        cost_estimate=cost(3),
        name="joined",
    )(*arrays, *after)


def halves(own, below, above, after):
    count, rows, cols = own.shape
    half = count // 2

    def body(own_ref, below_ref, above_ref, low_ref, high_ref, all_ref):
        step = pl.program_id(0)
        all_ref[0] = own_ref[...]
        all_ref[1] = above_ref[...]
        all_ref[2] = below_ref[...]

        @pl.when(step == 0)
        def _():
            low_ref[...] = below_ref[...]

        @pl.when(step == 1)
        def _():
            high_ref[...] = above_ref[...]

    block = pl.BlockSpec((half, rows, cols), lambda i: (i, 0, 0))
    whole = pl.BlockSpec((half, rows, cols), lambda i: (0, 0, 0))
    low, high, together = pl.pallas_call(
        after_inputs(body, 3, len(after)),
        out_shape=(jax.ShapeDtypeStruct((half, rows, cols), bf16),) * 2
        + (jax.ShapeDtypeStruct((3, count, rows, cols), bf16),),
        grid=(2,),
        in_specs=[block] * 3 + anywhere(len(after)),
        out_specs=(
            whole,
            whole,
            pl.BlockSpec((3, half, rows, cols), lambda i: (0, i, 0, 0)),
        ),
        compiler_params=kernel_params(),
        cost_estimate=cost(4),
        name="halves",
    )(own, below, above, *after)
    return low, high, together.reshape(3 * count, rows, cols)


def finished(mix, sums, tokens, cotangent, after):
    rows, width = tokens.shape
    step = rows // 2

    def body(*refs):
        x_ref, dy_ref, mixed_ref, grad_ref = refs[8:]
        x = x_ref[...].astype(f32)
        mixed_ref[...] = (x + wide(*refs[:4])).astype(bf16)
        gain = wide(*refs[4:8])
        centre = x - jnp.mean(x, 1, keepdims=True)
        inverse = lax.rsqrt(jnp.mean(centre * centre, 1, keepdims=True) + EPS)
        normed = centre * inverse
        grad_ref[...] = dy_ref[...].astype(f32) + inverse * (
            gain
            - jnp.mean(gain, 1, keepdims=True)
            - normed * jnp.mean(gain * normed, 1, keepdims=True)
        )

    block = pl.BlockSpec((step, width), lambda i: (i, 0))
    later = pl.BlockSpec((step, width), lambda i: (i + 2, 0))
    return pl.pallas_call(
        after_inputs(body, 10, len(after)),
        out_shape=(
            jax.ShapeDtypeStruct((rows, width), bf16),
            jax.ShapeDtypeStruct((rows, width), f32),
        ),
        grid=(2,),
        in_specs=[block, later, block, block] * 2 + [block, block] + anywhere(len(after)),
        out_specs=(block, block),
        compiler_params=kernel_params(),
        cost_estimate=cost(3),
        name="finished",
    )(*mix, *sums, tokens, cotangent, *after)


def packed_sums(stays, crossed, own, below, above, norm_sums, qkv_sums, up_sums, dy_sums, numbers, ff, head, after):
    width = own.shape[1]

    def body(*refs):
        stay_ref, cross_ref, own_ref, below_ref, above_ref = refs[:5]
        norm_ref, q_ref, u_ref, y_ref, number_ref, out_ref, lanes_ref, keep_ref, small = refs[5:]
        shard = number_ref[1]
        inner = (stay_ref[0].astype(f32) + cross_ref[0].astype(f32)).astype(bf16)
        total = wide(own_ref, below_ref, above_ref).astype(bf16)
        for owner in range(8):
            mine = shard == owner
            small[...] = jnp.zeros_like(small)
            small[0:4] = norm_ref[:, owner * head : (owner + 1) * head]
            for n in range(3):
                third, source = divmod(owner * 3 + n, 8)
                lanes = slice(third * head, (third + 1) * head)
                small[4 + n : 5 + n] = jnp.where(shard == source, q_ref[:, lanes], 0.0)
            for n in range(4):
                lanes = slice(n * head, (n + 1) * head)
                small[7 + n : 8 + n] = jnp.where(mine, u_ref[:, lanes], 0.0)
            small[11:12] = jnp.where(mine, y_ref[...], 0.0)
            pieces = [
                total[16 * third : 16 * third + 16, owner * head : (owner + 1) * head]
                for third in range(3)
            ]
            row, col = 64 + 16 * (owner % 4), owner // 4 * ff
            pieces.append(inner[row : row + 16, col : col + ff])
            pieces.append(small[...].astype(bf16))
            out_ref[owner] = jnp.concatenate(pieces, 1)
            lanes_ref[owner] = total[48:64, owner * head : (owner + 1) * head]
        keep_ref[...] = inner[0:64]

    vmem = pl.BlockSpec(memory_space=pltpu.VMEM)
    return pl.pallas_call(
        after_inputs(body, 10, len(after)),
        out_shape=(
            jax.ShapeDtypeStruct((8, 16, 4 * head + ff), bf16),
            jax.ShapeDtypeStruct((8, 16, width // 8), bf16),
            jax.ShapeDtypeStruct((64, width), bf16),
        ),
        in_specs=[vmem] * 9 + [pl.BlockSpec(memory_space=pltpu.SMEM)] + anywhere(len(after)),
        out_specs=(vmem,) * 3,
        scratch_shapes=[pltpu.VMEM((16, head), f32)],
        compiler_params=kernel_params(),
        cost_estimate=cost(3),
        name="packed_sums",
    )(stays, crossed, own, below, above, norm_sums, qkv_sums, up_sums, dy_sums, numbers, *after)


def unpacked_sums(received, outs, downs, after):
    sources, rows, width = received.shape
    cols = width - outs.shape[2]

    def body(part_ref, outs_ref, down_ref, part_out, down_out):
        part_out[0] = jnp.concatenate(
            [
                jnp.concatenate([part_ref[n, :, 0:cols], outs_ref[n]], 1)
                for n in range(sources)
            ],
            0,
        )
        small = jnp.sum(part_ref[:, :, cols:].astype(f32), 0).astype(bf16)
        down_out[0, 0:64] = down_ref[...]
        down_out[0, 64 : 64 + rows] = jnp.concatenate(
            [small, jnp.zeros((rows, cols), bf16)], 1
        )

    vmem = pl.BlockSpec(memory_space=pltpu.VMEM)
    return pl.pallas_call(
        after_inputs(body, 3, len(after)),
        out_shape=(
            jax.ShapeDtypeStruct((1, sources * rows, width), bf16),
            jax.ShapeDtypeStruct((1, 64 + rows, width), bf16),
        ),
        in_specs=[vmem] * 3 + anywhere(len(after)),
        out_specs=(vmem,) * 2,
        compiler_params=kernel_params(),
        cost_estimate=cost(3),
        name="unpacked_sums",
    )(received, outs, downs, *after)


def blocks_call(name, body, numbers, terms, outs, after, time=3):
    def came(block, index):
        rest = (0,) * (len(block) - 1)
        return pl.BlockSpec(block, lambda i, n: (index(n),) + rest)

    return pl.pallas_call(
        after_inputs(body, 1 + len(terms), len(after)),
        out_shape=tuple(jax.ShapeDtypeStruct(out, bf16) for out in outs),
        grid_spec=pltpu.PrefetchScalarGridSpec(
            num_scalar_prefetch=1,
            grid=(1,),
            in_specs=[came(block, index) for _, block, index in terms] + anywhere(len(after)),
            out_specs=tuple(
                pl.BlockSpec(out, lambda i, n, size=len(out): (0,) * size) for out in outs
            ),
        ),
        compiler_params=kernel_params(),
        cost_estimate=cost(time),
        name=name,
    )(numbers, *[array for array, _, _ in terms], *after)


def wide(*refs):
    return functools.reduce(jnp.add, [ref[...].astype(f32) for ref in refs])


def spread(pieces, places, core, targets, count, before, after):
    rows, cols = pieces[0][0].shape[1:]
    firsts, total = [], 0
    for mine, _ in pieces:
        firsts.append(total)
        total += mine.shape[0]

    def body(place_ref, core_ref, *refs):
        step = pl.program_id(0)
        outs = refs[2 * len(pieces) + len(before) :]
        first_core = core_ref[0] == 0

        def fill(ref, low):
            for out_ref, (_, high, parts) in zip(outs, targets):
                for to, row, col, size in parts:
                    out_ref[low * high : (low + 1) * high, to : to + size] = ref[
                        0, row : row + high, col : col + size
                    ].astype(f32)

        for n, (first, (mine, _)) in enumerate(zip(firsts, pieces)):
            here = (step >= first) & (step < first + mine.shape[0])

            @pl.when(here & first_core)
            def _(n=n):
                fill(refs[2 * n], 0)
                fill(refs[2 * n + 1], 1)

            @pl.when(here & jnp.logical_not(first_core))
            def _(n=n):
                fill(refs[2 * n], 1)
                fill(refs[2 * n + 1], 0)

    def chosen(first, size):
        return pl.BlockSpec(
            (1, rows, cols), lambda i, place, core: (jnp.clip(i - first, 0, size - 1), 0, 0)
        )

    specs, arrays = [], []
    for first, (mine, yours) in zip(firsts, pieces):
        specs += [chosen(first, mine.shape[0])] * 2
        arrays += [mine, yours]
    return pl.pallas_call(
        after_inputs(body, 2 + 2 * len(pieces) + len(before), len(after)),
        out_shape=tuple(
            jax.ShapeDtypeStruct((2 * count * high, wide), f32) for wide, high, _ in targets
        ),
        grid_spec=pltpu.PrefetchScalarGridSpec(
            num_scalar_prefetch=2,
            grid=(total,),
            in_specs=specs + anywhere(len(before) + len(after)),
            out_specs=tuple(
                pl.BlockSpec((2 * high, wide), lambda i, place, core: (place[i], 0))
                for wide, high, _ in targets
            ),
        ),
        input_output_aliases={2 + len(arrays) + n: n for n in range(len(before))},
        compiler_params=kernel_params(),
        cost_estimate=cost(0.3 * total),
        name="spread",
    )(places, core, *arrays, *before, *after)


def local(
    tokens,
    doc_lengths,
    cotangent,
    ln1_gain,
    ln1_bias,
    ln2_gain,
    ln2_bias,
    qkv_weight,
    qkv_bias,
    out_weight,
    out_bias,
    up_weight,
    up_bias,
    down_weight,
    down_bias,
):
    rows, width = tokens.shape
    head = width // HEADS
    group = 8
    rep = lax.axis_index("rep")
    shard = lax.axis_index("shard")
    y, h, c = rep // 4, (rep // 2) % 2, rep % 2
    l, x = shard // 4, shard % 4
    ff = up_bias.shape[0]

    cols = 3 * head + ff
    vectors = [ln1_gain, ln1_bias, ln2_gain, ln2_bias, qkv_bias]
    place = (y * 2 + c).astype(jnp.int32).reshape(1)
    part, pair = packed(
        qkv_weight, up_weight, vectors, doc_lengths, place, head, tokens, cotangent
    )
    below, above, other = move(pair, x=1), move(pair, x=-1), move(pair, l=1)
    far, other_above, other_below = move(below, x=1), move(other, x=-1), move(below, l=1)
    pairs = (pair, above, far, below, other, other_above, None, other_below)

    part = lax.all_to_all(part, "shard", 0, 0)
    own, infos = unpacked(part, (pairs[1], pairs[3], pairs[4]))
    below, above = move(own, y=1), move(own, y=-1)
    x_other_far, dy_other_far = move(other_below[0], x=1), move(other_above[1], x=-1)
    low, high, yours = halves(own, below, above, (far, other_above, other_below))
    far_low, far_high = move(low, y=1), move(high, y=-1)
    x_all = tuple(x_other_far if p is None else p for p in pairs)
    dy_all = tuple(dy_other_far if p is None else p for p in pairs)
    yours = move(yours, c=1)
    far_low_c, far_high_c = move(far_low, c=1), move(far_high, c=1)
    weight = (
        (own, 0, 8, 0, 0),
        (above, 0, 8, 0, 1),
        (far_low, 0, 4, 0, 2),
        (far_high, 0, 4, 4, 2),
        (below, 0, 8, 0, 3),
        (yours, 0, 8, 0, 4),
        (yours, 8, 8, 0, 5),
        (far_low_c, 0, 4, 0, 6),
        (far_high_c, 0, 4, 4, 6),
        (yours, 16, 8, 0, 7),
    )
    steps4 = (y + jnp.arange(4)) % 4
    spots = jnp.concatenate([steps4 * 2 + c, steps4 * 2 + 1 - c]).astype(jnp.int32)

    gains = infos[:, 0, :1024].reshape(8, 4, 256).transpose(1, 0, 2).reshape(4, width)
    qkv_b = infos[:, 0, 1024:].reshape(8 * 3, 1, head)
    qkv_b = jnp.stack(
        [lax.dynamic_index_in_dim(qkv_b, third * 8 + shard, 0, False) for third in range(3)]
    )
    steps8 = jnp.arange(8)
    sources = ((steps8 // 4) ^ l) * 4 + (x + steps8 % 4) % 4
    sources = sources.astype(jnp.int32)
    lengths = infos[:, 1, :3]
    lengths = jnp.sum(
        jnp.where(sources[:, None, None] == steps8[None, :, None], lengths[None], 0.0), 1
    ).astype(jnp.int32)
    ends = jnp.cumsum(lengths, 1)
    starts = ends - lengths
    steps_t = jnp.arange(rows, dtype=jnp.int32)
    segment = jnp.sum((steps_t[None, :, None] >= ends[:, None, :]).astype(jnp.int32), -1)
    slots = jnp.arange(lengths.shape[1], dtype=jnp.int32)
    begin = jnp.sum(
        jnp.where(segment[:, :, None] == slots[None, None, :], starts[:, None, :], 0), -1
    )
    position = (steps_t[None, :] - begin).astype(f32).reshape(group * rows, 1)
    lane = jnp.arange(128)
    freq = 10000.0 ** (-2.0 * (lane % (ROT // 2)).astype(f32) / ROT)
    angle = position * freq[None, :]
    cosine = jnp.where(lane < ROT, jnp.cos(angle), 1.0)
    sine = jnp.sin(angle)
    sine = jnp.where(lane < ROT // 2, -sine, jnp.where(lane < ROT, sine, 0.0))

    both_bias = (out_bias.astype(f32) + down_bias.astype(f32))[None, :]
    wide_bias = lax.dynamic_update_slice(jnp.zeros((1, width), f32), both_bias, (0, shard * 256))
    numbers = jnp.stack([c, shard, y, h]).astype(jnp.int32)

    h1, active, d_hidden, keep, send, mean, inverse, up_sums, dy_sums = feed_forward(
        x_all,
        dy_all,
        gains,
        weight,
        spots,
        down_weight,
        up_bias.astype(f32)[None],
        numbers,
        3 * head,
        (cosine, sine),
    )
    got = move(send, c=1)
    attended, d_qkv, qkv_sums = attend(
        h1, dy_all, weight, spots, out_weight, qkv_b, cosine, sine, lengths, (send,)
    )

    pair_shape, one = (2, 128, width), (1, 128, width)

    def turn(k):
        return lambda n: (n[2] + k) % 4

    def far_body(n_ref, keep_ref, got_ref, low_ref, high_ref):
        total = wide(keep_ref, got_ref).astype(bf16)
        low_ref[0] = total[0]
        high_ref[0] = total[1]

    low, high = blocks_call(
        "far_sums",
        far_body,
        numbers,
        [(keep, pair_shape, turn(2)), (got, pair_shape, turn(2))],
        (one, one),
        (attended,),
    )
    from_low, from_high = move(low, y=1), move(high, y=-1)
    a_keep, a_send = attention_grads(h1, dy_all, d_qkv, attended, numbers, (low, high))
    a_got = move(a_send, c=1)
    def near_body(n_ref, k1_ref, g1_ref, k3_ref, g3_ref, low_ref, high_ref, above_ref, below_ref):
        above, below = wide(k1_ref, g1_ref), wide(k3_ref, g3_ref)
        above_ref[0] = (above[0] + low_ref[0].astype(f32)).astype(bf16)
        above_ref[1] = above[1].astype(bf16)
        below_ref[0] = below[0].astype(bf16)
        below_ref[1] = (below[1] + high_ref[0].astype(f32)).astype(bf16)

    above, below = blocks_call(
        "near_sums",
        near_body,
        numbers,
        [(v, pair_shape, turn(k)) for k in (1, 3) for v in (keep, got)]
        + [(v, one, lambda n: 0) for v in (from_low, from_high)],
        (pair_shape, pair_shape),
        (a_send,),
        20,
    )
    from_below, from_above = move(above, y=1), move(below, y=-1)

    four, part_shape = (4, 64, width), (1, 64, width)

    def away_body(n_ref, keep_ref, got_ref, out_ref):
        out_ref[...] = wide(keep_ref, got_ref).astype(bf16)

    (a_away,) = blocks_call(
        "away_sums",
        away_body,
        numbers,
        [(v, four, lambda n: 1 - n[3]) for v in (a_keep, a_got)],
        (four,),
        (above,),
    )
    a_crossed = move(a_away, h=1)
    mix = mixed_part(active, attended, down_weight, out_weight, wide_bias, (a_away, above, below))
    norm_sums, *sums = back_norms(
        d_qkv,
        d_hidden,
        weight,
        spots,
        x_all,
        mean,
        inverse,
        jnp.stack([gains[0], gains[2]]),
        (mix[0],),
    )

    flat, both = (128, width), (256, width)

    def passed_body(n_ref, up_ref, from_below, here_ref, down_ref, from_above, there_ref, up_out, down_out):
        up_out[0:128] = wide(up_ref, from_below).astype(bf16)
        up_out[128:256] = here_ref[...]
        down_out[0:128] = wide(down_ref, from_above).astype(bf16)
        down_out[128:256] = there_ref[...]

    def other_body(n_ref, own_ref, below_ref, above_ref, out_ref):
        out_ref[...] = wide(own_ref, below_ref, above_ref).astype(bf16)

    def first(n):
        return 0

    def ring_start(pieces):
        return move(pieces[6], x=1), move(pieces[2], x=-1)

    def ring_middle(pieces, passed, after):
        operands = (pieces[5], passed[0], pieces[1], pieces[3], passed[1], pieces[7])
        ups, downs = blocks_call(
            "passed_sums",
            passed_body,
            numbers,
            [(v, flat, first) for v in operands],
            (both, both),
            after,
        )
        return (move(ups, x=1), move(downs, x=-1)), ups

    def ring_end(pieces, arrived, after):
        (other,) = blocks_call(
            "other_sums",
            other_body,
            numbers,
            [
                (pieces[4], flat, first),
                (arrived[0], flat, first),
                (arrived[1], flat, lambda n: 1),
            ],
            (flat,),
            after,
        )
        return (pieces[0], *arrived, move(other, l=1)), other

    mix_passed = ring_start(mix)
    mix_arrived, mix_ups = ring_middle(mix, mix_passed, (norm_sums,))

    def ends_body(n_ref, keep_ref, got_ref, below_ref, above_ref, leave_ref, stay_ref):
        total = wide(keep_ref, got_ref, below_ref, above_ref).astype(bf16)
        first = n_ref[3] == 0
        leave_ref[0] = jnp.where(first, total[1], total[0])
        stay_ref[0] = jnp.where(first, total[0], total[1])

    leaves, stays = blocks_call(
        "end_sums",
        ends_body,
        numbers,
        [(v, pair_shape, turn(0)) for v in (keep, got)]
        + [(v, pair_shape, lambda n: 0) for v in (from_below, from_above)],
        (one, one),
        (mix_ups,),
    )
    crossed = move(leaves, h=1)

    def around_body(n_ref, keep_ref, got_ref, crossed_ref, low_ref, high_ref, above_ref, own_ref, below_ref):
        def part(k):
            at = (n_ref[2] + k) % 4
            return wide(keep_ref.at[at], got_ref.at[at], crossed_ref.at[at]).astype(bf16)

        far = part(2)
        low_ref[...] = far[:32]
        high_ref[...] = far[32:]
        above_ref[...] = part(1)
        own_ref[...] = part(0)
        below_ref[...] = part(3)

    a_low, a_high, a_above, a_own, a_below = blocks_call(
        "around_sums",
        around_body,
        numbers,
        [(v, four, lambda n: n[3]) for v in (a_keep, a_got)] + [(a_crossed, four, lambda n: 0)],
        ((32, width), (32, width), (64, width), (64, width), (64, width)),
        (leaves,),
    )
    a_low, a_high = move(a_low, y=1), move(a_high, y=-1)

    def beside_body(n_ref, above_ref, below_ref, low_ref, high_ref, up_ref, down_ref):
        up_ref[0:32] = (above_ref[0:32].astype(f32) + low_ref[...].astype(f32)).astype(bf16)
        up_ref[32:64] = above_ref[32:64]
        down_ref[0:32] = below_ref[0:32]
        down_ref[32:64] = (below_ref[32:64].astype(f32) + high_ref[...].astype(f32)).astype(bf16)

    a_above, a_below = blocks_call(
        "beside_sums",
        beside_body,
        numbers,
        [(v, v.shape, lambda n: 0) for v in (a_above, a_below, a_low, a_high)],
        ((64, width), (64, width)),
        (crossed,),
    )
    a_from_below, a_from_above = move(a_above, y=1), move(a_below, y=-1)

    part, outs, downs = packed_sums(
        stays,
        crossed,
        a_own,
        a_from_below,
        a_from_above,
        norm_sums,
        qkv_sums,
        up_sums,
        dy_sums,
        numbers,
        ff,
        head,
        (),
    )
    received = lax.all_to_all(part, "shard", 0, 0)
    mix_left, mix_other = ring_end(mix, mix_arrived, ())
    part, downs = unpacked_sums(received, outs, downs, (mix_other,))
    sums_arrived, sums_ups = ring_middle(sums, ring_start(sums), (received,))
    sums_left, sums_other = ring_end(sums, sums_arrived, ())

    order = ((0, h), (0, 1 - h), (1, h), (1, 1 - h), (3, h), (3, 1 - h), (2, h), (2, 1 - h))
    places = jnp.stack([(y + k) % 4 * 2 + high for k, high in order]).astype(jnp.int32)

    def rep_gather(own, after):
        own = jnp.concatenate([own, move(own, h=1)])
        below, above = move(own, y=1), move(own, y=-1)
        low, high, near = halves(own, below, above, after)
        return near, (move(low, y=1), move(high, y=-1))

    near, far = rep_gather(downs, (sums_ups,))
    downs_all = joined((near, *far), ())
    downs_yours = move(downs_all, c=1)
    (down_grad,) = spread(
        [(downs_all, downs_yours)],
        places,
        numbers[:1],
        [(width, 64, [(0, 0, 0, width)])],
        8,
        (),
        (),
    )
    near, far = rep_gather(part, (downs_all, sums_other))
    targets = [
        (
            3 * width,
            16,
            [
                ((third * 8 + source) * head, 16 * source, third * head, head)
                for source in range(8)
                for third in range(3)
            ],
        ),
        (8 * ff, 16, [(source * ff, 16 * source, 3 * head, ff) for source in range(8)]),
        (width, 16, [(source * head, 16 * source, cols, head) for source in range(8)]),
    ]
    grads = spread([(near, move(near, c=1))], places[:6], numbers[:1], targets, 8, (), (down_grad,))
    far = joined(far, (grads[0],))
    mixed, tokens_grad = finished(mix_left, sums_left, tokens, cotangent, (far,))
    qkv_grad, up_grad, out_grad = spread(
        [(far, move(far, c=1))],
        places[6:],
        numbers[:1],
        targets,
        8,
        grads,
        (tokens_grad,),
    )
    smalls = jnp.concatenate([downs_all[:, 64:80, 0:head], downs_yours[:, 64:80, 0:head]])
    smalls = jnp.sum(smalls.astype(f32), 0)
    norm_grads = smalls[:4]
    dy_total = smalls[11]
    return (
        mixed,
        tokens_grad,
        norm_grads[0],
        norm_grads[1],
        norm_grads[2],
        norm_grads[3],
        qkv_grad,
        smalls[4:7].reshape(3 * head),
        out_grad,
        dy_total,
        up_grad,
        smalls[7:11].reshape(ff),
        down_grad,
        dy_total,
    )


def solution(mesh):
    rows = P(BOTH, None)
    vector, matrix = P("shard"), P("shard", None)
    return jax.shard_map(
        local,
        mesh=mesh,
        in_specs=(rows, rows, rows, vector, vector, vector, vector)
        + (matrix, vector, matrix, vector, matrix, vector, matrix, vector),
        out_specs=(rows, rows, vector, vector, vector, vector)
        + (matrix, vector, matrix, vector, matrix, vector, matrix, vector),
        check_vma=False,
    )
```

```python
import functools
import math

import jax
import jax.numpy as jnp
from jax import lax
from jax.experimental import pallas as pl
from jax.experimental.pallas import tpu as pltpu
from jax.sharding import PartitionSpec as P

HEADS = 8
ROT = 64
EPS = 1e-05
f32 = jnp.float32
bf16 = jnp.bfloat16


def cost(time):
    return pl.CostEstimate(flops=int(time * 1.15e9), bytes_accessed=1000, transcendentals=0)


BOTH = ("rep", "shard")
SIZES = (4, 2, 2, 2, 4)
SAME_CORE = [[2 * n + c for n in range(8)] for c in range(2)]
SAME_CORE_ALL = [[(2 * n + c) * 8 + s for n in range(8) for s in range(8)] for c in range(2)]


def coords():
    for y in range(4):
        for h in range(2):
            for c in range(2):
                for l in range(2):
                    for x in range(4):
                        yield (y, h, c, l, x)


def linear(t):
    y, h, c, l, x = (v % m for v, m in zip(t, SIZES))
    return ((y * 2 + h) * 2 + c) * 8 + l * 4 + x


def move(value, y=0, h=0, c=0, l=0, x=0):
    step = (y, h, c, l, x)
    pairs = [(linear(t), linear(tuple(a + b for a, b in zip(t, step)))) for t in coords()]
    return lax.ppermute(value, BOTH, pairs)


def pick(value, index, axis):
    return lax.dynamic_index_in_dim(value, index, axis, keepdims=False)


def kernel_params():
    return pltpu.CompilerParams(vmem_limit_bytes=56 * 1024 * 1024)


def after_inputs(body, count, extra):
    return lambda *refs: body(*refs[:count], *refs[count + extra :])


def anywhere(count):
    return [pl.BlockSpec(memory_space=pl.ANY)] * count


def dot(a, b, ca=1, cb=0):
    return lax.dot_general(a, b, (((ca,), (cb,)), ((), ())), preferred_element_type=f32)


def swap_halves(value):
    lane = lax.broadcasted_iota(jnp.int32, value.shape, 1)
    return jnp.where(lane < 32, pltpu.roll(value, 96, 1), pltpu.roll(value, 32, 1))


def allowed_mask(lengths_ref, block, rows):
    e0 = lengths_ref[block, 0]
    e1 = e0 + lengths_ref[block, 1]
    t = lax.broadcasted_iota(jnp.int32, (rows, rows), 0)
    s = lax.broadcasted_iota(jnp.int32, (rows, rows), 1)
    seg_t = (t >= e0).astype(jnp.int32) + (t >= e1).astype(jnp.int32)
    seg_s = (s >= e0).astype(jnp.int32) + (s >= e1).astype(jnp.int32)
    return (seg_t == seg_s) & (s <= t)


def dot_rows(a, b):
    return lax.dot_general(a, b, (((0,), (0,)), ((), ())), preferred_element_type=f32)


def loads(copies):
    for copy in copies:
        copy.start()
    return copies


def piece_copies(pieces, half, target, sems, rows):
    return [
        pltpu.make_async_copy(
            piece.at[half] if len(piece.shape) == 3 else piece,
            target.at[pl.ds(at * rows, rows)],
            sems.at[at],
        )
        for at, piece in enumerate(pieces)
    ]


def weight_copies(pieces, refs, spot_ref, target, lanes, sems):
    return [
        pltpu.make_async_copy(
            ref.at[pl.ds(begin, size), :, lanes],
            target.at[pl.ds(first, size), spot_ref[spot]],
            sems.at[at],
        )
        for at, (ref, (_, begin, size, first, spot)) in enumerate(zip(refs, pieces))
    ]


def feed_forward(x, dy, gains, weight, spots, down, bias, numbers, first, after):
    rows, width = x[0].shape[1:]
    count = len(x)
    total = rows * count
    ff = bias.shape[1]

    parts = len(weight)

    def body(number_ref, spot_ref, g_ref, b_ref, *refs):
        w_refs, refs = refs[:parts], refs[parts:]
        x_refs, dy_refs, d_hbm = refs[:count], refs[count : 2 * count], refs[2 * count]
        (h1_hbm, act_hbm, du_hbm, keep_hbm, send_hbm, m_ref, i_ref, db_ref, sum_ref) = refs[
            2 * count + 1 : 2 * count + 10
        ]
        (x_v, dy_v, h1_v, h2_v, w_v, d_v, act_v, du_v, keep_v, send_v, x_sem, dy_sem, w_sem, sems) = refs[
            2 * count + 10 :
        ]
        own = number_ref[0] == 0
        x_copies = loads(piece_copies(x_refs, 0, x_v, x_sem, rows))
        w_copies = loads(
            weight_copies(weight, w_refs, spot_ref, w_v, pl.ds(first, ff), w_sem)
        )
        dy_copies = loads(piece_copies(dy_refs, 1, dy_v, dy_sem, rows))
        d_copy = pltpu.make_async_copy(d_hbm, d_v, sems.at[1])
        d_copy.start()
        for copy in x_copies:
            copy.wait()

        @pl.loop(0, count)
        def _(n):
            at = pl.ds(pl.multiple_of(n * rows, rows), rows)
            value = x_v[at, :].astype(f32)
            mean = jnp.mean(value, 1, keepdims=True)
            centre = value - mean
            inverse = lax.rsqrt(jnp.mean(centre * centre, 1, keepdims=True) + EPS)
            normed = centre * inverse
            m_ref[at, :] = mean
            i_ref[at, :] = inverse
            h1_v[at, :] = (normed * g_ref[0:1] + g_ref[1:2]).astype(bf16)
            h2_v[at, :] = (normed * g_ref[2:3] + g_ref[3:4]).astype(bf16)

        h1_copy = pltpu.make_async_copy(h1_v, h1_hbm, sems.at[2])
        h1_copy.start()
        for copy in w_copies + dy_copies:
            copy.wait()
        d_copy.wait()
        mine = dy_v[:, pl.ds(pl.multiple_of(number_ref[1] * 256, 256), 256)]
        sum_ref[...] = jnp.sum(mine.astype(f32), 0, keepdims=True)

        def split(part, places, high, wide):
            at = (places, high, wide)

            @pl.when(own)
            def _():
                keep_v[at] = part[:, 0]
                send_v[at] = part[:, 1]

            @pl.when(jnp.logical_not(own))
            def _():
                keep_v[at] = part[:, 1]
                send_v[at] = part[:, 0]

        def leaving(n):
            at = (pl.ds(n * 2, 2), pl.ds(0, 64))
            return (
                pltpu.make_async_copy(keep_v.at[at], keep_hbm.at[at], sems.at[3]),
                pltpu.make_async_copy(send_v.at[at], send_hbm.at[at], sems.at[4]),
            )

        @pl.loop(0, ff // 256)
        def _(n):
            at = pl.ds(pl.multiple_of(n * 256, 256), 256)
            u = dot(h2_v[...], w_v[:, :, :, at].reshape(width, 256)) + b_ref[:, at]
            cdf = 0.5 * (1.0 + lax.erf(u * math.sqrt(0.5)))
            pdf = jnp.exp(-0.5 * u * u) * (1.0 / math.sqrt(2.0 * math.pi))
            act = (u * cdf).astype(bf16)
            act_v[:, at] = act
            du = (dot(dy_v[...], d_v[at, :], 1, 1) * (cdf + u * pdf)).astype(bf16)
            du_v[:, at] = du
            db_ref[:, at] = jnp.sum(du.astype(f32), 0, keepdims=True)
            part = dot_rows(act, dy_v[...]).astype(bf16).reshape(2, 2, 64, width)
            split(part, pl.ds(n * 2, 2), pl.ds(0, 64), slice(None))
            for copy in leaving(n):
                copy.start()

        act_copy = pltpu.make_async_copy(act_v, act_hbm, sems.at[0])
        act_copy.start()
        du_copy = pltpu.make_async_copy(du_v, du_hbm, sems.at[1])
        du_copy.start()
        for n in range(ff // 256):
            for copy in leaving(n):
                copy.wait()

        def block(n):
            at = (
                slice(None),
                pl.ds(pl.multiple_of(64 + 16 * (n % 4), 16), 16),
                pl.ds(pl.multiple_of(n // 4 * ff, ff), ff),
            )
            return at

        def away(n):
            at = block(n)
            return (
                pltpu.make_async_copy(keep_v.at[at], keep_hbm.at[at], sems.at[3]),
                pltpu.make_async_copy(send_v.at[at], send_hbm.at[at], sems.at[4]),
            )

        @pl.loop(0, 8)
        def _(n):
            lanes = pl.ds(pl.multiple_of(n * 256, 256), 256)
            part = dot_rows(h2_v[:, lanes], du_v[...]).astype(bf16).reshape(8, 2, 16, ff)
            split(part, *block(n))
            for copy in away(n):
                copy.start()

        for n in range(8):
            for copy in away(n):
                copy.wait()
        h1_copy.wait()
        act_copy.wait()
        du_copy.wait()

    wide = jax.ShapeDtypeStruct((total, width), bf16)
    thin = jax.ShapeDtypeStruct((total, ff), bf16)
    column = jax.ShapeDtypeStruct((total, 1), f32)
    grads = jax.ShapeDtypeStruct((8, 128, width), bf16)
    vmem = pl.BlockSpec(memory_space=pltpu.VMEM)
    return pl.pallas_call(
        after_inputs(body, 5 + parts + 2 * count, len(after)),
        out_shape=(
            wide,
            thin,
            thin,
            grads,
            grads,
            column,
            column,
            jax.ShapeDtypeStruct((1, ff), f32),
            jax.ShapeDtypeStruct((1, 256), f32),
        ),
        in_specs=[pl.BlockSpec(memory_space=pltpu.SMEM)] * 2
        + [vmem, vmem]
        + anywhere(parts + 2 * count + 1 + len(after)),
        out_specs=tuple(anywhere(5)) + (vmem,) * 4,
        scratch_shapes=[
            pltpu.VMEM((total, width), bf16),
            pltpu.VMEM((total, width), bf16),
            pltpu.VMEM((total, width), bf16),
            pltpu.VMEM((total, width), bf16),
            pltpu.VMEM((8, 8, width // 64, ff), bf16),
            pltpu.VMEM((ff, width), bf16),
            pltpu.VMEM((total, ff), bf16),
            pltpu.VMEM((total, ff), bf16),
            pltpu.VMEM((8, 128, width), bf16),
            pltpu.VMEM((8, 128, width), bf16),
            pltpu.SemaphoreType.DMA((count,)),
            pltpu.SemaphoreType.DMA((count,)),
            pltpu.SemaphoreType.DMA((parts,)),
            pltpu.SemaphoreType.DMA((5,)),
        ],
        compiler_params=kernel_params(),
        cost_estimate=cost(32),
        name="feed_forward",
    )(numbers, spots, gains, bias, *[p[0] for p in weight], *x, *dy, down, *after)


def packed(qkv_weight, up_weight, vectors, lengths, place, head, tokens, cotangent):
    wide, up_wide = qkv_weight.shape[1], up_weight.shape[1]
    part, up_part = 3 * head, up_wide // 8
    cols = part + up_part

    def body(place_ref, len_ref, q_ref, u_ref, x_ref, dy_ref, *refs):
        v_refs, out_ref, pair_ref = refs[: len(vectors)], refs[-2], refs[-1]
        pair_ref[0] = x_ref[...]
        pair_ref[1] = dy_ref[...]
        lane = lax.broadcasted_iota(jnp.int32, (8, cols), 1)
        row = lax.broadcasted_iota(jnp.int32, (8, cols), 0)
        sizes = jnp.zeros((8, cols), f32)
        for at in range(3):
            sizes = jnp.where(lane == at, len_ref[0, at].astype(f32), sizes)
        vector = jnp.concatenate([ref[...].astype(f32) for ref in v_refs])[None, :]
        vector = jnp.broadcast_to(vector, (8, cols))
        tail = jnp.where(row == 0, vector, jnp.where(row == 1, sizes, 0.0)).astype(bf16)
        for owner in range(8):
            pieces = [
                q_ref[:, (third * 8 + owner) * head : (third * 8 + owner + 1) * head]
                for third in range(3)
            ]
            pieces.append(u_ref[:, owner * up_part : (owner + 1) * up_part])
            out_ref[owner] = jnp.concatenate([jnp.concatenate(pieces, 1), tail], 0)

    return pl.pallas_call(
        body,
        out_shape=(
            jax.ShapeDtypeStruct((8, 40, cols), bf16),
            jax.ShapeDtypeStruct((2,) + tokens.shape, bf16),
        ),
        grid_spec=pltpu.PrefetchScalarGridSpec(
            num_scalar_prefetch=2,
            grid=(1,),
            in_specs=[
                pl.BlockSpec((32, wide), lambda i, place, lens: (place[0], 0)),
                pl.BlockSpec((32, up_wide), lambda i, place, lens: (place[0], 0)),
                pl.BlockSpec(tokens.shape, lambda i, place, lens: (0, 0)),
                pl.BlockSpec(tokens.shape, lambda i, place, lens: (0, 0)),
            ]
            + [pl.BlockSpec(v.shape, lambda i, place, lens: (0,)) for v in vectors],
            out_specs=(
                pl.BlockSpec((8, 40, cols), lambda i, place, lens: (0, 0, 0)),
                pl.BlockSpec((2,) + tokens.shape, lambda i, place, lens: (0, 0, 0)),
            ),
        ),
        compiler_params=kernel_params(),
        cost_estimate=cost(3),
        name="packed",
    )(place, lengths, qkv_weight, up_weight, tokens, cotangent, *vectors)


def attend(h1, dy, weight, spots, out, bias, cosine, sine, lengths, after, rows=128):
    total, width = h1.shape
    count = len(dy)
    head = out.shape[0]
    scale = head ** (-0.5)

    parts = len(weight)

    def body(len_ref, spot_ref, b_ref, *refs):
        w_refs, refs = refs[:parts], refs[parts:]
        dy_refs = refs[:count]
        h1_hbm, out_hbm, cos_hbm, sin_hbm = refs[count : count + 4]
        ol_hbm, dq_hbm, sum_ref = refs[count + 4 : count + 7]
        (dy_v, h1_v, w_v, wo_v, cos_v, sin_v, qkv_v, do_v, ol_v, dq_v, dy_sem, w_sem, sems) = (
            refs[count + 7 :]
        )
        pairs = (
            (h1_hbm, h1_v),
            (out_hbm, wo_v),
            (cos_hbm, cos_v),
            (sin_hbm, sin_v),
        )
        copies = loads(
            [pltpu.make_async_copy(*pair, sems.at[n]) for n, pair in enumerate(pairs)]
        )
        w_copies = loads(
            weight_copies(weight, w_refs, spot_ref, w_v, pl.ds(0, 3 * head), w_sem)
        )
        dy_copies = loads(piece_copies(dy_refs, 1, dy_v, dy_sem, rows))
        for copy in copies[:1] + w_copies:
            copy.wait()

        @pl.loop(0, 3)
        def _(n):
            at = pl.ds(pl.multiple_of(n * head, head), head)
            qkv_v[:, at] = dot(h1_v[...], w_v[:, :, :, at].reshape(width, head)) + b_ref[n]

        for copy in copies[1:] + dy_copies:
            copy.wait()
        do_v[...] = dot(dy_v[...], wo_v[...], 1, 1).astype(bf16)
        sum_ref[...] = jnp.zeros_like(sum_ref)

        @pl.loop(0, total // rows, unroll=2)
        def _(block):
            at = pl.ds(pl.multiple_of(block * rows, rows), rows)
            cos, sin = cos_v[at, :], sin_v[at, :]

            def turned(value, sign):
                left = value[:, :128]
                left = left * cos + swap_halves(left) * (sin * sign)
                return jnp.concatenate([left, value[:, 128:]], 1).astype(bf16)

            q, k = turned(qkv_v[at, 0:head], 1.0), turned(qkv_v[at, head : 2 * head], 1.0)
            v = qkv_v[at, 2 * head :].astype(bf16)
            scores = dot(q, k, 1, 1) * scale
            masked = jnp.where(allowed_mask(len_ref, block, rows), scores, -1e30)
            shifted = jnp.exp(masked - jnp.max(masked, 1, keepdims=True))
            probs = shifted / jnp.sum(shifted, 1, keepdims=True)
            low = probs.astype(bf16)
            ol_v[at, :] = dot(low, v).astype(bf16)
            d_out = do_v[at, :]
            d_value = dot(low, d_out, 0, 0)
            d_probs = dot(d_out, v, 1, 1)
            centred = d_probs - jnp.sum(d_probs * probs, 1, keepdims=True)
            d_scores = (probs * centred).astype(bf16)
            d_query = turned(dot(d_scores, k) * scale, -1.0)
            d_key = turned(dot(d_scores, q, 0, 0) * scale, -1.0)
            for n, grad in enumerate((d_query, d_key, d_value.astype(bf16))):
                lanes = slice(n * head, (n + 1) * head)
                dq_v[at, lanes] = grad
                sum_ref[:, lanes] += jnp.sum(grad.astype(f32), 0, keepdims=True)

        ol_copy = pltpu.make_async_copy(ol_v, ol_hbm, sems.at[0])
        ol_copy.start()
        dq_copy = pltpu.make_async_copy(dq_v, dq_hbm, sems.at[1])
        dq_copy.start()

        for copy in (ol_copy, dq_copy):
            copy.wait()

    vmem = pl.BlockSpec(memory_space=pltpu.VMEM)
    smem = pl.BlockSpec(memory_space=pltpu.SMEM)
    return pl.pallas_call(
        after_inputs(body, 7 + parts + count, len(after)),
        out_shape=(
            jax.ShapeDtypeStruct((total, head), bf16),
            jax.ShapeDtypeStruct((total, 3 * head), bf16),
            jax.ShapeDtypeStruct((1, 3 * head), f32),
        ),
        in_specs=[smem, smem, vmem] + anywhere(parts + count + 4 + len(after)),
        out_specs=tuple(anywhere(2)) + (vmem,),
        scratch_shapes=[
            pltpu.VMEM((total, width), bf16),
            pltpu.VMEM((total, width), bf16),
            pltpu.VMEM((8, 8, width // 64, 3 * head), bf16),
            pltpu.VMEM((head, width), bf16),
            pltpu.VMEM((total, 128), f32),
            pltpu.VMEM((total, 128), f32),
            pltpu.VMEM((total, 3 * head), f32),
            pltpu.VMEM((total, head), bf16),
            pltpu.VMEM((total, head), bf16),
            pltpu.VMEM((total, 3 * head), bf16),
            pltpu.SemaphoreType.DMA((count,)),
            pltpu.SemaphoreType.DMA((parts,)),
            pltpu.SemaphoreType.DMA((4,)),
        ],
        compiler_params=kernel_params(),
        cost_estimate=cost(17),
        name="attend",
    )(
        lengths,
        spots,
        bias,
        *[p[0] for p in weight],
        *dy,
        h1,
        out,
        cosine,
        sine,
        *after,
    )


def attention_grads(h1, dy, d_qkv, attended, numbers, after):
    total, width = h1.shape
    count = len(dy)
    rows = total // count
    head = attended.shape[1]

    def body(number_ref, *refs):
        dy_refs = refs[:count]
        h1_hbm, dq_hbm, ol_hbm, keep_hbm, send_hbm = refs[count : count + 5]
        dy_v, h1_v, dq_v, ol_v, keep_v, send_v, dy_sem, sems = refs[count + 5 :]
        own = number_ref[0] == 0
        pairs = ((h1_hbm, h1_v), (dq_hbm, dq_v), (ol_hbm, ol_v))
        copies = loads(
            [pltpu.make_async_copy(*pair, sems.at[n]) for n, pair in enumerate(pairs)]
        )
        dy_copies = loads(piece_copies(dy_refs, 1, dy_v, dy_sem, rows))
        for copy in copies:
            copy.wait()

        def split(part, high, lanes):
            for z_hi in range(2):
                at = (pl.ds(4 * z_hi, 4), high, lanes)

                @pl.when(own)
                def _(z_hi=z_hi, at=at):
                    keep_v[at] = part[:, z_hi, 0]
                    send_v[at] = part[:, z_hi, 1]

                @pl.when(jnp.logical_not(own))
                def _(z_hi=z_hi, at=at):
                    keep_v[at] = part[:, z_hi, 1]
                    send_v[at] = part[:, z_hi, 0]

        @pl.loop(0, 8)
        def _(n):
            lanes = pl.ds(pl.multiple_of(n * 256, 256), 256)
            part = dot_rows(h1_v[:, lanes], dq_v[...]).astype(bf16).reshape(4, 2, 2, 16, 3 * head)
            for third in range(3):
                split(
                    part[..., third * head : (third + 1) * head],
                    pl.ds(16 * third, 16),
                    pl.ds(pl.multiple_of(n * head, head), head),
                )

        for copy in dy_copies:
            copy.wait()
        part = dot_rows(ol_v[...], dy_v[...]).astype(bf16).reshape(4, 2, 2, 16, width)
        split(part, pl.ds(48, 16), slice(None))
        keep_copy = pltpu.make_async_copy(keep_v, keep_hbm, sems.at[0])
        keep_copy.start()
        send_copy = pltpu.make_async_copy(send_v, send_hbm, sems.at[1])
        send_copy.start()
        keep_copy.wait()
        send_copy.wait()

    grads = jax.ShapeDtypeStruct((8, 64, width), bf16)
    return pl.pallas_call(
        after_inputs(body, 4 + count, len(after)),
        out_shape=(grads, grads),
        in_specs=[pl.BlockSpec(memory_space=pltpu.SMEM)] + anywhere(count + 3 + len(after)),
        out_specs=tuple(anywhere(2)),
        scratch_shapes=[
            pltpu.VMEM((total, width), bf16),
            pltpu.VMEM((total, width), bf16),
            pltpu.VMEM((total, 3 * head), bf16),
            pltpu.VMEM((total, head), bf16),
            pltpu.VMEM((8, 64, width), bf16),
            pltpu.VMEM((8, 64, width), bf16),
            pltpu.SemaphoreType.DMA((count,)),
            pltpu.SemaphoreType.DMA((3,)),
        ],
        compiler_params=kernel_params(),
        cost_estimate=cost(12),
        name="attention_grads",
    )(numbers, *dy, h1, d_qkv, attended, *after)


def mixed_part(active, attended, down, out, bias, after):
    rows, ff = active.shape
    head, width = out.shape
    step = 512
    count = rows // 128

    def body(act_ref, ol_ref, wd_ref, wo_ref, b_ref, *refs):
        total = dot(act_ref[...], wd_ref[...]) + dot(ol_ref[...], wo_ref[...]) + b_ref[...]
        for at in range(count):
            refs[at][...] = total[at * 128 : (at + 1) * 128].astype(bf16)

    return pl.pallas_call(
        after_inputs(body, 5, len(after)),
        out_shape=(jax.ShapeDtypeStruct((128, width), bf16),) * count,
        grid=(width // step,),
        in_specs=[
            pl.BlockSpec((rows, ff), lambda i: (0, 0)),
            pl.BlockSpec((rows, head), lambda i: (0, 0)),
            pl.BlockSpec((ff, step), lambda i: (0, i)),
            pl.BlockSpec((head, step), lambda i: (0, i)),
            pl.BlockSpec((1, step), lambda i: (0, i)),
        ]
        + anywhere(len(after)),
        out_specs=(pl.BlockSpec((128, step), lambda i: (0, i)),) * count,
        compiler_params=kernel_params(),
        cost_estimate=cost(10),
        name="mixed_part",
    )(active, attended, down, out, bias, *after)


def back_norms(d_qkv, d_hidden, weight, spots, x, mean, inverse, gains, after):
    total, n1 = d_qkv.shape
    n2 = d_hidden.shape[1]
    count = len(x)
    parts = len(weight)
    width = x[0].shape[-1]
    step = 512

    def body(spot_ref, m_ref, i_ref, g_ref, *refs):
        w_refs, refs = refs[:parts], refs[parts:]
        x_refs, refs = refs[:count], refs[count:]
        plain, sums_ref, outs = refs[:2], refs[2], refs[3 : 3 + count]
        dq_v, du_v, w_v, x_v, s_v, w_sem, x_sem, sems, out_sem = refs[3 + count :]
        plain_v = (dq_v, du_v)
        copies = loads(
            [
                pltpu.make_async_copy(plain[n], plain_v[n], sems.at[n]) for n in range(2)
            ]
            + weight_copies(weight, w_refs, spot_ref, w_v, slice(None), w_sem)
            + piece_copies(x_refs, 0, x_v, x_sem, 128)
        )
        def leaving(n):
            lanes = pl.ds(pl.multiple_of(n * step, step), step)
            return [
                pltpu.make_async_copy(
                    s_v.at[pl.ds(at * 128, 128), lanes], outs[at].at[:, lanes], out_sem.at[at]
                )
                for at in range(count)
            ]

        for copy in copies:
            copy.wait()

        @pl.loop(0, width // step)
        def _(n):
            lanes = pl.ds(pl.multiple_of(n * step, step), step)
            sources = pl.ds(n * (step // 256), step // 256)
            d1 = dot(dq_v[...], w_v[sources, :, :, 0:n1].reshape(step, n1), 1, 1)
            d2 = dot(du_v[...], w_v[sources, :, :, n1:].reshape(step, n2), 1, 1)
            s_v[:, lanes] = (d1 * g_ref[0:1, lanes] + d2 * g_ref[1:2, lanes]).astype(bf16)
            for copy in leaving(n):
                copy.start()
            normed = (x_v[:, lanes].astype(f32) - m_ref[...]) * i_ref[...]
            sums_ref[0:1, lanes] = jnp.sum(d1 * normed, 0, keepdims=True)
            sums_ref[1:2, lanes] = jnp.sum(d1, 0, keepdims=True)
            sums_ref[2:3, lanes] = jnp.sum(d2 * normed, 0, keepdims=True)
            sums_ref[3:4, lanes] = jnp.sum(d2, 0, keepdims=True)

        for n in range(width // step):
            for copy in leaving(n):
                copy.wait()

    vmem = pl.BlockSpec(memory_space=pltpu.VMEM)
    return pl.pallas_call(
        after_inputs(body, 6 + parts + count, len(after)),
        out_shape=(jax.ShapeDtypeStruct((4, width), f32),)
        + (jax.ShapeDtypeStruct((128, width), bf16),) * count,
        in_specs=[pl.BlockSpec(memory_space=pltpu.SMEM)]
        + [vmem] * 3
        + anywhere(parts + count + 2 + len(after)),
        out_specs=(vmem,) + tuple(anywhere(count)),
        scratch_shapes=[
            pltpu.VMEM((total, n1), bf16),
            pltpu.VMEM((total, n2), bf16),
            pltpu.VMEM((8, 8, width // 64, n1 + n2), bf16),
            pltpu.VMEM((total, width), bf16),
            pltpu.VMEM((total, width), bf16),
            pltpu.SemaphoreType.DMA((parts,)),
            pltpu.SemaphoreType.DMA((count,)),
            pltpu.SemaphoreType.DMA((2,)),
            pltpu.SemaphoreType.DMA((count,)),
        ],
        compiler_params=kernel_params(),
        cost_estimate=cost(15),
        name="back_norms",
    )(
        spots,
        mean,
        inverse,
        gains,
        *[p[0] for p in weight],
        *x,
        d_qkv,
        d_hidden,
        *after,
    )


def unpacked(part, after):
    owners, _, cols = part.shape

    def body(part_ref, rows_ref, info_ref):
        for owner in range(owners):
            rows_ref[owner] = part_ref[owner, 0:32]
            info_ref[owner] = part_ref[owner, 32:40].astype(f32)

    return pl.pallas_call(
        after_inputs(body, 1, len(after)),
        out_shape=(
            jax.ShapeDtypeStruct((owners, 32, cols), bf16),
            jax.ShapeDtypeStruct((owners, 8, cols), f32),
        ),
        in_specs=[pl.BlockSpec(memory_space=pltpu.VMEM)] + anywhere(len(after)),
        out_specs=(pl.BlockSpec(memory_space=pltpu.VMEM),) * 2,
        compiler_params=kernel_params(),
        cost_estimate=cost(3),
        name="unpacked",
    )(part, *after)


def joined(arrays, after):
    sizes = [array.shape[0] for array in arrays]
    unit = math.gcd(*sizes)
    block = (unit,) + arrays[0].shape[1:]
    count = len(arrays)
    firsts = [sum(sizes[:n]) // unit for n in range(count)]

    def body(*refs):
        step = pl.program_id(0)
        for ref, first, size in zip(refs, firsts, sizes):

            @pl.when((step >= first) & (step < first + size // unit))
            def _(ref=ref):
                refs[count][...] = ref[...]

    def came(first, size):
        return pl.BlockSpec(block, lambda i: (jnp.clip(i - first, 0, size // unit - 1), 0, 0))

    return pl.pallas_call(
        after_inputs(body, count, len(after)),
        out_shape=jax.ShapeDtypeStruct((sum(sizes),) + block[1:], bf16),
        grid=(sum(sizes) // unit,),
        in_specs=[came(first, size) for first, size in zip(firsts, sizes)] + anywhere(len(after)),
        out_specs=pl.BlockSpec(block, lambda i: (i, 0, 0)),
        compiler_params=kernel_params(),
        cost_estimate=cost(3),
        name="joined",
    )(*arrays, *after)


def halves(own, below, above, after):
    count, rows, cols = own.shape
    half = count // 2

    def body(own_ref, below_ref, above_ref, low_ref, high_ref, all_ref):
        step = pl.program_id(0)
        all_ref[0] = own_ref[...]
        all_ref[1] = above_ref[...]
        all_ref[2] = below_ref[...]

        @pl.when(step == 0)
        def _():
            low_ref[...] = below_ref[...]

        @pl.when(step == 1)
        def _():
            high_ref[...] = above_ref[...]

    block = pl.BlockSpec((half, rows, cols), lambda i: (i, 0, 0))
    whole = pl.BlockSpec((half, rows, cols), lambda i: (0, 0, 0))
    low, high, together = pl.pallas_call(
        after_inputs(body, 3, len(after)),
        out_shape=(jax.ShapeDtypeStruct((half, rows, cols), bf16),) * 2
        + (jax.ShapeDtypeStruct((3, count, rows, cols), bf16),),
        grid=(2,),
        in_specs=[block] * 3 + anywhere(len(after)),
        out_specs=(
            whole,
            whole,
            pl.BlockSpec((3, half, rows, cols), lambda i: (0, i, 0, 0)),
        ),
        compiler_params=kernel_params(),
        cost_estimate=cost(4),
        name="halves",
    )(own, below, above, *after)
    return low, high, together.reshape(3 * count, rows, cols)


def finished(mix, sums, tokens, cotangent, after):
    rows, width = tokens.shape
    step = rows // 2

    def body(*refs):
        x_ref, dy_ref, mixed_ref, grad_ref = refs[8:]
        x = x_ref[...].astype(f32)
        mixed_ref[...] = (x + wide(*refs[:4])).astype(bf16)
        gain = wide(*refs[4:8])
        centre = x - jnp.mean(x, 1, keepdims=True)
        inverse = lax.rsqrt(jnp.mean(centre * centre, 1, keepdims=True) + EPS)
        normed = centre * inverse
        grad_ref[...] = dy_ref[...].astype(f32) + inverse * (
            gain
            - jnp.mean(gain, 1, keepdims=True)
            - normed * jnp.mean(gain * normed, 1, keepdims=True)
        )

    block = pl.BlockSpec((step, width), lambda i: (i, 0))
    later = pl.BlockSpec((step, width), lambda i: (i + 2, 0))
    return pl.pallas_call(
        after_inputs(body, 10, len(after)),
        out_shape=(
            jax.ShapeDtypeStruct((rows, width), bf16),
            jax.ShapeDtypeStruct((rows, width), f32),
        ),
        grid=(2,),
        in_specs=[block, later, block, block] * 2 + [block, block] + anywhere(len(after)),
        out_specs=(block, block),
        compiler_params=kernel_params(),
        cost_estimate=cost(3),
        name="finished",
    )(*mix, *sums, tokens, cotangent, *after)


def packed_sums(stays, crossed, own, below, above, norm_sums, qkv_sums, up_sums, dy_sums, numbers, ff, head, after):
    width = own.shape[1]

    def body(*refs):
        stay_ref, cross_ref, own_ref, below_ref, above_ref = refs[:5]
        norm_ref, q_ref, u_ref, y_ref, number_ref, out_ref, keep_ref, small = refs[5:]
        shard = number_ref[1]
        inner = (stay_ref[0].astype(f32) + cross_ref[0].astype(f32)).astype(bf16)
        total = wide(own_ref, below_ref, above_ref).astype(bf16)
        for owner in range(8):
            mine = shard == owner
            small[...] = jnp.zeros_like(small)
            small[0:4] = norm_ref[:, owner * head : (owner + 1) * head]
            for n in range(3):
                third, source = divmod(owner * 3 + n, 8)
                lanes = slice(third * head, (third + 1) * head)
                small[4 + n : 5 + n] = jnp.where(shard == source, q_ref[:, lanes], 0.0)
            for n in range(4):
                lanes = slice(n * head, (n + 1) * head)
                small[7 + n : 8 + n] = jnp.where(mine, u_ref[:, lanes], 0.0)
            small[11:12] = jnp.where(mine, y_ref[...], 0.0)
            pieces = [
                total[16 * third : 16 * third + 16, owner * head : (owner + 1) * head]
                for third in range(3)
            ]
            row, col = 64 + 16 * (owner % 4), owner // 4 * ff
            pieces.append(inner[row : row + 16, col : col + ff])
            pieces.append(small[...].astype(bf16))
            out_ref[owner] = jnp.concatenate(pieces, 1)
        keep_ref[0:64] = inner[0:64]
        keep_ref[64:80] = total[48:64]

    vmem = pl.BlockSpec(memory_space=pltpu.VMEM)
    return pl.pallas_call(
        after_inputs(body, 10, len(after)),
        out_shape=(
            jax.ShapeDtypeStruct((8, 16, 4 * head + ff), bf16),
            jax.ShapeDtypeStruct((80, width), bf16),
        ),
        in_specs=[vmem] * 9 + [pl.BlockSpec(memory_space=pltpu.SMEM)] + anywhere(len(after)),
        out_specs=(vmem,) * 2,
        scratch_shapes=[pltpu.VMEM((16, head), f32)],
        compiler_params=kernel_params(),
        cost_estimate=cost(3),
        name="packed_sums",
    )(stays, crossed, own, below, above, norm_sums, qkv_sums, up_sums, dy_sums, numbers, *after)


def unpacked_sums(received, cols, after):
    sources, rows, width = received.shape

    def body(part_ref, out_ref):
        small = jnp.sum(part_ref[:, :, cols:].astype(f32), 0).astype(bf16)
        out_ref[0] = jnp.concatenate(
            [jnp.concatenate([part_ref[0, :, 0:cols], small], 1)]
            + [part_ref[n] for n in range(1, sources)],
            0,
        )

    vmem = pl.BlockSpec(memory_space=pltpu.VMEM)
    return pl.pallas_call(
        after_inputs(body, 1, len(after)),
        out_shape=jax.ShapeDtypeStruct((1, sources * rows, width), bf16),
        in_specs=[vmem] + anywhere(len(after)),
        out_specs=vmem,
        compiler_params=kernel_params(),
        cost_estimate=cost(3),
        name="unpacked_sums",
    )(received, *after)


def blocks_call(name, body, numbers, terms, outs, after, time=3):
    def came(block, index):
        rest = (0,) * (len(block) - 1)
        return pl.BlockSpec(block, lambda i, n: (index(n),) + rest)

    return pl.pallas_call(
        after_inputs(body, 1 + len(terms), len(after)),
        out_shape=tuple(jax.ShapeDtypeStruct(out, bf16) for out in outs),
        grid_spec=pltpu.PrefetchScalarGridSpec(
            num_scalar_prefetch=1,
            grid=(1,),
            in_specs=[came(block, index) for _, block, index in terms] + anywhere(len(after)),
            out_specs=tuple(
                pl.BlockSpec(out, lambda i, n, size=len(out): (0,) * size) for out in outs
            ),
        ),
        compiler_params=kernel_params(),
        cost_estimate=cost(time),
        name=name,
    )(numbers, *[array for array, _, _ in terms], *after)


def wide(*refs):
    return functools.reduce(jnp.add, [ref[...].astype(f32) for ref in refs])


def spread(pieces, places, core, targets, count, before, after):
    rows, cols = pieces[0][0].shape[1:]
    firsts, total = [], 0
    for mine, _ in pieces:
        firsts.append(total)
        total += mine.shape[0]

    def body(place_ref, core_ref, *refs):
        step = pl.program_id(0)
        outs = refs[2 * len(pieces) + len(before) :]
        first_core = core_ref[0] == 0

        def fill(ref, low):
            for out_ref, (_, high, parts) in zip(outs, targets):
                for to, row, col, size in parts:
                    out_ref[low * high : (low + 1) * high, to : to + size] = ref[
                        0, row : row + high, col : col + size
                    ].astype(f32)

        for n, (first, (mine, _)) in enumerate(zip(firsts, pieces)):
            here = (step >= first) & (step < first + mine.shape[0])

            @pl.when(here & first_core)
            def _(n=n):
                fill(refs[2 * n], 0)
                fill(refs[2 * n + 1], 1)

            @pl.when(here & jnp.logical_not(first_core))
            def _(n=n):
                fill(refs[2 * n], 1)
                fill(refs[2 * n + 1], 0)

    def chosen(first, size):
        return pl.BlockSpec(
            (1, rows, cols), lambda i, place, core: (jnp.clip(i - first, 0, size - 1), 0, 0)
        )

    specs, arrays = [], []
    for first, (mine, yours) in zip(firsts, pieces):
        specs += [chosen(first, mine.shape[0])] * 2
        arrays += [mine, yours]
    return pl.pallas_call(
        after_inputs(body, 2 + 2 * len(pieces) + len(before), len(after)),
        out_shape=tuple(
            jax.ShapeDtypeStruct((2 * count * high, wide), f32) for wide, high, _ in targets
        ),
        grid_spec=pltpu.PrefetchScalarGridSpec(
            num_scalar_prefetch=2,
            grid=(total,),
            in_specs=specs + anywhere(len(before) + len(after)),
            out_specs=tuple(
                pl.BlockSpec((2 * high, wide), lambda i, place, core: (place[i], 0))
                for wide, high, _ in targets
            ),
        ),
        input_output_aliases={2 + len(arrays) + n: n for n in range(len(before))},
        compiler_params=kernel_params(),
        cost_estimate=cost(0.3 * total),
        name="spread",
    )(places, core, *arrays, *before, *after)


def local(
    tokens,
    doc_lengths,
    cotangent,
    ln1_gain,
    ln1_bias,
    ln2_gain,
    ln2_bias,
    qkv_weight,
    qkv_bias,
    out_weight,
    out_bias,
    up_weight,
    up_bias,
    down_weight,
    down_bias,
):
    rows, width = tokens.shape
    head = width // HEADS
    group = 8
    rep = lax.axis_index("rep")
    shard = lax.axis_index("shard")
    y, h, c = rep // 4, (rep // 2) % 2, rep % 2
    l, x = shard // 4, shard % 4
    ff = up_bias.shape[0]

    cols = 3 * head + ff
    vectors = [ln1_gain, ln1_bias, ln2_gain, ln2_bias, qkv_bias]
    place = (y * 2 + c).astype(jnp.int32).reshape(1)
    part, pair = packed(
        qkv_weight, up_weight, vectors, doc_lengths, place, head, tokens, cotangent
    )
    below, above, other = move(pair, x=1), move(pair, x=-1), move(pair, l=1)
    far, other_above, other_below = move(below, x=1), move(other, x=-1), move(below, l=1)
    pairs = (pair, above, far, below, other, other_above, None, other_below)

    part = lax.all_to_all(part, "shard", 0, 0)
    own, infos = unpacked(part, (pairs[1], pairs[3], pairs[4]))
    below, above = move(own, y=1), move(own, y=-1)
    x_other_far, dy_other_far = move(other_below[0], x=1), move(other_above[1], x=-1)
    low, high, yours = halves(own, below, above, (far, other_above, other_below))
    far_low, far_high = move(low, y=1), move(high, y=-1)
    x_all = tuple(x_other_far if p is None else p for p in pairs)
    dy_all = tuple(dy_other_far if p is None else p for p in pairs)
    yours = move(yours, c=1)
    far_low_c, far_high_c = move(far_low, c=1), move(far_high, c=1)
    weight = (
        (own, 0, 8, 0, 0),
        (above, 0, 8, 0, 1),
        (far_low, 0, 4, 0, 2),
        (far_high, 0, 4, 4, 2),
        (below, 0, 8, 0, 3),
        (yours, 0, 8, 0, 4),
        (yours, 8, 8, 0, 5),
        (far_low_c, 0, 4, 0, 6),
        (far_high_c, 0, 4, 4, 6),
        (yours, 16, 8, 0, 7),
    )
    steps4 = (y + jnp.arange(4)) % 4
    spots = jnp.concatenate([steps4 * 2 + c, steps4 * 2 + 1 - c]).astype(jnp.int32)

    gains = infos[:, 0, :1024].reshape(8, 4, 256).transpose(1, 0, 2).reshape(4, width)
    qkv_b = infos[:, 0, 1024:].reshape(8 * 3, 1, head)
    qkv_b = jnp.stack(
        [lax.dynamic_index_in_dim(qkv_b, third * 8 + shard, 0, False) for third in range(3)]
    )
    steps8 = jnp.arange(8)
    sources = ((steps8 // 4) ^ l) * 4 + (x + steps8 % 4) % 4
    sources = sources.astype(jnp.int32)
    lengths = infos[:, 1, :3]
    lengths = jnp.sum(
        jnp.where(sources[:, None, None] == steps8[None, :, None], lengths[None], 0.0), 1
    ).astype(jnp.int32)
    ends = jnp.cumsum(lengths, 1)
    starts = ends - lengths
    steps_t = jnp.arange(rows, dtype=jnp.int32)
    segment = jnp.sum((steps_t[None, :, None] >= ends[:, None, :]).astype(jnp.int32), -1)
    slots = jnp.arange(lengths.shape[1], dtype=jnp.int32)
    begin = jnp.sum(
        jnp.where(segment[:, :, None] == slots[None, None, :], starts[:, None, :], 0), -1
    )
    position = (steps_t[None, :] - begin).astype(f32).reshape(group * rows, 1)
    lane = jnp.arange(128)
    freq = 10000.0 ** (-2.0 * (lane % (ROT // 2)).astype(f32) / ROT)
    angle = position * freq[None, :]
    cosine = jnp.where(lane < ROT, jnp.cos(angle), 1.0)
    sine = jnp.sin(angle)
    sine = jnp.where(lane < ROT // 2, -sine, jnp.where(lane < ROT, sine, 0.0))

    both_bias = (out_bias.astype(f32) + down_bias.astype(f32))[None, :]
    wide_bias = lax.dynamic_update_slice(jnp.zeros((1, width), f32), both_bias, (0, shard * 256))
    numbers = jnp.stack([c, shard, y, h]).astype(jnp.int32)

    h1, active, d_hidden, keep, send, mean, inverse, up_sums, dy_sums = feed_forward(
        x_all,
        dy_all,
        gains,
        weight,
        spots,
        down_weight,
        up_bias.astype(f32)[None],
        numbers,
        3 * head,
        (cosine, sine),
    )
    got = move(send, c=1)
    attended, d_qkv, qkv_sums = attend(
        h1, dy_all, weight, spots, out_weight, qkv_b, cosine, sine, lengths, (send,)
    )

    pair_shape, one = (2, 128, width), (1, 128, width)

    def turn(k):
        return lambda n: (n[2] + k) % 4

    def far_body(n_ref, keep_ref, got_ref, low_ref, high_ref):
        total = wide(keep_ref, got_ref).astype(bf16)
        low_ref[0] = total[0]
        high_ref[0] = total[1]

    low, high = blocks_call(
        "far_sums",
        far_body,
        numbers,
        [(keep, pair_shape, turn(2)), (got, pair_shape, turn(2))],
        (one, one),
        (attended,),
    )
    from_low, from_high = move(low, y=1), move(high, y=-1)
    a_keep, a_send = attention_grads(h1, dy_all, d_qkv, attended, numbers, (low, high))
    a_got = move(a_send, c=1)
    def near_body(n_ref, k1_ref, g1_ref, k3_ref, g3_ref, low_ref, high_ref, above_ref, below_ref):
        above, below = wide(k1_ref, g1_ref), wide(k3_ref, g3_ref)
        above_ref[0] = (above[0] + low_ref[0].astype(f32)).astype(bf16)
        above_ref[1] = above[1].astype(bf16)
        below_ref[0] = below[0].astype(bf16)
        below_ref[1] = (below[1] + high_ref[0].astype(f32)).astype(bf16)

    above, below = blocks_call(
        "near_sums",
        near_body,
        numbers,
        [(v, pair_shape, turn(k)) for k in (1, 3) for v in (keep, got)]
        + [(v, one, lambda n: 0) for v in (from_low, from_high)],
        (pair_shape, pair_shape),
        (a_send,),
        20,
    )
    from_below, from_above = move(above, y=1), move(below, y=-1)

    four, part_shape = (4, 64, width), (1, 64, width)

    def away_body(n_ref, keep_ref, got_ref, out_ref):
        out_ref[...] = wide(keep_ref, got_ref).astype(bf16)

    (a_away,) = blocks_call(
        "away_sums",
        away_body,
        numbers,
        [(v, four, lambda n: 1 - n[3]) for v in (a_keep, a_got)],
        (four,),
        (above,),
    )
    a_crossed = move(a_away, h=1)
    mix = mixed_part(active, attended, down_weight, out_weight, wide_bias, (a_away, above, below))
    norm_sums, *sums = back_norms(
        d_qkv,
        d_hidden,
        weight,
        spots,
        x_all,
        mean,
        inverse,
        jnp.stack([gains[0], gains[2]]),
        (mix[0],),
    )

    flat, both = (128, width), (256, width)

    def passed_body(n_ref, up_ref, from_below, here_ref, down_ref, from_above, there_ref, up_out, down_out):
        up_out[0:128] = wide(up_ref, from_below).astype(bf16)
        up_out[128:256] = here_ref[...]
        down_out[0:128] = wide(down_ref, from_above).astype(bf16)
        down_out[128:256] = there_ref[...]

    def other_body(n_ref, own_ref, below_ref, above_ref, *refs):
        passing = len(refs) // 2
        refs[passing][...] = wide(own_ref, below_ref, above_ref).astype(bf16)
        for at in range(passing):
            refs[passing + 1 + at][...] = refs[at][...]

    def first(n):
        return 0

    def ring_start(high, low):
        return move(high, x=1), move(low, x=-1)

    def ring_middle(pieces, passed, after):
        operands = (pieces[5], passed[0], pieces[1], pieces[3], passed[1], pieces[7])
        ups, downs = blocks_call(
            "passed_sums",
            passed_body,
            numbers,
            [(v, flat, first) for v in operands],
            (both, both),
            after,
        )
        return (move(ups, x=1), move(downs, x=-1)), ups

    def ring_end(pieces, arrived, passing):
        other, *copies = blocks_call(
            "other_sums",
            other_body,
            numbers,
            [
                (pieces[4], flat, first),
                (arrived[0], flat, first),
                (arrived[1], flat, lambda n: 1),
            ]
            + [(v, flat, first) for v in passing],
            (flat,) * (1 + len(passing)),
            (),
        )
        return (pieces[0], *arrived, move(other, l=1)), other, *copies

    mix_passed = ring_start(mix[6], mix[2])
    mix_arrived, mix_ups = ring_middle(mix, mix_passed, (norm_sums,))

    def ends_body(n_ref, keep_ref, got_ref, below_ref, above_ref, leave_ref, stay_ref):
        total = wide(keep_ref, got_ref, below_ref, above_ref).astype(bf16)
        first = n_ref[3] == 0
        leave_ref[0] = jnp.where(first, total[1], total[0])
        stay_ref[0] = jnp.where(first, total[0], total[1])

    leaves, stays = blocks_call(
        "end_sums",
        ends_body,
        numbers,
        [(v, pair_shape, turn(0)) for v in (keep, got)]
        + [(v, pair_shape, lambda n: 0) for v in (from_below, from_above)],
        (one, one),
        (mix_ups,),
    )
    crossed = move(leaves, h=1)

    def around_body(n_ref, keep_ref, got_ref, crossed_ref, low_ref, high_ref, above_ref, own_ref, below_ref):
        def part(k):
            at = (n_ref[2] + k) % 4
            return wide(keep_ref.at[at], got_ref.at[at], crossed_ref.at[at]).astype(bf16)

        far = part(2)
        low_ref[...] = far[:32]
        high_ref[...] = far[32:]
        above_ref[...] = part(1)
        own_ref[...] = part(0)
        below_ref[...] = part(3)

    a_low, a_high, a_above, a_own, a_below = blocks_call(
        "around_sums",
        around_body,
        numbers,
        [(v, four, lambda n: n[3]) for v in (a_keep, a_got)] + [(a_crossed, four, lambda n: 0)],
        ((32, width), (32, width), (64, width), (64, width), (64, width)),
        (leaves,),
    )
    a_low, a_high = move(a_low, y=1), move(a_high, y=-1)

    def beside_body(n_ref, above_ref, below_ref, low_ref, high_ref, up_ref, down_ref):
        up_ref[0:32] = (above_ref[0:32].astype(f32) + low_ref[...].astype(f32)).astype(bf16)
        up_ref[32:64] = above_ref[32:64]
        down_ref[0:32] = below_ref[0:32]
        down_ref[32:64] = (below_ref[32:64].astype(f32) + high_ref[...].astype(f32)).astype(bf16)

    a_above, a_below = blocks_call(
        "beside_sums",
        beside_body,
        numbers,
        [(v, v.shape, lambda n: 0) for v in (a_above, a_below, a_low, a_high)],
        ((64, width), (64, width)),
        (crossed,),
    )
    a_from_below, a_from_above = move(a_above, y=1), move(a_below, y=-1)

    part, stays = packed_sums(
        stays,
        crossed,
        a_own,
        a_from_below,
        a_from_above,
        norm_sums,
        qkv_sums,
        up_sums,
        dy_sums,
        numbers,
        ff,
        head,
        (),
    )
    received = lax.all_to_all(part, "shard", 0, 0)
    mix_left, mix_other, high, low = ring_end(mix, mix_arrived, (sums[6], sums[2]))
    part = unpacked_sums(received, cols, (mix_other,))
    sums_arrived, sums_ups = ring_middle(sums, ring_start(high, low), (received,))
    sums_left, sums_other = ring_end(sums, sums_arrived, ())

    order = ((0, h), (0, 1 - h), (1, h), (1, 1 - h), (3, h), (3, 1 - h), (2, h), (2, 1 - h))
    places = jnp.stack([(y + k) % 4 * 2 + high for k, high in order]).astype(jnp.int32)

    def rep_gather(own, after):
        own = jnp.concatenate([own, move(own, h=1)])
        below, above = move(own, y=1), move(own, y=-1)
        low, high, near = halves(own, below, above, after)
        return near, (move(low, y=1), move(high, y=-1))

    near, far = rep_gather(stays[None], ())
    stays = joined((near, *far), ())
    down_grad, out_grad = spread(
        [(stays, move(stays, c=1))],
        places,
        numbers[:1],
        [(width, 64, [(0, 0, 0, width)]), (width, 16, [(0, 64, 0, width)])],
        8,
        (),
        (mix_left[3],),
    )
    near, far = rep_gather(part, (stays, sums_other, mix_left[3]))
    targets = [
        (
            3 * width,
            16,
            [
                ((third * 8 + source) * head, 16 * source, third * head, head)
                for source in range(8)
                for third in range(3)
            ],
        ),
        (8 * ff, 16, [(source * ff, 16 * source, 3 * head, ff) for source in range(8)]),
    ]
    near_yours = move(near, c=1)
    grads = spread(
        [(near, near_yours)], places[:6], numbers[:1], targets, 8, (), (down_grad, sums_left[3])
    )
    far = joined(far, (grads[0],))
    mixed, tokens_grad = finished(mix_left, sums_left, tokens, cotangent, (far,))
    far_yours = move(far, c=1)
    qkv_grad, up_grad = spread(
        [(far, far_yours)],
        places[6:],
        numbers[:1],
        targets,
        8,
        grads,
        (tokens_grad,),
    )
    smalls = [v[:, 0:16, cols:] for v in (near, near_yours, far, far_yours)]
    smalls = jnp.sum(jnp.concatenate(smalls).astype(f32), 0)
    norm_grads = smalls[:4]
    dy_total = smalls[11]
    return (
        mixed,
        tokens_grad,
        norm_grads[0],
        norm_grads[1],
        norm_grads[2],
        norm_grads[3],
        qkv_grad,
        smalls[4:7].reshape(3 * head),
        out_grad,
        dy_total,
        up_grad,
        smalls[7:11].reshape(ff),
        down_grad,
        dy_total,
    )


def solution(mesh):
    rows = P(BOTH, None)
    vector, matrix = P("shard"), P("shard", None)
    return jax.shard_map(
        local,
        mesh=mesh,
        in_specs=(rows, rows, rows, vector, vector, vector, vector)
        + (matrix, vector, matrix, vector, matrix, vector, matrix, vector),
        out_specs=(rows, rows, vector, vector, vector, vector)
        + (matrix, vector, matrix, vector, matrix, vector, matrix, vector),
        check_vma=False,
    )
```

```python
import functools
import math

import jax
import jax.numpy as jnp
from jax import lax
from jax.experimental import pallas as pl
from jax.experimental.pallas import tpu as pltpu
from jax.sharding import PartitionSpec as P

HEADS = 8
ROT = 64
EPS = 1e-05
f32 = jnp.float32
bf16 = jnp.bfloat16


def cost(time):
    return pl.CostEstimate(flops=int(time * 1.15e9), bytes_accessed=1000, transcendentals=0)


BOTH = ("rep", "shard")
SIZES = (4, 2, 2, 2, 4)
SAME_CORE = [[2 * n + c for n in range(8)] for c in range(2)]
SAME_CORE_ALL = [[(2 * n + c) * 8 + s for n in range(8) for s in range(8)] for c in range(2)]


def coords():
    for y in range(4):
        for h in range(2):
            for c in range(2):
                for l in range(2):
                    for x in range(4):
                        yield (y, h, c, l, x)


def linear(t):
    y, h, c, l, x = (v % m for v, m in zip(t, SIZES))
    return ((y * 2 + h) * 2 + c) * 8 + l * 4 + x


def move(value, y=0, h=0, c=0, l=0, x=0):
    step = (y, h, c, l, x)
    pairs = [(linear(t), linear(tuple(a + b for a, b in zip(t, step)))) for t in coords()]
    return lax.ppermute(value, BOTH, pairs)


def pick(value, index, axis):
    return lax.dynamic_index_in_dim(value, index, axis, keepdims=False)


def kernel_params():
    return pltpu.CompilerParams(vmem_limit_bytes=56 * 1024 * 1024)


def after_inputs(body, count, extra):
    return lambda *refs: body(*refs[:count], *refs[count + extra :])


def anywhere(count):
    return [pl.BlockSpec(memory_space=pl.ANY)] * count


def dot(a, b, ca=1, cb=0):
    return lax.dot_general(a, b, (((ca,), (cb,)), ((), ())), preferred_element_type=f32)


def swap_halves(value):
    lane = lax.broadcasted_iota(jnp.int32, value.shape, 1)
    return jnp.where(lane < 32, pltpu.roll(value, 96, 1), pltpu.roll(value, 32, 1))


def allowed_mask(lengths_ref, block, rows):
    e0 = lengths_ref[block, 0]
    e1 = e0 + lengths_ref[block, 1]
    t = lax.broadcasted_iota(jnp.int32, (rows, rows), 0)
    s = lax.broadcasted_iota(jnp.int32, (rows, rows), 1)
    seg_t = (t >= e0).astype(jnp.int32) + (t >= e1).astype(jnp.int32)
    seg_s = (s >= e0).astype(jnp.int32) + (s >= e1).astype(jnp.int32)
    return (seg_t == seg_s) & (s <= t)


def dot_rows(a, b):
    return lax.dot_general(a, b, (((0,), (0,)), ((), ())), preferred_element_type=f32)


def loads(copies):
    for copy in copies:
        copy.start()
    return copies


def piece_copies(pieces, half, target, sems, rows, lanes=slice(None)):
    return [
        pltpu.make_async_copy(
            piece.at[half, :, lanes] if len(piece.shape) == 3 else piece.at[:, lanes],
            target.at[pl.ds(at * rows, rows)],
            sems.at[at],
        )
        for at, piece in enumerate(pieces)
    ]


def weight_copies(pieces, refs, spot_ref, target, lanes, sems, source=None):
    if source is not None:
        pieces = [
            (
                array,
                begin + max(source - first, 0),
                min(size, 4),
                max(first, source) - source,
                spot,
                ref,
            )
            for (array, begin, size, first, spot), ref in zip(pieces, refs)
            if first <= source < first + size
        ]
    else:
        pieces = [(*piece, ref) for piece, ref in zip(pieces, refs)]
    return [
        pltpu.make_async_copy(
            ref.at[pl.ds(begin, size), :, lanes],
            target.at[pl.ds(first, size), spot_ref[spot]],
            sems.at[at],
        )
        for at, (_, begin, size, first, spot, ref) in enumerate(pieces)
    ]


def feed_forward(x, dy, gains, weight, spots, down, bias, numbers, first, after):
    rows, width = x[0].shape[1:]
    count = len(x)
    total = rows * count
    ff = bias.shape[1]

    parts = len(weight)

    def body(number_ref, spot_ref, g_ref, b_ref, *refs):
        w_refs, refs = refs[:parts], refs[parts:]
        x_refs, dy_refs, d_hbm = refs[:count], refs[count : 2 * count], refs[2 * count]
        (h1_hbm, act_hbm, du_hbm, keep_hbm, send_hbm, m_ref, i_ref, db_ref, sum_ref) = refs[
            2 * count + 1 : 2 * count + 10
        ]
        (x_v, dy_v, h1_v, h2_v, w_v, d_v, act_v, du_v, keep_v, send_v, x_sem, dy_sem, w_sem, sems) = refs[
            2 * count + 10 :
        ]
        own = number_ref[0] == 0
        x_copies = loads(piece_copies(x_refs, 0, x_v, x_sem, rows))
        w_copies = loads(
            weight_copies(weight, w_refs, spot_ref, w_v, pl.ds(first, ff), w_sem)
        )
        dy_copies = loads(piece_copies(dy_refs, 1, dy_v, dy_sem, rows))
        d_copy = pltpu.make_async_copy(d_hbm, d_v, sems.at[1])
        d_copy.start()
        for copy in x_copies:
            copy.wait()

        @pl.loop(0, count)
        def _(n):
            at = pl.ds(pl.multiple_of(n * rows, rows), rows)
            value = x_v[at, :].astype(f32)
            mean = jnp.mean(value, 1, keepdims=True)
            centre = value - mean
            inverse = lax.rsqrt(jnp.mean(centre * centre, 1, keepdims=True) + EPS)
            normed = centre * inverse
            m_ref[at, :] = mean
            i_ref[at, :] = inverse
            h1_v[at, :] = (normed * g_ref[0:1] + g_ref[1:2]).astype(bf16)
            h2_v[at, :] = (normed * g_ref[2:3] + g_ref[3:4]).astype(bf16)

        h1_copy = pltpu.make_async_copy(h1_v, h1_hbm, sems.at[2])
        h1_copy.start()
        for copy in w_copies + dy_copies:
            copy.wait()
        d_copy.wait()
        mine = dy_v[:, pl.ds(pl.multiple_of(number_ref[1] * 256, 256), 256)]
        sum_ref[...] = jnp.sum(mine.astype(f32), 0, keepdims=True)

        def split(part, places, high, wide):
            at = (places, high, wide)

            @pl.when(own)
            def _():
                keep_v[at] = part[:, 0]
                send_v[at] = part[:, 1]

            @pl.when(jnp.logical_not(own))
            def _():
                keep_v[at] = part[:, 1]
                send_v[at] = part[:, 0]

        def leaving(n):
            at = (pl.ds(n * 2, 2), pl.ds(0, 64))
            return (
                pltpu.make_async_copy(keep_v.at[at], keep_hbm.at[at], sems.at[3]),
                pltpu.make_async_copy(send_v.at[at], send_hbm.at[at], sems.at[4]),
            )

        @pl.loop(0, ff // 256)
        def _(n):
            at = pl.ds(pl.multiple_of(n * 256, 256), 256)
            u = dot(h2_v[...], w_v[:, :, :, at].reshape(width, 256)) + b_ref[:, at]
            cdf = 0.5 * (1.0 + lax.erf(u * math.sqrt(0.5)))
            pdf = jnp.exp(-0.5 * u * u) * (1.0 / math.sqrt(2.0 * math.pi))
            act = (u * cdf).astype(bf16)
            act_v[:, at] = act
            du = (dot(dy_v[...], d_v[at, :], 1, 1) * (cdf + u * pdf)).astype(bf16)
            du_v[:, at] = du
            db_ref[:, at] = jnp.sum(du.astype(f32), 0, keepdims=True)
            part = dot_rows(act, dy_v[...]).astype(bf16).reshape(2, 2, 64, width)
            split(part, pl.ds(n * 2, 2), pl.ds(0, 64), slice(None))
            for copy in leaving(n):
                copy.start()

        act_copy = pltpu.make_async_copy(act_v, act_hbm, sems.at[0])
        act_copy.start()
        du_copy = pltpu.make_async_copy(du_v, du_hbm, sems.at[1])
        du_copy.start()
        for n in range(ff // 256):
            for copy in leaving(n):
                copy.wait()

        def block(n):
            at = (
                slice(None),
                pl.ds(pl.multiple_of(64 + 16 * (n % 4), 16), 16),
                pl.ds(pl.multiple_of(n // 4 * ff, ff), ff),
            )
            return at

        def away(n):
            at = block(n)
            return (
                pltpu.make_async_copy(keep_v.at[at], keep_hbm.at[at], sems.at[3]),
                pltpu.make_async_copy(send_v.at[at], send_hbm.at[at], sems.at[4]),
            )

        @pl.loop(0, 8)
        def _(n):
            lanes = pl.ds(pl.multiple_of(n * 256, 256), 256)
            part = dot_rows(h2_v[:, lanes], du_v[...]).astype(bf16).reshape(8, 2, 16, ff)
            split(part, *block(n))
            for copy in away(n):
                copy.start()

        for n in range(8):
            for copy in away(n):
                copy.wait()
        h1_copy.wait()
        act_copy.wait()
        du_copy.wait()

    wide = jax.ShapeDtypeStruct((total, width), bf16)
    thin = jax.ShapeDtypeStruct((total, ff), bf16)
    column = jax.ShapeDtypeStruct((total, 1), f32)
    grads = jax.ShapeDtypeStruct((8, 128, width), bf16)
    vmem = pl.BlockSpec(memory_space=pltpu.VMEM)
    return pl.pallas_call(
        after_inputs(body, 5 + parts + 2 * count, len(after)),
        out_shape=(
            wide,
            thin,
            thin,
            grads,
            grads,
            column,
            column,
            jax.ShapeDtypeStruct((1, ff), f32),
            jax.ShapeDtypeStruct((1, 256), f32),
        ),
        in_specs=[pl.BlockSpec(memory_space=pltpu.SMEM)] * 2
        + [vmem, vmem]
        + anywhere(parts + 2 * count + 1 + len(after)),
        out_specs=tuple(anywhere(5)) + (vmem,) * 4,
        scratch_shapes=[
            pltpu.VMEM((total, width), bf16),
            pltpu.VMEM((total, width), bf16),
            pltpu.VMEM((total, width), bf16),
            pltpu.VMEM((total, width), bf16),
            pltpu.VMEM((8, 8, width // 64, ff), bf16),
            pltpu.VMEM((ff, width), bf16),
            pltpu.VMEM((total, ff), bf16),
            pltpu.VMEM((total, ff), bf16),
            pltpu.VMEM((8, 128, width), bf16),
            pltpu.VMEM((8, 128, width), bf16),
            pltpu.SemaphoreType.DMA((count,)),
            pltpu.SemaphoreType.DMA((count,)),
            pltpu.SemaphoreType.DMA((parts,)),
            pltpu.SemaphoreType.DMA((5,)),
        ],
        compiler_params=kernel_params(),
        cost_estimate=cost(32),
        name="feed_forward",
    )(numbers, spots, gains, bias, *[p[0] for p in weight], *x, *dy, down, *after)


def packed(qkv_weight, up_weight, vectors, lengths, place, head, tokens, cotangent):
    wide, up_wide = qkv_weight.shape[1], up_weight.shape[1]
    part, up_part = 3 * head, up_wide // 8
    cols = part + up_part

    def body(place_ref, len_ref, q_ref, u_ref, x_ref, dy_ref, *refs):
        v_refs, out_ref, pair_ref = refs[: len(vectors)], refs[-2], refs[-1]
        pair_ref[0] = x_ref[...]
        pair_ref[1] = dy_ref[...]
        lane = lax.broadcasted_iota(jnp.int32, (8, cols), 1)
        row = lax.broadcasted_iota(jnp.int32, (8, cols), 0)
        sizes = jnp.zeros((8, cols), f32)
        for at in range(3):
            sizes = jnp.where(lane == at, len_ref[0, at].astype(f32), sizes)
        vector = jnp.concatenate([ref[...].astype(f32) for ref in v_refs])[None, :]
        vector = jnp.broadcast_to(vector, (8, cols))
        tail = jnp.where(row == 0, vector, jnp.where(row == 1, sizes, 0.0)).astype(bf16)
        for owner in range(8):
            pieces = [
                q_ref[:, (third * 8 + owner) * head : (third * 8 + owner + 1) * head]
                for third in range(3)
            ]
            pieces.append(u_ref[:, owner * up_part : (owner + 1) * up_part])
            out_ref[owner] = jnp.concatenate([jnp.concatenate(pieces, 1), tail], 0)

    return pl.pallas_call(
        body,
        out_shape=(
            jax.ShapeDtypeStruct((8, 40, cols), bf16),
            jax.ShapeDtypeStruct((2,) + tokens.shape, bf16),
        ),
        grid_spec=pltpu.PrefetchScalarGridSpec(
            num_scalar_prefetch=2,
            grid=(1,),
            in_specs=[
                pl.BlockSpec((32, wide), lambda i, place, lens: (place[0], 0)),
                pl.BlockSpec((32, up_wide), lambda i, place, lens: (place[0], 0)),
                pl.BlockSpec(tokens.shape, lambda i, place, lens: (0, 0)),
                pl.BlockSpec(tokens.shape, lambda i, place, lens: (0, 0)),
            ]
            + [pl.BlockSpec(v.shape, lambda i, place, lens: (0,)) for v in vectors],
            out_specs=(
                pl.BlockSpec((8, 40, cols), lambda i, place, lens: (0, 0, 0)),
                pl.BlockSpec((2,) + tokens.shape, lambda i, place, lens: (0, 0, 0)),
            ),
        ),
        compiler_params=kernel_params(),
        cost_estimate=cost(3),
        name="packed",
    )(place, lengths, qkv_weight, up_weight, tokens, cotangent, *vectors)


def attend(h1, dy, weight, spots, out, bias, cosine, sine, lengths, after, rows=128):
    total, width = h1.shape
    count = len(dy)
    head = out.shape[0]
    scale = head ** (-0.5)

    parts = len(weight)

    def body(len_ref, spot_ref, b_ref, *refs):
        w_refs, refs = refs[:parts], refs[parts:]
        dy_refs = refs[:count]
        h1_hbm, out_hbm, cos_hbm, sin_hbm = refs[count : count + 4]
        ol_hbm, dq_hbm, sum_ref = refs[count + 4 : count + 7]
        (dy_v, h1_v, w_v, wo_v, cos_v, sin_v, qkv_v, do_v, ol_v, dq_v, dy_sem, w_sem, sems) = (
            refs[count + 7 :]
        )
        pairs = (
            (h1_hbm, h1_v),
            (out_hbm, wo_v),
            (cos_hbm, cos_v),
            (sin_hbm, sin_v),
        )
        copies = loads(
            [pltpu.make_async_copy(*pair, sems.at[n]) for n, pair in enumerate(pairs)]
        )
        w_copies = loads(
            weight_copies(weight, w_refs, spot_ref, w_v, pl.ds(0, 3 * head), w_sem)
        )
        dy_copies = loads(piece_copies(dy_refs, 1, dy_v, dy_sem, rows))
        for copy in copies[:1] + w_copies:
            copy.wait()

        @pl.loop(0, 3)
        def _(n):
            at = pl.ds(pl.multiple_of(n * head, head), head)
            qkv_v[:, at] = dot(h1_v[...], w_v[:, :, :, at].reshape(width, head)) + b_ref[n]

        for copy in copies[1:] + dy_copies:
            copy.wait()
        do_v[...] = dot(dy_v[...], wo_v[...], 1, 1).astype(bf16)
        sum_ref[...] = jnp.zeros_like(sum_ref)

        @pl.loop(0, total // rows, unroll=2)
        def _(block):
            at = pl.ds(pl.multiple_of(block * rows, rows), rows)
            cos, sin = cos_v[at, :], sin_v[at, :]

            def turned(value, sign):
                left = value[:, :128]
                left = left * cos + swap_halves(left) * (sin * sign)
                return jnp.concatenate([left, value[:, 128:]], 1).astype(bf16)

            q, k = turned(qkv_v[at, 0:head], 1.0), turned(qkv_v[at, head : 2 * head], 1.0)
            v = qkv_v[at, 2 * head :].astype(bf16)
            scores = dot(q, k, 1, 1) * scale
            masked = jnp.where(allowed_mask(len_ref, block, rows), scores, -1e30)
            shifted = jnp.exp(masked - jnp.max(masked, 1, keepdims=True))
            probs = shifted / jnp.sum(shifted, 1, keepdims=True)
            low = probs.astype(bf16)
            ol_v[at, :] = dot(low, v).astype(bf16)
            d_out = do_v[at, :]
            d_value = dot(low, d_out, 0, 0)
            d_probs = dot(d_out, v, 1, 1)
            centred = d_probs - jnp.sum(d_probs * probs, 1, keepdims=True)
            d_scores = (probs * centred).astype(bf16)
            d_query = turned(dot(d_scores, k) * scale, -1.0)
            d_key = turned(dot(d_scores, q, 0, 0) * scale, -1.0)
            for n, grad in enumerate((d_query, d_key, d_value.astype(bf16))):
                lanes = slice(n * head, (n + 1) * head)
                dq_v[at, lanes] = grad
                sum_ref[:, lanes] += jnp.sum(grad.astype(f32), 0, keepdims=True)

        ol_copy = pltpu.make_async_copy(ol_v, ol_hbm, sems.at[0])
        ol_copy.start()
        dq_copy = pltpu.make_async_copy(dq_v, dq_hbm, sems.at[1])
        dq_copy.start()

        for copy in (ol_copy, dq_copy):
            copy.wait()

    vmem = pl.BlockSpec(memory_space=pltpu.VMEM)
    smem = pl.BlockSpec(memory_space=pltpu.SMEM)
    return pl.pallas_call(
        after_inputs(body, 7 + parts + count, len(after)),
        out_shape=(
            jax.ShapeDtypeStruct((total, head), bf16),
            jax.ShapeDtypeStruct((total, 3 * head), bf16),
            jax.ShapeDtypeStruct((1, 3 * head), f32),
        ),
        in_specs=[smem, smem, vmem] + anywhere(parts + count + 4 + len(after)),
        out_specs=tuple(anywhere(2)) + (vmem,),
        scratch_shapes=[
            pltpu.VMEM((total, width), bf16),
            pltpu.VMEM((total, width), bf16),
            pltpu.VMEM((8, 8, width // 64, 3 * head), bf16),
            pltpu.VMEM((head, width), bf16),
            pltpu.VMEM((total, 128), f32),
            pltpu.VMEM((total, 128), f32),
            pltpu.VMEM((total, 3 * head), f32),
            pltpu.VMEM((total, head), bf16),
            pltpu.VMEM((total, head), bf16),
            pltpu.VMEM((total, 3 * head), bf16),
            pltpu.SemaphoreType.DMA((count,)),
            pltpu.SemaphoreType.DMA((parts,)),
            pltpu.SemaphoreType.DMA((4,)),
        ],
        compiler_params=kernel_params(),
        cost_estimate=cost(17),
        name="attend",
    )(
        lengths,
        spots,
        bias,
        *[p[0] for p in weight],
        *dy,
        h1,
        out,
        cosine,
        sine,
        *after,
    )


def attention_grads(h1, dy, d_qkv, attended, numbers, after):
    total, width = h1.shape
    count = len(dy)
    rows = total // count
    head = attended.shape[1]

    def body(number_ref, *refs):
        dy_refs = refs[:count]
        h1_hbm, dq_hbm, ol_hbm, keep_hbm, send_hbm = refs[count : count + 5]
        dy_v, h1_v, dq_v, ol_v, keep_v, send_v, dy_sem, sems = refs[count + 5 :]
        own = number_ref[0] == 0
        pairs = ((h1_hbm, h1_v), (dq_hbm, dq_v), (ol_hbm, ol_v))
        copies = loads(
            [pltpu.make_async_copy(*pair, sems.at[n]) for n, pair in enumerate(pairs)]
        )
        dy_copies = loads(piece_copies(dy_refs, 1, dy_v, dy_sem, rows))
        for copy in copies:
            copy.wait()

        def split(part, high, lanes):
            for z_hi in range(2):
                at = (pl.ds(4 * z_hi, 4), high, lanes)

                @pl.when(own)
                def _(z_hi=z_hi, at=at):
                    keep_v[at] = part[:, z_hi, 0]
                    send_v[at] = part[:, z_hi, 1]

                @pl.when(jnp.logical_not(own))
                def _(z_hi=z_hi, at=at):
                    keep_v[at] = part[:, z_hi, 1]
                    send_v[at] = part[:, z_hi, 0]

        @pl.loop(0, 8)
        def _(n):
            lanes = pl.ds(pl.multiple_of(n * 256, 256), 256)
            part = dot_rows(h1_v[:, lanes], dq_v[...]).astype(bf16).reshape(4, 2, 2, 16, 3 * head)
            for third in range(3):
                split(
                    part[..., third * head : (third + 1) * head],
                    pl.ds(16 * third, 16),
                    pl.ds(pl.multiple_of(n * head, head), head),
                )

        for copy in dy_copies:
            copy.wait()
        part = dot_rows(ol_v[...], dy_v[...]).astype(bf16).reshape(4, 2, 2, 16, width)
        split(part, pl.ds(48, 16), slice(None))
        keep_copy = pltpu.make_async_copy(keep_v, keep_hbm, sems.at[0])
        keep_copy.start()
        send_copy = pltpu.make_async_copy(send_v, send_hbm, sems.at[1])
        send_copy.start()
        keep_copy.wait()
        send_copy.wait()

    grads = jax.ShapeDtypeStruct((8, 64, width), bf16)
    return pl.pallas_call(
        after_inputs(body, 4 + count, len(after)),
        out_shape=(grads, grads),
        in_specs=[pl.BlockSpec(memory_space=pltpu.SMEM)] + anywhere(count + 3 + len(after)),
        out_specs=tuple(anywhere(2)),
        scratch_shapes=[
            pltpu.VMEM((total, width), bf16),
            pltpu.VMEM((total, width), bf16),
            pltpu.VMEM((total, 3 * head), bf16),
            pltpu.VMEM((total, head), bf16),
            pltpu.VMEM((8, 64, width), bf16),
            pltpu.VMEM((8, 64, width), bf16),
            pltpu.SemaphoreType.DMA((count,)),
            pltpu.SemaphoreType.DMA((3,)),
        ],
        compiler_params=kernel_params(),
        cost_estimate=cost(12),
        name="attention_grads",
    )(numbers, *dy, h1, d_qkv, attended, *after)


def mixed_part(active, attended, down, out, bias, after):
    rows, ff = active.shape
    head, width = out.shape
    step = 512
    count = rows // 128

    def body(act_ref, ol_ref, wd_ref, wo_ref, b_ref, *refs):
        total = dot(act_ref[...], wd_ref[...]) + dot(ol_ref[...], wo_ref[...]) + b_ref[...]
        for at in range(count):
            refs[at][...] = total[at * 128 : (at + 1) * 128].astype(bf16)

    return pl.pallas_call(
        after_inputs(body, 5, len(after)),
        out_shape=(jax.ShapeDtypeStruct((128, width), bf16),) * count,
        grid=(width // step,),
        in_specs=[
            pl.BlockSpec((rows, ff), lambda i: (0, 0)),
            pl.BlockSpec((rows, head), lambda i: (0, 0)),
            pl.BlockSpec((ff, step), lambda i: (0, i)),
            pl.BlockSpec((head, step), lambda i: (0, i)),
            pl.BlockSpec((1, step), lambda i: (0, i)),
        ]
        + anywhere(len(after)),
        out_specs=(pl.BlockSpec((128, step), lambda i: (0, i)),) * count,
        compiler_params=kernel_params(),
        cost_estimate=cost(10),
        name="mixed_part",
    )(active, attended, down, out, bias, *after)


def back_norms(d_qkv, d_hidden, weight, spots, x, mean, inverse, gains, part, before, after):
    total, n1 = d_qkv.shape
    n2 = d_hidden.shape[1]
    count = len(x)
    parts = len(weight)
    width = x[0].shape[-1]
    step = 512
    half = width // 2

    def body(spot_ref, m_ref, i_ref, g_ref, *refs):
        w_refs, refs = refs[:parts], refs[parts:]
        x_refs, refs = refs[:count], refs[count:]
        plain, refs = refs[:2], refs[2 + len(before) :]
        sums_ref, outs = refs[0], refs[1 : 1 + count]
        dq_v, du_v, w_v, x_v, s_v, w_sem, x_sem, sems, out_sem = refs[1 + count :]
        plain_v = (dq_v, du_v)
        copies = loads(
            [
                pltpu.make_async_copy(plain[n], plain_v[n], sems.at[n]) for n in range(2)
            ]
            + weight_copies(weight, w_refs, spot_ref, w_v, slice(None), w_sem, part * 4)
            + piece_copies(x_refs, 0, x_v, x_sem, 128, pl.ds(part * half, half))
        )
        def leaving(n):
            lanes = pl.ds(pl.multiple_of(n * step, step), step)
            there = pl.ds(pl.multiple_of(part * half + n * step, step), step)
            return [
                pltpu.make_async_copy(
                    s_v.at[pl.ds(at * 128, 128), lanes], outs[at].at[:, there], out_sem.at[at]
                )
                for at in range(count)
            ]

        for copy in copies:
            copy.wait()

        @pl.loop(0, half // step)
        def _(n):
            lanes = pl.ds(pl.multiple_of(n * step, step), step)
            gain = pl.ds(pl.multiple_of(part * half + n * step, step), step)
            sources = pl.ds(n * (step // 256), step // 256)
            d1 = dot(dq_v[...], w_v[sources, :, :, 0:n1].reshape(step, n1), 1, 1)
            d2 = dot(du_v[...], w_v[sources, :, :, n1:].reshape(step, n2), 1, 1)
            s_v[:, lanes] = (d1 * g_ref[0:1, gain] + d2 * g_ref[1:2, gain]).astype(bf16)
            for copy in leaving(n):
                copy.start()
            normed = (x_v[:, lanes].astype(f32) - m_ref[...]) * i_ref[...]
            sums_ref[0:1, lanes] = jnp.sum(d1 * normed, 0, keepdims=True)
            sums_ref[1:2, lanes] = jnp.sum(d1, 0, keepdims=True)
            sums_ref[2:3, lanes] = jnp.sum(d2 * normed, 0, keepdims=True)
            sums_ref[3:4, lanes] = jnp.sum(d2, 0, keepdims=True)

        for n in range(half // step):
            for copy in leaving(n):
                copy.wait()

    vmem = pl.BlockSpec(memory_space=pltpu.VMEM)
    return pl.pallas_call(
        after_inputs(body, 6 + parts + count + len(before), len(after)),
        out_shape=(jax.ShapeDtypeStruct((4, half), f32),)
        + (jax.ShapeDtypeStruct((128, width), bf16),) * count,
        in_specs=[pl.BlockSpec(memory_space=pltpu.SMEM)]
        + [vmem] * 3
        + anywhere(parts + count + 2 + len(before) + len(after)),
        out_specs=(vmem,) + tuple(anywhere(count)),
        scratch_shapes=[
            pltpu.VMEM((total, n1), bf16),
            pltpu.VMEM((total, n2), bf16),
            pltpu.VMEM((4, 8, width // 64, n1 + n2), bf16),
            pltpu.VMEM((total, half), bf16),
            pltpu.VMEM((total, half), bf16),
            pltpu.SemaphoreType.DMA((parts,)),
            pltpu.SemaphoreType.DMA((count,)),
            pltpu.SemaphoreType.DMA((2,)),
            pltpu.SemaphoreType.DMA((count,)),
        ],
        input_output_aliases={6 + parts + count + n: 1 + n for n in range(len(before))},
        compiler_params=kernel_params(),
        cost_estimate=cost(9),
        name="back_norms",
    )(
        spots,
        mean,
        inverse,
        gains,
        *[p[0] for p in weight],
        *x,
        d_qkv,
        d_hidden,
        *before,
        *after,
    )


def unpacked(part, after):
    owners, _, cols = part.shape

    def body(part_ref, rows_ref, info_ref):
        for owner in range(owners):
            rows_ref[owner] = part_ref[owner, 0:32]
            info_ref[owner] = part_ref[owner, 32:40].astype(f32)

    return pl.pallas_call(
        after_inputs(body, 1, len(after)),
        out_shape=(
            jax.ShapeDtypeStruct((owners, 32, cols), bf16),
            jax.ShapeDtypeStruct((owners, 8, cols), f32),
        ),
        in_specs=[pl.BlockSpec(memory_space=pltpu.VMEM)] + anywhere(len(after)),
        out_specs=(pl.BlockSpec(memory_space=pltpu.VMEM),) * 2,
        compiler_params=kernel_params(),
        cost_estimate=cost(3),
        name="unpacked",
    )(part, *after)


def joined(arrays, after):
    sizes = [array.shape[0] for array in arrays]
    unit = math.gcd(*sizes)
    block = (unit,) + arrays[0].shape[1:]
    count = len(arrays)
    firsts = [sum(sizes[:n]) // unit for n in range(count)]

    def body(*refs):
        step = pl.program_id(0)
        for ref, first, size in zip(refs, firsts, sizes):

            @pl.when((step >= first) & (step < first + size // unit))
            def _(ref=ref):
                refs[count][...] = ref[...]

    def came(first, size):
        return pl.BlockSpec(block, lambda i: (jnp.clip(i - first, 0, size // unit - 1), 0, 0))

    return pl.pallas_call(
        after_inputs(body, count, len(after)),
        out_shape=jax.ShapeDtypeStruct((sum(sizes),) + block[1:], bf16),
        grid=(sum(sizes) // unit,),
        in_specs=[came(first, size) for first, size in zip(firsts, sizes)] + anywhere(len(after)),
        out_specs=pl.BlockSpec(block, lambda i: (i, 0, 0)),
        compiler_params=kernel_params(),
        cost_estimate=cost(3),
        name="joined",
    )(*arrays, *after)


def halves(own, below, above, after):
    count, rows, cols = own.shape
    half = count // 2

    def body(own_ref, below_ref, above_ref, low_ref, high_ref, all_ref):
        step = pl.program_id(0)
        all_ref[0] = own_ref[...]
        all_ref[1] = above_ref[...]
        all_ref[2] = below_ref[...]

        @pl.when(step == 0)
        def _():
            low_ref[...] = below_ref[...]

        @pl.when(step == 1)
        def _():
            high_ref[...] = above_ref[...]

    block = pl.BlockSpec((half, rows, cols), lambda i: (i, 0, 0))
    whole = pl.BlockSpec((half, rows, cols), lambda i: (0, 0, 0))
    low, high, together = pl.pallas_call(
        after_inputs(body, 3, len(after)),
        out_shape=(jax.ShapeDtypeStruct((half, rows, cols), bf16),) * 2
        + (jax.ShapeDtypeStruct((3, count, rows, cols), bf16),),
        grid=(2,),
        in_specs=[block] * 3 + anywhere(len(after)),
        out_specs=(
            whole,
            whole,
            pl.BlockSpec((3, half, rows, cols), lambda i: (0, i, 0, 0)),
        ),
        compiler_params=kernel_params(),
        cost_estimate=cost(4),
        name="halves",
    )(own, below, above, *after)
    return low, high, together.reshape(3 * count, rows, cols)


def finished(mix, sums, tokens, cotangent, after):
    rows, width = tokens.shape
    step = rows // 2

    def body(*refs):
        x_ref, dy_ref, mixed_ref, grad_ref = refs[8:]
        x = x_ref[...].astype(f32)
        mixed_ref[...] = (x + wide(*refs[:4])).astype(bf16)
        gain = wide(*refs[4:8])
        centre = x - jnp.mean(x, 1, keepdims=True)
        inverse = lax.rsqrt(jnp.mean(centre * centre, 1, keepdims=True) + EPS)
        normed = centre * inverse
        grad_ref[...] = dy_ref[...].astype(f32) + inverse * (
            gain
            - jnp.mean(gain, 1, keepdims=True)
            - normed * jnp.mean(gain * normed, 1, keepdims=True)
        )

    block = pl.BlockSpec((step, width), lambda i: (i, 0))
    later = pl.BlockSpec((step, width), lambda i: (i + 2, 0))
    return pl.pallas_call(
        after_inputs(body, 10, len(after)),
        out_shape=(
            jax.ShapeDtypeStruct((rows, width), bf16),
            jax.ShapeDtypeStruct((rows, width), f32),
        ),
        grid=(2,),
        in_specs=[block, later, block, block] * 2 + [block, block] + anywhere(len(after)),
        out_specs=(block, block),
        compiler_params=kernel_params(),
        cost_estimate=cost(3),
        name="finished",
    )(*mix, *sums, tokens, cotangent, *after)


def packed_sums(stays, crossed, own, below, above, norm_sums, qkv_sums, up_sums, dy_sums, numbers, ff, head, after):
    width = own.shape[1]

    def body(*refs):
        stay_ref, cross_ref, own_ref, below_ref, above_ref = refs[:5]
        norm_ref, q_ref, u_ref, y_ref, number_ref, out_ref, keep_ref, small = refs[5:]
        shard = number_ref[1]
        inner = (stay_ref[0].astype(f32) + cross_ref[0].astype(f32)).astype(bf16)
        total = wide(own_ref, below_ref, above_ref).astype(bf16)
        for owner in range(8):
            mine = shard == owner
            small[...] = jnp.zeros_like(small)
            small[0:4] = norm_ref[:, owner * head : (owner + 1) * head]
            for n in range(3):
                third, source = divmod(owner * 3 + n, 8)
                lanes = slice(third * head, (third + 1) * head)
                small[4 + n : 5 + n] = jnp.where(shard == source, q_ref[:, lanes], 0.0)
            for n in range(4):
                lanes = slice(n * head, (n + 1) * head)
                small[7 + n : 8 + n] = jnp.where(mine, u_ref[:, lanes], 0.0)
            small[11:12] = jnp.where(mine, y_ref[...], 0.0)
            pieces = [
                total[16 * third : 16 * third + 16, owner * head : (owner + 1) * head]
                for third in range(3)
            ]
            row, col = 64 + 16 * (owner % 4), owner // 4 * ff
            pieces.append(inner[row : row + 16, col : col + ff])
            pieces.append(small[...].astype(bf16))
            out_ref[owner] = jnp.concatenate(pieces, 1)
        keep_ref[0:64] = inner[0:64]
        keep_ref[64:80] = total[48:64]

    vmem = pl.BlockSpec(memory_space=pltpu.VMEM)
    return pl.pallas_call(
        after_inputs(body, 10, len(after)),
        out_shape=(
            jax.ShapeDtypeStruct((8, 16, 4 * head + ff), bf16),
            jax.ShapeDtypeStruct((80, width), bf16),
        ),
        in_specs=[vmem] * 9 + [pl.BlockSpec(memory_space=pltpu.SMEM)] + anywhere(len(after)),
        out_specs=(vmem,) * 2,
        scratch_shapes=[pltpu.VMEM((16, head), f32)],
        compiler_params=kernel_params(),
        cost_estimate=cost(3),
        name="packed_sums",
    )(stays, crossed, own, below, above, norm_sums, qkv_sums, up_sums, dy_sums, numbers, *after)


def unpacked_sums(received, cols, after):
    sources, rows, width = received.shape

    def body(part_ref, out_ref):
        small = jnp.sum(part_ref[:, :, cols:].astype(f32), 0).astype(bf16)
        out_ref[0] = jnp.concatenate(
            [jnp.concatenate([part_ref[0, :, 0:cols], small], 1)]
            + [part_ref[n] for n in range(1, sources)],
            0,
        )

    vmem = pl.BlockSpec(memory_space=pltpu.VMEM)
    return pl.pallas_call(
        after_inputs(body, 1, len(after)),
        out_shape=jax.ShapeDtypeStruct((1, sources * rows, width), bf16),
        in_specs=[vmem] + anywhere(len(after)),
        out_specs=vmem,
        compiler_params=kernel_params(),
        cost_estimate=cost(3),
        name="unpacked_sums",
    )(received, *after)


def blocks_call(name, body, numbers, terms, outs, after, time=3):
    def came(block, index):
        rest = (0,) * (len(block) - 1)
        return pl.BlockSpec(block, lambda i, n: (index(n),) + rest)

    return pl.pallas_call(
        after_inputs(body, 1 + len(terms), len(after)),
        out_shape=tuple(jax.ShapeDtypeStruct(out, bf16) for out in outs),
        grid_spec=pltpu.PrefetchScalarGridSpec(
            num_scalar_prefetch=1,
            grid=(1,),
            in_specs=[came(block, index) for _, block, index in terms] + anywhere(len(after)),
            out_specs=tuple(
                pl.BlockSpec(out, lambda i, n, size=len(out): (0,) * size) for out in outs
            ),
        ),
        compiler_params=kernel_params(),
        cost_estimate=cost(time),
        name=name,
    )(numbers, *[array for array, _, _ in terms], *after)


def wide(*refs):
    return functools.reduce(jnp.add, [ref[...].astype(f32) for ref in refs])


def spread(pieces, places, core, targets, count, before, after):
    rows, cols = pieces[0][0].shape[1:]
    firsts, total = [], 0
    for mine, _ in pieces:
        firsts.append(total)
        total += mine.shape[0]

    def body(place_ref, core_ref, *refs):
        step = pl.program_id(0)
        outs = refs[2 * len(pieces) + len(before) :]
        first_core = core_ref[0] == 0

        def fill(ref, low):
            for out_ref, (_, high, parts) in zip(outs, targets):
                for to, row, col, size in parts:
                    out_ref[low * high : (low + 1) * high, to : to + size] = ref[
                        0, row : row + high, col : col + size
                    ].astype(f32)

        for n, (first, (mine, _)) in enumerate(zip(firsts, pieces)):
            here = (step >= first) & (step < first + mine.shape[0])

            @pl.when(here & first_core)
            def _(n=n):
                fill(refs[2 * n], 0)
                fill(refs[2 * n + 1], 1)

            @pl.when(here & jnp.logical_not(first_core))
            def _(n=n):
                fill(refs[2 * n], 1)
                fill(refs[2 * n + 1], 0)

    def chosen(first, size):
        return pl.BlockSpec(
            (1, rows, cols), lambda i, place, core: (jnp.clip(i - first, 0, size - 1), 0, 0)
        )

    specs, arrays = [], []
    for first, (mine, yours) in zip(firsts, pieces):
        specs += [chosen(first, mine.shape[0])] * 2
        arrays += [mine, yours]
    return pl.pallas_call(
        after_inputs(body, 2 + 2 * len(pieces) + len(before), len(after)),
        out_shape=tuple(
            jax.ShapeDtypeStruct((2 * count * high, wide), f32) for wide, high, _ in targets
        ),
        grid_spec=pltpu.PrefetchScalarGridSpec(
            num_scalar_prefetch=2,
            grid=(total,),
            in_specs=specs + anywhere(len(before) + len(after)),
            out_specs=tuple(
                pl.BlockSpec((2 * high, wide), lambda i, place, core: (place[i], 0))
                for wide, high, _ in targets
            ),
        ),
        input_output_aliases={2 + len(arrays) + n: n for n in range(len(before))},
        compiler_params=kernel_params(),
        cost_estimate=cost(0.3 * total),
        name="spread",
    )(places, core, *arrays, *before, *after)


def local(
    tokens,
    doc_lengths,
    cotangent,
    ln1_gain,
    ln1_bias,
    ln2_gain,
    ln2_bias,
    qkv_weight,
    qkv_bias,
    out_weight,
    out_bias,
    up_weight,
    up_bias,
    down_weight,
    down_bias,
):
    rows, width = tokens.shape
    head = width // HEADS
    group = 8
    rep = lax.axis_index("rep")
    shard = lax.axis_index("shard")
    y, h, c = rep // 4, (rep // 2) % 2, rep % 2
    l, x = shard // 4, shard % 4
    ff = up_bias.shape[0]

    cols = 3 * head + ff
    vectors = [ln1_gain, ln1_bias, ln2_gain, ln2_bias, qkv_bias]
    place = (y * 2 + c).astype(jnp.int32).reshape(1)
    part, pair = packed(
        qkv_weight, up_weight, vectors, doc_lengths, place, head, tokens, cotangent
    )
    below, above, other = move(pair, x=1), move(pair, x=-1), move(pair, l=1)
    far, other_above, other_below = move(below, x=1), move(other, x=-1), move(below, l=1)
    pairs = (pair, above, far, below, other, other_above, None, other_below)

    part = lax.all_to_all(part, "shard", 0, 0)
    own, infos = unpacked(part, (pairs[1], pairs[3], pairs[4]))
    below, above = move(own, y=1), move(own, y=-1)
    x_other_far, dy_other_far = move(other_below[0], x=1), move(other_above[1], x=-1)
    low, high, yours = halves(own, below, above, (far, other_above, other_below))
    far_low, far_high = move(low, y=1), move(high, y=-1)
    x_all = tuple(x_other_far if p is None else p for p in pairs)
    dy_all = tuple(dy_other_far if p is None else p for p in pairs)
    yours = move(yours, c=1)
    far_low_c, far_high_c = move(far_low, c=1), move(far_high, c=1)
    weight = (
        (own, 0, 8, 0, 0),
        (above, 0, 8, 0, 1),
        (far_low, 0, 4, 0, 2),
        (far_high, 0, 4, 4, 2),
        (below, 0, 8, 0, 3),
        (yours, 0, 8, 0, 4),
        (yours, 8, 8, 0, 5),
        (far_low_c, 0, 4, 0, 6),
        (far_high_c, 0, 4, 4, 6),
        (yours, 16, 8, 0, 7),
    )
    steps4 = (y + jnp.arange(4)) % 4
    spots = jnp.concatenate([steps4 * 2 + c, steps4 * 2 + 1 - c]).astype(jnp.int32)

    gains = infos[:, 0, :1024].reshape(8, 4, 256).transpose(1, 0, 2).reshape(4, width)
    qkv_b = infos[:, 0, 1024:].reshape(8 * 3, 1, head)
    qkv_b = jnp.stack(
        [lax.dynamic_index_in_dim(qkv_b, third * 8 + shard, 0, False) for third in range(3)]
    )
    steps8 = jnp.arange(8)
    sources = ((steps8 // 4) ^ l) * 4 + (x + steps8 % 4) % 4
    sources = sources.astype(jnp.int32)
    lengths = infos[:, 1, :3]
    lengths = jnp.sum(
        jnp.where(sources[:, None, None] == steps8[None, :, None], lengths[None], 0.0), 1
    ).astype(jnp.int32)
    ends = jnp.cumsum(lengths, 1)
    starts = ends - lengths
    steps_t = jnp.arange(rows, dtype=jnp.int32)
    segment = jnp.sum((steps_t[None, :, None] >= ends[:, None, :]).astype(jnp.int32), -1)
    slots = jnp.arange(lengths.shape[1], dtype=jnp.int32)
    begin = jnp.sum(
        jnp.where(segment[:, :, None] == slots[None, None, :], starts[:, None, :], 0), -1
    )
    position = (steps_t[None, :] - begin).astype(f32).reshape(group * rows, 1)
    lane = jnp.arange(128)
    freq = 10000.0 ** (-2.0 * (lane % (ROT // 2)).astype(f32) / ROT)
    angle = position * freq[None, :]
    cosine = jnp.where(lane < ROT, jnp.cos(angle), 1.0)
    sine = jnp.sin(angle)
    sine = jnp.where(lane < ROT // 2, -sine, jnp.where(lane < ROT, sine, 0.0))

    both_bias = (out_bias.astype(f32) + down_bias.astype(f32))[None, :]
    wide_bias = lax.dynamic_update_slice(jnp.zeros((1, width), f32), both_bias, (0, shard * 256))
    numbers = jnp.stack([c, shard, y, h]).astype(jnp.int32)

    h1, active, d_hidden, keep, send, mean, inverse, up_sums, dy_sums = feed_forward(
        x_all,
        dy_all,
        gains,
        weight,
        spots,
        down_weight,
        up_bias.astype(f32)[None],
        numbers,
        3 * head,
        (cosine, sine),
    )
    got = move(send, c=1)
    attended, d_qkv, qkv_sums = attend(
        h1, dy_all, weight, spots, out_weight, qkv_b, cosine, sine, lengths, (send,)
    )

    pair_shape, one = (2, 128, width), (1, 128, width)

    def turn(k):
        return lambda n: (n[2] + k) % 4

    def far_body(n_ref, keep_ref, got_ref, low_ref, high_ref):
        total = wide(keep_ref, got_ref).astype(bf16)
        low_ref[0] = total[0]
        high_ref[0] = total[1]

    low, high = blocks_call(
        "far_sums",
        far_body,
        numbers,
        [(keep, pair_shape, turn(2)), (got, pair_shape, turn(2))],
        (one, one),
        (attended,),
    )
    from_low, from_high = move(low, y=1), move(high, y=-1)
    a_keep, a_send = attention_grads(h1, dy_all, d_qkv, attended, numbers, (low, high))
    a_got = move(a_send, c=1)
    def near_body(n_ref, k1_ref, g1_ref, k3_ref, g3_ref, low_ref, high_ref, above_ref, below_ref):
        above, below = wide(k1_ref, g1_ref), wide(k3_ref, g3_ref)
        above_ref[0] = (above[0] + low_ref[0].astype(f32)).astype(bf16)
        above_ref[1] = above[1].astype(bf16)
        below_ref[0] = below[0].astype(bf16)
        below_ref[1] = (below[1] + high_ref[0].astype(f32)).astype(bf16)

    above, below = blocks_call(
        "near_sums",
        near_body,
        numbers,
        [(v, pair_shape, turn(k)) for k in (1, 3) for v in (keep, got)]
        + [(v, one, lambda n: 0) for v in (from_low, from_high)],
        (pair_shape, pair_shape),
        (a_send,),
        20,
    )
    from_below, from_above = move(above, y=1), move(below, y=-1)

    four, part_shape = (4, 64, width), (1, 64, width)

    def away_body(n_ref, keep_ref, got_ref, out_ref):
        out_ref[...] = wide(keep_ref, got_ref).astype(bf16)

    (a_away,) = blocks_call(
        "away_sums",
        away_body,
        numbers,
        [(v, four, lambda n: 1 - n[3]) for v in (a_keep, a_got)],
        (four,),
        (above,),
    )
    a_crossed = move(a_away, h=1)
    mix = mixed_part(active, attended, down_weight, out_weight, wide_bias, (a_away, above, below))
    def norms_back(part, before, after):
        return back_norms(
            d_qkv,
            d_hidden,
            weight,
            spots,
            x_all,
            mean,
            inverse,
            jnp.stack([gains[0], gains[2]]),
            part,
            before,
            after,
        )

    flat, both = (128, width), (256, width)

    def passed_body(n_ref, up_ref, from_below, here_ref, down_ref, from_above, there_ref, up_out, down_out):
        up_out[0:128] = wide(up_ref, from_below).astype(bf16)
        up_out[128:256] = here_ref[...]
        down_out[0:128] = wide(down_ref, from_above).astype(bf16)
        down_out[128:256] = there_ref[...]

    def other_body(n_ref, own_ref, below_ref, above_ref, *refs):
        passing = len(refs) // 2
        refs[passing][...] = wide(own_ref, below_ref, above_ref).astype(bf16)
        for at in range(passing):
            refs[passing + 1 + at][...] = refs[at][...]

    def first(n):
        return 0

    def ring_start(high, low):
        return move(high, x=1), move(low, x=-1)

    def ring_middle(pieces, passed, after):
        operands = (pieces[5], passed[0], pieces[1], pieces[3], passed[1], pieces[7])
        ups, downs = blocks_call(
            "passed_sums",
            passed_body,
            numbers,
            [(v, flat, first) for v in operands],
            (both, both),
            after,
        )
        return (move(ups, x=1), move(downs, x=-1)), ups

    def ring_end(pieces, arrived, passing):
        other, *copies = blocks_call(
            "other_sums",
            other_body,
            numbers,
            [
                (pieces[4], flat, first),
                (arrived[0], flat, first),
                (arrived[1], flat, lambda n: 1),
            ]
            + [(v, flat, first) for v in passing],
            (flat,) * (1 + len(passing)),
            (),
        )
        return (pieces[0], *arrived, move(other, l=1)), other, *copies

    mix_passed = ring_start(mix[6], mix[2])

    def ends_body(n_ref, keep_ref, got_ref, below_ref, above_ref, leave_ref, stay_ref):
        total = wide(keep_ref, got_ref, below_ref, above_ref).astype(bf16)
        first = n_ref[3] == 0
        leave_ref[0] = jnp.where(first, total[1], total[0])
        stay_ref[0] = jnp.where(first, total[0], total[1])

    leaves, stays = blocks_call(
        "end_sums",
        ends_body,
        numbers,
        [(v, pair_shape, turn(0)) for v in (keep, got)]
        + [(v, pair_shape, lambda n: 0) for v in (from_below, from_above)],
        (one, one),
        (mix[0],),
    )
    crossed = move(leaves, h=1)

    def around_body(n_ref, keep_ref, got_ref, crossed_ref, low_ref, high_ref, above_ref, own_ref, below_ref):
        def part(k):
            at = (n_ref[2] + k) % 4
            return wide(keep_ref.at[at], got_ref.at[at], crossed_ref.at[at]).astype(bf16)

        far = part(2)
        low_ref[...] = far[:32]
        high_ref[...] = far[32:]
        above_ref[...] = part(1)
        own_ref[...] = part(0)
        below_ref[...] = part(3)

    a_low, a_high, a_above, a_own, a_below = blocks_call(
        "around_sums",
        around_body,
        numbers,
        [(v, four, lambda n: n[3]) for v in (a_keep, a_got)] + [(a_crossed, four, lambda n: 0)],
        ((32, width), (32, width), (64, width), (64, width), (64, width)),
        (leaves,),
    )
    low_sums, *sums = norms_back(0, (), (a_low,))
    mix_arrived, mix_ups = ring_middle(mix, mix_passed, (low_sums,))
    a_low, a_high = move(a_low, y=1), move(a_high, y=-1)

    def beside_body(n_ref, above_ref, below_ref, low_ref, high_ref, up_ref, down_ref):
        up_ref[0:32] = (above_ref[0:32].astype(f32) + low_ref[...].astype(f32)).astype(bf16)
        up_ref[32:64] = above_ref[32:64]
        down_ref[0:32] = below_ref[0:32]
        down_ref[32:64] = (below_ref[32:64].astype(f32) + high_ref[...].astype(f32)).astype(bf16)

    a_above, a_below = blocks_call(
        "beside_sums",
        beside_body,
        numbers,
        [(v, v.shape, lambda n: 0) for v in (a_above, a_below, a_low, a_high)],
        ((64, width), (64, width)),
        (crossed, low_sums),
    )
    a_from_below, a_from_above = move(a_above, y=1), move(a_below, y=-1)
    high_sums, *sums = norms_back(1, tuple(sums), (a_above, mix_ups))

    part, stays = packed_sums(
        stays,
        crossed,
        a_own,
        a_from_below,
        a_from_above,
        jnp.concatenate([low_sums, high_sums], 1),
        qkv_sums,
        up_sums,
        dy_sums,
        numbers,
        ff,
        head,
        (),
    )
    received = lax.all_to_all(part, "shard", 0, 0)
    mix_left, mix_other, high, low = ring_end(mix, mix_arrived, (sums[6], sums[2]))
    part = unpacked_sums(received, cols, (mix_other,))
    order = ((0, h), (0, 1 - h), (1, h), (1, 1 - h), (3, h), (3, 1 - h), (2, h), (2, 1 - h))
    places = jnp.stack([(y + k) % 4 * 2 + high for k, high in order]).astype(jnp.int32)

    sums_arrived, sums_ups = ring_middle(sums, ring_start(high, low), (received,))
    sums_left, sums_other = ring_end(sums, sums_arrived, ())
    stays = stays[None]
    stays = jnp.concatenate([stays, move(stays, h=1)])
    below, above = move(stays, y=1), move(stays, y=-1)
    stays = joined((stays, above, below, move(below, y=1)), ())
    down_grad, out_grad = spread(
        [(stays, move(stays, c=1))],
        places,
        numbers[:1],
        [(width, 64, [(0, 0, 0, width)]), (width, 16, [(0, 64, 0, width)])],
        8,
        (),
        (mix_left[3],),
    )
    part = joined((part, move(part, h=1)), (sums_ups,))
    below, above = move(part, y=1), move(part, y=-1)
    low, high, near = halves(part, below, above, (stays, mix_left[3], sums_other))
    far = move(low, y=1), move(high, y=-1)
    targets = [
        (
            3 * width,
            16,
            [
                ((third * 8 + source) * head, 16 * source, third * head, head)
                for source in range(8)
                for third in range(3)
            ],
        ),
        (8 * ff, 16, [(source * ff, 16 * source, 3 * head, ff) for source in range(8)]),
    ]
    near_yours = move(near, c=1)
    grads = spread(
        [(near, near_yours)], places[:6], numbers[:1], targets, 8, (), (down_grad, sums_left[3])
    )
    far = joined(far, (grads[0],))
    mixed, tokens_grad = finished(mix_left, sums_left, tokens, cotangent, (far,))
    far_yours = move(far, c=1)
    qkv_grad, up_grad = spread(
        [(far, far_yours)],
        places[6:],
        numbers[:1],
        targets,
        8,
        grads,
        (tokens_grad,),
    )
    smalls = [v[:, 0:16, cols:] for v in (near, near_yours, far, far_yours)]
    smalls = jnp.sum(jnp.concatenate(smalls).astype(f32), 0)
    norm_grads = smalls[:4]
    dy_total = smalls[11]
    return (
        mixed,
        tokens_grad,
        norm_grads[0],
        norm_grads[1],
        norm_grads[2],
        norm_grads[3],
        qkv_grad,
        smalls[4:7].reshape(3 * head),
        out_grad,
        dy_total,
        up_grad,
        smalls[7:11].reshape(ff),
        down_grad,
        dy_total,
    )


def solution(mesh):
    rows = P(BOTH, None)
    vector, matrix = P("shard"), P("shard", None)
    return jax.shard_map(
        local,
        mesh=mesh,
        in_specs=(rows, rows, rows, vector, vector, vector, vector)
        + (matrix, vector, matrix, vector, matrix, vector, matrix, vector),
        out_specs=(rows, rows, vector, vector, vector, vector)
        + (matrix, vector, matrix, vector, matrix, vector, matrix, vector),
        check_vma=False,
    )
```

```python
import functools
import math

import jax
import jax.numpy as jnp
from jax import lax
from jax.experimental import pallas as pl
from jax.experimental.pallas import tpu as pltpu
from jax.sharding import PartitionSpec as P

HEADS = 8
ROT = 64
EPS = 1e-05
f32 = jnp.float32
bf16 = jnp.bfloat16


def cost(time):
    return pl.CostEstimate(flops=int(time * 1.15e9), bytes_accessed=1000, transcendentals=0)


BOTH = ("rep", "shard")
SIZES = (4, 2, 2, 2, 4)
SAME_CORE = [[2 * n + c for n in range(8)] for c in range(2)]
SAME_CORE_ALL = [[(2 * n + c) * 8 + s for n in range(8) for s in range(8)] for c in range(2)]


def coords():
    for y in range(4):
        for h in range(2):
            for c in range(2):
                for l in range(2):
                    for x in range(4):
                        yield (y, h, c, l, x)


def linear(t):
    y, h, c, l, x = (v % m for v, m in zip(t, SIZES))
    return ((y * 2 + h) * 2 + c) * 8 + l * 4 + x


def move(value, y=0, h=0, c=0, l=0, x=0):
    step = (y, h, c, l, x)
    pairs = [(linear(t), linear(tuple(a + b for a, b in zip(t, step)))) for t in coords()]
    return lax.ppermute(value, BOTH, pairs)


def pick(value, index, axis):
    return lax.dynamic_index_in_dim(value, index, axis, keepdims=False)


def kernel_params():
    return pltpu.CompilerParams(vmem_limit_bytes=56 * 1024 * 1024)


def after_inputs(body, count, extra):
    return lambda *refs: body(*refs[:count], *refs[count + extra :])


def anywhere(count):
    return [pl.BlockSpec(memory_space=pl.ANY)] * count


def dot(a, b, ca=1, cb=0):
    return lax.dot_general(a, b, (((ca,), (cb,)), ((), ())), preferred_element_type=f32)


def swap_halves(value):
    lane = lax.broadcasted_iota(jnp.int32, value.shape, 1)
    return jnp.where(lane < 32, pltpu.roll(value, 96, 1), pltpu.roll(value, 32, 1))


def allowed_mask(lengths_ref, block, rows):
    e0 = lengths_ref[block, 0]
    e1 = e0 + lengths_ref[block, 1]
    t = lax.broadcasted_iota(jnp.int32, (rows, rows), 0)
    s = lax.broadcasted_iota(jnp.int32, (rows, rows), 1)
    seg_t = (t >= e0).astype(jnp.int32) + (t >= e1).astype(jnp.int32)
    seg_s = (s >= e0).astype(jnp.int32) + (s >= e1).astype(jnp.int32)
    return (seg_t == seg_s) & (s <= t)


def dot_rows(a, b):
    return lax.dot_general(a, b, (((0,), (0,)), ((), ())), preferred_element_type=f32)


def loads(copies):
    for copy in copies:
        copy.start()
    return copies


def piece_copies(pieces, half, target, sems, rows, lanes=slice(None)):
    return [
        pltpu.make_async_copy(
            piece.at[half, :, lanes] if len(piece.shape) == 3 else piece.at[:, lanes],
            target.at[pl.ds(at * rows, rows)],
            sems.at[at],
        )
        for at, piece in enumerate(pieces)
    ]


def weight_copies(pieces, refs, spot_ref, target, lanes, sems, source=None):
    if source is not None:
        pieces = [
            (
                array,
                begin + max(source - first, 0),
                min(size, 4),
                max(first, source) - source,
                spot,
                ref,
            )
            for (array, begin, size, first, spot), ref in zip(pieces, refs)
            if first <= source < first + size
        ]
    else:
        pieces = [(*piece, ref) for piece, ref in zip(pieces, refs)]
    return [
        pltpu.make_async_copy(
            ref.at[pl.ds(begin, size), :, lanes],
            target.at[pl.ds(first, size), spot_ref[spot]],
            sems.at[at],
        )
        for at, (_, begin, size, first, spot, ref) in enumerate(pieces)
    ]


def feed_forward(x, dy, gains, weight, spots, down, bias, numbers, first, after):
    rows, width = x[0].shape[1:]
    count = len(x)
    total = rows * count
    ff = bias.shape[1]

    parts = len(weight)

    def body(number_ref, spot_ref, g_ref, b_ref, *refs):
        w_refs, refs = refs[:parts], refs[parts:]
        x_refs, dy_refs, d_hbm = refs[:count], refs[count : 2 * count], refs[2 * count]
        (h1_hbm, act_hbm, du_hbm, keep_hbm, send_hbm, m_ref, i_ref, db_ref, sum_ref) = refs[
            2 * count + 1 : 2 * count + 10
        ]
        (x_v, dy_v, h1_v, h2_v, w_v, d_v, act_v, du_v, keep_v, send_v, x_sem, dy_sem, w_sem, sems) = refs[
            2 * count + 10 :
        ]
        own = number_ref[0] == 0
        x_copies = loads(piece_copies(x_refs, 0, x_v, x_sem, rows))
        w_copies = loads(
            weight_copies(weight, w_refs, spot_ref, w_v, pl.ds(first, ff), w_sem)
        )
        dy_copies = loads(piece_copies(dy_refs, 1, dy_v, dy_sem, rows))
        d_copy = pltpu.make_async_copy(d_hbm, d_v, sems.at[1])
        d_copy.start()
        for copy in x_copies:
            copy.wait()

        @pl.loop(0, count)
        def _(n):
            at = pl.ds(pl.multiple_of(n * rows, rows), rows)
            value = x_v[at, :].astype(f32)
            mean = jnp.mean(value, 1, keepdims=True)
            centre = value - mean
            inverse = lax.rsqrt(jnp.mean(centre * centre, 1, keepdims=True) + EPS)
            normed = centre * inverse
            m_ref[at, :] = mean
            i_ref[at, :] = inverse
            h1_v[at, :] = (normed * g_ref[0:1] + g_ref[1:2]).astype(bf16)
            h2_v[at, :] = (normed * g_ref[2:3] + g_ref[3:4]).astype(bf16)

        h1_copy = pltpu.make_async_copy(h1_v, h1_hbm, sems.at[2])
        h1_copy.start()
        for copy in w_copies + dy_copies:
            copy.wait()
        d_copy.wait()
        mine = dy_v[:, pl.ds(pl.multiple_of(number_ref[1] * 256, 256), 256)]
        sum_ref[...] = jnp.sum(mine.astype(f32), 0, keepdims=True)

        def split(part, places, high, wide):
            at = (places, high, wide)

            @pl.when(own)
            def _():
                keep_v[at] = part[:, 0]
                send_v[at] = part[:, 1]

            @pl.when(jnp.logical_not(own))
            def _():
                keep_v[at] = part[:, 1]
                send_v[at] = part[:, 0]

        def leaving(n):
            at = (pl.ds(n * 2, 2), pl.ds(0, 64))
            return (
                pltpu.make_async_copy(keep_v.at[at], keep_hbm.at[at], sems.at[3]),
                pltpu.make_async_copy(send_v.at[at], send_hbm.at[at], sems.at[4]),
            )

        @pl.loop(0, ff // 256)
        def _(n):
            at = pl.ds(pl.multiple_of(n * 256, 256), 256)
            u = dot(h2_v[...], w_v[:, :, :, at].reshape(width, 256)) + b_ref[:, at]
            cdf = 0.5 * (1.0 + lax.erf(u * math.sqrt(0.5)))
            pdf = jnp.exp(-0.5 * u * u) * (1.0 / math.sqrt(2.0 * math.pi))
            act = (u * cdf).astype(bf16)
            act_v[:, at] = act
            du = (dot(dy_v[...], d_v[at, :], 1, 1) * (cdf + u * pdf)).astype(bf16)
            du_v[:, at] = du
            db_ref[:, at] = jnp.sum(du.astype(f32), 0, keepdims=True)
            part = dot_rows(act, dy_v[...]).astype(bf16).reshape(2, 2, 64, width)
            split(part, pl.ds(n * 2, 2), pl.ds(0, 64), slice(None))
            for copy in leaving(n):
                copy.start()

        act_copy = pltpu.make_async_copy(act_v, act_hbm, sems.at[0])
        act_copy.start()
        du_copy = pltpu.make_async_copy(du_v, du_hbm, sems.at[1])
        du_copy.start()
        for n in range(ff // 256):
            for copy in leaving(n):
                copy.wait()

        def block(n):
            at = (
                slice(None),
                pl.ds(pl.multiple_of(64 + 16 * (n % 4), 16), 16),
                pl.ds(pl.multiple_of(n // 4 * ff, ff), ff),
            )
            return at

        def away(n):
            at = block(n)
            return (
                pltpu.make_async_copy(keep_v.at[at], keep_hbm.at[at], sems.at[3]),
                pltpu.make_async_copy(send_v.at[at], send_hbm.at[at], sems.at[4]),
            )

        @pl.loop(0, 8)
        def _(n):
            lanes = pl.ds(pl.multiple_of(n * 256, 256), 256)
            part = dot_rows(h2_v[:, lanes], du_v[...]).astype(bf16).reshape(8, 2, 16, ff)
            split(part, *block(n))
            for copy in away(n):
                copy.start()

        for n in range(8):
            for copy in away(n):
                copy.wait()
        h1_copy.wait()
        act_copy.wait()
        du_copy.wait()

    wide = jax.ShapeDtypeStruct((total, width), bf16)
    thin = jax.ShapeDtypeStruct((total, ff), bf16)
    column = jax.ShapeDtypeStruct((total, 1), f32)
    grads = jax.ShapeDtypeStruct((8, 128, width), bf16)
    vmem = pl.BlockSpec(memory_space=pltpu.VMEM)
    return pl.pallas_call(
        after_inputs(body, 5 + parts + 2 * count, len(after)),
        out_shape=(
            wide,
            thin,
            thin,
            grads,
            grads,
            column,
            column,
            jax.ShapeDtypeStruct((1, ff), f32),
            jax.ShapeDtypeStruct((1, 256), f32),
        ),
        in_specs=[pl.BlockSpec(memory_space=pltpu.SMEM)] * 2
        + [vmem, vmem]
        + anywhere(parts + 2 * count + 1 + len(after)),
        out_specs=tuple(anywhere(5)) + (vmem,) * 4,
        scratch_shapes=[
            pltpu.VMEM((total, width), bf16),
            pltpu.VMEM((total, width), bf16),
            pltpu.VMEM((total, width), bf16),
            pltpu.VMEM((total, width), bf16),
            pltpu.VMEM((8, 8, width // 64, ff), bf16),
            pltpu.VMEM((ff, width), bf16),
            pltpu.VMEM((total, ff), bf16),
            pltpu.VMEM((total, ff), bf16),
            pltpu.VMEM((8, 128, width), bf16),
            pltpu.VMEM((8, 128, width), bf16),
            pltpu.SemaphoreType.DMA((count,)),
            pltpu.SemaphoreType.DMA((count,)),
            pltpu.SemaphoreType.DMA((parts,)),
            pltpu.SemaphoreType.DMA((5,)),
        ],
        compiler_params=kernel_params(),
        cost_estimate=cost(32),
        name="feed_forward",
    )(numbers, spots, gains, bias, *[p[0] for p in weight], *x, *dy, down, *after)


def packed(qkv_weight, up_weight, vectors, lengths, place, head, tokens, cotangent):
    wide, up_wide = qkv_weight.shape[1], up_weight.shape[1]
    part, up_part = 3 * head, up_wide // 8
    cols = part + up_part

    def body(place_ref, len_ref, q_ref, u_ref, x_ref, dy_ref, *refs):
        v_refs, out_ref, pair_ref = refs[: len(vectors)], refs[-2], refs[-1]
        pair_ref[0] = x_ref[...]
        pair_ref[1] = dy_ref[...]
        lane = lax.broadcasted_iota(jnp.int32, (8, cols), 1)
        row = lax.broadcasted_iota(jnp.int32, (8, cols), 0)
        sizes = jnp.zeros((8, cols), f32)
        for at in range(3):
            sizes = jnp.where(lane == at, len_ref[0, at].astype(f32), sizes)
        vector = jnp.concatenate([ref[...].astype(f32) for ref in v_refs])[None, :]
        vector = jnp.broadcast_to(vector, (8, cols))
        tail = jnp.where(row == 0, vector, jnp.where(row == 1, sizes, 0.0)).astype(bf16)
        for owner in range(8):
            pieces = [
                q_ref[:, (third * 8 + owner) * head : (third * 8 + owner + 1) * head]
                for third in range(3)
            ]
            pieces.append(u_ref[:, owner * up_part : (owner + 1) * up_part])
            out_ref[owner] = jnp.concatenate([jnp.concatenate(pieces, 1), tail], 0)

    return pl.pallas_call(
        body,
        out_shape=(
            jax.ShapeDtypeStruct((8, 40, cols), bf16),
            jax.ShapeDtypeStruct((2,) + tokens.shape, bf16),
        ),
        grid_spec=pltpu.PrefetchScalarGridSpec(
            num_scalar_prefetch=2,
            grid=(1,),
            in_specs=[
                pl.BlockSpec((32, wide), lambda i, place, lens: (place[0], 0)),
                pl.BlockSpec((32, up_wide), lambda i, place, lens: (place[0], 0)),
                pl.BlockSpec(tokens.shape, lambda i, place, lens: (0, 0)),
                pl.BlockSpec(tokens.shape, lambda i, place, lens: (0, 0)),
            ]
            + [pl.BlockSpec(v.shape, lambda i, place, lens: (0,)) for v in vectors],
            out_specs=(
                pl.BlockSpec((8, 40, cols), lambda i, place, lens: (0, 0, 0)),
                pl.BlockSpec((2,) + tokens.shape, lambda i, place, lens: (0, 0, 0)),
            ),
        ),
        compiler_params=kernel_params(),
        cost_estimate=cost(3),
        name="packed",
    )(place, lengths, qkv_weight, up_weight, tokens, cotangent, *vectors)


def attend(h1, dy, weight, spots, out, bias, cosine, sine, lengths, after, rows=128):
    total, width = h1.shape
    count = len(dy)
    head = out.shape[0]
    scale = head ** (-0.5)

    parts = len(weight)

    def body(len_ref, spot_ref, b_ref, *refs):
        w_refs, refs = refs[:parts], refs[parts:]
        dy_refs = refs[:count]
        h1_hbm, out_hbm, cos_hbm, sin_hbm = refs[count : count + 4]
        ol_hbm, dq_hbm, sum_ref = refs[count + 4 : count + 7]
        (dy_v, h1_v, w_v, wo_v, cos_v, sin_v, qkv_v, do_v, ol_v, dq_v, dy_sem, w_sem, sems) = (
            refs[count + 7 :]
        )
        pairs = (
            (h1_hbm, h1_v),
            (out_hbm, wo_v),
            (cos_hbm, cos_v),
            (sin_hbm, sin_v),
        )
        copies = loads(
            [pltpu.make_async_copy(*pair, sems.at[n]) for n, pair in enumerate(pairs)]
        )
        w_copies = loads(
            weight_copies(weight, w_refs, spot_ref, w_v, pl.ds(0, 3 * head), w_sem)
        )
        dy_copies = loads(piece_copies(dy_refs, 1, dy_v, dy_sem, rows))
        for copy in copies[:1] + w_copies:
            copy.wait()

        @pl.loop(0, 3)
        def _(n):
            at = pl.ds(pl.multiple_of(n * head, head), head)
            qkv_v[:, at] = dot(h1_v[...], w_v[:, :, :, at].reshape(width, head)) + b_ref[n]

        for copy in copies[1:] + dy_copies:
            copy.wait()
        do_v[...] = dot(dy_v[...], wo_v[...], 1, 1).astype(bf16)
        sum_ref[...] = jnp.zeros_like(sum_ref)

        @pl.loop(0, total // rows, unroll=2)
        def _(block):
            at = pl.ds(pl.multiple_of(block * rows, rows), rows)
            cos, sin = cos_v[at, :], sin_v[at, :]

            def turned(value, sign):
                left = value[:, :128]
                left = left * cos + swap_halves(left) * (sin * sign)
                return jnp.concatenate([left, value[:, 128:]], 1).astype(bf16)

            q, k = turned(qkv_v[at, 0:head], 1.0), turned(qkv_v[at, head : 2 * head], 1.0)
            v = qkv_v[at, 2 * head :].astype(bf16)
            scores = dot(q, k, 1, 1) * scale
            masked = jnp.where(allowed_mask(len_ref, block, rows), scores, -1e30)
            shifted = jnp.exp(masked - jnp.max(masked, 1, keepdims=True))
            probs = shifted / jnp.sum(shifted, 1, keepdims=True)
            low = probs.astype(bf16)
            ol_v[at, :] = dot(low, v).astype(bf16)
            d_out = do_v[at, :]
            d_value = dot(low, d_out, 0, 0)
            d_probs = dot(d_out, v, 1, 1)
            centred = d_probs - jnp.sum(d_probs * probs, 1, keepdims=True)
            d_scores = (probs * centred).astype(bf16)
            d_query = turned(dot(d_scores, k) * scale, -1.0)
            d_key = turned(dot(d_scores, q, 0, 0) * scale, -1.0)
            for n, grad in enumerate((d_query, d_key, d_value.astype(bf16))):
                lanes = slice(n * head, (n + 1) * head)
                dq_v[at, lanes] = grad
                sum_ref[:, lanes] += jnp.sum(grad.astype(f32), 0, keepdims=True)

        ol_copy = pltpu.make_async_copy(ol_v, ol_hbm, sems.at[0])
        ol_copy.start()
        dq_copy = pltpu.make_async_copy(dq_v, dq_hbm, sems.at[1])
        dq_copy.start()

        for copy in (ol_copy, dq_copy):
            copy.wait()

    vmem = pl.BlockSpec(memory_space=pltpu.VMEM)
    smem = pl.BlockSpec(memory_space=pltpu.SMEM)
    return pl.pallas_call(
        after_inputs(body, 7 + parts + count, len(after)),
        out_shape=(
            jax.ShapeDtypeStruct((total, head), bf16),
            jax.ShapeDtypeStruct((total, 3 * head), bf16),
            jax.ShapeDtypeStruct((1, 3 * head), f32),
        ),
        in_specs=[smem, smem, vmem] + anywhere(parts + count + 4 + len(after)),
        out_specs=tuple(anywhere(2)) + (vmem,),
        scratch_shapes=[
            pltpu.VMEM((total, width), bf16),
            pltpu.VMEM((total, width), bf16),
            pltpu.VMEM((8, 8, width // 64, 3 * head), bf16),
            pltpu.VMEM((head, width), bf16),
            pltpu.VMEM((total, 128), f32),
            pltpu.VMEM((total, 128), f32),
            pltpu.VMEM((total, 3 * head), f32),
            pltpu.VMEM((total, head), bf16),
            pltpu.VMEM((total, head), bf16),
            pltpu.VMEM((total, 3 * head), bf16),
            pltpu.SemaphoreType.DMA((count,)),
            pltpu.SemaphoreType.DMA((parts,)),
            pltpu.SemaphoreType.DMA((4,)),
        ],
        compiler_params=kernel_params(),
        cost_estimate=cost(17),
        name="attend",
    )(
        lengths,
        spots,
        bias,
        *[p[0] for p in weight],
        *dy,
        h1,
        out,
        cosine,
        sine,
        *after,
    )


def attention_grads(h1, dy, d_qkv, attended, numbers, after):
    total, width = h1.shape
    count = len(dy)
    rows = total // count
    head = attended.shape[1]

    def body(number_ref, *refs):
        dy_refs = refs[:count]
        h1_hbm, dq_hbm, ol_hbm, keep_hbm, send_hbm = refs[count : count + 5]
        dy_v, h1_v, dq_v, ol_v, keep_v, send_v, dy_sem, sems = refs[count + 5 :]
        own = number_ref[0] == 0
        pairs = ((h1_hbm, h1_v), (dq_hbm, dq_v), (ol_hbm, ol_v))
        copies = loads(
            [pltpu.make_async_copy(*pair, sems.at[n]) for n, pair in enumerate(pairs)]
        )
        dy_copies = loads(piece_copies(dy_refs, 1, dy_v, dy_sem, rows))
        for copy in copies:
            copy.wait()

        def split(part, high, lanes):
            at = (slice(None), high, lanes)

            @pl.when(own)
            def _():
                keep_v[at] = part[:, 0]
                send_v[at] = part[:, 1]

            @pl.when(jnp.logical_not(own))
            def _():
                keep_v[at] = part[:, 1]
                send_v[at] = part[:, 0]

        @pl.loop(0, 8)
        def _(n):
            lanes = pl.ds(pl.multiple_of(n * 256, 256), 256)
            part = dot_rows(h1_v[:, lanes], dq_v[...]).astype(bf16).reshape(8, 2, 16, 3 * head)
            for third in range(3):
                split(
                    part[..., third * head : (third + 1) * head],
                    pl.ds(16 * third, 16),
                    pl.ds(pl.multiple_of(n * head, head), head),
                )

        for copy in dy_copies:
            copy.wait()
        part = dot_rows(ol_v[...], dy_v[...]).astype(bf16).reshape(8, 2, 16, width)
        split(part, pl.ds(48, 16), slice(None))
        keep_copy = pltpu.make_async_copy(keep_v, keep_hbm, sems.at[0])
        keep_copy.start()
        send_copy = pltpu.make_async_copy(send_v, send_hbm, sems.at[1])
        send_copy.start()
        keep_copy.wait()
        send_copy.wait()

    grads = jax.ShapeDtypeStruct((8, 64, width), bf16)
    return pl.pallas_call(
        after_inputs(body, 4 + count, len(after)),
        out_shape=(grads, grads),
        in_specs=[pl.BlockSpec(memory_space=pltpu.SMEM)] + anywhere(count + 3 + len(after)),
        out_specs=tuple(anywhere(2)),
        scratch_shapes=[
            pltpu.VMEM((total, width), bf16),
            pltpu.VMEM((total, width), bf16),
            pltpu.VMEM((total, 3 * head), bf16),
            pltpu.VMEM((total, head), bf16),
            pltpu.VMEM((8, 64, width), bf16),
            pltpu.VMEM((8, 64, width), bf16),
            pltpu.SemaphoreType.DMA((count,)),
            pltpu.SemaphoreType.DMA((3,)),
        ],
        compiler_params=kernel_params(),
        cost_estimate=cost(12),
        name="attention_grads",
    )(numbers, *dy, h1, d_qkv, attended, *after)


def mixed_part(active, attended, down, out, bias, after):
    rows, ff = active.shape
    head, width = out.shape
    step = 512
    count = rows // 128

    def body(act_ref, ol_ref, wd_ref, wo_ref, b_ref, *refs):
        total = dot(act_ref[...], wd_ref[...]) + dot(ol_ref[...], wo_ref[...]) + b_ref[...]
        for at in range(count):
            refs[at][...] = total[at * 128 : (at + 1) * 128].astype(bf16)

    return pl.pallas_call(
        after_inputs(body, 5, len(after)),
        out_shape=(jax.ShapeDtypeStruct((128, width), bf16),) * count,
        grid=(width // step,),
        in_specs=[
            pl.BlockSpec((rows, ff), lambda i: (0, 0)),
            pl.BlockSpec((rows, head), lambda i: (0, 0)),
            pl.BlockSpec((ff, step), lambda i: (0, i)),
            pl.BlockSpec((head, step), lambda i: (0, i)),
            pl.BlockSpec((1, step), lambda i: (0, i)),
        ]
        + anywhere(len(after)),
        out_specs=(pl.BlockSpec((128, step), lambda i: (0, i)),) * count,
        compiler_params=kernel_params(),
        cost_estimate=cost(10),
        name="mixed_part",
    )(active, attended, down, out, bias, *after)


def back_norms(d_qkv, d_hidden, weight, spots, x, mean, inverse, gains, part, before, after):
    total, n1 = d_qkv.shape
    n2 = d_hidden.shape[1]
    count = len(x)
    parts = len(weight)
    width = x[0].shape[-1]
    step = 512
    half = width // 2

    def body(spot_ref, m_ref, i_ref, g_ref, *refs):
        w_refs, refs = refs[:parts], refs[parts:]
        x_refs, refs = refs[:count], refs[count:]
        plain, refs = refs[:2], refs[2 + len(before) :]
        sums_ref, outs = refs[0], refs[1 : 1 + count]
        dq_v, du_v, w_v, x_v, s_v, w_sem, x_sem, sems, out_sem = refs[1 + count :]
        plain_v = (dq_v, du_v)
        copies = loads(
            [
                pltpu.make_async_copy(plain[n], plain_v[n], sems.at[n]) for n in range(2)
            ]
            + weight_copies(weight, w_refs, spot_ref, w_v, slice(None), w_sem, part * 4)
            + piece_copies(x_refs, 0, x_v, x_sem, 128, pl.ds(part * half, half))
        )
        def leaving(n):
            lanes = pl.ds(pl.multiple_of(n * step, step), step)
            there = pl.ds(pl.multiple_of(part * half + n * step, step), step)
            return [
                pltpu.make_async_copy(
                    s_v.at[pl.ds(at * 128, 128), lanes], outs[at].at[:, there], out_sem.at[at]
                )
                for at in range(count)
            ]

        for copy in copies:
            copy.wait()

        @pl.loop(0, half // step)
        def _(n):
            lanes = pl.ds(pl.multiple_of(n * step, step), step)
            gain = pl.ds(pl.multiple_of(part * half + n * step, step), step)
            sources = pl.ds(n * (step // 256), step // 256)
            d1 = dot(dq_v[...], w_v[sources, :, :, 0:n1].reshape(step, n1), 1, 1)
            d2 = dot(du_v[...], w_v[sources, :, :, n1:].reshape(step, n2), 1, 1)
            s_v[:, lanes] = (d1 * g_ref[0:1, gain] + d2 * g_ref[1:2, gain]).astype(bf16)
            for copy in leaving(n):
                copy.start()
            normed = (x_v[:, lanes].astype(f32) - m_ref[...]) * i_ref[...]
            sums_ref[0:1, lanes] = jnp.sum(d1 * normed, 0, keepdims=True)
            sums_ref[1:2, lanes] = jnp.sum(d1, 0, keepdims=True)
            sums_ref[2:3, lanes] = jnp.sum(d2 * normed, 0, keepdims=True)
            sums_ref[3:4, lanes] = jnp.sum(d2, 0, keepdims=True)

        for n in range(half // step):
            for copy in leaving(n):
                copy.wait()

    vmem = pl.BlockSpec(memory_space=pltpu.VMEM)
    return pl.pallas_call(
        after_inputs(body, 6 + parts + count + len(before), len(after)),
        out_shape=(jax.ShapeDtypeStruct((4, half), f32),)
        + (jax.ShapeDtypeStruct((128, width), bf16),) * count,
        in_specs=[pl.BlockSpec(memory_space=pltpu.SMEM)]
        + [vmem] * 3
        + anywhere(parts + count + 2 + len(before) + len(after)),
        out_specs=(vmem,) + tuple(anywhere(count)),
        scratch_shapes=[
            pltpu.VMEM((total, n1), bf16),
            pltpu.VMEM((total, n2), bf16),
            pltpu.VMEM((4, 8, width // 64, n1 + n2), bf16),
            pltpu.VMEM((total, half), bf16),
            pltpu.VMEM((total, half), bf16),
            pltpu.SemaphoreType.DMA((parts,)),
            pltpu.SemaphoreType.DMA((count,)),
            pltpu.SemaphoreType.DMA((2,)),
            pltpu.SemaphoreType.DMA((count,)),
        ],
        input_output_aliases={6 + parts + count + n: 1 + n for n in range(len(before))},
        compiler_params=kernel_params(),
        cost_estimate=cost(9),
        name="back_norms",
    )(
        spots,
        mean,
        inverse,
        gains,
        *[p[0] for p in weight],
        *x,
        d_qkv,
        d_hidden,
        *before,
        *after,
    )


def unpacked(part, after):
    owners, _, cols = part.shape

    def body(part_ref, rows_ref, info_ref):
        for owner in range(owners):
            rows_ref[owner] = part_ref[owner, 0:32]
            info_ref[owner] = part_ref[owner, 32:40].astype(f32)

    return pl.pallas_call(
        after_inputs(body, 1, len(after)),
        out_shape=(
            jax.ShapeDtypeStruct((owners, 32, cols), bf16),
            jax.ShapeDtypeStruct((owners, 8, cols), f32),
        ),
        in_specs=[pl.BlockSpec(memory_space=pltpu.VMEM)] + anywhere(len(after)),
        out_specs=(pl.BlockSpec(memory_space=pltpu.VMEM),) * 2,
        compiler_params=kernel_params(),
        cost_estimate=cost(3),
        name="unpacked",
    )(part, *after)


def joined(arrays, after):
    sizes = [array.shape[0] for array in arrays]
    unit = math.gcd(*sizes)
    block = (unit,) + arrays[0].shape[1:]
    count = len(arrays)
    firsts = [sum(sizes[:n]) // unit for n in range(count)]

    def body(*refs):
        step = pl.program_id(0)
        for ref, first, size in zip(refs, firsts, sizes):

            @pl.when((step >= first) & (step < first + size // unit))
            def _(ref=ref):
                refs[count][...] = ref[...]

    def came(first, size):
        return pl.BlockSpec(block, lambda i: (jnp.clip(i - first, 0, size // unit - 1), 0, 0))

    return pl.pallas_call(
        after_inputs(body, count, len(after)),
        out_shape=jax.ShapeDtypeStruct((sum(sizes),) + block[1:], bf16),
        grid=(sum(sizes) // unit,),
        in_specs=[came(first, size) for first, size in zip(firsts, sizes)] + anywhere(len(after)),
        out_specs=pl.BlockSpec(block, lambda i: (i, 0, 0)),
        compiler_params=kernel_params(),
        cost_estimate=cost(3),
        name="joined",
    )(*arrays, *after)


def halves(own, below, above, after):
    count, rows, cols = own.shape
    half = count // 2

    def body(own_ref, below_ref, above_ref, low_ref, high_ref, all_ref):
        step = pl.program_id(0)
        all_ref[0] = own_ref[...]
        all_ref[1] = above_ref[...]
        all_ref[2] = below_ref[...]

        @pl.when(step == 0)
        def _():
            low_ref[...] = below_ref[...]

        @pl.when(step == 1)
        def _():
            high_ref[...] = above_ref[...]

    block = pl.BlockSpec((half, rows, cols), lambda i: (i, 0, 0))
    whole = pl.BlockSpec((half, rows, cols), lambda i: (0, 0, 0))
    low, high, together = pl.pallas_call(
        after_inputs(body, 3, len(after)),
        out_shape=(jax.ShapeDtypeStruct((half, rows, cols), bf16),) * 2
        + (jax.ShapeDtypeStruct((3, count, rows, cols), bf16),),
        grid=(2,),
        in_specs=[block] * 3 + anywhere(len(after)),
        out_specs=(
            whole,
            whole,
            pl.BlockSpec((3, half, rows, cols), lambda i: (0, i, 0, 0)),
        ),
        compiler_params=kernel_params(),
        cost_estimate=cost(4),
        name="halves",
    )(own, below, above, *after)
    return low, high, together.reshape(3 * count, rows, cols)


def finished(mix, sums, tokens, cotangent, after):
    rows, width = tokens.shape
    step = rows // 2

    def body(*refs):
        x_ref, dy_ref, mixed_ref, grad_ref = refs[8:]
        x = x_ref[...].astype(f32)
        mixed_ref[...] = (x + wide(*refs[:4])).astype(bf16)
        gain = wide(*refs[4:8])
        centre = x - jnp.mean(x, 1, keepdims=True)
        inverse = lax.rsqrt(jnp.mean(centre * centre, 1, keepdims=True) + EPS)
        normed = centre * inverse
        grad_ref[...] = dy_ref[...].astype(f32) + inverse * (
            gain
            - jnp.mean(gain, 1, keepdims=True)
            - normed * jnp.mean(gain * normed, 1, keepdims=True)
        )

    block = pl.BlockSpec((step, width), lambda i: (i, 0))
    later = pl.BlockSpec((step, width), lambda i: (i + 2, 0))
    return pl.pallas_call(
        after_inputs(body, 10, len(after)),
        out_shape=(
            jax.ShapeDtypeStruct((rows, width), bf16),
            jax.ShapeDtypeStruct((rows, width), f32),
        ),
        grid=(2,),
        in_specs=[block, later, block, block] * 2 + [block, block] + anywhere(len(after)),
        out_specs=(block, block),
        compiler_params=kernel_params(),
        cost_estimate=cost(3),
        name="finished",
    )(*mix, *sums, tokens, cotangent, *after)


def packed_sums(stays, crossed, parts, norm_sums, qkv_sums, up_sums, dy_sums, numbers, ff, head, after):
    width = parts.shape[2]

    def body(*refs):
        stay_ref, cross_ref, parts_ref = refs[:3]
        norm_ref, q_ref, u_ref, y_ref, number_ref, out_ref, keep_ref, small = refs[3:]
        shard = number_ref[1]
        inner = (stay_ref[0].astype(f32) + cross_ref[0].astype(f32)).astype(bf16)
        total = jnp.sum(parts_ref[...].astype(f32), 0).astype(bf16)
        for owner in range(8):
            mine = shard == owner
            small[...] = jnp.zeros_like(small)
            small[0:4] = norm_ref[:, owner * head : (owner + 1) * head]
            for n in range(3):
                third, source = divmod(owner * 3 + n, 8)
                lanes = slice(third * head, (third + 1) * head)
                small[4 + n : 5 + n] = jnp.where(shard == source, q_ref[:, lanes], 0.0)
            for n in range(4):
                lanes = slice(n * head, (n + 1) * head)
                small[7 + n : 8 + n] = jnp.where(mine, u_ref[:, lanes], 0.0)
            small[11:12] = jnp.where(mine, y_ref[...], 0.0)
            pieces = [
                total[16 * third : 16 * third + 16, owner * head : (owner + 1) * head]
                for third in range(3)
            ]
            row, col = 64 + 16 * (owner % 4), owner // 4 * ff
            pieces.append(inner[row : row + 16, col : col + ff])
            pieces.append(small[...].astype(bf16))
            out_ref[owner] = jnp.concatenate(pieces, 1)
        keep_ref[0:64] = inner[0:64]
        keep_ref[64:80] = total[48:64]

    vmem = pl.BlockSpec(memory_space=pltpu.VMEM)
    return pl.pallas_call(
        after_inputs(body, 8, len(after)),
        out_shape=(
            jax.ShapeDtypeStruct((8, 16, 4 * head + ff), bf16),
            jax.ShapeDtypeStruct((80, width), bf16),
        ),
        in_specs=[vmem] * 7 + [pl.BlockSpec(memory_space=pltpu.SMEM)] + anywhere(len(after)),
        out_specs=(vmem,) * 2,
        scratch_shapes=[pltpu.VMEM((16, head), f32)],
        compiler_params=kernel_params(),
        cost_estimate=cost(3),
        name="packed_sums",
    )(stays, crossed, parts, norm_sums, qkv_sums, up_sums, dy_sums, numbers, *after)


def unpacked_sums(received, n1, n2, after):
    sources, rows, width = received.shape
    cols = n1 + n2
    total = sources * rows

    def body(part_ref, up_ref, rest_ref):
        small = jnp.sum(part_ref[:, :, cols:].astype(f32), 0).astype(bf16)
        up_ref[0] = part_ref[:, :, n1:cols].reshape(total, n2)
        rest_ref[0] = jnp.concatenate(
            [jnp.concatenate([part_ref[0, :, 0:n1], small], 1)]
            + [
                jnp.concatenate([part_ref[n, :, 0:n1], part_ref[n, :, cols:]], 1)
                for n in range(1, sources)
            ],
            0,
        )

    def block(size):
        return pl.BlockSpec((1, total, size), lambda i: (i, 0, 0))

    return pl.pallas_call(
        after_inputs(body, 1, len(after)),
        out_shape=(
            jax.ShapeDtypeStruct((8, total, n2), bf16),
            jax.ShapeDtypeStruct((8, total, width - n2), bf16),
        ),
        grid=(8,),
        in_specs=[pl.BlockSpec(received.shape, lambda i: (0, 0, 0))] + anywhere(len(after)),
        out_specs=(block(n2), block(width - n2)),
        compiler_params=kernel_params(),
        cost_estimate=cost(3),
        name="unpacked_sums",
    )(received, *after)


def held(array, after):
    def body(*refs):
        pass

    return pl.pallas_call(
        body,
        out_shape=jax.ShapeDtypeStruct(array.shape, array.dtype),
        in_specs=anywhere(1 + len(after)),
        out_specs=pl.BlockSpec(memory_space=pl.ANY),
        input_output_aliases={0: 0},
        compiler_params=kernel_params(),
        cost_estimate=cost(1),
        name="held",
    )(array, *after)


def blocks_call(name, body, numbers, terms, outs, after, time=3):
    def came(block, index):
        rest = (0,) * (len(block) - 1)
        return pl.BlockSpec(block, lambda i, n: (index(n),) + rest)

    return pl.pallas_call(
        after_inputs(body, 1 + len(terms), len(after)),
        out_shape=tuple(jax.ShapeDtypeStruct(out, bf16) for out in outs),
        grid_spec=pltpu.PrefetchScalarGridSpec(
            num_scalar_prefetch=1,
            grid=(1,),
            in_specs=[came(block, index) for _, block, index in terms] + anywhere(len(after)),
            out_specs=tuple(
                pl.BlockSpec(out, lambda i, n, size=len(out): (0,) * size) for out in outs
            ),
        ),
        compiler_params=kernel_params(),
        cost_estimate=cost(time),
        name=name,
    )(numbers, *[array for array, _, _ in terms], *after)


def wide(*refs):
    return functools.reduce(jnp.add, [ref[...].astype(f32) for ref in refs])


def spread(pieces, places, core, targets, count, before, after):
    rows, cols = pieces[0][0].shape[1:]
    firsts, total = [], 0
    for mine, _ in pieces:
        firsts.append(total)
        total += mine.shape[0]

    def body(place_ref, core_ref, *refs):
        step = pl.program_id(0)
        outs = refs[2 * len(pieces) + len(before) :]
        first_core = core_ref[0] == 0

        def fill(ref, low):
            for out_ref, (_, high, parts) in zip(outs, targets):
                for to, row, col, size in parts:
                    out_ref[low * high : (low + 1) * high, to : to + size] = ref[
                        0, row : row + high, col : col + size
                    ].astype(f32)

        for n, (first, (mine, _)) in enumerate(zip(firsts, pieces)):
            here = (step >= first) & (step < first + mine.shape[0])

            @pl.when(here & first_core)
            def _(n=n):
                fill(refs[2 * n], 0)
                fill(refs[2 * n + 1], 1)

            @pl.when(here & jnp.logical_not(first_core))
            def _(n=n):
                fill(refs[2 * n], 1)
                fill(refs[2 * n + 1], 0)

    def chosen(first, size):
        return pl.BlockSpec(
            (1, rows, cols), lambda i, place, core: (jnp.clip(i - first, 0, size - 1), 0, 0)
        )

    specs, arrays = [], []
    for first, (mine, yours) in zip(firsts, pieces):
        specs += [chosen(first, mine.shape[0])] * 2
        arrays += [mine, yours]
    return pl.pallas_call(
        after_inputs(body, 2 + 2 * len(pieces) + len(before), len(after)),
        out_shape=tuple(
            jax.ShapeDtypeStruct((2 * count * high, wide), f32) for wide, high, _ in targets
        ),
        grid_spec=pltpu.PrefetchScalarGridSpec(
            num_scalar_prefetch=2,
            grid=(total,),
            in_specs=specs + anywhere(len(before) + len(after)),
            out_specs=tuple(
                pl.BlockSpec((2 * high, wide), lambda i, place, core: (place[i], 0))
                for wide, high, _ in targets
            ),
        ),
        input_output_aliases={2 + len(arrays) + n: n for n in range(len(before))},
        compiler_params=kernel_params(),
        cost_estimate=cost(0.3 * total),
        name="spread",
    )(places, core, *arrays, *before, *after)


def local(
    tokens,
    doc_lengths,
    cotangent,
    ln1_gain,
    ln1_bias,
    ln2_gain,
    ln2_bias,
    qkv_weight,
    qkv_bias,
    out_weight,
    out_bias,
    up_weight,
    up_bias,
    down_weight,
    down_bias,
):
    rows, width = tokens.shape
    head = width // HEADS
    group = 8
    rep = lax.axis_index("rep")
    shard = lax.axis_index("shard")
    y, h, c = rep // 4, (rep // 2) % 2, rep % 2
    l, x = shard // 4, shard % 4
    ff = up_bias.shape[0]

    cols = 3 * head + ff
    vectors = [ln1_gain, ln1_bias, ln2_gain, ln2_bias, qkv_bias]
    place = (y * 2 + c).astype(jnp.int32).reshape(1)
    part, pair = packed(
        qkv_weight, up_weight, vectors, doc_lengths, place, head, tokens, cotangent
    )
    below, above, other = move(pair, x=1), move(pair, x=-1), move(pair, l=1)
    far, other_above, other_below = move(below, x=1), move(other, x=-1), move(below, l=1)
    pairs = (pair, above, far, below, other, other_above, None, other_below)

    part = lax.all_to_all(part, "shard", 0, 0)
    own, infos = unpacked(part, (pairs[1], pairs[3], pairs[4]))
    below, above = move(own, y=1), move(own, y=-1)
    x_other_far, dy_other_far = move(other_below[0], x=1), move(other_above[1], x=-1)
    low, high, yours = halves(own, below, above, (far, other_above, other_below))
    far_low, far_high = move(low, y=1), move(high, y=-1)
    x_all = tuple(x_other_far if p is None else p for p in pairs)
    dy_all = tuple(dy_other_far if p is None else p for p in pairs)
    yours = move(yours, c=1)
    far_low_c, far_high_c = move(far_low, c=1), move(far_high, c=1)
    weight = (
        (own, 0, 8, 0, 0),
        (above, 0, 8, 0, 1),
        (far_low, 0, 4, 0, 2),
        (far_high, 0, 4, 4, 2),
        (below, 0, 8, 0, 3),
        (yours, 0, 8, 0, 4),
        (yours, 8, 8, 0, 5),
        (far_low_c, 0, 4, 0, 6),
        (far_high_c, 0, 4, 4, 6),
        (yours, 16, 8, 0, 7),
    )
    steps4 = (y + jnp.arange(4)) % 4
    spots = jnp.concatenate([steps4 * 2 + c, steps4 * 2 + 1 - c]).astype(jnp.int32)

    gains = infos[:, 0, :1024].reshape(8, 4, 256).transpose(1, 0, 2).reshape(4, width)
    qkv_b = infos[:, 0, 1024:].reshape(8 * 3, 1, head)
    qkv_b = jnp.stack(
        [lax.dynamic_index_in_dim(qkv_b, third * 8 + shard, 0, False) for third in range(3)]
    )
    steps8 = jnp.arange(8)
    sources = ((steps8 // 4) ^ l) * 4 + (x + steps8 % 4) % 4
    sources = sources.astype(jnp.int32)
    lengths = infos[:, 1, :3]
    lengths = jnp.sum(
        jnp.where(sources[:, None, None] == steps8[None, :, None], lengths[None], 0.0), 1
    ).astype(jnp.int32)
    ends = jnp.cumsum(lengths, 1)
    starts = ends - lengths
    steps_t = jnp.arange(rows, dtype=jnp.int32)
    segment = jnp.sum((steps_t[None, :, None] >= ends[:, None, :]).astype(jnp.int32), -1)
    slots = jnp.arange(lengths.shape[1], dtype=jnp.int32)
    begin = jnp.sum(
        jnp.where(segment[:, :, None] == slots[None, None, :], starts[:, None, :], 0), -1
    )
    position = (steps_t[None, :] - begin).astype(f32).reshape(group * rows, 1)
    lane = jnp.arange(128)
    freq = 10000.0 ** (-2.0 * (lane % (ROT // 2)).astype(f32) / ROT)
    angle = position * freq[None, :]
    cosine = jnp.where(lane < ROT, jnp.cos(angle), 1.0)
    sine = jnp.sin(angle)
    sine = jnp.where(lane < ROT // 2, -sine, jnp.where(lane < ROT, sine, 0.0))

    both_bias = (out_bias.astype(f32) + down_bias.astype(f32))[None, :]
    wide_bias = lax.dynamic_update_slice(jnp.zeros((1, width), f32), both_bias, (0, shard * 256))
    numbers = jnp.stack([c, shard, y, h]).astype(jnp.int32)

    h1, active, d_hidden, keep, send, mean, inverse, up_sums, dy_sums = feed_forward(
        x_all,
        dy_all,
        gains,
        weight,
        spots,
        down_weight,
        up_bias.astype(f32)[None],
        numbers,
        3 * head,
        (cosine, sine),
    )
    got = move(send, c=1)
    attended, d_qkv, qkv_sums = attend(
        h1, dy_all, weight, spots, out_weight, qkv_b, cosine, sine, lengths, (send,)
    )

    pair_shape, one = (2, 128, width), (1, 128, width)

    def turn(k):
        return lambda n: (n[2] + k) % 4

    def far_body(n_ref, keep_ref, got_ref, low_ref, high_ref):
        total = wide(keep_ref, got_ref).astype(bf16)
        low_ref[0] = total[0]
        high_ref[0] = total[1]

    low, high = blocks_call(
        "far_sums",
        far_body,
        numbers,
        [(keep, pair_shape, turn(2)), (got, pair_shape, turn(2))],
        (one, one),
        (attended,),
    )
    from_low, from_high = move(low, y=1), move(high, y=-1)
    a_keep, a_send = attention_grads(h1, dy_all, d_qkv, attended, numbers, (low, high))
    a_got = move(a_send, c=1)
    def near_body(n_ref, k1_ref, g1_ref, k3_ref, g3_ref, low_ref, high_ref, above_ref, below_ref):
        above, below = wide(k1_ref, g1_ref), wide(k3_ref, g3_ref)
        above_ref[0] = (above[0] + low_ref[0].astype(f32)).astype(bf16)
        above_ref[1] = above[1].astype(bf16)
        below_ref[0] = below[0].astype(bf16)
        below_ref[1] = (below[1] + high_ref[0].astype(f32)).astype(bf16)

    above, below = blocks_call(
        "near_sums",
        near_body,
        numbers,
        [(v, pair_shape, turn(k)) for k in (1, 3) for v in (keep, got)]
        + [(v, one, lambda n: 0) for v in (from_low, from_high)],
        (pair_shape, pair_shape),
        (a_send,),
        20,
    )
    from_below, from_above = move(above, y=1), move(below, y=-1)

    four = (4, 64, width)

    def both_body(n_ref, low_keep, low_got, high_keep, high_got, out_ref):
        out_ref[0:4] = wide(low_keep, low_got).astype(bf16)
        out_ref[4:8] = wide(high_keep, high_got).astype(bf16)

    (a_sent,) = blocks_call(
        "both_sums",
        both_body,
        numbers,
        [(v, four, lambda n, half=half: half) for half in range(2) for v in (a_keep, a_got)],
        ((8, 64, width),),
        (above,),
    )
    a_parts = lax.all_to_all(a_sent, "rep", 0, 0, axis_index_groups=SAME_CORE)
    mix = mixed_part(active, attended, down_weight, out_weight, wide_bias, (a_sent, above, below))
    def norms_back(part, before, after):
        return back_norms(
            d_qkv,
            d_hidden,
            weight,
            spots,
            x_all,
            mean,
            inverse,
            jnp.stack([gains[0], gains[2]]),
            part,
            before,
            after,
        )

    low_sums, *sums = norms_back(0, (), (mix[0],))

    flat, both = (128, width), (256, width)

    def passed_body(n_ref, up_ref, from_below, here_ref, down_ref, from_above, there_ref, up_out, down_out):
        up_out[0:128] = wide(up_ref, from_below).astype(bf16)
        up_out[128:256] = here_ref[...]
        down_out[0:128] = wide(down_ref, from_above).astype(bf16)
        down_out[128:256] = there_ref[...]

    def other_body(n_ref, own_ref, below_ref, above_ref, *refs):
        passing = len(refs) // 2
        refs[passing][...] = wide(own_ref, below_ref, above_ref).astype(bf16)
        for at in range(passing):
            refs[passing + 1 + at][...] = refs[at][...]

    def first(n):
        return 0

    def ring_start(high, low):
        return move(high, x=1), move(low, x=-1)

    def ring_middle(pieces, passed, after):
        operands = (pieces[5], passed[0], pieces[1], pieces[3], passed[1], pieces[7])
        ups, downs = blocks_call(
            "passed_sums",
            passed_body,
            numbers,
            [(v, flat, first) for v in operands],
            (both, both),
            after,
        )
        return (move(ups, x=1), move(downs, x=-1)), ups

    def ring_end(pieces, arrived, passing):
        other, *copies = blocks_call(
            "other_sums",
            other_body,
            numbers,
            [
                (pieces[4], flat, first),
                (arrived[0], flat, first),
                (arrived[1], flat, lambda n: 1),
            ]
            + [(v, flat, first) for v in passing],
            (flat,) * (1 + len(passing)),
            (),
        )
        return (pieces[0], *arrived, move(other, l=1)), other, *copies

    mix_passed = ring_start(mix[6], mix[2])

    def ends_body(n_ref, keep_ref, got_ref, below_ref, above_ref, leave_ref, stay_ref):
        total = wide(keep_ref, got_ref, below_ref, above_ref).astype(bf16)
        first = n_ref[3] == 0
        leave_ref[0] = jnp.where(first, total[1], total[0])
        stay_ref[0] = jnp.where(first, total[0], total[1])

    leaves, stays = blocks_call(
        "end_sums",
        ends_body,
        numbers,
        [(v, pair_shape, turn(0)) for v in (keep, got)]
        + [(v, pair_shape, lambda n: 0) for v in (from_below, from_above)],
        (one, one),
        (low_sums,),
    )
    crossed = move(leaves, h=1)

    mix_arrived, mix_ups = ring_middle(mix, mix_passed, (leaves,))
    high_sums, *sums = norms_back(1, tuple(sums), (mix_ups,))

    part, stays = packed_sums(
        stays,
        crossed,
        a_parts,
        jnp.concatenate([low_sums, high_sums], 1),
        qkv_sums,
        up_sums,
        dy_sums,
        numbers,
        ff,
        head,
        (),
    )
    received = lax.all_to_all(part, "shard", 0, 0)
    mix_left, mix_other, high, low = ring_end(mix, mix_arrived, (sums[6], sums[2]))
    stays_pair = jnp.concatenate([stays[None], move(stays[None], h=1)])
    up, rest = unpacked_sums(received, 3 * head, ff, (mix_other, stays_pair))
    order = ((0, h), (0, 1 - h), (1, h), (1, 1 - h), (3, h), (3, 1 - h), (2, h), (2, 1 - h))
    places = jnp.stack([(y + k) % 4 * 2 + high for k, high in order]).astype(jnp.int32)

    sums_arrived, sums_ups = ring_middle(sums, ring_start(high, low), (received,))
    sums_left, sums_other = ring_end(sums, sums_arrived, ())
    stays = stays_pair
    below, above = move(stays, y=1), move(stays, y=-1)
    stays = joined((stays, above, below, move(below, y=1)), ())
    down_grad, out_grad = spread(
        [(stays, move(stays, c=1))],
        places,
        numbers[:1],
        [(width, 64, [(0, 0, 0, width)]), (width, 16, [(0, 64, 0, width)])],
        8,
        (),
        (mix_left[3],),
    )
    mixed, tokens_grad = finished(mix_left, sums_left, tokens, cotangent, ())
    order = jnp.arange(8, dtype=jnp.int32)
    up = lax.all_to_all(up, "rep", 0, 0, axis_index_groups=SAME_CORE)
    up = held(up, (stays,))
    rest = lax.all_to_all(rest, "rep", 0, 0, axis_index_groups=SAME_CORE)
    (up_grad,) = spread(
        [(up, move(up, c=1))],
        order,
        numbers[:1],
        [(8 * ff, 16, [(source * ff, 16 * source, 0, ff) for source in range(8)])],
        8,
        (),
        (),
    )
    rest = held(rest, (down_grad, up_grad, tokens_grad))
    rest_yours = move(rest, c=1)
    (qkv_grad,) = spread(
        [(rest, rest_yours)],
        order,
        numbers[:1],
        [
            (
                3 * width,
                16,
                [
                    ((third * 8 + source) * head, 16 * source, third * head, head)
                    for source in range(8)
                    for third in range(3)
                ],
            )
        ],
        8,
        (),
        (),
    )
    smalls = [v[:, 0:16, 3 * head :] for v in (rest, rest_yours)]
    smalls = jnp.sum(jnp.concatenate(smalls).astype(f32), 0)
    norm_grads = smalls[:4]
    dy_total = smalls[11]
    return (
        mixed,
        tokens_grad,
        norm_grads[0],
        norm_grads[1],
        norm_grads[2],
        norm_grads[3],
        qkv_grad,
        smalls[4:7].reshape(3 * head),
        out_grad,
        dy_total,
        up_grad,
        smalls[7:11].reshape(ff),
        down_grad,
        dy_total,
    )


def solution(mesh):
    rows = P(BOTH, None)
    vector, matrix = P("shard"), P("shard", None)
    return jax.shard_map(
        local,
        mesh=mesh,
        in_specs=(rows, rows, rows, vector, vector, vector, vector)
        + (matrix, vector, matrix, vector, matrix, vector, matrix, vector),
        out_specs=(rows, rows, vector, vector, vector, vector)
        + (matrix, vector, matrix, vector, matrix, vector, matrix, vector),
        check_vma=False,
    )
```

```python
import functools
import math

import jax
import jax.numpy as jnp
from jax import lax
from jax.experimental import pallas as pl
from jax.experimental.pallas import tpu as pltpu
from jax.sharding import PartitionSpec as P

HEADS = 8
ROT = 64
EPS = 1e-05
f32 = jnp.float32
bf16 = jnp.bfloat16


def cost(time):
    return pl.CostEstimate(flops=int(time * 1.15e9), bytes_accessed=1000, transcendentals=0)


BOTH = ("rep", "shard")
SIZES = (4, 2, 2, 2, 4)
SAME_CORE = [[2 * n + c for n in range(8)] for c in range(2)]
SAME_CORE_ALL = [[(2 * n + c) * 8 + s for n in range(8) for s in range(8)] for c in range(2)]


def coords():
    for y in range(4):
        for h in range(2):
            for c in range(2):
                for l in range(2):
                    for x in range(4):
                        yield (y, h, c, l, x)


def linear(t):
    y, h, c, l, x = (v % m for v, m in zip(t, SIZES))
    return ((y * 2 + h) * 2 + c) * 8 + l * 4 + x


def move(value, y=0, h=0, c=0, l=0, x=0):
    step = (y, h, c, l, x)
    pairs = [(linear(t), linear(tuple(a + b for a, b in zip(t, step)))) for t in coords()]
    return lax.ppermute(value, BOTH, pairs)


def pick(value, index, axis):
    return lax.dynamic_index_in_dim(value, index, axis, keepdims=False)


def kernel_params():
    return pltpu.CompilerParams(vmem_limit_bytes=56 * 1024 * 1024)


def after_inputs(body, count, extra):
    return lambda *refs: body(*refs[:count], *refs[count + extra :])


def anywhere(count):
    return [pl.BlockSpec(memory_space=pl.ANY)] * count


def dot(a, b, ca=1, cb=0):
    return lax.dot_general(a, b, (((ca,), (cb,)), ((), ())), preferred_element_type=f32)


def swap_halves(value):
    lane = lax.broadcasted_iota(jnp.int32, value.shape, 1)
    return jnp.where(lane < 32, pltpu.roll(value, 96, 1), pltpu.roll(value, 32, 1))


def allowed_mask(lengths_ref, block, rows):
    e0 = lengths_ref[block, 0]
    e1 = e0 + lengths_ref[block, 1]
    t = lax.broadcasted_iota(jnp.int32, (rows, rows), 0)
    s = lax.broadcasted_iota(jnp.int32, (rows, rows), 1)
    seg_t = (t >= e0).astype(jnp.int32) + (t >= e1).astype(jnp.int32)
    seg_s = (s >= e0).astype(jnp.int32) + (s >= e1).astype(jnp.int32)
    return (seg_t == seg_s) & (s <= t)


def dot_rows(a, b):
    return lax.dot_general(a, b, (((0,), (0,)), ((), ())), preferred_element_type=f32)


def loads(copies):
    for copy in copies:
        copy.start()
    return copies


def piece_copies(pieces, half, target, sems, rows, lanes=slice(None)):
    return [
        pltpu.make_async_copy(
            piece.at[half, :, lanes] if len(piece.shape) == 3 else piece.at[:, lanes],
            target.at[pl.ds(at * rows, rows)],
            sems.at[at],
        )
        for at, piece in enumerate(pieces)
    ]


def weight_copies(pieces, refs, spot_ref, target, lanes, sems, source=None):
    if source is not None:
        pieces = [
            (
                array,
                begin + max(source - first, 0),
                min(size, 4),
                max(first, source) - source,
                spot,
                ref,
            )
            for (array, begin, size, first, spot), ref in zip(pieces, refs)
            if first <= source < first + size
        ]
    else:
        pieces = [(*piece, ref) for piece, ref in zip(pieces, refs)]
    return [
        pltpu.make_async_copy(
            ref.at[pl.ds(begin, size), :, lanes],
            target.at[pl.ds(first, size), spot_ref[spot]],
            sems.at[at],
        )
        for at, (_, begin, size, first, spot, ref) in enumerate(pieces)
    ]


def feed_forward(x, dy, gains, weight, spots, down, bias, numbers, first, after):
    rows, width = x[0].shape[1:]
    count = len(x)
    total = rows * count
    ff = bias.shape[1]

    parts = len(weight)

    def body(number_ref, spot_ref, g_ref, b_ref, *refs):
        w_refs, refs = refs[:parts], refs[parts:]
        x_refs, dy_refs, d_hbm = refs[:count], refs[count : 2 * count], refs[2 * count]
        (h1_hbm, act_hbm, du_hbm, keep_hbm, send_hbm, m_ref, i_ref, db_ref, sum_ref) = refs[
            2 * count + 1 : 2 * count + 10
        ]
        (x_v, dy_v, h1_v, h2_v, w_v, d_v, act_v, du_v, keep_v, send_v, x_sem, dy_sem, w_sem, sems) = refs[
            2 * count + 10 :
        ]
        own = number_ref[0] == 0
        x_copies = loads(piece_copies(x_refs, 0, x_v, x_sem, rows))
        w_copies = loads(
            weight_copies(weight, w_refs, spot_ref, w_v, pl.ds(first, ff), w_sem)
        )
        dy_copies = loads(piece_copies(dy_refs, 1, dy_v, dy_sem, rows))
        d_copy = pltpu.make_async_copy(d_hbm, d_v, sems.at[1])
        d_copy.start()
        for copy in x_copies:
            copy.wait()

        @pl.loop(0, count)
        def _(n):
            at = pl.ds(pl.multiple_of(n * rows, rows), rows)
            value = x_v[at, :].astype(f32)
            mean = jnp.mean(value, 1, keepdims=True)
            centre = value - mean
            inverse = lax.rsqrt(jnp.mean(centre * centre, 1, keepdims=True) + EPS)
            normed = centre * inverse
            m_ref[at, :] = mean
            i_ref[at, :] = inverse
            h1_v[at, :] = (normed * g_ref[0:1] + g_ref[1:2]).astype(bf16)
            h2_v[at, :] = (normed * g_ref[2:3] + g_ref[3:4]).astype(bf16)

        h1_copy = pltpu.make_async_copy(h1_v, h1_hbm, sems.at[2])
        h1_copy.start()
        for copy in w_copies + dy_copies:
            copy.wait()
        d_copy.wait()
        mine = dy_v[:, pl.ds(pl.multiple_of(number_ref[1] * 256, 256), 256)]
        sum_ref[...] = jnp.sum(mine.astype(f32), 0, keepdims=True)

        def split(part, places, high, wide):
            at = (places, high, wide)

            @pl.when(own)
            def _():
                keep_v[at] = part[:, 0]
                send_v[at] = part[:, 1]

            @pl.when(jnp.logical_not(own))
            def _():
                keep_v[at] = part[:, 1]
                send_v[at] = part[:, 0]

        def leaving(n):
            at = (pl.ds(n * 2, 2), pl.ds(0, 64))
            return (
                pltpu.make_async_copy(keep_v.at[at], keep_hbm.at[at], sems.at[3]),
                pltpu.make_async_copy(send_v.at[at], send_hbm.at[at], sems.at[4]),
            )

        @pl.loop(0, ff // 256)
        def _(n):
            at = pl.ds(pl.multiple_of(n * 256, 256), 256)
            u = dot(h2_v[...], w_v[:, :, :, at].reshape(width, 256)) + b_ref[:, at]
            cdf = 0.5 * (1.0 + lax.erf(u * math.sqrt(0.5)))
            pdf = jnp.exp(-0.5 * u * u) * (1.0 / math.sqrt(2.0 * math.pi))
            act = (u * cdf).astype(bf16)
            act_v[:, at] = act
            du = (dot(dy_v[...], d_v[at, :], 1, 1) * (cdf + u * pdf)).astype(bf16)
            du_v[:, at] = du
            db_ref[:, at] = jnp.sum(du.astype(f32), 0, keepdims=True)
            part = dot_rows(act, dy_v[...]).astype(bf16).reshape(2, 2, 64, width)
            split(part, pl.ds(n * 2, 2), pl.ds(0, 64), slice(None))
            for copy in leaving(n):
                copy.start()

        act_copy = pltpu.make_async_copy(act_v, act_hbm, sems.at[0])
        act_copy.start()
        du_copy = pltpu.make_async_copy(du_v, du_hbm, sems.at[1])
        du_copy.start()
        for n in range(ff // 256):
            for copy in leaving(n):
                copy.wait()

        def block(n):
            at = (
                slice(None),
                pl.ds(pl.multiple_of(64 + 16 * (n % 4), 16), 16),
                pl.ds(pl.multiple_of(n // 4 * ff, ff), ff),
            )
            return at

        def away(n):
            at = block(n)
            return (
                pltpu.make_async_copy(keep_v.at[at], keep_hbm.at[at], sems.at[3]),
                pltpu.make_async_copy(send_v.at[at], send_hbm.at[at], sems.at[4]),
            )

        @pl.loop(0, 8)
        def _(n):
            lanes = pl.ds(pl.multiple_of(n * 256, 256), 256)
            part = dot_rows(h2_v[:, lanes], du_v[...]).astype(bf16).reshape(8, 2, 16, ff)
            split(part, *block(n))
            for copy in away(n):
                copy.start()

        for n in range(8):
            for copy in away(n):
                copy.wait()
        h1_copy.wait()
        act_copy.wait()
        du_copy.wait()

    wide = jax.ShapeDtypeStruct((total, width), bf16)
    thin = jax.ShapeDtypeStruct((total, ff), bf16)
    column = jax.ShapeDtypeStruct((total, 1), f32)
    grads = jax.ShapeDtypeStruct((8, 128, width), bf16)
    vmem = pl.BlockSpec(memory_space=pltpu.VMEM)
    return pl.pallas_call(
        after_inputs(body, 5 + parts + 2 * count, len(after)),
        out_shape=(
            wide,
            thin,
            thin,
            grads,
            grads,
            column,
            column,
            jax.ShapeDtypeStruct((1, ff), f32),
            jax.ShapeDtypeStruct((1, 256), f32),
        ),
        in_specs=[pl.BlockSpec(memory_space=pltpu.SMEM)] * 2
        + [vmem, vmem]
        + anywhere(parts + 2 * count + 1 + len(after)),
        out_specs=tuple(anywhere(5)) + (vmem,) * 4,
        scratch_shapes=[
            pltpu.VMEM((total, width), bf16),
            pltpu.VMEM((total, width), bf16),
            pltpu.VMEM((total, width), bf16),
            pltpu.VMEM((total, width), bf16),
            pltpu.VMEM((8, 8, width // 64, ff), bf16),
            pltpu.VMEM((ff, width), bf16),
            pltpu.VMEM((total, ff), bf16),
            pltpu.VMEM((total, ff), bf16),
            pltpu.VMEM((8, 128, width), bf16),
            pltpu.VMEM((8, 128, width), bf16),
            pltpu.SemaphoreType.DMA((count,)),
            pltpu.SemaphoreType.DMA((count,)),
            pltpu.SemaphoreType.DMA((parts,)),
            pltpu.SemaphoreType.DMA((5,)),
        ],
        compiler_params=kernel_params(),
        cost_estimate=cost(32),
        name="feed_forward",
    )(numbers, spots, gains, bias, *[p[0] for p in weight], *x, *dy, down, *after)


def packed(qkv_weight, up_weight, vectors, lengths, place, head, tokens, cotangent):
    wide, up_wide = qkv_weight.shape[1], up_weight.shape[1]
    part, up_part = 3 * head, up_wide // 8
    cols = part + up_part

    def body(place_ref, len_ref, q_ref, u_ref, x_ref, dy_ref, *refs):
        v_refs, out_ref, pair_ref = refs[: len(vectors)], refs[-2], refs[-1]
        pair_ref[0] = x_ref[...]
        pair_ref[1] = dy_ref[...]
        lane = lax.broadcasted_iota(jnp.int32, (8, cols), 1)
        row = lax.broadcasted_iota(jnp.int32, (8, cols), 0)
        sizes = jnp.zeros((8, cols), f32)
        for at in range(3):
            sizes = jnp.where(lane == at, len_ref[0, at].astype(f32), sizes)
        vector = jnp.concatenate([ref[...].astype(f32) for ref in v_refs])[None, :]
        vector = jnp.broadcast_to(vector, (8, cols))
        tail = jnp.where(row == 0, vector, jnp.where(row == 1, sizes, 0.0)).astype(bf16)
        for owner in range(8):
            pieces = [
                q_ref[:, (third * 8 + owner) * head : (third * 8 + owner + 1) * head]
                for third in range(3)
            ]
            pieces.append(u_ref[:, owner * up_part : (owner + 1) * up_part])
            out_ref[owner] = jnp.concatenate([jnp.concatenate(pieces, 1), tail], 0)

    return pl.pallas_call(
        body,
        out_shape=(
            jax.ShapeDtypeStruct((8, 40, cols), bf16),
            jax.ShapeDtypeStruct((2,) + tokens.shape, bf16),
        ),
        grid_spec=pltpu.PrefetchScalarGridSpec(
            num_scalar_prefetch=2,
            grid=(1,),
            in_specs=[
                pl.BlockSpec((32, wide), lambda i, place, lens: (place[0], 0)),
                pl.BlockSpec((32, up_wide), lambda i, place, lens: (place[0], 0)),
                pl.BlockSpec(tokens.shape, lambda i, place, lens: (0, 0)),
                pl.BlockSpec(tokens.shape, lambda i, place, lens: (0, 0)),
            ]
            + [pl.BlockSpec(v.shape, lambda i, place, lens: (0,)) for v in vectors],
            out_specs=(
                pl.BlockSpec((8, 40, cols), lambda i, place, lens: (0, 0, 0)),
                pl.BlockSpec((2,) + tokens.shape, lambda i, place, lens: (0, 0, 0)),
            ),
        ),
        compiler_params=kernel_params(),
        cost_estimate=cost(3),
        name="packed",
    )(place, lengths, qkv_weight, up_weight, tokens, cotangent, *vectors)


def attend(h1, dy, weight, spots, out, bias, cosine, sine, lengths, after, rows=128):
    total, width = h1.shape
    count = len(dy)
    head = out.shape[0]
    scale = head ** (-0.5)

    parts = len(weight)

    def body(len_ref, spot_ref, b_ref, *refs):
        w_refs, refs = refs[:parts], refs[parts:]
        dy_refs = refs[:count]
        h1_hbm, out_hbm, cos_hbm, sin_hbm = refs[count : count + 4]
        ol_hbm, dq_hbm, sum_ref = refs[count + 4 : count + 7]
        (dy_v, h1_v, w_v, wo_v, cos_v, sin_v, qkv_v, do_v, ol_v, dq_v, dy_sem, w_sem, sems) = (
            refs[count + 7 :]
        )
        pairs = (
            (h1_hbm, h1_v),
            (out_hbm, wo_v),
            (cos_hbm, cos_v),
            (sin_hbm, sin_v),
        )
        copies = loads(
            [pltpu.make_async_copy(*pair, sems.at[n]) for n, pair in enumerate(pairs)]
        )
        w_copies = loads(
            weight_copies(weight, w_refs, spot_ref, w_v, pl.ds(0, 3 * head), w_sem)
        )
        dy_copies = loads(piece_copies(dy_refs, 1, dy_v, dy_sem, rows))
        for copy in copies[:1] + w_copies:
            copy.wait()

        @pl.loop(0, 3)
        def _(n):
            at = pl.ds(pl.multiple_of(n * head, head), head)
            qkv_v[:, at] = dot(h1_v[...], w_v[:, :, :, at].reshape(width, head)) + b_ref[n]

        for copy in copies[1:] + dy_copies:
            copy.wait()
        do_v[...] = dot(dy_v[...], wo_v[...], 1, 1).astype(bf16)
        sum_ref[...] = jnp.zeros_like(sum_ref)

        @pl.loop(0, total // rows, unroll=2)
        def _(block):
            at = pl.ds(pl.multiple_of(block * rows, rows), rows)
            cos, sin = cos_v[at, :], sin_v[at, :]

            def turned(value, sign):
                left = value[:, :128]
                left = left * cos + swap_halves(left) * (sin * sign)
                return jnp.concatenate([left, value[:, 128:]], 1).astype(bf16)

            q, k = turned(qkv_v[at, 0:head], 1.0), turned(qkv_v[at, head : 2 * head], 1.0)
            v = qkv_v[at, 2 * head :].astype(bf16)
            scores = dot(q, k, 1, 1) * scale
            masked = jnp.where(allowed_mask(len_ref, block, rows), scores, -1e30)
            shifted = jnp.exp(masked - jnp.max(masked, 1, keepdims=True))
            probs = shifted / jnp.sum(shifted, 1, keepdims=True)
            low = probs.astype(bf16)
            ol_v[at, :] = dot(low, v).astype(bf16)
            d_out = do_v[at, :]
            d_value = dot(low, d_out, 0, 0)
            d_probs = dot(d_out, v, 1, 1)
            centred = d_probs - jnp.sum(d_probs * probs, 1, keepdims=True)
            d_scores = (probs * centred).astype(bf16)
            d_query = turned(dot(d_scores, k) * scale, -1.0)
            d_key = turned(dot(d_scores, q, 0, 0) * scale, -1.0)
            for n, grad in enumerate((d_query, d_key, d_value.astype(bf16))):
                lanes = slice(n * head, (n + 1) * head)
                dq_v[at, lanes] = grad
                sum_ref[:, lanes] += jnp.sum(grad.astype(f32), 0, keepdims=True)

        ol_copy = pltpu.make_async_copy(ol_v, ol_hbm, sems.at[0])
        ol_copy.start()
        dq_copy = pltpu.make_async_copy(dq_v, dq_hbm, sems.at[1])
        dq_copy.start()

        for copy in (ol_copy, dq_copy):
            copy.wait()

    vmem = pl.BlockSpec(memory_space=pltpu.VMEM)
    smem = pl.BlockSpec(memory_space=pltpu.SMEM)
    return pl.pallas_call(
        after_inputs(body, 7 + parts + count, len(after)),
        out_shape=(
            jax.ShapeDtypeStruct((total, head), bf16),
            jax.ShapeDtypeStruct((total, 3 * head), bf16),
            jax.ShapeDtypeStruct((1, 3 * head), f32),
        ),
        in_specs=[smem, smem, vmem] + anywhere(parts + count + 4 + len(after)),
        out_specs=tuple(anywhere(2)) + (vmem,),
        scratch_shapes=[
            pltpu.VMEM((total, width), bf16),
            pltpu.VMEM((total, width), bf16),
            pltpu.VMEM((8, 8, width // 64, 3 * head), bf16),
            pltpu.VMEM((head, width), bf16),
            pltpu.VMEM((total, 128), f32),
            pltpu.VMEM((total, 128), f32),
            pltpu.VMEM((total, 3 * head), f32),
            pltpu.VMEM((total, head), bf16),
            pltpu.VMEM((total, head), bf16),
            pltpu.VMEM((total, 3 * head), bf16),
            pltpu.SemaphoreType.DMA((count,)),
            pltpu.SemaphoreType.DMA((parts,)),
            pltpu.SemaphoreType.DMA((4,)),
        ],
        compiler_params=kernel_params(),
        cost_estimate=cost(17),
        name="attend",
    )(
        lengths,
        spots,
        bias,
        *[p[0] for p in weight],
        *dy,
        h1,
        out,
        cosine,
        sine,
        *after,
    )


def attention_grads(h1, dy, d_qkv, attended, numbers, after):
    total, width = h1.shape
    count = len(dy)
    rows = total // count
    head = attended.shape[1]

    def body(number_ref, *refs):
        dy_refs = refs[:count]
        h1_hbm, dq_hbm, ol_hbm, keep_hbm, send_hbm = refs[count : count + 5]
        dy_v, h1_v, dq_v, ol_v, keep_v, send_v, dy_sem, sems = refs[count + 5 :]
        own = number_ref[0] == 0
        pairs = ((h1_hbm, h1_v), (dq_hbm, dq_v), (ol_hbm, ol_v))
        copies = loads(
            [pltpu.make_async_copy(*pair, sems.at[n]) for n, pair in enumerate(pairs)]
        )
        dy_copies = loads(piece_copies(dy_refs, 1, dy_v, dy_sem, rows))
        for copy in copies:
            copy.wait()

        def split(part, high, lanes):
            at = (slice(None), high, lanes)

            @pl.when(own)
            def _():
                keep_v[at] = part[:, 0]
                send_v[at] = part[:, 1]

            @pl.when(jnp.logical_not(own))
            def _():
                keep_v[at] = part[:, 1]
                send_v[at] = part[:, 0]

        @pl.loop(0, 8)
        def _(n):
            lanes = pl.ds(pl.multiple_of(n * 256, 256), 256)
            part = dot_rows(h1_v[:, lanes], dq_v[...]).astype(bf16).reshape(8, 2, 16, 3 * head)
            for third in range(3):
                split(
                    part[..., third * head : (third + 1) * head],
                    pl.ds(16 * third, 16),
                    pl.ds(pl.multiple_of(n * head, head), head),
                )

        for copy in dy_copies:
            copy.wait()
        part = dot_rows(ol_v[...], dy_v[...]).astype(bf16).reshape(8, 2, 16, width)
        split(part, pl.ds(48, 16), slice(None))
        keep_copy = pltpu.make_async_copy(keep_v, keep_hbm, sems.at[0])
        keep_copy.start()
        send_copy = pltpu.make_async_copy(send_v, send_hbm, sems.at[1])
        send_copy.start()
        keep_copy.wait()
        send_copy.wait()

    grads = jax.ShapeDtypeStruct((8, 64, width), bf16)
    return pl.pallas_call(
        after_inputs(body, 4 + count, len(after)),
        out_shape=(grads, grads),
        in_specs=[pl.BlockSpec(memory_space=pltpu.SMEM)] + anywhere(count + 3 + len(after)),
        out_specs=tuple(anywhere(2)),
        scratch_shapes=[
            pltpu.VMEM((total, width), bf16),
            pltpu.VMEM((total, width), bf16),
            pltpu.VMEM((total, 3 * head), bf16),
            pltpu.VMEM((total, head), bf16),
            pltpu.VMEM((8, 64, width), bf16),
            pltpu.VMEM((8, 64, width), bf16),
            pltpu.SemaphoreType.DMA((count,)),
            pltpu.SemaphoreType.DMA((3,)),
        ],
        compiler_params=kernel_params(),
        cost_estimate=cost(12),
        name="attention_grads",
    )(numbers, *dy, h1, d_qkv, attended, *after)


def outer(d_qkv, d_hidden, weight, spots, x, mean, inverse, gains, active, attended, down, out, bias, after):
    total, n1 = d_qkv.shape
    n2 = d_hidden.shape[1]
    count = len(x)
    parts = len(weight)
    head, width = out.shape
    step = 512

    def body(spot_ref, m_ref, i_ref, g_ref, b_ref, *refs):
        w_refs, refs = refs[:parts], refs[parts:]
        x_refs, refs = refs[:count], refs[count:]
        plain, sums_ref, outs = refs[:6], refs[6], refs[7 : 7 + count]
        dq_v, du_v, act_v, ol_v, wd_v, wo_v, w_v, x_v, pair_v, w_sem, x_sem, sems, out_sem = refs[
            7 + count :
        ]
        plain_v = (dq_v, du_v, act_v, ol_v, wd_v, wo_v)
        first = loads(
            [
                pltpu.make_async_copy(plain[n], plain_v[n], sems.at[n]) for n in range(2, 6)
            ]
        )
        copies = loads(
            [
                pltpu.make_async_copy(plain[n], plain_v[n], sems.at[n]) for n in range(2)
            ]
            + weight_copies(weight, w_refs, spot_ref, w_v, slice(None), w_sem)
            + piece_copies(x_refs, 0, x_v, x_sem, 128)
        )
        for copy in first:
            copy.wait()

        def leaving(n, half):
            lanes = pl.ds(pl.multiple_of(n * step, step), step)
            return [
                pltpu.make_async_copy(
                    pair_v.at[half, pl.ds(at * 128, 128), lanes],
                    outs[at].at[half, :, lanes],
                    out_sem.at[half, at],
                )
                for at in range(count)
            ]

        @pl.loop(0, width // step)
        def _(n):
            lanes = pl.ds(pl.multiple_of(n * step, step), step)
            mix = dot(act_v[...], wd_v[:, lanes]) + dot(ol_v[...], wo_v[:, lanes])
            pair_v[0, :, lanes] = (mix + b_ref[:, lanes]).astype(bf16)
            for copy in leaving(n, 0):
                copy.start()

        for copy in copies:
            copy.wait()

        @pl.loop(0, width // step)
        def _(n):
            lanes = pl.ds(pl.multiple_of(n * step, step), step)
            sources = pl.ds(n * (step // 256), step // 256)
            d1 = dot(dq_v[...], w_v[sources, :, :, 0:n1].reshape(step, n1), 1, 1)
            d2 = dot(du_v[...], w_v[sources, :, :, n1:].reshape(step, n2), 1, 1)
            pair_v[1, :, lanes] = (d1 * g_ref[0:1, lanes] + d2 * g_ref[1:2, lanes]).astype(bf16)
            for copy in leaving(n, 1):
                copy.start()
            normed = (x_v[:, lanes].astype(f32) - m_ref[...]) * i_ref[...]
            sums_ref[0:1, lanes] = jnp.sum(d1 * normed, 0, keepdims=True)
            sums_ref[1:2, lanes] = jnp.sum(d1, 0, keepdims=True)
            sums_ref[2:3, lanes] = jnp.sum(d2 * normed, 0, keepdims=True)
            sums_ref[3:4, lanes] = jnp.sum(d2, 0, keepdims=True)

        for n in range(width // step):
            for half in range(2):
                for copy in leaving(n, half):
                    copy.wait()

    vmem = pl.BlockSpec(memory_space=pltpu.VMEM)
    return pl.pallas_call(
        after_inputs(body, 11 + parts + count, len(after)),
        out_shape=(jax.ShapeDtypeStruct((4, width), f32),)
        + (jax.ShapeDtypeStruct((2, 128, width), bf16),) * count,
        in_specs=[pl.BlockSpec(memory_space=pltpu.SMEM)]
        + [vmem] * 4
        + anywhere(parts + count + 6 + len(after)),
        out_specs=(vmem,) + tuple(anywhere(count)),
        scratch_shapes=[
            pltpu.VMEM((total, n1), bf16),
            pltpu.VMEM((total, n2), bf16),
            pltpu.VMEM((total, n2), bf16),
            pltpu.VMEM((total, head), bf16),
            pltpu.VMEM((n2, width), bf16),
            pltpu.VMEM((head, width), bf16),
            pltpu.VMEM((8, 8, width // 64, n1 + n2), bf16),
            pltpu.VMEM((total, width), bf16),
            pltpu.VMEM((2, total, width), bf16),
            pltpu.SemaphoreType.DMA((parts,)),
            pltpu.SemaphoreType.DMA((count,)),
            pltpu.SemaphoreType.DMA((6,)),
            pltpu.SemaphoreType.DMA((2, count)),
        ],
        compiler_params=kernel_params(),
        cost_estimate=cost(20),
        name="outer",
    )(
        spots,
        mean,
        inverse,
        gains,
        bias,
        *[p[0] for p in weight],
        *x,
        d_qkv,
        d_hidden,
        active,
        attended,
        down,
        out,
        *after,
    )


def unpacked(part, after):
    owners, _, cols = part.shape

    def body(part_ref, rows_ref, info_ref):
        for owner in range(owners):
            rows_ref[owner] = part_ref[owner, 0:32]
            info_ref[owner] = part_ref[owner, 32:40].astype(f32)

    return pl.pallas_call(
        after_inputs(body, 1, len(after)),
        out_shape=(
            jax.ShapeDtypeStruct((owners, 32, cols), bf16),
            jax.ShapeDtypeStruct((owners, 8, cols), f32),
        ),
        in_specs=[pl.BlockSpec(memory_space=pltpu.VMEM)] + anywhere(len(after)),
        out_specs=(pl.BlockSpec(memory_space=pltpu.VMEM),) * 2,
        compiler_params=kernel_params(),
        cost_estimate=cost(3),
        name="unpacked",
    )(part, *after)


def joined(arrays, after):
    sizes = [array.shape[0] for array in arrays]
    unit = math.gcd(*sizes)
    block = (unit,) + arrays[0].shape[1:]
    count = len(arrays)
    firsts = [sum(sizes[:n]) // unit for n in range(count)]

    def body(*refs):
        step = pl.program_id(0)
        for ref, first, size in zip(refs, firsts, sizes):

            @pl.when((step >= first) & (step < first + size // unit))
            def _(ref=ref):
                refs[count][...] = ref[...]

    def came(first, size):
        return pl.BlockSpec(block, lambda i: (jnp.clip(i - first, 0, size // unit - 1), 0, 0))

    return pl.pallas_call(
        after_inputs(body, count, len(after)),
        out_shape=jax.ShapeDtypeStruct((sum(sizes),) + block[1:], bf16),
        grid=(sum(sizes) // unit,),
        in_specs=[came(first, size) for first, size in zip(firsts, sizes)] + anywhere(len(after)),
        out_specs=pl.BlockSpec(block, lambda i: (i, 0, 0)),
        compiler_params=kernel_params(),
        cost_estimate=cost(3),
        name="joined",
    )(*arrays, *after)


def halves(own, below, above, after):
    count, rows, cols = own.shape
    half = count // 2

    def body(own_ref, below_ref, above_ref, low_ref, high_ref, all_ref):
        step = pl.program_id(0)
        all_ref[0] = own_ref[...]
        all_ref[1] = above_ref[...]
        all_ref[2] = below_ref[...]

        @pl.when(step == 0)
        def _():
            low_ref[...] = below_ref[...]

        @pl.when(step == 1)
        def _():
            high_ref[...] = above_ref[...]

    block = pl.BlockSpec((half, rows, cols), lambda i: (i, 0, 0))
    whole = pl.BlockSpec((half, rows, cols), lambda i: (0, 0, 0))
    low, high, together = pl.pallas_call(
        after_inputs(body, 3, len(after)),
        out_shape=(jax.ShapeDtypeStruct((half, rows, cols), bf16),) * 2
        + (jax.ShapeDtypeStruct((3, count, rows, cols), bf16),),
        grid=(2,),
        in_specs=[block] * 3 + anywhere(len(after)),
        out_specs=(
            whole,
            whole,
            pl.BlockSpec((3, half, rows, cols), lambda i: (0, i, 0, 0)),
        ),
        compiler_params=kernel_params(),
        cost_estimate=cost(4),
        name="halves",
    )(own, below, above, *after)
    return low, high, together.reshape(3 * count, rows, cols)


def unpacked_sums(received, cols, after):
    sources, rows, width = received.shape

    def body(part_ref, out_ref):
        small = jnp.sum(part_ref[:, :, cols:].astype(f32), 0).astype(bf16)
        out_ref[0] = jnp.concatenate(
            [jnp.concatenate([part_ref[0, :, 0:cols], small], 1)]
            + [part_ref[n] for n in range(1, sources)],
            0,
        )

    vmem = pl.BlockSpec(memory_space=pltpu.VMEM)
    return pl.pallas_call(
        after_inputs(body, 1, len(after)),
        out_shape=jax.ShapeDtypeStruct((1, sources * rows, width), bf16),
        in_specs=[vmem] + anywhere(len(after)),
        out_specs=vmem,
        compiler_params=kernel_params(),
        cost_estimate=cost(3),
        name="unpacked_sums",
    )(received, *after)


def packed_sums(stays, crossed, parts, norm_sums, qkv_sums, up_sums, dy_sums, numbers, ff, head, after):
    width = parts.shape[2]

    def body(*refs):
        stay_ref, cross_ref, parts_ref = refs[:3]
        norm_ref, q_ref, u_ref, y_ref, number_ref, out_ref, keep_ref, small = refs[3:]
        shard = number_ref[1]
        inner = (stay_ref[0].astype(f32) + cross_ref[0].astype(f32)).astype(bf16)
        total = jnp.sum(parts_ref[...].astype(f32), 0).astype(bf16)
        for owner in range(8):
            mine = shard == owner
            small[...] = jnp.zeros_like(small)
            small[0:4] = norm_ref[:, owner * head : (owner + 1) * head]
            for n in range(3):
                third, source = divmod(owner * 3 + n, 8)
                lanes = slice(third * head, (third + 1) * head)
                small[4 + n : 5 + n] = jnp.where(shard == source, q_ref[:, lanes], 0.0)
            for n in range(4):
                lanes = slice(n * head, (n + 1) * head)
                small[7 + n : 8 + n] = jnp.where(mine, u_ref[:, lanes], 0.0)
            small[11:12] = jnp.where(mine, y_ref[...], 0.0)
            pieces = [
                total[16 * third : 16 * third + 16, owner * head : (owner + 1) * head]
                for third in range(3)
            ]
            row, col = 64 + 16 * (owner % 4), owner // 4 * ff
            pieces.append(inner[row : row + 16, col : col + ff])
            pieces.append(small[...].astype(bf16))
            out_ref[owner] = jnp.concatenate(pieces, 1)
        keep_ref[0:64] = inner[0:64]
        keep_ref[64:80] = total[48:64]

    vmem = pl.BlockSpec(memory_space=pltpu.VMEM)
    return pl.pallas_call(
        after_inputs(body, 8, len(after)),
        out_shape=(
            jax.ShapeDtypeStruct((8, 16, 4 * head + ff), bf16),
            jax.ShapeDtypeStruct((80, width), bf16),
        ),
        in_specs=[vmem] * 7 + [pl.BlockSpec(memory_space=pltpu.SMEM)] + anywhere(len(after)),
        out_specs=(vmem,) * 2,
        scratch_shapes=[pltpu.VMEM((16, head), f32)],
        compiler_params=kernel_params(),
        cost_estimate=cost(3),
        name="packed_sums",
    )(stays, crossed, parts, norm_sums, qkv_sums, up_sums, dy_sums, numbers, *after)


def finished(own, below, above, other, tokens, cotangent, after):
    rows, width = tokens.shape
    step = rows // 2

    def body(own_ref, below_ref, above_ref, other_ref, x_ref, dy_ref, mixed_ref, grad_ref):
        total = wide(own_ref, below_ref, above_ref, other_ref)
        x = x_ref[...].astype(f32)
        mixed_ref[...] = (x + total[0]).astype(bf16)
        centre = x - jnp.mean(x, 1, keepdims=True)
        inverse = lax.rsqrt(jnp.mean(centre * centre, 1, keepdims=True) + EPS)
        normed = centre * inverse
        gain = total[1]
        grad_ref[...] = dy_ref[...].astype(f32) + inverse * (
            gain
            - jnp.mean(gain, 1, keepdims=True)
            - normed * jnp.mean(gain * normed, 1, keepdims=True)
        )

    def pair(first):
        return pl.BlockSpec((2, step, width), lambda i: (first, i, 0))

    block = pl.BlockSpec((step, width), lambda i: (i, 0))
    return pl.pallas_call(
        after_inputs(body, 6, len(after)),
        out_shape=(
            jax.ShapeDtypeStruct((rows, width), bf16),
            jax.ShapeDtypeStruct((rows, width), f32),
        ),
        grid=(2,),
        in_specs=[pair(0), pair(1), pair(0), pair(0), block, block] + anywhere(len(after)),
        out_specs=(block, block),
        compiler_params=kernel_params(),
        cost_estimate=cost(3),
        name="finished",
    )(own, below, above, other, tokens, cotangent, *after)


def blocks_call(name, body, numbers, terms, outs, after, time=3):
    def came(block, index):
        rest = (0,) * (len(block) - 1)
        return pl.BlockSpec(block, lambda i, n: (index(n),) + rest)

    return pl.pallas_call(
        after_inputs(body, 1 + len(terms), len(after)),
        out_shape=tuple(jax.ShapeDtypeStruct(out, bf16) for out in outs),
        grid_spec=pltpu.PrefetchScalarGridSpec(
            num_scalar_prefetch=1,
            grid=(1,),
            in_specs=[came(block, index) for _, block, index in terms] + anywhere(len(after)),
            out_specs=tuple(
                pl.BlockSpec(out, lambda i, n, size=len(out): (0,) * size) for out in outs
            ),
        ),
        compiler_params=kernel_params(),
        cost_estimate=cost(time),
        name=name,
    )(numbers, *[array for array, _, _ in terms], *after)


def wide(*refs):
    return functools.reduce(jnp.add, [ref[...].astype(f32) for ref in refs])


def spread(pieces, places, core, targets, count, before, after):
    rows, cols = pieces[0][0].shape[1:]
    firsts, total = [], 0
    for mine, _ in pieces:
        firsts.append(total)
        total += mine.shape[0]

    def body(place_ref, core_ref, *refs):
        step = pl.program_id(0)
        outs = refs[2 * len(pieces) + len(before) :]
        first_core = core_ref[0] == 0

        def fill(ref, low):
            for out_ref, (_, high, parts) in zip(outs, targets):
                for to, row, col, size in parts:
                    out_ref[low * high : (low + 1) * high, to : to + size] = ref[
                        0, row : row + high, col : col + size
                    ].astype(f32)

        for n, (first, (mine, _)) in enumerate(zip(firsts, pieces)):
            here = (step >= first) & (step < first + mine.shape[0])

            @pl.when(here & first_core)
            def _(n=n):
                fill(refs[2 * n], 0)
                fill(refs[2 * n + 1], 1)

            @pl.when(here & jnp.logical_not(first_core))
            def _(n=n):
                fill(refs[2 * n], 1)
                fill(refs[2 * n + 1], 0)

    def chosen(first, size):
        return pl.BlockSpec(
            (1, rows, cols), lambda i, place, core: (jnp.clip(i - first, 0, size - 1), 0, 0)
        )

    specs, arrays = [], []
    for first, (mine, yours) in zip(firsts, pieces):
        specs += [chosen(first, mine.shape[0])] * 2
        arrays += [mine, yours]
    return pl.pallas_call(
        after_inputs(body, 2 + 2 * len(pieces) + len(before), len(after)),
        out_shape=tuple(
            jax.ShapeDtypeStruct((2 * count * high, wide), f32) for wide, high, _ in targets
        ),
        grid_spec=pltpu.PrefetchScalarGridSpec(
            num_scalar_prefetch=2,
            grid=(total,),
            in_specs=specs + anywhere(len(before) + len(after)),
            out_specs=tuple(
                pl.BlockSpec((2 * high, wide), lambda i, place, core: (place[i], 0))
                for wide, high, _ in targets
            ),
        ),
        input_output_aliases={2 + len(arrays) + n: n for n in range(len(before))},
        compiler_params=kernel_params(),
        cost_estimate=cost(0.3 * total),
        name="spread",
    )(places, core, *arrays, *before, *after)


def local(
    tokens,
    doc_lengths,
    cotangent,
    ln1_gain,
    ln1_bias,
    ln2_gain,
    ln2_bias,
    qkv_weight,
    qkv_bias,
    out_weight,
    out_bias,
    up_weight,
    up_bias,
    down_weight,
    down_bias,
):
    rows, width = tokens.shape
    head = width // HEADS
    group = 8
    rep = lax.axis_index("rep")
    shard = lax.axis_index("shard")
    y, h, c = rep // 4, (rep // 2) % 2, rep % 2
    l, x = shard // 4, shard % 4
    ff = up_bias.shape[0]

    cols = 3 * head + ff
    vectors = [ln1_gain, ln1_bias, ln2_gain, ln2_bias, qkv_bias]
    place = (y * 2 + c).astype(jnp.int32).reshape(1)
    part, pair = packed(
        qkv_weight, up_weight, vectors, doc_lengths, place, head, tokens, cotangent
    )
    below, above, other = move(pair, x=1), move(pair, x=-1), move(pair, l=1)
    far, other_above, other_below = move(below, x=1), move(other, x=-1), move(below, l=1)
    pairs = (pair, above, far, below, other, other_above, None, other_below)

    part = lax.all_to_all(part, "shard", 0, 0)
    own, infos = unpacked(part, (pairs[1], pairs[3], pairs[4]))
    below, above = move(own, y=1), move(own, y=-1)
    x_other_far, dy_other_far = move(other_below[0], x=1), move(other_above[1], x=-1)
    low, high, yours = halves(own, below, above, (far, other_above, other_below))
    far_low, far_high = move(low, y=1), move(high, y=-1)
    x_all = tuple(x_other_far if p is None else p for p in pairs)
    dy_all = tuple(dy_other_far if p is None else p for p in pairs)
    yours = move(yours, c=1)
    far_low_c, far_high_c = move(far_low, c=1), move(far_high, c=1)
    weight = (
        (own, 0, 8, 0, 0),
        (above, 0, 8, 0, 1),
        (far_low, 0, 4, 0, 2),
        (far_high, 0, 4, 4, 2),
        (below, 0, 8, 0, 3),
        (yours, 0, 8, 0, 4),
        (yours, 8, 8, 0, 5),
        (far_low_c, 0, 4, 0, 6),
        (far_high_c, 0, 4, 4, 6),
        (yours, 16, 8, 0, 7),
    )
    steps4 = (y + jnp.arange(4)) % 4
    spots = jnp.concatenate([steps4 * 2 + c, steps4 * 2 + 1 - c]).astype(jnp.int32)

    gains = infos[:, 0, :1024].reshape(8, 4, 256).transpose(1, 0, 2).reshape(4, width)
    qkv_b = infos[:, 0, 1024:].reshape(8 * 3, 1, head)
    qkv_b = jnp.stack(
        [lax.dynamic_index_in_dim(qkv_b, third * 8 + shard, 0, False) for third in range(3)]
    )
    steps8 = jnp.arange(8)
    sources = ((steps8 // 4) ^ l) * 4 + (x + steps8 % 4) % 4
    sources = sources.astype(jnp.int32)
    lengths = infos[:, 1, :3]
    lengths = jnp.sum(
        jnp.where(sources[:, None, None] == steps8[None, :, None], lengths[None], 0.0), 1
    ).astype(jnp.int32)
    ends = jnp.cumsum(lengths, 1)
    starts = ends - lengths
    steps_t = jnp.arange(rows, dtype=jnp.int32)
    segment = jnp.sum((steps_t[None, :, None] >= ends[:, None, :]).astype(jnp.int32), -1)
    slots = jnp.arange(lengths.shape[1], dtype=jnp.int32)
    begin = jnp.sum(
        jnp.where(segment[:, :, None] == slots[None, None, :], starts[:, None, :], 0), -1
    )
    position = (steps_t[None, :] - begin).astype(f32).reshape(group * rows, 1)
    lane = jnp.arange(128)
    freq = 10000.0 ** (-2.0 * (lane % (ROT // 2)).astype(f32) / ROT)
    angle = position * freq[None, :]
    cosine = jnp.where(lane < ROT, jnp.cos(angle), 1.0)
    sine = jnp.sin(angle)
    sine = jnp.where(lane < ROT // 2, -sine, jnp.where(lane < ROT, sine, 0.0))

    both_bias = (out_bias.astype(f32) + down_bias.astype(f32))[None, :]
    wide_bias = lax.dynamic_update_slice(jnp.zeros((1, width), f32), both_bias, (0, shard * 256))
    numbers = jnp.stack([c, shard, y, h]).astype(jnp.int32)

    h1, active, d_hidden, keep, send, mean, inverse, up_sums, dy_sums = feed_forward(
        x_all,
        dy_all,
        gains,
        weight,
        spots,
        down_weight,
        up_bias.astype(f32)[None],
        numbers,
        3 * head,
        (cosine, sine),
    )
    got = move(send, c=1)
    attended, d_qkv, qkv_sums = attend(
        h1, dy_all, weight, spots, out_weight, qkv_b, cosine, sine, lengths, (send,)
    )

    pair_shape, one = (2, 128, width), (1, 128, width)

    def turn(k):
        return lambda n: (n[2] + k) % 4

    def far_body(n_ref, keep_ref, got_ref, low_ref, high_ref):
        total = wide(keep_ref, got_ref).astype(bf16)
        low_ref[0] = total[0]
        high_ref[0] = total[1]

    low, high = blocks_call(
        "far_sums",
        far_body,
        numbers,
        [(keep, pair_shape, turn(2)), (got, pair_shape, turn(2))],
        (one, one),
        (attended,),
    )
    from_low, from_high = move(low, y=1), move(high, y=-1)
    a_keep, a_send = attention_grads(h1, dy_all, d_qkv, attended, numbers, (low, high))
    a_got = move(a_send, c=1)
    def near_body(n_ref, k1_ref, g1_ref, k3_ref, g3_ref, low_ref, high_ref, above_ref, below_ref):
        above, below = wide(k1_ref, g1_ref), wide(k3_ref, g3_ref)
        above_ref[0] = (above[0] + low_ref[0].astype(f32)).astype(bf16)
        above_ref[1] = above[1].astype(bf16)
        below_ref[0] = below[0].astype(bf16)
        below_ref[1] = (below[1] + high_ref[0].astype(f32)).astype(bf16)

    above, below = blocks_call(
        "near_sums",
        near_body,
        numbers,
        [(v, pair_shape, turn(k)) for k in (1, 3) for v in (keep, got)]
        + [(v, one, lambda n: 0) for v in (from_low, from_high)],
        (pair_shape, pair_shape),
        (a_send,),
        20,
    )
    from_below, from_above = move(above, y=1), move(below, y=-1)

    four = (4, 64, width)

    def both_body(n_ref, low_keep, low_got, high_keep, high_got, out_ref):
        out_ref[0:4] = wide(low_keep, low_got).astype(bf16)
        out_ref[4:8] = wide(high_keep, high_got).astype(bf16)

    (a_sent,) = blocks_call(
        "both_sums",
        both_body,
        numbers,
        [(v, four, lambda n, half=half: half) for half in range(2) for v in (a_keep, a_got)],
        ((8, 64, width),),
        (above,),
    )
    a_parts = lax.all_to_all(a_sent, "rep", 0, 0, axis_index_groups=SAME_CORE)
    norm_sums, *pairs_out = outer(
        d_qkv,
        d_hidden,
        weight,
        spots,
        x_all,
        mean,
        inverse,
        jnp.stack([gains[0], gains[2]]),
        active,
        attended,
        down_weight,
        out_weight,
        wide_bias,
        (a_sent, above, below),
    )

    passed_below, passed_above = move(pairs_out[6], x=1), move(pairs_out[2], x=-1)

    def passed_body(n_ref, up_ref, from_below, here_ref, down_ref, from_above, there_ref, up_out, down_out):
        up_out[0:2] = wide(up_ref, from_below).astype(bf16)
        up_out[2:4] = here_ref[...]
        down_out[0:2] = wide(down_ref, from_above).astype(bf16)
        down_out[2:4] = there_ref[...]

    def other_body(n_ref, own_ref, below_ref, above_ref, out_ref):
        out_ref[...] = wide(own_ref, below_ref, above_ref).astype(bf16)

    def first(n):
        return 0

    def ends_body(n_ref, keep_ref, got_ref, below_ref, above_ref, leave_ref, stay_ref):
        total = wide(keep_ref, got_ref, below_ref, above_ref).astype(bf16)
        first = n_ref[3] == 0
        leave_ref[0] = jnp.where(first, total[1], total[0])
        stay_ref[0] = jnp.where(first, total[0], total[1])

    leaves, stays = blocks_call(
        "end_sums",
        ends_body,
        numbers,
        [(v, pair_shape, turn(0)) for v in (keep, got)]
        + [(v, pair_shape, lambda n: 0) for v in (from_below, from_above)],
        (one, one),
        (norm_sums,),
    )
    crossed = move(leaves, h=1)

    part, stays = packed_sums(
        stays,
        crossed,
        a_parts,
        norm_sums,
        qkv_sums,
        up_sums,
        dy_sums,
        numbers,
        ff,
        head,
        (),
    )
    received = lax.all_to_all(part, "shard", 0, 0)
    ups, downs = blocks_call(
        "passed_sums",
        passed_body,
        numbers,
        [
            (v, pair_shape, first)
            for v in (
                pairs_out[5],
                passed_below,
                pairs_out[1],
                pairs_out[3],
                passed_above,
                pairs_out[7],
            )
        ],
        ((4, 128, width),) * 2,
        (part,),
    )
    stays = stays[None]
    stays = jnp.concatenate([stays, move(stays, h=1)])
    part = unpacked_sums(received, cols, (ups, stays))
    beside = move(stays, y=1), move(stays, y=-1)
    stays = joined((stays, beside[1], beside[0], move(beside[0], y=1)), ())
    from_device_below, from_device_above = move(ups, x=1), move(downs, x=-1)
    (sent_other,) = blocks_call(
        "other_sums",
        other_body,
        numbers,
        [
            (pairs_out[4], pair_shape, first),
            (from_device_below, pair_shape, first),
            (from_device_above, pair_shape, lambda n: 1),
        ],
        (pair_shape,),
        (),
    )
    total_other = move(sent_other, l=1)

    order = ((0, h), (0, 1 - h), (1, h), (1, 1 - h), (3, h), (3, 1 - h), (2, h), (2, 1 - h))
    places = jnp.stack([(y + k) % 4 * 2 + high for k, high in order]).astype(jnp.int32)

    down_grad, out_grad = spread(
        [(stays, move(stays, c=1))],
        places,
        numbers[:1],
        [(width, 64, [(0, 0, 0, width)]), (width, 16, [(0, 64, 0, width)])],
        8,
        (),
        (),
    )
    part = joined((part, move(part, h=1)), beside)
    below, above = move(part, y=1), move(part, y=-1)
    low, high, near = halves(part, below, above, (stays, sent_other))
    far = move(low, y=1), move(high, y=-1)
    targets = [
        (
            3 * width,
            16,
            [
                ((third * 8 + source) * head, 16 * source, third * head, head)
                for source in range(8)
                for third in range(3)
            ],
        ),
        (8 * ff, 16, [(source * ff, 16 * source, 3 * head, ff) for source in range(8)]),
    ]
    near_yours = move(near, c=1)
    grads = spread(
        [(near, near_yours)], places[:6], numbers[:1], targets, 8, (), (down_grad, sent_other)
    )
    far = joined(far, (grads[0],))
    mixed, tokens_grad = finished(
        pairs_out[0], from_device_below, from_device_above, total_other, tokens, cotangent, (far,)
    )
    far_yours = move(far, c=1)
    qkv_grad, up_grad = spread(
        [(far, far_yours)],
        places[6:],
        numbers[:1],
        targets,
        8,
        grads,
        (tokens_grad,),
    )
    smalls = [v[:, 0:16, cols:] for v in (near, near_yours, far, far_yours)]
    smalls = jnp.sum(jnp.concatenate(smalls).astype(f32), 0)
    norm_grads = smalls[:4]
    dy_total = smalls[11]
    return (
        mixed,
        tokens_grad,
        norm_grads[0],
        norm_grads[1],
        norm_grads[2],
        norm_grads[3],
        qkv_grad,
        smalls[4:7].reshape(3 * head),
        out_grad,
        dy_total,
        up_grad,
        smalls[7:11].reshape(ff),
        down_grad,
        dy_total,
    )


def solution(mesh):
    rows = P(BOTH, None)
    vector, matrix = P("shard"), P("shard", None)
    return jax.shard_map(
        local,
        mesh=mesh,
        in_specs=(rows, rows, rows, vector, vector, vector, vector)
        + (matrix, vector, matrix, vector, matrix, vector, matrix, vector),
        out_specs=(rows, rows, vector, vector, vector, vector)
        + (matrix, vector, matrix, vector, matrix, vector, matrix, vector),
        check_vma=False,
    )
```

```python
import functools
import math

import jax
import jax.numpy as jnp
from jax import lax
from jax.experimental import pallas as pl
from jax.experimental.pallas import tpu as pltpu
from jax.sharding import PartitionSpec as P

HEADS = 8
ROT = 64
EPS = 1e-05
f32 = jnp.float32
bf16 = jnp.bfloat16


def cost(time):
    return pl.CostEstimate(flops=int(time * 1.15e9), bytes_accessed=1000, transcendentals=0)


BOTH = ("rep", "shard")
SIZES = (4, 2, 2, 2, 4)
SAME_CORE = [[2 * n + c for n in range(8)] for c in range(2)]
SAME_CORE_ALL = [[(2 * n + c) * 8 + s for n in range(8) for s in range(8)] for c in range(2)]


def coords():
    for y in range(4):
        for h in range(2):
            for c in range(2):
                for l in range(2):
                    for x in range(4):
                        yield (y, h, c, l, x)


def linear(t):
    y, h, c, l, x = (v % m for v, m in zip(t, SIZES))
    return ((y * 2 + h) * 2 + c) * 8 + l * 4 + x


def move(value, y=0, h=0, c=0, l=0, x=0):
    step = (y, h, c, l, x)
    pairs = [(linear(t), linear(tuple(a + b for a, b in zip(t, step)))) for t in coords()]
    return lax.ppermute(value, BOTH, pairs)


def pick(value, index, axis):
    return lax.dynamic_index_in_dim(value, index, axis, keepdims=False)


def kernel_params():
    return pltpu.CompilerParams(vmem_limit_bytes=56 * 1024 * 1024)


def after_inputs(body, count, extra):
    return lambda *refs: body(*refs[:count], *refs[count + extra :])


def anywhere(count):
    return [pl.BlockSpec(memory_space=pl.ANY)] * count


def dot(a, b, ca=1, cb=0):
    return lax.dot_general(a, b, (((ca,), (cb,)), ((), ())), preferred_element_type=f32)


def swap_halves(value):
    lane = lax.broadcasted_iota(jnp.int32, value.shape, 1)
    return jnp.where(lane < 32, pltpu.roll(value, 96, 1), pltpu.roll(value, 32, 1))


def allowed_mask(lengths_ref, block, rows):
    e0 = lengths_ref[block, 0]
    e1 = e0 + lengths_ref[block, 1]
    t = lax.broadcasted_iota(jnp.int32, (rows, rows), 0)
    s = lax.broadcasted_iota(jnp.int32, (rows, rows), 1)
    seg_t = (t >= e0).astype(jnp.int32) + (t >= e1).astype(jnp.int32)
    seg_s = (s >= e0).astype(jnp.int32) + (s >= e1).astype(jnp.int32)
    return (seg_t == seg_s) & (s <= t)


def dot_rows(a, b):
    return lax.dot_general(a, b, (((0,), (0,)), ((), ())), preferred_element_type=f32)


def loads(copies):
    for copy in copies:
        copy.start()
    return copies


def piece_copies(pieces, half, target, sems, rows, lanes=slice(None)):
    return [
        pltpu.make_async_copy(
            piece.at[half, :, lanes] if len(piece.shape) == 3 else piece.at[:, lanes],
            target.at[pl.ds(at * rows, rows)],
            sems.at[at],
        )
        for at, piece in enumerate(pieces)
    ]


def weight_copies(pieces, refs, spot_ref, target, lanes, sems, source=None):
    if source is not None:
        pieces = [
            (
                array,
                begin + max(source - first, 0),
                min(size, 4),
                max(first, source) - source,
                spot,
                ref,
            )
            for (array, begin, size, first, spot), ref in zip(pieces, refs)
            if first <= source < first + size
        ]
    else:
        pieces = [(*piece, ref) for piece, ref in zip(pieces, refs)]
    return [
        pltpu.make_async_copy(
            ref.at[pl.ds(begin, size), :, lanes],
            target.at[pl.ds(first, size), spot_ref[spot]],
            sems.at[at],
        )
        for at, (_, begin, size, first, spot, ref) in enumerate(pieces)
    ]


def feed_forward(x, dy, gains, weight, spots, down, bias, numbers, first, after):
    rows, width = x[0].shape[1:]
    count = len(x)
    total = rows * count
    ff = bias.shape[1]

    parts = len(weight)

    def body(number_ref, spot_ref, g_ref, b_ref, *refs):
        w_refs, refs = refs[:parts], refs[parts:]
        x_refs, dy_refs, d_hbm = refs[:count], refs[count : 2 * count], refs[2 * count]
        (h1_hbm, act_hbm, du_hbm, keep_hbm, send_hbm, m_ref, i_ref, db_ref, sum_ref) = refs[
            2 * count + 1 : 2 * count + 10
        ]
        (x_v, dy_v, h1_v, h2_v, w_v, d_v, act_v, du_v, keep_v, send_v, x_sem, dy_sem, w_sem, sems) = refs[
            2 * count + 10 :
        ]
        own = number_ref[0] == 0
        x_copies = loads(piece_copies(x_refs, 0, x_v, x_sem, rows))
        w_copies = loads(
            weight_copies(weight, w_refs, spot_ref, w_v, pl.ds(first, ff), w_sem)
        )
        dy_copies = loads(piece_copies(dy_refs, 1, dy_v, dy_sem, rows))
        d_copy = pltpu.make_async_copy(d_hbm, d_v, sems.at[1])
        d_copy.start()
        for copy in x_copies:
            copy.wait()

        @pl.loop(0, count)
        def _(n):
            at = pl.ds(pl.multiple_of(n * rows, rows), rows)
            value = x_v[at, :].astype(f32)
            mean = jnp.mean(value, 1, keepdims=True)
            centre = value - mean
            inverse = lax.rsqrt(jnp.mean(centre * centre, 1, keepdims=True) + EPS)
            normed = centre * inverse
            m_ref[at, :] = mean
            i_ref[at, :] = inverse
            h1_v[at, :] = (normed * g_ref[0:1] + g_ref[1:2]).astype(bf16)
            h2_v[at, :] = (normed * g_ref[2:3] + g_ref[3:4]).astype(bf16)

        h1_copy = pltpu.make_async_copy(h1_v, h1_hbm, sems.at[2])
        h1_copy.start()
        for copy in w_copies + dy_copies:
            copy.wait()
        d_copy.wait()
        mine = dy_v[:, pl.ds(pl.multiple_of(number_ref[1] * 256, 256), 256)]
        sum_ref[...] = jnp.sum(mine.astype(f32), 0, keepdims=True)

        def split(part, places, high, wide):
            at = (places, high, wide)

            @pl.when(own)
            def _():
                keep_v[at] = part[:, 0]
                send_v[at] = part[:, 1]

            @pl.when(jnp.logical_not(own))
            def _():
                keep_v[at] = part[:, 1]
                send_v[at] = part[:, 0]

        def leaving(n):
            at = (pl.ds(n * 2, 2), pl.ds(0, 64))
            return (
                pltpu.make_async_copy(keep_v.at[at], keep_hbm.at[at], sems.at[3]),
                pltpu.make_async_copy(send_v.at[at], send_hbm.at[at], sems.at[4]),
            )

        @pl.loop(0, ff // 256)
        def _(n):
            at = pl.ds(pl.multiple_of(n * 256, 256), 256)
            u = dot(h2_v[...], w_v[:, :, :, at].reshape(width, 256)) + b_ref[:, at]
            cdf = 0.5 * (1.0 + lax.erf(u * math.sqrt(0.5)))
            pdf = jnp.exp(-0.5 * u * u) * (1.0 / math.sqrt(2.0 * math.pi))
            act = (u * cdf).astype(bf16)
            act_v[:, at] = act
            du = (dot(dy_v[...], d_v[at, :], 1, 1) * (cdf + u * pdf)).astype(bf16)
            du_v[:, at] = du
            db_ref[:, at] = jnp.sum(du.astype(f32), 0, keepdims=True)
            part = dot_rows(act, dy_v[...]).astype(bf16).reshape(2, 2, 64, width)
            split(part, pl.ds(n * 2, 2), pl.ds(0, 64), slice(None))
            for copy in leaving(n):
                copy.start()

        act_copy = pltpu.make_async_copy(act_v, act_hbm, sems.at[0])
        act_copy.start()
        du_copy = pltpu.make_async_copy(du_v, du_hbm, sems.at[1])
        du_copy.start()
        for n in range(ff // 256):
            for copy in leaving(n):
                copy.wait()

        def block(n):
            at = (
                slice(None),
                pl.ds(pl.multiple_of(64 + 16 * (n % 4), 16), 16),
                pl.ds(pl.multiple_of(n // 4 * ff, ff), ff),
            )
            return at

        def away(n):
            at = block(n)
            return (
                pltpu.make_async_copy(keep_v.at[at], keep_hbm.at[at], sems.at[3]),
                pltpu.make_async_copy(send_v.at[at], send_hbm.at[at], sems.at[4]),
            )

        @pl.loop(0, 8)
        def _(n):
            lanes = pl.ds(pl.multiple_of(n * 256, 256), 256)
            part = dot_rows(h2_v[:, lanes], du_v[...]).astype(bf16).reshape(8, 2, 16, ff)
            split(part, *block(n))
            for copy in away(n):
                copy.start()

        for n in range(8):
            for copy in away(n):
                copy.wait()
        h1_copy.wait()
        act_copy.wait()
        du_copy.wait()

    wide = jax.ShapeDtypeStruct((total, width), bf16)
    thin = jax.ShapeDtypeStruct((total, ff), bf16)
    column = jax.ShapeDtypeStruct((total, 1), f32)
    grads = jax.ShapeDtypeStruct((8, 128, width), bf16)
    vmem = pl.BlockSpec(memory_space=pltpu.VMEM)
    return pl.pallas_call(
        after_inputs(body, 5 + parts + 2 * count, len(after)),
        out_shape=(
            wide,
            thin,
            thin,
            grads,
            grads,
            column,
            column,
            jax.ShapeDtypeStruct((1, ff), f32),
            jax.ShapeDtypeStruct((1, 256), f32),
        ),
        in_specs=[pl.BlockSpec(memory_space=pltpu.SMEM)] * 2
        + [vmem, vmem]
        + anywhere(parts + 2 * count + 1 + len(after)),
        out_specs=tuple(anywhere(5)) + (vmem,) * 4,
        scratch_shapes=[
            pltpu.VMEM((total, width), bf16),
            pltpu.VMEM((total, width), bf16),
            pltpu.VMEM((total, width), bf16),
            pltpu.VMEM((total, width), bf16),
            pltpu.VMEM((8, 8, width // 64, ff), bf16),
            pltpu.VMEM((ff, width), bf16),
            pltpu.VMEM((total, ff), bf16),
            pltpu.VMEM((total, ff), bf16),
            pltpu.VMEM((8, 128, width), bf16),
            pltpu.VMEM((8, 128, width), bf16),
            pltpu.SemaphoreType.DMA((count,)),
            pltpu.SemaphoreType.DMA((count,)),
            pltpu.SemaphoreType.DMA((parts,)),
            pltpu.SemaphoreType.DMA((5,)),
        ],
        compiler_params=kernel_params(),
        cost_estimate=cost(32),
        name="feed_forward",
    )(numbers, spots, gains, bias, *[p[0] for p in weight], *x, *dy, down, *after)


def packed(qkv_weight, up_weight, vectors, lengths, place, head, tokens, cotangent):
    wide, up_wide = qkv_weight.shape[1], up_weight.shape[1]
    part, up_part = 3 * head, up_wide // 8
    cols = part + up_part

    def body(place_ref, len_ref, q_ref, u_ref, x_ref, dy_ref, *refs):
        v_refs, out_ref, pair_ref = refs[: len(vectors)], refs[-2], refs[-1]
        pair_ref[0] = x_ref[...]
        pair_ref[1] = dy_ref[...]
        lane = lax.broadcasted_iota(jnp.int32, (8, cols), 1)
        row = lax.broadcasted_iota(jnp.int32, (8, cols), 0)
        sizes = jnp.zeros((8, cols), f32)
        for at in range(3):
            sizes = jnp.where(lane == at, len_ref[0, at].astype(f32), sizes)
        vector = jnp.concatenate([ref[...].astype(f32) for ref in v_refs])[None, :]
        vector = jnp.broadcast_to(vector, (8, cols))
        tail = jnp.where(row == 0, vector, jnp.where(row == 1, sizes, 0.0)).astype(bf16)
        for owner in range(8):
            pieces = [
                q_ref[:, (third * 8 + owner) * head : (third * 8 + owner + 1) * head]
                for third in range(3)
            ]
            pieces.append(u_ref[:, owner * up_part : (owner + 1) * up_part])
            out_ref[owner] = jnp.concatenate([jnp.concatenate(pieces, 1), tail], 0)

    return pl.pallas_call(
        body,
        out_shape=(
            jax.ShapeDtypeStruct((8, 40, cols), bf16),
            jax.ShapeDtypeStruct((2,) + tokens.shape, bf16),
        ),
        grid_spec=pltpu.PrefetchScalarGridSpec(
            num_scalar_prefetch=2,
            grid=(1,),
            in_specs=[
                pl.BlockSpec((32, wide), lambda i, place, lens: (place[0], 0)),
                pl.BlockSpec((32, up_wide), lambda i, place, lens: (place[0], 0)),
                pl.BlockSpec(tokens.shape, lambda i, place, lens: (0, 0)),
                pl.BlockSpec(tokens.shape, lambda i, place, lens: (0, 0)),
            ]
            + [pl.BlockSpec(v.shape, lambda i, place, lens: (0,)) for v in vectors],
            out_specs=(
                pl.BlockSpec((8, 40, cols), lambda i, place, lens: (0, 0, 0)),
                pl.BlockSpec((2,) + tokens.shape, lambda i, place, lens: (0, 0, 0)),
            ),
        ),
        compiler_params=kernel_params(),
        cost_estimate=cost(3),
        name="packed",
    )(place, lengths, qkv_weight, up_weight, tokens, cotangent, *vectors)


def attend(h1, dy, weight, spots, out, bias, cosine, sine, lengths, after, rows=128):
    total, width = h1.shape
    count = len(dy)
    head = out.shape[0]
    scale = head ** (-0.5)

    parts = len(weight)

    def body(len_ref, spot_ref, b_ref, *refs):
        w_refs, refs = refs[:parts], refs[parts:]
        dy_refs = refs[:count]
        h1_hbm, out_hbm, cos_hbm, sin_hbm = refs[count : count + 4]
        ol_hbm, dq_hbm, sum_ref = refs[count + 4 : count + 7]
        (dy_v, h1_v, w_v, wo_v, cos_v, sin_v, qkv_v, do_v, ol_v, dq_v, dy_sem, w_sem, sems) = (
            refs[count + 7 :]
        )
        pairs = (
            (h1_hbm, h1_v),
            (out_hbm, wo_v),
            (cos_hbm, cos_v),
            (sin_hbm, sin_v),
        )
        copies = loads(
            [pltpu.make_async_copy(*pair, sems.at[n]) for n, pair in enumerate(pairs)]
        )
        w_copies = loads(
            weight_copies(weight, w_refs, spot_ref, w_v, pl.ds(0, 3 * head), w_sem)
        )
        dy_copies = loads(piece_copies(dy_refs, 1, dy_v, dy_sem, rows))
        for copy in copies[:1] + w_copies:
            copy.wait()

        @pl.loop(0, 3)
        def _(n):
            at = pl.ds(pl.multiple_of(n * head, head), head)
            qkv_v[:, at] = dot(h1_v[...], w_v[:, :, :, at].reshape(width, head)) + b_ref[n]

        for copy in copies[1:] + dy_copies:
            copy.wait()
        do_v[...] = dot(dy_v[...], wo_v[...], 1, 1).astype(bf16)
        sum_ref[...] = jnp.zeros_like(sum_ref)

        @pl.loop(0, total // rows, unroll=2)
        def _(block):
            at = pl.ds(pl.multiple_of(block * rows, rows), rows)
            cos, sin = cos_v[at, :], sin_v[at, :]

            def turned(value, sign):
                left = value[:, :128]
                left = left * cos + swap_halves(left) * (sin * sign)
                return jnp.concatenate([left, value[:, 128:]], 1).astype(bf16)

            q, k = turned(qkv_v[at, 0:head], 1.0), turned(qkv_v[at, head : 2 * head], 1.0)
            v = qkv_v[at, 2 * head :].astype(bf16)
            scores = dot(q, k, 1, 1) * scale
            masked = jnp.where(allowed_mask(len_ref, block, rows), scores, -1e30)
            shifted = jnp.exp(masked - jnp.max(masked, 1, keepdims=True))
            probs = shifted / jnp.sum(shifted, 1, keepdims=True)
            low = probs.astype(bf16)
            ol_v[at, :] = dot(low, v).astype(bf16)
            d_out = do_v[at, :]
            d_value = dot(low, d_out, 0, 0)
            d_probs = dot(d_out, v, 1, 1)
            centred = d_probs - jnp.sum(d_probs * probs, 1, keepdims=True)
            d_scores = (probs * centred).astype(bf16)
            d_query = turned(dot(d_scores, k) * scale, -1.0)
            d_key = turned(dot(d_scores, q, 0, 0) * scale, -1.0)
            for n, grad in enumerate((d_query, d_key, d_value.astype(bf16))):
                lanes = slice(n * head, (n + 1) * head)
                dq_v[at, lanes] = grad
                sum_ref[:, lanes] += jnp.sum(grad.astype(f32), 0, keepdims=True)

        ol_copy = pltpu.make_async_copy(ol_v, ol_hbm, sems.at[0])
        ol_copy.start()
        dq_copy = pltpu.make_async_copy(dq_v, dq_hbm, sems.at[1])
        dq_copy.start()

        for copy in (ol_copy, dq_copy):
            copy.wait()

    vmem = pl.BlockSpec(memory_space=pltpu.VMEM)
    smem = pl.BlockSpec(memory_space=pltpu.SMEM)
    return pl.pallas_call(
        after_inputs(body, 7 + parts + count, len(after)),
        out_shape=(
            jax.ShapeDtypeStruct((total, head), bf16),
            jax.ShapeDtypeStruct((total, 3 * head), bf16),
            jax.ShapeDtypeStruct((1, 3 * head), f32),
        ),
        in_specs=[smem, smem, vmem] + anywhere(parts + count + 4 + len(after)),
        out_specs=tuple(anywhere(2)) + (vmem,),
        scratch_shapes=[
            pltpu.VMEM((total, width), bf16),
            pltpu.VMEM((total, width), bf16),
            pltpu.VMEM((8, 8, width // 64, 3 * head), bf16),
            pltpu.VMEM((head, width), bf16),
            pltpu.VMEM((total, 128), f32),
            pltpu.VMEM((total, 128), f32),
            pltpu.VMEM((total, 3 * head), f32),
            pltpu.VMEM((total, head), bf16),
            pltpu.VMEM((total, head), bf16),
            pltpu.VMEM((total, 3 * head), bf16),
            pltpu.SemaphoreType.DMA((count,)),
            pltpu.SemaphoreType.DMA((parts,)),
            pltpu.SemaphoreType.DMA((4,)),
        ],
        compiler_params=kernel_params(),
        cost_estimate=cost(17),
        name="attend",
    )(
        lengths,
        spots,
        bias,
        *[p[0] for p in weight],
        *dy,
        h1,
        out,
        cosine,
        sine,
        *after,
    )


def attention_grads(h1, dy, d_qkv, attended, numbers, after):
    total, width = h1.shape
    count = len(dy)
    rows = total // count
    head = attended.shape[1]

    def body(number_ref, *refs):
        dy_refs = refs[:count]
        h1_hbm, dq_hbm, ol_hbm, keep_hbm, send_hbm = refs[count : count + 5]
        dy_v, h1_v, dq_v, ol_v, keep_v, send_v, dy_sem, sems = refs[count + 5 :]
        own = number_ref[0] == 0
        pairs = ((h1_hbm, h1_v), (dq_hbm, dq_v), (ol_hbm, ol_v))
        copies = loads(
            [pltpu.make_async_copy(*pair, sems.at[n]) for n, pair in enumerate(pairs)]
        )
        dy_copies = loads(piece_copies(dy_refs, 1, dy_v, dy_sem, rows))
        for copy in copies:
            copy.wait()

        def split(part, high, lanes):
            at = (slice(None), high, lanes)

            @pl.when(own)
            def _():
                keep_v[at] = part[:, 0]
                send_v[at] = part[:, 1]

            @pl.when(jnp.logical_not(own))
            def _():
                keep_v[at] = part[:, 1]
                send_v[at] = part[:, 0]

        @pl.loop(0, 8)
        def _(n):
            lanes = pl.ds(pl.multiple_of(n * 256, 256), 256)
            part = dot_rows(h1_v[:, lanes], dq_v[...]).astype(bf16).reshape(8, 2, 16, 3 * head)
            for third in range(3):
                split(
                    part[..., third * head : (third + 1) * head],
                    pl.ds(16 * third, 16),
                    pl.ds(pl.multiple_of(n * head, head), head),
                )

        for copy in dy_copies:
            copy.wait()
        part = dot_rows(ol_v[...], dy_v[...]).astype(bf16).reshape(8, 2, 16, width)
        split(part, pl.ds(48, 16), slice(None))
        keep_copy = pltpu.make_async_copy(keep_v, keep_hbm, sems.at[0])
        keep_copy.start()
        send_copy = pltpu.make_async_copy(send_v, send_hbm, sems.at[1])
        send_copy.start()
        keep_copy.wait()
        send_copy.wait()

    grads = jax.ShapeDtypeStruct((8, 64, width), bf16)
    return pl.pallas_call(
        after_inputs(body, 4 + count, len(after)),
        out_shape=(grads, grads),
        in_specs=[pl.BlockSpec(memory_space=pltpu.SMEM)] + anywhere(count + 3 + len(after)),
        out_specs=tuple(anywhere(2)),
        scratch_shapes=[
            pltpu.VMEM((total, width), bf16),
            pltpu.VMEM((total, width), bf16),
            pltpu.VMEM((total, 3 * head), bf16),
            pltpu.VMEM((total, head), bf16),
            pltpu.VMEM((8, 64, width), bf16),
            pltpu.VMEM((8, 64, width), bf16),
            pltpu.SemaphoreType.DMA((count,)),
            pltpu.SemaphoreType.DMA((3,)),
        ],
        compiler_params=kernel_params(),
        cost_estimate=cost(12),
        name="attention_grads",
    )(numbers, *dy, h1, d_qkv, attended, *after)


def outer(d_qkv, d_hidden, weight, spots, x, mean, inverse, gains, active, attended, down, out, bias, after):
    total, n1 = d_qkv.shape
    n2 = d_hidden.shape[1]
    count = len(x)
    parts = len(weight)
    head, width = out.shape
    step = 512

    def body(spot_ref, m_ref, i_ref, g_ref, b_ref, *refs):
        w_refs, refs = refs[:parts], refs[parts:]
        x_refs, refs = refs[:count], refs[count:]
        plain, sums_ref, outs = refs[:6], refs[6], refs[7 : 7 + count]
        dq_v, du_v, act_v, ol_v, wd_v, wo_v, w_v, x_v, pair_v, w_sem, x_sem, sems, out_sem = refs[
            7 + count :
        ]
        plain_v = (dq_v, du_v, act_v, ol_v, wd_v, wo_v)
        first = loads(
            [
                pltpu.make_async_copy(plain[n], plain_v[n], sems.at[n]) for n in range(2, 6)
            ]
        )
        copies = loads(
            [
                pltpu.make_async_copy(plain[n], plain_v[n], sems.at[n]) for n in range(2)
            ]
            + weight_copies(weight, w_refs, spot_ref, w_v, slice(None), w_sem)
            + piece_copies(x_refs, 0, x_v, x_sem, 128)
        )
        for copy in first:
            copy.wait()

        def leaving(n, half):
            lanes = pl.ds(pl.multiple_of(n * step, step), step)
            return [
                pltpu.make_async_copy(
                    pair_v.at[half, pl.ds(at * 128, 128), lanes],
                    outs[at].at[half, :, lanes],
                    out_sem.at[half, at],
                )
                for at in range(count)
            ]

        @pl.loop(0, width // step)
        def _(n):
            lanes = pl.ds(pl.multiple_of(n * step, step), step)
            mix = dot(act_v[...], wd_v[:, lanes]) + dot(ol_v[...], wo_v[:, lanes])
            pair_v[0, :, lanes] = (mix + b_ref[:, lanes]).astype(bf16)
            for copy in leaving(n, 0):
                copy.start()

        for copy in copies:
            copy.wait()

        @pl.loop(0, width // step)
        def _(n):
            lanes = pl.ds(pl.multiple_of(n * step, step), step)
            sources = pl.ds(n * (step // 256), step // 256)
            d1 = dot(dq_v[...], w_v[sources, :, :, 0:n1].reshape(step, n1), 1, 1)
            d2 = dot(du_v[...], w_v[sources, :, :, n1:].reshape(step, n2), 1, 1)
            pair_v[1, :, lanes] = (d1 * g_ref[0:1, lanes] + d2 * g_ref[1:2, lanes]).astype(bf16)
            for copy in leaving(n, 1):
                copy.start()
            normed = (x_v[:, lanes].astype(f32) - m_ref[...]) * i_ref[...]
            sums_ref[0:1, lanes] = jnp.sum(d1 * normed, 0, keepdims=True)
            sums_ref[1:2, lanes] = jnp.sum(d1, 0, keepdims=True)
            sums_ref[2:3, lanes] = jnp.sum(d2 * normed, 0, keepdims=True)
            sums_ref[3:4, lanes] = jnp.sum(d2, 0, keepdims=True)

        for n in range(width // step):
            for half in range(2):
                for copy in leaving(n, half):
                    copy.wait()

    vmem = pl.BlockSpec(memory_space=pltpu.VMEM)
    return pl.pallas_call(
        after_inputs(body, 11 + parts + count, len(after)),
        out_shape=(jax.ShapeDtypeStruct((4, width), f32),)
        + (jax.ShapeDtypeStruct((2, 128, width), bf16),) * count,
        in_specs=[pl.BlockSpec(memory_space=pltpu.SMEM)]
        + [vmem] * 4
        + anywhere(parts + count + 6 + len(after)),
        out_specs=(vmem,) + tuple(anywhere(count)),
        scratch_shapes=[
            pltpu.VMEM((total, n1), bf16),
            pltpu.VMEM((total, n2), bf16),
            pltpu.VMEM((total, n2), bf16),
            pltpu.VMEM((total, head), bf16),
            pltpu.VMEM((n2, width), bf16),
            pltpu.VMEM((head, width), bf16),
            pltpu.VMEM((8, 8, width // 64, n1 + n2), bf16),
            pltpu.VMEM((total, width), bf16),
            pltpu.VMEM((2, total, width), bf16),
            pltpu.SemaphoreType.DMA((parts,)),
            pltpu.SemaphoreType.DMA((count,)),
            pltpu.SemaphoreType.DMA((6,)),
            pltpu.SemaphoreType.DMA((2, count)),
        ],
        compiler_params=kernel_params(),
        cost_estimate=cost(20),
        name="outer",
    )(
        spots,
        mean,
        inverse,
        gains,
        bias,
        *[p[0] for p in weight],
        *x,
        d_qkv,
        d_hidden,
        active,
        attended,
        down,
        out,
        *after,
    )


def unpacked(part, after):
    owners, _, cols = part.shape

    def body(part_ref, rows_ref, info_ref):
        for owner in range(owners):
            rows_ref[owner] = part_ref[owner, 0:32]
            info_ref[owner] = part_ref[owner, 32:40].astype(f32)

    return pl.pallas_call(
        after_inputs(body, 1, len(after)),
        out_shape=(
            jax.ShapeDtypeStruct((owners, 32, cols), bf16),
            jax.ShapeDtypeStruct((owners, 8, cols), f32),
        ),
        in_specs=[pl.BlockSpec(memory_space=pltpu.VMEM)] + anywhere(len(after)),
        out_specs=(pl.BlockSpec(memory_space=pltpu.VMEM),) * 2,
        compiler_params=kernel_params(),
        cost_estimate=cost(3),
        name="unpacked",
    )(part, *after)


def joined(arrays, after):
    sizes = [array.shape[0] for array in arrays]
    unit = math.gcd(*sizes)
    block = (unit,) + arrays[0].shape[1:]
    count = len(arrays)
    firsts = [sum(sizes[:n]) // unit for n in range(count)]

    def body(*refs):
        step = pl.program_id(0)
        for ref, first, size in zip(refs, firsts, sizes):

            @pl.when((step >= first) & (step < first + size // unit))
            def _(ref=ref):
                refs[count][...] = ref[...]

    def came(first, size):
        return pl.BlockSpec(block, lambda i: (jnp.clip(i - first, 0, size // unit - 1), 0, 0))

    return pl.pallas_call(
        after_inputs(body, count, len(after)),
        out_shape=jax.ShapeDtypeStruct((sum(sizes),) + block[1:], bf16),
        grid=(sum(sizes) // unit,),
        in_specs=[came(first, size) for first, size in zip(firsts, sizes)] + anywhere(len(after)),
        out_specs=pl.BlockSpec(block, lambda i: (i, 0, 0)),
        compiler_params=kernel_params(),
        cost_estimate=cost(3),
        name="joined",
    )(*arrays, *after)


def halves(own, below, above, after):
    count, rows, cols = own.shape
    half = count // 2

    def body(own_ref, below_ref, above_ref, low_ref, high_ref, all_ref):
        step = pl.program_id(0)
        all_ref[0] = own_ref[...]
        all_ref[1] = above_ref[...]
        all_ref[2] = below_ref[...]

        @pl.when(step == 0)
        def _():
            low_ref[...] = below_ref[...]

        @pl.when(step == 1)
        def _():
            high_ref[...] = above_ref[...]

    block = pl.BlockSpec((half, rows, cols), lambda i: (i, 0, 0))
    whole = pl.BlockSpec((half, rows, cols), lambda i: (0, 0, 0))
    low, high, together = pl.pallas_call(
        after_inputs(body, 3, len(after)),
        out_shape=(jax.ShapeDtypeStruct((half, rows, cols), bf16),) * 2
        + (jax.ShapeDtypeStruct((3, count, rows, cols), bf16),),
        grid=(2,),
        in_specs=[block] * 3 + anywhere(len(after)),
        out_specs=(
            whole,
            whole,
            pl.BlockSpec((3, half, rows, cols), lambda i: (0, i, 0, 0)),
        ),
        compiler_params=kernel_params(),
        cost_estimate=cost(4),
        name="halves",
    )(own, below, above, *after)
    return low, high, together.reshape(3 * count, rows, cols)


def unpacked_sums(received, cols, after):
    sources, rows, width = received.shape

    def body(part_ref, out_ref):
        small = jnp.sum(part_ref[:, :, cols:].astype(f32), 0).astype(bf16)
        out_ref[0] = jnp.concatenate(
            [jnp.concatenate([part_ref[0, :, 0:cols], small], 1)]
            + [part_ref[n] for n in range(1, sources)],
            0,
        )

    vmem = pl.BlockSpec(memory_space=pltpu.VMEM)
    return pl.pallas_call(
        after_inputs(body, 1, len(after)),
        out_shape=jax.ShapeDtypeStruct((1, sources * rows, width), bf16),
        in_specs=[vmem] + anywhere(len(after)),
        out_specs=vmem,
        compiler_params=kernel_params(),
        cost_estimate=cost(3),
        name="unpacked_sums",
    )(received, *after)


def packed_sums(stays, crossed, parts, norm_sums, qkv_sums, up_sums, dy_sums, numbers, ff, head, after):
    width = parts.shape[2]

    def body(*refs):
        stay_ref, cross_ref, parts_ref = refs[:3]
        norm_ref, q_ref, u_ref, y_ref, number_ref, out_ref, keep_ref, small = refs[3:]
        shard = number_ref[1]
        inner = (stay_ref[0].astype(f32) + cross_ref[0].astype(f32)).astype(bf16)
        total = jnp.sum(parts_ref[...].astype(f32), 0).astype(bf16)
        for owner in range(8):
            mine = shard == owner
            small[...] = jnp.zeros_like(small)
            small[0:4] = norm_ref[:, owner * head : (owner + 1) * head]
            for n in range(3):
                third, source = divmod(owner * 3 + n, 8)
                lanes = slice(third * head, (third + 1) * head)
                small[4 + n : 5 + n] = jnp.where(shard == source, q_ref[:, lanes], 0.0)
            for n in range(4):
                lanes = slice(n * head, (n + 1) * head)
                small[7 + n : 8 + n] = jnp.where(mine, u_ref[:, lanes], 0.0)
            small[11:12] = jnp.where(mine, y_ref[...], 0.0)
            pieces = [
                total[16 * third : 16 * third + 16, owner * head : (owner + 1) * head]
                for third in range(3)
            ]
            row, col = 64 + 16 * (owner % 4), owner // 4 * ff
            pieces.append(inner[row : row + 16, col : col + ff])
            pieces.append(small[...].astype(bf16))
            out_ref[owner] = jnp.concatenate(pieces, 1)
        keep_ref[0:64] = inner[0:64]
        keep_ref[64:80] = total[48:64]

    vmem = pl.BlockSpec(memory_space=pltpu.VMEM)
    return pl.pallas_call(
        after_inputs(body, 8, len(after)),
        out_shape=(
            jax.ShapeDtypeStruct((8, 16, 4 * head + ff), bf16),
            jax.ShapeDtypeStruct((80, width), bf16),
        ),
        in_specs=[vmem] * 7 + [pl.BlockSpec(memory_space=pltpu.SMEM)] + anywhere(len(after)),
        out_specs=(vmem,) * 2,
        scratch_shapes=[pltpu.VMEM((16, head), f32)],
        compiler_params=kernel_params(),
        cost_estimate=cost(3),
        name="packed_sums",
    )(stays, crossed, parts, norm_sums, qkv_sums, up_sums, dy_sums, numbers, *after)


def finished(own, below, above, other, tokens, cotangent, after):
    rows, width = tokens.shape
    step = rows // 2

    def body(own_ref, below_ref, above_ref, other_ref, x_ref, dy_ref, mixed_ref, grad_ref):
        total = wide(own_ref, below_ref, above_ref, other_ref)
        x = x_ref[...].astype(f32)
        mixed_ref[...] = (x + total[0]).astype(bf16)
        centre = x - jnp.mean(x, 1, keepdims=True)
        inverse = lax.rsqrt(jnp.mean(centre * centre, 1, keepdims=True) + EPS)
        normed = centre * inverse
        gain = total[1]
        grad_ref[...] = dy_ref[...].astype(f32) + inverse * (
            gain
            - jnp.mean(gain, 1, keepdims=True)
            - normed * jnp.mean(gain * normed, 1, keepdims=True)
        )

    def pair(first):
        return pl.BlockSpec((2, step, width), lambda i: (first, i, 0))

    block = pl.BlockSpec((step, width), lambda i: (i, 0))
    return pl.pallas_call(
        after_inputs(body, 6, len(after)),
        out_shape=(
            jax.ShapeDtypeStruct((rows, width), bf16),
            jax.ShapeDtypeStruct((rows, width), f32),
        ),
        grid=(2,),
        in_specs=[pair(0), pair(1), pair(0), pair(0), block, block] + anywhere(len(after)),
        out_specs=(block, block),
        compiler_params=kernel_params(),
        cost_estimate=cost(14),
        name="finished",
    )(own, below, above, other, tokens, cotangent, *after)


def blocks_call(name, body, numbers, terms, outs, after, time=3):
    def came(block, index):
        rest = (0,) * (len(block) - 1)
        return pl.BlockSpec(block, lambda i, n: (index(n),) + rest)

    return pl.pallas_call(
        after_inputs(body, 1 + len(terms), len(after)),
        out_shape=tuple(jax.ShapeDtypeStruct(out, bf16) for out in outs),
        grid_spec=pltpu.PrefetchScalarGridSpec(
            num_scalar_prefetch=1,
            grid=(1,),
            in_specs=[came(block, index) for _, block, index in terms] + anywhere(len(after)),
            out_specs=tuple(
                pl.BlockSpec(out, lambda i, n, size=len(out): (0,) * size) for out in outs
            ),
        ),
        compiler_params=kernel_params(),
        cost_estimate=cost(time),
        name=name,
    )(numbers, *[array for array, _, _ in terms], *after)


def wide(*refs):
    return functools.reduce(jnp.add, [ref[...].astype(f32) for ref in refs])


def spread(pieces, places, core, targets, count, before, after, time=2):
    rows, cols = pieces[0][0].shape[1:]
    firsts, total = [], 0
    for mine, _ in pieces:
        firsts.append(total)
        total += mine.shape[0]

    def body(place_ref, core_ref, *refs):
        step = pl.program_id(0)
        outs = refs[2 * len(pieces) + len(before) :]
        first_core = core_ref[0] == 0

        def fill(ref, low):
            for out_ref, (_, high, parts) in zip(outs, targets):
                for to, row, col, size in parts:
                    out_ref[low * high : (low + 1) * high, to : to + size] = ref[
                        0, row : row + high, col : col + size
                    ].astype(f32)

        for n, (first, (mine, _)) in enumerate(zip(firsts, pieces)):
            here = (step >= first) & (step < first + mine.shape[0])

            @pl.when(here & first_core)
            def _(n=n):
                fill(refs[2 * n], 0)
                fill(refs[2 * n + 1], 1)

            @pl.when(here & jnp.logical_not(first_core))
            def _(n=n):
                fill(refs[2 * n], 1)
                fill(refs[2 * n + 1], 0)

    def chosen(first, size):
        return pl.BlockSpec(
            (1, rows, cols), lambda i, place, core: (jnp.clip(i - first, 0, size - 1), 0, 0)
        )

    specs, arrays = [], []
    for first, (mine, yours) in zip(firsts, pieces):
        specs += [chosen(first, mine.shape[0])] * 2
        arrays += [mine, yours]
    return pl.pallas_call(
        after_inputs(body, 2 + 2 * len(pieces) + len(before), len(after)),
        out_shape=tuple(
            jax.ShapeDtypeStruct((2 * count * high, wide), f32) for wide, high, _ in targets
        ),
        grid_spec=pltpu.PrefetchScalarGridSpec(
            num_scalar_prefetch=2,
            grid=(total,),
            in_specs=specs + anywhere(len(before) + len(after)),
            out_specs=tuple(
                pl.BlockSpec((2 * high, wide), lambda i, place, core: (place[i], 0))
                for wide, high, _ in targets
            ),
        ),
        input_output_aliases={2 + len(arrays) + n: n for n in range(len(before))},
        compiler_params=kernel_params(),
        cost_estimate=cost(time),
        name="spread",
    )(places, core, *arrays, *before, *after)


def local(
    tokens,
    doc_lengths,
    cotangent,
    ln1_gain,
    ln1_bias,
    ln2_gain,
    ln2_bias,
    qkv_weight,
    qkv_bias,
    out_weight,
    out_bias,
    up_weight,
    up_bias,
    down_weight,
    down_bias,
):
    rows, width = tokens.shape
    head = width // HEADS
    group = 8
    rep = lax.axis_index("rep")
    shard = lax.axis_index("shard")
    y, h, c = rep // 4, (rep // 2) % 2, rep % 2
    l, x = shard // 4, shard % 4
    ff = up_bias.shape[0]

    cols = 3 * head + ff
    vectors = [ln1_gain, ln1_bias, ln2_gain, ln2_bias, qkv_bias]
    place = (y * 2 + c).astype(jnp.int32).reshape(1)
    part, pair = packed(
        qkv_weight, up_weight, vectors, doc_lengths, place, head, tokens, cotangent
    )
    below, above, other = move(pair, x=1), move(pair, x=-1), move(pair, l=1)
    far, other_above, other_below = move(below, x=1), move(other, x=-1), move(below, l=1)
    pairs = (pair, above, far, below, other, other_above, None, other_below)

    part = lax.all_to_all(part, "shard", 0, 0)
    own, infos = unpacked(part, (pairs[1], pairs[3], pairs[4]))
    below, above = move(own, y=1), move(own, y=-1)
    x_other_far, dy_other_far = move(other_below[0], x=1), move(other_above[1], x=-1)
    low, high, yours = halves(own, below, above, (far, other_above, other_below))
    far_low, far_high = move(low, y=1), move(high, y=-1)
    x_all = tuple(x_other_far if p is None else p for p in pairs)
    dy_all = tuple(dy_other_far if p is None else p for p in pairs)
    yours = move(yours, c=1)
    far_low_c, far_high_c = move(far_low, c=1), move(far_high, c=1)
    weight = (
        (own, 0, 8, 0, 0),
        (above, 0, 8, 0, 1),
        (far_low, 0, 4, 0, 2),
        (far_high, 0, 4, 4, 2),
        (below, 0, 8, 0, 3),
        (yours, 0, 8, 0, 4),
        (yours, 8, 8, 0, 5),
        (far_low_c, 0, 4, 0, 6),
        (far_high_c, 0, 4, 4, 6),
        (yours, 16, 8, 0, 7),
    )
    steps4 = (y + jnp.arange(4)) % 4
    spots = jnp.concatenate([steps4 * 2 + c, steps4 * 2 + 1 - c]).astype(jnp.int32)

    gains = infos[:, 0, :1024].reshape(8, 4, 256).transpose(1, 0, 2).reshape(4, width)
    qkv_b = infos[:, 0, 1024:].reshape(8 * 3, 1, head)
    qkv_b = jnp.stack(
        [lax.dynamic_index_in_dim(qkv_b, third * 8 + shard, 0, False) for third in range(3)]
    )
    steps8 = jnp.arange(8)
    sources = ((steps8 // 4) ^ l) * 4 + (x + steps8 % 4) % 4
    sources = sources.astype(jnp.int32)
    lengths = infos[:, 1, :3]
    lengths = jnp.sum(
        jnp.where(sources[:, None, None] == steps8[None, :, None], lengths[None], 0.0), 1
    ).astype(jnp.int32)
    ends = jnp.cumsum(lengths, 1)
    starts = ends - lengths
    steps_t = jnp.arange(rows, dtype=jnp.int32)
    segment = jnp.sum((steps_t[None, :, None] >= ends[:, None, :]).astype(jnp.int32), -1)
    slots = jnp.arange(lengths.shape[1], dtype=jnp.int32)
    begin = jnp.sum(
        jnp.where(segment[:, :, None] == slots[None, None, :], starts[:, None, :], 0), -1
    )
    position = (steps_t[None, :] - begin).astype(f32).reshape(group * rows, 1)
    lane = jnp.arange(128)
    freq = 10000.0 ** (-2.0 * (lane % (ROT // 2)).astype(f32) / ROT)
    angle = position * freq[None, :]
    cosine = jnp.where(lane < ROT, jnp.cos(angle), 1.0)
    sine = jnp.sin(angle)
    sine = jnp.where(lane < ROT // 2, -sine, jnp.where(lane < ROT, sine, 0.0))

    both_bias = (out_bias.astype(f32) + down_bias.astype(f32))[None, :]
    wide_bias = lax.dynamic_update_slice(jnp.zeros((1, width), f32), both_bias, (0, shard * 256))
    numbers = jnp.stack([c, shard, y, h]).astype(jnp.int32)

    h1, active, d_hidden, keep, send, mean, inverse, up_sums, dy_sums = feed_forward(
        x_all,
        dy_all,
        gains,
        weight,
        spots,
        down_weight,
        up_bias.astype(f32)[None],
        numbers,
        3 * head,
        (cosine, sine),
    )
    got = move(send, c=1)
    attended, d_qkv, qkv_sums = attend(
        h1, dy_all, weight, spots, out_weight, qkv_b, cosine, sine, lengths, (send,)
    )

    pair_shape, one = (2, 128, width), (1, 128, width)

    def turn(k):
        return lambda n: (n[2] + k) % 4

    def far_body(n_ref, keep_ref, got_ref, low_ref, high_ref):
        total = wide(keep_ref, got_ref).astype(bf16)
        low_ref[0] = total[0]
        high_ref[0] = total[1]

    low, high = blocks_call(
        "far_sums",
        far_body,
        numbers,
        [(keep, pair_shape, turn(2)), (got, pair_shape, turn(2))],
        (one, one),
        (attended,),
    )
    from_low, from_high = move(low, y=1), move(high, y=-1)
    a_keep, a_send = attention_grads(h1, dy_all, d_qkv, attended, numbers, (low, high))
    a_got = move(a_send, c=1)
    def near_body(n_ref, k1_ref, g1_ref, k3_ref, g3_ref, low_ref, high_ref, above_ref, below_ref):
        above, below = wide(k1_ref, g1_ref), wide(k3_ref, g3_ref)
        above_ref[0] = (above[0] + low_ref[0].astype(f32)).astype(bf16)
        above_ref[1] = above[1].astype(bf16)
        below_ref[0] = below[0].astype(bf16)
        below_ref[1] = (below[1] + high_ref[0].astype(f32)).astype(bf16)

    above, below = blocks_call(
        "near_sums",
        near_body,
        numbers,
        [(v, pair_shape, turn(k)) for k in (1, 3) for v in (keep, got)]
        + [(v, one, lambda n: 0) for v in (from_low, from_high)],
        (pair_shape, pair_shape),
        (a_send,),
        20,
    )
    from_below, from_above = move(above, y=1), move(below, y=-1)

    four = (4, 64, width)

    def both_body(n_ref, low_keep, low_got, high_keep, high_got, out_ref):
        out_ref[0:4] = wide(low_keep, low_got).astype(bf16)
        out_ref[4:8] = wide(high_keep, high_got).astype(bf16)

    (a_sent,) = blocks_call(
        "both_sums",
        both_body,
        numbers,
        [(v, four, lambda n, half=half: half) for half in range(2) for v in (a_keep, a_got)],
        ((8, 64, width),),
        (above,),
    )
    a_parts = lax.all_to_all(a_sent, "rep", 0, 0, axis_index_groups=SAME_CORE)
    norm_sums, *pairs_out = outer(
        d_qkv,
        d_hidden,
        weight,
        spots,
        x_all,
        mean,
        inverse,
        jnp.stack([gains[0], gains[2]]),
        active,
        attended,
        down_weight,
        out_weight,
        wide_bias,
        (a_sent, above, below),
    )

    passed_below, passed_above = move(pairs_out[6], x=1), move(pairs_out[2], x=-1)

    def passed_body(n_ref, up_ref, from_below, here_ref, down_ref, from_above, there_ref, up_out, down_out):
        up_out[0:2] = wide(up_ref, from_below).astype(bf16)
        up_out[2:4] = here_ref[...]
        down_out[0:2] = wide(down_ref, from_above).astype(bf16)
        down_out[2:4] = there_ref[...]

    def other_body(n_ref, own_ref, below_ref, above_ref, out_ref):
        out_ref[...] = wide(own_ref, below_ref, above_ref).astype(bf16)

    def first(n):
        return 0

    def ends_body(n_ref, keep_ref, got_ref, below_ref, above_ref, leave_ref, stay_ref):
        total = wide(keep_ref, got_ref, below_ref, above_ref).astype(bf16)
        first = n_ref[3] == 0
        leave_ref[0] = jnp.where(first, total[1], total[0])
        stay_ref[0] = jnp.where(first, total[0], total[1])

    leaves, stays = blocks_call(
        "end_sums",
        ends_body,
        numbers,
        [(v, pair_shape, turn(0)) for v in (keep, got)]
        + [(v, pair_shape, lambda n: 0) for v in (from_below, from_above)],
        (one, one),
        (norm_sums,),
    )
    crossed = move(leaves, h=1)

    part, stays = packed_sums(
        stays,
        crossed,
        a_parts,
        norm_sums,
        qkv_sums,
        up_sums,
        dy_sums,
        numbers,
        ff,
        head,
        (),
    )
    received = lax.all_to_all(part, "shard", 0, 0)
    ups, downs = blocks_call(
        "passed_sums",
        passed_body,
        numbers,
        [
            (v, pair_shape, first)
            for v in (
                pairs_out[5],
                passed_below,
                pairs_out[1],
                pairs_out[3],
                passed_above,
                pairs_out[7],
            )
        ],
        ((4, 128, width),) * 2,
        (part,),
    )
    stays = stays[None]
    stays = jnp.concatenate([stays, move(stays, h=1)])
    part = unpacked_sums(received, cols, (ups, stays))
    beside = move(stays, y=1), move(stays, y=-1)
    stays = joined((stays, beside[1], beside[0], move(beside[0], y=1)), ())
    from_device_below, from_device_above = move(ups, x=1), move(downs, x=-1)
    (sent_other,) = blocks_call(
        "other_sums",
        other_body,
        numbers,
        [
            (pairs_out[4], pair_shape, first),
            (from_device_below, pair_shape, first),
            (from_device_above, pair_shape, lambda n: 1),
        ],
        (pair_shape,),
        (),
    )
    total_other = move(sent_other, l=1)

    order = ((0, h), (0, 1 - h), (1, h), (1, 1 - h), (3, h), (3, 1 - h), (2, h), (2, 1 - h))
    places = jnp.stack([(y + k) % 4 * 2 + high for k, high in order]).astype(jnp.int32)

    down_grad, out_grad = spread(
        [(stays, move(stays, c=1))],
        places,
        numbers[:1],
        [(width, 64, [(0, 0, 0, width)]), (width, 16, [(0, 64, 0, width)])],
        8,
        (),
        (),
        14,
    )
    part = joined((part, move(part, h=1)), beside)
    below, above = move(part, y=1), move(part, y=-1)
    low, high, near = halves(part, below, above, (stays, sent_other))
    far = move(low, y=1), move(high, y=-1)
    targets = [
        (
            3 * width,
            16,
            [
                ((third * 8 + source) * head, 16 * source, third * head, head)
                for source in range(8)
                for third in range(3)
            ],
        ),
        (8 * ff, 16, [(source * ff, 16 * source, 3 * head, ff) for source in range(8)]),
    ]
    near_yours = move(near, c=1)
    grads = spread(
        [(near, near_yours)], places[:6], numbers[:1], targets, 8, (), (down_grad, sent_other)
    )
    far = joined(far, (grads[0],))
    mixed, tokens_grad = finished(
        pairs_out[0], from_device_below, from_device_above, total_other, tokens, cotangent, (far,)
    )
    far_yours = move(far, c=1)
    qkv_grad, up_grad = spread(
        [(far, far_yours)],
        places[6:],
        numbers[:1],
        targets,
        8,
        grads,
        (tokens_grad,),
    )
    smalls = [v[:, 0:16, cols:] for v in (near, near_yours, far, far_yours)]
    smalls = jnp.sum(jnp.concatenate(smalls).astype(f32), 0)
    norm_grads = smalls[:4]
    dy_total = smalls[11]
    return (
        mixed,
        tokens_grad,
        norm_grads[0],
        norm_grads[1],
        norm_grads[2],
        norm_grads[3],
        qkv_grad,
        smalls[4:7].reshape(3 * head),
        out_grad,
        dy_total,
        up_grad,
        smalls[7:11].reshape(ff),
        down_grad,
        dy_total,
    )


def solution(mesh):
    rows = P(BOTH, None)
    vector, matrix = P("shard"), P("shard", None)
    return jax.shard_map(
        local,
        mesh=mesh,
        in_specs=(rows, rows, rows, vector, vector, vector, vector)
        + (matrix, vector, matrix, vector, matrix, vector, matrix, vector),
        out_specs=(rows, rows, vector, vector, vector, vector)
        + (matrix, vector, matrix, vector, matrix, vector, matrix, vector),
        check_vma=False,
    )
```

```python
import functools
import math

import jax
import jax.numpy as jnp
from jax import lax
from jax.experimental import pallas as pl
from jax.experimental.pallas import tpu as pltpu
from jax.sharding import PartitionSpec as P

HEADS = 8
ROT = 64
EPS = 1e-05
f32 = jnp.float32
bf16 = jnp.bfloat16


def cost(time):
    return pl.CostEstimate(flops=int(time * 1.15e9), bytes_accessed=1000, transcendentals=0)


BOTH = ("rep", "shard")
SIZES = (4, 2, 2, 2, 4)
SAME_CORE = [[2 * n + c for n in range(8)] for c in range(2)]
SAME_CORE_ALL = [[(2 * n + c) * 8 + s for n in range(8) for s in range(8)] for c in range(2)]


def coords():
    for y in range(4):
        for h in range(2):
            for c in range(2):
                for l in range(2):
                    for x in range(4):
                        yield (y, h, c, l, x)


def linear(t):
    y, h, c, l, x = (v % m for v, m in zip(t, SIZES))
    return ((y * 2 + h) * 2 + c) * 8 + l * 4 + x


def move(value, y=0, h=0, c=0, l=0, x=0):
    step = (y, h, c, l, x)
    pairs = [(linear(t), linear(tuple(a + b for a, b in zip(t, step)))) for t in coords()]
    return lax.ppermute(value, BOTH, pairs)


def pick(value, index, axis):
    return lax.dynamic_index_in_dim(value, index, axis, keepdims=False)


def kernel_params():
    return pltpu.CompilerParams(vmem_limit_bytes=56 * 1024 * 1024)


def after_inputs(body, count, extra):
    return lambda *refs: body(*refs[:count], *refs[count + extra :])


def anywhere(count):
    return [pl.BlockSpec(memory_space=pl.ANY)] * count


def dot(a, b, ca=1, cb=0):
    return lax.dot_general(a, b, (((ca,), (cb,)), ((), ())), preferred_element_type=f32)


def swap_halves(value):
    lane = lax.broadcasted_iota(jnp.int32, value.shape, 1)
    return jnp.where(lane < 32, pltpu.roll(value, 96, 1), pltpu.roll(value, 32, 1))


def allowed_mask(lengths_ref, block, rows):
    e0 = lengths_ref[block, 0]
    e1 = e0 + lengths_ref[block, 1]
    t = lax.broadcasted_iota(jnp.int32, (rows, rows), 0)
    s = lax.broadcasted_iota(jnp.int32, (rows, rows), 1)
    seg_t = (t >= e0).astype(jnp.int32) + (t >= e1).astype(jnp.int32)
    seg_s = (s >= e0).astype(jnp.int32) + (s >= e1).astype(jnp.int32)
    return (seg_t == seg_s) & (s <= t)


def dot_rows(a, b):
    return lax.dot_general(a, b, (((0,), (0,)), ((), ())), preferred_element_type=f32)


def loads(copies):
    for copy in copies:
        copy.start()
    return copies


def piece_copies(pieces, half, target, sems, rows, lanes=slice(None)):
    return [
        pltpu.make_async_copy(
            piece.at[half, :, lanes] if len(piece.shape) == 3 else piece.at[:, lanes],
            target.at[pl.ds(at * rows, rows)],
            sems.at[at],
        )
        for at, piece in enumerate(pieces)
    ]


def weight_copies(pieces, refs, spot_ref, target, lanes, sems, source=None):
    if source is not None:
        pieces = [
            (
                array,
                begin + max(source - first, 0),
                min(size, 4),
                max(first, source) - source,
                spot,
                ref,
            )
            for (array, begin, size, first, spot), ref in zip(pieces, refs)
            if first <= source < first + size
        ]
    else:
        pieces = [(*piece, ref) for piece, ref in zip(pieces, refs)]
    return [
        pltpu.make_async_copy(
            ref.at[pl.ds(begin, size), :, lanes],
            target.at[pl.ds(first, size), spot_ref[spot]],
            sems.at[at],
        )
        for at, (_, begin, size, first, spot, ref) in enumerate(pieces)
    ]


def feed_forward(x, dy, gains, weight, spots, down, bias, numbers, first, after):
    rows, width = x[0].shape[1:]
    count = len(x)
    total = rows * count
    ff = bias.shape[1]

    parts = len(weight)

    def body(number_ref, spot_ref, g_ref, b_ref, *refs):
        w_refs, refs = refs[:parts], refs[parts:]
        x_refs, dy_refs, d_hbm = refs[:count], refs[count : 2 * count], refs[2 * count]
        (h1_hbm, act_hbm, du_hbm, keep_hbm, send_hbm, m_ref, i_ref, db_ref, sum_ref) = refs[
            2 * count + 1 : 2 * count + 10
        ]
        (x_v, dy_v, h1_v, h2_v, w_v, d_v, act_v, du_v, keep_v, send_v, x_sem, dy_sem, w_sem, sems) = refs[
            2 * count + 10 :
        ]
        own = number_ref[0] == 0
        x_copies = loads(piece_copies(x_refs, 0, x_v, x_sem, rows))
        w_copies = loads(
            weight_copies(weight, w_refs, spot_ref, w_v, pl.ds(first, ff), w_sem)
        )
        dy_copies = loads(piece_copies(dy_refs, 1, dy_v, dy_sem, rows))
        d_copy = pltpu.make_async_copy(d_hbm, d_v, sems.at[1])
        d_copy.start()
        for copy in x_copies:
            copy.wait()

        @pl.loop(0, count)
        def _(n):
            at = pl.ds(pl.multiple_of(n * rows, rows), rows)
            value = x_v[at, :].astype(f32)
            mean = jnp.mean(value, 1, keepdims=True)
            centre = value - mean
            inverse = lax.rsqrt(jnp.mean(centre * centre, 1, keepdims=True) + EPS)
            normed = centre * inverse
            m_ref[at, :] = mean
            i_ref[at, :] = inverse
            h1_v[at, :] = (normed * g_ref[0:1] + g_ref[1:2]).astype(bf16)
            h2_v[at, :] = (normed * g_ref[2:3] + g_ref[3:4]).astype(bf16)

        h1_copy = pltpu.make_async_copy(h1_v, h1_hbm, sems.at[2])
        h1_copy.start()
        for copy in w_copies + dy_copies:
            copy.wait()
        d_copy.wait()
        mine = dy_v[:, pl.ds(pl.multiple_of(number_ref[1] * 256, 256), 256)]
        sum_ref[...] = jnp.sum(mine.astype(f32), 0, keepdims=True)

        def split(part, places, high, wide):
            at = (places, high, wide)

            @pl.when(own)
            def _():
                keep_v[at] = part[:, 0]
                send_v[at] = part[:, 1]

            @pl.when(jnp.logical_not(own))
            def _():
                keep_v[at] = part[:, 1]
                send_v[at] = part[:, 0]

        def leaving(n):
            at = (pl.ds(n * 2, 2), pl.ds(0, 64))
            return (
                pltpu.make_async_copy(keep_v.at[at], keep_hbm.at[at], sems.at[3]),
                pltpu.make_async_copy(send_v.at[at], send_hbm.at[at], sems.at[4]),
            )

        @pl.loop(0, ff // 256)
        def _(n):
            at = pl.ds(pl.multiple_of(n * 256, 256), 256)
            u = dot(h2_v[...], w_v[:, :, :, at].reshape(width, 256)) + b_ref[:, at]
            cdf = 0.5 * (1.0 + lax.erf(u * math.sqrt(0.5)))
            pdf = jnp.exp(-0.5 * u * u) * (1.0 / math.sqrt(2.0 * math.pi))
            act = (u * cdf).astype(bf16)
            act_v[:, at] = act
            du = (dot(dy_v[...], d_v[at, :], 1, 1) * (cdf + u * pdf)).astype(bf16)
            du_v[:, at] = du
            db_ref[:, at] = jnp.sum(du.astype(f32), 0, keepdims=True)
            part = dot_rows(act, dy_v[...]).astype(bf16).reshape(2, 2, 64, width)
            split(part, pl.ds(n * 2, 2), pl.ds(0, 64), slice(None))
            for copy in leaving(n):
                copy.start()

        act_copy = pltpu.make_async_copy(act_v, act_hbm, sems.at[0])
        act_copy.start()
        du_copy = pltpu.make_async_copy(du_v, du_hbm, sems.at[1])
        du_copy.start()
        for n in range(ff // 256):
            for copy in leaving(n):
                copy.wait()

        def block(n):
            at = (
                slice(None),
                pl.ds(pl.multiple_of(64 + 16 * (n % 4), 16), 16),
                pl.ds(pl.multiple_of(n // 4 * ff, ff), ff),
            )
            return at

        def away(n):
            at = block(n)
            return (
                pltpu.make_async_copy(keep_v.at[at], keep_hbm.at[at], sems.at[3]),
                pltpu.make_async_copy(send_v.at[at], send_hbm.at[at], sems.at[4]),
            )

        @pl.loop(0, 8)
        def _(n):
            lanes = pl.ds(pl.multiple_of(n * 256, 256), 256)
            part = dot_rows(h2_v[:, lanes], du_v[...]).astype(bf16).reshape(8, 2, 16, ff)
            split(part, *block(n))
            for copy in away(n):
                copy.start()

        for n in range(8):
            for copy in away(n):
                copy.wait()
        h1_copy.wait()
        act_copy.wait()
        du_copy.wait()

    wide = jax.ShapeDtypeStruct((total, width), bf16)
    thin = jax.ShapeDtypeStruct((total, ff), bf16)
    column = jax.ShapeDtypeStruct((total, 1), f32)
    grads = jax.ShapeDtypeStruct((8, 128, width), bf16)
    vmem = pl.BlockSpec(memory_space=pltpu.VMEM)
    return pl.pallas_call(
        after_inputs(body, 5 + parts + 2 * count, len(after)),
        out_shape=(
            wide,
            thin,
            thin,
            grads,
            grads,
            column,
            column,
            jax.ShapeDtypeStruct((1, ff), f32),
            jax.ShapeDtypeStruct((1, 256), f32),
        ),
        in_specs=[pl.BlockSpec(memory_space=pltpu.SMEM)] * 2
        + [vmem, vmem]
        + anywhere(parts + 2 * count + 1 + len(after)),
        out_specs=tuple(anywhere(5)) + (vmem,) * 4,
        scratch_shapes=[
            pltpu.VMEM((total, width), bf16),
            pltpu.VMEM((total, width), bf16),
            pltpu.VMEM((total, width), bf16),
            pltpu.VMEM((total, width), bf16),
            pltpu.VMEM((8, 8, width // 64, ff), bf16),
            pltpu.VMEM((ff, width), bf16),
            pltpu.VMEM((total, ff), bf16),
            pltpu.VMEM((total, ff), bf16),
            pltpu.VMEM((8, 128, width), bf16),
            pltpu.VMEM((8, 128, width), bf16),
            pltpu.SemaphoreType.DMA((count,)),
            pltpu.SemaphoreType.DMA((count,)),
            pltpu.SemaphoreType.DMA((parts,)),
            pltpu.SemaphoreType.DMA((5,)),
        ],
        compiler_params=kernel_params(),
        cost_estimate=cost(32),
        name="feed_forward",
    )(numbers, spots, gains, bias, *[p[0] for p in weight], *x, *dy, down, *after)


def packed(qkv_weight, up_weight, vectors, lengths, place, head, tokens, cotangent):
    wide, up_wide = qkv_weight.shape[1], up_weight.shape[1]
    part, up_part = 3 * head, up_wide // 8
    cols = part + up_part

    def body(place_ref, len_ref, q_ref, u_ref, x_ref, dy_ref, *refs):
        v_refs, out_ref, pair_ref = refs[: len(vectors)], refs[-2], refs[-1]
        pair_ref[0] = x_ref[...]
        pair_ref[1] = dy_ref[...]
        lane = lax.broadcasted_iota(jnp.int32, (8, cols), 1)
        row = lax.broadcasted_iota(jnp.int32, (8, cols), 0)
        sizes = jnp.zeros((8, cols), f32)
        for at in range(3):
            sizes = jnp.where(lane == at, len_ref[0, at].astype(f32), sizes)
        vector = jnp.concatenate([ref[...].astype(f32) for ref in v_refs])[None, :]
        vector = jnp.broadcast_to(vector, (8, cols))
        tail = jnp.where(row == 0, vector, jnp.where(row == 1, sizes, 0.0)).astype(bf16)
        for owner in range(8):
            pieces = [
                q_ref[:, (third * 8 + owner) * head : (third * 8 + owner + 1) * head]
                for third in range(3)
            ]
            pieces.append(u_ref[:, owner * up_part : (owner + 1) * up_part])
            out_ref[owner] = jnp.concatenate([jnp.concatenate(pieces, 1), tail], 0)

    return pl.pallas_call(
        body,
        out_shape=(
            jax.ShapeDtypeStruct((8, 40, cols), bf16),
            jax.ShapeDtypeStruct((2,) + tokens.shape, bf16),
        ),
        grid_spec=pltpu.PrefetchScalarGridSpec(
            num_scalar_prefetch=2,
            grid=(1,),
            in_specs=[
                pl.BlockSpec((32, wide), lambda i, place, lens: (place[0], 0)),
                pl.BlockSpec((32, up_wide), lambda i, place, lens: (place[0], 0)),
                pl.BlockSpec(tokens.shape, lambda i, place, lens: (0, 0)),
                pl.BlockSpec(tokens.shape, lambda i, place, lens: (0, 0)),
            ]
            + [pl.BlockSpec(v.shape, lambda i, place, lens: (0,)) for v in vectors],
            out_specs=(
                pl.BlockSpec((8, 40, cols), lambda i, place, lens: (0, 0, 0)),
                pl.BlockSpec((2,) + tokens.shape, lambda i, place, lens: (0, 0, 0)),
            ),
        ),
        compiler_params=kernel_params(),
        cost_estimate=cost(3),
        name="packed",
    )(place, lengths, qkv_weight, up_weight, tokens, cotangent, *vectors)


def attend(h1, dy, weight, spots, out, bias, cosine, sine, lengths, after, rows=128):
    total, width = h1.shape
    count = len(dy)
    head = out.shape[0]
    scale = head ** (-0.5)

    parts = len(weight)

    def body(len_ref, spot_ref, b_ref, *refs):
        w_refs, refs = refs[:parts], refs[parts:]
        dy_refs = refs[:count]
        h1_hbm, out_hbm, cos_hbm, sin_hbm = refs[count : count + 4]
        ol_hbm, dq_hbm, sum_ref = refs[count + 4 : count + 7]
        (dy_v, h1_v, w_v, wo_v, cos_v, sin_v, qkv_v, do_v, ol_v, dq_v, dy_sem, w_sem, sems) = (
            refs[count + 7 :]
        )
        pairs = (
            (h1_hbm, h1_v),
            (out_hbm, wo_v),
            (cos_hbm, cos_v),
            (sin_hbm, sin_v),
        )
        copies = loads(
            [pltpu.make_async_copy(*pair, sems.at[n]) for n, pair in enumerate(pairs)]
        )
        w_copies = loads(
            weight_copies(weight, w_refs, spot_ref, w_v, pl.ds(0, 3 * head), w_sem)
        )
        dy_copies = loads(piece_copies(dy_refs, 1, dy_v, dy_sem, rows))
        for copy in copies[:1] + w_copies:
            copy.wait()

        @pl.loop(0, 3)
        def _(n):
            at = pl.ds(pl.multiple_of(n * head, head), head)
            qkv_v[:, at] = dot(h1_v[...], w_v[:, :, :, at].reshape(width, head)) + b_ref[n]

        for copy in copies[1:] + dy_copies:
            copy.wait()
        do_v[...] = dot(dy_v[...], wo_v[...], 1, 1).astype(bf16)
        sum_ref[...] = jnp.zeros_like(sum_ref)

        @pl.loop(0, total // rows, unroll=2)
        def _(block):
            at = pl.ds(pl.multiple_of(block * rows, rows), rows)
            cos, sin = cos_v[at, :], sin_v[at, :]

            def turned(value, sign):
                left = value[:, :128]
                left = left * cos + swap_halves(left) * (sin * sign)
                return jnp.concatenate([left, value[:, 128:]], 1).astype(bf16)

            q, k = turned(qkv_v[at, 0:head], 1.0), turned(qkv_v[at, head : 2 * head], 1.0)
            v = qkv_v[at, 2 * head :].astype(bf16)
            scores = dot(q, k, 1, 1) * scale
            masked = jnp.where(allowed_mask(len_ref, block, rows), scores, -1e30)
            shifted = jnp.exp(masked - jnp.max(masked, 1, keepdims=True))
            probs = shifted / jnp.sum(shifted, 1, keepdims=True)
            low = probs.astype(bf16)
            ol_v[at, :] = dot(low, v).astype(bf16)
            d_out = do_v[at, :]
            d_value = dot(low, d_out, 0, 0)
            d_probs = dot(d_out, v, 1, 1)
            centred = d_probs - jnp.sum(d_probs * probs, 1, keepdims=True)
            d_scores = (probs * centred).astype(bf16)
            d_query = turned(dot(d_scores, k) * scale, -1.0)
            d_key = turned(dot(d_scores, q, 0, 0) * scale, -1.0)
            for n, grad in enumerate((d_query, d_key, d_value.astype(bf16))):
                lanes = slice(n * head, (n + 1) * head)
                dq_v[at, lanes] = grad
                sum_ref[:, lanes] += jnp.sum(grad.astype(f32), 0, keepdims=True)

        ol_copy = pltpu.make_async_copy(ol_v, ol_hbm, sems.at[0])
        ol_copy.start()
        dq_copy = pltpu.make_async_copy(dq_v, dq_hbm, sems.at[1])
        dq_copy.start()

        for copy in (ol_copy, dq_copy):
            copy.wait()

    vmem = pl.BlockSpec(memory_space=pltpu.VMEM)
    smem = pl.BlockSpec(memory_space=pltpu.SMEM)
    return pl.pallas_call(
        after_inputs(body, 7 + parts + count, len(after)),
        out_shape=(
            jax.ShapeDtypeStruct((total, head), bf16),
            jax.ShapeDtypeStruct((total, 3 * head), bf16),
            jax.ShapeDtypeStruct((1, 3 * head), f32),
        ),
        in_specs=[smem, smem, vmem] + anywhere(parts + count + 4 + len(after)),
        out_specs=tuple(anywhere(2)) + (vmem,),
        scratch_shapes=[
            pltpu.VMEM((total, width), bf16),
            pltpu.VMEM((total, width), bf16),
            pltpu.VMEM((8, 8, width // 64, 3 * head), bf16),
            pltpu.VMEM((head, width), bf16),
            pltpu.VMEM((total, 128), f32),
            pltpu.VMEM((total, 128), f32),
            pltpu.VMEM((total, 3 * head), f32),
            pltpu.VMEM((total, head), bf16),
            pltpu.VMEM((total, head), bf16),
            pltpu.VMEM((total, 3 * head), bf16),
            pltpu.SemaphoreType.DMA((count,)),
            pltpu.SemaphoreType.DMA((parts,)),
            pltpu.SemaphoreType.DMA((4,)),
        ],
        compiler_params=kernel_params(),
        cost_estimate=cost(17),
        name="attend",
    )(
        lengths,
        spots,
        bias,
        *[p[0] for p in weight],
        *dy,
        h1,
        out,
        cosine,
        sine,
        *after,
    )


def attention_grads(h1, dy, d_qkv, attended, numbers, after):
    total, width = h1.shape
    count = len(dy)
    rows = total // count
    head = attended.shape[1]

    def body(number_ref, *refs):
        dy_refs = refs[:count]
        h1_hbm, dq_hbm, ol_hbm, keep_hbm, send_hbm = refs[count : count + 5]
        dy_v, h1_v, dq_v, ol_v, keep_v, send_v, dy_sem, sems = refs[count + 5 :]
        own = number_ref[0] == 0
        pairs = ((h1_hbm, h1_v), (dq_hbm, dq_v), (ol_hbm, ol_v))
        copies = loads(
            [pltpu.make_async_copy(*pair, sems.at[n]) for n, pair in enumerate(pairs)]
        )
        dy_copies = loads(piece_copies(dy_refs, 1, dy_v, dy_sem, rows))
        for copy in copies:
            copy.wait()

        def split(part, high, lanes):
            at = (slice(None), high, lanes)

            @pl.when(own)
            def _():
                keep_v[at] = part[:, 0]
                send_v[at] = part[:, 1]

            @pl.when(jnp.logical_not(own))
            def _():
                keep_v[at] = part[:, 1]
                send_v[at] = part[:, 0]

        @pl.loop(0, 8)
        def _(n):
            lanes = pl.ds(pl.multiple_of(n * 256, 256), 256)
            part = dot_rows(h1_v[:, lanes], dq_v[...]).astype(bf16).reshape(8, 2, 16, 3 * head)
            for third in range(3):
                split(
                    part[..., third * head : (third + 1) * head],
                    pl.ds(16 * third, 16),
                    pl.ds(pl.multiple_of(n * head, head), head),
                )

        for copy in dy_copies:
            copy.wait()
        part = dot_rows(ol_v[...], dy_v[...]).astype(bf16).reshape(8, 2, 16, width)
        split(part, pl.ds(48, 16), slice(None))
        keep_copy = pltpu.make_async_copy(keep_v, keep_hbm, sems.at[0])
        keep_copy.start()
        send_copy = pltpu.make_async_copy(send_v, send_hbm, sems.at[1])
        send_copy.start()
        keep_copy.wait()
        send_copy.wait()

    grads = jax.ShapeDtypeStruct((8, 64, width), bf16)
    return pl.pallas_call(
        after_inputs(body, 4 + count, len(after)),
        out_shape=(grads, grads),
        in_specs=[pl.BlockSpec(memory_space=pltpu.SMEM)] + anywhere(count + 3 + len(after)),
        out_specs=tuple(anywhere(2)),
        scratch_shapes=[
            pltpu.VMEM((total, width), bf16),
            pltpu.VMEM((total, width), bf16),
            pltpu.VMEM((total, 3 * head), bf16),
            pltpu.VMEM((total, head), bf16),
            pltpu.VMEM((8, 64, width), bf16),
            pltpu.VMEM((8, 64, width), bf16),
            pltpu.SemaphoreType.DMA((count,)),
            pltpu.SemaphoreType.DMA((3,)),
        ],
        compiler_params=kernel_params(),
        cost_estimate=cost(12),
        name="attention_grads",
    )(numbers, *dy, h1, d_qkv, attended, *after)


def outer(d_qkv, d_hidden, weight, spots, x, mean, inverse, gains, active, attended, down, out, bias, after):
    total, n1 = d_qkv.shape
    n2 = d_hidden.shape[1]
    count = len(x)
    parts = len(weight)
    head, width = out.shape
    step = 512

    def body(spot_ref, m_ref, i_ref, g_ref, b_ref, *refs):
        w_refs, refs = refs[:parts], refs[parts:]
        x_refs, refs = refs[:count], refs[count:]
        plain, sums_ref, outs = refs[:6], refs[6], refs[7 : 7 + count]
        dq_v, du_v, act_v, ol_v, wd_v, wo_v, w_v, x_v, pair_v, w_sem, x_sem, sems, out_sem = refs[
            7 + count :
        ]
        plain_v = (dq_v, du_v, act_v, ol_v, wd_v, wo_v)
        first = loads(
            [
                pltpu.make_async_copy(plain[n], plain_v[n], sems.at[n]) for n in range(2, 6)
            ]
        )
        copies = loads(
            [
                pltpu.make_async_copy(plain[n], plain_v[n], sems.at[n]) for n in range(2)
            ]
            + weight_copies(weight, w_refs, spot_ref, w_v, slice(None), w_sem)
            + piece_copies(x_refs, 0, x_v, x_sem, 128)
        )
        for copy in first:
            copy.wait()

        def leaving(n, half):
            lanes = pl.ds(pl.multiple_of(n * step, step), step)
            return [
                pltpu.make_async_copy(
                    pair_v.at[half, pl.ds(at * 128, 128), lanes],
                    outs[at].at[half, :, lanes],
                    out_sem.at[half, at],
                )
                for at in range(count)
            ]

        @pl.loop(0, width // step)
        def _(n):
            lanes = pl.ds(pl.multiple_of(n * step, step), step)
            mix = dot(act_v[...], wd_v[:, lanes]) + dot(ol_v[...], wo_v[:, lanes])
            pair_v[0, :, lanes] = (mix + b_ref[:, lanes]).astype(bf16)
            for copy in leaving(n, 0):
                copy.start()

        for copy in copies:
            copy.wait()

        @pl.loop(0, width // step)
        def _(n):
            lanes = pl.ds(pl.multiple_of(n * step, step), step)
            sources = pl.ds(n * (step // 256), step // 256)
            d1 = dot(dq_v[...], w_v[sources, :, :, 0:n1].reshape(step, n1), 1, 1)
            d2 = dot(du_v[...], w_v[sources, :, :, n1:].reshape(step, n2), 1, 1)
            pair_v[1, :, lanes] = (d1 * g_ref[0:1, lanes] + d2 * g_ref[1:2, lanes]).astype(bf16)
            for copy in leaving(n, 1):
                copy.start()
            normed = (x_v[:, lanes].astype(f32) - m_ref[...]) * i_ref[...]
            sums_ref[0:1, lanes] = jnp.sum(d1 * normed, 0, keepdims=True)
            sums_ref[1:2, lanes] = jnp.sum(d1, 0, keepdims=True)
            sums_ref[2:3, lanes] = jnp.sum(d2 * normed, 0, keepdims=True)
            sums_ref[3:4, lanes] = jnp.sum(d2, 0, keepdims=True)

        for n in range(width // step):
            for half in range(2):
                for copy in leaving(n, half):
                    copy.wait()

    vmem = pl.BlockSpec(memory_space=pltpu.VMEM)
    return pl.pallas_call(
        after_inputs(body, 11 + parts + count, len(after)),
        out_shape=(jax.ShapeDtypeStruct((4, width), f32),)
        + (jax.ShapeDtypeStruct((2, 128, width), bf16),) * count,
        in_specs=[pl.BlockSpec(memory_space=pltpu.SMEM)]
        + [vmem] * 4
        + anywhere(parts + count + 6 + len(after)),
        out_specs=(vmem,) + tuple(anywhere(count)),
        scratch_shapes=[
            pltpu.VMEM((total, n1), bf16),
            pltpu.VMEM((total, n2), bf16),
            pltpu.VMEM((total, n2), bf16),
            pltpu.VMEM((total, head), bf16),
            pltpu.VMEM((n2, width), bf16),
            pltpu.VMEM((head, width), bf16),
            pltpu.VMEM((8, 8, width // 64, n1 + n2), bf16),
            pltpu.VMEM((total, width), bf16),
            pltpu.VMEM((2, total, width), bf16),
            pltpu.SemaphoreType.DMA((parts,)),
            pltpu.SemaphoreType.DMA((count,)),
            pltpu.SemaphoreType.DMA((6,)),
            pltpu.SemaphoreType.DMA((2, count)),
        ],
        compiler_params=kernel_params(),
        cost_estimate=cost(20),
        name="outer",
    )(
        spots,
        mean,
        inverse,
        gains,
        bias,
        *[p[0] for p in weight],
        *x,
        d_qkv,
        d_hidden,
        active,
        attended,
        down,
        out,
        *after,
    )


def unpacked(part, after):
    owners, _, cols = part.shape

    def body(part_ref, rows_ref, info_ref):
        for owner in range(owners):
            rows_ref[owner] = part_ref[owner, 0:32]
            info_ref[owner] = part_ref[owner, 32:40].astype(f32)

    return pl.pallas_call(
        after_inputs(body, 1, len(after)),
        out_shape=(
            jax.ShapeDtypeStruct((owners, 32, cols), bf16),
            jax.ShapeDtypeStruct((owners, 8, cols), f32),
        ),
        in_specs=[pl.BlockSpec(memory_space=pltpu.VMEM)] + anywhere(len(after)),
        out_specs=(pl.BlockSpec(memory_space=pltpu.VMEM),) * 2,
        compiler_params=kernel_params(),
        cost_estimate=cost(3),
        name="unpacked",
    )(part, *after)


def joined(arrays, after):
    sizes = [array.shape[0] for array in arrays]
    unit = math.gcd(*sizes)
    block = (unit,) + arrays[0].shape[1:]
    count = len(arrays)
    firsts = [sum(sizes[:n]) // unit for n in range(count)]

    def body(*refs):
        step = pl.program_id(0)
        for ref, first, size in zip(refs, firsts, sizes):

            @pl.when((step >= first) & (step < first + size // unit))
            def _(ref=ref):
                refs[count][...] = ref[...]

    def came(first, size):
        return pl.BlockSpec(block, lambda i: (jnp.clip(i - first, 0, size // unit - 1), 0, 0))

    return pl.pallas_call(
        after_inputs(body, count, len(after)),
        out_shape=jax.ShapeDtypeStruct((sum(sizes),) + block[1:], bf16),
        grid=(sum(sizes) // unit,),
        in_specs=[came(first, size) for first, size in zip(firsts, sizes)] + anywhere(len(after)),
        out_specs=pl.BlockSpec(block, lambda i: (i, 0, 0)),
        compiler_params=kernel_params(),
        cost_estimate=cost(3),
        name="joined",
    )(*arrays, *after)


def halves(own, below, above, after):
    count, rows, cols = own.shape
    half = count // 2

    def body(own_ref, below_ref, above_ref, low_ref, high_ref, all_ref):
        step = pl.program_id(0)
        all_ref[0] = own_ref[...]
        all_ref[1] = above_ref[...]
        all_ref[2] = below_ref[...]

        @pl.when(step == 0)
        def _():
            low_ref[...] = below_ref[...]

        @pl.when(step == 1)
        def _():
            high_ref[...] = above_ref[...]

    block = pl.BlockSpec((half, rows, cols), lambda i: (i, 0, 0))
    whole = pl.BlockSpec((half, rows, cols), lambda i: (0, 0, 0))
    low, high, together = pl.pallas_call(
        after_inputs(body, 3, len(after)),
        out_shape=(jax.ShapeDtypeStruct((half, rows, cols), bf16),) * 2
        + (jax.ShapeDtypeStruct((3, count, rows, cols), bf16),),
        grid=(2,),
        in_specs=[block] * 3 + anywhere(len(after)),
        out_specs=(
            whole,
            whole,
            pl.BlockSpec((3, half, rows, cols), lambda i: (0, i, 0, 0)),
        ),
        compiler_params=kernel_params(),
        cost_estimate=cost(4),
        name="halves",
    )(own, below, above, *after)
    return low, high, together.reshape(3 * count, rows, cols)


def unpacked_sums(received, cols, after):
    sources, rows, width = received.shape

    def body(part_ref, out_ref):
        small = jnp.sum(part_ref[:, :, cols:].astype(f32), 0).astype(bf16)
        out_ref[0] = jnp.concatenate(
            [jnp.concatenate([part_ref[0, :, 0:cols], small], 1)]
            + [part_ref[n] for n in range(1, sources)],
            0,
        )

    vmem = pl.BlockSpec(memory_space=pltpu.VMEM)
    return pl.pallas_call(
        after_inputs(body, 1, len(after)),
        out_shape=jax.ShapeDtypeStruct((1, sources * rows, width), bf16),
        in_specs=[vmem] + anywhere(len(after)),
        out_specs=vmem,
        compiler_params=kernel_params(),
        cost_estimate=cost(3),
        name="unpacked_sums",
    )(received, *after)


def spread(pieces, places, numbers, targets, count, before, after, time=2):
    rows, cols = pieces[0][0].shape[1:]
    firsts, total = [], 0
    for mine, _ in pieces:
        firsts.append(total)
        total += mine.shape[0] // 2

    def body(place_ref, number_ref, *refs):
        step = pl.program_id(0)
        outs = refs[2 * len(pieces) + len(before) :]
        core, z_hi = number_ref[0], number_ref[3]
        for n, (first, (mine, _)) in enumerate(zip(firsts, pieces)):

            @pl.when((step >= first) & (step < first + mine.shape[0] // 2))
            def _(n=n):
                for other_core in range(2):
                    ref = refs[2 * n + other_core]
                    low = 1 - core if other_core else core
                    for other_z in range(2):
                        at = (1 - z_hi if other_z else z_hi) * 2 + low
                        for out_ref, (_, high, parts) in zip(outs, targets):
                            to_rows = pl.ds(pl.multiple_of(at * high, high), high)
                            for to, row, col, size in parts:
                                out_ref[to_rows, to : to + size] = ref[
                                    other_z, row : row + high, col : col + size
                                ].astype(f32)

    def chosen(first, size):
        return pl.BlockSpec(
            (2, rows, cols), lambda i, place, n: (jnp.clip(i - first, 0, size - 1), 0, 0)
        )

    specs, arrays = [], []
    for first, (mine, yours) in zip(firsts, pieces):
        specs += [chosen(first, mine.shape[0] // 2)] * 2
        arrays += [mine, yours]
    return pl.pallas_call(
        after_inputs(body, 2 + 2 * len(pieces) + len(before), len(after)),
        out_shape=tuple(
            jax.ShapeDtypeStruct((4 * count * high, wide), f32) for wide, high, _ in targets
        ),
        grid_spec=pltpu.PrefetchScalarGridSpec(
            num_scalar_prefetch=2,
            grid=(total,),
            in_specs=specs + anywhere(len(before) + len(after)),
            out_specs=tuple(
                pl.BlockSpec((4 * high, wide), lambda i, place, n: (place[i], 0))
                for wide, high, _ in targets
            ),
        ),
        input_output_aliases={2 + len(arrays) + n: n for n in range(len(before))},
        compiler_params=kernel_params(),
        cost_estimate=cost(time),
        name="spread",
    )(places, numbers, *arrays, *before, *after)


def packed_sums(stays, crossed, parts, norm_sums, qkv_sums, up_sums, dy_sums, numbers, ff, head, after):
    width = parts.shape[2]

    def body(*refs):
        stay_ref, cross_ref, parts_ref = refs[:3]
        norm_ref, q_ref, u_ref, y_ref, number_ref, out_ref, keep_ref, small = refs[3:]
        shard = number_ref[1]
        inner = (stay_ref[0].astype(f32) + cross_ref[0].astype(f32)).astype(bf16)
        total = jnp.sum(parts_ref[...].astype(f32), 0).astype(bf16)
        for owner in range(8):
            mine = shard == owner
            small[...] = jnp.zeros_like(small)
            small[0:4] = norm_ref[:, owner * head : (owner + 1) * head]
            for n in range(3):
                third, source = divmod(owner * 3 + n, 8)
                lanes = slice(third * head, (third + 1) * head)
                small[4 + n : 5 + n] = jnp.where(shard == source, q_ref[:, lanes], 0.0)
            for n in range(4):
                lanes = slice(n * head, (n + 1) * head)
                small[7 + n : 8 + n] = jnp.where(mine, u_ref[:, lanes], 0.0)
            small[11:12] = jnp.where(mine, y_ref[...], 0.0)
            pieces = [
                total[16 * third : 16 * third + 16, owner * head : (owner + 1) * head]
                for third in range(3)
            ]
            row, col = 64 + 16 * (owner % 4), owner // 4 * ff
            pieces.append(inner[row : row + 16, col : col + ff])
            pieces.append(small[...].astype(bf16))
            out_ref[owner] = jnp.concatenate(pieces, 1)
        keep_ref[0:64] = inner[0:64]
        keep_ref[64:80] = total[48:64]

    vmem = pl.BlockSpec(memory_space=pltpu.VMEM)
    return pl.pallas_call(
        after_inputs(body, 8, len(after)),
        out_shape=(
            jax.ShapeDtypeStruct((8, 16, 4 * head + ff), bf16),
            jax.ShapeDtypeStruct((80, width), bf16),
        ),
        in_specs=[vmem] * 7 + [pl.BlockSpec(memory_space=pltpu.SMEM)] + anywhere(len(after)),
        out_specs=(vmem,) * 2,
        scratch_shapes=[pltpu.VMEM((16, head), f32)],
        compiler_params=kernel_params(),
        cost_estimate=cost(3),
        name="packed_sums",
    )(stays, crossed, parts, norm_sums, qkv_sums, up_sums, dy_sums, numbers, *after)


def finished(own, below, above, other, tokens, cotangent, after):
    rows, width = tokens.shape
    step = rows // 2

    def body(own_ref, below_ref, above_ref, other_ref, x_ref, dy_ref, mixed_ref, grad_ref):
        total = wide(own_ref, below_ref, above_ref, other_ref)
        x = x_ref[...].astype(f32)
        mixed_ref[...] = (x + total[0]).astype(bf16)
        centre = x - jnp.mean(x, 1, keepdims=True)
        inverse = lax.rsqrt(jnp.mean(centre * centre, 1, keepdims=True) + EPS)
        normed = centre * inverse
        gain = total[1]
        grad_ref[...] = dy_ref[...].astype(f32) + inverse * (
            gain
            - jnp.mean(gain, 1, keepdims=True)
            - normed * jnp.mean(gain * normed, 1, keepdims=True)
        )

    def pair(first):
        return pl.BlockSpec((2, step, width), lambda i: (first, i, 0))

    block = pl.BlockSpec((step, width), lambda i: (i, 0))
    return pl.pallas_call(
        after_inputs(body, 6, len(after)),
        out_shape=(
            jax.ShapeDtypeStruct((rows, width), bf16),
            jax.ShapeDtypeStruct((rows, width), f32),
        ),
        grid=(2,),
        in_specs=[pair(0), pair(1), pair(0), pair(0), block, block] + anywhere(len(after)),
        out_specs=(block, block),
        compiler_params=kernel_params(),
        cost_estimate=cost(14),
        name="finished",
    )(own, below, above, other, tokens, cotangent, *after)


def blocks_call(name, body, numbers, terms, outs, after, time=3):
    def came(block, index):
        rest = (0,) * (len(block) - 1)
        return pl.BlockSpec(block, lambda i, n: (index(n),) + rest)

    return pl.pallas_call(
        after_inputs(body, 1 + len(terms), len(after)),
        out_shape=tuple(jax.ShapeDtypeStruct(out, bf16) for out in outs),
        grid_spec=pltpu.PrefetchScalarGridSpec(
            num_scalar_prefetch=1,
            grid=(1,),
            in_specs=[came(block, index) for _, block, index in terms] + anywhere(len(after)),
            out_specs=tuple(
                pl.BlockSpec(out, lambda i, n, size=len(out): (0,) * size) for out in outs
            ),
        ),
        compiler_params=kernel_params(),
        cost_estimate=cost(time),
        name=name,
    )(numbers, *[array for array, _, _ in terms], *after)


def wide(*refs):
    return functools.reduce(jnp.add, [ref[...].astype(f32) for ref in refs])


def local(
    tokens,
    doc_lengths,
    cotangent,
    ln1_gain,
    ln1_bias,
    ln2_gain,
    ln2_bias,
    qkv_weight,
    qkv_bias,
    out_weight,
    out_bias,
    up_weight,
    up_bias,
    down_weight,
    down_bias,
):
    rows, width = tokens.shape
    head = width // HEADS
    group = 8
    rep = lax.axis_index("rep")
    shard = lax.axis_index("shard")
    y, h, c = rep // 4, (rep // 2) % 2, rep % 2
    l, x = shard // 4, shard % 4
    ff = up_bias.shape[0]

    cols = 3 * head + ff
    vectors = [ln1_gain, ln1_bias, ln2_gain, ln2_bias, qkv_bias]
    place = (y * 2 + c).astype(jnp.int32).reshape(1)
    part, pair = packed(
        qkv_weight, up_weight, vectors, doc_lengths, place, head, tokens, cotangent
    )
    below, above, other = move(pair, x=1), move(pair, x=-1), move(pair, l=1)
    far, other_above, other_below = move(below, x=1), move(other, x=-1), move(below, l=1)
    pairs = (pair, above, far, below, other, other_above, None, other_below)

    part = lax.all_to_all(part, "shard", 0, 0)
    own, infos = unpacked(part, (pairs[1], pairs[3], pairs[4]))
    below, above = move(own, y=1), move(own, y=-1)
    x_other_far, dy_other_far = move(other_below[0], x=1), move(other_above[1], x=-1)
    low, high, yours = halves(own, below, above, (far, other_above, other_below))
    far_low, far_high = move(low, y=1), move(high, y=-1)
    x_all = tuple(x_other_far if p is None else p for p in pairs)
    dy_all = tuple(dy_other_far if p is None else p for p in pairs)
    yours = move(yours, c=1)
    far_low_c, far_high_c = move(far_low, c=1), move(far_high, c=1)
    weight = (
        (own, 0, 8, 0, 0),
        (above, 0, 8, 0, 1),
        (far_low, 0, 4, 0, 2),
        (far_high, 0, 4, 4, 2),
        (below, 0, 8, 0, 3),
        (yours, 0, 8, 0, 4),
        (yours, 8, 8, 0, 5),
        (far_low_c, 0, 4, 0, 6),
        (far_high_c, 0, 4, 4, 6),
        (yours, 16, 8, 0, 7),
    )
    steps4 = (y + jnp.arange(4)) % 4
    spots = jnp.concatenate([steps4 * 2 + c, steps4 * 2 + 1 - c]).astype(jnp.int32)

    gains = infos[:, 0, :1024].reshape(8, 4, 256).transpose(1, 0, 2).reshape(4, width)
    qkv_b = infos[:, 0, 1024:].reshape(8 * 3, 1, head)
    qkv_b = jnp.stack(
        [lax.dynamic_index_in_dim(qkv_b, third * 8 + shard, 0, False) for third in range(3)]
    )
    steps8 = jnp.arange(8)
    sources = ((steps8 // 4) ^ l) * 4 + (x + steps8 % 4) % 4
    sources = sources.astype(jnp.int32)
    lengths = infos[:, 1, :3]
    lengths = jnp.sum(
        jnp.where(sources[:, None, None] == steps8[None, :, None], lengths[None], 0.0), 1
    ).astype(jnp.int32)
    ends = jnp.cumsum(lengths, 1)
    starts = ends - lengths
    steps_t = jnp.arange(rows, dtype=jnp.int32)
    segment = jnp.sum((steps_t[None, :, None] >= ends[:, None, :]).astype(jnp.int32), -1)
    slots = jnp.arange(lengths.shape[1], dtype=jnp.int32)
    begin = jnp.sum(
        jnp.where(segment[:, :, None] == slots[None, None, :], starts[:, None, :], 0), -1
    )
    position = (steps_t[None, :] - begin).astype(f32).reshape(group * rows, 1)
    lane = jnp.arange(128)
    freq = 10000.0 ** (-2.0 * (lane % (ROT // 2)).astype(f32) / ROT)
    angle = position * freq[None, :]
    cosine = jnp.where(lane < ROT, jnp.cos(angle), 1.0)
    sine = jnp.sin(angle)
    sine = jnp.where(lane < ROT // 2, -sine, jnp.where(lane < ROT, sine, 0.0))

    both_bias = (out_bias.astype(f32) + down_bias.astype(f32))[None, :]
    wide_bias = lax.dynamic_update_slice(jnp.zeros((1, width), f32), both_bias, (0, shard * 256))
    numbers = jnp.stack([c, shard, y, h]).astype(jnp.int32)

    h1, active, d_hidden, keep, send, mean, inverse, up_sums, dy_sums = feed_forward(
        x_all,
        dy_all,
        gains,
        weight,
        spots,
        down_weight,
        up_bias.astype(f32)[None],
        numbers,
        3 * head,
        (cosine, sine),
    )
    got = move(send, c=1)
    attended, d_qkv, qkv_sums = attend(
        h1, dy_all, weight, spots, out_weight, qkv_b, cosine, sine, lengths, (send,)
    )

    pair_shape, one = (2, 128, width), (1, 128, width)

    def turn(k):
        return lambda n: (n[2] + k) % 4

    def far_body(n_ref, keep_ref, got_ref, low_ref, high_ref):
        total = wide(keep_ref, got_ref).astype(bf16)
        low_ref[0] = total[0]
        high_ref[0] = total[1]

    low, high = blocks_call(
        "far_sums",
        far_body,
        numbers,
        [(keep, pair_shape, turn(2)), (got, pair_shape, turn(2))],
        (one, one),
        (attended,),
    )
    from_low, from_high = move(low, y=1), move(high, y=-1)
    a_keep, a_send = attention_grads(h1, dy_all, d_qkv, attended, numbers, (low, high))
    a_got = move(a_send, c=1)
    def near_body(n_ref, k1_ref, g1_ref, k3_ref, g3_ref, low_ref, high_ref, above_ref, below_ref):
        above, below = wide(k1_ref, g1_ref), wide(k3_ref, g3_ref)
        above_ref[0] = (above[0] + low_ref[0].astype(f32)).astype(bf16)
        above_ref[1] = above[1].astype(bf16)
        below_ref[0] = below[0].astype(bf16)
        below_ref[1] = (below[1] + high_ref[0].astype(f32)).astype(bf16)

    above, below = blocks_call(
        "near_sums",
        near_body,
        numbers,
        [(v, pair_shape, turn(k)) for k in (1, 3) for v in (keep, got)]
        + [(v, one, lambda n: 0) for v in (from_low, from_high)],
        (pair_shape, pair_shape),
        (a_send,),
        20,
    )
    from_below, from_above = move(above, y=1), move(below, y=-1)

    four = (4, 64, width)

    def both_body(n_ref, low_keep, low_got, high_keep, high_got, out_ref):
        out_ref[0:4] = wide(low_keep, low_got).astype(bf16)
        out_ref[4:8] = wide(high_keep, high_got).astype(bf16)

    (a_sent,) = blocks_call(
        "both_sums",
        both_body,
        numbers,
        [(v, four, lambda n, half=half: half) for half in range(2) for v in (a_keep, a_got)],
        ((8, 64, width),),
        (above,),
    )
    a_parts = lax.all_to_all(a_sent, "rep", 0, 0, axis_index_groups=SAME_CORE)
    norm_sums, *pairs_out = outer(
        d_qkv,
        d_hidden,
        weight,
        spots,
        x_all,
        mean,
        inverse,
        jnp.stack([gains[0], gains[2]]),
        active,
        attended,
        down_weight,
        out_weight,
        wide_bias,
        (a_sent, above, below),
    )

    passed_below, passed_above = move(pairs_out[6], x=1), move(pairs_out[2], x=-1)

    def passed_body(n_ref, up_ref, from_below, here_ref, down_ref, from_above, there_ref, up_out, down_out):
        up_out[0:2] = wide(up_ref, from_below).astype(bf16)
        up_out[2:4] = here_ref[...]
        down_out[0:2] = wide(down_ref, from_above).astype(bf16)
        down_out[2:4] = there_ref[...]

    def other_body(n_ref, own_ref, below_ref, above_ref, out_ref):
        out_ref[...] = wide(own_ref, below_ref, above_ref).astype(bf16)

    def first(n):
        return 0

    def ends_body(n_ref, keep_ref, got_ref, below_ref, above_ref, leave_ref, stay_ref):
        total = wide(keep_ref, got_ref, below_ref, above_ref).astype(bf16)
        first = n_ref[3] == 0
        leave_ref[0] = jnp.where(first, total[1], total[0])
        stay_ref[0] = jnp.where(first, total[0], total[1])

    leaves, stays = blocks_call(
        "end_sums",
        ends_body,
        numbers,
        [(v, pair_shape, turn(0)) for v in (keep, got)]
        + [(v, pair_shape, lambda n: 0) for v in (from_below, from_above)],
        (one, one),
        (norm_sums,),
    )
    crossed = move(leaves, h=1)

    part, stays = packed_sums(
        stays,
        crossed,
        a_parts,
        norm_sums,
        qkv_sums,
        up_sums,
        dy_sums,
        numbers,
        ff,
        head,
        (),
    )
    received = lax.all_to_all(part, "shard", 0, 0)
    ups, downs = blocks_call(
        "passed_sums",
        passed_body,
        numbers,
        [
            (v, pair_shape, first)
            for v in (
                pairs_out[5],
                passed_below,
                pairs_out[1],
                pairs_out[3],
                passed_above,
                pairs_out[7],
            )
        ],
        ((4, 128, width),) * 2,
        (part,),
    )
    stays = stays[None]
    stays = jnp.concatenate([stays, move(stays, h=1)])
    part = unpacked_sums(received, cols, (ups, stays))
    beside = move(stays, y=1), move(stays, y=-1)
    stays = joined((stays, beside[1], beside[0], move(beside[0], y=1)), ())
    from_device_below, from_device_above = move(ups, x=1), move(downs, x=-1)
    (sent_other,) = blocks_call(
        "other_sums",
        other_body,
        numbers,
        [
            (pairs_out[4], pair_shape, first),
            (from_device_below, pair_shape, first),
            (from_device_above, pair_shape, lambda n: 1),
        ],
        (pair_shape,),
        (),
    )
    total_other = move(sent_other, l=1)

    places = jnp.stack([(y + k) % 4 for k in (0, 1, 3, 2)]).astype(jnp.int32)

    down_grad, out_grad = spread(
        [(stays, move(stays, c=1))],
        places,
        numbers,
        [(width, 64, [(0, 0, 0, width)]), (width, 16, [(0, 64, 0, width)])],
        4,
        (),
        (),
        14,
    )
    part = joined((part, move(part, h=1)), beside)
    below, above = move(part, y=1), move(part, y=-1)
    low, high, near = halves(part, below, above, (stays, sent_other))
    far = move(low, y=1), move(high, y=-1)
    targets = [
        (
            3 * width,
            16,
            [
                ((third * 8 + source) * head, 16 * source, third * head, head)
                for source in range(8)
                for third in range(3)
            ],
        ),
        (8 * ff, 16, [(source * ff, 16 * source, 3 * head, ff) for source in range(8)]),
    ]
    near_yours = move(near, c=1)
    grads = spread(
        [(near, near_yours)], places[:3], numbers, targets, 4, (), (down_grad, sent_other)
    )
    far = joined(far, (grads[0],))
    mixed, tokens_grad = finished(
        pairs_out[0], from_device_below, from_device_above, total_other, tokens, cotangent, (far,)
    )
    far_yours = move(far, c=1)
    qkv_grad, up_grad = spread(
        [(far, far_yours)],
        places[3:],
        numbers,
        targets,
        4,
        grads,
        (tokens_grad,),
    )
    smalls = [v[:, 0:16, cols:] for v in (near, near_yours, far, far_yours)]
    smalls = jnp.sum(jnp.concatenate(smalls).astype(f32), 0)
    norm_grads = smalls[:4]
    dy_total = smalls[11]
    return (
        mixed,
        tokens_grad,
        norm_grads[0],
        norm_grads[1],
        norm_grads[2],
        norm_grads[3],
        qkv_grad,
        smalls[4:7].reshape(3 * head),
        out_grad,
        dy_total,
        up_grad,
        smalls[7:11].reshape(ff),
        down_grad,
        dy_total,
    )


def solution(mesh):
    rows = P(BOTH, None)
    vector, matrix = P("shard"), P("shard", None)
    return jax.shard_map(
        local,
        mesh=mesh,
        in_specs=(rows, rows, rows, vector, vector, vector, vector)
        + (matrix, vector, matrix, vector, matrix, vector, matrix, vector),
        out_specs=(rows, rows, vector, vector, vector, vector)
        + (matrix, vector, matrix, vector, matrix, vector, matrix, vector),
        check_vma=False,
    )
```

```python
import functools
import math

import jax
import jax.numpy as jnp
from jax import lax
from jax.experimental import pallas as pl
from jax.experimental.pallas import tpu as pltpu
from jax.sharding import PartitionSpec as P

HEADS = 8
ROT = 64
EPS = 1e-05
f32 = jnp.float32
bf16 = jnp.bfloat16


def cost(time):
    return pl.CostEstimate(flops=int(time * 1.15e9), bytes_accessed=1000, transcendentals=0)


BOTH = ("rep", "shard")
SIZES = (4, 2, 2, 2, 4)
SAME_CORE = [[2 * n + c for n in range(8)] for c in range(2)]
SAME_CORE_ALL = [[(2 * n + c) * 8 + s for n in range(8) for s in range(8)] for c in range(2)]


def coords():
    for y in range(4):
        for h in range(2):
            for c in range(2):
                for l in range(2):
                    for x in range(4):
                        yield (y, h, c, l, x)


def linear(t):
    y, h, c, l, x = (v % m for v, m in zip(t, SIZES))
    return ((y * 2 + h) * 2 + c) * 8 + l * 4 + x


def move(value, y=0, h=0, c=0, l=0, x=0):
    step = (y, h, c, l, x)
    pairs = [(linear(t), linear(tuple(a + b for a, b in zip(t, step)))) for t in coords()]
    return lax.ppermute(value, BOTH, pairs)


def pick(value, index, axis):
    return lax.dynamic_index_in_dim(value, index, axis, keepdims=False)


def kernel_params():
    return pltpu.CompilerParams(vmem_limit_bytes=56 * 1024 * 1024)


def after_inputs(body, count, extra):
    return lambda *refs: body(*refs[:count], *refs[count + extra :])


def anywhere(count):
    return [pl.BlockSpec(memory_space=pl.ANY)] * count


def dot(a, b, ca=1, cb=0):
    return lax.dot_general(a, b, (((ca,), (cb,)), ((), ())), preferred_element_type=f32)


def swap_halves(value):
    lane = lax.broadcasted_iota(jnp.int32, value.shape, 1)
    return jnp.where(lane < 32, pltpu.roll(value, 96, 1), pltpu.roll(value, 32, 1))


def allowed_mask(lengths_ref, block, rows):
    e0 = lengths_ref[block, 0]
    e1 = e0 + lengths_ref[block, 1]
    t = lax.broadcasted_iota(jnp.int32, (rows, rows), 0)
    s = lax.broadcasted_iota(jnp.int32, (rows, rows), 1)
    seg_t = (t >= e0).astype(jnp.int32) + (t >= e1).astype(jnp.int32)
    seg_s = (s >= e0).astype(jnp.int32) + (s >= e1).astype(jnp.int32)
    return (seg_t == seg_s) & (s <= t)


def dot_rows(a, b):
    return lax.dot_general(a, b, (((0,), (0,)), ((), ())), preferred_element_type=f32)


def loads(copies):
    for copy in copies:
        copy.start()
    return copies


def piece_copies(pieces, half, target, sems, rows, lanes=slice(None)):
    return [
        pltpu.make_async_copy(
            piece.at[half, :, lanes] if len(piece.shape) == 3 else piece.at[:, lanes],
            target.at[pl.ds(at * rows, rows)],
            sems.at[at],
        )
        for at, piece in enumerate(pieces)
    ]


def weight_copies(pieces, refs, spot_ref, target, lanes, sems, source=None):
    if source is not None:
        pieces = [
            (
                array,
                begin + max(source - first, 0),
                min(size, 4),
                max(first, source) - source,
                spot,
                ref,
            )
            for (array, begin, size, first, spot), ref in zip(pieces, refs)
            if first <= source < first + size
        ]
    else:
        pieces = [(*piece, ref) for piece, ref in zip(pieces, refs)]
    return [
        pltpu.make_async_copy(
            ref.at[pl.ds(begin, size), :, lanes],
            target.at[pl.ds(first, size), spot_ref[spot]],
            sems.at[at],
        )
        for at, (_, begin, size, first, spot, ref) in enumerate(pieces)
    ]


def packed(qkv_weight, up_weight, vectors, lengths, place, head, tokens, cotangent):
    wide, up_wide = qkv_weight.shape[1], up_weight.shape[1]
    part, up_part = 3 * head, up_wide // 8
    cols = part + up_part

    def body(place_ref, len_ref, q_ref, u_ref, x_ref, dy_ref, *refs):
        v_refs, out_ref, pair_ref = refs[: len(vectors)], refs[-2], refs[-1]
        pair_ref[0] = x_ref[...]
        pair_ref[1] = dy_ref[...]
        lane = lax.broadcasted_iota(jnp.int32, (8, cols), 1)
        row = lax.broadcasted_iota(jnp.int32, (8, cols), 0)
        sizes = jnp.zeros((8, cols), f32)
        for at in range(3):
            sizes = jnp.where(lane == at, len_ref[0, at].astype(f32), sizes)
        vector = jnp.concatenate([ref[...].astype(f32) for ref in v_refs])[None, :]
        vector = jnp.broadcast_to(vector, (8, cols))
        tail = jnp.where(row == 0, vector, jnp.where(row == 1, sizes, 0.0)).astype(bf16)
        for owner in range(8):
            pieces = [
                q_ref[:, (third * 8 + owner) * head : (third * 8 + owner + 1) * head]
                for third in range(3)
            ]
            pieces.append(u_ref[:, owner * up_part : (owner + 1) * up_part])
            out_ref[owner] = jnp.concatenate([jnp.concatenate(pieces, 1), tail], 0)

    return pl.pallas_call(
        body,
        out_shape=(
            jax.ShapeDtypeStruct((8, 40, cols), bf16),
            jax.ShapeDtypeStruct((2,) + tokens.shape, bf16),
        ),
        grid_spec=pltpu.PrefetchScalarGridSpec(
            num_scalar_prefetch=2,
            grid=(1,),
            in_specs=[
                pl.BlockSpec((32, wide), lambda i, place, lens: (place[0], 0)),
                pl.BlockSpec((32, up_wide), lambda i, place, lens: (place[0], 0)),
                pl.BlockSpec(tokens.shape, lambda i, place, lens: (0, 0)),
                pl.BlockSpec(tokens.shape, lambda i, place, lens: (0, 0)),
            ]
            + [pl.BlockSpec(v.shape, lambda i, place, lens: (0,)) for v in vectors],
            out_specs=(
                pl.BlockSpec((8, 40, cols), lambda i, place, lens: (0, 0, 0)),
                pl.BlockSpec((2,) + tokens.shape, lambda i, place, lens: (0, 0, 0)),
            ),
        ),
        compiler_params=kernel_params(),
        cost_estimate=cost(3),
        name="packed",
    )(place, lengths, qkv_weight, up_weight, tokens, cotangent, *vectors)


def feed_forward(x, dy, gains, weight, spots, down, bias, numbers, first, after):
    rows, width = x[0].shape[1:]
    count = len(x)
    total = rows * count
    ff = bias.shape[1]

    parts = len(weight)

    def body(number_ref, spot_ref, g_ref, b_ref, *refs):
        w_refs, refs = refs[:parts], refs[parts:]
        x_refs, dy_refs, d_hbm = refs[:count], refs[count : 2 * count], refs[2 * count]
        (h1_hbm, act_hbm, du_hbm, keep_hbm, send_hbm, m_ref, i_ref, db_ref, sum_ref) = refs[
            2 * count + 1 : 2 * count + 10
        ]
        (x_v, dy_v, h1_v, h2_v, w_v, d_v, act_v, du_v, keep_v, send_v, x_sem, dy_sem, w_sem, sems) = refs[
            2 * count + 10 :
        ]
        own = number_ref[0] == 0
        x_copies = loads(piece_copies(x_refs, 0, x_v, x_sem, rows))
        w_copies = loads(
            weight_copies(weight, w_refs, spot_ref, w_v, pl.ds(first, ff), w_sem)
        )
        dy_copies = loads(piece_copies(dy_refs, 1, dy_v, dy_sem, rows))
        d_copy = pltpu.make_async_copy(d_hbm, d_v, sems.at[1])
        d_copy.start()
        for copy in x_copies:
            copy.wait()

        @pl.loop(0, count)
        def _(n):
            at = pl.ds(pl.multiple_of(n * rows, rows), rows)
            value = x_v[at, :].astype(f32)
            mean = jnp.mean(value, 1, keepdims=True)
            centre = value - mean
            inverse = lax.rsqrt(jnp.mean(centre * centre, 1, keepdims=True) + EPS)
            normed = centre * inverse
            m_ref[at, :] = mean
            i_ref[at, :] = inverse
            h1_v[at, :] = (normed * g_ref[0:1] + g_ref[1:2]).astype(bf16)
            h2_v[at, :] = (normed * g_ref[2:3] + g_ref[3:4]).astype(bf16)

        h1_copy = pltpu.make_async_copy(h1_v, h1_hbm, sems.at[2])
        h1_copy.start()
        for copy in w_copies + dy_copies:
            copy.wait()
        d_copy.wait()
        mine = dy_v[:, pl.ds(pl.multiple_of(number_ref[1] * 256, 256), 256)]
        sum_ref[...] = jnp.sum(mine.astype(f32), 0, keepdims=True)

        def split(part, places, high, wide):
            at = (places, high, wide)

            @pl.when(own)
            def _():
                keep_v[at] = part[:, 0]
                send_v[at] = part[:, 1]

            @pl.when(jnp.logical_not(own))
            def _():
                keep_v[at] = part[:, 1]
                send_v[at] = part[:, 0]

        def leaving(n):
            at = (pl.ds(n * 4, 4), pl.ds(0, 64))
            return (
                pltpu.make_async_copy(keep_v.at[at], keep_hbm.at[at], sems.at[3]),
                pltpu.make_async_copy(send_v.at[at], send_hbm.at[at], sems.at[4]),
            )

        @pl.loop(0, ff // 512)
        def _(n):
            at = pl.ds(pl.multiple_of(n * 512, 512), 512)
            u = dot(h2_v[...], w_v[:, :, :, at].reshape(width, 512)) + b_ref[:, at]
            cdf = 0.5 * (1.0 + lax.erf(u * math.sqrt(0.5)))
            pdf = jnp.exp(-0.5 * u * u) * (1.0 / math.sqrt(2.0 * math.pi))
            act = (u * cdf).astype(bf16)
            act_v[:, at] = act
            du = (dot(dy_v[...], d_v[at, :], 1, 1) * (cdf + u * pdf)).astype(bf16)
            du_v[:, at] = du
            db_ref[:, at] = jnp.sum(du.astype(f32), 0, keepdims=True)
            part = dot_rows(act, dy_v[...]).astype(bf16).reshape(4, 2, 64, width)
            split(part, pl.ds(n * 4, 4), pl.ds(0, 64), slice(None))
            for copy in leaving(n):
                copy.start()

        act_copy = pltpu.make_async_copy(act_v, act_hbm, sems.at[0])
        act_copy.start()
        du_copy = pltpu.make_async_copy(du_v, du_hbm, sems.at[1])
        du_copy.start()
        for n in range(ff // 512):
            for copy in leaving(n):
                copy.wait()

        def block(n):
            at = (
                slice(None),
                pl.ds(pl.multiple_of(64 + 16 * (n % 4), 16), 16),
                pl.ds(pl.multiple_of(n // 4 * ff, ff), ff),
            )
            return at

        def away(n):
            at = block(n)
            return (
                pltpu.make_async_copy(keep_v.at[at], keep_hbm.at[at], sems.at[3]),
                pltpu.make_async_copy(send_v.at[at], send_hbm.at[at], sems.at[4]),
            )

        @pl.loop(0, 8)
        def _(n):
            lanes = pl.ds(pl.multiple_of(n * 256, 256), 256)
            part = dot_rows(h2_v[:, lanes], du_v[...]).astype(bf16).reshape(8, 2, 16, ff)
            split(part, *block(n))
            for copy in away(n):
                copy.start()

        for n in range(8):
            for copy in away(n):
                copy.wait()
        h1_copy.wait()
        act_copy.wait()
        du_copy.wait()

    wide = jax.ShapeDtypeStruct((total, width), bf16)
    thin = jax.ShapeDtypeStruct((total, ff), bf16)
    column = jax.ShapeDtypeStruct((total, 1), f32)
    grads = jax.ShapeDtypeStruct((8, 128, width), bf16)
    vmem = pl.BlockSpec(memory_space=pltpu.VMEM)
    return pl.pallas_call(
        after_inputs(body, 5 + parts + 2 * count, len(after)),
        out_shape=(
            wide,
            thin,
            thin,
            grads,
            grads,
            column,
            column,
            jax.ShapeDtypeStruct((1, ff), f32),
            jax.ShapeDtypeStruct((1, 256), f32),
        ),
        in_specs=[pl.BlockSpec(memory_space=pltpu.SMEM)] * 2
        + [vmem, vmem]
        + anywhere(parts + 2 * count + 1 + len(after)),
        out_specs=tuple(anywhere(5)) + (vmem,) * 4,
        scratch_shapes=[
            pltpu.VMEM((total, width), bf16),
            pltpu.VMEM((total, width), bf16),
            pltpu.VMEM((total, width), bf16),
            pltpu.VMEM((total, width), bf16),
            pltpu.VMEM((8, 8, width // 64, ff), bf16),
            pltpu.VMEM((ff, width), bf16),
            pltpu.VMEM((total, ff), bf16),
            pltpu.VMEM((total, ff), bf16),
            pltpu.VMEM((8, 128, width), bf16),
            pltpu.VMEM((8, 128, width), bf16),
            pltpu.SemaphoreType.DMA((count,)),
            pltpu.SemaphoreType.DMA((count,)),
            pltpu.SemaphoreType.DMA((parts,)),
            pltpu.SemaphoreType.DMA((5,)),
        ],
        compiler_params=kernel_params(),
        cost_estimate=cost(32),
        name="feed_forward",
    )(numbers, spots, gains, bias, *[p[0] for p in weight], *x, *dy, down, *after)


def attend(h1, dy, weight, spots, out, bias, cosine, sine, lengths, after, rows=128):
    total, width = h1.shape
    count = len(dy)
    head = out.shape[0]
    scale = head ** (-0.5)

    parts = len(weight)

    def body(len_ref, spot_ref, b_ref, *refs):
        w_refs, refs = refs[:parts], refs[parts:]
        dy_refs = refs[:count]
        h1_hbm, out_hbm, cos_hbm, sin_hbm = refs[count : count + 4]
        ol_hbm, dq_hbm, sum_ref = refs[count + 4 : count + 7]
        (dy_v, h1_v, w_v, wo_v, cos_v, sin_v, qkv_v, do_v, ol_v, dq_v, dy_sem, w_sem, sems) = (
            refs[count + 7 :]
        )
        pairs = (
            (h1_hbm, h1_v),
            (out_hbm, wo_v),
            (cos_hbm, cos_v),
            (sin_hbm, sin_v),
        )
        copies = loads(
            [pltpu.make_async_copy(*pair, sems.at[n]) for n, pair in enumerate(pairs)]
        )
        w_copies = loads(
            weight_copies(weight, w_refs, spot_ref, w_v, pl.ds(0, 3 * head), w_sem)
        )
        dy_copies = loads(piece_copies(dy_refs, 1, dy_v, dy_sem, rows))
        for copy in copies[:1] + w_copies:
            copy.wait()

        @pl.loop(0, 3)
        def _(n):
            at = pl.ds(pl.multiple_of(n * head, head), head)
            qkv_v[:, at] = dot(h1_v[...], w_v[:, :, :, at].reshape(width, head)) + b_ref[n]

        for copy in copies[1:] + dy_copies:
            copy.wait()
        do_v[...] = dot(dy_v[...], wo_v[...], 1, 1).astype(bf16)
        sum_ref[...] = jnp.zeros_like(sum_ref)

        @pl.loop(0, total // rows, unroll=2)
        def _(block):
            at = pl.ds(pl.multiple_of(block * rows, rows), rows)
            cos, sin = cos_v[at, :], sin_v[at, :]

            def turned(value, sign):
                left = value[:, :128]
                left = left * cos + swap_halves(left) * (sin * sign)
                return jnp.concatenate([left, value[:, 128:]], 1).astype(bf16)

            q, k = turned(qkv_v[at, 0:head], 1.0), turned(qkv_v[at, head : 2 * head], 1.0)
            v = qkv_v[at, 2 * head :].astype(bf16)
            scores = dot(q, k, 1, 1) * scale
            masked = jnp.where(allowed_mask(len_ref, block, rows), scores, -1e30)
            shifted = jnp.exp(masked - jnp.max(masked, 1, keepdims=True))
            probs = shifted / jnp.sum(shifted, 1, keepdims=True)
            low = probs.astype(bf16)
            ol_v[at, :] = dot(low, v).astype(bf16)
            d_out = do_v[at, :]
            d_value = dot(low, d_out, 0, 0)
            d_probs = dot(d_out, v, 1, 1)
            centred = d_probs - jnp.sum(d_probs * probs, 1, keepdims=True)
            d_scores = (probs * centred).astype(bf16)
            d_query = turned(dot(d_scores, k) * scale, -1.0)
            d_key = turned(dot(d_scores, q, 0, 0) * scale, -1.0)
            for n, grad in enumerate((d_query, d_key, d_value.astype(bf16))):
                lanes = slice(n * head, (n + 1) * head)
                dq_v[at, lanes] = grad
                sum_ref[:, lanes] += jnp.sum(grad.astype(f32), 0, keepdims=True)

        ol_copy = pltpu.make_async_copy(ol_v, ol_hbm, sems.at[0])
        ol_copy.start()
        dq_copy = pltpu.make_async_copy(dq_v, dq_hbm, sems.at[1])
        dq_copy.start()

        for copy in (ol_copy, dq_copy):
            copy.wait()

    vmem = pl.BlockSpec(memory_space=pltpu.VMEM)
    smem = pl.BlockSpec(memory_space=pltpu.SMEM)
    return pl.pallas_call(
        after_inputs(body, 7 + parts + count, len(after)),
        out_shape=(
            jax.ShapeDtypeStruct((total, head), bf16),
            jax.ShapeDtypeStruct((total, 3 * head), bf16),
            jax.ShapeDtypeStruct((1, 3 * head), f32),
        ),
        in_specs=[smem, smem, vmem] + anywhere(parts + count + 4 + len(after)),
        out_specs=tuple(anywhere(2)) + (vmem,),
        scratch_shapes=[
            pltpu.VMEM((total, width), bf16),
            pltpu.VMEM((total, width), bf16),
            pltpu.VMEM((8, 8, width // 64, 3 * head), bf16),
            pltpu.VMEM((head, width), bf16),
            pltpu.VMEM((total, 128), f32),
            pltpu.VMEM((total, 128), f32),
            pltpu.VMEM((total, 3 * head), f32),
            pltpu.VMEM((total, head), bf16),
            pltpu.VMEM((total, head), bf16),
            pltpu.VMEM((total, 3 * head), bf16),
            pltpu.SemaphoreType.DMA((count,)),
            pltpu.SemaphoreType.DMA((parts,)),
            pltpu.SemaphoreType.DMA((4,)),
        ],
        compiler_params=kernel_params(),
        cost_estimate=cost(17),
        name="attend",
    )(
        lengths,
        spots,
        bias,
        *[p[0] for p in weight],
        *dy,
        h1,
        out,
        cosine,
        sine,
        *after,
    )


def attention_grads(h1, dy, d_qkv, attended, numbers, after):
    total, width = h1.shape
    count = len(dy)
    rows = total // count
    head = attended.shape[1]

    def body(number_ref, *refs):
        dy_refs = refs[:count]
        h1_hbm, dq_hbm, ol_hbm, keep_hbm, send_hbm = refs[count : count + 5]
        dy_v, h1_v, dq_v, ol_v, keep_v, send_v, dy_sem, sems = refs[count + 5 :]
        own = number_ref[0] == 0
        pairs = ((h1_hbm, h1_v), (dq_hbm, dq_v), (ol_hbm, ol_v))
        copies = loads(
            [pltpu.make_async_copy(*pair, sems.at[n]) for n, pair in enumerate(pairs)]
        )
        dy_copies = loads(piece_copies(dy_refs, 1, dy_v, dy_sem, rows))
        for copy in copies:
            copy.wait()

        def split(part, high, lanes):
            at = (slice(None), high, lanes)

            @pl.when(own)
            def _():
                keep_v[at] = part[:, 0]
                send_v[at] = part[:, 1]

            @pl.when(jnp.logical_not(own))
            def _():
                keep_v[at] = part[:, 1]
                send_v[at] = part[:, 0]

        @pl.loop(0, 8)
        def _(n):
            lanes = pl.ds(pl.multiple_of(n * 256, 256), 256)
            part = dot_rows(h1_v[:, lanes], dq_v[...]).astype(bf16).reshape(8, 2, 16, 3 * head)
            for third in range(3):
                split(
                    part[..., third * head : (third + 1) * head],
                    pl.ds(16 * third, 16),
                    pl.ds(pl.multiple_of(n * head, head), head),
                )

        for copy in dy_copies:
            copy.wait()
        part = dot_rows(ol_v[...], dy_v[...]).astype(bf16).reshape(8, 2, 16, width)
        split(part, pl.ds(48, 16), slice(None))
        keep_copy = pltpu.make_async_copy(keep_v, keep_hbm, sems.at[0])
        keep_copy.start()
        send_copy = pltpu.make_async_copy(send_v, send_hbm, sems.at[1])
        send_copy.start()
        keep_copy.wait()
        send_copy.wait()

    grads = jax.ShapeDtypeStruct((8, 64, width), bf16)
    return pl.pallas_call(
        after_inputs(body, 4 + count, len(after)),
        out_shape=(grads, grads),
        in_specs=[pl.BlockSpec(memory_space=pltpu.SMEM)] + anywhere(count + 3 + len(after)),
        out_specs=tuple(anywhere(2)),
        scratch_shapes=[
            pltpu.VMEM((total, width), bf16),
            pltpu.VMEM((total, width), bf16),
            pltpu.VMEM((total, 3 * head), bf16),
            pltpu.VMEM((total, head), bf16),
            pltpu.VMEM((8, 64, width), bf16),
            pltpu.VMEM((8, 64, width), bf16),
            pltpu.SemaphoreType.DMA((count,)),
            pltpu.SemaphoreType.DMA((3,)),
        ],
        compiler_params=kernel_params(),
        cost_estimate=cost(12),
        name="attention_grads",
    )(numbers, *dy, h1, d_qkv, attended, *after)


def outer(d_qkv, d_hidden, weight, spots, x, mean, inverse, gains, active, attended, down, out, bias, after):
    total, n1 = d_qkv.shape
    n2 = d_hidden.shape[1]
    count = len(x)
    parts = len(weight)
    head, width = out.shape
    step = 512

    def body(spot_ref, m_ref, i_ref, g_ref, b_ref, *refs):
        w_refs, refs = refs[:parts], refs[parts:]
        x_refs, refs = refs[:count], refs[count:]
        plain, sums_ref, outs = refs[:6], refs[6], refs[7 : 7 + count]
        dq_v, du_v, act_v, ol_v, wd_v, wo_v, w_v, x_v, pair_v, w_sem, x_sem, sems, out_sem = refs[
            7 + count :
        ]
        plain_v = (dq_v, du_v, act_v, ol_v, wd_v, wo_v)
        first = loads(
            [
                pltpu.make_async_copy(plain[n], plain_v[n], sems.at[n]) for n in range(2, 6)
            ]
        )
        copies = loads(
            [
                pltpu.make_async_copy(plain[n], plain_v[n], sems.at[n]) for n in range(2)
            ]
            + weight_copies(weight, w_refs, spot_ref, w_v, slice(None), w_sem)
            + piece_copies(x_refs, 0, x_v, x_sem, 128)
        )
        for copy in first:
            copy.wait()

        def leaving(n, half):
            lanes = pl.ds(pl.multiple_of(n * step, step), step)
            return [
                pltpu.make_async_copy(
                    pair_v.at[half, pl.ds(at * 128, 128), lanes],
                    outs[at].at[half, :, lanes],
                    out_sem.at[half, at],
                )
                for at in range(count)
            ]

        @pl.loop(0, width // step)
        def _(n):
            lanes = pl.ds(pl.multiple_of(n * step, step), step)
            mix = dot(act_v[...], wd_v[:, lanes]) + dot(ol_v[...], wo_v[:, lanes])
            pair_v[0, :, lanes] = (mix + b_ref[:, lanes]).astype(bf16)
            for copy in leaving(n, 0):
                copy.start()

        for copy in copies:
            copy.wait()

        @pl.loop(0, width // step)
        def _(n):
            lanes = pl.ds(pl.multiple_of(n * step, step), step)
            sources = pl.ds(n * (step // 256), step // 256)
            d1 = dot(dq_v[...], w_v[sources, :, :, 0:n1].reshape(step, n1), 1, 1)
            d2 = dot(du_v[...], w_v[sources, :, :, n1:].reshape(step, n2), 1, 1)
            pair_v[1, :, lanes] = (d1 * g_ref[0:1, lanes] + d2 * g_ref[1:2, lanes]).astype(bf16)
            for copy in leaving(n, 1):
                copy.start()
            normed = (x_v[:, lanes].astype(f32) - m_ref[...]) * i_ref[...]
            sums_ref[0:1, lanes] = jnp.sum(d1 * normed, 0, keepdims=True)
            sums_ref[1:2, lanes] = jnp.sum(d1, 0, keepdims=True)
            sums_ref[2:3, lanes] = jnp.sum(d2 * normed, 0, keepdims=True)
            sums_ref[3:4, lanes] = jnp.sum(d2, 0, keepdims=True)

        for n in range(width // step):
            for half in range(2):
                for copy in leaving(n, half):
                    copy.wait()

    vmem = pl.BlockSpec(memory_space=pltpu.VMEM)
    return pl.pallas_call(
        after_inputs(body, 11 + parts + count, len(after)),
        out_shape=(jax.ShapeDtypeStruct((4, width), f32),)
        + (jax.ShapeDtypeStruct((2, 128, width), bf16),) * count,
        in_specs=[pl.BlockSpec(memory_space=pltpu.SMEM)]
        + [vmem] * 4
        + anywhere(parts + count + 6 + len(after)),
        out_specs=(vmem,) + tuple(anywhere(count)),
        scratch_shapes=[
            pltpu.VMEM((total, n1), bf16),
            pltpu.VMEM((total, n2), bf16),
            pltpu.VMEM((total, n2), bf16),
            pltpu.VMEM((total, head), bf16),
            pltpu.VMEM((n2, width), bf16),
            pltpu.VMEM((head, width), bf16),
            pltpu.VMEM((8, 8, width // 64, n1 + n2), bf16),
            pltpu.VMEM((total, width), bf16),
            pltpu.VMEM((2, total, width), bf16),
            pltpu.SemaphoreType.DMA((parts,)),
            pltpu.SemaphoreType.DMA((count,)),
            pltpu.SemaphoreType.DMA((6,)),
            pltpu.SemaphoreType.DMA((2, count)),
        ],
        compiler_params=kernel_params(),
        cost_estimate=cost(20),
        name="outer",
    )(
        spots,
        mean,
        inverse,
        gains,
        bias,
        *[p[0] for p in weight],
        *x,
        d_qkv,
        d_hidden,
        active,
        attended,
        down,
        out,
        *after,
    )


def unpacked(part, after):
    owners, _, cols = part.shape

    def body(part_ref, rows_ref, info_ref):
        for owner in range(owners):
            rows_ref[owner] = part_ref[owner, 0:32]
            info_ref[owner] = part_ref[owner, 32:40].astype(f32)

    return pl.pallas_call(
        after_inputs(body, 1, len(after)),
        out_shape=(
            jax.ShapeDtypeStruct((owners, 32, cols), bf16),
            jax.ShapeDtypeStruct((owners, 8, cols), f32),
        ),
        in_specs=[pl.BlockSpec(memory_space=pltpu.VMEM)] + anywhere(len(after)),
        out_specs=(pl.BlockSpec(memory_space=pltpu.VMEM),) * 2,
        compiler_params=kernel_params(),
        cost_estimate=cost(3),
        name="unpacked",
    )(part, *after)


def joined(arrays, after):
    sizes = [array.shape[0] for array in arrays]
    unit = math.gcd(*sizes)
    block = (unit,) + arrays[0].shape[1:]
    count = len(arrays)
    firsts = [sum(sizes[:n]) // unit for n in range(count)]

    def body(*refs):
        step = pl.program_id(0)
        for ref, first, size in zip(refs, firsts, sizes):

            @pl.when((step >= first) & (step < first + size // unit))
            def _(ref=ref):
                refs[count][...] = ref[...]

    def came(first, size):
        return pl.BlockSpec(block, lambda i: (jnp.clip(i - first, 0, size // unit - 1), 0, 0))

    return pl.pallas_call(
        after_inputs(body, count, len(after)),
        out_shape=jax.ShapeDtypeStruct((sum(sizes),) + block[1:], bf16),
        grid=(sum(sizes) // unit,),
        in_specs=[came(first, size) for first, size in zip(firsts, sizes)] + anywhere(len(after)),
        out_specs=pl.BlockSpec(block, lambda i: (i, 0, 0)),
        compiler_params=kernel_params(),
        cost_estimate=cost(3),
        name="joined",
    )(*arrays, *after)


def halves(own, below, above, after):
    count, rows, cols = own.shape
    half = count // 2

    def body(own_ref, below_ref, above_ref, low_ref, high_ref, all_ref):
        step = pl.program_id(0)
        all_ref[0] = own_ref[...]
        all_ref[1] = above_ref[...]
        all_ref[2] = below_ref[...]

        @pl.when(step == 0)
        def _():
            low_ref[...] = below_ref[...]

        @pl.when(step == 1)
        def _():
            high_ref[...] = above_ref[...]

    block = pl.BlockSpec((half, rows, cols), lambda i: (i, 0, 0))
    whole = pl.BlockSpec((half, rows, cols), lambda i: (0, 0, 0))
    low, high, together = pl.pallas_call(
        after_inputs(body, 3, len(after)),
        out_shape=(jax.ShapeDtypeStruct((half, rows, cols), bf16),) * 2
        + (jax.ShapeDtypeStruct((3, count, rows, cols), bf16),),
        grid=(2,),
        in_specs=[block] * 3 + anywhere(len(after)),
        out_specs=(
            whole,
            whole,
            pl.BlockSpec((3, half, rows, cols), lambda i: (0, i, 0, 0)),
        ),
        compiler_params=kernel_params(),
        cost_estimate=cost(4),
        name="halves",
    )(own, below, above, *after)
    return low, high, together.reshape(3 * count, rows, cols)


def unpacked_sums(received, cols, after):
    sources, rows, width = received.shape

    def body(part_ref, out_ref):
        small = jnp.sum(part_ref[:, :, cols:].astype(f32), 0).astype(bf16)
        out_ref[0] = jnp.concatenate(
            [jnp.concatenate([part_ref[0, :, 0:cols], small], 1)]
            + [part_ref[n] for n in range(1, sources)],
            0,
        )

    vmem = pl.BlockSpec(memory_space=pltpu.VMEM)
    return pl.pallas_call(
        after_inputs(body, 1, len(after)),
        out_shape=jax.ShapeDtypeStruct((1, sources * rows, width), bf16),
        in_specs=[vmem] + anywhere(len(after)),
        out_specs=vmem,
        compiler_params=kernel_params(),
        cost_estimate=cost(3),
        name="unpacked_sums",
    )(received, *after)


def spread(pieces, places, numbers, targets, count, before, after, time=2):
    rows, cols = pieces[0][0].shape[1:]
    firsts, total = [], 0
    for mine, _ in pieces:
        firsts.append(total)
        total += mine.shape[0] // 2

    def body(place_ref, number_ref, *refs):
        step = pl.program_id(0)
        outs = refs[2 * len(pieces) + len(before) :]
        core, z_hi = number_ref[0], number_ref[3]
        for n, (first, (mine, _)) in enumerate(zip(firsts, pieces)):

            @pl.when((step >= first) & (step < first + mine.shape[0] // 2))
            def _(n=n):
                for other_core in range(2):
                    ref = refs[2 * n + other_core]
                    low = 1 - core if other_core else core
                    for other_z in range(2):
                        at = (1 - z_hi if other_z else z_hi) * 2 + low
                        for out_ref, (_, high, parts) in zip(outs, targets):
                            to_rows = pl.ds(pl.multiple_of(at * high, high), high)
                            for to, row, col, size in parts:
                                out_ref[to_rows, to : to + size] = ref[
                                    other_z, row : row + high, col : col + size
                                ].astype(f32)

    def chosen(first, size):
        return pl.BlockSpec(
            (2, rows, cols), lambda i, place, n: (jnp.clip(i - first, 0, size - 1), 0, 0)
        )

    specs, arrays = [], []
    for first, (mine, yours) in zip(firsts, pieces):
        specs += [chosen(first, mine.shape[0] // 2)] * 2
        arrays += [mine, yours]
    return pl.pallas_call(
        after_inputs(body, 2 + 2 * len(pieces) + len(before), len(after)),
        out_shape=tuple(
            jax.ShapeDtypeStruct((4 * count * high, wide), f32) for wide, high, _ in targets
        ),
        grid_spec=pltpu.PrefetchScalarGridSpec(
            num_scalar_prefetch=2,
            grid=(total,),
            in_specs=specs + anywhere(len(before) + len(after)),
            out_specs=tuple(
                pl.BlockSpec((4 * high, wide), lambda i, place, n: (place[i], 0))
                for wide, high, _ in targets
            ),
        ),
        input_output_aliases={2 + len(arrays) + n: n for n in range(len(before))},
        compiler_params=kernel_params(),
        cost_estimate=cost(time),
        name="spread",
    )(places, numbers, *arrays, *before, *after)


def packed_sums(stays, crossed, parts, norm_sums, qkv_sums, up_sums, dy_sums, numbers, ff, head, after):
    width = parts.shape[2]

    def body(*refs):
        stay_ref, cross_ref, parts_ref = refs[:3]
        norm_ref, q_ref, u_ref, y_ref, number_ref, out_ref, keep_ref, small = refs[3:]
        shard = number_ref[1]
        inner = (stay_ref[0].astype(f32) + cross_ref[0].astype(f32)).astype(bf16)
        total = jnp.sum(parts_ref[...].astype(f32), 0).astype(bf16)
        for owner in range(8):
            mine = shard == owner
            small[...] = jnp.zeros_like(small)
            small[0:4] = norm_ref[:, owner * head : (owner + 1) * head]
            for n in range(3):
                third, source = divmod(owner * 3 + n, 8)
                lanes = slice(third * head, (third + 1) * head)
                small[4 + n : 5 + n] = jnp.where(shard == source, q_ref[:, lanes], 0.0)
            for n in range(4):
                lanes = slice(n * head, (n + 1) * head)
                small[7 + n : 8 + n] = jnp.where(mine, u_ref[:, lanes], 0.0)
            small[11:12] = jnp.where(mine, y_ref[...], 0.0)
            pieces = [
                total[16 * third : 16 * third + 16, owner * head : (owner + 1) * head]
                for third in range(3)
            ]
            row, col = 64 + 16 * (owner % 4), owner // 4 * ff
            pieces.append(inner[row : row + 16, col : col + ff])
            pieces.append(small[...].astype(bf16))
            out_ref[owner] = jnp.concatenate(pieces, 1)
        keep_ref[0:64] = inner[0:64]
        keep_ref[64:80] = total[48:64]

    vmem = pl.BlockSpec(memory_space=pltpu.VMEM)
    return pl.pallas_call(
        after_inputs(body, 8, len(after)),
        out_shape=(
            jax.ShapeDtypeStruct((8, 16, 4 * head + ff), bf16),
            jax.ShapeDtypeStruct((80, width), bf16),
        ),
        in_specs=[vmem] * 7 + [pl.BlockSpec(memory_space=pltpu.SMEM)] + anywhere(len(after)),
        out_specs=(vmem,) * 2,
        scratch_shapes=[pltpu.VMEM((16, head), f32)],
        compiler_params=kernel_params(),
        cost_estimate=cost(3),
        name="packed_sums",
    )(stays, crossed, parts, norm_sums, qkv_sums, up_sums, dy_sums, numbers, *after)


def finished(own, below, above, other, tokens, cotangent, after):
    rows, width = tokens.shape
    step = rows // 2

    def body(own_ref, below_ref, above_ref, other_ref, x_ref, dy_ref, mixed_ref, grad_ref):
        total = wide(own_ref, below_ref, above_ref, other_ref)
        x = x_ref[...].astype(f32)
        mixed_ref[...] = (x + total[0]).astype(bf16)
        centre = x - jnp.mean(x, 1, keepdims=True)
        inverse = lax.rsqrt(jnp.mean(centre * centre, 1, keepdims=True) + EPS)
        normed = centre * inverse
        gain = total[1]
        grad_ref[...] = dy_ref[...].astype(f32) + inverse * (
            gain
            - jnp.mean(gain, 1, keepdims=True)
            - normed * jnp.mean(gain * normed, 1, keepdims=True)
        )

    def pair(first):
        return pl.BlockSpec((2, step, width), lambda i: (first, i, 0))

    block = pl.BlockSpec((step, width), lambda i: (i, 0))
    return pl.pallas_call(
        after_inputs(body, 6, len(after)),
        out_shape=(
            jax.ShapeDtypeStruct((rows, width), bf16),
            jax.ShapeDtypeStruct((rows, width), f32),
        ),
        grid=(2,),
        in_specs=[pair(0), pair(1), pair(0), pair(0), block, block] + anywhere(len(after)),
        out_specs=(block, block),
        compiler_params=kernel_params(),
        cost_estimate=cost(14),
        name="finished",
    )(own, below, above, other, tokens, cotangent, *after)


def blocks_call(name, body, numbers, terms, outs, after, time=3):
    def came(block, index):
        rest = (0,) * (len(block) - 1)
        return pl.BlockSpec(block, lambda i, n: (index(n),) + rest)

    return pl.pallas_call(
        after_inputs(body, 1 + len(terms), len(after)),
        out_shape=tuple(jax.ShapeDtypeStruct(out, bf16) for out in outs),
        grid_spec=pltpu.PrefetchScalarGridSpec(
            num_scalar_prefetch=1,
            grid=(1,),
            in_specs=[came(block, index) for _, block, index in terms] + anywhere(len(after)),
            out_specs=tuple(
                pl.BlockSpec(out, lambda i, n, size=len(out): (0,) * size) for out in outs
            ),
        ),
        compiler_params=kernel_params(),
        cost_estimate=cost(time),
        name=name,
    )(numbers, *[array for array, _, _ in terms], *after)


def wide(*refs):
    return functools.reduce(jnp.add, [ref[...].astype(f32) for ref in refs])


def local(
    tokens,
    doc_lengths,
    cotangent,
    ln1_gain,
    ln1_bias,
    ln2_gain,
    ln2_bias,
    qkv_weight,
    qkv_bias,
    out_weight,
    out_bias,
    up_weight,
    up_bias,
    down_weight,
    down_bias,
):
    rows, width = tokens.shape
    head = width // HEADS
    group = 8
    rep = lax.axis_index("rep")
    shard = lax.axis_index("shard")
    y, h, c = rep // 4, (rep // 2) % 2, rep % 2
    l, x = shard // 4, shard % 4
    ff = up_bias.shape[0]

    cols = 3 * head + ff
    vectors = [ln1_gain, ln1_bias, ln2_gain, ln2_bias, qkv_bias]
    place = (y * 2 + c).astype(jnp.int32).reshape(1)
    part, pair = packed(
        qkv_weight, up_weight, vectors, doc_lengths, place, head, tokens, cotangent
    )
    below, above, other = move(pair, x=1), move(pair, x=-1), move(pair, l=1)
    far, other_above, other_below = move(below, x=1), move(other, x=-1), move(below, l=1)
    pairs = (pair, above, far, below, other, other_above, None, other_below)

    part = lax.all_to_all(part, "shard", 0, 0)
    own, infos = unpacked(part, (pairs[1], pairs[3], pairs[4]))
    below, above = move(own, y=1), move(own, y=-1)
    x_other_far, dy_other_far = move(other_below[0], x=1), move(other_above[1], x=-1)
    low, high, yours = halves(own, below, above, (far, other_above, other_below))
    far_low, far_high = move(low, y=1), move(high, y=-1)
    x_all = tuple(x_other_far if p is None else p for p in pairs)
    dy_all = tuple(dy_other_far if p is None else p for p in pairs)
    yours = move(yours, c=1)
    far_low_c, far_high_c = move(far_low, c=1), move(far_high, c=1)
    weight = (
        (own, 0, 8, 0, 0),
        (above, 0, 8, 0, 1),
        (far_low, 0, 4, 0, 2),
        (far_high, 0, 4, 4, 2),
        (below, 0, 8, 0, 3),
        (yours, 0, 8, 0, 4),
        (yours, 8, 8, 0, 5),
        (far_low_c, 0, 4, 0, 6),
        (far_high_c, 0, 4, 4, 6),
        (yours, 16, 8, 0, 7),
    )
    steps4 = (y + jnp.arange(4)) % 4
    spots = jnp.concatenate([steps4 * 2 + c, steps4 * 2 + 1 - c]).astype(jnp.int32)

    gains = infos[:, 0, :1024].reshape(8, 4, 256).transpose(1, 0, 2).reshape(4, width)
    qkv_b = infos[:, 0, 1024:].reshape(8 * 3, 1, head)
    qkv_b = jnp.stack(
        [lax.dynamic_index_in_dim(qkv_b, third * 8 + shard, 0, False) for third in range(3)]
    )
    steps8 = jnp.arange(8)
    sources = ((steps8 // 4) ^ l) * 4 + (x + steps8 % 4) % 4
    sources = sources.astype(jnp.int32)
    lengths = infos[:, 1, :3]
    lengths = jnp.sum(
        jnp.where(sources[:, None, None] == steps8[None, :, None], lengths[None], 0.0), 1
    ).astype(jnp.int32)
    ends = jnp.cumsum(lengths, 1)
    starts = ends - lengths
    steps_t = jnp.arange(rows, dtype=jnp.int32)
    segment = jnp.sum((steps_t[None, :, None] >= ends[:, None, :]).astype(jnp.int32), -1)
    slots = jnp.arange(lengths.shape[1], dtype=jnp.int32)
    begin = jnp.sum(
        jnp.where(segment[:, :, None] == slots[None, None, :], starts[:, None, :], 0), -1
    )
    position = (steps_t[None, :] - begin).astype(f32).reshape(group * rows, 1)
    lane = jnp.arange(128)
    freq = 10000.0 ** (-2.0 * (lane % (ROT // 2)).astype(f32) / ROT)
    angle = position * freq[None, :]
    cosine = jnp.where(lane < ROT, jnp.cos(angle), 1.0)
    sine = jnp.sin(angle)
    sine = jnp.where(lane < ROT // 2, -sine, jnp.where(lane < ROT, sine, 0.0))

    both_bias = (out_bias.astype(f32) + down_bias.astype(f32))[None, :]
    wide_bias = lax.dynamic_update_slice(jnp.zeros((1, width), f32), both_bias, (0, shard * 256))
    numbers = jnp.stack([c, shard, y, h]).astype(jnp.int32)

    h1, active, d_hidden, keep, send, mean, inverse, up_sums, dy_sums = feed_forward(
        x_all,
        dy_all,
        gains,
        weight,
        spots,
        down_weight,
        up_bias.astype(f32)[None],
        numbers,
        3 * head,
        (cosine, sine),
    )
    got = move(send, c=1)
    attended, d_qkv, qkv_sums = attend(
        h1, dy_all, weight, spots, out_weight, qkv_b, cosine, sine, lengths, (send,)
    )

    pair_shape, one = (2, 128, width), (1, 128, width)

    def turn(k):
        return lambda n: (n[2] + k) % 4

    def far_body(n_ref, keep_ref, got_ref, low_ref, high_ref):
        total = wide(keep_ref, got_ref).astype(bf16)
        low_ref[0] = total[0]
        high_ref[0] = total[1]

    low, high = blocks_call(
        "far_sums",
        far_body,
        numbers,
        [(keep, pair_shape, turn(2)), (got, pair_shape, turn(2))],
        (one, one),
        (attended,),
    )
    from_low, from_high = move(low, y=1), move(high, y=-1)
    a_keep, a_send = attention_grads(h1, dy_all, d_qkv, attended, numbers, (low, high))
    a_got = move(a_send, c=1)
    def near_body(n_ref, k1_ref, g1_ref, k3_ref, g3_ref, low_ref, high_ref, above_ref, below_ref):
        above, below = wide(k1_ref, g1_ref), wide(k3_ref, g3_ref)
        above_ref[0] = (above[0] + low_ref[0].astype(f32)).astype(bf16)
        above_ref[1] = above[1].astype(bf16)
        below_ref[0] = below[0].astype(bf16)
        below_ref[1] = (below[1] + high_ref[0].astype(f32)).astype(bf16)

    above, below = blocks_call(
        "near_sums",
        near_body,
        numbers,
        [(v, pair_shape, turn(k)) for k in (1, 3) for v in (keep, got)]
        + [(v, one, lambda n: 0) for v in (from_low, from_high)],
        (pair_shape, pair_shape),
        (a_send,),
        20,
    )
    from_below, from_above = move(above, y=1), move(below, y=-1)

    four = (4, 64, width)

    def both_body(n_ref, low_keep, low_got, high_keep, high_got, out_ref):
        out_ref[0:4] = wide(low_keep, low_got).astype(bf16)
        out_ref[4:8] = wide(high_keep, high_got).astype(bf16)

    (a_sent,) = blocks_call(
        "both_sums",
        both_body,
        numbers,
        [(v, four, lambda n, half=half: half) for half in range(2) for v in (a_keep, a_got)],
        ((8, 64, width),),
        (above,),
    )
    a_parts = lax.all_to_all(a_sent, "rep", 0, 0, axis_index_groups=SAME_CORE)
    norm_sums, *pairs_out = outer(
        d_qkv,
        d_hidden,
        weight,
        spots,
        x_all,
        mean,
        inverse,
        jnp.stack([gains[0], gains[2]]),
        active,
        attended,
        down_weight,
        out_weight,
        wide_bias,
        (a_sent, above, below),
    )

    passed_below, passed_above = move(pairs_out[6], x=1), move(pairs_out[2], x=-1)

    def passed_body(n_ref, up_ref, from_below, here_ref, down_ref, from_above, there_ref, up_out, down_out):
        up_out[0:2] = wide(up_ref, from_below).astype(bf16)
        up_out[2:4] = here_ref[...]
        down_out[0:2] = wide(down_ref, from_above).astype(bf16)
        down_out[2:4] = there_ref[...]

    def other_body(n_ref, own_ref, below_ref, above_ref, out_ref):
        out_ref[...] = wide(own_ref, below_ref, above_ref).astype(bf16)

    def first(n):
        return 0

    def ends_body(n_ref, keep_ref, got_ref, below_ref, above_ref, leave_ref, stay_ref):
        total = wide(keep_ref, got_ref, below_ref, above_ref).astype(bf16)
        first = n_ref[3] == 0
        leave_ref[0] = jnp.where(first, total[1], total[0])
        stay_ref[0] = jnp.where(first, total[0], total[1])

    leaves, stays = blocks_call(
        "end_sums",
        ends_body,
        numbers,
        [(v, pair_shape, turn(0)) for v in (keep, got)]
        + [(v, pair_shape, lambda n: 0) for v in (from_below, from_above)],
        (one, one),
        (norm_sums,),
    )
    crossed = move(leaves, h=1)

    part, stays = packed_sums(
        stays,
        crossed,
        a_parts,
        norm_sums,
        qkv_sums,
        up_sums,
        dy_sums,
        numbers,
        ff,
        head,
        (),
    )
    received = lax.all_to_all(part, "shard", 0, 0)
    ups, downs = blocks_call(
        "passed_sums",
        passed_body,
        numbers,
        [
            (v, pair_shape, first)
            for v in (
                pairs_out[5],
                passed_below,
                pairs_out[1],
                pairs_out[3],
                passed_above,
                pairs_out[7],
            )
        ],
        ((4, 128, width),) * 2,
        (part,),
    )
    stays = stays[None]
    stays = jnp.concatenate([stays, move(stays, h=1)])
    part = unpacked_sums(received, cols, (ups, stays))
    beside = move(stays, y=1), move(stays, y=-1)
    stays = joined((stays, beside[1], beside[0], move(beside[0], y=1)), ())
    from_device_below, from_device_above = move(ups, x=1), move(downs, x=-1)
    (sent_other,) = blocks_call(
        "other_sums",
        other_body,
        numbers,
        [
            (pairs_out[4], pair_shape, first),
            (from_device_below, pair_shape, first),
            (from_device_above, pair_shape, lambda n: 1),
        ],
        (pair_shape,),
        (),
    )
    total_other = move(sent_other, l=1)

    places = jnp.stack([(y + k) % 4 for k in (0, 1, 3, 2)]).astype(jnp.int32)

    down_grad, out_grad = spread(
        [(stays, move(stays, c=1))],
        places,
        numbers,
        [(width, 64, [(0, 0, 0, width)]), (width, 16, [(0, 64, 0, width)])],
        4,
        (),
        (),
        14,
    )
    part = joined((part, move(part, h=1)), beside)
    below, above = move(part, y=1), move(part, y=-1)
    low, high, near = halves(part, below, above, (stays, sent_other))
    far = move(low, y=1), move(high, y=-1)
    targets = [
        (
            3 * width,
            16,
            [
                ((third * 8 + source) * head, 16 * source, third * head, head)
                for source in range(8)
                for third in range(3)
            ],
        ),
        (8 * ff, 16, [(source * ff, 16 * source, 3 * head, ff) for source in range(8)]),
    ]
    near_yours = move(near, c=1)
    grads = spread(
        [(near, near_yours)], places[:3], numbers, targets, 4, (), (down_grad, sent_other)
    )
    far = joined(far, (grads[0],))
    mixed, tokens_grad = finished(
        pairs_out[0], from_device_below, from_device_above, total_other, tokens, cotangent, (far,)
    )
    far_yours = move(far, c=1)
    qkv_grad, up_grad = spread(
        [(far, far_yours)],
        places[3:],
        numbers,
        targets,
        4,
        grads,
        (tokens_grad,),
    )
    smalls = [v[:, 0:16, cols:] for v in (near, near_yours, far, far_yours)]
    smalls = jnp.sum(jnp.concatenate(smalls).astype(f32), 0)
    norm_grads = smalls[:4]
    dy_total = smalls[11]
    return (
        mixed,
        tokens_grad,
        norm_grads[0],
        norm_grads[1],
        norm_grads[2],
        norm_grads[3],
        qkv_grad,
        smalls[4:7].reshape(3 * head),
        out_grad,
        dy_total,
        up_grad,
        smalls[7:11].reshape(ff),
        down_grad,
        dy_total,
    )


def solution(mesh):
    rows = P(BOTH, None)
    vector, matrix = P("shard"), P("shard", None)
    return jax.shard_map(
        local,
        mesh=mesh,
        in_specs=(rows, rows, rows, vector, vector, vector, vector)
        + (matrix, vector, matrix, vector, matrix, vector, matrix, vector),
        out_specs=(rows, rows, vector, vector, vector, vector)
        + (matrix, vector, matrix, vector, matrix, vector, matrix, vector),
        check_vma=False,
    )
```
